32 devices in a mesh: dp: 8 (over z, x), mp: 4 (over y, core).
Axes of the slice: x: 2, y: 2, z: 4, core: 2. Of those that a mesh axis runs over, the one named last changes fastest.
Arguments:
- inputs: bfloat16 [18432, 768], P(('dp', 'mp')), may hold values from -6 to 6
- history: bfloat16 [5, 18432, 768], P(None, ('dp', 'mp')), may hold values from -6 to 6
- cotangent: float32 [18432, 768], P(('dp', 'mp')), may hold values from -12 to 12
- qkv_weight: bfloat16 [768, 3, 768], P(None, None, 'mp'), may hold values from -0.21875 to 0.21875
- out_weight: bfloat16 [768, 768], P('mp'), may hold values from -1.25 to 1.25
- up_weight: bfloat16 [768, 3072], P(None, 'mp'), may hold values from -0.21875 to 0.21875
- down_weight: bfloat16 [3072, 768], P('mp'), may hold values from -0.109375 to 0.109375
- gain_attn: float32 [768], replicated, may hold values from 0.5 to 1.5
- gain_mlp: float32 [768], replicated, may hold values from 0.5 to 1.5
- dwa_weights: float32 [6], replicated, may hold values from 0.3 to 1
Outputs:
- combined: bfloat16 [18432, 768], P(('dp', 'mp'))
- input_grad: bfloat16 [18432, 768], P(('dp', 'mp'))
- history_grad: bfloat16 [5, 18432, 768], P(None, ('dp', 'mp'))
- qkv_grad: float32 [768, 3, 768], P(None, None, 'mp')
- out_grad: float32 [768, 768], P('mp')
- up_grad: float32 [768, 3072], P(None, 'mp')
- down_grad: float32 [3072, 768], P('mp')
- gain_attn_grad: float32 [768], replicated
- gain_mlp_grad: float32 [768], replicated
- dwa_grad: float32 [6], replicated
The draws below stay inside these ranges and needn't reach their ends.
All inputs are finite; a program needn't handle non-finite values.
Results may differ from the reference program's by a relative error of at most 0.019.
Values may be sent and summed in bfloat16 or wider, within the bound.
No kernel may reach another device: no remote copies, remote signals or barrier semaphores. Data moves between devices by JAX's collectives and lax.ppermute only.
A program may use at most 256 MiB of HBM per device.

```python
import jax
import jax.numpy as jnp
from jax import lax

D = 768
H = 12
DH = 64
FF = 3072
SEQ = 1152
HIST = 5
NSEQ = 16
TOKENS = 18432


def draw_cotangent(key, part):
    key = jax.random.fold_in(key, 11)
    position = lax.broadcasted_iota(jnp.float32, (TOKENS, D), 0) / (TOKENS - 1)
    rising = 1.0 + 2.0 * position
    sampled = jnp.clip(jax.random.normal(key, (TOKENS, D), jnp.float32), -4.0, 4.0)
    return sampled * rising


def steps_of(rng, dims, shards, low, top_value):
    gain = 1.0
    for dim, parts in shards:
        heights = jax.random.uniform(jax.random.fold_in(jax.random.fold_in(rng, 6), dim), (parts,), jnp.float32, low / len(shards), top_value / len(shards))
        gain = gain * jnp.repeat(jnp.exp(heights), dims[dim] // parts).reshape((-1,) + (1,) * (len(dims) - 1 - dim))
    return gain


def bell_draw(own_key, shape, scale, bound, split=(), held_as=jnp.bfloat16):
    level = steps_of(own_key, shape, split, -0.22, 0.18) if split else 1.0
    values = jax.random.normal(own_key, shape, jnp.float32) * scale * level
    return jnp.minimum(jnp.maximum(values, -bound), bound).astype(held_as)


def setup_inputs(seed: int = 0) -> dict:
    key_of = jax.random.split(jax.random.key(seed), 11)
    return {
        "inputs": bell_draw(key_of[0], (TOKENS, D), 1.0, 6.0, ((0, 32),)),
        "history": bell_draw(key_of[1], (HIST, TOKENS, D), 1.0, 6.0, ((1, 32),)),
        "cotangent": draw_cotangent(jax.random.fold_in(key_of[10], 71), 0),
        "qkv_weight": bell_draw(key_of[3], (D, 3, H * DH), D ** -0.5, 0.21875, ((2, 4),)),
        "out_weight": bell_draw(key_of[4], (H * DH, D), (H * DH // 32) ** -0.5, 1.25, ((0, 4),)),
        "up_weight": bell_draw(key_of[5], (D, FF), D ** -0.5, 0.21875, ((1, 4),)),
        "down_weight": bell_draw(key_of[6], (FF, D), FF ** -0.5, 0.109375, ((0, 4),)),
        "gain_attn": jnp.clip(1.0 + 0.1 * jax.random.normal(key_of[7], (D,), jnp.float32), 0.5, 1.5),
        "gain_mlp": jnp.clip(1.0 + 0.1 * jax.random.normal(key_of[8], (D,), jnp.float32), 0.5, 1.5),
        "dwa_weights": jnp.clip(jax.random.uniform(key_of[9], (HIST + 1,), jnp.float32, 0.3, 1.0), 0.3, 1.0),
    }


highest = lax.Precision.HIGHEST

@jax.custom_vjp
def low(v):
    return lax.optimization_barrier(v.astype(jnp.bfloat16)).astype(jnp.float32)

@jax.custom_vjp
def low_back(v):
    return v

def low_keep(v):
    return (low(v), None)

def low_pass(kept, grad):
    return (grad,)

def back_keep(v):
    return (v, None)

def back_low(kept, grad):
    return (low(grad),)
low.defvjp(low_keep, low_pass)
low_back.defvjp(back_keep, back_low)

def normed(row_values, gain_vector):
    centre = row_values - lax.optimization_barrier(jnp.mean(row_values, axis=-1, keepdims=True))
    spread = lax.optimization_barrier(jnp.mean(centre * centre, axis=-1, keepdims=True))
    return centre * lax.rsqrt(spread + 1e-05) * gain_vector

def tables():
    half_width = DH // 2
    places = jnp.arange(SEQ, dtype=jnp.float32)
    frequency = 10000.0 ** (-jnp.arange(half_width, dtype=jnp.float32) * 2.0 / DH)
    angles = places[:, None] * frequency[None, :]
    return (jnp.cos(angles), jnp.sin(angles))

def rotate(row_values, cosine_table, sine_table):
    half_width = row_values.shape[-1] // 2
    leading = row_values[..., :half_width]
    trailing = row_values[..., half_width:]
    cosine_part = cosine_table[:, None, :]
    sine_part = sine_table[:, None, :]
    return jnp.concatenate([leading * cosine_part - trailing * sine_part, trailing * cosine_part + leading * sine_part], axis=-1)

def layer_block(row_values, weights_all):
    qkv_weight, out_weight, up_weight, down_weight, gain_attn, gain_mlp = weights_all
    first_norm = low(normed(row_values, gain_attn))
    projected = low_back(jnp.einsum('td,dcf->tcf', first_norm, qkv_weight, precision=highest))
    cosine_table, sine_table = tables()
    shaped = projected.reshape(SEQ, 3, H, DH)
    queries = low(rotate(shaped[:, 0], cosine_table, sine_table))
    keys_rot = low(rotate(shaped[:, 1], cosine_table, sine_table))
    values = low(shaped[:, 2])
    scores = low_back(jnp.einsum('thd,uhd->htu', queries, keys_rot, precision=highest) * DH ** (-0.5))
    allowed = jnp.arange(SEQ)[:, None] >= jnp.arange(SEQ)[None, :]
    scores = jnp.where(allowed[None], scores, -jnp.inf)
    row_top = lax.optimization_barrier(jnp.max(scores, axis=-1, keepdims=True))
    exponent = jnp.exp(scores - row_top)
    probabilities = low(exponent / lax.optimization_barrier(jnp.sum(exponent, axis=-1, keepdims=True)))
    attended = jnp.einsum('htu,uhd->thd', probabilities, values, precision=highest).reshape(SEQ, H * DH)
    attended = low_back(low(attended))
    branch = low_back(jnp.dot(attended, out_weight, precision=highest))
    middle = row_values + branch
    second_norm = low(normed(middle, gain_mlp))
    hidden = low_back(jnp.dot(second_norm, up_weight, precision=highest))
    active = low(jax.nn.gelu(hidden, approximate=True))
    return middle + low_back(jnp.dot(active, down_weight, precision=highest))

def forward(inputs, history, weights_all, dwa_weights):
    sequences = inputs.reshape(NSEQ, SEQ, D)
    per_sequence = jax.checkpoint(lambda row_values: layer_block(row_values, weights_all))

    def advance(carried, row_values):
        return (carried, per_sequence(row_values))
    _, outputs = lax.scan(advance, jnp.zeros((), jnp.float32), sequences)
    outputs = outputs.reshape(TOKENS, D)
    combined = dwa_weights[HIST] * outputs
    for layer_index in range(HIST):
        combined = combined + dwa_weights[layer_index] * history[layer_index]
    return combined

def reference(inputs, history, cotangent, qkv_weight, out_weight, up_weight, down_weight, gain_attn, gain_mlp, dwa_weights):
    weights_all = tuple((weight.astype(jnp.float32) for weight in (qkv_weight, out_weight, up_weight, down_weight, gain_attn, gain_mlp)))
    combined, pullback = jax.vjp(forward, inputs.astype(jnp.float32), history.astype(jnp.float32), weights_all, dwa_weights.astype(jnp.float32))
    input_grad, history_grad, weight_grads, dwa_grad = pullback(cotangent.astype(jnp.float32))
    return (combined.astype(jnp.bfloat16), input_grad.astype(jnp.bfloat16), history_grad.astype(jnp.bfloat16), weight_grads[0], weight_grads[1], weight_grads[2], weight_grads[3], weight_grads[4], weight_grads[5], dwa_grad)
```

```python
import jax
import jax.numpy as jnp
from jax import lax
from jax.sharding import PartitionSpec as P

DH = 64
SEQ = 1152
bfloat = jnp.bfloat16
single = jnp.float32


def normed(row_values, gain_vector):
    centre = row_values - jnp.mean(row_values, axis=-1, keepdims=True)
    spread = jnp.mean(centre * centre, axis=-1, keepdims=True)
    return centre * lax.rsqrt(spread + 1e-05) * gain_vector


def tables():
    half_width = DH // 2
    places = jnp.arange(SEQ, dtype=jnp.float32)
    frequency = 10000.0 ** (-jnp.arange(half_width, dtype=jnp.float32) * 2.0 / DH)
    angles = places[:, None] * frequency[None, :]
    return (jnp.cos(angles), jnp.sin(angles))


def turn(row_values, cosine_table, sine_table):
    half_width = row_values.shape[-1] // 2
    leading = row_values[..., :half_width]
    trailing = row_values[..., half_width:]
    cosine_part = cosine_table[:, None, :]
    sine_part = sine_table[:, None, :]
    return jnp.concatenate(
        [
            leading * cosine_part - trailing * sine_part,
            trailing * cosine_part + leading * sine_part,
        ],
        axis=-1,
    )


def softened(hidden):
    return jax.nn.gelu(hidden, approximate=True)


def block_scores(query_block, key_block, row_begin):
    scores = (
        jnp.einsum("nhd,mhd->hnm", query_block, key_block, preferred_element_type=single)
        * DH ** (-0.5)
    )
    query_pos = row_begin + lax.broadcasted_iota(jnp.int32, scores.shape, 1)
    key_pos = lax.broadcasted_iota(jnp.int32, scores.shape, 2)
    return jnp.where(query_pos >= key_pos, scores, -jnp.inf)


def shards(
    inputs,
    history,
    cotangent,
    qkv_weight,
    out_weight,
    up_weight,
    down_weight,
    gain_attn,
    gain_mlp,
    dwa_weights,
):
    own_rows = inputs.shape[0]
    members = lax.axis_size("mp")
    core = lax.rem(lax.axis_index("mp"), 2)
    core_pairs = [(i, i ^ 1) for i in range(members)]
    chip_pairs = [(i, i ^ 2) for i in range(members)]
    depth = history.shape[0]
    width = out_weight.shape[0]

    def other_core(value):
        return lax.ppermute(value, "mp", core_pairs)

    def other_chip(value):
        return lax.ppermute(value, "mp", chip_pairs)

    def both(value):
        return jnp.concatenate([value, other_core(value)], axis=0)

    def fold(value):
        return value[:own_rows] + other_core(value[own_rows:].astype(bfloat)).astype(single)

    def ordered(value):
        return jnp.where(core == 0, value, jnp.roll(value, own_rows, axis=0))

    qkv_w = jnp.concatenate([qkv_weight, other_chip(qkv_weight)], axis=2)
    out_w = jnp.concatenate([out_weight, other_chip(out_weight)], axis=0)
    up_w = jnp.concatenate([up_weight, other_chip(up_weight)], axis=1)
    down_w = jnp.concatenate([down_weight, other_chip(down_weight)], axis=0)

    cosine_table, sine_table = tables()
    heads = 2 * width // DH
    head_shape = (SEQ, heads, DH)
    block_rows = SEQ // 2
    rows_in = inputs.astype(single)
    first_norm = both(normed(rows_in, gain_attn).astype(bfloat))
    first_norm = ordered(first_norm)
    projected = jnp.einsum("td,dcf->tcf", first_norm, qkv_w, preferred_element_type=single)
    queries = turn(projected[:, 0].reshape(head_shape), cosine_table, sine_table).astype(bfloat)
    keys_rot = turn(projected[:, 1].reshape(head_shape), cosine_table, sine_table).astype(bfloat)
    values = projected[:, 2].reshape(head_shape).astype(bfloat)
    pieces = []
    log_totals = []
    for part_index in range(2):
        row_begin = part_index * block_rows
        row_end = row_begin + block_rows
        scores = block_scores(queries[row_begin:row_end], keys_rot[:row_end], row_begin)
        row_top = jnp.max(scores, axis=-1, keepdims=True)
        exponent = jnp.exp(scores - row_top)
        row_total = jnp.sum(exponent, axis=-1, keepdims=True)
        probabilities = (exponent / row_total).astype(bfloat)
        pieces.append(
            jnp.einsum("hnm,mhd->nhd", probabilities, values[:row_end], preferred_element_type=single)
        )
        log_totals.append(row_top + jnp.log(row_total))
    attended = jnp.concatenate(pieces, axis=0).reshape(SEQ, 2 * width).astype(bfloat)
    attended = ordered(attended)
    middle = rows_in + fold(jnp.dot(attended, out_w, preferred_element_type=single))
    second_norm = both(normed(middle, gain_mlp).astype(bfloat))
    hidden = jnp.dot(second_norm, up_w, preferred_element_type=single)
    active = softened(hidden).astype(bfloat)
    outputs = middle + fold(jnp.dot(active, down_w, preferred_element_type=single))
    history_full = history.astype(single)
    mixing = dwa_weights[depth] * outputs
    for layer_index in range(depth):
        mixing = mixing + dwa_weights[layer_index] * history_full[layer_index]
    combined = mixing.astype(bfloat)
    dwa_partial = jnp.concatenate(
        [jnp.sum(history_full * cotangent[None], axis=(1, 2)), jnp.sum(outputs * cotangent)[None]]
    )
    history_grad = (dwa_weights[:depth, None, None] * cotangent[None]).astype(bfloat)
    grad_outputs = dwa_weights[depth] * cotangent
    _, gelu_pull = jax.vjp(softened, hidden)
    grad_mlp = both(grad_outputs.astype(bfloat))
    down_grad = jnp.einsum("tf,td->fd", active, grad_mlp, preferred_element_type=single)
    grad_active = jnp.einsum("td,fd->tf", grad_mlp, down_w, preferred_element_type=single)
    grad_hidden = gelu_pull(grad_active)[0].astype(bfloat)
    up_grad = jnp.einsum("td,tf->fd", second_norm, grad_hidden, preferred_element_type=single)
    grad_norm_mlp = fold(jnp.einsum("tf,df->td", grad_hidden, up_w, preferred_element_type=single))

    def across(value):
        half = value.shape[0] // 2
        return (value[:half] + other_chip(value[half:].astype(bfloat)).astype(single)).astype(bfloat)

    down_sum = lax.psum(across(down_grad), "dp")
    up_sum = lax.psum(across(up_grad), "dp")
    _, norm_pull = jax.vjp(normed, middle, gain_mlp)
    grad_middle_norm, gain_mlp_grad = norm_pull(grad_norm_mlp)
    grad_middle = grad_outputs + grad_middle_norm
    grad_branch = both(grad_middle.astype(bfloat))
    out_grad = jnp.einsum("tf,td->fd", attended, grad_branch, preferred_element_type=single)
    grad_attended = (
        ordered(jnp.einsum("td,fd->tf", grad_branch, out_w, preferred_element_type=single).astype(bfloat))
        .reshape(head_shape)
    )
    grad_queries = []
    grad_keys = jnp.zeros(head_shape, single)
    grad_values = jnp.zeros(head_shape, single)
    for part_index in range(2):
        row_begin = part_index * block_rows
        row_end = row_begin + block_rows
        query_block = queries[row_begin:row_end]
        key_block = keys_rot[:row_end]
        value_block = values[:row_end]
        scores = block_scores(query_block, key_block, row_begin)
        probabilities = jnp.exp(scores - log_totals[part_index])
        grad_piece = grad_attended[row_begin:row_end]
        grad_probs = jnp.einsum("nhd,mhd->hnm", grad_piece, value_block, preferred_element_type=single)
        centred = jnp.sum(probabilities * grad_probs, axis=-1, keepdims=True)
        grad_scores = (probabilities * (grad_probs - centred)).astype(bfloat)
        grad_queries.append(
            jnp.einsum("hnm,mhd->nhd", grad_scores, key_block, preferred_element_type=single)
            * DH ** (-0.5)
        )
        key_part = (
            jnp.einsum("hnm,nhd->mhd", grad_scores, query_block, preferred_element_type=single)
            * DH ** (-0.5)
        )
        value_part = jnp.einsum(
            "hnm,nhd->mhd", probabilities.astype(bfloat), grad_piece, preferred_element_type=single
        )
        grad_keys = grad_keys.at[:row_end].add(key_part)
        grad_values = grad_values.at[:row_end].add(value_part)
    grad_query_all = jnp.concatenate(grad_queries, axis=0)
    grad_projected = jnp.stack(
        [
            turn(grad_query_all, cosine_table, -sine_table).reshape(SEQ, 2 * width),
            turn(grad_keys, cosine_table, -sine_table).reshape(SEQ, 2 * width),
            grad_values.reshape(SEQ, 2 * width),
        ],
        axis=1,
    ).astype(bfloat)
    grad_norm_attn = fold(
        ordered(jnp.einsum("tcf,dcf->td", grad_projected, qkv_w, preferred_element_type=single))
    )
    qkv_grad = jnp.einsum("td,tcf->fdc", first_norm, grad_projected, preferred_element_type=single)
    _, first_pull = jax.vjp(normed, rows_in, gain_attn)
    grad_rows_norm, gain_attn_grad = first_pull(grad_norm_attn)
    input_grad = (grad_middle + grad_rows_norm).astype(bfloat)
    out_sum = lax.psum(across(out_grad), "dp")
    qkv_sum = lax.psum(across(qkv_grad), "dp")
    gain_attn_grad, gain_mlp_grad, dwa_grad = lax.psum(
        (gain_attn_grad, gain_mlp_grad, dwa_partial), ("dp", "mp")
    )
    return (
        combined,
        input_grad,
        history_grad,
        qkv_sum.transpose(1, 2, 0).astype(single),
        out_sum.astype(single),
        up_sum.T.astype(single),
        down_sum.astype(single),
        gain_attn_grad,
        gain_mlp_grad,
        dwa_grad,
    )


def solution(mesh):
    placed = (
        P(("dp", "mp"), None),
        P(None, ("dp", "mp"), None),
        P(("dp", "mp"), None),
        P(None, None, "mp"),
        P("mp", None),
        P(None, "mp"),
        P("mp", None),
        P(),
        P(),
        P(),
    )
    return jax.shard_map(
        shards,
        mesh=mesh,
        in_specs=placed,
        out_specs=(
            P(("dp", "mp"), None),
            P(("dp", "mp"), None),
            P(None, ("dp", "mp"), None),
            P(None, None, "mp"),
            P("mp", None),
            P(None, "mp"),
            P("mp", None),
            P(),
            P(),
            P(),
        ),
        check_vma=False,
    )
```

```python
import functools

import jax
import jax.numpy as jnp
import numpy as np
from jax import lax
from jax.experimental import pallas as pl
from jax.experimental.pallas import tpu as pltpu
from jax.sharding import PartitionSpec as P

DH = 64
SEQ = 1152
HALF = SEQ // 2
EPS = 1e-05
bfloat = jnp.bfloat16
single = jnp.float32
MIB = 1 << 20


def tables():
    half_width = DH // 2
    places = np.arange(SEQ, dtype=np.float32)
    frequency = np.float32(10000.0) ** (-np.arange(half_width, dtype=np.float32) * np.float32(2.0 / DH))
    angles = frequency[:, None] * places[None, :]
    return (np.cos(angles).astype(np.float32), np.sin(angles).astype(np.float32))


def mul(a, b, ca=1, cb=0):
    return lax.dot_general(a, b, (((ca,), (cb,)), ((), ())), preferred_element_type=single)


def call(kernel, outs, scratch=(), vmem=48, flops=0, moved=0, scalar=False, count=0):
    in_specs = [pl.BlockSpec(memory_space=pltpu.VMEM)] * count
    if scalar:
        in_specs = [pl.BlockSpec(memory_space=pltpu.SMEM)] + in_specs
    return pl.pallas_call(
        kernel,
        out_shape=[jax.ShapeDtypeStruct(shape, kind) for shape, kind in outs],
        in_specs=in_specs,
        out_specs=[pl.BlockSpec(memory_space=pltpu.VMEM)] * len(outs),
        scratch_shapes=list(scratch),
        compiler_params=pltpu.CompilerParams(vmem_limit_bytes=vmem * MIB),
        cost_estimate=pl.CostEstimate(flops=flops, bytes_accessed=moved, transcendentals=0),
    )


ROWS = 144


def norm_body(x_ref, gain_ref, out_ref):
    x = x_ref[...].astype(single)
    centre = x - jnp.mean(x, axis=-1, keepdims=True)
    spread = jnp.mean(centre * centre, axis=-1, keepdims=True)
    out_ref[...] = (centre * lax.rsqrt(spread + EPS) * gain_ref[...]).astype(bfloat)


def rows_spec(width):
    return pl.BlockSpec((ROWS, width), lambda i: (i, 0))


def one_spec(shape):
    return pl.BlockSpec(shape, lambda i: (0,) * len(shape))


def norm_rows(x, gain):
    rows, width = x.shape
    return pl.pallas_call(
        norm_body,
        grid=(rows // ROWS,),
        out_shape=jax.ShapeDtypeStruct((rows, width), bfloat),
        in_specs=[rows_spec(width), one_spec((1, width))],
        out_specs=rows_spec(width),
    )(x, gain)


def middle_body(x_ref, keep_ref, recv_ref, gain_ref, mid_ref, out_ref):
    x = x_ref[...].astype(single) + (keep_ref[...] + recv_ref[...].astype(single))
    mid_ref[...] = x
    centre = x - jnp.mean(x, axis=-1, keepdims=True)
    spread = jnp.mean(centre * centre, axis=-1, keepdims=True)
    out_ref[...] = (centre * lax.rsqrt(spread + EPS) * gain_ref[...]).astype(bfloat)


def middle_rows(x, keep, recv, gain):
    rows, width = x.shape
    spec = rows_spec(width)
    return pl.pallas_call(
        middle_body,
        grid=(rows // ROWS,),
        out_shape=[
            jax.ShapeDtypeStruct((rows, width), single),
            jax.ShapeDtypeStruct((rows, width), bfloat),
        ],
        in_specs=[spec, spec, spec, one_spec((1, width))],
        out_specs=[spec, spec],
    )(x, keep, recv, gain)


def norm_back(x, grad, gain):
    centre = x - jnp.mean(x, axis=-1, keepdims=True)
    spread = jnp.mean(centre * centre, axis=-1, keepdims=True)
    scale = lax.rsqrt(spread + EPS)
    normal = centre * scale
    lifted = grad * gain
    back = scale * (
        lifted
        - jnp.mean(lifted, axis=-1, keepdims=True)
        - normal * jnp.mean(lifted * normal, axis=-1, keepdims=True)
    )
    return back, normal


def middle_back_body(mix_ref, x_ref, keep_ref, recv_ref, cot_ref, gain_ref, mid_ref, low_ref, part_ref):
    grad = keep_ref[...] + recv_ref[...].astype(single)
    back, normal = norm_back(x_ref[...], grad, gain_ref[...])
    total = mix_ref[0] * cot_ref[...] + back
    mid_ref[...] = total
    low_ref[...] = total.astype(bfloat)

    @pl.when(pl.program_id(0) == 0)
    def _():
        part_ref[...] = jnp.zeros_like(part_ref)

    part_ref[...] += jnp.sum(grad * normal, axis=0, keepdims=True)


def middle_back(mix, x, keep, recv, cot, gain):
    rows, width = x.shape
    spec = rows_spec(width)
    return pl.pallas_call(
        middle_back_body,
        grid=(rows // ROWS,),
        out_shape=[
            jax.ShapeDtypeStruct((rows, width), single),
            jax.ShapeDtypeStruct((rows, width), bfloat),
            jax.ShapeDtypeStruct((1, width), single),
        ],
        in_specs=[pl.BlockSpec(memory_space=pltpu.SMEM), spec, spec, spec, spec, one_spec((1, width))],
        out_specs=[spec, spec, one_spec((1, width))],
    )(mix, x, keep, recv, cot, gain)


def first_back_body(x_ref, keep_ref, recv_ref, mid_ref, gain_ref, out_ref):
    grad = keep_ref[...] + recv_ref[...].astype(single)
    back, _ = norm_back(x_ref[...].astype(single), grad, gain_ref[...])
    out_ref[...] = (mid_ref[...] + back).astype(bfloat)


def first_back(x, keep, recv, mid, gain):
    rows, width = x.shape
    spec = rows_spec(width)
    return pl.pallas_call(
        first_back_body,
        grid=(rows // ROWS,),
        out_shape=jax.ShapeDtypeStruct((rows, width), bfloat),
        in_specs=[spec, spec, spec, spec, one_spec((1, width))],
        out_specs=spec,
    )(x, keep, recv, mid, gain)


BLOCKS = tuple((begin, min(256, SEQ - begin)) for begin in range(0, SEQ, 256))


def place(core_ref, own_ref, peer_ref, whole):
    low = pl.multiple_of(core_ref[0] * HALF, HALF)
    high = pl.multiple_of((1 - core_ref[0]) * HALF, HALF)
    whole[pl.ds(low, HALF), :] = own_ref[...]
    whole[pl.ds(high, HALF), :] = peer_ref[...]
    return low, high


def allowed(size):
    key_pos = lax.broadcasted_iota(jnp.int32, (size, size), 0)
    query_pos = lax.broadcasted_iota(jnp.int32, (size, size), 1)
    return query_pos >= key_pos


def turn(rows, cosine, sine):
    half = rows.shape[0] // 2
    a, b = rows[:half], rows[half:]
    return jnp.concatenate([a * cosine - b * sine, b * cosine + a * sine], axis=0)


def attend(core_ref, own_ref, peer_ref, weight_ref, cos_ref, sin_ref, qkv_ref, att_ref, log_ref, tokens):
    low, high = place(core_ref, own_ref, peer_ref, tokens)
    width = weight_ref.shape[0] // 3
    projected = mul(weight_ref[...], tokens[...], 1, 1)
    cosine, sine = cos_ref[...], sin_ref[...]
    for part in range(3):
        for head in range(width // DH):
            begin = part * width + head * DH
            rows = projected[begin : begin + DH]
            if part < 2:
                rows = turn(rows, cosine, sine)
            if part == 0:
                rows = rows * DH ** (-0.5)
            qkv_ref[begin : begin + DH, :] = rows.astype(bfloat)
    log_ref[...] = jnp.zeros_like(log_ref)
    for head in range(width // DH):
        base = head * DH
        keys = qkv_ref[width + base : width + base + DH, :].T
        for begin, size in BLOCKS:
            end = begin + size
            query = qkv_ref[base : base + DH, begin:end]
            scores = mul(keys[:end], query)
            corner = jnp.where(allowed(size), scores[begin:], -jnp.inf)
            top = jnp.max(corner, axis=0, keepdims=True)
            if begin:
                top = jnp.maximum(top, jnp.max(scores[:begin], axis=0, keepdims=True))
                scores = jnp.concatenate([scores[:begin], corner], axis=0)
            else:
                scores = corner
            weights = jnp.exp(scores - top)
            total = jnp.sum(weights, axis=0, keepdims=True)
            value = qkv_ref[2 * width + base : 2 * width + base + DH, :end]
            mixed = mul(value, weights.astype(bfloat)) / total
            att_ref[base : base + DH, begin:end] = mixed.astype(bfloat)
            log_ref[head : head + 1, begin:end] = top + jnp.log(total)
    return low, high


def attend_first(core_ref, own_ref, peer_ref, weight_ref, cos_ref, sin_ref, qkv_ref, att_ref, log_ref, tokens):
    attend(core_ref, own_ref, peer_ref, weight_ref, cos_ref, sin_ref, qkv_ref, att_ref, log_ref, tokens)


def attend_second(
    core_ref, own_ref, peer_ref, weight_ref, cos_ref, sin_ref, other_ref, out_a_ref, out_b_ref,
    qkv_ref, att_ref, log_ref, keep_ref, send_ref, tokens, branch,
):
    low, high = attend(
        core_ref, own_ref, peer_ref, weight_ref, cos_ref, sin_ref, qkv_ref, att_ref, log_ref, tokens
    )
    branch[...] = mul(other_ref[...], out_a_ref[...], 0, 0) + mul(att_ref[...], out_b_ref[...], 0, 0)
    keep_ref[...] = branch[pl.ds(low, HALF), :]
    send_ref[...] = branch[pl.ds(high, HALF), :].astype(bfloat)


def attend_back(
    second, core_ref, grad_own_ref, grad_peer_ref, own_ref, peer_ref, weight_ref, out_ref, qkv_ref, att_ref,
    log_ref, cos_ref, sin_ref, *rest,
):
    if second:
        before_ref, gain_ref, both_ref, keep_ref, send_ref, part_ref, tokens, grads, turned, whole = rest
    else:
        both_ref, whole, tokens, grads, turned = rest
    low, high = place(core_ref, own_ref, peer_ref, tokens)
    place(core_ref, grad_own_ref, grad_peer_ref, grads)
    width = out_ref.shape[0]
    both_ref[3 * width :, :] = mul(att_ref[...], grads[...])
    grad_att = mul(out_ref[...], grads[...], 1, 1).astype(bfloat)
    cosine, sine = cos_ref[...], sin_ref[...]
    for head in range(width // DH):
        base = head * DH
        query = qkv_ref[base : base + DH, :]
        key = qkv_ref[width + base : width + base + DH, :]
        value = qkv_ref[2 * width + base : 2 * width + base + DH, :]
        above = grad_att[base : base + DH]
        centre = jnp.sum(
            above.astype(single) * att_ref[base : base + DH, :].astype(single), axis=0, keepdims=True
        )
        keys, values = key.T, value.T
        grad_query, grad_key, grad_value = [], None, None
        for begin, size in reversed(BLOCKS):
            end = begin + size
            scores = mul(keys[:end], query[:, begin:end])
            corner = jnp.where(allowed(size), scores[begin:], -jnp.inf)
            scores = jnp.concatenate([scores[:begin], corner], axis=0) if begin else corner
            probs = jnp.exp(scores - log_ref[head : head + 1, begin:end])
            grad_probs = mul(values[:end], above[:, begin:end])
            grad_scores = (probs * (grad_probs - centre[:, begin:end])).astype(bfloat)
            grad_query.insert(0, mul(key[:, :end], grad_scores))
            key_part = mul(query[:, begin:end], grad_scores, 1, 1)
            value_part = mul(above[:, begin:end], probs.astype(bfloat), 1, 1)
            if grad_key is None:
                grad_key, grad_value = key_part, value_part
            else:
                grad_key = jnp.concatenate([grad_key[:, :end] + key_part, grad_key[:, end:]], axis=1)
                grad_value = jnp.concatenate([grad_value[:, :end] + value_part, grad_value[:, end:]], axis=1)
        grad_query = jnp.concatenate(grad_query, axis=1) * DH ** (-0.5)
        turned[base : base + DH, :] = turn(grad_query, cosine, -sine).astype(bfloat)
        turned[width + base : width + base + DH, :] = turn(grad_key, cosine, -sine).astype(bfloat)
        turned[2 * width + base : 2 * width + base + DH, :] = grad_value.astype(bfloat)
    both_ref[: 3 * width, :] = mul(turned[...], tokens[...])
    result = mul(turned[...], weight_ref[...], 0, 0)
    if second:
        whole[...] = before_ref[...] + result
        keep_ref[...] = whole[pl.ds(low, HALF), :]
        send_ref[...] = whole[pl.ds(high, HALF), :].astype(bfloat)
        part_ref[...] = (
            jnp.sum(whole[...] * tokens[...].astype(single), axis=0, keepdims=True) / gain_ref[...]
        )
    else:
        whole[...] = result


CURVE = float(np.sqrt(2.0 / np.pi))
STEP = 256


def mlp_body(second, x_own_ref, x_peer_ref, g_own_ref, g_peer_ref, up_ref, down_ref, *rest):
    if second:
        keep_out_a, keep_norm_a, send_out_a, send_norm_a = rest[:4]
        rest = rest[4:]
    keep_out_ref, send_out_ref, keep_norm_ref, send_norm_ref, up_grad_ref, down_grad_ref = rest[:6]
    x_all, g_all, x_turned, active, grad_hidden = rest[6:]
    rows = x_own_ref.shape[0]
    hidden_units = down_ref.shape[0]
    x_all[:rows, :] = x_own_ref[...]
    x_all[rows:, :] = x_peer_ref[...]
    g_all[:rows, :] = g_own_ref[...]
    g_all[rows:, :] = g_peer_ref[...]
    x_turned[...] = x_all[...].T
    for begin in range(0, hidden_units, STEP):
        columns = slice(begin, begin + STEP)
        for top in range(0, 2 * rows, rows):
            span = slice(top, top + rows)
            v = mul(x_all[span, :], up_ref[:, columns])
            grad = mul(g_all[span, :], down_ref[columns, :], 1, 1)
            square = v * v
            half = 0.5 + 0.5 * jnp.tanh(v * (CURVE + (CURVE * 0.044715) * square))
            act = v * half
            slope = half + act * (1.0 - half) * (2.0 * CURVE + (6.0 * CURVE * 0.044715) * square)
            active[span, columns] = act.astype(bfloat)
            grad_hidden[span, columns] = (grad * slope).astype(bfloat)
    out_own = mul(active[:rows, :], down_ref[...])
    out_peer = mul(active[rows:, :], down_ref[...])
    norm_own = mul(grad_hidden[:rows, :], up_ref[...], 1, 1)
    norm_peer = mul(grad_hidden[rows:, :], up_ref[...], 1, 1)
    if second:
        out_own = out_own + keep_out_a[...]
        out_peer = out_peer + send_out_a[...].astype(single)
        norm_own = norm_own + keep_norm_a[...]
        norm_peer = norm_peer + send_norm_a[...].astype(single)
    keep_out_ref[...] = out_own
    send_out_ref[...] = out_peer.astype(bfloat)
    keep_norm_ref[...] = norm_own
    send_norm_ref[...] = norm_peer.astype(bfloat)
    down_grad_ref[...] = mul(active[...], g_all[...], 0, 0)
    up_grad_ref[...] = mul(x_turned[...], grad_hidden[...])


def mlp(x_own, x_peer, g_own, g_peer, up, down, before=()):
    rows, width = x_own.shape
    units = down.shape[0]
    outs = [
        ((rows, width), single),
        ((rows, width), bfloat),
        ((rows, width), single),
        ((rows, width), bfloat),
        ((width, units), single),
        ((units, width), single),
    ]
    scratch = [
        pltpu.VMEM((2 * rows, width), bfloat),
        pltpu.VMEM((2 * rows, width), bfloat),
        pltpu.VMEM((width, 2 * rows), bfloat),
        pltpu.VMEM((2 * rows, units), bfloat),
        pltpu.VMEM((2 * rows, units), bfloat),
    ]
    return call(
        functools.partial(mlp_body, bool(before)),
        outs,
        scratch,
        count=6 + len(before),
        vmem=56,
        flops=24 * rows * width * units,
        moved=20 * MIB,
    )(x_own, x_peer, g_own, g_peer, up, down, *before)


def shards(
    inputs,
    history,
    cotangent,
    qkv_weight,
    out_weight,
    up_weight,
    down_weight,
    gain_attn,
    gain_mlp,
    dwa_weights,
):
    rows, width = inputs.shape
    members = lax.axis_size("mp")
    copies = lax.axis_size("dp")
    core = lax.rem(lax.axis_index("mp"), 2).astype(jnp.int32).reshape(1)
    copy_index = lax.axis_index("dp")
    core_pairs = [(i, i ^ 1) for i in range(members)]
    chip_pairs = [(i, i ^ 2) for i in range(members)]
    depth = history.shape[0]
    part = out_weight.shape[0]

    def other_core(value):
        return lax.ppermute(value, "mp", core_pairs)

    def other_chip(value):
        return lax.ppermute(value, "mp", chip_pairs)

    def other_copy(value, bit):
        return lax.ppermute(value, "dp", [(i, i ^ (1 << bit)) for i in range(copies)])

    gain_attn_row = gain_attn.reshape(1, width)
    gain_mlp_row = gain_mlp.reshape(1, width)
    cosine, sine = (jnp.asarray(table) for table in tables())

    qkv_own = qkv_weight.transpose(1, 2, 0).reshape(3 * part, width)
    qkv_peer = other_chip(qkv_own)
    out_peer = other_chip(out_weight)
    up_peer = other_chip(up_weight)
    down_peer = other_chip(down_weight)

    x_own = norm_rows(inputs, gain_attn_row)
    x_peer = other_core(x_own)
    grad_outputs = dwa_weights[depth] * cotangent
    g_own = grad_outputs.astype(bfloat)
    g_peer = other_core(g_own)

    tokens = pltpu.VMEM((SEQ, width), bfloat)
    first_outs = [((3 * part, SEQ), bfloat), ((part, SEQ), bfloat), ((8, SEQ), single)]
    attend_flops = 2 * SEQ * width * 3 * part + 4 * SEQ * SEQ * part
    qkv_a, att_a, log_a = call(
        attend_first, first_outs, [tokens], scalar=True, count=5, flops=attend_flops, moved=6 * MIB
    )(core, x_own, x_peer, qkv_own, cosine, sine)
    qkv_b, att_b, log_b, keep, send = call(
        attend_second,
        first_outs + [((rows, width), single), ((rows, width), bfloat)],
        [tokens, pltpu.VMEM((SEQ, width), single)],
        scalar=True,
        count=8,
        flops=attend_flops + 4 * SEQ * width * part,
        moved=10 * MIB,
    )(core, x_own, x_peer, qkv_peer, cosine, sine, att_a, out_weight, out_peer)
    middle, y_own = middle_rows(inputs, keep, other_core(send), gain_mlp_row)
    y_peer = other_core(y_own)

    first = mlp(y_own, y_peer, g_own, g_peer, up_weight, down_weight)
    second = mlp(
        y_own, y_peer, g_own, g_peer, up_peer, down_peer, (first[0], first[2], first[1], first[3])
    )
    keep_out, send_out, keep_norm, send_norm = second[:4]
    up_mine, down_mine = first[4:]
    up_theirs, down_theirs = (value.astype(bfloat) for value in second[4:])
    grad_middle, gb_own, gain_mlp_part = middle_back(
        dwa_weights[depth:], middle, keep_norm, other_core(send_norm), cotangent, gain_mlp_row
    )
    gb_peer = other_core(gb_own)

    def summed(mine, theirs):
        value = mine + other_chip(theirs).astype(single)
        bits = copies.bit_length() - 1
        for bit in range(bits - 1):
            size = value.shape[0] // 2
            upper = (copy_index >> bit) & 1
            kept = lax.dynamic_slice_in_dim(value, upper * size, size, 0)
            sent = lax.dynamic_slice_in_dim(value, (1 - upper) * size, size, 0).astype(bfloat)
            value = kept + other_copy(sent, bit).astype(single)
        value = value.astype(bfloat)
        if bits:
            value = (value.astype(single) + other_copy(value, bits - 1).astype(single)).astype(bfloat)
        for bit in reversed(range(bits - 1)):
            upper = (copy_index >> bit) & 1
            come = other_copy(value, bit)
            value = jnp.where(
                upper == 1, jnp.concatenate([come, value], 0), jnp.concatenate([value, come], 0)
            )
        return value.astype(single)

    def in_chunks(mine, theirs, chunks):
        size = mine.shape[0] // chunks
        return jnp.concatenate(
            [summed(mine[i : i + size], theirs[i : i + size]) for i in range(0, mine.shape[0], size)], 0
        )

    down_grad = in_chunks(down_mine, down_theirs, 2)
    up_grad = in_chunks(up_mine, up_theirs, 2)

    back_flops = 2 * SEQ * width * 8 * part + 10 * SEQ * SEQ * part
    both_theirs, before = call(
        functools.partial(attend_back, False),
        [((4 * part, width), single), ((SEQ, width), single)],
        [tokens, tokens, pltpu.VMEM((3 * part, SEQ), bfloat)],
        scalar=True,
        count=11,
        flops=back_flops,
        moved=14 * MIB,
    )(core, gb_own, gb_peer, x_own, x_peer, qkv_peer, out_peer, qkv_b, att_b, log_b, cosine, sine)
    both_mine, keep_first, send_first, gain_attn_part = call(
        functools.partial(attend_back, True),
        [((4 * part, width), single), ((rows, width), single), ((rows, width), bfloat), ((1, width), single)],
        [tokens, tokens, pltpu.VMEM((3 * part, SEQ), bfloat), pltpu.VMEM((SEQ, width), single)],
        scalar=True,
        count=13,
        flops=back_flops,
        moved=14 * MIB,
    )(
        core, gb_own, gb_peer, x_own, x_peer, qkv_own, out_weight, qkv_a, att_a, log_a, cosine, sine,
        before, gain_attn_row,
    )
    both_grad = in_chunks(both_mine, both_theirs.astype(bfloat), 2)
    input_grad = first_back(inputs, keep_first, other_core(send_first), grad_middle, gain_attn_row)

    outputs = middle + (keep_out + other_core(send_out).astype(single))
    history_full = history.astype(single)
    mixing = dwa_weights[depth] * outputs
    for layer_index in range(depth):
        mixing = mixing + dwa_weights[layer_index] * history_full[layer_index]
    combined = mixing.astype(bfloat)
    dwa_part = jnp.concatenate(
        [jnp.sum(history_full * cotangent[None], axis=(1, 2)), jnp.sum(outputs * cotangent)[None]]
    )
    history_grad = (dwa_weights[:depth, None, None] * cotangent[None]).astype(bfloat)

    small = jnp.concatenate(
        [gain_attn_part, gain_mlp_part, jnp.pad(dwa_part, (0, width - depth - 1)).reshape(1, width)], axis=0
    )
    small = small + other_core(small)
    small = small + other_chip(small)
    for bit in range(copies.bit_length() - 1):
        small = small + other_copy(small, bit)

    return (
        combined,
        input_grad,
        history_grad,
        both_grad[: 3 * part].reshape(3, part, width).transpose(2, 0, 1),
        both_grad[3 * part :],
        up_grad,
        down_grad,
        small[0],
        small[1],
        small[2, : depth + 1],
    )


def solution(mesh):
    placed = (
        P(("dp", "mp"), None),
        P(None, ("dp", "mp"), None),
        P(("dp", "mp"), None),
        P(None, None, "mp"),
        P("mp", None),
        P(None, "mp"),
        P("mp", None),
        P(),
        P(),
        P(),
    )
    return jax.shard_map(
        shards,
        mesh=mesh,
        in_specs=placed,
        out_specs=(
            P(("dp", "mp"), None),
            P(("dp", "mp"), None),
            P(None, ("dp", "mp"), None),
            P(None, None, "mp"),
            P("mp", None),
            P(None, "mp"),
            P("mp", None),
            P(),
            P(),
            P(),
        ),
        check_vma=False,
    )
```

```python
import functools

import jax
import jax.numpy as jnp
import numpy as np
from jax import lax
from jax.experimental import pallas as pl
from jax.experimental.pallas import tpu as pltpu
from jax.sharding import PartitionSpec as P

DH = 64
SEQ = 1152
HALF = SEQ // 2
EPS = 1e-05
bfloat = jnp.bfloat16
single = jnp.float32
MIB = 1 << 20


def tables():
    half_width = DH // 2
    places = np.arange(SEQ, dtype=np.float32)
    frequency = np.float32(10000.0) ** (-np.arange(half_width, dtype=np.float32) * np.float32(2.0 / DH))
    angles = frequency[:, None] * places[None, :]
    return (np.cos(angles).astype(np.float32), np.sin(angles).astype(np.float32))


def mul(a, b, ca=1, cb=0):
    return lax.dot_general(a, b, (((ca,), (cb,)), ((), ())), preferred_element_type=single)


def call(kernel, outs, operands, scratch=(), scalars=0, after=(), vmem=16):
    count, waits = len(operands), len(after)

    def body(*refs):
        kernel(*refs[:count], *refs[count + waits :])

    small = pl.BlockSpec(memory_space=pltpu.SMEM)
    whole = pl.BlockSpec(memory_space=pltpu.VMEM)
    apart = pl.BlockSpec(memory_space=pl.ANY)
    return pl.pallas_call(
        body,
        out_shape=[jax.ShapeDtypeStruct(shape, kind) for shape, kind in outs],
        in_specs=[small] * scalars + [whole] * (count - scalars) + [apart] * waits,
        out_specs=[whole] * len(outs),
        scratch_shapes=list(scratch),
        compiler_params=pltpu.CompilerParams(vmem_limit_bytes=vmem * MIB),
        cost_estimate=pl.CostEstimate(flops=0, bytes_accessed=0, transcendentals=0),
    )(*operands, *after)


ROWS = 64


def spans(rows, step=ROWS):
    return [slice(begin, begin + step) for begin in range(0, rows, step)]


def normal_of(x):
    centre = x - jnp.mean(x, axis=-1, keepdims=True)
    spread = jnp.mean(centre * centre, axis=-1, keepdims=True)
    scale = lax.rsqrt(spread + EPS)
    return centre * scale, scale


def norm_body(x_ref, gain_ref, out_ref):
    gain = gain_ref[...].reshape(1, -1)
    for span in spans(x_ref.shape[0]):
        normal, _ = normal_of(x_ref[span, :].astype(single))
        out_ref[span, :] = (normal * gain).astype(bfloat)


def middle_body(x_ref, keep_ref, recv_ref, gain_ref, mid_ref, out_ref):
    gain = gain_ref[...].reshape(1, -1)
    for span in spans(x_ref.shape[0]):
        x = x_ref[span, :].astype(single) + (keep_ref[span, :] + recv_ref[span, :].astype(single))
        mid_ref[span, :] = x
        normal, _ = normal_of(x)
        out_ref[span, :] = (normal * gain).astype(bfloat)


def norm_back(x, grad, gain):
    normal, scale = normal_of(x)
    lifted = grad * gain
    back = scale * (
        lifted
        - jnp.mean(lifted, axis=-1, keepdims=True)
        - normal * jnp.mean(lifted * normal, axis=-1, keepdims=True)
    )
    return back, normal


def fold_rows(value):
    total = value[:8]
    for begin in range(8, value.shape[0], 8):
        total = total + value[begin : begin + 8]
    return total


def middle_back_body(mix_ref, x_ref, keep_ref, recv_ref, cot_ref, gain_ref, mid_ref, low_ref, part_ref):
    gain = gain_ref[...].reshape(1, -1)
    part = jnp.zeros((8, x_ref.shape[1]), single)
    for span in spans(x_ref.shape[0]):
        grad = keep_ref[span, :] + recv_ref[span, :].astype(single)
        back, normal = norm_back(x_ref[span, :], grad, gain)
        total = mix_ref[mix_ref.shape[0] - 1] * cot_ref[span, :] + back
        mid_ref[span, :] = total
        low_ref[span, :] = total.astype(bfloat)
        part = part + fold_rows(grad * normal)
    part_ref[...] = jnp.sum(part, axis=0, keepdims=True)


def first_back_body(x_ref, keep_ref, recv_ref, mid_ref, gain_ref, out_ref):
    gain = gain_ref[...].reshape(1, -1)
    for span in spans(x_ref.shape[0]):
        grad = keep_ref[span, :] + recv_ref[span, :].astype(single)
        back, _ = norm_back(x_ref[span, :].astype(single), grad, gain)
        out_ref[span, :] = (mid_ref[span, :] + back).astype(bfloat)


def history_body(mix_ref, history_ref, cot_ref, grad_ref, mixed_ref, low_ref, part_ref):
    depth = history_ref.shape[0]

    @pl.when(pl.program_id(0) == 0)
    def _():
        part_ref[...] = jnp.zeros_like(part_ref)

    for span in spans(cot_ref.shape[0], 32):
        cot = cot_ref[span, :]
        low_ref[span, :] = (mix_ref[depth] * cot).astype(bfloat)
        mixed = None
        for j in range(depth):
            layer = history_ref[j, span, :].astype(single)
            mixed = mix_ref[j] * layer if mixed is None else mixed + mix_ref[j] * layer
            grad_ref[j, span, :] = (mix_ref[j] * cot).astype(bfloat)
            part_ref[8 * j : 8 * j + 8, :] += fold_rows(layer * cot)
        mixed_ref[span, :] = mixed


def average_history(mix, history, cot, after=()):
    depth, rows, width = history.shape
    step = 96
    waits = len(after)

    def body(*refs):
        history_body(*refs[:3], *refs[3 + waits :])

    row_block = pl.BlockSpec((step, width), lambda i: (i, 0))
    deep_block = pl.BlockSpec((depth, step, width), lambda i: (0, i, 0))
    return pl.pallas_call(
        body,
        grid=(rows // step,),
        out_shape=[
            jax.ShapeDtypeStruct(history.shape, bfloat),
            jax.ShapeDtypeStruct((rows, width), single),
            jax.ShapeDtypeStruct((rows, width), bfloat),
            jax.ShapeDtypeStruct((8 * depth, width), single),
        ],
        in_specs=[pl.BlockSpec(memory_space=pltpu.SMEM), deep_block, row_block]
        + [pl.BlockSpec(memory_space=pl.ANY)] * waits,
        out_specs=[deep_block, row_block, row_block, pl.BlockSpec((8 * depth, width), lambda i: (0, 0))],
        compiler_params=pltpu.CompilerParams(vmem_limit_bytes=16 * MIB),
        cost_estimate=pl.CostEstimate(flops=0, bytes_accessed=0, transcendentals=0),
    )(mix, history, cot, *after)


def combine_body(mix_ref, mixed_ref, mid_ref, keep_ref, recv_ref, cot_ref, parts_ref, out_ref, part_ref):
    depth = mix_ref.shape[0] - 1
    last = jnp.zeros((8, mid_ref.shape[1]), single)
    for span in spans(mid_ref.shape[0]):
        outputs = mid_ref[span, :] + (keep_ref[span, :] + recv_ref[span, :].astype(single))
        out_ref[span, :] = (mixed_ref[span, :] + mix_ref[depth] * outputs).astype(bfloat)
        last = last + fold_rows(outputs * cot_ref[span, :])
    for j in range(depth):
        part_ref[j : j + 1, :] = jnp.sum(parts_ref[8 * j : 8 * j + 8, :], axis=0, keepdims=True)
    part_ref[depth : depth + 1, :] = jnp.sum(last, axis=0, keepdims=True)


def halving_body(upper_ref, mine_ref, come_ref, kept_ref, sent_ref, total):
    size = kept_ref.shape[0]
    total[...] = mine_ref[...] + come_ref[...].astype(single)
    low = pl.multiple_of(upper_ref[0] * size, size)
    high = pl.multiple_of((1 - upper_ref[0]) * size, size)
    kept_ref[...] = total[pl.ds(low, size), :]
    sent_ref[...] = total[pl.ds(high, size), :].astype(bfloat)


def low_body(mine_ref, come_ref, out_ref):
    out_ref[...] = (mine_ref[...].astype(single) + come_ref[...].astype(single)).astype(bfloat)


def order_body(upper_ref, mine_ref, come_ref, out_ref):
    size = mine_ref.shape[0]
    low = pl.multiple_of(upper_ref[0] * size, size)
    high = pl.multiple_of((1 - upper_ref[0]) * size, size)
    out_ref[pl.ds(low, size), :] = mine_ref[...].astype(out_ref.dtype)
    out_ref[pl.ds(high, size), :] = come_ref[...].astype(out_ref.dtype)


BLOCKS = tuple((begin, min(256, SEQ - begin)) for begin in range(0, SEQ, 256))


def place(core_ref, own_ref, peer_ref, whole):
    low = pl.multiple_of(core_ref[0] * HALF, HALF)
    high = pl.multiple_of((1 - core_ref[0]) * HALF, HALF)
    whole[pl.ds(low, HALF), :] = own_ref[...]
    whole[pl.ds(high, HALF), :] = peer_ref[...]
    return low, high


def allowed(size):
    key_pos = lax.broadcasted_iota(jnp.int32, (size, size), 0)
    query_pos = lax.broadcasted_iota(jnp.int32, (size, size), 1)
    return query_pos >= key_pos


def turn(rows, cosine, sine):
    half = rows.shape[0] // 2
    a, b = rows[:half], rows[half:]
    return jnp.concatenate([a * cosine - b * sine, b * cosine + a * sine], axis=0)


def attend(core_ref, own_ref, peer_ref, weight_ref, cos_ref, sin_ref, qkv_ref, att_ref, nat_ref, log_ref, tokens):
    place(core_ref, own_ref, peer_ref, tokens)
    width = weight_ref.shape[0] // 3
    projected = mul(weight_ref[...], tokens[...], 1, 1)
    cosine, sine = cos_ref[...], sin_ref[...]
    for part in range(3):
        for head in range(width // DH):
            begin = part * width + head * DH
            rows = projected[begin : begin + DH]
            if part < 2:
                rows = turn(rows, cosine, sine)
            if part == 0:
                rows = rows * DH ** (-0.5)
            qkv_ref[begin : begin + DH, :] = rows.astype(bfloat)
    log_ref[...] = jnp.zeros_like(log_ref)
    for head in range(width // DH):
        base = head * DH
        keys = qkv_ref[width + base : width + base + DH, :].T
        for begin, size in BLOCKS:
            end = begin + size
            query = qkv_ref[base : base + DH, begin:end]
            scores = mul(keys[:end], query)
            corner = jnp.where(allowed(size), scores[begin:], -jnp.inf)
            top = jnp.max(corner, axis=0, keepdims=True)
            if begin:
                top = jnp.maximum(top, jnp.max(scores[:begin], axis=0, keepdims=True))
                scores = jnp.concatenate([scores[:begin], corner], axis=0)
            else:
                scores = corner
            weights = jnp.exp(scores - top)
            total = jnp.sum(weights, axis=0, keepdims=True)
            value = qkv_ref[2 * width + base : 2 * width + base + DH, :end]
            mixed = mul(value, weights.astype(bfloat)) / total
            att_ref[base : base + DH, begin:end] = mixed.astype(bfloat)
            log_ref[head : head + 1, begin:end] = top + jnp.log(total)
    nat_ref[...] = att_ref[...].T


def branch_body(core_ref, att_a_ref, att_b_ref, out_a_ref, out_b_ref, keep_ref, send_ref):
    low = pl.multiple_of(core_ref[0] * HALF, HALF)
    high = pl.multiple_of((1 - core_ref[0]) * HALF, HALF)
    send = mul(att_a_ref[pl.ds(high, HALF), :], out_a_ref[...])
    send_ref[...] = (send + mul(att_b_ref[pl.ds(high, HALF), :], out_b_ref[...])).astype(bfloat)
    keep = mul(att_a_ref[pl.ds(low, HALF), :], out_a_ref[...])
    keep_ref[...] = keep + mul(att_b_ref[pl.ds(low, HALF), :], out_b_ref[...])


def attend_back(
    second, core_ref, grad_own_ref, grad_peer_ref, own_ref, peer_ref, weight_ref, out_ref, qkv_ref, att_ref,
    log_ref, cos_ref, sin_ref, *rest,
):
    if second:
        before_ref, gain_ref, first_ref, last_ref, keep_ref, send_ref, part_ref, tokens, grads, turned, whole = rest
    else:
        first_ref, last_ref, whole, tokens, grads, turned = rest
    low, high = place(core_ref, own_ref, peer_ref, tokens)
    place(core_ref, grad_own_ref, grad_peer_ref, grads)
    width = out_ref.shape[0]
    out_grad = mul(att_ref[...], grads[...])
    grad_att = mul(out_ref[...], grads[...], 1, 1).astype(bfloat)
    cosine, sine = cos_ref[...], sin_ref[...]
    for head in range(width // DH):
        base = head * DH
        query = qkv_ref[base : base + DH, :]
        key = qkv_ref[width + base : width + base + DH, :]
        value = qkv_ref[2 * width + base : 2 * width + base + DH, :]
        above = grad_att[base : base + DH]
        centre = jnp.sum(
            above.astype(single) * att_ref[base : base + DH, :].astype(single), axis=0, keepdims=True
        )
        keys, values = key.T, value.T
        grad_query, grad_key, grad_value = [], None, None
        for begin, size in reversed(BLOCKS):
            end = begin + size
            scores = mul(keys[:end], query[:, begin:end])
            corner = jnp.where(allowed(size), scores[begin:], -jnp.inf)
            scores = jnp.concatenate([scores[:begin], corner], axis=0) if begin else corner
            probs = jnp.exp(scores - log_ref[head : head + 1, begin:end])
            grad_probs = mul(values[:end], above[:, begin:end])
            grad_scores = (probs * (grad_probs - centre[:, begin:end])).astype(bfloat)
            grad_query.insert(0, mul(key[:, :end], grad_scores))
            key_part = mul(query[:, begin:end], grad_scores, 1, 1)
            value_part = mul(above[:, begin:end], probs.astype(bfloat), 1, 1)
            if grad_key is None:
                grad_key, grad_value = key_part, value_part
            else:
                grad_key = jnp.concatenate([grad_key[:, :end] + key_part, grad_key[:, end:]], axis=1)
                grad_value = jnp.concatenate([grad_value[:, :end] + value_part, grad_value[:, end:]], axis=1)
        grad_query = jnp.concatenate(grad_query, axis=1) * DH ** (-0.5)
        turned[base : base + DH, :] = turn(grad_query, cosine, -sine).astype(bfloat)
        turned[width + base : width + base + DH, :] = turn(grad_key, cosine, -sine).astype(bfloat)
        turned[2 * width + base : 2 * width + base + DH, :] = grad_value.astype(bfloat)
    first_ref[...] = mul(turned[: 2 * width, :], tokens[...]).astype(first_ref.dtype)
    last_ref[:width, :] = mul(turned[2 * width :, :], tokens[...]).astype(last_ref.dtype)
    last_ref[width:, :] = out_grad.astype(last_ref.dtype)
    result = mul(turned[...], weight_ref[...], 0, 0)
    if second:
        whole[...] = before_ref[...] + result
        keep_ref[...] = whole[pl.ds(low, HALF), :]
        send_ref[...] = whole[pl.ds(high, HALF), :].astype(bfloat)
        part_ref[...] = (
            jnp.sum(whole[...] * tokens[...].astype(single), axis=0, keepdims=True) / gain_ref[...].reshape(1, -1)
        )
    else:
        whole[...] = result


CURVE = float(np.sqrt(2.0 / np.pi))
STEP = 256


def mlp_body(second, x_own_ref, x_peer_ref, g_own_ref, g_peer_ref, up_ref, down_ref, *rest):
    if second:
        keep_out_a, keep_norm_a, send_out_a, send_norm_a = rest[:4]
        rest = rest[4:]
    keep_out_ref, send_out_ref, keep_norm_ref, send_norm_ref = rest[:4]
    grad_refs = rest[4:8]
    x_all, g_all, x_turned, active, grad_hidden = rest[8:]
    rows = x_own_ref.shape[0]
    hidden_units = down_ref.shape[0]
    x_all[:rows, :] = x_own_ref[...]
    x_all[rows:, :] = x_peer_ref[...]
    g_all[:rows, :] = g_own_ref[...]
    g_all[rows:, :] = g_peer_ref[...]
    x_turned[...] = x_all[...].T
    for begin in range(0, hidden_units, STEP):
        columns = slice(begin, begin + STEP)
        for top in range(0, 2 * rows, rows):
            span = slice(top, top + rows)
            v = mul(x_all[span, :], up_ref[:, columns])
            grad = mul(g_all[span, :], down_ref[columns, :], 1, 1)
            square = v * v
            half = 0.5 + 0.5 * jnp.tanh(v * (CURVE + (CURVE * 0.044715) * square))
            act = v * half
            slope = half + act * (1.0 - half) * (2.0 * CURVE + (6.0 * CURVE * 0.044715) * square)
            active[span, columns] = act.astype(bfloat)
            grad_hidden[span, columns] = (grad * slope).astype(bfloat)
    out_own = mul(active[:rows, :], down_ref[...])
    out_peer = mul(active[rows:, :], down_ref[...])
    norm_own = mul(grad_hidden[:rows, :], up_ref[...], 1, 1)
    norm_peer = mul(grad_hidden[rows:, :], up_ref[...], 1, 1)
    if second:
        out_own = out_own + keep_out_a[...]
        out_peer = out_peer + send_out_a[...].astype(single)
        norm_own = norm_own + keep_norm_a[...]
        norm_peer = norm_peer + send_norm_a[...].astype(single)
    keep_out_ref[...] = out_own
    send_out_ref[...] = out_peer.astype(bfloat)
    keep_norm_ref[...] = norm_own
    send_norm_ref[...] = norm_peer.astype(bfloat)
    size = hidden_units // 2
    for index in range(2):
        columns = slice(index * size, (index + 1) * size)
        down_part = mul(active[:, columns], g_all[...], 0, 0)
        grad_refs[index][...] = down_part.astype(grad_refs[index].dtype)
        up_part = mul(x_turned[columns, :], grad_hidden[...])
        grad_refs[2 + index][...] = up_part.astype(grad_refs[2 + index].dtype)


def mlp(x_own, x_peer, g_own, g_peer, up, down, before=(), after=()):
    rows, width = x_own.shape
    units = down.shape[0]
    kind = single if before else bfloat
    outs = [((rows, width), single), ((rows, width), bfloat)] * 2 + [((units // 2, width), kind)] * 4
    scratch = [
        pltpu.VMEM((2 * rows, width), bfloat),
        pltpu.VMEM((2 * rows, width), bfloat),
        pltpu.VMEM((width, 2 * rows), bfloat),
        pltpu.VMEM((2 * rows, units), bfloat),
        pltpu.VMEM((2 * rows, units), bfloat),
    ]
    operands = (x_own, x_peer, g_own, g_peer, up, down) + tuple(before)
    return call(functools.partial(mlp_body, bool(before)), outs, operands, scratch, after=after, vmem=48)


def shards(
    inputs,
    history,
    cotangent,
    qkv_weight,
    out_weight,
    up_weight,
    down_weight,
    gain_attn,
    gain_mlp,
    dwa_weights,
):
    rows, width = inputs.shape
    members = lax.axis_size("mp")
    copies = lax.axis_size("dp")
    bits = copies.bit_length() - 1
    core = lax.rem(lax.axis_index("mp"), 2).astype(jnp.int32).reshape(1)
    copy_index = lax.axis_index("dp").astype(jnp.int32).reshape(1)
    core_pairs = [(i, i ^ 1) for i in range(members)]
    chip_pairs = [(i, i ^ 2) for i in range(members)]
    depth = history.shape[0]
    part = out_weight.shape[0]

    def other_core(value):
        return lax.ppermute(value, "mp", core_pairs)

    def other_chip(value):
        return lax.ppermute(value, "mp", chip_pairs)

    def other_copy(value, bit):
        return lax.ppermute(value, "dp", [(i, i ^ (1 << bit)) for i in range(copies)])

    uppers = [(copy_index >> bit) & 1 for bit in range(bits)]
    cosine, sine = (jnp.asarray(table) for table in tables())

    qkv_own = qkv_weight.transpose(1, 2, 0).reshape(3 * part, width)
    share = width // copies
    up_share = other_chip(lax.dynamic_slice_in_dim(up_weight, copy_index[0] * share, share, 0))
    up_peer = lax.all_gather(up_share, "dp", axis=0, tiled=True)
    qkv_peer = other_chip(qkv_own)
    out_peer = other_chip(out_weight)
    down_peer = other_chip(down_weight)

    full = (rows, width)
    (x_own,) = call(norm_body, [(full, bfloat)], (inputs, gain_attn))
    x_peer = other_core(x_own)
    history_grad, mixed, g_own, history_parts = average_history(dwa_weights, history, cotangent, (x_own,))
    g_peer = other_core(g_own)

    tokens = pltpu.VMEM((SEQ, width), bfloat)
    first_outs = [
        ((3 * part, SEQ), bfloat), ((part, SEQ), bfloat), ((SEQ, part), bfloat), ((8, SEQ), single),
    ]
    qkv_a, att_a, nat_a, log_a = call(
        attend, first_outs, (core, x_own, x_peer, qkv_own, cosine, sine), [tokens], 1, (history_parts,), 32
    )
    qkv_b, att_b, nat_b, log_b = call(
        attend, first_outs, (core, x_own, x_peer, qkv_peer, cosine, sine), [tokens], 1, (log_a,), 32
    )
    keep, send = call(
        branch_body,
        [(full, single), (full, bfloat)],
        (core, nat_a, nat_b, out_weight, out_peer),
        scalars=1,
    )
    middle, y_own = call(
        middle_body, [(full, single), (full, bfloat)], (inputs, keep, other_core(send), gain_mlp)
    )
    y_peer = other_core(y_own)

    first = mlp(y_own, y_peer, g_own, g_peer, up_peer, down_peer)
    theirs = [other_chip(value) for value in first[4:]]
    second = mlp(
        y_own, y_peer, g_own, g_peer, up_weight, down_weight, (first[0], first[2], first[1], first[3])
    )
    keep_out, send_out, keep_norm, send_norm = second[:4]
    mine = second[4:]
    grad_middle, gb_own, gain_mlp_part = call(
        middle_back_body,
        [(full, single), (full, bfloat), ((1, width), single)],
        (dwa_weights, middle, keep_norm, other_core(send_norm), cotangent, gain_mlp),
        scalars=1,
    )
    gb_peer = other_core(gb_own)
    combined, dwa_part = call(
        combine_body,
        [(full, bfloat), ((depth + 1, width), single)],
        (dwa_weights, mixed, middle, keep_out, other_core(send_out), cotangent, history_parts),
        scalars=1,
        after=(gain_mlp_part,),
    )

    quarter = mine[0].shape[0]

    def sum_two(mine_a, come_a, mine_b, come_b, after):
        def body(mine_a_ref, come_a_ref, mine_b_ref, come_b_ref, out_ref):
            out_ref[:quarter, :] = (mine_a_ref[...] + come_a_ref[...].astype(single)).astype(bfloat)
            out_ref[quarter:, :] = (mine_b_ref[...] + come_b_ref[...].astype(single)).astype(bfloat)

        (total,) = call(
            body, [((2 * quarter, width), bfloat)], (mine_a, come_a, mine_b, come_b), after=after
        )
        return total

    back_scratch = [tokens, tokens, pltpu.VMEM((3 * part, SEQ), bfloat)]
    first_back = call(
        functools.partial(attend_back, False),
        [((2 * part, width), bfloat)] * 2 + [((SEQ, width), single)],
        (core, gb_own, gb_peer, x_own, x_peer, qkv_peer, out_peer, qkv_b, att_b, log_b, cosine, sine),
        back_scratch,
        1,
        (dwa_part,),
        40,
    )
    theirs += [other_chip(value) for value in first_back[:2]]
    down_low = sum_two(mine[0], theirs[0], mine[1], theirs[1], (first_back[2],))
    down_grad = lax.psum(down_low, "dp").astype(single)
    second_back = call(
        functools.partial(attend_back, True),
        [((2 * part, width), single)] * 2
        + [(full, single), (full, bfloat), ((1, width), single)],
        (
            core, gb_own, gb_peer, x_own, x_peer, qkv_own, out_weight, qkv_a, att_a, log_a, cosine, sine,
            first_back[2], gain_attn,
        ),
        back_scratch + [pltpu.VMEM((SEQ, width), single)],
        1,
        (down_low,),
        40,
    )
    mine = list(mine) + list(second_back[:2])
    keep_first, send_first, gain_attn_part = second_back[2:]
    small = jnp.concatenate([gain_attn_part, gain_mlp_part, dwa_part], axis=0)
    small = small + other_core(small)
    small = small + other_chip(small)
    for bit in range(bits):
        small = small + other_copy(small, bit)

    token = [gain_attn_part]

    def chain(index):
        value, come = mine[index], theirs[index]
        for bit in range(halvings):
            size = value.shape[0] // 2
            value, sent = call(
                halving_body,
                [((size, width), single), ((size, width), bfloat)],
                (uppers[bit], value, come),
                [pltpu.VMEM(value.shape, single)],
                1,
                tuple(token),
            )
            token[0] = value
            come = other_copy(sent, bit)
            yield
        for bit in range(halvings, bits):
            (value,) = call(low_body, [(value.shape, bfloat)], (value, come), after=tuple(token))
            token[0] = value
            come = other_copy(value, bit)
            yield
        (value,) = call(low_body, [(value.shape, bfloat)], (value, come), after=tuple(token))
        token[0] = value
        for bit in reversed(range(halvings)):
            come = other_copy(value, bit)
            yield
            kind = bfloat if bit else single
            (value,) = call(
                order_body,
                [((2 * value.shape[0], width), kind)],
                (uppers[bit], value, come),
                scalars=1,
                after=tuple(token),
            )
            token[0] = value
        results[index] = value

    halvings = min(2, bits - 1)
    results = {}
    chains = {index: chain(index) for index in range(2, 6)}

    def advance(*order):
        for index in order:
            next(chains[index], None)

    advance(2, 3)
    (input_grad,) = call(
        first_back_body,
        [(full, bfloat)],
        (inputs, keep_first, other_core(send_first), grad_middle, gain_attn),
        after=tuple(token),
    )
    token[0] = input_grad
    advance(2, 4, 3, 2, 4, 3, 2, 4, 3, 5, 2, 4, 3, 5, 2, 4, 5, 3, 4, 5, 4, 5)
    for index in range(2, 6):
        for _ in range(2 * bits + 2):
            advance(index)
    up_grad = jnp.concatenate([results[2], results[3]], axis=0)

    return (
        combined,
        input_grad,
        history_grad,
        jnp.concatenate([results[4], results[5][:part]], axis=0).reshape(3, part, width).transpose(2, 0, 1),
        results[5][part:],
        up_grad,
        down_grad,
        small[0],
        small[1],
        jnp.sum(small[2:], axis=1),
    )


def solution(mesh):
    placed = (
        P(("dp", "mp"), None),
        P(None, ("dp", "mp"), None),
        P(("dp", "mp"), None),
        P(None, None, "mp"),
        P("mp", None),
        P(None, "mp"),
        P("mp", None),
        P(),
        P(),
        P(),
    )
    return jax.shard_map(
        shards,
        mesh=mesh,
        in_specs=placed,
        out_specs=(
            P(("dp", "mp"), None),
            P(("dp", "mp"), None),
            P(None, ("dp", "mp"), None),
            P(None, None, "mp"),
            P("mp", None),
            P(None, "mp"),
            P("mp", None),
            P(),
            P(),
            P(),
        ),
        check_vma=False,
    )
```

```python
import functools

import jax
import jax.numpy as jnp
import numpy as np
from jax import lax
from jax.experimental import pallas as pl
from jax.experimental.pallas import tpu as pltpu
from jax.sharding import PartitionSpec as P

DH = 64
SEQ = 1152
HALF = SEQ // 2
EPS = 1e-05
bfloat = jnp.bfloat16
single = jnp.float32
MIB = 1 << 20


def tables():
    half_width = DH // 2
    places = np.arange(SEQ, dtype=np.float32)
    frequency = np.float32(10000.0) ** (-np.arange(half_width, dtype=np.float32) * np.float32(2.0 / DH))
    angles = frequency[:, None] * places[None, :]
    return (np.cos(angles).astype(np.float32), np.sin(angles).astype(np.float32))


def mul(a, b, ca=1, cb=0):
    return lax.dot_general(a, b, (((ca,), (cb,)), ((), ())), preferred_element_type=single)


def call(kernel, outs, operands, scratch=(), scalars=0, after=(), vmem=16):
    count, waits = len(operands), len(after)

    def body(*refs):
        kernel(*refs[:count], *refs[count + waits :])

    small = pl.BlockSpec(memory_space=pltpu.SMEM)
    whole = pl.BlockSpec(memory_space=pltpu.VMEM)
    apart = pl.BlockSpec(memory_space=pl.ANY)
    return pl.pallas_call(
        body,
        out_shape=[jax.ShapeDtypeStruct(shape, kind) for shape, kind in outs],
        in_specs=[small] * scalars + [whole] * (count - scalars) + [apart] * waits,
        out_specs=[whole] * len(outs),
        scratch_shapes=list(scratch),
        compiler_params=pltpu.CompilerParams(vmem_limit_bytes=vmem * MIB),
        cost_estimate=pl.CostEstimate(flops=0, bytes_accessed=0, transcendentals=0),
    )(*operands, *after)


ROWS = 64


def spans(rows, step=ROWS):
    return [slice(begin, begin + step) for begin in range(0, rows, step)]


def normal_of(x):
    centre = x - jnp.mean(x, axis=-1, keepdims=True)
    spread = jnp.mean(centre * centre, axis=-1, keepdims=True)
    scale = lax.rsqrt(spread + EPS)
    return centre * scale, scale


def norm_body(x_ref, gain_ref, out_ref):
    gain = gain_ref[...].reshape(1, -1)
    for span in spans(x_ref.shape[0]):
        normal, _ = normal_of(x_ref[span, :].astype(single))
        out_ref[span, :] = (normal * gain).astype(bfloat)


def middle_body(x_ref, keep_ref, recv_ref, gain_ref, mid_ref, out_ref):
    gain = gain_ref[...].reshape(1, -1)
    for span in spans(x_ref.shape[0]):
        x = x_ref[span, :].astype(single) + (keep_ref[span, :] + recv_ref[span, :].astype(single))
        mid_ref[span, :] = x
        normal, _ = normal_of(x)
        out_ref[span, :] = (normal * gain).astype(bfloat)


def norm_back(x, grad, gain):
    normal, scale = normal_of(x)
    lifted = grad * gain
    back = scale * (
        lifted
        - jnp.mean(lifted, axis=-1, keepdims=True)
        - normal * jnp.mean(lifted * normal, axis=-1, keepdims=True)
    )
    return back, normal


def fold_rows(value):
    total = value[:8]
    for begin in range(8, value.shape[0], 8):
        total = total + value[begin : begin + 8]
    return total


def middle_back_body(mix_ref, x_ref, keep_ref, recv_ref, cot_ref, gain_ref, mid_ref, low_ref, part_ref):
    gain = gain_ref[...].reshape(1, -1)
    part = jnp.zeros((8, x_ref.shape[1]), single)
    for span in spans(x_ref.shape[0]):
        grad = keep_ref[span, :] + recv_ref[span, :].astype(single)
        back, normal = norm_back(x_ref[span, :], grad, gain)
        total = mix_ref[mix_ref.shape[0] - 1] * cot_ref[span, :] + back
        mid_ref[span, :] = total
        low_ref[span, :] = total.astype(bfloat)
        part = part + fold_rows(grad * normal)
    part_ref[...] = jnp.sum(part, axis=0, keepdims=True)


def first_back_body(x_ref, keep_ref, recv_ref, mid_ref, gain_ref, out_ref):
    gain = gain_ref[...].reshape(1, -1)
    for span in spans(x_ref.shape[0]):
        grad = keep_ref[span, :] + recv_ref[span, :].astype(single)
        back, _ = norm_back(x_ref[span, :].astype(single), grad, gain)
        out_ref[span, :] = (mid_ref[span, :] + back).astype(bfloat)


def history_body(mix_ref, history_ref, cot_ref, grad_ref, mixed_ref, low_ref, part_ref):
    depth = history_ref.shape[0]

    @pl.when(pl.program_id(0) == 0)
    def _():
        part_ref[...] = jnp.zeros_like(part_ref)

    for span in spans(cot_ref.shape[0], 32):
        cot = cot_ref[span, :]
        low_ref[span, :] = (mix_ref[depth] * cot).astype(bfloat)
        mixed = None
        for j in range(depth):
            layer = history_ref[j, span, :].astype(single)
            mixed = mix_ref[j] * layer if mixed is None else mixed + mix_ref[j] * layer
            grad_ref[j, span, :] = (mix_ref[j] * cot).astype(bfloat)
            part_ref[8 * j : 8 * j + 8, :] += fold_rows(layer * cot)
        mixed_ref[span, :] = mixed


def average_history(mix, history, cot, after=()):
    depth, rows, width = history.shape
    step = 96
    waits = len(after)

    def body(*refs):
        history_body(*refs[:3], *refs[3 + waits :])

    row_block = pl.BlockSpec((step, width), lambda i: (i, 0))
    deep_block = pl.BlockSpec((depth, step, width), lambda i: (0, i, 0))
    return pl.pallas_call(
        body,
        grid=(rows // step,),
        out_shape=[
            jax.ShapeDtypeStruct(history.shape, bfloat),
            jax.ShapeDtypeStruct((rows, width), single),
            jax.ShapeDtypeStruct((rows, width), bfloat),
            jax.ShapeDtypeStruct((8 * depth, width), single),
        ],
        in_specs=[pl.BlockSpec(memory_space=pltpu.SMEM), deep_block, row_block]
        + [pl.BlockSpec(memory_space=pl.ANY)] * waits,
        out_specs=[deep_block, row_block, row_block, pl.BlockSpec((8 * depth, width), lambda i: (0, 0))],
        compiler_params=pltpu.CompilerParams(vmem_limit_bytes=16 * MIB),
        cost_estimate=pl.CostEstimate(flops=0, bytes_accessed=0, transcendentals=0),
    )(mix, history, cot, *after)


def combine_body(mix_ref, mixed_ref, mid_ref, keep_ref, recv_ref, cot_ref, parts_ref, out_ref, part_ref):
    depth = mix_ref.shape[0] - 1
    last = jnp.zeros((8, mid_ref.shape[1]), single)
    for span in spans(mid_ref.shape[0]):
        outputs = mid_ref[span, :] + (keep_ref[span, :] + recv_ref[span, :].astype(single))
        out_ref[span, :] = (mixed_ref[span, :] + mix_ref[depth] * outputs).astype(bfloat)
        last = last + fold_rows(outputs * cot_ref[span, :])
    for j in range(depth):
        part_ref[j : j + 1, :] = jnp.sum(parts_ref[8 * j : 8 * j + 8, :], axis=0, keepdims=True)
    part_ref[depth : depth + 1, :] = jnp.sum(last, axis=0, keepdims=True)


def part_rows(upper_ref, size):
    low = pl.multiple_of(upper_ref[0] * size, size)
    high = pl.multiple_of((1 - upper_ref[0]) * size, size)
    return pl.ds(low, size), pl.ds(high, size)


def halve_body(upper_ref, mine_ref, come_ref, kept_ref, sent_ref):
    low, high = part_rows(upper_ref, kept_ref.shape[0])
    kept_ref[...] = mine_ref[low, :] + come_ref[low, :].astype(single)
    sent_ref[...] = (mine_ref[high, :] + come_ref[high, :].astype(single)).astype(bfloat)


def part_body(upper_ref, mine_ref, theirs_ref, kept_ref, sent_ref):
    size = mine_ref.shape[0] // 2
    low, high = part_rows(upper_ref, size)
    kept_ref[:size, :] = mine_ref[low, :]
    kept_ref[size:, :] = theirs_ref[low, :].astype(single)
    sent_ref[:size, :] = mine_ref[high, :].astype(bfloat)
    sent_ref[size:, :] = theirs_ref[high, :]


def cross_body(kept_ref, come_ref, mine_ref, theirs_ref):
    size = mine_ref.shape[0]
    mine_ref[...] = kept_ref[:size, :] + come_ref[:size, :].astype(single)
    theirs_ref[...] = (kept_ref[size:, :] + come_ref[size:, :].astype(single)).astype(bfloat)


def low_body(mine_ref, come_ref, out_ref):
    out_ref[...] = (mine_ref[...].astype(single) + come_ref[...].astype(single)).astype(bfloat)


def order_body(upper_ref, mine_ref, come_ref, out_ref):
    low, high = part_rows(upper_ref, mine_ref.shape[0])
    out_ref[low, :] = mine_ref[...].astype(out_ref.dtype)
    out_ref[high, :] = come_ref[...].astype(out_ref.dtype)


def order_two_body(upper_ref, mine_a_ref, come_a_ref, mine_b_ref, come_b_ref, top_ref, end_ref, hold):
    size = mine_a_ref.shape[0]
    low, high = part_rows(upper_ref, size)
    rest = top_ref.shape[0] - 2 * size
    hold[low, :] = mine_a_ref[...].astype(single)
    hold[high, :] = come_a_ref[...].astype(single)
    top_ref[: 2 * size, :] = hold[...]
    hold[low, :] = mine_b_ref[...].astype(single)
    hold[high, :] = come_b_ref[...].astype(single)
    top_ref[2 * size :, :] = hold[:rest, :]
    end_ref[...] = hold[rest:, :]


BLOCKS = tuple((begin, min(256, SEQ - begin)) for begin in range(0, SEQ, 256))


def place(core_ref, own_ref, peer_ref, whole):
    low = pl.multiple_of(core_ref[0] * HALF, HALF)
    high = pl.multiple_of((1 - core_ref[0]) * HALF, HALF)
    whole[pl.ds(low, HALF), :] = own_ref[...]
    whole[pl.ds(high, HALF), :] = peer_ref[...]
    return low, high


def allowed(size):
    key_pos = lax.broadcasted_iota(jnp.int32, (size, size), 0)
    query_pos = lax.broadcasted_iota(jnp.int32, (size, size), 1)
    return query_pos >= key_pos


def turn(rows, cosine, sine):
    half = rows.shape[0] // 2
    a, b = rows[:half], rows[half:]
    return jnp.concatenate([a * cosine - b * sine, b * cosine + a * sine], axis=0)


def attend(core_ref, own_ref, peer_ref, weight_ref, cos_ref, sin_ref, qkv_ref, att_ref, nat_ref, log_ref, tokens):
    place(core_ref, own_ref, peer_ref, tokens)
    width = weight_ref.shape[0] // 3
    projected = mul(weight_ref[...], tokens[...], 1, 1)
    cosine, sine = cos_ref[...], sin_ref[...]
    for part in range(3):
        for head in range(width // DH):
            begin = part * width + head * DH
            rows = projected[begin : begin + DH]
            if part < 2:
                rows = turn(rows, cosine, sine)
            if part == 0:
                rows = rows * DH ** (-0.5)
            qkv_ref[begin : begin + DH, :] = rows.astype(bfloat)
    log_ref[...] = jnp.zeros_like(log_ref)
    for head in range(width // DH):
        base = head * DH
        keys = qkv_ref[width + base : width + base + DH, :].T
        for begin, size in BLOCKS:
            end = begin + size
            query = qkv_ref[base : base + DH, begin:end]
            scores = mul(keys[:end], query)
            corner = jnp.where(allowed(size), scores[begin:], -jnp.inf)
            top = jnp.max(corner, axis=0, keepdims=True)
            if begin:
                top = jnp.maximum(top, jnp.max(scores[:begin], axis=0, keepdims=True))
                scores = jnp.concatenate([scores[:begin], corner], axis=0)
            else:
                scores = corner
            weights = jnp.exp(scores - top)
            total = jnp.sum(weights, axis=0, keepdims=True)
            value = qkv_ref[2 * width + base : 2 * width + base + DH, :end]
            mixed = mul(value, weights.astype(bfloat)) / total
            att_ref[base : base + DH, begin:end] = mixed.astype(bfloat)
            log_ref[head : head + 1, begin:end] = top + jnp.log(total)
    nat_ref[...] = att_ref[...].T


def branch_body(core_ref, att_a_ref, att_b_ref, out_a_ref, out_b_ref, keep_ref, send_ref):
    low = pl.multiple_of(core_ref[0] * HALF, HALF)
    high = pl.multiple_of((1 - core_ref[0]) * HALF, HALF)
    send = mul(att_a_ref[pl.ds(high, HALF), :], out_a_ref[...])
    send_ref[...] = (send + mul(att_b_ref[pl.ds(high, HALF), :], out_b_ref[...])).astype(bfloat)
    keep = mul(att_a_ref[pl.ds(low, HALF), :], out_a_ref[...])
    keep_ref[...] = keep + mul(att_b_ref[pl.ds(low, HALF), :], out_b_ref[...])


def attend_back(
    second, core_ref, grad_own_ref, grad_peer_ref, own_ref, peer_ref, weight_ref, out_ref, qkv_ref, att_ref,
    log_ref, cos_ref, sin_ref, *rest,
):
    if second:
        before_ref, gain_ref, first_ref, last_ref, keep_ref, send_ref, part_ref, tokens, grads, turned, whole = rest
    else:
        first_ref, last_ref, whole, tokens, grads, turned = rest
    low, high = place(core_ref, own_ref, peer_ref, tokens)
    place(core_ref, grad_own_ref, grad_peer_ref, grads)
    width = out_ref.shape[0]
    out_grad = mul(att_ref[...], grads[...])
    grad_att = mul(out_ref[...], grads[...], 1, 1).astype(bfloat)
    cosine, sine = cos_ref[...], sin_ref[...]
    for head in range(width // DH):
        base = head * DH
        query = qkv_ref[base : base + DH, :]
        key = qkv_ref[width + base : width + base + DH, :]
        value = qkv_ref[2 * width + base : 2 * width + base + DH, :]
        above = grad_att[base : base + DH]
        centre = jnp.sum(
            above.astype(single) * att_ref[base : base + DH, :].astype(single), axis=0, keepdims=True
        )
        keys, values = key.T, value.T
        grad_query, grad_key, grad_value = [], None, None
        for begin, size in reversed(BLOCKS):
            end = begin + size
            scores = mul(keys[:end], query[:, begin:end])
            corner = jnp.where(allowed(size), scores[begin:], -jnp.inf)
            scores = jnp.concatenate([scores[:begin], corner], axis=0) if begin else corner
            probs = jnp.exp(scores - log_ref[head : head + 1, begin:end])
            grad_probs = mul(values[:end], above[:, begin:end])
            grad_scores = (probs * (grad_probs - centre[:, begin:end])).astype(bfloat)
            grad_query.insert(0, mul(key[:, :end], grad_scores))
            key_part = mul(query[:, begin:end], grad_scores, 1, 1)
            value_part = mul(above[:, begin:end], probs.astype(bfloat), 1, 1)
            if grad_key is None:
                grad_key, grad_value = key_part, value_part
            else:
                grad_key = jnp.concatenate([grad_key[:, :end] + key_part, grad_key[:, end:]], axis=1)
                grad_value = jnp.concatenate([grad_value[:, :end] + value_part, grad_value[:, end:]], axis=1)
        grad_query = jnp.concatenate(grad_query, axis=1) * DH ** (-0.5)
        turned[base : base + DH, :] = turn(grad_query, cosine, -sine).astype(bfloat)
        turned[width + base : width + base + DH, :] = turn(grad_key, cosine, -sine).astype(bfloat)
        turned[2 * width + base : 2 * width + base + DH, :] = grad_value.astype(bfloat)
    first_ref[...] = mul(turned[: 2 * width, :], tokens[...]).astype(first_ref.dtype)
    last_ref[:width, :] = mul(turned[2 * width :, :], tokens[...]).astype(last_ref.dtype)
    last_ref[width:, :] = out_grad.astype(last_ref.dtype)
    result = mul(turned[...], weight_ref[...], 0, 0)
    if second:
        whole[...] = before_ref[...] + result
        keep_ref[...] = whole[pl.ds(low, HALF), :]
        send_ref[...] = whole[pl.ds(high, HALF), :].astype(bfloat)
        part_ref[...] = (
            jnp.sum(whole[...] * tokens[...].astype(single), axis=0, keepdims=True) / gain_ref[...].reshape(1, -1)
        )
    else:
        whole[...] = result


CURVE = float(np.sqrt(2.0 / np.pi))
STEP = 256


def mlp_body(second, x_own_ref, x_peer_ref, g_own_ref, g_peer_ref, up_ref, down_ref, *rest):
    if second:
        keep_out_a, keep_norm_a, send_out_a, send_norm_a = rest[:4]
        rest = rest[4:]
    keep_out_ref, send_out_ref, keep_norm_ref, send_norm_ref = rest[:4]
    down_grad_ref, up_grad_ref, x_all, g_all, x_turned, active, grad_hidden = rest[4:]
    rows = x_own_ref.shape[0]
    hidden_units = down_ref.shape[0]
    x_all[:rows, :] = x_own_ref[...]
    x_all[rows:, :] = x_peer_ref[...]
    g_all[:rows, :] = g_own_ref[...]
    g_all[rows:, :] = g_peer_ref[...]
    x_turned[...] = x_all[...].T
    for begin in range(0, hidden_units, STEP):
        columns = slice(begin, begin + STEP)
        for top in range(0, 2 * rows, rows):
            span = slice(top, top + rows)
            v = mul(x_all[span, :], up_ref[:, columns])
            grad = mul(g_all[span, :], down_ref[columns, :], 1, 1)
            square = v * v
            half = 0.5 + 0.5 * jnp.tanh(v * (CURVE + (CURVE * 0.044715) * square))
            act = v * half
            slope = half + act * (1.0 - half) * (2.0 * CURVE + (6.0 * CURVE * 0.044715) * square)
            active[span, columns] = act.astype(bfloat)
            grad_hidden[span, columns] = (grad * slope).astype(bfloat)
    out_own = mul(active[:rows, :], down_ref[...])
    out_peer = mul(active[rows:, :], down_ref[...])
    norm_own = mul(grad_hidden[:rows, :], up_ref[...], 1, 1)
    norm_peer = mul(grad_hidden[rows:, :], up_ref[...], 1, 1)
    if second:
        out_own = out_own + keep_out_a[...]
        out_peer = out_peer + send_out_a[...].astype(single)
        norm_own = norm_own + keep_norm_a[...]
        norm_peer = norm_peer + send_norm_a[...].astype(single)
    keep_out_ref[...] = out_own
    send_out_ref[...] = out_peer.astype(bfloat)
    keep_norm_ref[...] = norm_own
    send_norm_ref[...] = norm_peer.astype(bfloat)
    size = hidden_units // 2
    for begin in range(0, hidden_units, size):
        columns = slice(begin, begin + size)
        down_grad_ref[columns, :] = mul(active[:, columns], g_all[...], 0, 0).astype(down_grad_ref.dtype)
        up_grad_ref[columns, :] = mul(x_turned[columns, :], grad_hidden[...]).astype(up_grad_ref.dtype)


def mlp(x_own, x_peer, g_own, g_peer, up, down, before=(), after=()):
    rows, width = x_own.shape
    units = down.shape[0]
    kind = bfloat if before else single
    outs = [((rows, width), single), ((rows, width), bfloat)] * 2 + [((units, width), kind), ((width, units), kind)]
    scratch = [
        pltpu.VMEM((2 * rows, width), bfloat),
        pltpu.VMEM((2 * rows, width), bfloat),
        pltpu.VMEM((width, 2 * rows), bfloat),
        pltpu.VMEM((2 * rows, units), bfloat),
        pltpu.VMEM((2 * rows, units), bfloat),
    ]
    operands = (x_own, x_peer, g_own, g_peer, up, down) + tuple(before)
    return call(functools.partial(mlp_body, bool(before)), outs, operands, scratch, after=after, vmem=60)


def shards(
    inputs,
    history,
    cotangent,
    qkv_weight,
    out_weight,
    up_weight,
    down_weight,
    gain_attn,
    gain_mlp,
    dwa_weights,
):
    rows, width = inputs.shape
    members = lax.axis_size("mp")
    copies = lax.axis_size("dp")
    bits = copies.bit_length() - 1
    core = lax.rem(lax.axis_index("mp"), 2).astype(jnp.int32).reshape(1)
    copy_index = lax.axis_index("dp").astype(jnp.int32).reshape(1)
    core_pairs = [(i, i ^ 1) for i in range(members)]
    chip_pairs = [(i, i ^ 2) for i in range(members)]
    depth = history.shape[0]
    part = out_weight.shape[0]

    def other_core(value):
        return lax.ppermute(value, "mp", core_pairs)

    def other_chip(value):
        return lax.ppermute(value, "mp", chip_pairs)

    def other_copy(value, bit):
        return lax.ppermute(value, "dp", [(i, i ^ (1 << bit)) for i in range(copies)])

    uppers = [(copy_index >> bit) & 1 for bit in range(bits)]
    cosine, sine = (jnp.asarray(table) for table in tables())

    qkv_own = qkv_weight.transpose(1, 2, 0).reshape(3 * part, width)
    share = width // copies
    up_share = other_chip(lax.dynamic_slice_in_dim(up_weight, copy_index[0] * share, share, 0))
    up_peer = lax.all_gather(up_share, "dp", axis=0, tiled=True)
    qkv_peer = other_chip(qkv_own)
    out_peer = other_chip(out_weight)
    down_peer = other_chip(down_weight)

    full = (rows, width)
    (x_own,) = call(norm_body, [(full, bfloat)], (inputs, gain_attn))
    x_peer = other_core(x_own)
    history_grad, mixed, g_own, history_parts = average_history(dwa_weights, history, cotangent, (x_own,))
    g_peer = other_core(g_own)

    tokens = pltpu.VMEM((SEQ, width), bfloat)
    first_outs = [
        ((3 * part, SEQ), bfloat), ((part, SEQ), bfloat), ((SEQ, part), bfloat), ((8, SEQ), single),
    ]
    qkv_a, att_a, nat_a, log_a = call(
        attend, first_outs, (core, x_own, x_peer, qkv_own, cosine, sine), [tokens], 1, (history_parts,), 32
    )
    qkv_b, att_b, nat_b, log_b = call(
        attend, first_outs, (core, x_own, x_peer, qkv_peer, cosine, sine), [tokens], 1, (log_a,), 32
    )
    keep, send = call(
        branch_body,
        [(full, single), (full, bfloat)],
        (core, nat_a, nat_b, out_weight, out_peer),
        scalars=1,
    )
    middle, y_own = call(
        middle_body, [(full, single), (full, bfloat)], (inputs, keep, other_core(send), gain_mlp)
    )
    y_peer = other_core(y_own)

    first = mlp(y_own, y_peer, g_own, g_peer, up_weight, down_weight)
    second = mlp(
        y_own, y_peer, g_own, g_peer, up_peer, down_peer, (first[0], first[2], first[1], first[3])
    )
    keep_out, send_out, keep_norm, send_norm, down_theirs, up_theirs = second
    down_mine, up_mine = first[4:]
    half = (width // 2, width)

    token = [keep_norm]

    def step(body, outs, operands, scalars=0, scratch=(), vmem=16):
        results = call(body, outs, operands, scratch, scalars, tuple(token), vmem)
        token[0] = results[0]
        return results

    def halve(bit, mine, come):
        shape = (mine.shape[0] // 2, width)
        return step(halve_body, [(shape, single), (shape, bfloat)], (uppers[bit], mine, come), 1)

    def low(mine, come):
        return step(low_body, [(mine.shape, bfloat)], (mine, come))[0]

    def order(bit, mine, come, kind):
        shape = (2 * mine.shape[0], width)
        return step(order_body, [(shape, kind)], (uppers[bit], mine, come), 1)[0]

    down_come = other_chip(down_theirs)
    up_kept, up_sent = step(
        part_body, [(full_square := (width, width), single), (full_square, bfloat)], (uppers[0], up_mine, up_theirs), 1
    )
    up_come = other_copy(up_sent, 0)
    grad_middle, gb_own, gain_mlp_part = step(
        middle_back_body,
        [(full, single), (full, bfloat), ((1, width), single)],
        (dwa_weights, middle, keep_norm, other_core(send_norm), cotangent, gain_mlp),
        1,
    )
    gb_peer = other_core(gb_own)
    combined, dwa_part = step(
        combine_body,
        [(full, bfloat), ((depth + 1, width), single)],
        (dwa_weights, mixed, middle, keep_out, other_core(send_out), cotangent, history_parts),
        1,
    )
    back_scratch = [tokens, tokens, pltpu.VMEM((3 * part, SEQ), bfloat)]
    att_theirs = step(
        functools.partial(attend_back, False),
        [((2 * part, width), bfloat)] * 2 + [((SEQ, width), single)],
        (core, gb_own, gb_peer, x_own, x_peer, qkv_peer, out_peer, qkv_b, att_b, log_b, cosine, sine),
        1,
        back_scratch,
        60,
    )
    att_come = [other_chip(value) for value in att_theirs[:2]]
    down, sent = halve(0, down_mine, down_come)
    down_come = other_copy(sent, 0)
    up, sent = step(cross_body, [(half, single), (half, bfloat)], (up_kept, up_come))
    up_come = other_chip(sent)
    att_mine = step(
        functools.partial(attend_back, True),
        [((2 * part, width), single)] * 2
        + [(full, single), (full, bfloat), ((1, width), single)],
        (
            core, gb_own, gb_peer, x_own, x_peer, qkv_own, out_weight, qkv_a, att_a, log_a, cosine, sine,
            att_theirs[2], gain_attn,
        ),
        1,
        back_scratch + [pltpu.VMEM((SEQ, width), single)],
        60,
    )
    keep_first, send_first, gain_attn_part = att_mine[2:]
    small = jnp.concatenate([gain_attn_part, gain_mlp_part, dwa_part], axis=0)
    small = small + other_core(small)
    small = small + other_chip(small)
    for bit in range(bits):
        small = small + other_copy(small, bit)

    done = {}

    def chain(name, value, come, begun):
        if begun < 1:
            value, sent = halve(0, value, come)
            come = other_copy(sent, 0)
            yield
        if begun < 2 or name == "up":
            value, sent = halve(1, value, come)
            come = other_copy(sent, 1)
            yield
        for bit in range(2, bits):
            value = low(value, come)
            come = other_copy(value, bit)
            yield
        value = low(value, come)
        come = other_copy(value, 1)
        yield
        value = order(1, value, come, bfloat)
        come = other_copy(value, 0)
        yield
        done[name] = (value, come)

    chains = {
        "down": chain("down", down, down_come, 1),
        "up": chain("up", up, up_come, 2),
        "a": chain("a", att_mine[0], att_come[0], 0),
        "b": chain("b", att_mine[1], att_come[1], 0),
    }

    def advance(text):
        for name in text.split():
            next(chains[name], None)

    advance("a down")
    (input_grad,) = step(
        first_back_body,
        [(full, bfloat)],
        (inputs, keep_first, other_core(send_first), grad_middle, gain_attn),
    )
    advance("b a down b a up b down up a b")
    for name in ("down", "a", "b", "up"):
        for _ in range(bits + 4):
            advance(name)
    down_grad = order(0, *done["down"], single)
    qkv_grad, out_grad = step(
        order_two_body,
        [((3 * part, width), single), ((part, width), single)],
        (uppers[0], *done["a"], *done["b"]),
        1,
        [pltpu.VMEM((2 * part, width), single)],
    )
    up_grad = order(0, *done["up"], single)

    return (
        combined,
        input_grad,
        history_grad,
        qkv_grad.reshape(3, part, width).transpose(2, 0, 1),
        out_grad,
        up_grad,
        down_grad,
        small[0],
        small[1],
        jnp.sum(small[2:], axis=1),
    )


def solution(mesh):
    placed = (
        P(("dp", "mp"), None),
        P(None, ("dp", "mp"), None),
        P(("dp", "mp"), None),
        P(None, None, "mp"),
        P("mp", None),
        P(None, "mp"),
        P("mp", None),
        P(),
        P(),
        P(),
    )
    return jax.shard_map(
        shards,
        mesh=mesh,
        in_specs=placed,
        out_specs=(
            P(("dp", "mp"), None),
            P(("dp", "mp"), None),
            P(None, ("dp", "mp"), None),
            P(None, None, "mp"),
            P("mp", None),
            P(None, "mp"),
            P("mp", None),
            P(),
            P(),
            P(),
        ),
        check_vma=False,
    )
```

```python
import functools

import jax
import jax.numpy as jnp
import numpy as np
from jax import lax
from jax.experimental import pallas as pl
from jax.experimental.pallas import tpu as pltpu
from jax.sharding import PartitionSpec as P

DH = 64
SEQ = 1152
HALF = SEQ // 2
EPS = 1e-05
bfloat = jnp.bfloat16
single = jnp.float32
MIB = 1 << 20


def tables():
    half_width = DH // 2
    places = np.arange(SEQ, dtype=np.float32)
    frequency = np.float32(10000.0) ** (-np.arange(half_width, dtype=np.float32) * np.float32(2.0 / DH))
    angles = frequency[:, None] * places[None, :]
    return (np.cos(angles).astype(np.float32), np.sin(angles).astype(np.float32))


def mul(a, b, ca=1, cb=0):
    return lax.dot_general(a, b, (((ca,), (cb,)), ((), ())), preferred_element_type=single)


def call(kernel, outs, operands, scratch=(), scalars=0, after=(), vmem=16):
    count, waits = len(operands), len(after)

    def body(*refs):
        kernel(*refs[:count], *refs[count + waits :])

    small = pl.BlockSpec(memory_space=pltpu.SMEM)
    whole = pl.BlockSpec(memory_space=pltpu.VMEM)
    apart = pl.BlockSpec(memory_space=pl.ANY)
    return pl.pallas_call(
        body,
        out_shape=[jax.ShapeDtypeStruct(shape, kind) for shape, kind in outs],
        in_specs=[small] * scalars + [whole] * (count - scalars) + [apart] * waits,
        out_specs=[whole] * len(outs),
        scratch_shapes=list(scratch),
        compiler_params=pltpu.CompilerParams(vmem_limit_bytes=vmem * MIB),
        cost_estimate=pl.CostEstimate(flops=0, bytes_accessed=0, transcendentals=0),
    )(*operands, *after)


ROWS = 64
PARTS = 3


def spans(rows, step=ROWS):
    return [slice(begin, begin + step) for begin in range(0, rows, step)]


def normal_of(x):
    centre = x - jnp.mean(x, axis=-1, keepdims=True)
    spread = jnp.mean(centre * centre, axis=-1, keepdims=True)
    scale = lax.rsqrt(spread + EPS)
    return centre * scale, scale


def copy_body(in_ref, out_ref):
    out_ref[...] = in_ref[...]


def norm_body(x_ref, gain_ref, out_ref):
    gain = gain_ref[...].reshape(1, -1)
    for span in spans(x_ref.shape[0]):
        normal, _ = normal_of(x_ref[span, :].astype(single))
        out_ref[span, :] = (normal * gain).astype(bfloat)


def middle_body(x_ref, keep_ref, gain_ref, *rest):
    recv_refs, mid_ref, out_refs = rest[:PARTS], rest[PARTS], rest[PARTS + 1 :]
    gain = gain_ref[...].reshape(1, -1)
    rows = x_ref.shape[0] // PARTS
    for index in range(PARTS):
        for span in spans(rows):
            here = slice(index * rows + span.start, index * rows + span.stop)
            recv = recv_refs[index][span, :].astype(single)
            x = x_ref[here, :].astype(single) + (keep_ref[here, :] + recv)
            mid_ref[here, :] = x
            normal, _ = normal_of(x)
            out_refs[index][span, :] = (normal * gain).astype(bfloat)


def norm_back(x, grad, gain):
    normal, scale = normal_of(x)
    lifted = grad * gain
    back = scale * (
        lifted
        - jnp.mean(lifted, axis=-1, keepdims=True)
        - normal * jnp.mean(lifted * normal, axis=-1, keepdims=True)
    )
    return back, normal


def fold_rows(value):
    total = value[:8]
    for begin in range(8, value.shape[0], 8):
        total = total + value[begin : begin + 8]
    return total


def middle_back_body(mix_ref, x_ref, keep_ref, recv_ref, cot_ref, gain_ref, mid_ref, low_ref, part_ref):
    gain = gain_ref[...].reshape(1, -1)
    part = jnp.zeros((8, x_ref.shape[1]), single)
    for span in spans(x_ref.shape[0]):
        grad = keep_ref[span, :] + recv_ref[span, :].astype(single)
        back, normal = norm_back(x_ref[span, :], grad, gain)
        total = mix_ref[mix_ref.shape[0] - 1] * cot_ref[span, :] + back
        mid_ref[span, :] = total
        low_ref[span, :] = total.astype(bfloat)
        part = part + fold_rows(grad * normal)
    part_ref[...] = jnp.sum(part, axis=0, keepdims=True)


def first_back_body(x_ref, keep_ref, recv_ref, mid_ref, gain_ref, out_ref):
    gain = gain_ref[...].reshape(1, -1)
    for span in spans(x_ref.shape[0]):
        grad = keep_ref[span, :] + recv_ref[span, :].astype(single)
        back, _ = norm_back(x_ref[span, :].astype(single), grad, gain)
        out_ref[span, :] = (mid_ref[span, :] + back).astype(bfloat)


def history_body(mix_ref, history_ref, cot_ref, grad_ref, mixed_ref, low_ref, part_ref):
    depth = history_ref.shape[0]

    @pl.when(pl.program_id(0) == 0)
    def _():
        part_ref[...] = jnp.zeros_like(part_ref)

    for span in spans(cot_ref.shape[0], 32):
        cot = cot_ref[span, :]
        low_ref[span, :] = (mix_ref[depth] * cot).astype(bfloat)
        mixed = None
        for j in range(depth):
            layer = history_ref[j, span, :].astype(single)
            mixed = mix_ref[j] * layer if mixed is None else mixed + mix_ref[j] * layer
            grad_ref[j, span, :] = (mix_ref[j] * cot).astype(bfloat)
            part_ref[8 * j : 8 * j + 8, :] += fold_rows(layer * cot)
        mixed_ref[span, :] = mixed


def average_history(mix, history, cot, after=()):
    depth, rows, width = history.shape
    step = 96
    waits = len(after)

    def body(*refs):
        history_body(*refs[:3], *refs[3 + waits :])

    row_block = pl.BlockSpec((step, width), lambda i: (i, 0))
    deep_block = pl.BlockSpec((depth, step, width), lambda i: (0, i, 0))
    return pl.pallas_call(
        body,
        grid=(rows // step,),
        out_shape=[
            jax.ShapeDtypeStruct(history.shape, bfloat),
            jax.ShapeDtypeStruct((rows, width), single),
            jax.ShapeDtypeStruct((rows, width), bfloat),
            jax.ShapeDtypeStruct((8 * depth, width), single),
        ],
        in_specs=[pl.BlockSpec(memory_space=pltpu.SMEM), deep_block, row_block]
        + [pl.BlockSpec(memory_space=pl.ANY)] * waits,
        out_specs=[deep_block, row_block, row_block, pl.BlockSpec((8 * depth, width), lambda i: (0, 0))],
        compiler_params=pltpu.CompilerParams(vmem_limit_bytes=16 * MIB),
        cost_estimate=pl.CostEstimate(flops=0, bytes_accessed=0, transcendentals=0),
    )(mix, history, cot, *after)


def combine_body(mix_ref, mixed_ref, mid_ref, keep_ref, recv_ref, cot_ref, parts_ref, out_ref, part_ref):
    depth = mix_ref.shape[0] - 1
    last = jnp.zeros((8, mid_ref.shape[1]), single)
    for span in spans(mid_ref.shape[0]):
        outputs = mid_ref[span, :] + (keep_ref[span, :] + recv_ref[span, :].astype(single))
        out_ref[span, :] = (mixed_ref[span, :] + mix_ref[depth] * outputs).astype(bfloat)
        last = last + fold_rows(outputs * cot_ref[span, :])
    for j in range(depth):
        part_ref[j : j + 1, :] = jnp.sum(parts_ref[8 * j : 8 * j + 8, :], axis=0, keepdims=True)
    part_ref[depth : depth + 1, :] = jnp.sum(last, axis=0, keepdims=True)


def part_rows(upper_ref, size):
    low = pl.multiple_of(upper_ref[0] * size, size)
    high = pl.multiple_of((1 - upper_ref[0]) * size, size)
    return pl.ds(low, size), pl.ds(high, size)


def halve_body(upper_ref, mine_ref, come_ref, kept_ref, sent_ref):
    low, high = part_rows(upper_ref, kept_ref.shape[0])
    kept_ref[...] = mine_ref[low, :] + come_ref[low, :].astype(single)
    sent_ref[...] = (mine_ref[high, :] + come_ref[high, :].astype(single)).astype(bfloat)


def part_body(upper_ref, mine_ref, theirs_ref, kept_ref, sent_ref):
    size = mine_ref.shape[0] // 2
    low, high = part_rows(upper_ref, size)
    kept_ref[:size, :] = mine_ref[low, :]
    kept_ref[size:, :] = theirs_ref[low, :].astype(single)
    sent_ref[:size, :] = mine_ref[high, :].astype(bfloat)
    sent_ref[size:, :] = theirs_ref[high, :]


def cross_body(kept_ref, come_ref, mine_ref, theirs_ref):
    size = mine_ref.shape[0]
    mine_ref[...] = kept_ref[:size, :] + come_ref[:size, :].astype(single)
    theirs_ref[...] = (kept_ref[size:, :] + come_ref[size:, :].astype(single)).astype(bfloat)


def low_body(mine_ref, come_ref, out_ref):
    out_ref[...] = (mine_ref[...].astype(single) + come_ref[...].astype(single)).astype(bfloat)


def order_body(upper_ref, mine_ref, come_ref, out_ref):
    low, high = part_rows(upper_ref, mine_ref.shape[0])
    out_ref[low, :] = mine_ref[...].astype(out_ref.dtype)
    out_ref[high, :] = come_ref[...].astype(out_ref.dtype)


def order_two_body(upper_ref, mine_a_ref, come_a_ref, mine_b_ref, come_b_ref, top_ref, end_ref, hold):
    size = mine_a_ref.shape[0]
    low, high = part_rows(upper_ref, size)
    rest = top_ref.shape[0] - 2 * size
    top_ref[low, :] = mine_a_ref[...].astype(single)
    top_ref[high, :] = come_a_ref[...].astype(single)
    hold[low, :] = mine_b_ref[...].astype(single)
    hold[high, :] = come_b_ref[...].astype(single)
    top_ref[2 * size :, :] = hold[:rest, :]
    end_ref[...] = hold[rest:, :]


EXTRA = 64


def halve_more_body(upper_ref, mine_ref, come_ref, extra_ref, kept_ref, sent_ref, hold):
    rows, extra = mine_ref.shape[0], extra_ref.shape[0]
    hold[:rows, :] = mine_ref[...] + come_ref[...].astype(single)
    hold[rows:, :] = jnp.zeros((EXTRA, hold.shape[1]), single)
    hold[rows : rows + extra, :] = extra_ref[...]
    low, high = part_rows(upper_ref, kept_ref.shape[0])
    kept_ref[...] = hold[low, :]
    sent_ref[...] = hold[high, :].astype(bfloat)


def order_more_body(upper_ref, mine_ref, come_ref, out_ref, small_ref):
    size, extra = out_ref.shape[0] // 2, small_ref.shape[0]
    low, high = part_rows(upper_ref, size)
    out_ref[low, :] = mine_ref[:size, :].astype(single)
    out_ref[high, :] = come_ref[:size, :].astype(single)
    mine = mine_ref[size:, :].astype(single)
    come = come_ref[size:, :].astype(single)
    small_ref[...] = mine[:extra] + come[:extra]


BLOCKS = tuple((begin, min(256, SEQ - begin)) for begin in range(0, SEQ, 256))


def place(core_ref, own_ref, peer_ref, whole):
    low = pl.multiple_of(core_ref[0] * HALF, HALF)
    high = pl.multiple_of((1 - core_ref[0]) * HALF, HALF)
    whole[pl.ds(low, HALF), :] = own_ref[...]
    whole[pl.ds(high, HALF), :] = peer_ref[...]
    return low, high


def allowed(size):
    key_pos = lax.broadcasted_iota(jnp.int32, (size, size), 0)
    query_pos = lax.broadcasted_iota(jnp.int32, (size, size), 1)
    return query_pos >= key_pos


def turn(rows, cosine, sine):
    half = rows.shape[0] // 2
    a, b = rows[:half], rows[half:]
    return jnp.concatenate([a * cosine - b * sine, b * cosine + a * sine], axis=0)


def attend_copy(*refs):
    attend(*refs[:6], *refs[7:11], refs[12])
    refs[11][...] = refs[6][...]


def attend(core_ref, own_ref, peer_ref, weight_ref, cos_ref, sin_ref, qkv_ref, att_ref, nat_ref, log_ref, tokens):
    place(core_ref, own_ref, peer_ref, tokens)
    width = weight_ref.shape[0] // 3
    projected = mul(weight_ref[...], tokens[...], 1, 1)
    cosine, sine = cos_ref[...], sin_ref[...]
    for part in range(3):
        for head in range(width // DH):
            begin = part * width + head * DH
            rows = projected[begin : begin + DH]
            if part < 2:
                rows = turn(rows, cosine, sine)
            if part == 0:
                rows = rows * DH ** (-0.5)
            qkv_ref[begin : begin + DH, :] = rows.astype(bfloat)
    log_ref[...] = jnp.zeros_like(log_ref)
    for head in range(width // DH):
        base = head * DH
        keys = qkv_ref[width + base : width + base + DH, :].T
        for begin, size in BLOCKS:
            end = begin + size
            query = qkv_ref[base : base + DH, begin:end]
            scores = mul(keys[:end], query)
            corner = jnp.where(allowed(size), scores[begin:], -jnp.inf)
            top = jnp.max(corner, axis=0, keepdims=True)
            if begin:
                top = jnp.maximum(top, jnp.max(scores[:begin], axis=0, keepdims=True))
                scores = jnp.concatenate([scores[:begin], corner], axis=0)
            else:
                scores = corner
            weights = jnp.exp(scores - top)
            total = jnp.sum(weights, axis=0, keepdims=True)
            value = qkv_ref[2 * width + base : 2 * width + base + DH, :end]
            mixed = mul(value, weights.astype(bfloat)) / total
            att_ref[base : base + DH, begin:end] = mixed.astype(bfloat)
            log_ref[head : head + 1, begin:end] = top + jnp.log(total)
    nat_ref[...] = att_ref[...].T


def branch_body(core_ref, att_a_ref, att_b_ref, out_a_ref, out_b_ref, keep_ref, *send_refs):
    low = pl.multiple_of(core_ref[0] * HALF, HALF)
    rows = HALF // PARTS
    for index in range(PARTS):
        high = pl.multiple_of((1 - core_ref[0]) * HALF + index * rows, rows)
        send = mul(att_a_ref[pl.ds(high, rows), :], out_a_ref[...])
        send_refs[index][...] = (send + mul(att_b_ref[pl.ds(high, rows), :], out_b_ref[...])).astype(bfloat)
    keep = mul(att_a_ref[pl.ds(low, HALF), :], out_a_ref[...])
    keep_ref[...] = keep + mul(att_b_ref[pl.ds(low, HALF), :], out_b_ref[...])


def attend_back(
    second, core_ref, grad_own_ref, grad_peer_ref, own_ref, peer_ref, weight_ref, out_ref, qkv_ref, att_ref,
    log_ref, cos_ref, sin_ref, *rest,
):
    if second:
        before_ref, gain_ref, first_ref, last_ref, keep_ref, send_ref, part_ref, tokens, grads, turned, whole = rest
    else:
        first_ref, last_ref, whole, tokens, grads, turned = rest
    low, high = place(core_ref, own_ref, peer_ref, tokens)
    place(core_ref, grad_own_ref, grad_peer_ref, grads)
    width = out_ref.shape[0]
    out_grad = mul(att_ref[...], grads[...])
    grad_att = mul(out_ref[...], grads[...], 1, 1).astype(bfloat)
    cosine, sine = cos_ref[...], sin_ref[...]
    for head in range(width // DH):
        base = head * DH
        query = qkv_ref[base : base + DH, :]
        key = qkv_ref[width + base : width + base + DH, :]
        value = qkv_ref[2 * width + base : 2 * width + base + DH, :]
        above = grad_att[base : base + DH]
        centre = jnp.sum(
            above.astype(single) * att_ref[base : base + DH, :].astype(single), axis=0, keepdims=True
        )
        keys, values = key.T, value.T
        grad_query, grad_key, grad_value = [], None, None
        for begin, size in reversed(BLOCKS):
            end = begin + size
            scores = mul(keys[:end], query[:, begin:end])
            corner = jnp.where(allowed(size), scores[begin:], -jnp.inf)
            scores = jnp.concatenate([scores[:begin], corner], axis=0) if begin else corner
            probs = jnp.exp(scores - log_ref[head : head + 1, begin:end])
            grad_probs = mul(values[:end], above[:, begin:end])
            grad_scores = (probs * (grad_probs - centre[:, begin:end])).astype(bfloat)
            grad_query.insert(0, mul(key[:, :end], grad_scores))
            key_part = mul(query[:, begin:end], grad_scores, 1, 1)
            value_part = mul(above[:, begin:end], probs.astype(bfloat), 1, 1)
            if grad_key is None:
                grad_key, grad_value = key_part, value_part
            else:
                grad_key = jnp.concatenate([grad_key[:, :end] + key_part, grad_key[:, end:]], axis=1)
                grad_value = jnp.concatenate([grad_value[:, :end] + value_part, grad_value[:, end:]], axis=1)
        grad_query = jnp.concatenate(grad_query, axis=1) * DH ** (-0.5)
        turned[base : base + DH, :] = turn(grad_query, cosine, -sine).astype(bfloat)
        turned[width + base : width + base + DH, :] = turn(grad_key, cosine, -sine).astype(bfloat)
        turned[2 * width + base : 2 * width + base + DH, :] = grad_value.astype(bfloat)
    first_ref[...] = mul(turned[: 2 * width, :], tokens[...]).astype(first_ref.dtype)
    last_ref[:width, :] = mul(turned[2 * width :, :], tokens[...]).astype(last_ref.dtype)
    last_ref[width:, :] = out_grad.astype(last_ref.dtype)
    result = mul(turned[...], weight_ref[...], 0, 0)
    if second:
        whole[...] = before_ref[...] + result
        keep_ref[...] = whole[pl.ds(low, HALF), :]
        send_ref[...] = whole[pl.ds(high, HALF), :].astype(bfloat)
        part_ref[...] = (
            jnp.sum(whole[...] * tokens[...].astype(single), axis=0, keepdims=True) / gain_ref[...].reshape(1, -1)
        )
    else:
        whole[...] = result


CURVE = float(np.sqrt(2.0 / np.pi))
STEP = 256


def mlp_body(second, *rest):
    x_refs, rest = rest[: 2 * PARTS], rest[2 * PARTS :]
    g_own_ref, g_peer_ref, up_ref, down_ref = rest[:4]
    rest = rest[4:]
    if second:
        keep_out_a, keep_norm_a, send_out_a, send_norm_a = rest[:4]
        rest = rest[4:]
    keep_out_ref, send_out_ref, keep_norm_ref, send_norm_ref = rest[:4]
    down_grad_ref, up_grad_ref, x_all, g_all, x_turned, active, grad_hidden = rest[4:]
    rows = g_own_ref.shape[0]
    hidden_units = down_ref.shape[0]
    for index in range(2 * PARTS):
        size = rows // PARTS
        x_all[index * size : (index + 1) * size, :] = x_refs[index][...]
    g_all[:rows, :] = g_own_ref[...]
    g_all[rows:, :] = g_peer_ref[...]
    x_turned[...] = x_all[...].T
    for begin in range(0, hidden_units, STEP):
        columns = slice(begin, begin + STEP)
        for top in range(0, 2 * rows, rows):
            span = slice(top, top + rows)
            v = mul(x_all[span, :], up_ref[:, columns])
            grad = mul(g_all[span, :], down_ref[columns, :], 1, 1)
            square = v * v
            half = 0.5 + 0.5 * jnp.tanh(v * (CURVE + (CURVE * 0.044715) * square))
            act = v * half
            slope = half + act * (1.0 - half) * (2.0 * CURVE + (6.0 * CURVE * 0.044715) * square)
            active[span, columns] = act.astype(bfloat)
            grad_hidden[span, columns] = (grad * slope).astype(bfloat)
    out_own = mul(active[:rows, :], down_ref[...])
    out_peer = mul(active[rows:, :], down_ref[...])
    norm_own = mul(grad_hidden[:rows, :], up_ref[...], 1, 1)
    norm_peer = mul(grad_hidden[rows:, :], up_ref[...], 1, 1)
    if second:
        out_own = out_own + keep_out_a[...]
        out_peer = out_peer + send_out_a[...].astype(single)
        norm_own = norm_own + keep_norm_a[...]
        norm_peer = norm_peer + send_norm_a[...].astype(single)
    keep_out_ref[...] = out_own
    send_out_ref[...] = out_peer.astype(bfloat)
    keep_norm_ref[...] = norm_own
    send_norm_ref[...] = norm_peer.astype(bfloat)
    size = hidden_units // 2
    for begin in range(0, hidden_units, size):
        columns = slice(begin, begin + size)
        down_grad_ref[columns, :] = mul(active[:, columns], g_all[...], 0, 0).astype(down_grad_ref.dtype)
        up_grad_ref[columns, :] = mul(x_turned[columns, :], grad_hidden[...]).astype(up_grad_ref.dtype)


def mlp(x_own, x_peer, g_own, g_peer, up, down, before=(), after=()):
    rows, width = g_own.shape
    units = down.shape[0]
    kind = bfloat if before else single
    outs = [((rows, width), single), ((rows, width), bfloat)] * 2 + [((units, width), kind), ((width, units), kind)]
    scratch = [
        pltpu.VMEM((2 * rows, width), bfloat),
        pltpu.VMEM((2 * rows, width), bfloat),
        pltpu.VMEM((width, 2 * rows), bfloat),
        pltpu.VMEM((2 * rows, units), bfloat),
        pltpu.VMEM((2 * rows, units), bfloat),
    ]
    operands = (*x_own, *x_peer, g_own, g_peer, up, down) + tuple(before)
    return call(functools.partial(mlp_body, bool(before)), outs, operands, scratch, after=after, vmem=60)


def shards(
    inputs,
    history,
    cotangent,
    qkv_weight,
    out_weight,
    up_weight,
    down_weight,
    gain_attn,
    gain_mlp,
    dwa_weights,
):
    rows, width = inputs.shape
    members = lax.axis_size("mp")
    copies = lax.axis_size("dp")
    bits = copies.bit_length() - 1
    core = lax.rem(lax.axis_index("mp"), 2).astype(jnp.int32).reshape(1)
    copy_index = lax.axis_index("dp").astype(jnp.int32).reshape(1)
    core_pairs = [(i, i ^ 1) for i in range(members)]
    chip_pairs = [(i, i ^ 2) for i in range(members)]
    depth = history.shape[0]
    part = out_weight.shape[0]

    def other_core(value):
        return lax.ppermute(value, "mp", core_pairs)

    def other_chip(value):
        return lax.ppermute(value, "mp", chip_pairs)

    def other_copy(value, bit):
        return lax.ppermute(value, "dp", [(i, i ^ (1 << bit)) for i in range(copies)])

    uppers = [(copy_index >> bit) & 1 for bit in range(bits)]
    cosine, sine = (jnp.asarray(table) for table in tables())

    qkv_own = qkv_weight.transpose(1, 2, 0).reshape(3 * part, width)
    share = width // copies
    up_share = lax.dynamic_slice_in_dim(up_weight, copy_index[0] * share, share, 0)
    up_share = other_chip(up_share)
    up_peer = lax.all_gather(up_share, "dp", axis=0, tiled=True)
    out_peer = other_chip(out_weight)

    full = (rows, width)
    (x_own,) = call(norm_body, [(full, bfloat)], (inputs, gain_attn))
    (qkv_copy,) = call(copy_body, [(qkv_own.shape, bfloat)], (qkv_own,), after=(x_own, up_share))
    qkv_peer = other_chip(qkv_copy)
    x_peer = other_core(x_own)
    history_grad, mixed, g_own, history_parts = average_history(dwa_weights, history, cotangent, (qkv_copy,))
    g_peer = other_core(g_own)

    tokens = pltpu.VMEM((SEQ, width), bfloat)
    first_outs = [
        ((3 * part, SEQ), bfloat), ((part, SEQ), bfloat), ((SEQ, part), bfloat), ((8, SEQ), single),
    ]
    qkv_a, att_a, nat_a, log_a = call(
        attend, first_outs, (core, x_own, x_peer, qkv_own, cosine, sine), [tokens], 1, (history_parts,), 32
    )
    qkv_b, att_b, nat_b, log_b, down_copy = call(
        attend_copy,
        first_outs + [(down_weight.shape, bfloat)],
        (core, x_own, x_peer, qkv_peer, cosine, sine, down_weight),
        [tokens],
        1,
        (log_a,),
        32,
    )
    down_peer = other_chip(down_copy)
    third = (rows // PARTS, width)
    keep, *send = call(
        branch_body,
        [(full, single)] + [(third, bfloat)] * PARTS,
        (core, nat_a, nat_b, out_weight, out_peer),
        scalars=1,
    )
    recv = [other_core(value) for value in send]
    middle, *y_own = call(
        middle_body, [(full, single)] + [(third, bfloat)] * PARTS, (inputs, keep, gain_mlp, *recv)
    )
    y_peer = [other_core(value) for value in y_own]

    first = mlp(y_own, y_peer, g_own, g_peer, up_weight, down_weight)
    second = mlp(
        y_own, y_peer, g_own, g_peer, up_peer, down_peer, (first[0], first[2], first[1], first[3])
    )
    keep_out, send_out, keep_norm, send_norm, down_theirs, up_theirs = second
    down_mine, up_mine = first[4:]
    half = (width // 2, width)

    token = [keep_norm]

    def step(body, outs, operands, scalars=0, scratch=(), vmem=16):
        results = call(body, outs, operands, scratch, scalars, tuple(token), vmem)
        token[0] = results[0]
        return results

    def halve(bit, mine, come):
        shape = (mine.shape[0] // 2, width)
        return step(halve_body, [(shape, single), (shape, bfloat)], (uppers[bit], mine, come), 1)

    def low(mine, come):
        return step(low_body, [(mine.shape, bfloat)], (mine, come))[0]

    def order(bit, mine, come, kind):
        shape = (2 * mine.shape[0], width)
        return step(order_body, [(shape, kind)], (uppers[bit], mine, come), 1)[0]

    down_come = other_chip(down_theirs)
    square = (width, width)
    up_kept, up_sent = step(
        part_body, [(square, single), (square, bfloat)], (uppers[1], up_mine, up_theirs), 1
    )
    up_come = other_copy(up_sent, 1)
    grad_middle, gb_own, gain_mlp_part = step(
        middle_back_body,
        [(full, single), (full, bfloat), ((1, width), single)],
        (dwa_weights, middle, keep_norm, other_core(send_norm), cotangent, gain_mlp),
        1,
    )
    gb_peer = other_core(gb_own)
    combined, dwa_part = step(
        combine_body,
        [(full, bfloat), ((depth + 1, width), single)],
        (dwa_weights, mixed, middle, keep_out, other_core(send_out), cotangent, history_parts),
        1,
    )
    back_scratch = [tokens, tokens, pltpu.VMEM((3 * part, SEQ), bfloat)]
    att_theirs = step(
        functools.partial(attend_back, False),
        [((2 * part, width), bfloat)] * 2 + [((SEQ, width), single)],
        (core, gb_own, gb_peer, x_own, x_peer, qkv_peer, out_peer, qkv_b, att_b, log_b, cosine, sine),
        1,
        back_scratch,
        60,
    )
    att_come = [other_chip(value) for value in att_theirs[:2]]
    down, sent = halve(0, down_mine, down_come)
    down_come = other_copy(sent, 0)
    up, sent = step(cross_body, [(half, single), (half, bfloat)], (up_kept, up_come))
    up_come = other_chip(sent)
    att_mine = step(
        functools.partial(attend_back, True),
        [((2 * part, width), single)] * 2
        + [(full, single), (full, bfloat), ((1, width), single)],
        (
            core, gb_own, gb_peer, x_own, x_peer, qkv_own, out_weight, qkv_a, att_a, log_a, cosine, sine,
            att_theirs[2], gain_attn,
        ),
        1,
        back_scratch + [pltpu.VMEM((SEQ, width), single)],
        60,
    )
    keep_first, send_first, gain_attn_part = att_mine[2:]
    small = jnp.concatenate([gain_attn_part, gain_mlp_part, dwa_part], axis=0)
    small = small + other_core(small)
    small = small + other_chip(small)
    extra_rows = depth + 3

    done = {}

    def chain(name, first_bit, second_bit, value, come, begun, extra=None):
        if not begun:
            value, sent = halve(first_bit, value, come)
            come = other_copy(sent, first_bit)
            yield
        if extra is None:
            value, sent = halve(second_bit, value, come)
        else:
            shape = ((value.shape[0] + EXTRA) // 2, width)
            value, sent = step(
                halve_more_body,
                [(shape, single), (shape, bfloat)],
                (uppers[second_bit], value, come, extra),
                1,
                [pltpu.VMEM((2 * shape[0], width), single)],
            )
        come = other_copy(sent, second_bit)
        yield
        for bit in range(2, bits):
            value = low(value, come)
            come = other_copy(value, bit)
            yield
        value = low(value, come)
        come = other_copy(value, second_bit)
        yield
        value = order(second_bit, value, come, bfloat)
        come = other_copy(value, first_bit)
        yield
        done[name] = (value, come)

    chains = {
        "d": chain("d", 0, 1, down, down_come, True),
        "u": chain("u", 1, 0, up, up_come, True, small),
        "a": chain("a", 0, 1, att_mine[0], att_come[0], False),
        "b": chain("b", 0, 1, att_mine[1], att_come[1], False),
    }
    for name in "dabdababudabudabu":
        next(chains[name], None)
    for name in "dabu":
        for _ in range(bits + 4):
            next(chains[name], None)
    down_grad = order(0, *done["d"], single)
    (input_grad,) = step(
        first_back_body,
        [(full, bfloat)],
        (inputs, keep_first, other_core(send_first), grad_middle, gain_attn),
    )
    qkv_grad, out_grad = step(
        order_two_body,
        [((3 * part, width), single), ((part, width), single)],
        (uppers[0], *done["a"], *done["b"]),
        1,
        [pltpu.VMEM((2 * part, width), single)],
    )
    up_grad, small = step(
        order_more_body, [(square, single), ((extra_rows, width), single)], (uppers[1], *done["u"]), 1
    )

    return (
        combined,
        input_grad,
        history_grad,
        qkv_grad.reshape(3, part, width).transpose(2, 0, 1),
        out_grad,
        up_grad,
        down_grad,
        small[0],
        small[1],
        jnp.sum(small[2:], axis=1),
    )


def solution(mesh):
    placed = (
        P(("dp", "mp"), None),
        P(None, ("dp", "mp"), None),
        P(("dp", "mp"), None),
        P(None, None, "mp"),
        P("mp", None),
        P(None, "mp"),
        P("mp", None),
        P(),
        P(),
        P(),
    )
    return jax.shard_map(
        shards,
        mesh=mesh,
        in_specs=placed,
        out_specs=(
            P(("dp", "mp"), None),
            P(("dp", "mp"), None),
            P(None, ("dp", "mp"), None),
            P(None, None, "mp"),
            P("mp", None),
            P(None, "mp"),
            P("mp", None),
            P(),
            P(),
            P(),
        ),
        check_vma=False,
    )
```

```python
import functools

import jax
import jax.numpy as jnp
import numpy as np
from jax import lax
from jax.experimental import pallas as pl
from jax.experimental.pallas import tpu as pltpu
from jax.sharding import PartitionSpec as P

DH = 64
SEQ = 1152
HALF = SEQ // 2
EPS = 1e-05
bfloat = jnp.bfloat16
single = jnp.float32
MIB = 1 << 20
MUCH = 10**11


def tables():
    half_width = DH // 2
    places = np.arange(SEQ, dtype=np.float32)
    frequency = np.float32(10000.0) ** (-np.arange(half_width, dtype=np.float32) * np.float32(2.0 / DH))
    angles = frequency[:, None] * places[None, :]
    return (np.cos(angles).astype(np.float32), np.sin(angles).astype(np.float32))


def mul(a, b, ca=1, cb=0):
    return lax.dot_general(a, b, (((ca,), (cb,)), ((), ())), preferred_element_type=single)


def call(kernel, outs, operands, scratch=(), scalars=0, after=(), vmem=16, flops=0):
    count, waits = len(operands), len(after)

    def body(*refs):
        kernel(*refs[:count], *refs[count + waits :])

    small = pl.BlockSpec(memory_space=pltpu.SMEM)
    whole = pl.BlockSpec(memory_space=pltpu.VMEM)
    apart = pl.BlockSpec(memory_space=pl.ANY)
    return pl.pallas_call(
        body,
        out_shape=[jax.ShapeDtypeStruct(shape, kind) for shape, kind in outs],
        in_specs=[small] * scalars + [whole] * (count - scalars) + [apart] * waits,
        out_specs=[whole] * len(outs),
        scratch_shapes=list(scratch),
        compiler_params=pltpu.CompilerParams(vmem_limit_bytes=vmem * MIB),
        cost_estimate=pl.CostEstimate(flops=flops, bytes_accessed=0, transcendentals=0),
    )(*operands, *after)


ROWS = 64
PARTS = 3


def spans(rows, step=ROWS):
    return [slice(begin, begin + step) for begin in range(0, rows, step)]


def normal_of(x):
    centre = x - jnp.mean(x, axis=-1, keepdims=True)
    spread = jnp.mean(centre * centre, axis=-1, keepdims=True)
    scale = lax.rsqrt(spread + EPS)
    return centre * scale, scale


def join_body(first_ref, second_ref, out_ref):
    size = first_ref.shape[0]
    out_ref[:size, :] = first_ref[...]
    out_ref[size:, :] = second_ref[...]


def norm_body(x_ref, gain_ref, out_ref):
    gain = gain_ref[...].reshape(1, -1)
    for span in spans(x_ref.shape[0]):
        normal, _ = normal_of(x_ref[span, :].astype(single))
        out_ref[span, :] = (normal * gain).astype(bfloat)


def middle_body(x_ref, keep_ref, gain_ref, *rest):
    recv_refs, mid_ref, out_refs = rest[:PARTS], rest[PARTS], rest[PARTS + 1 :]
    gain = gain_ref[...].reshape(1, -1)
    rows = x_ref.shape[0] // PARTS
    for index in range(PARTS):
        for span in spans(rows):
            here = slice(index * rows + span.start, index * rows + span.stop)
            recv = recv_refs[index][span, :].astype(single)
            x = x_ref[here, :].astype(single) + (keep_ref[here, :] + recv)
            mid_ref[here, :] = x
            normal, _ = normal_of(x)
            out_refs[index][span, :] = (normal * gain).astype(bfloat)


def norm_back(x, grad, gain):
    normal, scale = normal_of(x)
    lifted = grad * gain
    back = scale * (
        lifted
        - jnp.mean(lifted, axis=-1, keepdims=True)
        - normal * jnp.mean(lifted * normal, axis=-1, keepdims=True)
    )
    return back, normal


def fold_rows(value):
    total = value[:8]
    for begin in range(8, value.shape[0], 8):
        total = total + value[begin : begin + 8]
    return total


def middle_back_body(mix_ref, x_ref, keep_ref, recv_ref, cot_ref, gain_ref, mid_ref, low_ref, part_ref):
    gain = gain_ref[...].reshape(1, -1)
    part = jnp.zeros((8, x_ref.shape[1]), single)
    for span in spans(x_ref.shape[0]):
        grad = keep_ref[span, :] + recv_ref[span, :].astype(single)
        back, normal = norm_back(x_ref[span, :], grad, gain)
        total = mix_ref[mix_ref.shape[0] - 1] * cot_ref[span, :] + back
        mid_ref[span, :] = total
        low_ref[span, :] = total.astype(bfloat)
        part = part + fold_rows(grad * normal)
    part_ref[...] = jnp.sum(part, axis=0, keepdims=True)


def first_back_body(x_ref, keep_ref, recv_ref, mid_ref, gain_ref, out_ref):
    gain = gain_ref[...].reshape(1, -1)
    for span in spans(x_ref.shape[0]):
        grad = keep_ref[span, :] + recv_ref[span, :].astype(single)
        back, _ = norm_back(x_ref[span, :].astype(single), grad, gain)
        out_ref[span, :] = (mid_ref[span, :] + back).astype(bfloat)


def history_body(mix_ref, history_ref, cot_ref, grad_ref, mixed_ref, low_ref, part_ref):
    depth = history_ref.shape[0]

    @pl.when(pl.program_id(0) == 0)
    def _():
        part_ref[...] = jnp.zeros_like(part_ref)

    for span in spans(cot_ref.shape[0], 32):
        cot = cot_ref[span, :]
        low_ref[span, :] = (mix_ref[depth] * cot).astype(bfloat)
        mixed = None
        for j in range(depth):
            layer = history_ref[j, span, :].astype(single)
            mixed = mix_ref[j] * layer if mixed is None else mixed + mix_ref[j] * layer
            grad_ref[j, span, :] = (mix_ref[j] * cot).astype(bfloat)
            part_ref[8 * j : 8 * j + 8, :] += fold_rows(layer * cot)
        mixed_ref[span, :] = mixed


def average_history(mix, history, cot, after=()):
    depth, rows, width = history.shape
    step = 96
    waits = len(after)

    def body(*refs):
        history_body(*refs[:3], *refs[3 + waits :])

    row_block = pl.BlockSpec((step, width), lambda i: (i, 0))
    deep_block = pl.BlockSpec((depth, step, width), lambda i: (0, i, 0))
    return pl.pallas_call(
        body,
        grid=(rows // step,),
        out_shape=[
            jax.ShapeDtypeStruct(history.shape, bfloat),
            jax.ShapeDtypeStruct((rows, width), single),
            jax.ShapeDtypeStruct((rows, width), bfloat),
            jax.ShapeDtypeStruct((8 * depth, width), single),
        ],
        in_specs=[pl.BlockSpec(memory_space=pltpu.SMEM), deep_block, row_block]
        + [pl.BlockSpec(memory_space=pl.ANY)] * waits,
        out_specs=[deep_block, row_block, row_block, pl.BlockSpec((8 * depth, width), lambda i: (0, 0))],
        compiler_params=pltpu.CompilerParams(vmem_limit_bytes=16 * MIB),
        cost_estimate=pl.CostEstimate(flops=0, bytes_accessed=0, transcendentals=0),
    )(mix, history, cot, *after)


def combine_body(mix_ref, mixed_ref, mid_ref, keep_ref, recv_ref, cot_ref, parts_ref, out_ref, part_ref):
    depth = mix_ref.shape[0] - 1
    last = jnp.zeros((8, mid_ref.shape[1]), single)
    for span in spans(mid_ref.shape[0]):
        outputs = mid_ref[span, :] + (keep_ref[span, :] + recv_ref[span, :].astype(single))
        out_ref[span, :] = (mixed_ref[span, :] + mix_ref[depth] * outputs).astype(bfloat)
        last = last + fold_rows(outputs * cot_ref[span, :])
    for j in range(depth):
        part_ref[j : j + 1, :] = jnp.sum(parts_ref[8 * j : 8 * j + 8, :], axis=0, keepdims=True)
    part_ref[depth : depth + 1, :] = jnp.sum(last, axis=0, keepdims=True)


def part_rows(upper_ref, size):
    low = pl.multiple_of(upper_ref[0] * size, size)
    high = pl.multiple_of((1 - upper_ref[0]) * size, size)
    return pl.ds(low, size), pl.ds(high, size)


def halve_body(upper_ref, mine_ref, come_ref, kept_ref, sent_ref):
    low, high = part_rows(upper_ref, kept_ref.shape[0])
    kept_ref[...] = mine_ref[low, :] + come_ref[low, :].astype(single)
    sent_ref[...] = (mine_ref[high, :] + come_ref[high, :].astype(single)).astype(bfloat)


def part_body(upper_ref, mine_ref, theirs_ref, kept_ref, sent_ref):
    size = mine_ref.shape[0] // 2
    low, high = part_rows(upper_ref, size)
    kept_ref[:size, :] = mine_ref[low, :]
    kept_ref[size:, :] = theirs_ref[low, :].astype(single)
    sent_ref[:size, :] = mine_ref[high, :].astype(bfloat)
    sent_ref[size:, :] = theirs_ref[high, :]


def cross_body(kept_ref, come_ref, mine_ref, theirs_ref):
    size = mine_ref.shape[0]
    mine_ref[...] = kept_ref[:size, :] + come_ref[:size, :].astype(single)
    theirs_ref[...] = (kept_ref[size:, :] + come_ref[size:, :].astype(single)).astype(bfloat)


def low_body(mine_ref, come_ref, out_ref):
    out_ref[...] = (mine_ref[...].astype(single) + come_ref[...].astype(single)).astype(bfloat)


def order_body(upper_ref, mine_ref, come_ref, out_ref):
    low, high = part_rows(upper_ref, mine_ref.shape[0])
    out_ref[low, :] = mine_ref[...].astype(out_ref.dtype)
    out_ref[high, :] = come_ref[...].astype(out_ref.dtype)


def order_two_body(upper_ref, mine_ref, come_ref, top_ref, end_ref, hold):
    low, high = part_rows(upper_ref, mine_ref.shape[0])
    rest = top_ref.shape[0]
    hold[low, :] = mine_ref[...].astype(single)
    hold[high, :] = come_ref[...].astype(single)
    top_ref[...] = hold[:rest, :]
    end_ref[...] = hold[rest:, :]


def add_body(mine_ref, come_ref, out_ref):
    out_ref[...] = mine_ref[...] + come_ref[...]


def small_body(attn_ref, mlp_ref, dwa_ref, out_ref):
    out_ref[:1, :] = attn_ref[...]
    out_ref[1:2, :] = mlp_ref[...]
    out_ref[2:, :] = dwa_ref[...]


EXTRA = 64


def halve_more_body(upper_ref, mine_ref, come_ref, extra_ref, more_ref, kept_ref, sent_ref, hold):
    rows, extra = mine_ref.shape[0], extra_ref.shape[0]
    hold[:rows, :] = mine_ref[...] + come_ref[...].astype(single)
    hold[rows:, :] = jnp.zeros((EXTRA, hold.shape[1]), single)
    hold[rows : rows + extra, :] = extra_ref[...] + more_ref[...]
    low, high = part_rows(upper_ref, kept_ref.shape[0])
    kept_ref[...] = hold[low, :]
    sent_ref[...] = hold[high, :].astype(bfloat)


def order_more_body(upper_ref, mine_ref, come_ref, out_ref, small_ref):
    size, extra = out_ref.shape[0] // 2, small_ref.shape[0]
    low, high = part_rows(upper_ref, size)
    out_ref[low, :] = mine_ref[:size, :].astype(single)
    out_ref[high, :] = come_ref[:size, :].astype(single)
    mine = mine_ref[size:, :].astype(single)
    come = come_ref[size:, :].astype(single)
    small_ref[...] = mine[:extra] + come[:extra]


BLOCKS = tuple((begin, min(256, SEQ - begin)) for begin in range(0, SEQ, 256))


def place(core_ref, own_ref, peer_ref, whole):
    low = pl.multiple_of(core_ref[0] * HALF, HALF)
    high = pl.multiple_of((1 - core_ref[0]) * HALF, HALF)
    whole[pl.ds(low, HALF), :] = own_ref[...]
    whole[pl.ds(high, HALF), :] = peer_ref[...]
    return low, high


def allowed(size):
    key_pos = lax.broadcasted_iota(jnp.int32, (size, size), 0)
    query_pos = lax.broadcasted_iota(jnp.int32, (size, size), 1)
    return query_pos >= key_pos


def turn(rows, cosine, sine):
    half = rows.shape[0] // 2
    a, b = rows[:half], rows[half:]
    return jnp.concatenate([a * cosine - b * sine, b * cosine + a * sine], axis=0)


def attend_copy(*refs):
    attend(*refs[:6], *refs[7:11], refs[12])
    refs[11][...] = refs[6][...]


def attend(core_ref, own_ref, peer_ref, weight_ref, cos_ref, sin_ref, qkv_ref, att_ref, nat_ref, log_ref, tokens):
    place(core_ref, own_ref, peer_ref, tokens)
    width = weight_ref.shape[0] // 4
    projected = mul(weight_ref[: 3 * width, :], tokens[...], 1, 1)
    cosine, sine = cos_ref[...], sin_ref[...]
    for part in range(3):
        for head in range(width // DH):
            begin = part * width + head * DH
            rows = projected[begin : begin + DH]
            if part < 2:
                rows = turn(rows, cosine, sine)
            if part == 0:
                rows = rows * DH ** (-0.5)
            qkv_ref[begin : begin + DH, :] = rows.astype(bfloat)
    log_ref[...] = jnp.zeros_like(log_ref)
    for head in range(width // DH):
        base = head * DH
        keys = qkv_ref[width + base : width + base + DH, :].T
        for begin, size in BLOCKS:
            end = begin + size
            query = qkv_ref[base : base + DH, begin:end]
            scores = mul(keys[:end], query)
            corner = jnp.where(allowed(size), scores[begin:], -jnp.inf)
            top = jnp.max(corner, axis=0, keepdims=True)
            if begin:
                top = jnp.maximum(top, jnp.max(scores[:begin], axis=0, keepdims=True))
                scores = jnp.concatenate([scores[:begin], corner], axis=0)
            else:
                scores = corner
            weights = jnp.exp(scores - top)
            total = jnp.sum(weights, axis=0, keepdims=True)
            value = qkv_ref[2 * width + base : 2 * width + base + DH, :end]
            mixed = mul(value, weights.astype(bfloat)) / total
            att_ref[base : base + DH, begin:end] = mixed.astype(bfloat)
            log_ref[head : head + 1, begin:end] = top + jnp.log(total)
    nat_ref[...] = att_ref[...].T


def branch_body(core_ref, att_a_ref, att_b_ref, out_a_ref, out_b_ref, keep_ref, *send_refs):
    low = pl.multiple_of(core_ref[0] * HALF, HALF)
    rows = HALF // PARTS
    begin = out_a_ref.shape[0] - att_a_ref.shape[1]
    for index in range(PARTS):
        high = pl.multiple_of((1 - core_ref[0]) * HALF + index * rows, rows)
        send = mul(att_a_ref[pl.ds(high, rows), :], out_a_ref[begin:, :])
        send_refs[index][...] = (send + mul(att_b_ref[pl.ds(high, rows), :], out_b_ref[begin:, :])).astype(bfloat)
    keep = mul(att_a_ref[pl.ds(low, HALF), :], out_a_ref[begin:, :])
    keep_ref[...] = keep + mul(att_b_ref[pl.ds(low, HALF), :], out_b_ref[begin:, :])


def attend_back(
    second, core_ref, grad_own_ref, grad_peer_ref, own_ref, peer_ref, weight_ref, qkv_ref, att_ref,
    log_ref, cos_ref, sin_ref, *rest,
):
    if second:
        before_ref, gain_ref, first_ref, keep_ref, send_ref, part_ref, tokens, grads, turned, whole = rest
    else:
        first_ref, whole, tokens, grads, turned = rest
    low, high = place(core_ref, own_ref, peer_ref, tokens)
    place(core_ref, grad_own_ref, grad_peer_ref, grads)
    width = att_ref.shape[0]
    out_grad = mul(att_ref[...], grads[...])
    grad_att = mul(weight_ref[3 * width :, :], grads[...], 1, 1).astype(bfloat)
    cosine, sine = cos_ref[...], sin_ref[...]
    for head in range(width // DH):
        base = head * DH
        query = qkv_ref[base : base + DH, :]
        key = qkv_ref[width + base : width + base + DH, :]
        value = qkv_ref[2 * width + base : 2 * width + base + DH, :]
        above = grad_att[base : base + DH]
        centre = jnp.sum(
            above.astype(single) * att_ref[base : base + DH, :].astype(single), axis=0, keepdims=True
        )
        keys, values = key.T, value.T
        grad_query, grad_key, grad_value = [], None, None
        for begin, size in reversed(BLOCKS):
            end = begin + size
            scores = mul(keys[:end], query[:, begin:end])
            corner = jnp.where(allowed(size), scores[begin:], -jnp.inf)
            scores = jnp.concatenate([scores[:begin], corner], axis=0) if begin else corner
            probs = jnp.exp(scores - log_ref[head : head + 1, begin:end])
            grad_probs = mul(values[:end], above[:, begin:end])
            grad_scores = (probs * (grad_probs - centre[:, begin:end])).astype(bfloat)
            grad_query.insert(0, mul(key[:, :end], grad_scores))
            key_part = mul(query[:, begin:end], grad_scores, 1, 1)
            value_part = mul(above[:, begin:end], probs.astype(bfloat), 1, 1)
            if grad_key is None:
                grad_key, grad_value = key_part, value_part
            else:
                grad_key = jnp.concatenate([grad_key[:, :end] + key_part, grad_key[:, end:]], axis=1)
                grad_value = jnp.concatenate([grad_value[:, :end] + value_part, grad_value[:, end:]], axis=1)
        grad_query = jnp.concatenate(grad_query, axis=1) * DH ** (-0.5)
        turned[base : base + DH, :] = turn(grad_query, cosine, -sine).astype(bfloat)
        turned[width + base : width + base + DH, :] = turn(grad_key, cosine, -sine).astype(bfloat)
        turned[2 * width + base : 2 * width + base + DH, :] = grad_value.astype(bfloat)
    first_ref[: 3 * width, :] = mul(turned[...], tokens[...]).astype(first_ref.dtype)
    first_ref[3 * width :, :] = out_grad.astype(first_ref.dtype)
    result = mul(turned[...], weight_ref[: 3 * width, :], 0, 0)
    if second:
        whole[...] = before_ref[...] + result
        keep_ref[...] = whole[pl.ds(low, HALF), :]
        send_ref[...] = whole[pl.ds(high, HALF), :].astype(bfloat)
        part_ref[...] = (
            jnp.sum(whole[...] * tokens[...].astype(single), axis=0, keepdims=True) / gain_ref[...].reshape(1, -1)
        )
    else:
        whole[...] = result


CURVE = float(np.sqrt(2.0 / np.pi))
STEP = 256


def mlp_body(second, *rest):
    if second:
        upper_ref, up_mine_ref, rest = rest[0], rest[1], rest[2:]
    x_refs, rest = rest[: 2 * PARTS], rest[2 * PARTS :]
    g_own_ref, g_peer_ref, up_ref, down_ref = rest[:4]
    rest = rest[4:]
    if second:
        keep_out_a, keep_norm_a, send_out_a, send_norm_a = rest[:4]
        rest = rest[4:]
    keep_out_ref, send_out_ref, keep_norm_ref, send_norm_ref = rest[:4]
    if second:
        down_grad_ref, kept_ref, sent_ref, x_all, g_all, x_turned, active, grad_hidden, up_grad_ref = rest[4:]
    else:
        down_grad_ref, up_grad_ref, x_all, g_all, x_turned, active, grad_hidden = rest[4:]
    rows = g_own_ref.shape[0]
    hidden_units = down_ref.shape[0]
    for index in range(2 * PARTS):
        size = rows // PARTS
        x_all[index * size : (index + 1) * size, :] = x_refs[index][...]
    g_all[:rows, :] = g_own_ref[...]
    g_all[rows:, :] = g_peer_ref[...]
    x_turned[...] = x_all[...].T
    for begin in range(0, hidden_units, STEP):
        columns = slice(begin, begin + STEP)
        for top in range(0, 2 * rows, rows):
            span = slice(top, top + rows)
            v = mul(x_all[span, :], up_ref[:, columns])
            grad = mul(g_all[span, :], down_ref[columns, :], 1, 1)
            square = v * v
            half = 0.5 + 0.5 * jnp.tanh(v * (CURVE + (CURVE * 0.044715) * square))
            act = v * half
            slope = half + act * (1.0 - half) * (2.0 * CURVE + (6.0 * CURVE * 0.044715) * square)
            active[span, columns] = act.astype(bfloat)
            grad_hidden[span, columns] = (grad * slope).astype(bfloat)
    out_own = mul(active[:rows, :], down_ref[...])
    out_peer = mul(active[rows:, :], down_ref[...])
    norm_own = mul(grad_hidden[:rows, :], up_ref[...], 1, 1)
    norm_peer = mul(grad_hidden[rows:, :], up_ref[...], 1, 1)
    if second:
        out_own = out_own + keep_out_a[...]
        out_peer = out_peer + send_out_a[...].astype(single)
        norm_own = norm_own + keep_norm_a[...]
        norm_peer = norm_peer + send_norm_a[...].astype(single)
    keep_out_ref[...] = out_own
    send_out_ref[...] = out_peer.astype(bfloat)
    keep_norm_ref[...] = norm_own
    send_norm_ref[...] = norm_peer.astype(bfloat)
    size = hidden_units // 2
    for begin in range(0, hidden_units, size):
        columns = slice(begin, begin + size)
        down_grad_ref[columns, :] = mul(active[:, columns], g_all[...], 0, 0).astype(down_grad_ref.dtype)
        up_grad_ref[columns, :] = mul(x_turned[columns, :], grad_hidden[...])
    if second:
        low, high = part_rows(upper_ref, size)
        kept_ref[:size, :] = up_mine_ref[low, :]
        kept_ref[size:, :] = up_grad_ref[low, :]
        sent_ref[:size, :] = up_mine_ref[high, :].astype(bfloat)
        sent_ref[size:, :] = up_grad_ref[high, :].astype(bfloat)


def mlp(x_own, x_peer, g_own, g_peer, up, down, before=(), parted=()):
    rows, width = g_own.shape
    units = down.shape[0]
    outs = [((rows, width), single), ((rows, width), bfloat)] * 2
    scratch = [
        pltpu.VMEM((2 * rows, width), bfloat),
        pltpu.VMEM((2 * rows, width), bfloat),
        pltpu.VMEM((width, 2 * rows), bfloat),
        pltpu.VMEM((2 * rows, units), bfloat),
        pltpu.VMEM((2 * rows, units), bfloat),
    ]
    if before:
        outs += [((units, width), bfloat), ((width, units), single), ((width, units), bfloat)]
        scratch.append(pltpu.VMEM((width, units), single))
    else:
        outs += [((units, width), single), ((width, units), single)]
    operands = (*parted, *x_own, *x_peer, g_own, g_peer, up, down, *before)
    return call(functools.partial(mlp_body, bool(before)), outs, operands, scratch, min(1, len(parted)), vmem=60)


def shards(
    inputs,
    history,
    cotangent,
    qkv_weight,
    out_weight,
    up_weight,
    down_weight,
    gain_attn,
    gain_mlp,
    dwa_weights,
):
    rows, width = inputs.shape
    members = lax.axis_size("mp")
    copies = lax.axis_size("dp")
    bits = copies.bit_length() - 1
    core = lax.rem(lax.axis_index("mp"), 2).astype(jnp.int32).reshape(1)
    copy_index = lax.axis_index("dp").astype(jnp.int32).reshape(1)
    core_pairs = [(i, i ^ 1) for i in range(members)]
    chip_pairs = [(i, i ^ 2) for i in range(members)]
    depth = history.shape[0]
    part = out_weight.shape[0]

    def other_core(value):
        return lax.ppermute(value, "mp", core_pairs)

    def other_chip(value):
        return lax.ppermute(value, "mp", chip_pairs)

    def other_copy(value, bit):
        return lax.ppermute(value, "dp", [(i, i ^ (1 << bit)) for i in range(copies)])

    uppers = [(copy_index >> bit) & 1 for bit in range(bits)]
    cosine, sine = (jnp.asarray(table) for table in tables())

    qkv_own = qkv_weight.transpose(1, 2, 0).reshape(3 * part, width)
    share = width // copies
    up_share = lax.dynamic_slice_in_dim(up_weight, copy_index[0] * share, share, 0)
    up_share = other_chip(up_share)
    up_peer = lax.all_gather(up_share, "dp", axis=0, tiled=True)

    full = (rows, width)
    (x_own,) = call(norm_body, [(full, bfloat)], (inputs, gain_attn))
    (both_own,) = call(
        join_body, [((4 * part, width), bfloat)], (qkv_own, out_weight), after=(x_own, up_share), vmem=60
    )
    both_peer = other_chip(both_own)
    x_peer = other_core(x_own)
    history_grad, mixed, g_own, history_parts = average_history(dwa_weights, history, cotangent, (both_own,))
    g_peer = other_core(g_own)

    tokens = pltpu.VMEM((SEQ, width), bfloat)
    first_outs = [
        ((3 * part, SEQ), bfloat), ((part, SEQ), bfloat), ((SEQ, part), bfloat), ((8, SEQ), single),
    ]
    qkv_a, att_a, nat_a, log_a, down_copy = call(
        attend_copy,
        first_outs + [(down_weight.shape, bfloat)],
        (core, x_own, x_peer, both_own, cosine, sine, down_weight),
        [tokens],
        1,
        (history_parts,),
        32,
    )
    down_peer = other_chip(down_copy)
    qkv_b, att_b, nat_b, log_b = call(
        attend, first_outs, (core, x_own, x_peer, both_peer, cosine, sine), [tokens], 1, (log_a,), 32
    )
    third = (rows // PARTS, width)
    keep, *send = call(
        branch_body,
        [(full, single)] + [(third, bfloat)] * PARTS,
        (core, nat_a, nat_b, both_own, both_peer),
        scalars=1,
    )
    recv = [other_core(value) for value in send]
    middle, *y_own = call(
        middle_body, [(full, single)] + [(third, bfloat)] * PARTS, (inputs, keep, gain_mlp, *recv)
    )
    y_peer = [other_core(value) for value in y_own]

    first = mlp(y_own, y_peer, g_own, g_peer, up_weight, down_weight)
    down_mine, up_mine = first[4:]
    second = mlp(
        y_own, y_peer, g_own, g_peer, up_peer, down_peer, (first[0], first[2], first[1], first[3]),
        (uppers[1], up_mine),
    )
    keep_out, send_out, keep_norm, send_norm, down_theirs, up_kept, up_sent = second
    half = (width // 2, width)
    square = (width, width)

    token = [keep_norm]

    def step(body, outs, operands, scalars=0, scratch=(), vmem=16, flops=MUCH):
        results = call(body, outs, operands, scratch, scalars, tuple(token), vmem, flops)
        token[0] = results[0]
        return results

    def halve(bit, mine, come):
        shape = (mine.shape[0] // 2, width)
        return step(halve_body, [(shape, single), (shape, bfloat)], (uppers[bit], mine, come), 1)

    def low(mine, come):
        return step(low_body, [(mine.shape, bfloat)], (mine, come))[0]

    def order(bit, mine, come, kind):
        shape = (2 * mine.shape[0], width)
        return step(order_body, [(shape, kind)], (uppers[bit], mine, come), 1)[0]

    down_come = other_chip(down_theirs)
    up_come = other_copy(up_sent, 1)
    grad_middle, gb_own, gain_mlp_part = step(
        middle_back_body,
        [(full, single), (full, bfloat), ((1, width), single)],
        (dwa_weights, middle, keep_norm, other_core(send_norm), cotangent, gain_mlp),
        1,
        flops=0,
    )
    gb_peer = other_core(gb_own)
    back_scratch = [tokens, tokens, pltpu.VMEM((3 * part, SEQ), bfloat)]
    att_theirs, before = step(
        functools.partial(attend_back, False),
        [((4 * part, width), bfloat), ((SEQ, width), single)],
        (core, gb_own, gb_peer, x_own, x_peer, both_peer, qkv_b, att_b, log_b, cosine, sine),
        1,
        back_scratch,
        60,
        0,
    )
    att_come = other_chip(att_theirs)
    down, sent = halve(0, down_mine, down_come)
    down_come = other_copy(sent, 0)
    up, sent = step(cross_body, [(half, single), (half, bfloat)], (up_kept, up_come))
    up_come = other_chip(sent)
    att_mine, keep_first, send_first, gain_attn_part = step(
        functools.partial(attend_back, True),
        [((4 * part, width), single), (full, single), (full, bfloat), ((1, width), single)],
        (
            core, gb_own, gb_peer, x_own, x_peer, both_own, qkv_a, att_a, log_a, cosine, sine,
            before, gain_attn,
        ),
        1,
        back_scratch + [pltpu.VMEM((SEQ, width), single)],
        60,
    )

    done = {}

    def chain(name, first_bit, second_bit, value, come, begun, extra=()):
        if not begun:
            value, sent = halve(first_bit, value, come)
            come = other_copy(sent, first_bit)
            yield
        if not extra:
            value, sent = halve(second_bit, value, come)
        else:
            shape = ((value.shape[0] + EXTRA) // 2, width)
            value, sent = step(
                halve_more_body,
                [(shape, single), (shape, bfloat)],
                (uppers[second_bit], value, come, *extra),
                1,
                [pltpu.VMEM((2 * shape[0], width), single)],
            )
        come = other_copy(sent, second_bit)
        yield
        for bit in range(2, bits):
            value = low(value, come)
            come = other_copy(value, bit)
            yield
        value = low(value, come)
        come = other_copy(value, second_bit)
        yield
        value = order(second_bit, value, come, bfloat)
        come = other_copy(value, first_bit)
        yield
        done[name] = (value, come)

    small = []
    chains = {
        "d": chain("d", 0, 1, down, down_come, True),
        "u": chain("u", 1, 0, up, up_come, True, small),
        "a": chain("a", 0, 1, att_mine, att_come, False),
    }

    def advance(names):
        for name in names:
            next(chains[name], None)

    advance("da")
    combined, dwa_part = step(
        combine_body,
        [(full, bfloat), ((depth + 1, width), single)],
        (dwa_weights, mixed, middle, keep_out, other_core(send_out), cotangent, history_parts),
        1,
        vmem=60,
    )
    extra_rows = depth + 3
    (part_sums,) = step(
        small_body, [((extra_rows, width), single)], (gain_attn_part, gain_mlp_part, dwa_part)
    )
    core_sums = other_core(part_sums)
    advance("d")
    (part_sums,) = step(add_body, [(part_sums.shape, single)], (part_sums, core_sums))
    small += [part_sums, other_chip(part_sums)]
    (input_grad,) = step(
        first_back_body,
        [(full, bfloat)],
        (inputs, keep_first, other_core(send_first), grad_middle, gain_attn),
        vmem=60,
    )
    advance("uadauda")
    for name in "dua":
        for _ in range(bits + 4):
            next(chains[name], None)
    down_grad = order(0, *done["d"], single)
    up_grad, small = step(
        order_more_body, [(square, single), ((extra_rows, width), single)], (uppers[1], *done["u"]), 1
    )
    qkv_grad, out_grad = step(
        order_two_body,
        [((3 * part, width), single), ((part, width), single)],
        (uppers[0], *done["a"]),
        1,
        [pltpu.VMEM(square, single)],
    )

    return (
        combined,
        input_grad,
        history_grad,
        qkv_grad.reshape(3, part, width).transpose(2, 0, 1),
        out_grad,
        up_grad,
        down_grad,
        small[0],
        small[1],
        jnp.sum(small[2:], axis=1),
    )


def solution(mesh):
    placed = (
        P(("dp", "mp"), None),
        P(None, ("dp", "mp"), None),
        P(("dp", "mp"), None),
        P(None, None, "mp"),
        P("mp", None),
        P(None, "mp"),
        P("mp", None),
        P(),
        P(),
        P(),
    )
    return jax.shard_map(
        shards,
        mesh=mesh,
        in_specs=placed,
        out_specs=(
            P(("dp", "mp"), None),
            P(("dp", "mp"), None),
            P(None, ("dp", "mp"), None),
            P(None, None, "mp"),
            P("mp", None),
            P(None, "mp"),
            P("mp", None),
            P(),
            P(),
            P(),
        ),
        check_vma=False,
    )
```

```python
import functools

import jax
import jax.numpy as jnp
import numpy as np
from jax import lax
from jax.experimental import pallas as pl
from jax.experimental.pallas import tpu as pltpu
from jax.sharding import PartitionSpec as P

DH = 64
SEQ = 1152
HALF = SEQ // 2
EPS = 1e-05
bfloat = jnp.bfloat16
single = jnp.float32
MIB = 1 << 20
MUCH = 10**11


def tables():
    half_width = DH // 2
    places = np.arange(SEQ, dtype=np.float32)
    frequency = np.float32(10000.0) ** (-np.arange(half_width, dtype=np.float32) * np.float32(2.0 / DH))
    angles = frequency[:, None] * places[None, :]
    return (np.cos(angles).astype(np.float32), np.sin(angles).astype(np.float32))


def mul(a, b, ca=1, cb=0):
    return lax.dot_general(a, b, (((ca,), (cb,)), ((), ())), preferred_element_type=single)


def call(kernel, outs, operands, scratch=(), scalars=0, after=(), vmem=16, flops=0, far=0, far_outs=0):
    count, waits = len(operands), len(after)

    def body(*refs):
        kernel(*refs[:count], *refs[count + waits :])

    small = pl.BlockSpec(memory_space=pltpu.SMEM)
    whole = pl.BlockSpec(memory_space=pltpu.VMEM)
    apart = pl.BlockSpec(memory_space=pl.ANY)
    return pl.pallas_call(
        body,
        out_shape=[jax.ShapeDtypeStruct(shape, kind) for shape, kind in outs],
        in_specs=[small] * scalars + [whole] * (count - scalars - far) + [apart] * (far + waits),
        out_specs=[whole] * (len(outs) - far_outs) + [apart] * far_outs,
        scratch_shapes=list(scratch),
        compiler_params=pltpu.CompilerParams(vmem_limit_bytes=vmem * MIB),
        cost_estimate=pl.CostEstimate(flops=flops, bytes_accessed=0, transcendentals=0),
    )(*operands, *after)


def move(marks, begin, *pairs):
    copies = [
        pltpu.make_async_copy(source, target, marks.at[begin + index])
        for index, (source, target) in enumerate(pairs)
    ]
    for copy in copies:
        copy.start()
    return copies


def wait(copies):
    for copy in copies:
        copy.wait()


ROWS = 64
PARTS = 3


def spans(rows, step=ROWS):
    return [slice(begin, begin + step) for begin in range(0, rows, step)]


def normal_of(x):
    centre = x - jnp.mean(x, axis=-1, keepdims=True)
    spread = jnp.mean(centre * centre, axis=-1, keepdims=True)
    scale = lax.rsqrt(spread + EPS)
    return centre * scale, scale


def join_body(first_ref, second_ref, out_ref, marks):
    size = first_ref.shape[0]
    wait(
        move(
            marks,
            0,
            (first_ref, out_ref.at[pl.ds(0, size), :]),
            (second_ref, out_ref.at[pl.ds(size, second_ref.shape[0]), :]),
        )
    )


def norm_body(x_ref, gain_ref, out_ref):
    gain = gain_ref[...].reshape(1, -1)
    for span in spans(x_ref.shape[0]):
        normal, _ = normal_of(x_ref[span, :].astype(single))
        out_ref[span, :] = (normal * gain).astype(bfloat)


def middle_body(x_ref, keep_ref, gain_ref, *rest):
    recv_refs, mid_ref, out_refs = rest[:PARTS], rest[PARTS], rest[PARTS + 1 :]
    gain = gain_ref[...].reshape(1, -1)
    rows = x_ref.shape[0] // PARTS
    for index in range(PARTS):
        for span in spans(rows):
            here = slice(index * rows + span.start, index * rows + span.stop)
            recv = recv_refs[index][span, :].astype(single)
            x = x_ref[here, :].astype(single) + (keep_ref[here, :] + recv)
            mid_ref[here, :] = x
            normal, _ = normal_of(x)
            out_refs[index][span, :] = (normal * gain).astype(bfloat)


def norm_back(x, grad, gain):
    normal, scale = normal_of(x)
    lifted = grad * gain
    back = scale * (
        lifted
        - jnp.mean(lifted, axis=-1, keepdims=True)
        - normal * jnp.mean(lifted * normal, axis=-1, keepdims=True)
    )
    return back, normal


def fold_rows(value):
    total = value[:8]
    for begin in range(8, value.shape[0], 8):
        total = total + value[begin : begin + 8]
    return total


def middle_back_body(mix_ref, x_ref, keep_ref, recv_ref, cot_ref, gain_ref, mid_ref, low_ref, part_ref):
    gain = gain_ref[...].reshape(1, -1)
    part = jnp.zeros((8, x_ref.shape[1]), single)
    for span in spans(x_ref.shape[0]):
        grad = keep_ref[span, :] + recv_ref[span, :].astype(single)
        back, normal = norm_back(x_ref[span, :], grad, gain)
        total = mix_ref[mix_ref.shape[0] - 1] * cot_ref[span, :] + back
        mid_ref[span, :] = total
        low_ref[span, :] = total.astype(bfloat)
        part = part + fold_rows(grad * normal)
    part_ref[...] = jnp.sum(part, axis=0, keepdims=True)


def first_back_body(x_ref, keep_ref, recv_ref, mid_ref, gain_ref, out_ref):
    gain = gain_ref[...].reshape(1, -1)
    for span in spans(x_ref.shape[0]):
        grad = keep_ref[span, :] + recv_ref[span, :].astype(single)
        back, _ = norm_back(x_ref[span, :].astype(single), grad, gain)
        out_ref[span, :] = (mid_ref[span, :] + back).astype(bfloat)


def history_body(mix_ref, history_ref, cot_ref, grad_ref, mixed_ref, low_ref, part_ref):
    depth = history_ref.shape[0]

    @pl.when(pl.program_id(0) == 0)
    def _():
        part_ref[...] = jnp.zeros_like(part_ref)

    for span in spans(cot_ref.shape[0], 32):
        cot = cot_ref[span, :]
        low_ref[span, :] = (mix_ref[depth] * cot).astype(bfloat)
        mixed = None
        for j in range(depth):
            layer = history_ref[j, span, :].astype(single)
            mixed = mix_ref[j] * layer if mixed is None else mixed + mix_ref[j] * layer
            grad_ref[j, span, :] = (mix_ref[j] * cot).astype(bfloat)
            part_ref[8 * j : 8 * j + 8, :] += fold_rows(layer * cot)
        mixed_ref[span, :] = mixed


def average_history(mix, history, cot, after=()):
    depth, rows, width = history.shape
    step = 96
    waits = len(after)

    def body(*refs):
        history_body(*refs[:3], *refs[3 + waits :])

    row_block = pl.BlockSpec((step, width), lambda i: (i, 0))
    deep_block = pl.BlockSpec((depth, step, width), lambda i: (0, i, 0))
    return pl.pallas_call(
        body,
        grid=(rows // step,),
        out_shape=[
            jax.ShapeDtypeStruct(history.shape, bfloat),
            jax.ShapeDtypeStruct((rows, width), single),
            jax.ShapeDtypeStruct((rows, width), bfloat),
            jax.ShapeDtypeStruct((8 * depth, width), single),
        ],
        in_specs=[pl.BlockSpec(memory_space=pltpu.SMEM), deep_block, row_block]
        + [pl.BlockSpec(memory_space=pl.ANY)] * waits,
        out_specs=[deep_block, row_block, row_block, pl.BlockSpec((8 * depth, width), lambda i: (0, 0))],
        compiler_params=pltpu.CompilerParams(vmem_limit_bytes=16 * MIB),
        cost_estimate=pl.CostEstimate(flops=0, bytes_accessed=0, transcendentals=0),
    )(mix, history, cot, *after)


def combine_body(mix_ref, mixed_ref, mid_ref, keep_ref, recv_ref, cot_ref, parts_ref, out_ref, part_ref):
    depth = mix_ref.shape[0] - 1
    last = jnp.zeros((8, mid_ref.shape[1]), single)
    for span in spans(mid_ref.shape[0]):
        outputs = mid_ref[span, :] + (keep_ref[span, :] + recv_ref[span, :].astype(single))
        out_ref[span, :] = (mixed_ref[span, :] + mix_ref[depth] * outputs).astype(bfloat)
        last = last + fold_rows(outputs * cot_ref[span, :])
    for j in range(depth):
        part_ref[j : j + 1, :] = jnp.sum(parts_ref[8 * j : 8 * j + 8, :], axis=0, keepdims=True)
    part_ref[depth : depth + 1, :] = jnp.sum(last, axis=0, keepdims=True)


def part_rows(upper_ref, size):
    low = pl.multiple_of(upper_ref[0] * size, size)
    high = pl.multiple_of((1 - upper_ref[0]) * size, size)
    return pl.ds(low, size), pl.ds(high, size)


def halve_body(upper_ref, mine_ref, come_ref, kept_ref, sent_ref):
    low, high = part_rows(upper_ref, kept_ref.shape[0])
    kept_ref[...] = mine_ref[low, :] + come_ref[low, :].astype(single)
    sent_ref[...] = (mine_ref[high, :] + come_ref[high, :].astype(single)).astype(bfloat)


def cross_body(kept_ref, come_ref, mine_ref, theirs_ref):
    size = mine_ref.shape[0]
    mine_ref[...] = kept_ref[:size, :] + come_ref[:size, :].astype(single)
    theirs_ref[...] = (kept_ref[size:, :] + come_ref[size:, :].astype(single)).astype(bfloat)


def low_body(mine_ref, come_ref, out_ref):
    out_ref[...] = (mine_ref[...].astype(single) + come_ref[...].astype(single)).astype(bfloat)


def gather(first_ref, second_ref, pieces, hold):
    size = pieces[0].shape[0]
    for index, piece in enumerate(pieces):
        first = first_ref[0] if index < 2 else 1 - first_ref[0]
        second = second_ref[0] if index % 2 == 0 else 1 - second_ref[0]
        hold[pl.ds(pl.multiple_of((2 * first + second) * size, size), size), :] = piece[...]


def whole_body(first_ref, second_ref, a_ref, b_ref, c_ref, d_ref, out_ref, hold):
    gather(first_ref, second_ref, (a_ref, b_ref, c_ref, d_ref), hold)
    out_ref[...] = hold[...].astype(single)


def two_body(first_ref, second_ref, a_ref, b_ref, c_ref, d_ref, top_ref, end_ref, hold):
    gather(first_ref, second_ref, (a_ref, b_ref, c_ref, d_ref), hold)
    rest = top_ref.shape[0]
    top_ref[...] = hold[:rest, :].astype(single)
    end_ref[...] = hold[rest:, :].astype(single)


EXTRA = 64


def halve_more_body(upper_ref, mine_ref, come_ref, extra_ref, more_ref, kept_ref, sent_ref, hold):
    rows, extra = mine_ref.shape[0], extra_ref.shape[0]
    hold[:rows, :] = mine_ref[...] + come_ref[...].astype(single)
    hold[rows:, :] = jnp.zeros((EXTRA, hold.shape[1]), single)
    hold[rows : rows + extra, :] = extra_ref[...] + more_ref[...]
    low, high = part_rows(upper_ref, kept_ref.shape[0])
    kept_ref[...] = hold[low, :]
    sent_ref[...] = hold[high, :].astype(bfloat)


def more_body(first_ref, second_ref, a_ref, b_ref, c_ref, d_ref, out_ref, small_ref, hold):
    gather(first_ref, second_ref, (a_ref, b_ref, c_ref, d_ref), hold)
    rows, extra = out_ref.shape[0] // 2, small_ref.shape[0]
    block = hold.shape[0] // 2
    out_ref[:rows, :] = hold[:rows, :].astype(single)
    out_ref[rows:, :] = hold[block : block + rows, :].astype(single)
    low = hold[rows:block, :].astype(single)
    high = hold[block + rows :, :].astype(single)
    small_ref[...] = low[:extra] + high[:extra]


def add_body(mine_ref, come_ref, out_ref):
    out_ref[...] = mine_ref[...] + come_ref[...]


def small_body(attn_ref, mlp_ref, dwa_ref, out_ref):
    out_ref[:1, :] = attn_ref[...]
    out_ref[1:2, :] = mlp_ref[...]
    out_ref[2:, :] = dwa_ref[...]


BLOCKS = tuple((begin, min(256, SEQ - begin)) for begin in range(0, SEQ, 256))


def place(core_ref, own_ref, peer_ref, whole):
    low = pl.multiple_of(core_ref[0] * HALF, HALF)
    high = pl.multiple_of((1 - core_ref[0]) * HALF, HALF)
    whole[pl.ds(low, HALF), :] = own_ref[...]
    whole[pl.ds(high, HALF), :] = peer_ref[...]
    return low, high


def allowed(size):
    key_pos = lax.broadcasted_iota(jnp.int32, (size, size), 0)
    query_pos = lax.broadcasted_iota(jnp.int32, (size, size), 1)
    return query_pos >= key_pos


def turn(rows, cosine, sine):
    half = rows.shape[0] // 2
    a, b = rows[:half], rows[half:]
    return jnp.concatenate([a * cosine - b * sine, b * cosine + a * sine], axis=0)


def attend_copy(*refs):
    attend(*refs[:6], *refs[7:11], refs[12])
    refs[11][...] = refs[6][...]


def attend(core_ref, own_ref, peer_ref, weight_ref, cos_ref, sin_ref, qkv_ref, att_ref, nat_ref, log_ref, tokens):
    place(core_ref, own_ref, peer_ref, tokens)
    width = weight_ref.shape[0] // 4
    projected = mul(weight_ref[: 3 * width, :], tokens[...], 1, 1)
    cosine, sine = cos_ref[...], sin_ref[...]
    for part in range(3):
        for head in range(width // DH):
            begin = part * width + head * DH
            rows = projected[begin : begin + DH]
            if part < 2:
                rows = turn(rows, cosine, sine)
            if part == 0:
                rows = rows * DH ** (-0.5)
            qkv_ref[begin : begin + DH, :] = rows.astype(bfloat)
    log_ref[...] = jnp.zeros_like(log_ref)
    for head in range(width // DH):
        base = head * DH
        keys = qkv_ref[width + base : width + base + DH, :].T
        for begin, size in BLOCKS:
            end = begin + size
            query = qkv_ref[base : base + DH, begin:end]
            scores = mul(keys[:end], query)
            corner = jnp.where(allowed(size), scores[begin:], -jnp.inf)
            top = jnp.max(corner, axis=0, keepdims=True)
            if begin:
                top = jnp.maximum(top, jnp.max(scores[:begin], axis=0, keepdims=True))
                scores = jnp.concatenate([scores[:begin], corner], axis=0)
            else:
                scores = corner
            weights = jnp.exp(scores - top)
            total = jnp.sum(weights, axis=0, keepdims=True)
            value = qkv_ref[2 * width + base : 2 * width + base + DH, :end]
            mixed = mul(value, weights.astype(bfloat)) / total
            att_ref[base : base + DH, begin:end] = mixed.astype(bfloat)
            log_ref[head : head + 1, begin:end] = top + jnp.log(total)
    nat_ref[...] = att_ref[...].T


def branch_body(core_ref, att_a_ref, att_b_ref, out_a_ref, out_b_ref, keep_ref, *send_refs):
    low = pl.multiple_of(core_ref[0] * HALF, HALF)
    rows = HALF // PARTS
    begin = out_a_ref.shape[0] - att_a_ref.shape[1]
    for index in range(PARTS):
        high = pl.multiple_of((1 - core_ref[0]) * HALF + index * rows, rows)
        send = mul(att_a_ref[pl.ds(high, rows), :], out_a_ref[begin:, :])
        send_refs[index][...] = (send + mul(att_b_ref[pl.ds(high, rows), :], out_b_ref[begin:, :])).astype(bfloat)
    keep = mul(att_a_ref[pl.ds(low, HALF), :], out_a_ref[begin:, :])
    keep_ref[...] = keep + mul(att_b_ref[pl.ds(low, HALF), :], out_b_ref[begin:, :])


def attend_back(
    core_ref, log_ref, cos_ref, sin_ref, grad_own_ref, grad_peer_ref, own_ref, peer_ref, weight_ref, qkv_ref, att_ref,
    out_ref, turned_ref, grads, tokens, weight, qkv, att, turned, result, marks,
):
    low = pl.multiple_of(core_ref[0] * HALF, HALF)
    high = pl.multiple_of((1 - core_ref[0]) * HALF, HALF)
    first = move(
        marks,
        0,
        (grad_own_ref, grads.at[pl.ds(low, HALF), :]),
        (grad_peer_ref, grads.at[pl.ds(high, HALF), :]),
        (weight_ref, weight),
        (att_ref, att),
        (qkv_ref, qkv),
    )
    later = move(
        marks, 5, (own_ref, tokens.at[pl.ds(low, HALF), :]), (peer_ref, tokens.at[pl.ds(high, HALF), :])
    )
    wait(first)
    width = att.shape[0]
    grad_att = mul(weight[3 * width :, :], grads[...], 1, 1).astype(bfloat)
    result[3 * width :, :] = mul(att[...], grads[...]).astype(result.dtype)
    cosine, sine = cos_ref[...], sin_ref[...]
    for head in range(width // DH):
        base = head * DH
        query = qkv[base : base + DH, :]
        key = qkv[width + base : width + base + DH, :]
        value = qkv[2 * width + base : 2 * width + base + DH, :]
        above = grad_att[base : base + DH]
        centre = jnp.sum(
            above.astype(single) * att[base : base + DH, :].astype(single), axis=0, keepdims=True
        )
        keys, values = key.T, value.T
        grad_query, grad_key, grad_value = [], None, None
        for begin, size in reversed(BLOCKS):
            end = begin + size
            scores = mul(keys[:end], query[:, begin:end])
            corner = jnp.where(allowed(size), scores[begin:], -jnp.inf)
            scores = jnp.concatenate([scores[:begin], corner], axis=0) if begin else corner
            probs = jnp.exp(scores - log_ref[head : head + 1, begin:end])
            grad_probs = mul(values[:end], above[:, begin:end])
            grad_scores = (probs * (grad_probs - centre[:, begin:end])).astype(bfloat)
            grad_query.insert(0, mul(key[:, :end], grad_scores))
            key_part = mul(query[:, begin:end], grad_scores, 1, 1)
            value_part = mul(above[:, begin:end], probs.astype(bfloat), 1, 1)
            if grad_key is None:
                grad_key, grad_value = key_part, value_part
            else:
                grad_key = jnp.concatenate([grad_key[:, :end] + key_part, grad_key[:, end:]], axis=1)
                grad_value = jnp.concatenate([grad_value[:, :end] + value_part, grad_value[:, end:]], axis=1)
        grad_query = jnp.concatenate(grad_query, axis=1) * DH ** (-0.5)
        turned[base : base + DH, :] = turn(grad_query, cosine, -sine).astype(bfloat)
        turned[width + base : width + base + DH, :] = turn(grad_key, cosine, -sine).astype(bfloat)
        turned[2 * width + base : 2 * width + base + DH, :] = grad_value.astype(bfloat)
    back = move(marks, 7, (turned, turned_ref))
    wait(later)
    result[: 3 * width, :] = mul(turned[...], tokens[...]).astype(result.dtype)
    wait(back + move(marks, 8, (result, out_ref)))


def first_grad_body(
    core_ref, gain_ref, turned_a_ref, turned_b_ref, weight_a_ref, weight_b_ref, own_ref, peer_ref,
    keep_ref, send_ref, part_ref, turned_a, turned_b, weight_a, weight_b, tokens, whole, marks,
):
    low = pl.multiple_of(core_ref[0] * HALF, HALF)
    high = pl.multiple_of((1 - core_ref[0]) * HALF, HALF)
    wait(
        move(
            marks,
            0,
            (turned_a_ref, turned_a),
            (weight_a_ref, weight_a),
            (turned_b_ref, turned_b),
            (weight_b_ref, weight_b),
            (own_ref, tokens.at[pl.ds(low, HALF), :]),
            (peer_ref, tokens.at[pl.ds(high, HALF), :]),
        )
    )
    depth = turned_a.shape[0]
    whole[...] = mul(turned_a[...], weight_a[:depth, :], 0, 0) + mul(turned_b[...], weight_b[:depth, :], 0, 0)
    keep_ref[...] = whole[pl.ds(low, HALF), :]
    send_ref[...] = whole[pl.ds(high, HALF), :].astype(bfloat)
    part = jnp.zeros((8, whole.shape[1]), single)
    for span in spans(whole.shape[0]):
        part = part + fold_rows(whole[span, :] * tokens[span, :].astype(single))
    part_ref[...] = jnp.sum(part, axis=0, keepdims=True) / gain_ref[...].reshape(1, -1)


CURVE = float(np.sqrt(2.0 / np.pi))
STEP = 256


def mlp_body(second, *refs):
    x_refs, refs = refs[: 2 * PARTS], refs[2 * PARTS :]
    g_own_ref, g_peer_ref, up_ref, down_ref = refs[:4]
    refs = refs[4:]
    if second:
        keep_a_ref, send_a_ref, send_ref, keep_ref, active_ref, hidden_ref = refs[:6]
        x_all, g_all, up, down, active, grad_hidden, keep, send, marks = refs[6:]
    else:
        send_ref, keep_ref, active_ref, hidden_ref, turned_ref = refs[:5]
        x_all, g_all, up, down, active, grad_hidden, keep, x_turned, marks = refs[5:]
    rows, size = x_all.shape[0] // 2, x_all.shape[0] // (2 * PARTS)
    units = down.shape[0]
    loads = move(
        marks,
        0,
        *[(x_refs[index], x_all.at[pl.ds(index * size, size), :]) for index in range(2 * PARTS)],
        (up_ref, up),
        (g_own_ref, g_all.at[pl.ds(0, rows), :]),
        (g_peer_ref, g_all.at[pl.ds(rows, rows), :]),
        (down_ref, down),
    )
    more = move(marks, 10, (keep_a_ref, keep), (send_a_ref, send)) if second else []
    wait(loads)
    for begin in range(0, units, STEP):
        columns = slice(begin, begin + STEP)
        for top in range(0, 2 * rows, rows):
            span = slice(top, top + rows)
            v = mul(x_all[span, :], up[:, columns])
            grad = mul(g_all[span, :], down[columns, :], 1, 1)
            square = v * v
            half = 0.5 + 0.5 * jnp.tanh(v * (CURVE + (CURVE * 0.044715) * square))
            act = v * half
            slope = half + act * (1.0 - half) * (2.0 * CURVE + (6.0 * CURVE * 0.044715) * square)
            active[span, columns] = act.astype(bfloat)
            grad_hidden[span, columns] = (grad * slope).astype(bfloat)
    stores = move(marks, 12, (active, active_ref), (grad_hidden, hidden_ref))
    wait(more)
    norm_own = mul(grad_hidden[:rows, :], up[...], 1, 1)
    keep[...] = norm_own + keep[...] if second else norm_own
    stores += move(marks, 14, (keep, keep_ref))
    norm_peer = mul(grad_hidden[rows:, :], up[...], 1, 1)
    if second:
        norm_peer = norm_peer + send[...].astype(single)
    else:
        x_turned[...] = x_all[...].T
        stores += move(marks, 15, (x_turned, turned_ref))
    send_ref[...] = norm_peer.astype(bfloat)
    wait(stores)


def mlp(x_own, x_peer, g_own, g_peer, up, down, before=(), after=()):
    rows, width = g_own.shape
    units = down.shape[0]
    tall = (2 * rows, width)
    outs = [
        ((rows, width), bfloat), ((rows, width), single), ((2 * rows, units), bfloat), ((2 * rows, units), bfloat),
    ]
    scratch = [
        pltpu.VMEM(tall, bfloat),
        pltpu.VMEM(tall, bfloat),
        pltpu.VMEM((width, units), bfloat),
        pltpu.VMEM((units, width), bfloat),
        pltpu.VMEM((2 * rows, units), bfloat),
        pltpu.VMEM((2 * rows, units), bfloat),
        pltpu.VMEM((rows, width), single),
    ]
    if before:
        scratch.append(pltpu.VMEM((rows, width), bfloat))
    else:
        outs.append(((width, 2 * rows), bfloat))
        scratch.append(pltpu.VMEM((width, 2 * rows), bfloat))
    operands = (*x_own, *x_peer, g_own, g_peer, up, down, *before)
    return call(
        functools.partial(mlp_body, bool(before)),
        outs,
        operands,
        scratch + [pltpu.SemaphoreType.DMA((16,))],
        after=after,
        vmem=60,
        far=len(operands),
        far_outs=len(outs) - 1,
    )


def theirs_body(
    active_ref, g_own_ref, g_peer_ref, hidden_ref, turned_ref, down_ref, up_ref,
    active, g_all, hidden, x_turned, down, up, marks,
):
    rows = g_own_ref.shape[0]
    first = move(
        marks,
        0,
        (active_ref, active),
        (g_own_ref, g_all.at[pl.ds(0, rows), :]),
        (g_peer_ref, g_all.at[pl.ds(rows, rows), :]),
    )
    later = move(marks, 3, (hidden_ref, hidden), (turned_ref, x_turned))
    wait(first)
    down[...] = mul(active[...], g_all[...], 0, 0).astype(bfloat)
    stores = move(marks, 5, (down, down_ref))
    wait(later)
    up[...] = mul(x_turned[...], hidden[...]).astype(bfloat)
    wait(stores + move(marks, 6, (up, up_ref)))


def mine_up_body(
    upper_ref, theirs_ref, hidden_ref, turned_ref, kept_ref, sent_ref, hidden, x_turned, mine, theirs, marks
):
    wait(move(marks, 0, (hidden_ref, hidden), (turned_ref, x_turned)))
    mine[...] = mul(x_turned[...], hidden[...])
    theirs[...] = theirs_ref[...].astype(single)
    size = mine.shape[0] // 2
    low, high = part_rows(upper_ref, size)
    kept_ref[:size, :] = mine[low, :]
    kept_ref[size:, :] = theirs[low, :]
    sent_ref[:size, :] = mine[high, :].astype(bfloat)
    sent_ref[size:, :] = theirs[high, :].astype(bfloat)


def mine_down_body(
    upper_ref, come_ref, active_ref, g_own_ref, g_peer_ref, kept_ref, sent_ref, active, g_all, total, marks
):
    rows = g_own_ref.shape[0]
    wait(
        move(
            marks,
            0,
            (active_ref, active),
            (g_own_ref, g_all.at[pl.ds(0, rows), :]),
            (g_peer_ref, g_all.at[pl.ds(rows, rows), :]),
        )
    )
    total[...] = mul(active[...], g_all[...], 0, 0) + come_ref[...].astype(single)
    low, high = part_rows(upper_ref, kept_ref.shape[0])
    kept_ref[...] = total[low, :]
    sent_ref[...] = total[high, :].astype(bfloat)


def outputs_body(
    active_a_ref, down_a_ref, active_b_ref, down_b_ref, keep_ref, send_ref, active_a, down_a, active_b, down_b, marks
):
    wait(
        move(
            marks,
            0,
            (active_a_ref, active_a),
            (down_a_ref, down_a),
            (active_b_ref, active_b),
            (down_b_ref, down_b),
        )
    )
    rows = keep_ref.shape[0]
    send = mul(active_a[rows:, :], down_a[...]) + mul(active_b[rows:, :], down_b[...])
    send_ref[...] = send.astype(bfloat)
    keep_ref[...] = mul(active_a[:rows, :], down_a[...]) + mul(active_b[:rows, :], down_b[...])


def shards(
    inputs,
    history,
    cotangent,
    qkv_weight,
    out_weight,
    up_weight,
    down_weight,
    gain_attn,
    gain_mlp,
    dwa_weights,
):
    rows, width = inputs.shape
    members = lax.axis_size("mp")
    copies = lax.axis_size("dp")
    bits = copies.bit_length() - 1
    core = lax.rem(lax.axis_index("mp"), 2).astype(jnp.int32).reshape(1)
    copy_index = lax.axis_index("dp").astype(jnp.int32).reshape(1)
    core_pairs = [(i, i ^ 1) for i in range(members)]
    chip_pairs = [(i, i ^ 2) for i in range(members)]
    depth = history.shape[0]
    part = out_weight.shape[0]

    def other_core(value):
        return lax.ppermute(value, "mp", core_pairs)

    def other_chip(value):
        return lax.ppermute(value, "mp", chip_pairs)

    def other_copy(value, bit):
        return lax.ppermute(value, "dp", [(i, i ^ (1 << bit)) for i in range(copies)])

    uppers = [(copy_index >> bit) & 1 for bit in range(bits)]
    cosine, sine = (jnp.asarray(table) for table in tables())

    qkv_own = qkv_weight.transpose(1, 2, 0).reshape(3 * part, width)
    share = width // copies
    up_share = lax.dynamic_slice_in_dim(up_weight, copy_index[0] * share, share, 0)
    up_share = other_chip(up_share)
    up_peer = lax.all_gather(up_share, "dp", axis=0, tiled=True)

    full = (rows, width)
    (x_own,) = call(norm_body, [(full, bfloat)], (inputs, gain_attn))
    (both_own,) = call(
        join_body,
        [((4 * part, width), bfloat)],
        (qkv_own, out_weight),
        [pltpu.SemaphoreType.DMA((2,))],
        after=(x_own, up_share),
        far=2,
        far_outs=1,
    )
    both_peer = other_chip(both_own)
    x_peer = other_core(x_own)
    history_grad, mixed, g_own, history_parts = average_history(dwa_weights, history, cotangent, (both_own,))
    g_peer = other_core(g_own)

    tokens = pltpu.VMEM((SEQ, width), bfloat)
    first_outs = [
        ((3 * part, SEQ), bfloat), ((part, SEQ), bfloat), ((SEQ, part), bfloat), ((8, SEQ), single),
    ]
    qkv_a, att_a, nat_a, log_a, down_copy = call(
        attend_copy,
        first_outs + [(down_weight.shape, bfloat)],
        (core, x_own, x_peer, both_own, cosine, sine, down_weight),
        [tokens],
        1,
        (history_parts,),
        32,
    )
    down_peer = other_chip(down_copy)
    qkv_b, att_b, nat_b, log_b = call(
        attend, first_outs, (core, x_own, x_peer, both_peer, cosine, sine), [tokens], 1, (log_a,), 32
    )
    third = (rows // PARTS, width)
    keep, *send = call(
        branch_body,
        [(full, single)] + [(third, bfloat)] * PARTS,
        (core, nat_a, nat_b, both_own, both_peer),
        scalars=1,
    )
    recv = [other_core(value) for value in send]
    middle, *y_own = call(
        middle_body, [(full, single)] + [(third, bfloat)] * PARTS, (inputs, keep, gain_mlp, *recv)
    )
    y_peer = [other_core(value) for value in y_own]

    square = (width, width)
    half = (width // 2, width)
    tall = (SEQ, width)
    marks = pltpu.SemaphoreType.DMA((16,))

    send_a, keep_a, active_a, hidden_a, x_turned = mlp(y_own, y_peer, g_own, g_peer, up_weight, down_weight)
    send_norm, keep_norm, active_b, hidden_b = mlp(
        y_own, y_peer, g_own, g_peer, up_peer, down_peer, (keep_a, send_a)
    )
    token = [send_norm]

    def step(body, outs, operands, scratch=(), scalars=0, vmem=16, flops=MUCH, far=0, far_outs=0):
        results = call(body, outs, operands, scratch, scalars, tuple(token), vmem, flops, far, far_outs)
        token[0] = results[0]
        return results

    down_theirs, up_theirs = step(
        theirs_body,
        [(square, bfloat)] * 2,
        (active_b, g_own, g_peer, hidden_b, x_turned),
        [pltpu.VMEM(tall, bfloat)] * 3
        + [pltpu.VMEM((width, SEQ), bfloat), pltpu.VMEM(square, bfloat), pltpu.VMEM(square, bfloat), marks],
        flops=0,
        vmem=60,
        far=5,
        far_outs=2,
    )
    down_come = other_chip(down_theirs)
    grad_middle, gb_own, gain_mlp_part = step(
        middle_back_body,
        [(full, single), (full, bfloat), ((1, width), single)],
        (dwa_weights, middle, keep_norm, other_core(send_norm), cotangent, gain_mlp),
        scalars=1,
        flops=0,
    )
    gb_peer = other_core(gb_own)
    up_kept, up_sent = step(
        mine_up_body,
        [(square, single), (square, bfloat)],
        (uppers[1], up_theirs, hidden_a, x_turned),
        [pltpu.VMEM(tall, bfloat), pltpu.VMEM((width, SEQ), bfloat), pltpu.VMEM(square, single)]
        + [pltpu.VMEM(square, single), marks],
        1,
        flops=0,
        vmem=60,
        far=2,
    )
    up_come = other_copy(up_sent, 1)

    def back(kind, weight, qkv, att, log, flops):
        return step(
            attend_back,
            [((4 * part, width), kind), ((3 * part, SEQ), bfloat)],
            (core, log, cosine, sine, gb_own, gb_peer, x_own, x_peer, weight, qkv, att),
            [
                pltpu.VMEM(tall, bfloat),
                pltpu.VMEM(tall, bfloat),
                pltpu.VMEM((4 * part, width), bfloat),
                pltpu.VMEM((3 * part, SEQ), bfloat),
                pltpu.VMEM((part, SEQ), bfloat),
                pltpu.VMEM((3 * part, SEQ), bfloat),
                pltpu.VMEM((4 * part, width), kind),
                marks,
            ],
            1,
            60,
            flops,
            7,
            2,
        )

    att_theirs, turned_b = back(bfloat, both_peer, qkv_b, att_b, log_b, 0)
    att_come = other_chip(att_theirs)
    att_mine, turned_a = back(single, both_own, qkv_a, att_a, log_a, MUCH)

    done = {}
    small = []

    def chain(name, first_bit, second_bit, value, come, begun):
        if not begun:
            shape = (value.shape[0] // 2, width)
            value, sent = step(
                halve_body, [(shape, single), (shape, bfloat)], (uppers[first_bit], value, come), scalars=1
            )
            come = other_copy(sent, first_bit)
            yield
        if name == "u":
            shape = ((value.shape[0] + EXTRA) // 2, width)
            value, sent = step(
                halve_more_body,
                [(shape, single), (shape, bfloat)],
                (uppers[second_bit], value, come, *small),
                [pltpu.VMEM((2 * shape[0], width), single)],
                1,
            )
        else:
            shape = (value.shape[0] // 2, width)
            value, sent = step(
                halve_body, [(shape, single), (shape, bfloat)], (uppers[second_bit], value, come), scalars=1
            )
        come = other_copy(sent, second_bit)
        yield
        for bit in range(2, bits):
            (value,) = step(low_body, [(shape, bfloat)], (value, come))
            come = other_copy(value, bit)
            yield
        (value,) = step(low_body, [(shape, bfloat)], (value, come))
        come = other_copy(value, second_bit)
        done[name] = (uppers[first_bit], uppers[second_bit], value, come) + (
            other_copy(value, first_bit), other_copy(come, first_bit),
        )
        yield

    down, sent = step(
        mine_down_body,
        [(half, single), (half, bfloat)],
        (uppers[0], down_come, active_a, g_own, g_peer),
        [pltpu.VMEM(tall, bfloat), pltpu.VMEM(tall, bfloat), pltpu.VMEM(square, single), marks],
        1,
        60,
        far=3,
    )
    down_come = other_copy(sent, 0)
    up, sent = step(cross_body, [(half, single), (half, bfloat)], (up_kept, up_come))
    up_come = other_chip(sent)
    chains = {
        "d": chain("d", 0, 1, down, down_come, True),
        "u": chain("u", 1, 0, up, up_come, True),
        "a": chain("a", 0, 1, att_mine, att_come, False),
    }

    def advance(names):
        for name in names:
            next(chains[name], None)

    keep_first, send_first, gain_attn_part = step(
        first_grad_body,
        [(full, single), (full, bfloat), ((1, width), single)],
        (core, gain_attn, turned_a, turned_b, both_own, both_peer, x_own, x_peer),
        [pltpu.VMEM((3 * part, SEQ), bfloat)] * 2
        + [pltpu.VMEM((4 * part, width), bfloat)] * 2
        + [pltpu.VMEM(tall, bfloat), pltpu.VMEM(tall, single), marks],
        1,
        60,
        far=6,
    )
    first_come = other_core(send_first)
    keep_out, send_out = step(
        outputs_body,
        [(full, single), (full, bfloat)],
        (active_a, down_weight, active_b, down_peer),
        [pltpu.VMEM(tall, bfloat), pltpu.VMEM(square, bfloat)] * 2 + [marks],
        vmem=60,
        far=4,
    )
    out_come = other_core(send_out)
    advance("ad")
    combined, dwa_part = step(
        combine_body,
        [(full, bfloat), ((depth + 1, width), single)],
        (dwa_weights, mixed, middle, keep_out, out_come, cotangent, history_parts),
        scalars=1,
        vmem=60,
    )
    extra_rows = depth + 3
    (part_sums,) = step(
        small_body, [((extra_rows, width), single)], (gain_attn_part, gain_mlp_part, dwa_part)
    )
    core_sums = other_core(part_sums)
    advance("d")
    (part_sums,) = step(add_body, [(part_sums.shape, single)], (part_sums, core_sums))
    small += [part_sums, other_chip(part_sums)]
    (input_grad,) = step(
        first_back_body, [(full, bfloat)], (inputs, keep_first, first_come, grad_middle, gain_attn), vmem=60
    )
    advance("auadu")
    for name in "dau":
        for _ in range(bits + 4):
            advance(name)
    (down_grad,) = step(whole_body, [(square, single)], done["d"], [pltpu.VMEM(square, bfloat)], 2)
    qkv_grad, out_grad = step(
        two_body,
        [((3 * part, width), single), ((part, width), single)],
        done["a"],
        [pltpu.VMEM(square, bfloat)],
        2,
    )
    up_grad, small = step(
        more_body,
        [(square, single), ((extra_rows, width), single)],
        done["u"],
        [pltpu.VMEM((width + 2 * EXTRA, width), bfloat)],
        2,
    )

    return (
        combined,
        input_grad,
        history_grad,
        qkv_grad.reshape(3, part, width).transpose(2, 0, 1),
        out_grad,
        up_grad,
        down_grad,
        small[0],
        small[1],
        jnp.sum(small[2:], axis=1),
    )


def solution(mesh):
    placed = (
        P(("dp", "mp"), None),
        P(None, ("dp", "mp"), None),
        P(("dp", "mp"), None),
        P(None, None, "mp"),
        P("mp", None),
        P(None, "mp"),
        P("mp", None),
        P(),
        P(),
        P(),
    )
    return jax.shard_map(
        shards,
        mesh=mesh,
        in_specs=placed,
        out_specs=(
            P(("dp", "mp"), None),
            P(("dp", "mp"), None),
            P(None, ("dp", "mp"), None),
            P(None, None, "mp"),
            P("mp", None),
            P(None, "mp"),
            P("mp", None),
            P(),
            P(),
            P(),
        ),
        check_vma=False,
    )
```

```python
import functools

import jax
import jax.numpy as jnp
import numpy as np
from jax import lax
from jax.experimental import pallas as pl
from jax.experimental.pallas import tpu as pltpu
from jax.sharding import PartitionSpec as P

DH = 64
SEQ = 1152
HALF = SEQ // 2
EPS = 1e-05
bfloat = jnp.bfloat16
single = jnp.float32
MIB = 1 << 20
MUCH = 10**11


def tables():
    half_width = DH // 2
    places = np.arange(SEQ, dtype=np.float32)
    frequency = np.float32(10000.0) ** (-np.arange(half_width, dtype=np.float32) * np.float32(2.0 / DH))
    angles = frequency[:, None] * places[None, :]
    return (np.cos(angles).astype(np.float32), np.sin(angles).astype(np.float32))


def mul(a, b, ca=1, cb=0):
    return lax.dot_general(a, b, (((ca,), (cb,)), ((), ())), preferred_element_type=single)


def call(kernel, outs, operands, scratch=(), scalars=0, after=(), vmem=16, flops=0, far=0, far_outs=0):
    count, waits = len(operands), len(after)

    def body(*refs):
        kernel(*refs[:count], *refs[count + waits :])

    small = pl.BlockSpec(memory_space=pltpu.SMEM)
    whole = pl.BlockSpec(memory_space=pltpu.VMEM)
    apart = pl.BlockSpec(memory_space=pl.ANY)
    return pl.pallas_call(
        body,
        out_shape=[jax.ShapeDtypeStruct(shape, kind) for shape, kind in outs],
        in_specs=[small] * scalars + [whole] * (count - scalars - far) + [apart] * (far + waits),
        out_specs=[whole] * (len(outs) - far_outs) + [apart] * far_outs,
        scratch_shapes=list(scratch),
        compiler_params=pltpu.CompilerParams(vmem_limit_bytes=vmem * MIB),
        cost_estimate=pl.CostEstimate(flops=flops, bytes_accessed=0, transcendentals=0),
    )(*operands, *after)


def move(marks, begin, *pairs):
    copies = [
        pltpu.make_async_copy(source, target, marks.at[begin + index])
        for index, (source, target) in enumerate(pairs)
    ]
    for copy in copies:
        copy.start()
    return copies


def wait(copies):
    for copy in copies:
        copy.wait()


ROWS = 64
PARTS = 3


def spans(rows, step=ROWS):
    return [slice(begin, begin + step) for begin in range(0, rows, step)]


def normal_of(x):
    centre = x - jnp.mean(x, axis=-1, keepdims=True)
    spread = jnp.mean(centre * centre, axis=-1, keepdims=True)
    scale = lax.rsqrt(spread + EPS)
    return centre * scale, scale


def join_body(first_ref, second_ref, out_ref, marks):
    size = first_ref.shape[0]
    wait(
        move(
            marks,
            0,
            (first_ref, out_ref.at[pl.ds(0, size), :]),
            (second_ref, out_ref.at[pl.ds(size, second_ref.shape[0]), :]),
        )
    )


def norm_body(x_ref, gain_ref, out_ref):
    gain = gain_ref[...].reshape(1, -1)
    for span in spans(x_ref.shape[0]):
        normal, _ = normal_of(x_ref[span, :].astype(single))
        out_ref[span, :] = (normal * gain).astype(bfloat)


def middle_body(x_ref, keep_ref, gain_ref, *rest):
    recv_refs, mid_ref, out_refs = rest[:PARTS], rest[PARTS], rest[PARTS + 1 :]
    gain = gain_ref[...].reshape(1, -1)
    rows = x_ref.shape[0] // PARTS
    for index in range(PARTS):
        for span in spans(rows):
            here = slice(index * rows + span.start, index * rows + span.stop)
            recv = recv_refs[index][span, :].astype(single)
            x = x_ref[here, :].astype(single) + (keep_ref[here, :] + recv)
            mid_ref[here, :] = x
            normal, _ = normal_of(x)
            out_refs[index][span, :] = (normal * gain).astype(bfloat)


def norm_back(x, grad, gain):
    normal, scale = normal_of(x)
    lifted = grad * gain
    back = scale * (
        lifted
        - jnp.mean(lifted, axis=-1, keepdims=True)
        - normal * jnp.mean(lifted * normal, axis=-1, keepdims=True)
    )
    return back, normal


def fold_rows(value):
    total = value[:8]
    for begin in range(8, value.shape[0], 8):
        total = total + value[begin : begin + 8]
    return total


def middle_back_body(mix_ref, x_ref, keep_ref, recv_ref, cot_ref, gain_ref, mid_ref, low_ref, part_ref):
    gain = gain_ref[...].reshape(1, -1)
    part = jnp.zeros((8, x_ref.shape[1]), single)
    for span in spans(x_ref.shape[0]):
        grad = keep_ref[span, :] + recv_ref[span, :].astype(single)
        back, normal = norm_back(x_ref[span, :], grad, gain)
        total = mix_ref[mix_ref.shape[0] - 1] * cot_ref[span, :] + back
        mid_ref[span, :] = total
        low_ref[span, :] = total.astype(bfloat)
        part = part + fold_rows(grad * normal)
    part_ref[...] = jnp.sum(part, axis=0, keepdims=True)


def first_back_body(x_ref, keep_ref, recv_ref, mid_ref, gain_ref, out_ref):
    gain = gain_ref[...].reshape(1, -1)
    for span in spans(x_ref.shape[0]):
        grad = keep_ref[span, :] + recv_ref[span, :].astype(single)
        back, _ = norm_back(x_ref[span, :].astype(single), grad, gain)
        out_ref[span, :] = (mid_ref[span, :] + back).astype(bfloat)


def history_body(mix_ref, history_ref, cot_ref, grad_ref, mixed_ref, low_ref, part_ref):
    depth = history_ref.shape[0]

    @pl.when(pl.program_id(0) == 0)
    def _():
        part_ref[...] = jnp.zeros_like(part_ref)

    for span in spans(cot_ref.shape[0], 32):
        cot = cot_ref[span, :]
        low_ref[span, :] = (mix_ref[depth] * cot).astype(bfloat)
        mixed = None
        for j in range(depth):
            layer = history_ref[j, span, :].astype(single)
            mixed = mix_ref[j] * layer if mixed is None else mixed + mix_ref[j] * layer
            grad_ref[j, span, :] = (mix_ref[j] * cot).astype(bfloat)
            part_ref[8 * j : 8 * j + 8, :] += fold_rows(layer * cot)
        mixed_ref[span, :] = mixed


def average_history(mix, history, cot, after=()):
    depth, rows, width = history.shape
    step = 96
    waits = len(after)

    def body(*refs):
        history_body(*refs[:3], *refs[3 + waits :])

    row_block = pl.BlockSpec((step, width), lambda i: (i, 0))
    deep_block = pl.BlockSpec((depth, step, width), lambda i: (0, i, 0))
    return pl.pallas_call(
        body,
        grid=(rows // step,),
        out_shape=[
            jax.ShapeDtypeStruct(history.shape, bfloat),
            jax.ShapeDtypeStruct((rows, width), single),
            jax.ShapeDtypeStruct((rows, width), bfloat),
            jax.ShapeDtypeStruct((8 * depth, width), single),
        ],
        in_specs=[pl.BlockSpec(memory_space=pltpu.SMEM), deep_block, row_block]
        + [pl.BlockSpec(memory_space=pl.ANY)] * waits,
        out_specs=[deep_block, row_block, row_block, pl.BlockSpec((8 * depth, width), lambda i: (0, 0))],
        compiler_params=pltpu.CompilerParams(vmem_limit_bytes=16 * MIB),
        cost_estimate=pl.CostEstimate(flops=0, bytes_accessed=0, transcendentals=0),
    )(mix, history, cot, *after)


def combine_body(mix_ref, mixed_ref, mid_ref, keep_ref, recv_ref, cot_ref, parts_ref, out_ref, part_ref):
    depth = mix_ref.shape[0] - 1
    last = jnp.zeros((8, mid_ref.shape[1]), single)
    for span in spans(mid_ref.shape[0]):
        outputs = mid_ref[span, :] + (keep_ref[span, :] + recv_ref[span, :].astype(single))
        out_ref[span, :] = (mixed_ref[span, :] + mix_ref[depth] * outputs).astype(bfloat)
        last = last + fold_rows(outputs * cot_ref[span, :])
    for j in range(depth):
        part_ref[j : j + 1, :] = jnp.sum(parts_ref[8 * j : 8 * j + 8, :], axis=0, keepdims=True)
    part_ref[depth : depth + 1, :] = jnp.sum(last, axis=0, keepdims=True)


def part_rows(upper_ref, size):
    low = pl.multiple_of(upper_ref[0] * size, size)
    high = pl.multiple_of((1 - upper_ref[0]) * size, size)
    return pl.ds(low, size), pl.ds(high, size)


def halve_body(upper_ref, mine_ref, come_ref, kept_ref, sent_ref):
    low, high = part_rows(upper_ref, kept_ref.shape[0])
    kept_ref[...] = mine_ref[low, :] + come_ref[low, :].astype(single)
    sent_ref[...] = (mine_ref[high, :] + come_ref[high, :].astype(single)).astype(bfloat)


def cross_body(kept_ref, come_ref, mine_ref, theirs_ref):
    size = mine_ref.shape[0]
    mine_ref[...] = kept_ref[:size, :] + come_ref[:size, :].astype(single)
    theirs_ref[...] = (kept_ref[size:, :] + come_ref[size:, :].astype(single)).astype(bfloat)


def low_body(mine_ref, come_ref, out_ref):
    out_ref[...] = (mine_ref[...].astype(single) + come_ref[...].astype(single)).astype(bfloat)


def gather(first_ref, second_ref, pieces, hold):
    size = pieces[0].shape[0]
    for index, piece in enumerate(pieces):
        first = first_ref[0] if index < 2 else 1 - first_ref[0]
        second = second_ref[0] if index % 2 == 0 else 1 - second_ref[0]
        hold[pl.ds(pl.multiple_of((2 * first + second) * size, size), size), :] = piece[...]


def whole_body(first_ref, second_ref, a_ref, b_ref, c_ref, d_ref, out_ref, hold):
    gather(first_ref, second_ref, (a_ref, b_ref, c_ref, d_ref), hold)
    out_ref[...] = hold[...].astype(single)


def two_body(first_ref, second_ref, a_ref, b_ref, c_ref, d_ref, top_ref, end_ref, hold):
    gather(first_ref, second_ref, (a_ref, b_ref, c_ref, d_ref), hold)
    rest = top_ref.shape[0]
    top_ref[...] = hold[:rest, :].astype(single)
    end_ref[...] = hold[rest:, :].astype(single)


EXTRA = 64


def halve_more_body(upper_ref, mine_ref, come_ref, extra_ref, more_ref, kept_ref, sent_ref, hold):
    rows, extra = mine_ref.shape[0], extra_ref.shape[0]
    hold[:rows, :] = mine_ref[...] + come_ref[...].astype(single)
    hold[rows:, :] = jnp.zeros((EXTRA, hold.shape[1]), single)
    hold[rows : rows + extra, :] = extra_ref[...] + more_ref[...]
    low, high = part_rows(upper_ref, kept_ref.shape[0])
    kept_ref[...] = hold[low, :]
    sent_ref[...] = hold[high, :].astype(bfloat)


def more_body(first_ref, second_ref, a_ref, b_ref, c_ref, d_ref, out_ref, small_ref, hold):
    gather(first_ref, second_ref, (a_ref, b_ref, c_ref, d_ref), hold)
    rows, extra = out_ref.shape[0] // 2, small_ref.shape[0]
    block = hold.shape[0] // 2
    out_ref[:rows, :] = hold[:rows, :].astype(single)
    out_ref[rows:, :] = hold[block : block + rows, :].astype(single)
    low = hold[rows:block, :].astype(single)
    high = hold[block + rows :, :].astype(single)
    small_ref[...] = low[:extra] + high[:extra]


def add_body(mine_ref, come_ref, out_ref):
    out_ref[...] = mine_ref[...] + come_ref[...]


def small_body(attn_ref, mlp_ref, dwa_ref, out_ref):
    out_ref[:1, :] = attn_ref[...]
    out_ref[1:2, :] = mlp_ref[...]
    out_ref[2:, :] = dwa_ref[...]


BLOCKS = tuple((begin, min(256, SEQ - begin)) for begin in range(0, SEQ, 256))


def place(core_ref, own_ref, peer_ref, whole):
    low = pl.multiple_of(core_ref[0] * HALF, HALF)
    high = pl.multiple_of((1 - core_ref[0]) * HALF, HALF)
    whole[pl.ds(low, HALF), :] = own_ref[...]
    whole[pl.ds(high, HALF), :] = peer_ref[...]
    return low, high


def allowed(size):
    key_pos = lax.broadcasted_iota(jnp.int32, (size, size), 0)
    query_pos = lax.broadcasted_iota(jnp.int32, (size, size), 1)
    return query_pos >= key_pos


def turn(rows, cosine, sine):
    half = rows.shape[0] // 2
    a, b = rows[:half], rows[half:]
    return jnp.concatenate([a * cosine - b * sine, b * cosine + a * sine], axis=0)


def attend_copy(*refs):
    attend(*refs[:6], *refs[7:11], refs[12])
    refs[11][...] = refs[6][...]


def attend(core_ref, own_ref, peer_ref, weight_ref, cos_ref, sin_ref, qkv_ref, att_ref, nat_ref, log_ref, tokens):
    place(core_ref, own_ref, peer_ref, tokens)
    width = weight_ref.shape[0] // 4
    projected = mul(weight_ref[: 3 * width, :], tokens[...], 1, 1)
    cosine, sine = cos_ref[...], sin_ref[...]
    for part in range(3):
        for head in range(width // DH):
            begin = part * width + head * DH
            rows = projected[begin : begin + DH]
            if part < 2:
                rows = turn(rows, cosine, sine)
            if part == 0:
                rows = rows * DH ** (-0.5)
            qkv_ref[begin : begin + DH, :] = rows.astype(bfloat)
    log_ref[...] = jnp.zeros_like(log_ref)
    for head in range(width // DH):
        base = head * DH
        keys = qkv_ref[width + base : width + base + DH, :].T
        for begin, size in BLOCKS:
            end = begin + size
            query = qkv_ref[base : base + DH, begin:end]
            scores = mul(keys[:end], query)
            corner = jnp.where(allowed(size), scores[begin:], -jnp.inf)
            top = jnp.max(corner, axis=0, keepdims=True)
            if begin:
                top = jnp.maximum(top, jnp.max(scores[:begin], axis=0, keepdims=True))
                scores = jnp.concatenate([scores[:begin], corner], axis=0)
            else:
                scores = corner
            weights = jnp.exp(scores - top)
            total = jnp.sum(weights, axis=0, keepdims=True)
            value = qkv_ref[2 * width + base : 2 * width + base + DH, :end]
            mixed = mul(value, weights.astype(bfloat)) / total
            att_ref[base : base + DH, begin:end] = mixed.astype(bfloat)
            log_ref[head : head + 1, begin:end] = top + jnp.log(total)
    nat_ref[...] = att_ref[...].T


def branch_body(core_ref, att_a_ref, att_b_ref, out_a_ref, out_b_ref, keep_ref, *send_refs):
    low = pl.multiple_of(core_ref[0] * HALF, HALF)
    rows = HALF // PARTS
    begin = out_a_ref.shape[0] - att_a_ref.shape[1]
    for index in range(PARTS):
        high = pl.multiple_of((1 - core_ref[0]) * HALF + index * rows, rows)
        send = mul(att_a_ref[pl.ds(high, rows), :], out_a_ref[begin:, :])
        send_refs[index][...] = (send + mul(att_b_ref[pl.ds(high, rows), :], out_b_ref[begin:, :])).astype(bfloat)
    keep = mul(att_a_ref[pl.ds(low, HALF), :], out_a_ref[begin:, :])
    keep_ref[...] = keep + mul(att_b_ref[pl.ds(low, HALF), :], out_b_ref[begin:, :])


def attend_back(
    second, core_ref, log_ref, cos_ref, sin_ref, *rest
):
    if second:
        gain_ref, rest = rest[0], rest[1:]
    grad_own_ref, grad_peer_ref, own_ref, peer_ref, weight_ref, qkv_ref, att_ref = rest[:7]
    rest = rest[7:]
    if second:
        turned_b_ref, weight_b_ref, send_ref, part_ref, out_ref, keep_ref = rest[:6]
        grads, tokens, weight, qkv, att, turned, result, marks, turned_b, weight_b, whole = rest[6:]
    else:
        out_ref, turned_ref, grads, tokens, weight, qkv, att, turned, result, marks = rest
    low = pl.multiple_of(core_ref[0] * HALF, HALF)
    high = pl.multiple_of((1 - core_ref[0]) * HALF, HALF)
    first = move(
        marks,
        0,
        (grad_own_ref, grads.at[pl.ds(low, HALF), :]),
        (grad_peer_ref, grads.at[pl.ds(high, HALF), :]),
        (weight_ref, weight),
        (att_ref, att),
        (qkv_ref, qkv),
    )
    later = move(
        marks, 5, (own_ref, tokens.at[pl.ds(low, HALF), :]), (peer_ref, tokens.at[pl.ds(high, HALF), :])
    )
    if second:
        later += move(marks, 7, (turned_b_ref, turned_b), (weight_b_ref, weight_b))
    wait(first)
    width = att.shape[0]
    grad_att = mul(weight[3 * width :, :], grads[...], 1, 1).astype(bfloat)
    result[3 * width :, :] = mul(att[...], grads[...]).astype(result.dtype)
    cosine, sine = cos_ref[...], sin_ref[...]
    for head in range(width // DH):
        base = head * DH
        query = qkv[base : base + DH, :]
        key = qkv[width + base : width + base + DH, :]
        value = qkv[2 * width + base : 2 * width + base + DH, :]
        above = grad_att[base : base + DH]
        centre = jnp.sum(
            above.astype(single) * att[base : base + DH, :].astype(single), axis=0, keepdims=True
        )
        keys, values, queries, aboves = key.T, value.T, query.T, above.T
        grad_query, grad_key, grad_value = [], None, None
        for begin, size in reversed(BLOCKS):
            end = begin + size
            scores = mul(keys[:end], query[:, begin:end])
            corner = jnp.where(allowed(size), scores[begin:], -jnp.inf)
            scores = jnp.concatenate([scores[:begin], corner], axis=0) if begin else corner
            probs = jnp.exp(scores - log_ref[head : head + 1, begin:end])
            grad_probs = mul(values[:end], above[:, begin:end])
            grad_scores = (probs * (grad_probs - centre[:, begin:end])).astype(bfloat)
            grad_query.insert(0, mul(key[:, :end], grad_scores))
            key_part = mul(grad_scores, queries[begin:end])
            value_part = mul(probs.astype(bfloat), aboves[begin:end])
            if grad_key is None:
                grad_key, grad_value = key_part, value_part
            else:
                grad_key = jnp.concatenate([grad_key[:end] + key_part, grad_key[end:]], axis=0)
                grad_value = jnp.concatenate([grad_value[:end] + value_part, grad_value[end:]], axis=0)
        grad_query = jnp.concatenate(grad_query, axis=1) * DH ** (-0.5)
        turned[base : base + DH, :] = turn(grad_query, cosine, -sine).astype(bfloat)
        turned[width + base : width + base + DH, :] = turn(grad_key.T, cosine, -sine).astype(bfloat)
        turned[2 * width + base : 2 * width + base + DH, :] = grad_value.T.astype(bfloat)
    stores = [] if second else move(marks, 10, (turned, turned_ref))
    wait(later)
    result[: 3 * width, :] = mul(turned[...], tokens[...]).astype(result.dtype)
    stores += move(marks, 11, (result, out_ref))
    if second:
        depth = 3 * width
        whole[...] = mul(turned[...], weight[:depth, :], 0, 0) + mul(turned_b[...], weight_b[:depth, :], 0, 0)
        stores += move(marks, 12, (whole.at[pl.ds(low, HALF), :], keep_ref))
        send_ref[...] = whole[pl.ds(high, HALF), :].astype(bfloat)
        part = jnp.zeros((8, whole.shape[1]), single)
        for span in spans(whole.shape[0]):
            part = part + fold_rows(whole[span, :] * tokens[span, :].astype(single))
        part_ref[...] = jnp.sum(part, axis=0, keepdims=True) / gain_ref[...].reshape(1, -1)
    wait(stores)


CURVE = float(np.sqrt(2.0 / np.pi))
STEP = 256


def mlp_body(second, *refs):
    if second:
        upper_ref, refs = refs[0], refs[1:]
    x_refs, refs = refs[: 2 * PARTS], refs[2 * PARTS :]
    g_own_ref, g_peer_ref, up_ref, down_ref = refs[:4]
    refs = refs[4:]
    if second:
        before_refs, up_mine_ref = refs[:4], refs[4]
        down_grad_ref, sent_ref, kept_ref = refs[9:12]
        refs = refs[5:9] + refs[12:]
    else:
        down_grad_ref, up_grad_ref = refs[4:6]
        refs = refs[:4] + refs[6:]
    send_norm_ref, keep_norm_ref, send_out_ref, keep_out_ref = refs[:4]
    x_all, g_all, up, down, active, grad_hidden, x_turned = refs[4:11]
    send_norm, keep_norm, send_out, keep_out, down_grad, up_grad, marks = refs[11:18]
    rows, size = x_all.shape[0] // 2, x_all.shape[0] // (2 * PARTS)
    units = down.shape[0]
    x_loads = move(
        marks, 0, *[(x_refs[index], x_all.at[pl.ds(index * size, size), :]) for index in range(2 * PARTS)]
    )
    loads = move(
        marks,
        6,
        (up_ref, up),
        (g_own_ref, g_all.at[pl.ds(0, rows), :]),
        (g_peer_ref, g_all.at[pl.ds(rows, rows), :]),
        (down_ref, down),
    )
    more, mine, stores = [], [], []
    if second:
        sent, up_mine = refs[18:]
        more = move(marks, 10, *zip(before_refs, (send_norm, keep_norm, send_out, keep_out)))
        mine = move(marks, 14, (up_mine_ref, up_mine))
    wait(x_loads)
    x_turned[...] = x_all[...].T
    wait(loads)
    for begin in range(0, units, STEP):
        columns = slice(begin, begin + STEP)
        for top in range(0, 2 * rows, rows):
            span = slice(top, top + rows)
            v = mul(x_all[span, :], up[:, columns])
            grad = mul(g_all[span, :], down[columns, :], 1, 1)
            square = v * v
            half = 0.5 + 0.5 * jnp.tanh(v * (CURVE + (CURVE * 0.044715) * square))
            act = v * half
            slope = half + act * (1.0 - half) * (2.0 * CURVE + (6.0 * CURVE * 0.044715) * square)
            active[span, columns] = act.astype(bfloat)
            grad_hidden[span, columns] = (grad * slope).astype(bfloat)

    def put(target, value):
        target[...] = (value + target[...].astype(single) if second else value).astype(target.dtype)

    wait(more)
    put(keep_norm, mul(grad_hidden[:rows, :], up[...], 1, 1))
    put(send_norm, mul(grad_hidden[rows:, :], up[...], 1, 1))
    stores += move(marks, 15, (keep_norm, keep_norm_ref), (send_norm, send_norm_ref))
    down_grad[...] = mul(active[...], g_all[...], 0, 0).astype(down_grad.dtype)
    stores += move(marks, 17, (down_grad, down_grad_ref))
    up_grad[...] = mul(x_turned[...], grad_hidden[...])
    if second:
        wait(mine)
        part = up_grad.shape[0] // 2
        low, high = part_rows(upper_ref, part)
        stores += move(
            marks,
            18,
            (up_mine.at[low, :], kept_ref.at[pl.ds(0, part), :]),
            (up_grad.at[low, :], kept_ref.at[pl.ds(part, part), :]),
        )
        sent[:part, :] = up_mine[high, :].astype(bfloat)
        sent[part:, :] = up_grad[high, :].astype(bfloat)
        stores += move(marks, 20, (sent, sent_ref))
    else:
        stores += move(marks, 18, (up_grad, up_grad_ref))
    put(keep_out, mul(active[:rows, :], down[...]))
    stores += move(marks, 21, (keep_out, keep_out_ref))
    put(send_out, mul(active[rows:, :], down[...]))
    wait(stores + move(marks, 22, (send_out, send_out_ref)))


def mlp(x_own, x_peer, g_own, g_peer, up, down, upper=(), before=(), flops=0):
    rows, width = g_own.shape
    units = down.shape[0]
    tall = (2 * rows, width)
    pair = [((rows, width), bfloat), ((rows, width), single)] * 2
    down_kind = bfloat if before else single
    outs = pair + [((units, width), down_kind)]
    outs += [((width, units), bfloat), ((width, units), single)] if before else [((width, units), single)]
    scratch = [
        pltpu.VMEM(tall, bfloat),
        pltpu.VMEM(tall, bfloat),
        pltpu.VMEM((width, units), bfloat),
        pltpu.VMEM((units, width), bfloat),
        pltpu.VMEM((2 * rows, units), bfloat),
        pltpu.VMEM((2 * rows, units), bfloat),
        pltpu.VMEM((width, 2 * rows), bfloat),
    ]
    scratch += [pltpu.VMEM(shape, kind) for shape, kind in pair]
    scratch += [
        pltpu.VMEM((units, width), down_kind), pltpu.VMEM((width, units), single), pltpu.SemaphoreType.DMA((24,)),
    ]
    if before:
        scratch += [pltpu.VMEM((width, units), bfloat), pltpu.VMEM((width, units), single)]
    operands = (*upper, *x_own, *x_peer, g_own, g_peer, up, down, *before)
    return call(
        functools.partial(mlp_body, bool(before)),
        outs,
        operands,
        scratch,
        len(upper),
        vmem=60,
        flops=flops,
        far=len(operands) - len(upper),
        far_outs=len(outs),
    )


def shards(
    inputs,
    history,
    cotangent,
    qkv_weight,
    out_weight,
    up_weight,
    down_weight,
    gain_attn,
    gain_mlp,
    dwa_weights,
):
    rows, width = inputs.shape
    members = lax.axis_size("mp")
    copies = lax.axis_size("dp")
    bits = copies.bit_length() - 1
    core = lax.rem(lax.axis_index("mp"), 2).astype(jnp.int32).reshape(1)
    copy_index = lax.axis_index("dp").astype(jnp.int32).reshape(1)
    core_pairs = [(i, i ^ 1) for i in range(members)]
    chip_pairs = [(i, i ^ 2) for i in range(members)]
    depth = history.shape[0]
    part = out_weight.shape[0]

    def other_core(value):
        return lax.ppermute(value, "mp", core_pairs)

    def other_chip(value):
        return lax.ppermute(value, "mp", chip_pairs)

    def other_copy(value, bit):
        return lax.ppermute(value, "dp", [(i, i ^ (1 << bit)) for i in range(copies)])

    uppers = [(copy_index >> bit) & 1 for bit in range(bits)]
    cosine, sine = (jnp.asarray(table) for table in tables())

    qkv_own = qkv_weight.transpose(1, 2, 0).reshape(3 * part, width)
    share = width // copies
    up_share = lax.dynamic_slice_in_dim(up_weight, copy_index[0] * share, share, 0)
    up_share = other_chip(up_share)
    up_peer = lax.all_gather(up_share, "dp", axis=0, tiled=True)

    full = (rows, width)
    (x_own,) = call(norm_body, [(full, bfloat)], (inputs, gain_attn))
    (both_own,) = call(
        join_body,
        [((4 * part, width), bfloat)],
        (qkv_own, out_weight),
        [pltpu.SemaphoreType.DMA((2,))],
        after=(x_own, up_share),
        far=2,
        far_outs=1,
    )
    both_peer = other_chip(both_own)
    x_peer = other_core(x_own)
    history_grad, mixed, g_own, history_parts = average_history(dwa_weights, history, cotangent, (both_own,))
    g_peer = other_core(g_own)

    tokens = pltpu.VMEM((SEQ, width), bfloat)
    first_outs = [
        ((3 * part, SEQ), bfloat), ((part, SEQ), bfloat), ((SEQ, part), bfloat), ((8, SEQ), single),
    ]
    qkv_a, att_a, nat_a, log_a, down_copy = call(
        attend_copy,
        first_outs + [(down_weight.shape, bfloat)],
        (core, x_own, x_peer, both_own, cosine, sine, down_weight),
        [tokens],
        1,
        (history_parts,),
        32,
    )
    down_peer = other_chip(down_copy)
    qkv_b, att_b, nat_b, log_b = call(
        attend, first_outs, (core, x_own, x_peer, both_peer, cosine, sine), [tokens], 1, (log_a,), 32
    )
    third = (rows // PARTS, width)
    keep, *send = call(
        branch_body,
        [(full, single)] + [(third, bfloat)] * PARTS,
        (core, nat_a, nat_b, both_own, both_peer),
        scalars=1,
    )
    recv = [other_core(value) for value in send]
    middle, *y_own = call(
        middle_body, [(full, single)] + [(third, bfloat)] * PARTS, (inputs, keep, gain_mlp, *recv)
    )
    y_peer = [other_core(value) for value in y_own]

    square = (width, width)
    half = (width // 2, width)
    tall = (SEQ, width)
    marks = pltpu.SemaphoreType.DMA((16,))

    first = mlp(y_own, y_peer, g_own, g_peer, up_weight, down_weight)
    down_mine, up_mine = first[4:]
    second = mlp(
        y_own, y_peer, g_own, g_peer, up_peer, down_peer, (uppers[1],), (*first[:4], up_mine)
    )
    send_norm, keep_norm, send_out, keep_out, down_theirs, up_sent, up_kept = second
    token = [send_norm]

    def step(body, outs, operands, scratch=(), scalars=0, vmem=16, flops=MUCH, far=0, far_outs=0):
        results = call(body, outs, operands, scratch, scalars, tuple(token), vmem, flops, far, far_outs)
        token[0] = results[0]
        return results

    down_come = other_chip(down_theirs)
    up_come = other_copy(up_sent, 1)
    out_come = other_core(send_out)
    grad_middle, gb_own, gain_mlp_part = step(
        middle_back_body,
        [(full, single), (full, bfloat), ((1, width), single)],
        (dwa_weights, middle, keep_norm, other_core(send_norm), cotangent, gain_mlp),
        scalars=1,
        flops=0,
    )
    gb_peer = other_core(gb_own)

    def back(second, kind, outs, operands, flops, far, scratch=()):
        return step(
            functools.partial(attend_back, second),
            outs,
            operands,
            [
                pltpu.VMEM(tall, bfloat),
                pltpu.VMEM(tall, bfloat),
                pltpu.VMEM((4 * part, width), bfloat),
                pltpu.VMEM((3 * part, SEQ), bfloat),
                pltpu.VMEM((part, SEQ), bfloat),
                pltpu.VMEM((3 * part, SEQ), bfloat),
                pltpu.VMEM((4 * part, width), kind),
                marks,
                *scratch,
            ],
            1,
            60,
            flops,
            far,
            2,
        )

    shared = (cosine, sine, gb_own, gb_peer, x_own, x_peer)
    att_theirs, turned_b = back(
        False,
        bfloat,
        [((4 * part, width), bfloat), ((3 * part, SEQ), bfloat)],
        (core, log_b, *shared, both_peer, qkv_b, att_b),
        0,
        7,
    )
    att_come = other_chip(att_theirs)
    down, sent = step(
        halve_body, [(half, single), (half, bfloat)], (uppers[0], down_mine, down_come), scalars=1
    )
    down_come = other_copy(sent, 0)
    send_first, gain_attn_part, att_mine, keep_first = back(
        True,
        single,
        [(full, bfloat), ((1, width), single), ((4 * part, width), single), (full, single)],
        (core, log_a, cosine, sine, gain_attn, *shared[2:], both_own, qkv_a, att_a, turned_b, both_peer),
        MUCH,
        9,
        [pltpu.VMEM((3 * part, SEQ), bfloat), pltpu.VMEM((4 * part, width), bfloat), pltpu.VMEM(tall, single)],
    )
    first_come = other_core(send_first)

    done = {}
    small = []

    def chain(name, first_bit, second_bit, value, come, begun):
        if not begun:
            shape = (value.shape[0] // 2, width)
            value, sent = step(
                halve_body, [(shape, single), (shape, bfloat)], (uppers[first_bit], value, come), scalars=1
            )
            come = other_copy(sent, first_bit)
            yield
        if name == "u":
            shape = ((value.shape[0] + EXTRA) // 2, width)
            value, sent = step(
                halve_more_body,
                [(shape, single), (shape, bfloat)],
                (uppers[second_bit], value, come, *small),
                [pltpu.VMEM((2 * shape[0], width), single)],
                1,
            )
        else:
            shape = (value.shape[0] // 2, width)
            value, sent = step(
                halve_body, [(shape, single), (shape, bfloat)], (uppers[second_bit], value, come), scalars=1
            )
        come = other_copy(sent, second_bit)
        yield
        for bit in range(2, bits):
            (value,) = step(low_body, [(shape, bfloat)], (value, come))
            come = other_copy(value, bit)
            yield
        (value,) = step(low_body, [(shape, bfloat)], (value, come))
        come = other_copy(value, second_bit)
        done[name] = (uppers[first_bit], uppers[second_bit], value, come) + (
            other_copy(value, first_bit), other_copy(come, first_bit),
        )
        yield

    up, sent = step(cross_body, [(half, single), (half, bfloat)], (up_kept, up_come))
    up_come = other_chip(sent)
    chains = {
        "d": chain("d", 0, 1, down, down_come, True),
        "u": chain("u", 1, 0, up, up_come, True),
        "a": chain("a", 0, 1, att_mine, att_come, False),
    }

    def advance(names):
        for name in names:
            next(chains[name], None)

    advance("ad")
    combined, dwa_part = step(
        combine_body,
        [(full, bfloat), ((depth + 1, width), single)],
        (dwa_weights, mixed, middle, keep_out, out_come, cotangent, history_parts),
        scalars=1,
        vmem=60,
    )
    extra_rows = depth + 3
    (part_sums,) = step(
        small_body, [((extra_rows, width), single)], (gain_attn_part, gain_mlp_part, dwa_part)
    )
    core_sums = other_core(part_sums)
    advance("d")
    (part_sums,) = step(add_body, [(part_sums.shape, single)], (part_sums, core_sums))
    small += [part_sums, other_chip(part_sums)]
    (input_grad,) = step(
        first_back_body, [(full, bfloat)], (inputs, keep_first, first_come, grad_middle, gain_attn), vmem=60
    )
    advance("auadu")
    for name in "dau":
        for _ in range(bits + 4):
            advance(name)
    (down_grad,) = step(whole_body, [(square, single)], done["d"], [pltpu.VMEM(square, bfloat)], 2)
    qkv_grad, out_grad = step(
        two_body,
        [((3 * part, width), single), ((part, width), single)],
        done["a"],
        [pltpu.VMEM(square, bfloat)],
        2,
    )
    up_grad, small = step(
        more_body,
        [(square, single), ((extra_rows, width), single)],
        done["u"],
        [pltpu.VMEM((width + 2 * EXTRA, width), bfloat)],
        2,
    )

    return (
        combined,
        input_grad,
        history_grad,
        qkv_grad.reshape(3, part, width).transpose(2, 0, 1),
        out_grad,
        up_grad,
        down_grad,
        small[0],
        small[1],
        jnp.sum(small[2:], axis=1),
    )


def solution(mesh):
    placed = (
        P(("dp", "mp"), None),
        P(None, ("dp", "mp"), None),
        P(("dp", "mp"), None),
        P(None, None, "mp"),
        P("mp", None),
        P(None, "mp"),
        P("mp", None),
        P(),
        P(),
        P(),
    )
    return jax.shard_map(
        shards,
        mesh=mesh,
        in_specs=placed,
        out_specs=(
            P(("dp", "mp"), None),
            P(("dp", "mp"), None),
            P(None, ("dp", "mp"), None),
            P(None, None, "mp"),
            P("mp", None),
            P(None, "mp"),
            P("mp", None),
            P(),
            P(),
            P(),
        ),
        check_vma=False,
    )
```

```python
import functools

import jax
import jax.numpy as jnp
import numpy as np
from jax import lax
from jax.experimental import pallas as pl
from jax.experimental.pallas import tpu as pltpu
from jax.sharding import PartitionSpec as P

DH = 64
SEQ = 1152
HALF = SEQ // 2
EPS = 1e-05
bfloat = jnp.bfloat16
single = jnp.float32
MIB = 1 << 20
MUCH = 10**11


def tables():
    half_width = DH // 2
    places = np.arange(SEQ, dtype=np.float32)
    frequency = np.float32(10000.0) ** (-np.arange(half_width, dtype=np.float32) * np.float32(2.0 / DH))
    angles = frequency[:, None] * places[None, :]
    return (np.cos(angles).astype(np.float32), np.sin(angles).astype(np.float32))


def mul(a, b, ca=1, cb=0):
    return lax.dot_general(a, b, (((ca,), (cb,)), ((), ())), preferred_element_type=single)


def call(kernel, outs, operands, scratch=(), scalars=0, after=(), vmem=16, flops=0, far=0, far_outs=0):
    count, waits = len(operands), len(after)

    def body(*refs):
        kernel(*refs[:count], *refs[count + waits :])

    small = pl.BlockSpec(memory_space=pltpu.SMEM)
    whole = pl.BlockSpec(memory_space=pltpu.VMEM)
    apart = pl.BlockSpec(memory_space=pltpu.HBM)
    loose = pl.BlockSpec(memory_space=pl.ANY)
    inner = len(outs) - far_outs
    return pl.pallas_call(
        body,
        out_shape=[jax.ShapeDtypeStruct(out[0], out[1]) for out in outs],
        in_specs=[small] * scalars + [whole] * (count - scalars - far) + [apart] * far + [loose] * waits,
        out_specs=[small if len(out) > 2 else whole for out in outs[:inner]] + [apart] * far_outs,
        scratch_shapes=list(scratch),
        compiler_params=pltpu.CompilerParams(vmem_limit_bytes=vmem * MIB),
        cost_estimate=pl.CostEstimate(flops=flops, bytes_accessed=0, transcendentals=0),
    )(*operands, *after)


class Mover:
    def __init__(self, marks):
        self.marks = marks
        self.used = 0

    def __call__(self, *pairs):
        copies = []
        for source, target in pairs:
            copies.append(pltpu.make_async_copy(source, target, self.marks.at[self.used]))
            self.used += 1
        for copy in copies:
            copy.start()
        return copies


def wait(copies):
    for copy in copies:
        copy.wait()


ROWS = 64
PARTS = 3


def spans(rows, step=ROWS):
    return [slice(begin, begin + step) for begin in range(0, rows, step)]


def normal_of(x):
    centre = x - jnp.mean(x, axis=-1, keepdims=True)
    spread = jnp.mean(centre * centre, axis=-1, keepdims=True)
    scale = lax.rsqrt(spread + EPS)
    return centre * scale, scale


def split_body(upper_ref, qkv_ref, out_ref, down_ref, both_half, down_half, marks):
    go = Mover(marks)
    upper = upper_ref[0]
    copies = []
    begin = 0
    for source, target in ((qkv_ref, both_half), (out_ref, both_half), (down_ref, down_half)):
        size = source.shape[0] // 2
        rows = pl.ds(pl.multiple_of(upper * size, size), size)
        begin = begin if source is out_ref else 0
        copies += go((source.at[rows, :], target.at[pl.ds(begin, size), :]))
        begin += size
    wait(copies)


def joined(upper, mine_ref, other_ref, begin, target):
    size = target.shape[0] // 2
    part = pl.ds(begin, size)
    return (
        (mine_ref.at[part, :], target.at[pl.ds(pl.multiple_of(upper * size, size), size), :]),
        (other_ref.at[part, :], target.at[pl.ds(pl.multiple_of((1 - upper) * size, size), size), :]),
    )


def norm_body(x_ref, gain_ref, out_ref):
    gain = gain_ref[...].reshape(1, -1)
    for span in spans(x_ref.shape[0]):
        normal, _ = normal_of(x_ref[span, :].astype(single))
        out_ref[span, :] = (normal * gain).astype(bfloat)


def middle_body(x_ref, keep_ref, gain_ref, *rest):
    recv_refs, mid_ref, out_refs = rest[:PARTS], rest[PARTS], rest[PARTS + 1 :]
    gain = gain_ref[...].reshape(1, -1)
    rows = x_ref.shape[0] // PARTS
    for index in range(PARTS):
        for span in spans(rows):
            here = slice(index * rows + span.start, index * rows + span.stop)
            recv = recv_refs[index][span, :].astype(single)
            x = x_ref[here, :].astype(single) + (keep_ref[here, :] + recv)
            mid_ref[here, :] = x
            normal, _ = normal_of(x)
            out_refs[index][span, :] = (normal * gain).astype(bfloat)


def norm_back(x, grad, gain):
    normal, scale = normal_of(x)
    lifted = grad * gain
    back = scale * (
        lifted
        - jnp.mean(lifted, axis=-1, keepdims=True)
        - normal * jnp.mean(lifted * normal, axis=-1, keepdims=True)
    )
    return back, normal


def fold_rows(value):
    total = value[:8]
    for begin in range(8, value.shape[0], 8):
        total = total + value[begin : begin + 8]
    return total


def middle_back_body(mix_ref, x_ref, keep_ref, recv_ref, cot_ref, gain_ref, mid_ref, low_ref, part_ref):
    gain = gain_ref[...].reshape(1, -1)
    part = jnp.zeros((8, x_ref.shape[1]), single)
    for span in spans(x_ref.shape[0]):
        grad = keep_ref[span, :] + recv_ref[span, :].astype(single)
        back, normal = norm_back(x_ref[span, :], grad, gain)
        total = mix_ref[mix_ref.shape[0] - 1] * cot_ref[span, :] + back
        mid_ref[span, :] = total
        low_ref[span, :] = total.astype(bfloat)
        part = part + fold_rows(grad * normal)
    part_ref[...] = jnp.sum(part, axis=0, keepdims=True)


def first_back_body(x_ref, keep_ref, recv_ref, mid_ref, gain_ref, out_ref):
    gain = gain_ref[...].reshape(1, -1)
    for span in spans(x_ref.shape[0]):
        grad = keep_ref[span, :] + recv_ref[span, :].astype(single)
        back, _ = norm_back(x_ref[span, :].astype(single), grad, gain)
        out_ref[span, :] = (mid_ref[span, :] + back).astype(bfloat)


def history_body(mix_ref, history_ref, cot_ref, grad_ref, mixed_ref, low_ref, part_ref):
    depth = history_ref.shape[0]

    @pl.when(pl.program_id(0) == 0)
    def _():
        part_ref[...] = jnp.zeros_like(part_ref)

    for span in spans(cot_ref.shape[0], 32):
        cot = cot_ref[span, :]
        low_ref[span, :] = (mix_ref[depth] * cot).astype(bfloat)
        mixed = None
        for j in range(depth):
            layer = history_ref[j, span, :].astype(single)
            mixed = mix_ref[j] * layer if mixed is None else mixed + mix_ref[j] * layer
            grad_ref[j, span, :] = (mix_ref[j] * cot).astype(bfloat)
            part_ref[8 * j : 8 * j + 8, :] += fold_rows(layer * cot)
        mixed_ref[span, :] = mixed


def average_history(mix, history, cot, after=()):
    depth, rows, width = history.shape
    step = 96
    waits = len(after)

    def body(*refs):
        history_body(*refs[:3], *refs[3 + waits :])

    row_block = pl.BlockSpec((step, width), lambda i: (i, 0))
    deep_block = pl.BlockSpec((depth, step, width), lambda i: (0, i, 0))
    return pl.pallas_call(
        body,
        grid=(rows // step,),
        out_shape=[
            jax.ShapeDtypeStruct(history.shape, bfloat),
            jax.ShapeDtypeStruct((rows, width), single),
            jax.ShapeDtypeStruct((rows, width), bfloat),
            jax.ShapeDtypeStruct((8 * depth, width), single),
        ],
        in_specs=[pl.BlockSpec(memory_space=pltpu.SMEM), deep_block, row_block]
        + [pl.BlockSpec(memory_space=pl.ANY)] * waits,
        out_specs=[deep_block, row_block, row_block, pl.BlockSpec((8 * depth, width), lambda i: (0, 0))],
        compiler_params=pltpu.CompilerParams(vmem_limit_bytes=16 * MIB),
        cost_estimate=pl.CostEstimate(flops=0, bytes_accessed=0, transcendentals=0),
    )(mix, history, cot, *after)


def combine_body(mix_ref, mixed_ref, mid_ref, keep_ref, recv_ref, cot_ref, parts_ref, out_ref, part_ref):
    depth = mix_ref.shape[0] - 1
    last = jnp.zeros((8, mid_ref.shape[1]), single)
    for span in spans(mid_ref.shape[0]):
        outputs = mid_ref[span, :] + (keep_ref[span, :] + recv_ref[span, :].astype(single))
        out_ref[span, :] = (mixed_ref[span, :] + mix_ref[depth] * outputs).astype(bfloat)
        last = last + fold_rows(outputs * cot_ref[span, :])
    for j in range(depth):
        part_ref[j : j + 1, :] = jnp.sum(parts_ref[8 * j : 8 * j + 8, :], axis=0, keepdims=True)
    part_ref[depth : depth + 1, :] = jnp.sum(last, axis=0, keepdims=True)


def part_rows(upper_ref, size):
    low = pl.multiple_of(upper_ref[0] * size, size)
    high = pl.multiple_of((1 - upper_ref[0]) * size, size)
    return pl.ds(low, size), pl.ds(high, size)


def halve_body(upper_ref, mine_ref, come_ref, kept_ref, sent_ref):
    low, high = part_rows(upper_ref, kept_ref.shape[0])
    kept_ref[...] = mine_ref[low, :] + come_ref[low, :].astype(single)
    sent_ref[...] = (mine_ref[high, :] + come_ref[high, :].astype(single)).astype(bfloat)


def cross_body(kept_ref, come_ref, mine_ref, theirs_ref):
    size = mine_ref.shape[0]
    mine_ref[...] = kept_ref[:size, :] + come_ref[:size, :].astype(single)
    theirs_ref[...] = (kept_ref[size:, :] + come_ref[size:, :].astype(single)).astype(bfloat)


def low_body(mine_ref, come_ref, out_ref):
    out_ref[...] = (mine_ref[...].astype(single) + come_ref[...].astype(single)).astype(bfloat)


def gather(first_ref, second_ref, pieces, hold):
    size = pieces[0].shape[0]
    for index, piece in enumerate(pieces):
        first = first_ref[0] if index < 2 else 1 - first_ref[0]
        second = second_ref[0] if index % 2 == 0 else 1 - second_ref[0]
        hold[pl.ds(pl.multiple_of((2 * first + second) * size, size), size), :] = piece[...]


def whole_body(first_ref, second_ref, a_ref, b_ref, c_ref, d_ref, out_ref, hold):
    gather(first_ref, second_ref, (a_ref, b_ref, c_ref, d_ref), hold)
    out_ref[...] = hold[...].astype(single)


def two_body(first_ref, second_ref, a_ref, b_ref, c_ref, d_ref, top_ref, end_ref, hold):
    gather(first_ref, second_ref, (a_ref, b_ref, c_ref, d_ref), hold)
    rest = top_ref.shape[0]
    top_ref[...] = hold[:rest, :].astype(single)
    end_ref[...] = hold[rest:, :].astype(single)


EXTRA = 64


def halve_more_body(upper_ref, mine_ref, come_ref, extra_ref, more_ref, kept_ref, sent_ref, hold):
    rows, extra = mine_ref.shape[0], extra_ref.shape[0]
    hold[:rows, :] = mine_ref[...] + come_ref[...].astype(single)
    hold[rows:, :] = jnp.zeros((EXTRA, hold.shape[1]), single)
    hold[rows : rows + extra, :] = extra_ref[...] + more_ref[...]
    low, high = part_rows(upper_ref, kept_ref.shape[0])
    kept_ref[...] = hold[low, :]
    sent_ref[...] = hold[high, :].astype(bfloat)


def more_body(first_ref, second_ref, a_ref, b_ref, c_ref, d_ref, out_ref, attn_ref, mlp_ref, dwa_ref, hold):
    gather(first_ref, second_ref, (a_ref, b_ref, c_ref, d_ref), hold)
    rows = out_ref.shape[0] // 2
    block = hold.shape[0] // 2
    out_ref[:rows, :] = hold[:rows, :].astype(single)
    out_ref[rows:, :] = hold[block : block + rows, :].astype(single)
    small = hold[rows:block, :].astype(single) + hold[block + rows :, :].astype(single)
    attn_ref[...] = small[0]
    mlp_ref[...] = small[1]
    for index in range(dwa_ref.shape[0]):
        dwa_ref[index] = jnp.sum(small[2 + index : 3 + index])


def add_body(mine_ref, come_ref, out_ref):
    out_ref[...] = mine_ref[...] + come_ref[...]


def small_body(attn_ref, mlp_ref, dwa_ref, out_ref):
    out_ref[:1, :] = attn_ref[...]
    out_ref[1:2, :] = mlp_ref[...]
    out_ref[2:, :] = dwa_ref[...]


BLOCKS = tuple((begin, min(256, SEQ - begin)) for begin in range(0, SEQ, 256))


def place(core_ref, own_ref, peer_ref, whole):
    low = pl.multiple_of(core_ref[0] * HALF, HALF)
    high = pl.multiple_of((1 - core_ref[0]) * HALF, HALF)
    whole[pl.ds(low, HALF), :] = own_ref[...]
    whole[pl.ds(high, HALF), :] = peer_ref[...]
    return low, high


def allowed(size):
    key_pos = lax.broadcasted_iota(jnp.int32, (size, size), 0)
    query_pos = lax.broadcasted_iota(jnp.int32, (size, size), 1)
    return query_pos >= key_pos


def turn(rows, cosine, sine):
    half = rows.shape[0] // 2
    a, b = rows[:half], rows[half:]
    return jnp.concatenate([a * cosine - b * sine, b * cosine + a * sine], axis=0)


def attend_own(
    core_ref, own_ref, peer_ref, cos_ref, sin_ref, weight_ref, qkv_ref, att_ref, nat_ref, log_ref, tokens
):
    place(core_ref, own_ref, peer_ref, tokens)
    attend(weight_ref, cos_ref, sin_ref, qkv_ref, att_ref, nat_ref, log_ref, tokens)


def attend_peer(
    core_ref, upper_ref, own_ref, peer_ref, cos_ref, sin_ref, mine_ref, other_ref, pass_ref,
    qkv_ref, att_ref, nat_ref, log_ref, weight_out, out_out, pass_out, tokens, weight, marks,
):
    go = Mover(marks)
    loads = go(*joined(upper_ref[0], mine_ref, other_ref, 0, weight))
    copies = go(*joined(upper_ref[0], mine_ref, other_ref, weight.shape[0] // 2, out_out), (pass_ref, pass_out))
    place(core_ref, own_ref, peer_ref, tokens)
    wait(loads)
    copies += go((weight, weight_out))
    attend(weight, cos_ref, sin_ref, qkv_ref, att_ref, nat_ref, log_ref, tokens)
    wait(copies)


def attend(weight_ref, cos_ref, sin_ref, qkv_ref, att_ref, nat_ref, log_ref, tokens):
    width = weight_ref.shape[0] // 3
    projected = mul(weight_ref[...], tokens[...], 1, 1)
    cosine, sine = cos_ref[...], sin_ref[...]
    for part in range(3):
        for head in range(width // DH):
            begin = part * width + head * DH
            rows = projected[begin : begin + DH]
            if part < 2:
                rows = turn(rows, cosine, sine)
            if part == 0:
                rows = rows * DH ** (-0.5)
            qkv_ref[begin : begin + DH, :] = rows.astype(bfloat)
    log_ref[...] = jnp.zeros_like(log_ref)
    for head in range(width // DH):
        base = head * DH
        keys = qkv_ref[width + base : width + base + DH, :].T
        for begin, size in BLOCKS:
            end = begin + size
            query = qkv_ref[base : base + DH, begin:end]
            scores = mul(keys[:end], query)
            corner = jnp.where(allowed(size), scores[begin:], -jnp.inf)
            top = jnp.max(corner, axis=0, keepdims=True)
            if begin:
                top = jnp.maximum(top, jnp.max(scores[:begin], axis=0, keepdims=True))
                scores = jnp.concatenate([scores[:begin], corner], axis=0)
            else:
                scores = corner
            weights = jnp.exp(scores - top)
            total = jnp.sum(weights, axis=0, keepdims=True)
            value = qkv_ref[2 * width + base : 2 * width + base + DH, :end]
            mixed = mul(value, weights.astype(bfloat)) / total
            att_ref[base : base + DH, begin:end] = mixed.astype(bfloat)
            log_ref[head : head + 1, begin:end] = top + jnp.log(total)
    nat_ref[...] = att_ref[...].T


def branch_body(core_ref, att_a_ref, att_b_ref, out_a_ref, out_b_ref, keep_ref, *send_refs):
    low = pl.multiple_of(core_ref[0] * HALF, HALF)
    rows = HALF // PARTS
    for index in range(PARTS):
        high = pl.multiple_of((1 - core_ref[0]) * HALF + index * rows, rows)
        send = mul(att_a_ref[pl.ds(high, rows), :], out_a_ref[...])
        send_refs[index][...] = (send + mul(att_b_ref[pl.ds(high, rows), :], out_b_ref[...])).astype(bfloat)
    keep = mul(att_a_ref[pl.ds(low, HALF), :], out_a_ref[...])
    keep_ref[...] = keep + mul(att_b_ref[pl.ds(low, HALF), :], out_b_ref[...])


def attend_back(
    second, core_ref, log_ref, cos_ref, sin_ref, *rest
):
    if second:
        gain_ref, rest = rest[0], rest[1:]
    grad_own_ref, grad_peer_ref, own_ref, peer_ref, weight_ref, out_weight_ref, qkv_ref, att_ref = rest[:8]
    rest = rest[8:]
    if second:
        turned_b_ref, weight_b_ref, send_ref, part_ref, out_ref, keep_ref = rest[:6]
        grads, tokens, weight, qkv, att, turned, result, marks, turned_b, weight_b, whole = rest[6:]
    else:
        out_ref, turned_ref, grads, tokens, weight, qkv, att, turned, result, marks = rest
    low = pl.multiple_of(core_ref[0] * HALF, HALF)
    high = pl.multiple_of((1 - core_ref[0]) * HALF, HALF)
    go = Mover(marks)
    depth = weight_ref.shape[0]
    first = go(
        (out_weight_ref, weight.at[pl.ds(depth, out_weight_ref.shape[0]), :]),
        (grad_own_ref, grads.at[pl.ds(low, HALF), :]),
        (grad_peer_ref, grads.at[pl.ds(high, HALF), :]),
        (att_ref, att),
        (qkv_ref, qkv),
    )
    later = go(
        (own_ref, tokens.at[pl.ds(low, HALF), :]),
        (peer_ref, tokens.at[pl.ds(high, HALF), :]),
        (weight_ref, weight.at[pl.ds(0, depth), :]),
    )
    if second:
        later += go((turned_b_ref, turned_b), (weight_b_ref, weight_b))
    wait(first)
    width = att.shape[0]
    grad_att = mul(weight[3 * width :, :], grads[...], 1, 1).astype(bfloat)
    result[3 * width :, :] = mul(att[...], grads[...]).astype(result.dtype)
    cosine, sine = cos_ref[...], sin_ref[...]
    for head in range(width // DH):
        base = head * DH
        query = qkv[base : base + DH, :]
        key = qkv[width + base : width + base + DH, :]
        value = qkv[2 * width + base : 2 * width + base + DH, :]
        above = grad_att[base : base + DH]
        centre = jnp.sum(
            above.astype(single) * att[base : base + DH, :].astype(single), axis=0, keepdims=True
        )
        keys, values, queries, aboves = key.T, value.T, query.T, above.T
        grad_query, grad_key, grad_value = [], None, None
        for begin, size in reversed(BLOCKS):
            end = begin + size
            scores = mul(keys[:end], query[:, begin:end])
            corner = jnp.where(allowed(size), scores[begin:], -jnp.inf)
            scores = jnp.concatenate([scores[:begin], corner], axis=0) if begin else corner
            probs = jnp.exp(scores - log_ref[head : head + 1, begin:end])
            grad_probs = mul(values[:end], above[:, begin:end])
            grad_scores = (probs * (grad_probs - centre[:, begin:end])).astype(bfloat)
            grad_query.insert(0, mul(key[:, :end], grad_scores))
            key_part = mul(grad_scores, queries[begin:end])
            value_part = mul(probs.astype(bfloat), aboves[begin:end])
            if grad_key is None:
                grad_key, grad_value = key_part, value_part
            else:
                grad_key = jnp.concatenate([grad_key[:end] + key_part, grad_key[end:]], axis=0)
                grad_value = jnp.concatenate([grad_value[:end] + value_part, grad_value[end:]], axis=0)
        grad_query = jnp.concatenate(grad_query, axis=1) * DH ** (-0.5)
        turned[base : base + DH, :] = turn(grad_query, cosine, -sine).astype(bfloat)
        turned[width + base : width + base + DH, :] = turn(grad_key.T, cosine, -sine).astype(bfloat)
        turned[2 * width + base : 2 * width + base + DH, :] = grad_value.T.astype(bfloat)
    stores = [] if second else go((turned, turned_ref))
    wait(later)
    result[: 3 * width, :] = mul(turned[...], tokens[...]).astype(result.dtype)
    stores += go((result, out_ref))
    if second:
        whole[...] = mul(turned[...], weight[:depth, :], 0, 0) + mul(turned_b[...], weight_b[...], 0, 0)
        stores += go((whole.at[pl.ds(low, HALF), :], keep_ref))
        send_ref[...] = whole[pl.ds(high, HALF), :].astype(bfloat)
        part = jnp.zeros((8, whole.shape[1]), single)
        for span in spans(whole.shape[0]):
            part = part + fold_rows(whole[span, :] * tokens[span, :].astype(single))
        part_ref[...] = jnp.sum(part, axis=0, keepdims=True) / gain_ref[...].reshape(1, -1)
    wait(stores)


CURVE = float(np.sqrt(2.0 / np.pi))
STEP = 256


def mlp_body(second, *refs):
    if second:
        upper_ref, other_upper_ref, refs = refs[0], refs[1], refs[2:]
    x_refs, refs = refs[: 2 * PARTS], refs[2 * PARTS :]
    g_own_ref, g_peer_ref, refs = refs[0], refs[1], refs[2:]
    if second:
        up_ref, down_refs = refs[0], refs[1:3]
        before_refs, up_mine_ref = refs[3:7], refs[7]
        down_grad_ref, sent_ref, kept_ref = refs[12:15]
        refs = refs[8:12] + refs[15:]
    else:
        up_ref, down_ref = refs[:2]
        down_grad_ref, up_grad_ref = refs[6:8]
        refs = refs[2:6] + refs[8:]
    send_norm_ref, keep_norm_ref, send_out_ref, keep_out_ref = refs[:4]
    x_all, g_all, up, down, active, grad_hidden, x_turned = refs[4:11]
    send_norm, keep_norm, send_out, keep_out, down_grad, up_grad, marks = refs[11:18]
    rows, size = x_all.shape[0] // 2, x_all.shape[0] // (2 * PARTS)
    units = down.shape[0]
    go = Mover(marks)
    x_loads = go(*[(x_refs[index], x_all.at[pl.ds(index * size, size), :]) for index in range(2 * PARTS)])
    if second:
        loads = go((up_ref, up), *joined(other_upper_ref[0], *down_refs, 0, down))
    else:
        loads = go((up_ref, up), (down_ref, down))
    loads += go((g_own_ref, g_all.at[pl.ds(0, rows), :]), (g_peer_ref, g_all.at[pl.ds(rows, rows), :]))
    more, mine, stores = [], [], []
    if second:
        sent, up_mine = refs[18:]
        more = go(*zip(before_refs, (send_norm, keep_norm, send_out, keep_out)))
        mine = go((up_mine_ref, up_mine))
    wait(x_loads)
    x_turned[...] = x_all[...].T
    wait(loads)
    for begin in range(0, units, STEP):
        columns = slice(begin, begin + STEP)
        for top in range(0, 2 * rows, rows):
            span = slice(top, top + rows)
            v = mul(x_all[span, :], up[:, columns])
            grad = mul(g_all[span, :], down[columns, :], 1, 1)
            square = v * v
            half = 0.5 + 0.5 * jnp.tanh(v * (CURVE + (CURVE * 0.044715) * square))
            act = v * half
            slope = half + act * (1.0 - half) * (2.0 * CURVE + (6.0 * CURVE * 0.044715) * square)
            active[span, columns] = act.astype(bfloat)
            grad_hidden[span, columns] = (grad * slope).astype(bfloat)

    def put(target, value):
        target[...] = (value + target[...].astype(single) if second else value).astype(target.dtype)

    wait(more)
    put(keep_norm, mul(grad_hidden[:rows, :], up[...], 1, 1))
    put(send_norm, mul(grad_hidden[rows:, :], up[...], 1, 1))
    stores += go((keep_norm, keep_norm_ref), (send_norm, send_norm_ref))
    down_grad[...] = mul(active[...], g_all[...], 0, 0).astype(down_grad.dtype)
    stores += go((down_grad, down_grad_ref))
    up_grad[...] = mul(x_turned[...], grad_hidden[...])
    if second:
        wait(mine)
        part = up_grad.shape[0] // 2
        low, high = part_rows(upper_ref, part)
        stores += go(
            (up_mine.at[low, :], kept_ref.at[pl.ds(0, part), :]),
            (up_grad.at[low, :], kept_ref.at[pl.ds(part, part), :]),
        )
        sent[:part, :] = up_mine[high, :].astype(bfloat)
        sent[part:, :] = up_grad[high, :].astype(bfloat)
        stores += go((sent, sent_ref))
    else:
        stores += go((up_grad, up_grad_ref))
    put(keep_out, mul(active[:rows, :], down[...]))
    stores += go((keep_out, keep_out_ref))
    put(send_out, mul(active[rows:, :], down[...]))
    wait(stores + go((send_out, send_out_ref)))


def mlp(x_own, x_peer, g_own, g_peer, up, down, upper=(), before=(), flops=0):
    rows, width = g_own.shape
    units = sum(piece.shape[0] for piece in down)
    tall = (2 * rows, width)
    pair = [((rows, width), bfloat), ((rows, width), single)] * 2
    down_kind = bfloat if before else single
    outs = pair + [((units, width), down_kind)]
    outs += [((width, units), bfloat), ((width, units), single)] if before else [((width, units), single)]
    scratch = [
        pltpu.VMEM(tall, bfloat),
        pltpu.VMEM(tall, bfloat),
        pltpu.VMEM((width, units), bfloat),
        pltpu.VMEM((units, width), bfloat),
        pltpu.VMEM((2 * rows, units), bfloat),
        pltpu.VMEM((2 * rows, units), bfloat),
        pltpu.VMEM((width, 2 * rows), bfloat),
    ]
    scratch += [pltpu.VMEM(shape, kind) for shape, kind in pair]
    scratch += [
        pltpu.VMEM((units, width), down_kind), pltpu.VMEM((width, units), single), pltpu.SemaphoreType.DMA((32,)),
    ]
    if before:
        scratch += [pltpu.VMEM((width, units), bfloat), pltpu.VMEM((width, units), single)]
    operands = (*upper, *x_own, *x_peer, g_own, g_peer, *up, *down, *before)
    return call(
        functools.partial(mlp_body, bool(before)),
        outs,
        operands,
        scratch,
        len(upper),
        vmem=60,
        flops=flops,
        far=len(operands) - len(upper),
        far_outs=len(outs),
    )


def shards(
    inputs,
    history,
    cotangent,
    qkv_weight,
    out_weight,
    up_weight,
    down_weight,
    gain_attn,
    gain_mlp,
    dwa_weights,
):
    rows, width = inputs.shape
    members = lax.axis_size("mp")
    copies = lax.axis_size("dp")
    bits = copies.bit_length() - 1
    core = lax.rem(lax.axis_index("mp"), 2).astype(jnp.int32).reshape(1)
    copy_index = lax.axis_index("dp").astype(jnp.int32).reshape(1)
    core_pairs = [(i, i ^ 1) for i in range(members)]
    chip_pairs = [(i, i ^ 2) for i in range(members)]
    depth = history.shape[0]
    part = out_weight.shape[0]

    def other_core(value):
        return lax.ppermute(value, "mp", core_pairs)

    def other_chip(value):
        return lax.ppermute(value, "mp", chip_pairs)

    def other_copy(value, bit):
        return lax.ppermute(value, "dp", [(i, i ^ (1 << bit)) for i in range(copies)])

    uppers = [(copy_index >> bit) & 1 for bit in range(bits)]
    cosine, sine = (jnp.asarray(table) for table in tables())

    qkv_own = qkv_weight.transpose(1, 2, 0).reshape(3 * part, width)
    half = (width // 2, width)
    square = (width, width)
    marks = pltpu.SemaphoreType.DMA((16,))
    halves = call(
        split_body,
        [(half, bfloat)] * 2,
        (uppers[0], qkv_own, out_weight, down_weight),
        [marks],
        1,
        far=3,
        far_outs=2,
    )
    both_come, down_come = map(other_chip, halves)
    both_come = (both_come, other_copy(both_come, 0))
    up_peer = other_chip(up_weight)

    full = (rows, width)
    (x_own,) = call(norm_body, [(full, bfloat)], (inputs, gain_attn))
    x_peer = other_core(x_own)
    history_grad, mixed, g_own, history_parts = average_history(dwa_weights, history, cotangent, (x_own,))
    g_peer = other_core(g_own)

    tall = (SEQ, width)
    tokens = pltpu.VMEM(tall, bfloat)
    first_outs = [
        ((3 * part, SEQ), bfloat), ((part, SEQ), bfloat), ((SEQ, part), bfloat), ((8, SEQ), single),
    ]
    qkv_a, att_a, nat_a, log_a = call(
        attend_own,
        first_outs,
        (core, x_own, x_peer, cosine, sine, qkv_own),
        [tokens],
        1,
        (history_parts,),
        32,
    )
    qkv_b, att_b, nat_b, log_b, qkv_peer, out_peer, down_copy = call(
        attend_peer,
        first_outs + [(qkv_own.shape, bfloat), (out_weight.shape, bfloat), (half, bfloat)],
        (core, uppers[0], x_own, x_peer, cosine, sine, *both_come, down_come),
        [tokens, pltpu.VMEM(qkv_own.shape, bfloat), marks],
        2,
        (log_a,),
        32,
        MUCH,
        far=3,
        far_outs=3,
    )
    down_come = (down_come, other_copy(down_copy, 0))
    third = (rows // PARTS, width)
    keep, *send = call(
        branch_body,
        [(full, single)] + [(third, bfloat)] * PARTS,
        (core, nat_a, nat_b, out_weight, out_peer),
        scalars=1,
    )
    recv = [other_core(value) for value in send]
    middle, *y_own = call(
        middle_body, [(full, single)] + [(third, bfloat)] * PARTS, (inputs, keep, gain_mlp, *recv),
    )
    y_peer = [other_core(value) for value in y_own]

    first = mlp(y_own, y_peer, g_own, g_peer, (up_weight,), (down_weight,))
    down_mine, up_mine = first[4:]
    second = mlp(
        y_own, y_peer, g_own, g_peer, (up_peer,), down_come, (uppers[1], uppers[0]), (*first[:4], up_mine)
    )
    send_norm, keep_norm, send_out, keep_out, down_theirs, up_sent, up_kept = second
    token = [send_norm]

    def step(body, outs, operands, scratch=(), scalars=0, vmem=16, flops=MUCH, far=0, far_outs=0):
        results = call(body, outs, operands, scratch, scalars, tuple(token), vmem, flops, far, far_outs)
        token[0] = results[0]
        return results

    down_come = other_chip(down_theirs)
    up_come = other_copy(up_sent, 1)
    out_come = other_core(send_out)
    grad_middle, gb_own, gain_mlp_part = step(
        middle_back_body,
        [(full, single), (full, bfloat), ((1, width), single)],
        (dwa_weights, middle, keep_norm, other_core(send_norm), cotangent, gain_mlp),
        scalars=1,
        flops=0,
    )
    gb_peer = other_core(gb_own)
    combined, dwa_part = step(
        combine_body,
        [(full, bfloat), ((depth + 1, width), single)],
        (dwa_weights, mixed, middle, keep_out, out_come, cotangent, history_parts),
        scalars=1,
        flops=0,
    )

    def back(second, kind, outs, operands, flops, far, scratch=()):
        return step(
            functools.partial(attend_back, second),
            outs,
            operands,
            [
                pltpu.VMEM(tall, bfloat),
                pltpu.VMEM(tall, bfloat),
                pltpu.VMEM((4 * part, width), bfloat),
                pltpu.VMEM((3 * part, SEQ), bfloat),
                pltpu.VMEM((part, SEQ), bfloat),
                pltpu.VMEM((3 * part, SEQ), bfloat),
                pltpu.VMEM((4 * part, width), kind),
                marks,
                *scratch,
            ],
            1,
            60,
            flops,
            far,
            2,
        )

    shared = (cosine, sine, gb_own, gb_peer, x_own, x_peer)
    att_theirs, turned_b = back(
        False,
        bfloat,
        [((4 * part, width), bfloat), ((3 * part, SEQ), bfloat)],
        (core, log_b, *shared, qkv_peer, out_peer, qkv_b, att_b),
        0,
        8,
    )
    att_come = other_chip(att_theirs)
    down, sent = step(
        halve_body, [(half, single), (half, bfloat)], (uppers[0], down_mine, down_come), scalars=1
    )
    down_come = other_copy(sent, 0)
    up, sent = step(cross_body, [(half, single), (half, bfloat)], (up_kept, up_come))
    up_come = other_chip(sent)
    send_first, gain_attn_part, att_mine, keep_first = back(
        True,
        single,
        [(full, bfloat), ((1, width), single), ((4 * part, width), single), (full, single)],
        (core, log_a, cosine, sine, gain_attn, *shared[2:], qkv_own, out_weight, qkv_a, att_a, turned_b, qkv_peer),
        MUCH,
        10,
        [pltpu.VMEM((3 * part, SEQ), bfloat), pltpu.VMEM((3 * part, width), bfloat), pltpu.VMEM(tall, single)],
    )
    first_come = other_core(send_first)

    done = {}
    small = []

    def chain(name, first_bit, second_bit, value, come, begun):
        if not begun:
            shape = (value.shape[0] // 2, width)
            value, sent = step(
                halve_body, [(shape, single), (shape, bfloat)], (uppers[first_bit], value, come), scalars=1
            )
            come = other_copy(sent, first_bit)
            yield
        if name == "u":
            shape = ((value.shape[0] + EXTRA) // 2, width)
            value, sent = step(
                halve_more_body,
                [(shape, single), (shape, bfloat)],
                (uppers[second_bit], value, come, *small),
                [pltpu.VMEM((2 * shape[0], width), single)],
                1,
            )
        else:
            shape = (value.shape[0] // 2, width)
            value, sent = step(
                halve_body, [(shape, single), (shape, bfloat)], (uppers[second_bit], value, come), scalars=1
            )
        come = other_copy(sent, second_bit)
        yield
        for bit in range(2, bits):
            (value,) = step(low_body, [(shape, bfloat)], (value, come))
            come = other_copy(value, bit)
            yield
        (value,) = step(low_body, [(shape, bfloat)], (value, come))
        come = other_copy(value, second_bit)
        done[name] = (uppers[first_bit], uppers[second_bit], value, come) + (
            other_copy(value, first_bit), other_copy(come, first_bit),
        )
        yield

    chains = {
        "d": chain("d", 0, 1, down, down_come, True),
        "u": chain("u", 1, 0, up, up_come, True),
        "a": chain("a", 0, 1, att_mine, att_come, False),
    }

    def advance(names):
        for name in names:
            next(chains[name], None)

    advance("a")
    (part_sums,) = step(
        small_body, [((depth + 3, width), single)], (gain_attn_part, gain_mlp_part, dwa_part)
    )
    core_sums = other_core(part_sums)
    advance("d")
    (part_sums,) = step(add_body, [(part_sums.shape, single)], (part_sums, core_sums))
    small += [part_sums, other_chip(part_sums)]
    advance("dau")
    (input_grad,) = step(
        first_back_body, [(full, bfloat)], (inputs, keep_first, first_come, grad_middle, gain_attn), vmem=60
    )
    advance("dau")
    for _ in range(3, bits):
        advance("dau")
    (down_grad,) = step(whole_body, [(square, single)], done["d"], [pltpu.VMEM(square, bfloat)], 2)
    for _ in range(bits + 4):
        advance("au")
    qkv_grad, out_grad = step(
        two_body,
        [((3 * part, width), single), ((part, width), single)],
        done["a"],
        [pltpu.VMEM(square, bfloat)],
        2,
    )
    up_grad, gain_attn_grad, gain_mlp_grad, dwa_grad = step(
        more_body,
        [(square, single), ((width,), single), ((width,), single), ((depth + 1,), single, "scalars")],
        done["u"],
        [pltpu.VMEM((width + 2 * EXTRA, width), bfloat)],
        2,
    )

    return (
        combined,
        input_grad,
        history_grad,
        qkv_grad.reshape(3, part, width).transpose(2, 0, 1),
        out_grad,
        up_grad,
        down_grad,
        gain_attn_grad,
        gain_mlp_grad,
        dwa_grad,
    )


def solution(mesh):
    placed = (
        P(("dp", "mp"), None),
        P(None, ("dp", "mp"), None),
        P(("dp", "mp"), None),
        P(None, None, "mp"),
        P("mp", None),
        P(None, "mp"),
        P("mp", None),
        P(),
        P(),
        P(),
    )
    return jax.shard_map(
        shards,
        mesh=mesh,
        in_specs=placed,
        out_specs=(
            P(("dp", "mp"), None),
            P(("dp", "mp"), None),
            P(None, ("dp", "mp"), None),
            P(None, None, "mp"),
            P("mp", None),
            P(None, "mp"),
            P("mp", None),
            P(),
            P(),
            P(),
        ),
        check_vma=False,
    )
```

```python
import functools

import jax
import jax.numpy as jnp
import numpy as np
from jax import lax
from jax.experimental import pallas as pl
from jax.experimental.pallas import tpu as pltpu
from jax.sharding import PartitionSpec as P

DH = 64
SEQ = 1152
HALF = SEQ // 2
EPS = 1e-05
bfloat = jnp.bfloat16
single = jnp.float32
MIB = 1 << 20
MUCH = 10**11


def tables():
    half_width = DH // 2
    places = np.arange(SEQ, dtype=np.float32)
    frequency = np.float32(10000.0) ** (-np.arange(half_width, dtype=np.float32) * np.float32(2.0 / DH))
    angles = frequency[:, None] * places[None, :]
    return (np.cos(angles).astype(np.float32), np.sin(angles).astype(np.float32))


def mul(a, b, ca=1, cb=0):
    return lax.dot_general(a, b, (((ca,), (cb,)), ((), ())), preferred_element_type=single)


def call(kernel, outs, operands, scratch=(), scalars=0, after=(), vmem=16, flops=0, far=0, far_outs=0):
    count, waits = len(operands), len(after)

    def body(*refs):
        kernel(*refs[:count], *refs[count + waits :])

    small = pl.BlockSpec(memory_space=pltpu.SMEM)
    whole = pl.BlockSpec(memory_space=pltpu.VMEM)
    apart = pl.BlockSpec(memory_space=pltpu.HBM)
    loose = pl.BlockSpec(memory_space=pl.ANY)
    inner = len(outs) - far_outs
    return pl.pallas_call(
        body,
        out_shape=[jax.ShapeDtypeStruct(out[0], out[1]) for out in outs],
        in_specs=[small] * scalars + [whole] * (count - scalars - far) + [apart] * far + [loose] * waits,
        out_specs=[small if len(out) > 2 else whole for out in outs[:inner]] + [apart] * far_outs,
        scratch_shapes=list(scratch),
        compiler_params=pltpu.CompilerParams(vmem_limit_bytes=vmem * MIB),
        cost_estimate=pl.CostEstimate(flops=flops, bytes_accessed=0, transcendentals=0),
    )(*operands, *after)


class Mover:
    def __init__(self, marks):
        self.marks = marks
        self.used = 0

    def __call__(self, *pairs):
        copies = []
        for source, target in pairs:
            copies.append(pltpu.make_async_copy(source, target, self.marks.at[self.used]))
            self.used += 1
        for copy in copies:
            copy.start()
        return copies


def wait(copies):
    for copy in copies:
        copy.wait()


ROWS = 64
PARTS = 3


def spans(rows, step=ROWS):
    return [slice(begin, begin + step) for begin in range(0, rows, step)]


def normal_of(x):
    centre = x - jnp.mean(x, axis=-1, keepdims=True)
    spread = jnp.mean(centre * centre, axis=-1, keepdims=True)
    scale = lax.rsqrt(spread + EPS)
    return centre * scale, scale


def split_body(upper_ref, qkv_ref, out_ref, down_ref, both_half, down_half, both, down, marks):
    go = Mover(marks)
    upper = upper_ref[0]

    def rows(ref):
        size = ref.shape[0] // 2
        return ref.at[pl.ds(pl.multiple_of(upper * size, size), size), :]

    size = qkv_ref.shape[0] // 2
    loads = go(
        (rows(qkv_ref), both.at[pl.ds(0, size), :]),
        (rows(out_ref), both.at[pl.ds(size, out_ref.shape[0] // 2), :]),
    )
    later = go((rows(down_ref), down))
    wait(loads)
    stores = go((both, both_half))
    wait(later)
    wait(stores + go((down, down_half)))


def joined(upper, mine_ref, other_ref, begin, target):
    size = target.shape[0] // 2
    part = pl.ds(begin, size)
    return (
        (mine_ref.at[part, :], target.at[pl.ds(pl.multiple_of(upper * size, size), size), :]),
        (other_ref.at[part, :], target.at[pl.ds(pl.multiple_of((1 - upper) * size, size), size), :]),
    )


def norm_body(x_ref, gain_ref, out_ref):
    gain = gain_ref[...].reshape(1, -1)
    for span in spans(x_ref.shape[0]):
        normal, _ = normal_of(x_ref[span, :].astype(single))
        out_ref[span, :] = (normal * gain).astype(bfloat)


def middle_body(x_ref, keep_ref, gain_ref, *rest):
    recv_refs, mid_ref, out_refs = rest[:PARTS], rest[PARTS], rest[PARTS + 1 :]
    gain = gain_ref[...].reshape(1, -1)
    rows = x_ref.shape[0] // PARTS
    for index in range(PARTS):
        for span in spans(rows):
            here = slice(index * rows + span.start, index * rows + span.stop)
            recv = recv_refs[index][span, :].astype(single)
            x = x_ref[here, :].astype(single) + (keep_ref[here, :] + recv)
            mid_ref[here, :] = x
            normal, _ = normal_of(x)
            out_refs[index][span, :] = (normal * gain).astype(bfloat)


def norm_back(x, grad, gain):
    normal, scale = normal_of(x)
    lifted = grad * gain
    back = scale * (
        lifted
        - jnp.mean(lifted, axis=-1, keepdims=True)
        - normal * jnp.mean(lifted * normal, axis=-1, keepdims=True)
    )
    return back, normal


def fold_rows(value):
    total = value[:8]
    for begin in range(8, value.shape[0], 8):
        total = total + value[begin : begin + 8]
    return total


def middle_back_body(mix_ref, x_ref, keep_ref, recv_ref, cot_ref, gain_ref, mid_ref, low_ref, part_ref):
    gain = gain_ref[...].reshape(1, -1)
    part = jnp.zeros((8, x_ref.shape[1]), single)
    for span in spans(x_ref.shape[0]):
        grad = keep_ref[span, :] + recv_ref[span, :].astype(single)
        back, normal = norm_back(x_ref[span, :], grad, gain)
        total = mix_ref[mix_ref.shape[0] - 1] * cot_ref[span, :] + back
        mid_ref[span, :] = total
        low_ref[span, :] = total.astype(bfloat)
        part = part + fold_rows(grad * normal)
    part_ref[...] = jnp.sum(part, axis=0, keepdims=True)


def first_back_body(x_ref, keep_ref, recv_ref, mid_ref, gain_ref, out_ref):
    gain = gain_ref[...].reshape(1, -1)
    for span in spans(x_ref.shape[0]):
        grad = keep_ref[span, :] + recv_ref[span, :].astype(single)
        back, _ = norm_back(x_ref[span, :].astype(single), grad, gain)
        out_ref[span, :] = (mid_ref[span, :] + back).astype(bfloat)


def history_body(mix_ref, history_ref, cot_ref, grad_ref, mixed_ref, low_ref, part_ref):
    depth = history_ref.shape[0]

    @pl.when(pl.program_id(0) == 0)
    def _():
        part_ref[...] = jnp.zeros_like(part_ref)

    for span in spans(cot_ref.shape[0], 32):
        cot = cot_ref[span, :]
        low_ref[span, :] = (mix_ref[depth] * cot).astype(bfloat)
        mixed = None
        for j in range(depth):
            layer = history_ref[j, span, :].astype(single)
            mixed = mix_ref[j] * layer if mixed is None else mixed + mix_ref[j] * layer
            grad_ref[j, span, :] = (mix_ref[j] * cot).astype(bfloat)
            part_ref[8 * j : 8 * j + 8, :] += fold_rows(layer * cot)
        mixed_ref[span, :] = mixed


def average_history(mix, history, cot, after=()):
    depth, rows, width = history.shape
    step = 96
    waits = len(after)

    def body(*refs):
        history_body(*refs[:3], *refs[3 + waits :])

    row_block = pl.BlockSpec((step, width), lambda i: (i, 0))
    deep_block = pl.BlockSpec((depth, step, width), lambda i: (0, i, 0))
    return pl.pallas_call(
        body,
        grid=(rows // step,),
        out_shape=[
            jax.ShapeDtypeStruct(history.shape, bfloat),
            jax.ShapeDtypeStruct((rows, width), single),
            jax.ShapeDtypeStruct((rows, width), bfloat),
            jax.ShapeDtypeStruct((8 * depth, width), single),
        ],
        in_specs=[pl.BlockSpec(memory_space=pltpu.SMEM), deep_block, row_block]
        + [pl.BlockSpec(memory_space=pl.ANY)] * waits,
        out_specs=[deep_block, row_block, row_block, pl.BlockSpec((8 * depth, width), lambda i: (0, 0))],
        compiler_params=pltpu.CompilerParams(vmem_limit_bytes=16 * MIB),
        cost_estimate=pl.CostEstimate(flops=0, bytes_accessed=0, transcendentals=0),
    )(mix, history, cot, *after)


def combine_body(mix_ref, mixed_ref, mid_ref, keep_ref, recv_ref, cot_ref, parts_ref, out_ref, part_ref):
    depth = mix_ref.shape[0] - 1
    last = jnp.zeros((8, mid_ref.shape[1]), single)
    for span in spans(mid_ref.shape[0]):
        outputs = mid_ref[span, :] + (keep_ref[span, :] + recv_ref[span, :].astype(single))
        out_ref[span, :] = (mixed_ref[span, :] + mix_ref[depth] * outputs).astype(bfloat)
        last = last + fold_rows(outputs * cot_ref[span, :])
    for j in range(depth):
        part_ref[j : j + 1, :] = jnp.sum(parts_ref[8 * j : 8 * j + 8, :], axis=0, keepdims=True)
    part_ref[depth : depth + 1, :] = jnp.sum(last, axis=0, keepdims=True)


def part_rows(upper_ref, size):
    low = pl.multiple_of(upper_ref[0] * size, size)
    high = pl.multiple_of((1 - upper_ref[0]) * size, size)
    return pl.ds(low, size), pl.ds(high, size)


def both_rows(mine_ref, come_ref, rows):
    return (mine_ref[rows, :].astype(single) + come_ref[rows, :].astype(single)).astype(bfloat)


def halve_body(upper_ref, mine_ref, come_ref, kept_ref, sent_ref):
    low, high = part_rows(upper_ref, kept_ref.shape[0])
    kept_ref[...] = both_rows(mine_ref, come_ref, low)
    sent_ref[...] = both_rows(mine_ref, come_ref, high)


def halve_two_body(upper_ref, mine_ref, come_ref, kept_ref, sent_ref):
    size = kept_ref.shape[0] // 2
    for begin in (0, size):
        target = pl.ds(begin, size)
        low, high = (
            pl.ds(pl.multiple_of(2 * begin + upper * size, size), size) for upper in (upper_ref[0], 1 - upper_ref[0])
        )
        kept_ref[target, :] = both_rows(mine_ref, come_ref, low)
        sent_ref[target, :] = both_rows(mine_ref, come_ref, high)


def cross_body(kept_ref, come_ref, mine_ref, theirs_ref):
    size = mine_ref.shape[0]
    mine_ref[...] = both_rows(kept_ref, come_ref, pl.ds(0, size))
    theirs_ref[...] = both_rows(kept_ref, come_ref, pl.ds(size, size))


def low_body(mine_ref, come_ref, out_ref):
    out_ref[...] = (mine_ref[...].astype(single) + come_ref[...].astype(single)).astype(bfloat)


def gather(first_ref, second_ref, pieces, hold):
    size = pieces[0].shape[0]
    for index, piece in enumerate(pieces):
        first = first_ref[0] if index < 2 else 1 - first_ref[0]
        second = second_ref[0] if index % 2 == 0 else 1 - second_ref[0]
        hold[pl.ds(pl.multiple_of((2 * first + second) * size, size), size), :] = piece[...]


def whole_body(first_ref, second_ref, a_ref, b_ref, c_ref, d_ref, out_ref, hold):
    gather(first_ref, second_ref, (a_ref, b_ref, c_ref, d_ref), hold)
    out_ref[...] = hold[...].astype(single)


EXTRA = 64


def halve_more_body(upper_ref, mine_ref, come_ref, extra_ref, more_ref, kept_ref, sent_ref, hold):
    rows, extra = mine_ref.shape[0], extra_ref.shape[0]
    hold[:rows, :] = mine_ref[...].astype(single) + come_ref[...].astype(single)
    hold[rows:, :] = jnp.zeros((EXTRA, hold.shape[1]), single)
    hold[rows : rows + extra, :] = extra_ref[...] + more_ref[...]
    low, high = part_rows(upper_ref, kept_ref.shape[0])
    kept_ref[...] = hold[low, :].astype(bfloat)
    sent_ref[...] = hold[high, :].astype(bfloat)


def more_body(
    first_ref, second_ref, a_ref, b_ref, c_ref, d_ref, top_ref, end_ref, attn_ref, mlp_ref, dwa_ref, hold
):
    gather(first_ref, second_ref, (a_ref, b_ref, c_ref, d_ref), hold)
    block = hold.shape[0] // 2
    rows = block - EXTRA
    rest = top_ref.shape[0] - rows
    top_ref[:rows, :] = hold[:rows, :].astype(single)
    top_ref[rows:, :] = hold[block : block + rest, :].astype(single)
    end_ref[...] = hold[block + rest : block + rows, :].astype(single)
    small = hold[rows:block, :].astype(single) + hold[block + rows :, :].astype(single)
    attn_ref[...] = small[0]
    mlp_ref[...] = small[1]
    for index in range(dwa_ref.shape[0]):
        dwa_ref[index] = jnp.sum(small[2 + index : 3 + index])


def add_body(mine_ref, come_ref, out_ref):
    out_ref[...] = mine_ref[...] + come_ref[...]


def small_body(attn_ref, mlp_ref, dwa_ref, out_ref):
    out_ref[:1, :] = attn_ref[...]
    out_ref[1:2, :] = mlp_ref[...]
    out_ref[2:, :] = dwa_ref[...]


BLOCKS = tuple((begin, min(256, SEQ - begin)) for begin in range(0, SEQ, 256))


def place(core_ref, own_ref, peer_ref, whole):
    low = pl.multiple_of(core_ref[0] * HALF, HALF)
    high = pl.multiple_of((1 - core_ref[0]) * HALF, HALF)
    whole[pl.ds(low, HALF), :] = own_ref[...]
    whole[pl.ds(high, HALF), :] = peer_ref[...]
    return low, high


def allowed(size):
    key_pos = lax.broadcasted_iota(jnp.int32, (size, size), 0)
    query_pos = lax.broadcasted_iota(jnp.int32, (size, size), 1)
    return query_pos >= key_pos


def turn(rows, cosine, sine):
    half = rows.shape[0] // 2
    a, b = rows[:half], rows[half:]
    return jnp.concatenate([a * cosine - b * sine, b * cosine + a * sine], axis=0)


def attend_own(
    core_ref, own_ref, peer_ref, cos_ref, sin_ref, weight_ref, qkv_ref, att_ref, nat_ref, log_ref, tokens
):
    place(core_ref, own_ref, peer_ref, tokens)
    attend(weight_ref, cos_ref, sin_ref, qkv_ref, att_ref, nat_ref, log_ref, tokens)


def attend_peer(
    core_ref, upper_ref, own_ref, peer_ref, cos_ref, sin_ref, mine_ref, other_ref, pass_ref,
    qkv_ref, att_ref, nat_ref, log_ref, weight_out, out_out, pass_out, tokens, weight, out, hold, marks,
):
    go = Mover(marks)
    loads = go(*joined(upper_ref[0], mine_ref, other_ref, 0, weight))
    later = go(*joined(upper_ref[0], mine_ref, other_ref, weight.shape[0] // 2, out), (pass_ref, hold))
    place(core_ref, own_ref, peer_ref, tokens)
    wait(loads)
    wait(later)
    copies = go((weight, weight_out), (out, out_out), (hold, pass_out))
    attend(weight, cos_ref, sin_ref, qkv_ref, att_ref, nat_ref, log_ref, tokens)
    wait(copies)


def attend(weight_ref, cos_ref, sin_ref, qkv_ref, att_ref, nat_ref, log_ref, tokens):
    width = weight_ref.shape[0] // 3
    projected = mul(weight_ref[...], tokens[...], 1, 1)
    cosine, sine = cos_ref[...], sin_ref[...]
    for part in range(3):
        for head in range(width // DH):
            begin = part * width + head * DH
            rows = projected[begin : begin + DH]
            if part < 2:
                rows = turn(rows, cosine, sine)
            if part == 0:
                rows = rows * DH ** (-0.5)
            qkv_ref[begin : begin + DH, :] = rows.astype(bfloat)
    log_ref[...] = jnp.zeros_like(log_ref)
    for head in range(width // DH):
        base = head * DH
        keys = qkv_ref[width + base : width + base + DH, :].T
        for begin, size in BLOCKS:
            end = begin + size
            query = qkv_ref[base : base + DH, begin:end]
            scores = mul(keys[:end], query)
            corner = jnp.where(allowed(size), scores[begin:], -jnp.inf)
            top = jnp.max(corner, axis=0, keepdims=True)
            if begin:
                top = jnp.maximum(top, jnp.max(scores[:begin], axis=0, keepdims=True))
                scores = jnp.concatenate([scores[:begin], corner], axis=0)
            else:
                scores = corner
            weights = jnp.exp(scores - top)
            total = jnp.sum(weights, axis=0, keepdims=True)
            value = qkv_ref[2 * width + base : 2 * width + base + DH, :end]
            mixed = mul(value, weights.astype(bfloat)) / total
            att_ref[base : base + DH, begin:end] = mixed.astype(bfloat)
            log_ref[head : head + 1, begin:end] = top + jnp.log(total)
    nat_ref[...] = att_ref[...].T


def branch_body(core_ref, att_a_ref, att_b_ref, out_a_ref, out_b_ref, keep_ref, *send_refs):
    low = pl.multiple_of(core_ref[0] * HALF, HALF)
    rows = HALF // PARTS
    for index in range(PARTS):
        high = pl.multiple_of((1 - core_ref[0]) * HALF + index * rows, rows)
        send = mul(att_a_ref[pl.ds(high, rows), :], out_a_ref[...])
        send_refs[index][...] = (send + mul(att_b_ref[pl.ds(high, rows), :], out_b_ref[...])).astype(bfloat)
    keep = mul(att_a_ref[pl.ds(low, HALF), :], out_a_ref[...])
    keep_ref[...] = keep + mul(att_b_ref[pl.ds(low, HALF), :], out_b_ref[...])


def attend_back(
    second, core_ref, log_ref, cos_ref, sin_ref, *rest
):
    if second:
        gain_ref, rest = rest[0], rest[1:]
    grad_own_ref, grad_peer_ref, own_ref, peer_ref, weight_ref, out_weight_ref, qkv_ref, att_ref = rest[:8]
    rest = rest[8:]
    if second:
        turned_b_ref, weight_b_ref, send_ref, part_ref, out_ref, keep_ref = rest[:6]
        grads, tokens, weight, qkv, att, turned, result, marks, turned_b, weight_b, whole = rest[6:]
    else:
        out_ref, turned_ref, grads, tokens, weight, qkv, att, turned, result, marks = rest
    low = pl.multiple_of(core_ref[0] * HALF, HALF)
    high = pl.multiple_of((1 - core_ref[0]) * HALF, HALF)
    go = Mover(marks)
    depth = weight_ref.shape[0]
    first = go(
        (out_weight_ref, weight.at[pl.ds(depth, out_weight_ref.shape[0]), :]),
        (grad_own_ref, grads.at[pl.ds(low, HALF), :]),
        (grad_peer_ref, grads.at[pl.ds(high, HALF), :]),
        (att_ref, att),
        (qkv_ref, qkv),
    )
    later = go(
        (own_ref, tokens.at[pl.ds(low, HALF), :]),
        (peer_ref, tokens.at[pl.ds(high, HALF), :]),
        (weight_ref, weight.at[pl.ds(0, depth), :]),
    )
    if second:
        later += go((turned_b_ref, turned_b), (weight_b_ref, weight_b))
    wait(first)
    width = att.shape[0]
    grad_att = mul(weight[3 * width :, :], grads[...], 1, 1).astype(bfloat)
    result[3 * width :, :] = mul(att[...], grads[...]).astype(result.dtype)
    cosine, sine = cos_ref[...], sin_ref[...]
    for head in range(width // DH):
        base = head * DH
        query = qkv[base : base + DH, :]
        key = qkv[width + base : width + base + DH, :]
        value = qkv[2 * width + base : 2 * width + base + DH, :]
        above = grad_att[base : base + DH]
        centre = jnp.sum(
            above.astype(single) * att[base : base + DH, :].astype(single), axis=0, keepdims=True
        )
        keys, values, queries, aboves = key.T, value.T, query.T, above.T
        grad_query, grad_key, grad_value = [], None, None
        for begin, size in reversed(BLOCKS):
            end = begin + size
            scores = mul(keys[:end], query[:, begin:end])
            corner = jnp.where(allowed(size), scores[begin:], -jnp.inf)
            scores = jnp.concatenate([scores[:begin], corner], axis=0) if begin else corner
            probs = jnp.exp(scores - log_ref[head : head + 1, begin:end])
            grad_probs = mul(values[:end], above[:, begin:end])
            grad_scores = (probs * (grad_probs - centre[:, begin:end])).astype(bfloat)
            grad_query.insert(0, mul(key[:, :end], grad_scores))
            key_part = mul(grad_scores, queries[begin:end])
            value_part = mul(probs.astype(bfloat), aboves[begin:end])
            if grad_key is None:
                grad_key, grad_value = key_part, value_part
            else:
                grad_key = jnp.concatenate([grad_key[:end] + key_part, grad_key[end:]], axis=0)
                grad_value = jnp.concatenate([grad_value[:end] + value_part, grad_value[end:]], axis=0)
        grad_query = jnp.concatenate(grad_query, axis=1) * DH ** (-0.5)
        turned[base : base + DH, :] = turn(grad_query, cosine, -sine).astype(bfloat)
        turned[width + base : width + base + DH, :] = turn(grad_key.T, cosine, -sine).astype(bfloat)
        turned[2 * width + base : 2 * width + base + DH, :] = grad_value.T.astype(bfloat)
    stores = [] if second else go((turned, turned_ref))
    wait(later)
    result[: 3 * width, :] = mul(turned[...], tokens[...]).astype(result.dtype)
    stores += go((result, out_ref))
    if second:
        whole[...] = mul(turned[...], weight[:depth, :], 0, 0) + mul(turned_b[...], weight_b[...], 0, 0)
        stores += go((whole.at[pl.ds(low, HALF), :], keep_ref))
        send_ref[...] = whole[pl.ds(high, HALF), :].astype(bfloat)
        part = jnp.zeros((8, whole.shape[1]), single)
        for span in spans(whole.shape[0]):
            part = part + fold_rows(whole[span, :] * tokens[span, :].astype(single))
        part_ref[...] = jnp.sum(part, axis=0, keepdims=True) / gain_ref[...].reshape(1, -1)
    wait(stores)


CURVE = float(np.sqrt(2.0 / np.pi))
STEP = 256


def mlp_body(second, *refs):
    if second:
        upper_ref, other_upper_ref, refs = refs[0], refs[1], refs[2:]
    x_refs, refs = refs[: 2 * PARTS], refs[2 * PARTS :]
    g_own_ref, g_peer_ref, refs = refs[0], refs[1], refs[2:]
    if second:
        up_ref, down_refs = refs[0], refs[1:3]
        before_refs, up_mine_ref = refs[3:7], refs[7]
        down_grad_ref, sent_ref, kept_ref = refs[12:15]
        refs = refs[8:12] + refs[15:]
    else:
        up_ref, down_ref = refs[:2]
        down_grad_ref, up_grad_ref = refs[6:8]
        refs = refs[2:6] + refs[8:]
    send_norm_ref, keep_norm_ref, send_out_ref, keep_out_ref = refs[:4]
    x_all, g_all, up, down, active, grad_hidden, x_turned = refs[4:11]
    send_norm, keep_norm, send_out, keep_out, down_grad, up_grad, marks = refs[11:18]
    rows, size = x_all.shape[0] // 2, x_all.shape[0] // (2 * PARTS)
    units = down.shape[0]
    go = Mover(marks)
    x_loads = go(*[(x_refs[index], x_all.at[pl.ds(index * size, size), :]) for index in range(2 * PARTS)])
    if second:
        loads = go((up_ref, up), *joined(other_upper_ref[0], *down_refs, 0, down))
    else:
        loads = go((up_ref, up), (down_ref, down))
    loads += go((g_own_ref, g_all.at[pl.ds(0, rows), :]), (g_peer_ref, g_all.at[pl.ds(rows, rows), :]))
    more, mine, stores = [], [], []
    if second:
        (up_mine,) = refs[18:]
        more = go(*zip(before_refs, (send_norm, keep_norm, send_out, keep_out)))
        mine = go((up_mine_ref, up_mine))
    wait(x_loads)
    x_turned[...] = x_all[...].T
    wait(loads)
    for begin in range(0, units, STEP):
        columns = slice(begin, begin + STEP)
        for top in range(0, 2 * rows, rows):
            span = slice(top, top + rows)
            v = mul(x_all[span, :], up[:, columns])
            grad = mul(g_all[span, :], down[columns, :], 1, 1)
            square = v * v
            half = 0.5 + 0.5 * jnp.tanh(v * (CURVE + (CURVE * 0.044715) * square))
            act = v * half
            slope = half + act * (1.0 - half) * (2.0 * CURVE + (6.0 * CURVE * 0.044715) * square)
            active[span, columns] = act.astype(bfloat)
            grad_hidden[span, columns] = (grad * slope).astype(bfloat)

    def put(target, value):
        target[...] = (value + target[...].astype(single) if second else value).astype(target.dtype)

    wait(more)
    put(keep_norm, mul(grad_hidden[:rows, :], up[...], 1, 1))
    put(send_norm, mul(grad_hidden[rows:, :], up[...], 1, 1))
    stores += go((keep_norm, keep_norm_ref), (send_norm, send_norm_ref))
    down_grad[...] = mul(active[...], g_all[...], 0, 0).astype(down_grad.dtype)
    stores += go((down_grad, down_grad_ref))
    up_grad[...] = mul(x_turned[...], grad_hidden[...]).astype(bfloat)
    if second:
        wait(mine)
        part = up_grad.shape[0] // 2
        low, high = part_rows(upper_ref, part)
        for source, begin in ((up_mine, 0), (up_grad, part)):
            stores += go(
                (source.at[low, :], kept_ref.at[pl.ds(begin, part), :]),
                (source.at[high, :], sent_ref.at[pl.ds(begin, part), :]),
            )
    else:
        stores += go((up_grad, up_grad_ref))
    put(keep_out, mul(active[:rows, :], down[...]))
    stores += go((keep_out, keep_out_ref))
    put(send_out, mul(active[rows:, :], down[...]))
    wait(stores + go((send_out, send_out_ref)))


def mlp(x_own, x_peer, g_own, g_peer, up, down, upper=(), before=(), flops=0):
    rows, width = g_own.shape
    units = sum(piece.shape[0] for piece in down)
    tall = (2 * rows, width)
    pair = [((rows, width), bfloat), ((rows, width), single)] * 2
    outs = pair + [((units, width), bfloat)] + [((width, units), bfloat)] * (2 if before else 1)
    scratch = [
        pltpu.VMEM(tall, bfloat),
        pltpu.VMEM(tall, bfloat),
        pltpu.VMEM((width, units), bfloat),
        pltpu.VMEM((units, width), bfloat),
        pltpu.VMEM((2 * rows, units), bfloat),
        pltpu.VMEM((2 * rows, units), bfloat),
        pltpu.VMEM((width, 2 * rows), bfloat),
    ]
    scratch += [pltpu.VMEM(shape, kind) for shape, kind in pair]
    scratch += [
        pltpu.VMEM((units, width), bfloat), pltpu.VMEM((width, units), bfloat), pltpu.SemaphoreType.DMA((32,)),
    ]
    if before:
        scratch.append(pltpu.VMEM((width, units), bfloat))
    operands = (*upper, *x_own, *x_peer, g_own, g_peer, *up, *down, *before)
    return call(
        functools.partial(mlp_body, bool(before)),
        outs,
        operands,
        scratch,
        len(upper),
        vmem=60,
        flops=flops,
        far=len(operands) - len(upper),
        far_outs=len(outs),
    )


def shards(
    inputs,
    history,
    cotangent,
    qkv_weight,
    out_weight,
    up_weight,
    down_weight,
    gain_attn,
    gain_mlp,
    dwa_weights,
):
    rows, width = inputs.shape
    members = lax.axis_size("mp")
    copies = lax.axis_size("dp")
    bits = copies.bit_length() - 1
    core = lax.rem(lax.axis_index("mp"), 2).astype(jnp.int32).reshape(1)
    copy_index = lax.axis_index("dp").astype(jnp.int32).reshape(1)
    core_pairs = [(i, i ^ 1) for i in range(members)]
    chip_pairs = [(i, i ^ 2) for i in range(members)]
    depth = history.shape[0]
    part = out_weight.shape[0]

    def other_core(value):
        return lax.ppermute(value, "mp", core_pairs)

    def other_chip(value):
        return lax.ppermute(value, "mp", chip_pairs)

    def other_copy(value, *which):
        mask = sum(1 << bit for bit in which)
        return lax.ppermute(value, "dp", [(i, i ^ mask) for i in range(copies)])

    uppers = [(copy_index >> bit) & 1 for bit in range(bits)]
    cosine, sine = (jnp.asarray(table) for table in tables())

    qkv_own = qkv_weight.transpose(1, 2, 0).reshape(3 * part, width)
    half = (width // 2, width)
    square = (width, width)
    marks = pltpu.SemaphoreType.DMA((16,))
    halves = call(
        split_body,
        [(half, bfloat)] * 2,
        (uppers[0], qkv_own, out_weight, down_weight),
        [pltpu.VMEM(half, bfloat), pltpu.VMEM(half, bfloat), marks],
        1,
        vmem=60,
        far=3,
        far_outs=2,
    )
    both_come, down_come = map(other_chip, halves)
    both_come = (both_come, other_copy(both_come, 0))
    up_peer = other_chip(up_weight)

    full = (rows, width)
    (x_own,) = call(norm_body, [(full, bfloat)], (inputs, gain_attn))
    x_peer = other_core(x_own)
    history_grad, mixed, g_own, history_parts = average_history(dwa_weights, history, cotangent, (x_own,))
    g_peer = other_core(g_own)

    tall = (SEQ, width)
    tokens = pltpu.VMEM(tall, bfloat)
    first_outs = [
        ((3 * part, SEQ), bfloat), ((part, SEQ), bfloat), ((SEQ, part), bfloat), ((8, SEQ), single),
    ]
    qkv_a, att_a, nat_a, log_a = call(
        attend_own,
        first_outs,
        (core, x_own, x_peer, cosine, sine, qkv_own),
        [tokens],
        1,
        (history_parts,),
        60,
    )
    qkv_b, att_b, nat_b, log_b, qkv_peer, out_peer, down_copy = call(
        attend_peer,
        first_outs + [(qkv_own.shape, bfloat), (out_weight.shape, bfloat), (half, bfloat)],
        (core, uppers[0], x_own, x_peer, cosine, sine, *both_come, down_come),
        [
            tokens,
            pltpu.VMEM(qkv_own.shape, bfloat),
            pltpu.VMEM(out_weight.shape, bfloat),
            pltpu.VMEM(half, bfloat),
            marks,
        ],
        2,
        (log_a,),
        60,
        MUCH,
        far=3,
        far_outs=3,
    )
    down_come = (down_come, other_copy(down_copy, 0))
    third = (rows // PARTS, width)
    keep, *send = call(
        branch_body,
        [(full, single)] + [(third, bfloat)] * PARTS,
        (core, nat_a, nat_b, out_weight, out_peer),
        scalars=1,
    )
    recv = [other_core(value) for value in send]
    middle, *y_own = call(
        middle_body, [(full, single)] + [(third, bfloat)] * PARTS, (inputs, keep, gain_mlp, *recv),
    )
    y_peer = [other_core(value) for value in y_own]

    first = mlp(y_own, y_peer, g_own, g_peer, (up_weight,), (down_weight,))
    down_mine, up_mine = first[4:]
    second = mlp(
        y_own, y_peer, g_own, g_peer, (up_peer,), down_come, (uppers[1], uppers[0]), (*first[:4], up_mine)
    )
    send_norm, keep_norm, send_out, keep_out, down_theirs, up_sent, up_kept = second
    token = [send_norm]

    def step(body, outs, operands, scratch=(), scalars=0, vmem=16, flops=MUCH, far=0, far_outs=0):
        results = call(body, outs, operands, scratch, scalars, tuple(token), vmem, flops, far, far_outs)
        token[0] = results[0]
        return results

    down_come = other_chip(down_theirs)
    up_come = other_copy(up_sent, 1)
    out_come = other_core(send_out)
    grad_middle, gb_own, gain_mlp_part = step(
        middle_back_body,
        [(full, single), (full, bfloat), ((1, width), single)],
        (dwa_weights, middle, keep_norm, other_core(send_norm), cotangent, gain_mlp),
        scalars=1,
        flops=0,
    )
    gb_peer = other_core(gb_own)
    combined, dwa_part = step(
        combine_body,
        [(full, bfloat), ((depth + 1, width), single)],
        (dwa_weights, mixed, middle, keep_out, out_come, cotangent, history_parts),
        scalars=1,
        flops=0,
    )

    def back(second, kind, outs, operands, flops, far, scratch=()):
        return step(
            functools.partial(attend_back, second),
            outs,
            operands,
            [
                pltpu.VMEM(tall, bfloat),
                pltpu.VMEM(tall, bfloat),
                pltpu.VMEM((4 * part, width), bfloat),
                pltpu.VMEM((3 * part, SEQ), bfloat),
                pltpu.VMEM((part, SEQ), bfloat),
                pltpu.VMEM((3 * part, SEQ), bfloat),
                pltpu.VMEM((4 * part, width), kind),
                marks,
                *scratch,
            ],
            1,
            60,
            flops,
            far,
            2,
        )

    shared = (cosine, sine, gb_own, gb_peer, x_own, x_peer)
    att_theirs, turned_b = back(
        False,
        bfloat,
        [((4 * part, width), bfloat), ((3 * part, SEQ), bfloat)],
        (core, log_b, *shared, qkv_peer, out_peer, qkv_b, att_b),
        0,
        8,
    )
    att_come = other_chip(att_theirs)
    down, sent = step(
        halve_body, [(half, bfloat)] * 2, (uppers[0], down_mine, down_come), scalars=1, flops=0
    )
    down_come = other_copy(sent, 0)
    up, sent = step(halve_two_body, [(half, bfloat)] * 2, (uppers[0], up_kept, up_come), scalars=1, flops=0)
    up_come = other_copy(sent, 0)
    send_first, gain_attn_part, att_mine, keep_first = back(
        True,
        bfloat,
        [(full, bfloat), ((1, width), single), ((4 * part, width), bfloat), (full, single)],
        (core, log_a, cosine, sine, gain_attn, *shared[2:], qkv_own, out_weight, qkv_a, att_a, turned_b, qkv_peer),
        MUCH,
        10,
        [pltpu.VMEM((3 * part, SEQ), bfloat), pltpu.VMEM((3 * part, width), bfloat), pltpu.VMEM(tall, single)],
    )
    first_come = other_core(send_first)

    done = {}
    small = []

    def chain(name, first_bit, second_bit, value, come):
        if name == "a":
            shape = (value.shape[0] // 2, width)
            value, sent = step(halve_body, [(shape, bfloat)] * 2, (uppers[first_bit], value, come), scalars=1)
            come = other_copy(sent, first_bit)
            yield
        if name == "a":
            shape = ((value.shape[0] + EXTRA) // 2, width)
            value, sent = step(
                halve_more_body,
                [(shape, bfloat)] * 2,
                (uppers[second_bit], value, come, *small),
                [pltpu.VMEM((2 * shape[0], width), single)],
                1,
            )
            come = other_copy(sent, second_bit)
        elif name == "d":
            shape = (value.shape[0] // 2, width)
            value, sent = step(halve_body, [(shape, bfloat)] * 2, (uppers[second_bit], value, come), scalars=1)
            come = other_copy(sent, second_bit)
        else:
            shape = (value.shape[0] // 2, width)
            value, sent = step(cross_body, [(shape, bfloat)] * 2, (value, come))
            come = other_chip(sent)
        yield
        for bit in range(2, bits):
            (value,) = step(low_body, [(shape, bfloat)], (value, come))
            come = other_copy(value, bit)
            yield
        (value,) = step(low_body, [(shape, bfloat)], (value, come))
        done[name] = (
            uppers[first_bit],
            uppers[second_bit],
            value,
            other_copy(value, second_bit),
            other_copy(value, first_bit),
            other_copy(value, first_bit, second_bit),
        )
        yield

    chains = {
        "d": chain("d", 0, 1, down, down_come),
        "u": chain("u", 1, 0, up, up_come),
        "a": chain("a", 0, 1, att_mine, att_come),
    }

    def advance(names):
        for name in names:
            next(chains[name], None)

    def whole(name):
        return step(whole_body, [(square, single)], done[name], [pltpu.VMEM(square, bfloat)], 2)[0]

    advance("dua")
    (part_sums,) = step(
        small_body, [((depth + 3, width), single)], (gain_attn_part, gain_mlp_part, dwa_part)
    )
    core_sums = other_core(part_sums)
    advance("d")
    (part_sums,) = step(add_body, [(part_sums.shape, single)], (part_sums, core_sums))
    small += [part_sums, other_chip(part_sums)]
    advance("ua")
    (input_grad,) = step(
        first_back_body, [(full, bfloat)], (inputs, keep_first, first_come, grad_middle, gain_attn), vmem=60
    )
    advance("a")
    for _ in range(3, bits):
        advance("dua")
    advance("du")
    down_grad = whole("d")
    advance("a")
    up_grad = whole("u")
    qkv_grad, out_grad, gain_attn_grad, gain_mlp_grad, dwa_grad = step(
        more_body,
        [
            ((3 * part, width), single),
            ((part, width), single),
            ((width,), single),
            ((width,), single),
            ((depth + 1,), single, "scalars"),
        ],
        done["a"],
        [pltpu.VMEM((width + 2 * EXTRA, width), bfloat)],
        2,
    )

    return (
        combined,
        input_grad,
        history_grad,
        qkv_grad.reshape(3, part, width).transpose(2, 0, 1),
        out_grad,
        up_grad,
        down_grad,
        gain_attn_grad,
        gain_mlp_grad,
        dwa_grad,
    )


def solution(mesh):
    placed = (
        P(("dp", "mp"), None),
        P(None, ("dp", "mp"), None),
        P(("dp", "mp"), None),
        P(None, None, "mp"),
        P("mp", None),
        P(None, "mp"),
        P("mp", None),
        P(),
        P(),
        P(),
    )
    return jax.shard_map(
        shards,
        mesh=mesh,
        in_specs=placed,
        out_specs=(
            P(("dp", "mp"), None),
            P(("dp", "mp"), None),
            P(None, ("dp", "mp"), None),
            P(None, None, "mp"),
            P("mp", None),
            P(None, "mp"),
            P("mp", None),
            P(),
            P(),
            P(),
        ),
        check_vma=False,
    )
```

```python
import functools

import jax
import jax.numpy as jnp
import numpy as np
from jax import lax
from jax.experimental import pallas as pl
from jax.experimental.pallas import tpu as pltpu
from jax.sharding import PartitionSpec as P

DH = 64
SEQ = 1152
HALF = SEQ // 2
EPS = 1e-05
bfloat = jnp.bfloat16
single = jnp.float32
MIB = 1 << 20
MUCH = 10**11
COST = 10**10


def tables():
    half_width = DH // 2
    places = np.arange(SEQ, dtype=np.float32)
    frequency = np.float32(10000.0) ** (-np.arange(half_width, dtype=np.float32) * np.float32(2.0 / DH))
    angles = frequency[:, None] * places[None, :]
    return (np.cos(angles).astype(np.float32), np.sin(angles).astype(np.float32))


def mul(a, b, ca=1, cb=0):
    return lax.dot_general(a, b, (((ca,), (cb,)), ((), ())), preferred_element_type=single)


def call(kernel, outs, operands, scratch=(), scalars=0, after=(), vmem=16, flops=0, far=0, far_outs=0):
    count, waits = len(operands), len(after)

    def body(*refs):
        kernel(*refs[:count], *refs[count + waits :])

    small = pl.BlockSpec(memory_space=pltpu.SMEM)
    whole = pl.BlockSpec(memory_space=pltpu.VMEM)
    apart = pl.BlockSpec(memory_space=pltpu.HBM)
    loose = pl.BlockSpec(memory_space=pl.ANY)
    inner = len(outs) - far_outs
    return pl.pallas_call(
        body,
        out_shape=[jax.ShapeDtypeStruct(out[0], out[1]) for out in outs],
        in_specs=[small] * scalars + [whole] * (count - scalars - far) + [apart] * far + [loose] * waits,
        out_specs=[small if len(out) > 2 else whole for out in outs[:inner]] + [apart] * far_outs,
        scratch_shapes=list(scratch),
        compiler_params=pltpu.CompilerParams(vmem_limit_bytes=vmem * MIB),
        cost_estimate=pl.CostEstimate(flops=flops, bytes_accessed=0, transcendentals=0),
    )(*operands, *after)


class Mover:
    def __init__(self, marks):
        self.marks = marks
        self.used = 0

    def __call__(self, *pairs):
        copies = []
        for source, target in pairs:
            copies.append(pltpu.make_async_copy(source, target, self.marks.at[self.used]))
            self.used += 1
        for copy in copies:
            copy.start()
        return copies


def wait(copies):
    for copy in copies:
        copy.wait()


ROWS = 64
PARTS = 3


def spans(rows, step=ROWS):
    return [slice(begin, begin + step) for begin in range(0, rows, step)]


def normal_of(x):
    centre = x - jnp.mean(x, axis=-1, keepdims=True)
    spread = jnp.mean(centre * centre, axis=-1, keepdims=True)
    scale = lax.rsqrt(spread + EPS)
    return centre * scale, scale


def split_body(upper_ref, qkv_ref, out_ref, down_ref, both_half, down_half, both, down, marks):
    go = Mover(marks)
    upper = upper_ref[0]

    def rows(ref):
        size = ref.shape[0] // 2
        return ref.at[pl.ds(pl.multiple_of(upper * size, size), size), :]

    size = qkv_ref.shape[0] // 2
    loads = go(
        (rows(qkv_ref), both.at[pl.ds(0, size), :]),
        (rows(out_ref), both.at[pl.ds(size, out_ref.shape[0] // 2), :]),
    )
    later = go((rows(down_ref), down))
    wait(loads)
    stores = go((both, both_half))
    wait(later)
    wait(stores + go((down, down_half)))


def joined(upper, mine_ref, other_ref, begin, target):
    size = target.shape[0] // 2
    part = pl.ds(begin, size)
    return (
        (mine_ref.at[part, :], target.at[pl.ds(pl.multiple_of(upper * size, size), size), :]),
        (other_ref.at[part, :], target.at[pl.ds(pl.multiple_of((1 - upper) * size, size), size), :]),
    )


def norm_body(x_ref, gain_ref, out_ref):
    gain = gain_ref[...].reshape(1, -1)
    for span in spans(x_ref.shape[0]):
        normal, _ = normal_of(x_ref[span, :].astype(single))
        out_ref[span, :] = (normal * gain).astype(bfloat)


def middle_body(x_ref, keep_ref, gain_ref, *rest):
    recv_refs, mid_ref, out_refs = rest[:PARTS], rest[PARTS], rest[PARTS + 1 :]
    gain = gain_ref[...].reshape(1, -1)
    rows = x_ref.shape[0] // PARTS
    for index in range(PARTS):
        for span in spans(rows):
            here = slice(index * rows + span.start, index * rows + span.stop)
            recv = recv_refs[index][span, :].astype(single)
            x = x_ref[here, :].astype(single) + (keep_ref[here, :] + recv)
            mid_ref[here, :] = x
            normal, _ = normal_of(x)
            out_refs[index][span, :] = (normal * gain).astype(bfloat)


def norm_back(x, grad, gain):
    normal, scale = normal_of(x)
    lifted = grad * gain
    back = scale * (
        lifted
        - jnp.mean(lifted, axis=-1, keepdims=True)
        - normal * jnp.mean(lifted * normal, axis=-1, keepdims=True)
    )
    return back, normal


def fold_rows(value):
    total = value[:8]
    for begin in range(8, value.shape[0], 8):
        total = total + value[begin : begin + 8]
    return total


def middle_back_body(mix_ref, x_ref, keep_ref, recv_ref, cot_ref, gain_ref, mid_ref, low_ref, part_ref):
    gain = gain_ref[...].reshape(1, -1)
    part = jnp.zeros((8, x_ref.shape[1]), single)
    for span in spans(x_ref.shape[0]):
        grad = keep_ref[span, :] + recv_ref[span, :].astype(single)
        back, normal = norm_back(x_ref[span, :], grad, gain)
        total = mix_ref[mix_ref.shape[0] - 1] * cot_ref[span, :] + back
        mid_ref[span, :] = total
        low_ref[span, :] = total.astype(bfloat)
        part = part + fold_rows(grad * normal)
    part_ref[...] = jnp.sum(part, axis=0, keepdims=True)


def first_back_body(x_ref, keep_ref, recv_ref, mid_ref, gain_ref, out_ref):
    gain = gain_ref[...].reshape(1, -1)
    for span in spans(x_ref.shape[0]):
        grad = keep_ref[span, :] + recv_ref[span, :].astype(single)
        back, _ = norm_back(x_ref[span, :].astype(single), grad, gain)
        out_ref[span, :] = (mid_ref[span, :] + back).astype(bfloat)


def history_body(mix_ref, history_ref, cot_ref, grad_ref, mixed_ref, low_ref, part_ref):
    depth = history_ref.shape[0]

    @pl.when(pl.program_id(0) == 0)
    def _():
        part_ref[...] = jnp.zeros_like(part_ref)

    for span in spans(cot_ref.shape[0], 32):
        cot = cot_ref[span, :]
        low_ref[span, :] = (mix_ref[depth] * cot).astype(bfloat)
        mixed = None
        for j in range(depth):
            layer = history_ref[j, span, :].astype(single)
            mixed = mix_ref[j] * layer if mixed is None else mixed + mix_ref[j] * layer
            grad_ref[j, span, :] = (mix_ref[j] * cot).astype(bfloat)
            part_ref[8 * j : 8 * j + 8, :] += fold_rows(layer * cot)
        mixed_ref[span, :] = mixed


def average_history(mix, history, cot, after=()):
    depth, rows, width = history.shape
    step = 96
    waits = len(after)

    def body(*refs):
        history_body(*refs[:3], *refs[3 + waits :])

    row_block = pl.BlockSpec((step, width), lambda i: (i, 0))
    deep_block = pl.BlockSpec((depth, step, width), lambda i: (0, i, 0))
    return pl.pallas_call(
        body,
        grid=(rows // step,),
        out_shape=[
            jax.ShapeDtypeStruct(history.shape, bfloat),
            jax.ShapeDtypeStruct((rows, width), single),
            jax.ShapeDtypeStruct((rows, width), bfloat),
            jax.ShapeDtypeStruct((8 * depth, width), single),
        ],
        in_specs=[pl.BlockSpec(memory_space=pltpu.SMEM), deep_block, row_block]
        + [pl.BlockSpec(memory_space=pl.ANY)] * waits,
        out_specs=[deep_block, row_block, row_block, pl.BlockSpec((8 * depth, width), lambda i: (0, 0))],
        compiler_params=pltpu.CompilerParams(vmem_limit_bytes=16 * MIB),
        cost_estimate=pl.CostEstimate(flops=0, bytes_accessed=0, transcendentals=0),
    )(mix, history, cot, *after)


def combine_body(mix_ref, mixed_ref, mid_ref, keep_ref, recv_ref, cot_ref, parts_ref, out_ref, part_ref):
    depth = mix_ref.shape[0] - 1
    last = jnp.zeros((8, mid_ref.shape[1]), single)
    for span in spans(mid_ref.shape[0]):
        outputs = mid_ref[span, :] + (keep_ref[span, :] + recv_ref[span, :].astype(single))
        out_ref[span, :] = (mixed_ref[span, :] + mix_ref[depth] * outputs).astype(bfloat)
        last = last + fold_rows(outputs * cot_ref[span, :])
    for j in range(depth):
        part_ref[j : j + 1, :] = jnp.sum(parts_ref[8 * j : 8 * j + 8, :], axis=0, keepdims=True)
    part_ref[depth : depth + 1, :] = jnp.sum(last, axis=0, keepdims=True)


SQUARE = 4


def quarter(owner, mask, size):
    other = owner + (mask & 1) * (1 - 2 * (owner % 2)) + (mask & 2) * (1 - 2 * (owner // 2))
    return pl.ds(pl.multiple_of(other * size, size), size)


def part_body(owner_ref, mine_ref, come_ref, *out_refs):
    for mask, out_ref in enumerate(out_refs):
        rows = quarter(owner_ref[0], mask, out_ref.shape[0])
        out_ref[...] = (mine_ref[rows, :].astype(single) + come_ref[rows, :].astype(single)).astype(bfloat)


def sum_of(refs, rows):
    total = refs[0][rows, :].astype(single)
    for ref in refs[1:]:
        total = total + ref[rows, :].astype(single)
    return total


def four_body(*refs):
    refs[-1][...] = sum_of(refs[:-1], slice(None)).astype(bfloat)


def four_two_body(*refs):
    size = refs[-1].shape[0]
    refs[-2][...] = sum_of(refs[:-2], slice(0, size)).astype(bfloat)
    refs[-1][...] = sum_of(refs[:-2], slice(size, 2 * size)).astype(bfloat)


EXTRA = 16


def pair_body(up_ref, up_come_ref, a_ref, b_ref, c_ref, d_ref, out_ref):
    size = up_ref.shape[0]
    out_ref[:size, :] = sum_of((a_ref, b_ref, c_ref, d_ref), slice(None)).astype(bfloat)
    out_ref[size:, :] = sum_of((up_ref, up_come_ref), slice(None)).astype(bfloat)


def part_more_body(owner_ref, mine_ref, come_ref, small_ref, first_ref, *out_refs):
    part_body(owner_ref, mine_ref, come_ref, *out_refs[:-1])
    half = small_ref.shape[0]
    rows = first_ref.shape[0] - 2 * half
    come = first_ref[rows:, :].astype(single)
    out_refs[-1][...] = small_ref[...] + (come[:half] + come[half:])


def four_more_body(small_ref, more_ref, *refs):
    out_ref = refs[-1]
    size = out_ref.shape[0] - EXTRA
    out_ref[:size, :] = sum_of(refs[:-1], slice(None)).astype(bfloat)
    small = small_ref[...] + more_ref[...]
    rest = jnp.zeros((EXTRA - small.shape[0], small.shape[1]), single)
    out_ref[size:, :] = jnp.concatenate([small, rest], axis=0).astype(bfloat)


def gather(owner_ref, pieces, hold):
    for mask, piece in enumerate(pieces):
        hold[quarter(owner_ref[0], mask, piece.shape[0]), :] = piece[...]


def pair_whole_body(owner_ref, a_ref, b_ref, c_ref, d_ref, down_ref, up_ref, hold):
    gather(owner_ref, (a_ref, b_ref, c_ref, d_ref), hold)
    block = hold.shape[0] // SQUARE
    size = block // 2
    for index in range(SQUARE):
        begin, rows = index * block, slice(index * size, (index + 1) * size)
        down_ref[rows, :] = hold[begin : begin + size, :].astype(single)
        up_ref[rows, :] = hold[begin + size : begin + block, :].astype(single)


def more_body(owner_ref, a_ref, b_ref, c_ref, d_ref, top_ref, end_ref, attn_ref, mlp_ref, dwa_ref, hold):
    gather(owner_ref, (a_ref, b_ref, c_ref, d_ref), hold)
    block = hold.shape[0] // SQUARE
    rows = block - EXTRA
    small = jnp.zeros((EXTRA, hold.shape[1]), single)
    for index in range(SQUARE):
        begin = index * block
        target, place = (top_ref, index * rows) if index < SQUARE - 1 else (end_ref, 0)
        target[place : place + rows, :] = hold[begin : begin + rows, :].astype(single)
        small = small + hold[begin + rows : begin + block, :].astype(single)
    attn_ref[...] = small[0]
    mlp_ref[...] = small[1]
    for index in range(dwa_ref.shape[0]):
        dwa_ref[index] = jnp.sum(small[2 + index : 3 + index])


def low_body(mine_ref, come_ref, out_ref):
    out_ref[...] = (mine_ref[...].astype(single) + come_ref[...].astype(single)).astype(bfloat)


def pass_body(in_ref, out_ref, hold, marks):
    go = Mover(marks)
    wait(go((in_ref, hold)))
    wait(go((hold, out_ref)))


def add_body(mine_ref, come_ref, out_ref):
    out_ref[...] = mine_ref[...] + come_ref[...]


def small_body(attn_ref, mlp_ref, dwa_ref, out_ref):
    out_ref[:1, :] = attn_ref[...]
    out_ref[1:2, :] = mlp_ref[...]
    out_ref[2:, :] = dwa_ref[...]


BLOCKS = tuple((begin, min(256, SEQ - begin)) for begin in range(0, SEQ, 256))


def place(core_ref, own_ref, peer_ref, whole):
    low = pl.multiple_of(core_ref[0] * HALF, HALF)
    high = pl.multiple_of((1 - core_ref[0]) * HALF, HALF)
    whole[pl.ds(low, HALF), :] = own_ref[...]
    whole[pl.ds(high, HALF), :] = peer_ref[...]
    return low, high


def allowed(size):
    key_pos = lax.broadcasted_iota(jnp.int32, (size, size), 0)
    query_pos = lax.broadcasted_iota(jnp.int32, (size, size), 1)
    return query_pos >= key_pos


def turn(rows, cosine, sine):
    half = rows.shape[0] // 2
    a, b = rows[:half], rows[half:]
    return jnp.concatenate([a * cosine - b * sine, b * cosine + a * sine], axis=0)


def attend_own(
    core_ref, own_ref, peer_ref, cos_ref, sin_ref, weight_ref, qkv_ref, att_ref, nat_ref, log_ref, tokens
):
    place(core_ref, own_ref, peer_ref, tokens)
    attend(weight_ref, cos_ref, sin_ref, qkv_ref, att_ref, nat_ref, log_ref, tokens)


def attend_peer(
    core_ref, upper_ref, own_ref, peer_ref, cos_ref, sin_ref, mine_ref, other_ref, pass_ref,
    qkv_ref, att_ref, nat_ref, log_ref, weight_out, out_out, pass_out, tokens, weight, out, hold, marks,
):
    go = Mover(marks)
    loads = go(*joined(upper_ref[0], mine_ref, other_ref, 0, weight))
    later = go(*joined(upper_ref[0], mine_ref, other_ref, weight.shape[0] // 2, out), (pass_ref, hold))
    place(core_ref, own_ref, peer_ref, tokens)
    wait(loads)
    wait(later)
    copies = go((weight, weight_out), (out, out_out), (hold, pass_out))
    attend(weight, cos_ref, sin_ref, qkv_ref, att_ref, nat_ref, log_ref, tokens)
    wait(copies)


def attend(weight_ref, cos_ref, sin_ref, qkv_ref, att_ref, nat_ref, log_ref, tokens):
    width = weight_ref.shape[0] // 3
    projected = mul(weight_ref[...], tokens[...], 1, 1)
    cosine, sine = cos_ref[...], sin_ref[...]
    for part in range(3):
        for head in range(width // DH):
            begin = part * width + head * DH
            rows = projected[begin : begin + DH]
            if part < 2:
                rows = turn(rows, cosine, sine)
            if part == 0:
                rows = rows * DH ** (-0.5)
            qkv_ref[begin : begin + DH, :] = rows.astype(bfloat)
    log_ref[...] = jnp.zeros_like(log_ref)
    for head in range(width // DH):
        base = head * DH
        keys = qkv_ref[width + base : width + base + DH, :].T
        for begin, size in BLOCKS:
            end = begin + size
            query = qkv_ref[base : base + DH, begin:end]
            scores = mul(keys[:end], query)
            corner = jnp.where(allowed(size), scores[begin:], -jnp.inf)
            top = jnp.max(corner, axis=0, keepdims=True)
            if begin:
                top = jnp.maximum(top, jnp.max(scores[:begin], axis=0, keepdims=True))
                scores = jnp.concatenate([scores[:begin], corner], axis=0)
            else:
                scores = corner
            weights = jnp.exp(scores - top)
            total = jnp.sum(weights, axis=0, keepdims=True)
            value = qkv_ref[2 * width + base : 2 * width + base + DH, :end]
            mixed = mul(value, weights.astype(bfloat)) / total
            att_ref[base : base + DH, begin:end] = mixed.astype(bfloat)
            log_ref[head : head + 1, begin:end] = top + jnp.log(total)
    nat_ref[...] = att_ref[...].T


def branch_body(core_ref, att_a_ref, att_b_ref, out_a_ref, out_b_ref, keep_ref, *send_refs):
    low = pl.multiple_of(core_ref[0] * HALF, HALF)
    rows = HALF // PARTS
    for index in range(PARTS):
        high = pl.multiple_of((1 - core_ref[0]) * HALF + index * rows, rows)
        send = mul(att_a_ref[pl.ds(high, rows), :], out_a_ref[...])
        send_refs[index][...] = (send + mul(att_b_ref[pl.ds(high, rows), :], out_b_ref[...])).astype(bfloat)
    keep = mul(att_a_ref[pl.ds(low, HALF), :], out_a_ref[...])
    keep_ref[...] = keep + mul(att_b_ref[pl.ds(low, HALF), :], out_b_ref[...])


def attend_back(
    second, core_ref, log_ref, cos_ref, sin_ref, *rest
):
    if second:
        gain_ref, mlp_part_ref, dwa_part_ref, rest = rest[0], rest[1], rest[2], rest[3:]
    grad_own_ref, grad_peer_ref, own_ref, peer_ref, weight_ref, out_weight_ref, qkv_ref, att_ref = rest[:8]
    rest = rest[8:]
    if second:
        turned_b_ref, weight_b_ref, send_ref, small_ref, out_ref, keep_ref = rest[:6]
        grads, tokens, weight, qkv, att, turned, result, marks, turned_b, weight_b, whole = rest[6:]
    else:
        out_ref, turned_ref, grads, tokens, weight, qkv, att, turned, result, marks = rest
    low = pl.multiple_of(core_ref[0] * HALF, HALF)
    high = pl.multiple_of((1 - core_ref[0]) * HALF, HALF)
    go = Mover(marks)
    depth = weight_ref.shape[0]
    first = go(
        (out_weight_ref, weight.at[pl.ds(depth, out_weight_ref.shape[0]), :]),
        (grad_own_ref, grads.at[pl.ds(low, HALF), :]),
        (grad_peer_ref, grads.at[pl.ds(high, HALF), :]),
        (att_ref, att),
        (qkv_ref, qkv),
    )
    later = go(
        (own_ref, tokens.at[pl.ds(low, HALF), :]),
        (peer_ref, tokens.at[pl.ds(high, HALF), :]),
        (weight_ref, weight.at[pl.ds(0, depth), :]),
    )
    if second:
        later += go((turned_b_ref, turned_b), (weight_b_ref, weight_b))
    wait(first)
    width = att.shape[0]
    grad_att = mul(weight[3 * width :, :], grads[...], 1, 1).astype(bfloat)
    result[3 * width :, :] = mul(att[...], grads[...]).astype(result.dtype)
    cosine, sine = cos_ref[...], sin_ref[...]
    for head in range(width // DH):
        base = head * DH
        query = qkv[base : base + DH, :]
        key = qkv[width + base : width + base + DH, :]
        value = qkv[2 * width + base : 2 * width + base + DH, :]
        above = grad_att[base : base + DH]
        centre = jnp.sum(
            above.astype(single) * att[base : base + DH, :].astype(single), axis=0, keepdims=True
        )
        keys, values, queries, aboves = key.T, value.T, query.T, above.T
        grad_query, grad_key, grad_value = [], None, None
        for begin, size in reversed(BLOCKS):
            end = begin + size
            scores = mul(keys[:end], query[:, begin:end])
            corner = jnp.where(allowed(size), scores[begin:], -jnp.inf)
            scores = jnp.concatenate([scores[:begin], corner], axis=0) if begin else corner
            probs = jnp.exp(scores - log_ref[head : head + 1, begin:end])
            grad_probs = mul(values[:end], above[:, begin:end])
            grad_scores = (probs * (grad_probs - centre[:, begin:end])).astype(bfloat)
            grad_query.insert(0, mul(key[:, :end], grad_scores))
            key_part = mul(grad_scores, queries[begin:end])
            value_part = mul(probs.astype(bfloat), aboves[begin:end])
            if grad_key is None:
                grad_key, grad_value = key_part, value_part
            else:
                grad_key = jnp.concatenate([grad_key[:end] + key_part, grad_key[end:]], axis=0)
                grad_value = jnp.concatenate([grad_value[:end] + value_part, grad_value[end:]], axis=0)
        grad_query = jnp.concatenate(grad_query, axis=1) * DH ** (-0.5)
        turned[base : base + DH, :] = turn(grad_query, cosine, -sine).astype(bfloat)
        turned[width + base : width + base + DH, :] = turn(grad_key.T, cosine, -sine).astype(bfloat)
        turned[2 * width + base : 2 * width + base + DH, :] = grad_value.T.astype(bfloat)
    stores = [] if second else go((turned, turned_ref))
    wait(later)
    result[: 3 * width, :] = mul(turned[...], tokens[...]).astype(result.dtype)
    stores += go((result, out_ref))
    if second:
        whole[...] = mul(turned[...], weight[:depth, :], 0, 0) + mul(turned_b[...], weight_b[...], 0, 0)
        stores += go((whole.at[pl.ds(low, HALF), :], keep_ref))
        send_ref[:HALF, :] = whole[pl.ds(high, HALF), :].astype(bfloat)
        part = jnp.zeros((8, whole.shape[1]), single)
        for span in spans(whole.shape[0]):
            part = part + fold_rows(whole[span, :] * tokens[span, :].astype(single))
        small_ref[:1, :] = jnp.sum(part, axis=0, keepdims=True) / gain_ref[...].reshape(1, -1)
        small_ref[1:2, :] = mlp_part_ref[...]
        small_ref[2:, :] = dwa_part_ref[...]
        small = small_ref[...]
        high_part = small.astype(bfloat)
        low_part = (small - high_part.astype(single)).astype(bfloat)
        send_ref[HALF:, :] = jnp.concatenate([high_part, low_part], axis=0)
    wait(stores)


CURVE = float(np.sqrt(2.0 / np.pi))
STEP = 256


def mlp_body(second, *refs):
    if second:
        owner_ref, other_upper_ref, refs = refs[0], refs[1], refs[2:]
    x_refs, refs = refs[: 2 * PARTS], refs[2 * PARTS :]
    g_own_ref, g_peer_ref, refs = refs[0], refs[1], refs[2:]
    if second:
        up_ref, down_refs = refs[0], refs[1:3]
        before_refs, up_mine_ref = refs[3:7], refs[7]
        down_grad_ref, part_refs = refs[12], refs[13:17]
        refs = refs[8:12] + refs[17:]
    else:
        up_ref, down_ref = refs[:2]
        down_grad_ref, up_grad_ref = refs[6:8]
        refs = refs[2:6] + refs[8:]
    send_norm_ref, keep_norm_ref, send_out_ref, keep_out_ref = refs[:4]
    x_all, g_all, up, down, active, grad_hidden, x_turned = refs[4:11]
    send_norm, keep_norm, send_out, keep_out, down_grad, up_grad, marks = refs[11:18]
    rows, size = x_all.shape[0] // 2, x_all.shape[0] // (2 * PARTS)
    units = down.shape[0]
    go = Mover(marks)
    x_loads = go(*[(x_refs[index], x_all.at[pl.ds(index * size, size), :]) for index in range(2 * PARTS)])
    if second:
        loads = go((up_ref, up), *joined(other_upper_ref[0], *down_refs, 0, down))
    else:
        loads = go((up_ref, up), (down_ref, down))
    loads += go((g_own_ref, g_all.at[pl.ds(0, rows), :]), (g_peer_ref, g_all.at[pl.ds(rows, rows), :]))
    more, mine, stores = [], [], []
    if second:
        (up_mine,) = refs[18:]
        more = go(*zip(before_refs, (send_norm, keep_norm, send_out, keep_out)))
        mine = go((up_mine_ref, up_mine))
    wait(x_loads)
    x_turned[...] = x_all[...].T
    wait(loads)
    for begin in range(0, units, STEP):
        columns = slice(begin, begin + STEP)
        for top in range(0, 2 * rows, rows):
            span = slice(top, top + rows)
            v = mul(x_all[span, :], up[:, columns])
            grad = mul(g_all[span, :], down[columns, :], 1, 1)
            square = v * v
            half = 0.5 + 0.5 * jnp.tanh(v * (CURVE + (CURVE * 0.044715) * square))
            act = v * half
            slope = half + act * (1.0 - half) * (2.0 * CURVE + (6.0 * CURVE * 0.044715) * square)
            active[span, columns] = act.astype(bfloat)
            grad_hidden[span, columns] = (grad * slope).astype(bfloat)

    def put(target, value):
        target[...] = (value + target[...].astype(single) if second else value).astype(target.dtype)

    wait(more)
    put(keep_norm, mul(grad_hidden[:rows, :], up[...], 1, 1))
    put(send_norm, mul(grad_hidden[rows:, :], up[...], 1, 1))
    stores += go((keep_norm, keep_norm_ref), (send_norm, send_norm_ref))
    down_grad[...] = mul(active[...], g_all[...], 0, 0).astype(down_grad.dtype)
    stores += go((down_grad, down_grad_ref))
    up_grad[...] = mul(x_turned[...], grad_hidden[...]).astype(bfloat)
    if second:
        wait(mine)
        part = up_grad.shape[0] // SQUARE
        for mask, part_ref in enumerate(part_refs):
            rows_of = quarter(owner_ref[0], mask, part)
            stores += go(
                (up_mine.at[rows_of, :], part_ref.at[pl.ds(0, part), :]),
                (up_grad.at[rows_of, :], part_ref.at[pl.ds(part, part), :]),
            )
    else:
        stores += go((up_grad, up_grad_ref))
    put(keep_out, mul(active[:rows, :], down[...]))
    stores += go((keep_out, keep_out_ref))
    put(send_out, mul(active[rows:, :], down[...]))
    wait(stores + go((send_out, send_out_ref)))


def mlp(x_own, x_peer, g_own, g_peer, up, down, upper=(), before=(), flops=0):
    rows, width = g_own.shape
    units = sum(piece.shape[0] for piece in down)
    tall = (2 * rows, width)
    pair = [((rows, width), bfloat), ((rows, width), single)] * 2
    outs = pair + [((units, width), bfloat)]
    outs += [((2 * width // SQUARE, units), bfloat)] * SQUARE if before else [((width, units), bfloat)]
    scratch = [
        pltpu.VMEM(tall, bfloat),
        pltpu.VMEM(tall, bfloat),
        pltpu.VMEM((width, units), bfloat),
        pltpu.VMEM((units, width), bfloat),
        pltpu.VMEM((2 * rows, units), bfloat),
        pltpu.VMEM((2 * rows, units), bfloat),
        pltpu.VMEM((width, 2 * rows), bfloat),
    ]
    scratch += [pltpu.VMEM(shape, kind) for shape, kind in pair]
    scratch += [
        pltpu.VMEM((units, width), bfloat), pltpu.VMEM((width, units), bfloat), pltpu.SemaphoreType.DMA((32,)),
    ]
    if before:
        scratch.append(pltpu.VMEM((width, units), bfloat))
    operands = (*upper, *x_own, *x_peer, g_own, g_peer, *up, *down, *before)
    return call(
        functools.partial(mlp_body, bool(before)),
        outs,
        operands,
        scratch,
        len(upper),
        vmem=60,
        flops=flops,
        far=len(operands) - len(upper),
        far_outs=len(outs),
    )


def shards(
    inputs,
    history,
    cotangent,
    qkv_weight,
    out_weight,
    up_weight,
    down_weight,
    gain_attn,
    gain_mlp,
    dwa_weights,
):
    rows, width = inputs.shape
    members = lax.axis_size("mp")
    copies = lax.axis_size("dp")
    bits = copies.bit_length() - 1
    core = lax.rem(lax.axis_index("mp"), 2).astype(jnp.int32).reshape(1)
    copy_index = lax.axis_index("dp").astype(jnp.int32).reshape(1)
    core_pairs = [(i, i ^ 1) for i in range(members)]
    chip_pairs = [(i, i ^ 2) for i in range(members)]
    depth = history.shape[0]
    part = out_weight.shape[0]

    def other_core(value):
        return lax.ppermute(value, "mp", core_pairs)

    def other_chip(value):
        return lax.ppermute(value, "mp", chip_pairs)

    def other_copy(value, mask):
        return lax.ppermute(value, "dp", [(i, i ^ mask) for i in range(copies)])

    owner = copy_index & (SQUARE - 1)
    uppers = [copy_index & 1]
    cosine, sine = (jnp.asarray(table) for table in tables())

    qkv_own = qkv_weight.transpose(1, 2, 0).reshape(3 * part, width)
    half = (width // 2, width)
    square = (width, width)
    marks = pltpu.SemaphoreType.DMA((16,))
    halves = call(
        split_body,
        [(half, bfloat)] * 2,
        (uppers[0], qkv_own, out_weight, down_weight),
        [pltpu.VMEM(half, bfloat), pltpu.VMEM(half, bfloat), marks],
        1,
        vmem=60,
        far=3,
        far_outs=2,
    )
    both_come, down_come = map(other_chip, halves)

    up_peer = other_chip(up_weight)

    full = (rows, width)
    (x_own,) = call(norm_body, [(full, bfloat)], (inputs, gain_attn), after=(halves[0],))
    x_peer = other_core(x_own)
    tall = (SEQ, width)
    tokens = pltpu.VMEM(tall, bfloat)
    first_outs = [
        ((3 * part, SEQ), bfloat), ((part, SEQ), bfloat), ((SEQ, part), bfloat), ((8, SEQ), single),
    ]
    qkv_a, att_a, nat_a, log_a = call(
        attend_own,
        first_outs,
        (core, x_own, x_peer, cosine, sine, qkv_own),
        [tokens],
        1,
        vmem=32,
    )
    (both_copy,) = call(
        pass_body, [(half, bfloat)], (both_come,), [pltpu.VMEM(half, bfloat), marks], after=(log_a,), far=1, far_outs=1
    )
    both_come = (both_come, other_copy(both_copy, 1))
    history_grad, mixed, g_own, history_parts = average_history(dwa_weights, history, cotangent, (both_copy,))
    g_peer = other_core(g_own)
    qkv_b, att_b, nat_b, log_b, qkv_peer, out_peer, down_copy = call(
        attend_peer,
        first_outs + [(qkv_own.shape, bfloat), (out_weight.shape, bfloat), (half, bfloat)],
        (core, uppers[0], x_own, x_peer, cosine, sine, *both_come, down_come),
        [
            tokens,
            pltpu.VMEM(qkv_own.shape, bfloat),
            pltpu.VMEM(out_weight.shape, bfloat),
            pltpu.VMEM(half, bfloat),
            marks,
        ],
        2,
        (history_parts,),
        32,
        MUCH,
        far=3,
        far_outs=3,
    )
    down_come = (down_come, other_copy(down_copy, 1))
    third = (rows // PARTS, width)
    keep, *send = call(
        branch_body,
        [(full, single)] + [(third, bfloat)] * PARTS,
        (core, nat_a, nat_b, out_weight, out_peer),
        scalars=1,
    )
    recv = [other_core(value) for value in send]
    middle, *y_own = call(
        middle_body, [(full, single)] + [(third, bfloat)] * PARTS, (inputs, keep, gain_mlp, *recv),
    )
    y_peer = [other_core(value) for value in y_own]

    first = mlp(y_own, y_peer, g_own, g_peer, (up_weight,), (down_weight,))
    down_mine, up_mine = first[4:]
    second = mlp(
        y_own, y_peer, g_own, g_peer, (up_peer,), down_come, (owner, uppers[0]), (*first[:4], up_mine)
    )
    send_norm, keep_norm, send_out, keep_out, down_theirs = second[:5]
    token = [send_norm]

    def step(body, outs, operands, scratch=(), scalars=0, vmem=16, flops=MUCH, far=0, far_outs=0):
        results = call(body, outs, operands, scratch, scalars, tuple(token), vmem, flops, far, far_outs)
        token[0] = results[0]
        return results

    masks = range(1, SQUARE)
    down_come = other_chip(down_theirs)
    up_parts = [second[5]] + [other_copy(value, mask) for mask, value in zip(masks, second[6:])]
    out_come = other_core(send_out)
    grad_middle, gb_own, gain_mlp_part = step(
        middle_back_body,
        [(full, single), (full, bfloat), ((1, width), single)],
        (dwa_weights, middle, keep_norm, other_core(send_norm), cotangent, gain_mlp),
        scalars=1,
        flops=0,
    )
    gb_peer = other_core(gb_own)
    combined, dwa_part = step(
        combine_body,
        [(full, bfloat), ((depth + 1, width), single)],
        (dwa_weights, mixed, middle, keep_out, out_come, cotangent, history_parts),
        scalars=1,
        flops=0,
    )

    def back(second, kind, outs, operands, flops, far, scratch=()):
        return step(
            functools.partial(attend_back, second),
            outs,
            operands,
            [
                pltpu.VMEM(tall, bfloat),
                pltpu.VMEM(tall, bfloat),
                pltpu.VMEM((4 * part, width), bfloat),
                pltpu.VMEM((3 * part, SEQ), bfloat),
                pltpu.VMEM((part, SEQ), bfloat),
                pltpu.VMEM((3 * part, SEQ), bfloat),
                pltpu.VMEM((4 * part, width), kind),
                marks,
                *scratch,
            ],
            1,
            60,
            flops,
            far,
            2,
        )

    shared = (cosine, sine, gb_own, gb_peer, x_own, x_peer)
    att_theirs, turned_b = back(
        False,
        bfloat,
        [((4 * part, width), bfloat), ((3 * part, SEQ), bfloat)],
        (core, log_b, *shared, qkv_peer, out_peer, qkv_b, att_b),
        0,
        8,
    )
    att_come = other_chip(att_theirs)
    fourth = (width // SQUARE, width)

    def spread(mine, come, flops=MUCH):
        own, *sent = step(part_body, [(fourth, bfloat)] * SQUARE, (owner, mine, come), scalars=1, flops=flops)
        return [own] + [other_copy(value, mask) for mask, value in zip(masks, sent)]

    down_parts = spread(down_mine, down_come, 0)
    up, sent = step(four_two_body, [(fourth, bfloat)] * 2, up_parts, flops=0)
    up_come = other_chip(sent)
    send_first, part_sums, att_mine, keep_first = back(
        True,
        bfloat,
        [
            ((rows + EXTRA, width), bfloat),
            ((EXTRA // 2, width), single),
            ((4 * part, width), bfloat),
            (full, single),
        ],
        (core, log_a, cosine, sine, gain_attn, gain_mlp_part, dwa_part, *shared[2:], qkv_own, out_weight, qkv_a, att_a, turned_b, qkv_peer),
        MUCH,
        10,
        [pltpu.VMEM((3 * part, SEQ), bfloat), pltpu.VMEM((3 * part, width), bfloat), pltpu.VMEM(tall, single)],
    )
    first_come = other_core(send_first)

    def exchange(value):
        for bit in range(2, bits):
            come = other_copy(value, 1 << bit)
            if bit < bits - 1:
                (value,) = step(low_body, [(value.shape, bfloat)], (value, come))
        return value, come

    def finish(value, come):
        (value,) = step(low_body, [(value.shape, bfloat)], (value, come), flops=COST * 7)
        return [value] + [other_copy(value, mask) for mask in masks]

    pair = (2 * width // SQUARE, width)
    (both,) = step(pair_body, [(pair, bfloat)], (up, up_come, *down_parts), flops=COST * 4)
    both = exchange(both)
    own, *sent, part_sums = step(
        part_more_body,
        [(fourth, bfloat)] * SQUARE + [(part_sums.shape, single)],
        (owner, att_mine, att_come, part_sums, first_come),
        scalars=1,
        flops=COST * 8,
    )
    att_parts = [own] + [other_copy(value, mask) for mask, value in zip(masks, sent)]
    more_sums = other_chip(part_sums)
    (input_grad,) = step(
        first_back_body,
        [(full, bfloat)],
        (inputs, keep_first, first_come, grad_middle, gain_attn),
        vmem=60,
        flops=COST * 5,
    )
    block = (width // SQUARE + EXTRA, width)
    (att,) = step(four_more_body, [(block, bfloat)], (part_sums, more_sums, *att_parts), flops=COST * 4)
    att = exchange(att)
    both = finish(*both)
    att = finish(*att)
    down_grad, up_grad = step(
        pair_whole_body,
        [(square, single)] * 2,
        (owner, *both),
        [pltpu.VMEM((SQUARE * pair[0], width), bfloat)],
        1,
        flops=COST * 5,
    )
    qkv_grad, out_grad, gain_attn_grad, gain_mlp_grad, dwa_grad = step(
        more_body,
        [
            ((3 * part, width), single),
            ((part, width), single),
            ((width,), single),
            ((width,), single),
            ((depth + 1,), single, "scalars"),
        ],
        (owner, *att),
        [pltpu.VMEM((SQUARE * block[0], width), bfloat)],
        1,
        flops=COST * 5,
    )

    return (
        combined,
        input_grad,
        history_grad,
        qkv_grad.reshape(3, part, width).transpose(2, 0, 1),
        out_grad,
        up_grad,
        down_grad,
        gain_attn_grad,
        gain_mlp_grad,
        dwa_grad,
    )


def solution(mesh):
    placed = (
        P(("dp", "mp"), None),
        P(None, ("dp", "mp"), None),
        P(("dp", "mp"), None),
        P(None, None, "mp"),
        P("mp", None),
        P(None, "mp"),
        P("mp", None),
        P(),
        P(),
        P(),
    )
    return jax.shard_map(
        shards,
        mesh=mesh,
        in_specs=placed,
        out_specs=(
            P(("dp", "mp"), None),
            P(("dp", "mp"), None),
            P(None, ("dp", "mp"), None),
            P(None, None, "mp"),
            P("mp", None),
            P(None, "mp"),
            P("mp", None),
            P(),
            P(),
            P(),
        ),
        check_vma=False,
    )
```

```python
import functools

import jax
import jax.numpy as jnp
import numpy as np
from jax import lax
from jax.experimental import pallas as pl
from jax.experimental.pallas import tpu as pltpu
from jax.sharding import PartitionSpec as P

DH = 64
SEQ = 1152
HALF = SEQ // 2
EPS = 1e-05
bfloat = jnp.bfloat16
single = jnp.float32
MIB = 1 << 20
MUCH = 10**11
COST = 10**10


def tables():
    half_width = DH // 2
    places = np.arange(SEQ, dtype=np.float32)
    frequency = np.float32(10000.0) ** (-np.arange(half_width, dtype=np.float32) * np.float32(2.0 / DH))
    angles = frequency[:, None] * places[None, :]
    return (np.cos(angles).astype(np.float32), np.sin(angles).astype(np.float32))


def mul(a, b, ca=1, cb=0):
    return lax.dot_general(a, b, (((ca,), (cb,)), ((), ())), preferred_element_type=single)


def call(kernel, outs, operands, scratch=(), scalars=0, after=(), vmem=16, flops=0, far=0, far_outs=0):
    count, waits = len(operands), len(after)

    def body(*refs):
        kernel(*refs[:count], *refs[count + waits :])

    small = pl.BlockSpec(memory_space=pltpu.SMEM)
    whole = pl.BlockSpec(memory_space=pltpu.VMEM)
    apart = pl.BlockSpec(memory_space=pltpu.HBM)
    loose = pl.BlockSpec(memory_space=pl.ANY)
    inner = len(outs) - far_outs
    return pl.pallas_call(
        body,
        out_shape=[jax.ShapeDtypeStruct(out[0], out[1]) for out in outs],
        in_specs=[small] * scalars + [whole] * (count - scalars - far) + [apart] * far + [loose] * waits,
        out_specs=[small if len(out) > 2 else whole for out in outs[:inner]] + [apart] * far_outs,
        scratch_shapes=list(scratch),
        compiler_params=pltpu.CompilerParams(vmem_limit_bytes=vmem * MIB),
        cost_estimate=pl.CostEstimate(flops=flops, bytes_accessed=0, transcendentals=0),
    )(*operands, *after)


class Mover:
    def __init__(self, marks):
        self.marks = marks
        self.used = 0

    def __call__(self, *pairs):
        copies = []
        for source, target in pairs:
            copies.append(pltpu.make_async_copy(source, target, self.marks.at[self.used]))
            self.used += 1
        for copy in copies:
            copy.start()
        return copies


def wait(copies):
    for copy in copies:
        copy.wait()


ROWS = 64
PARTS = 1


def spans(rows, step=ROWS):
    return [slice(begin, begin + step) for begin in range(0, rows, step)]


def normal_of(x):
    centre = x - jnp.mean(x, axis=-1, keepdims=True)
    spread = jnp.mean(centre * centre, axis=-1, keepdims=True)
    scale = lax.rsqrt(spread + EPS)
    return centre * scale, scale


def split_body(owner_ref, in_ref, out_ref, hold, marks):
    go = Mover(marks)
    wait(go((in_ref.at[quarter(owner_ref[0], 0, hold.shape[0]), :], hold)))
    wait(go((hold, out_ref)))


def joined(owner, refs, target):
    size = refs[0].shape[0]
    return [(ref, target.at[quarter(owner, mask, size), :]) for mask, ref in enumerate(refs)]


def norm_body(x_ref, gain_ref, out_ref):
    gain = gain_ref[...].reshape(1, -1)
    for span in spans(x_ref.shape[0]):
        normal, _ = normal_of(x_ref[span, :].astype(single))
        out_ref[span, :] = (normal * gain).astype(bfloat)


def middle_body(x_ref, keep_ref, gain_ref, *rest):
    recv_refs, mid_ref, out_refs = rest[:PARTS], rest[PARTS], rest[PARTS + 1 :]
    gain = gain_ref[...].reshape(1, -1)
    rows = x_ref.shape[0] // PARTS
    for index in range(PARTS):
        for span in spans(rows):
            here = slice(index * rows + span.start, index * rows + span.stop)
            recv = recv_refs[index][span, :].astype(single)
            x = x_ref[here, :].astype(single) + (keep_ref[here, :] + recv)
            mid_ref[here, :] = x
            normal, _ = normal_of(x)
            out_refs[index][span, :] = (normal * gain).astype(bfloat)


def norm_back(x, grad, gain):
    normal, scale = normal_of(x)
    lifted = grad * gain
    back = scale * (
        lifted
        - jnp.mean(lifted, axis=-1, keepdims=True)
        - normal * jnp.mean(lifted * normal, axis=-1, keepdims=True)
    )
    return back, normal


def fold_rows(value):
    total = value[:8]
    for begin in range(8, value.shape[0], 8):
        total = total + value[begin : begin + 8]
    return total


def middle_back_body(mix_ref, x_ref, keep_ref, recv_ref, cot_ref, gain_ref, mid_ref, low_ref, part_ref):
    gain = gain_ref[...].reshape(1, -1)
    part = jnp.zeros((8, x_ref.shape[1]), single)
    for span in spans(x_ref.shape[0]):
        grad = keep_ref[span, :] + recv_ref[span, :].astype(single)
        back, normal = norm_back(x_ref[span, :], grad, gain)
        total = mix_ref[mix_ref.shape[0] - 1] * cot_ref[span, :] + back
        mid_ref[span, :] = total
        low_ref[span, :] = total.astype(bfloat)
        part = part + fold_rows(grad * normal)
    part_ref[...] = jnp.sum(part, axis=0, keepdims=True)


def first_back_body(x_ref, keep_ref, recv_ref, mid_ref, gain_ref, out_ref):
    gain = gain_ref[...].reshape(1, -1)
    for span in spans(x_ref.shape[0]):
        grad = keep_ref[span, :] + recv_ref[span, :].astype(single)
        back, _ = norm_back(x_ref[span, :].astype(single), grad, gain)
        out_ref[span, :] = (mid_ref[span, :] + back).astype(bfloat)


def history_body(mix_ref, history_ref, cot_ref, grad_ref, mixed_ref, low_ref, part_ref):
    depth = history_ref.shape[0]

    @pl.when(pl.program_id(0) == 0)
    def _():
        part_ref[...] = jnp.zeros_like(part_ref)

    for span in spans(cot_ref.shape[0], 32):
        cot = cot_ref[span, :]
        low_ref[span, :] = (mix_ref[depth] * cot).astype(bfloat)
        mixed = None
        for j in range(depth):
            layer = history_ref[j, span, :].astype(single)
            mixed = mix_ref[j] * layer if mixed is None else mixed + mix_ref[j] * layer
            grad_ref[j, span, :] = (mix_ref[j] * cot).astype(bfloat)
            part_ref[8 * j : 8 * j + 8, :] += fold_rows(layer * cot)
        mixed_ref[span, :] = mixed


def average_history(mix, history, cot, after=()):
    depth, rows, width = history.shape
    step = 96
    waits = len(after)

    def body(*refs):
        history_body(*refs[:3], *refs[3 + waits :])

    row_block = pl.BlockSpec((step, width), lambda i: (i, 0))
    deep_block = pl.BlockSpec((depth, step, width), lambda i: (0, i, 0))
    return pl.pallas_call(
        body,
        grid=(rows // step,),
        out_shape=[
            jax.ShapeDtypeStruct(history.shape, bfloat),
            jax.ShapeDtypeStruct((rows, width), single),
            jax.ShapeDtypeStruct((rows, width), bfloat),
            jax.ShapeDtypeStruct((8 * depth, width), single),
        ],
        in_specs=[pl.BlockSpec(memory_space=pltpu.SMEM), deep_block, row_block]
        + [pl.BlockSpec(memory_space=pl.ANY)] * waits,
        out_specs=[deep_block, row_block, row_block, pl.BlockSpec((8 * depth, width), lambda i: (0, 0))],
        compiler_params=pltpu.CompilerParams(vmem_limit_bytes=16 * MIB),
        cost_estimate=pl.CostEstimate(flops=0, bytes_accessed=0, transcendentals=0),
    )(mix, history, cot, *after)


def combine_body(mix_ref, mixed_ref, mid_ref, keep_ref, recv_ref, cot_ref, parts_ref, out_ref, part_ref):
    depth = mix_ref.shape[0] - 1
    last = jnp.zeros((8, mid_ref.shape[1]), single)
    for span in spans(mid_ref.shape[0]):
        outputs = mid_ref[span, :] + (keep_ref[span, :] + recv_ref[span, :].astype(single))
        out_ref[span, :] = (mixed_ref[span, :] + mix_ref[depth] * outputs).astype(bfloat)
        last = last + fold_rows(outputs * cot_ref[span, :])
    for j in range(depth):
        part_ref[j : j + 1, :] = jnp.sum(parts_ref[8 * j : 8 * j + 8, :], axis=0, keepdims=True)
    part_ref[depth : depth + 1, :] = jnp.sum(last, axis=0, keepdims=True)


SQUARE = 4


def quarter(owner, mask, size):
    other = owner + (mask & 1) * (1 - 2 * (owner % 2)) + (mask & 2) * (1 - 2 * (owner // 2))
    return pl.ds(pl.multiple_of(other * size, size), size)


def part_body(owner_ref, mine_ref, come_ref, *out_refs):
    for mask, out_ref in enumerate(out_refs):
        rows = quarter(owner_ref[0], mask, out_ref.shape[0])
        out_ref[...] = (mine_ref[rows, :].astype(single) + come_ref[rows, :].astype(single)).astype(bfloat)


def sum_of(refs, rows):
    total = refs[0][rows, :].astype(single)
    for ref in refs[1:]:
        total = total + ref[rows, :].astype(single)
    return total


def four_body(*refs):
    refs[-1][...] = sum_of(refs[:-1], slice(None)).astype(bfloat)


def four_two_body(*refs):
    size = refs[-1].shape[0]
    refs[-2][...] = sum_of(refs[:-2], slice(0, size)).astype(bfloat)
    refs[-1][...] = sum_of(refs[:-2], slice(size, 2 * size)).astype(bfloat)


EXTRA = 16


def add_body(mine_ref, come_ref, out_ref):
    out_ref[...] = mine_ref[...] + come_ref[...]


def four_more_body(small_ref, more_ref, *refs):
    out_ref = refs[-1]
    size = out_ref.shape[0] - EXTRA
    out_ref[:size, :] = sum_of(refs[:-1], slice(None)).astype(bfloat)
    small = small_ref[...] + more_ref[...]
    rest = jnp.zeros((EXTRA - small.shape[0], small.shape[1]), single)
    out_ref[size:, :] = jnp.concatenate([small, rest], axis=0).astype(bfloat)


def gather(owner_ref, pieces, hold):
    for mask, piece in enumerate(pieces):
        hold[quarter(owner_ref[0], mask, piece.shape[0]), :] = piece[...]


def pair_body(a_ref, a_come_ref, b_ref, b_come_ref, out_ref):
    size = a_ref.shape[0]
    out_ref[:size, :] = sum_of((a_ref, a_come_ref), slice(None)).astype(bfloat)
    out_ref[size:, :] = sum_of((b_ref, b_come_ref), slice(None)).astype(bfloat)


def pair_whole_body(owner_ref, a_ref, b_ref, c_ref, d_ref, down_ref, up_ref, hold):
    gather(owner_ref, (a_ref, b_ref, c_ref, d_ref), hold)
    block = hold.shape[0] // SQUARE
    size = block // 2
    for index in range(SQUARE):
        begin, rows = index * block, slice(index * size, (index + 1) * size)
        down_ref[rows, :] = hold[begin : begin + size, :].astype(single)
        up_ref[rows, :] = hold[begin + size : begin + block, :].astype(single)


def more_body(owner_ref, a_ref, b_ref, c_ref, d_ref, top_ref, end_ref, attn_ref, mlp_ref, dwa_ref, hold):
    gather(owner_ref, (a_ref, b_ref, c_ref, d_ref), hold)
    block = hold.shape[0] // SQUARE
    rows = block - EXTRA
    small = jnp.zeros((EXTRA, hold.shape[1]), single)
    for index in range(SQUARE):
        begin = index * block
        target, place = (top_ref, index * rows) if index < SQUARE - 1 else (end_ref, 0)
        target[place : place + rows, :] = hold[begin : begin + rows, :].astype(single)
        small = small + hold[begin + rows : begin + block, :].astype(single)
    attn_ref[...] = small[0]
    mlp_ref[...] = small[1]
    for index in range(dwa_ref.shape[0]):
        dwa_ref[index] = jnp.sum(small[2 + index : 3 + index])


def low_body(mine_ref, come_ref, out_ref):
    out_ref[...] = (mine_ref[...].astype(single) + come_ref[...].astype(single)).astype(bfloat)


def add_body(mine_ref, come_ref, out_ref):
    out_ref[...] = mine_ref[...] + come_ref[...]


BLOCKS = tuple((begin, min(256, SEQ - begin)) for begin in range(0, SEQ, 256))


def place(core_ref, own_ref, peer_ref, whole):
    low = pl.multiple_of(core_ref[0] * HALF, HALF)
    high = pl.multiple_of((1 - core_ref[0]) * HALF, HALF)
    whole[pl.ds(low, HALF), :] = own_ref[...]
    whole[pl.ds(high, HALF), :] = peer_ref[...]
    return low, high


def allowed(size):
    key_pos = lax.broadcasted_iota(jnp.int32, (size, size), 0)
    query_pos = lax.broadcasted_iota(jnp.int32, (size, size), 1)
    return query_pos >= key_pos


def turn(rows, cosine, sine):
    half = rows.shape[0] // 2
    a, b = rows[:half], rows[half:]
    return jnp.concatenate([a * cosine - b * sine, b * cosine + a * sine], axis=0)


KEYS = 128


def fold_top(value):
    top = value[:8]
    for begin in range(8, value.shape[0], 8):
        top = jnp.maximum(top, value[begin : begin + 8])
    return top


def masked(scores, offset):
    key_pos = lax.broadcasted_iota(jnp.int32, scores.shape, 0) + offset
    query_pos = lax.broadcasted_iota(jnp.int32, scores.shape, 1)
    return jnp.where(query_pos >= key_pos, scores, -jnp.inf)


def attend_placed(core_ref, own_ref, peer_ref, cos_ref, sin_ref, weight_ref, *rest):
    place(core_ref, own_ref, peer_ref, rest[4])
    attend(weight_ref, cos_ref, sin_ref, *rest)


def attend(weight_ref, cos_ref, sin_ref, qkv_ref, att_ref, nat_ref, log_ref, tokens, all_scores, all_weights):
    width = weight_ref.shape[0] // 3
    projected = mul(weight_ref[...], tokens[...], 1, 1)
    cosine, sine = cos_ref[...], sin_ref[...]
    for part in range(3):
        for head in range(width // DH):
            begin = part * width + head * DH
            rows = projected[begin : begin + DH]
            if part < 2:
                rows = turn(rows, cosine, sine)
            if part == 0:
                rows = rows * DH ** (-0.5)
            qkv_ref[begin : begin + DH, :] = rows.astype(bfloat)
    log_ref[...] = jnp.zeros_like(log_ref)
    turn_of = 0
    for head in range(width // DH):
        base = head * DH
        keys = qkv_ref[width + base : width + base + DH, :].T
        for begin, size in BLOCKS:
            end = begin + size
            scores, weights = all_scores.at[turn_of % 2], all_weights.at[turn_of % 2]
            turn_of += 1
            query = qkv_ref[base : base + DH, begin:end]
            top = None
            for row in range(0, end, KEYS):
                tile = mul(keys[row : row + KEYS], query)
                if row >= begin:
                    tile = masked(tile, row - begin)
                scores[row : row + KEYS, :size] = tile
                top = fold_top(tile) if top is None else jnp.maximum(top, fold_top(tile))
            top = jnp.max(top, axis=0, keepdims=True)
            total = jnp.zeros((8, size), single)
            for row in range(0, end, KEYS):
                tile = jnp.exp(scores[row : row + KEYS, :size] - top)
                total = total + fold_rows(tile)
                weights[row : row + KEYS, :size] = tile.astype(bfloat)
            total = jnp.sum(total, axis=0, keepdims=True)
            value = qkv_ref[2 * width + base : 2 * width + base + DH, :end]
            mixed = mul(value, weights[:end, :size]) / total
            att_ref[base : base + DH, begin:end] = mixed.astype(bfloat)
            log_ref[head : head + 1, begin:end] = top + jnp.log(total)
    nat_ref[...] = att_ref[...].T


def branch_body(core_ref, att_a_ref, att_b_ref, out_a_ref, out_b_ref, pass_ref, keep_ref, *rest):
    send_refs, pass_out, hold, marks = rest[:PARTS], rest[PARTS], rest[PARTS + 1], rest[PARTS + 2]
    go = Mover(marks)
    wait(go((pass_ref, hold)))
    stores = go((hold, pass_out))
    low = pl.multiple_of(core_ref[0] * HALF, HALF)
    rows = HALF // PARTS
    for index in range(PARTS):
        high = pl.multiple_of((1 - core_ref[0]) * HALF + index * rows, rows)
        send = mul(att_a_ref[pl.ds(high, rows), :], out_a_ref[...])
        send_refs[index][...] = (send + mul(att_b_ref[pl.ds(high, rows), :], out_b_ref[...])).astype(bfloat)
    keep = mul(att_a_ref[pl.ds(low, HALF), :], out_a_ref[...])
    keep_ref[...] = keep + mul(att_b_ref[pl.ds(low, HALF), :], out_b_ref[...])
    wait(stores)


def attend_back(
    core_ref, log_ref, cos_ref, sin_ref, gain_ref, *rest
):
    before_refs, rest = rest[:-23], rest[-23:]
    grad_own_ref, grad_peer_ref, own_ref, peer_ref, weight_ref, qkv_weight_ref, qkv_ref, att_ref = rest[:8]
    small_ref, out_ref, turned_ref = rest[8:11]
    grads, tokens, weight, qkv_weight, qkv, att, turned, result, all_probs, all_scores, hold, marks = rest[11:]
    low = pl.multiple_of(core_ref[0] * HALF, HALF)
    high = pl.multiple_of((1 - core_ref[0]) * HALF, HALF)
    go = Mover(marks)
    first = go(
        (weight_ref, weight),
        (grad_own_ref, grads.at[pl.ds(low, HALF), :]),
        (grad_peer_ref, grads.at[pl.ds(high, HALF), :]),
        (att_ref, att),
        (qkv_ref, qkv),
    )
    later = go(
        (own_ref, tokens.at[pl.ds(low, HALF), :]),
        (peer_ref, tokens.at[pl.ds(high, HALF), :]),
        (qkv_weight_ref, qkv_weight),
    )
    wait(first)
    width = att.shape[0]
    grad_att = mul(weight[...], grads[...], 1, 1).astype(bfloat)
    result[3 * width :, :] = mul(att[...], grads[...]).astype(result.dtype)
    cosine, sine = cos_ref[...], sin_ref[...]
    for head in range(width // DH):
        base = head * DH
        probs, scores = all_probs.at[head % 2], all_scores.at[head % 2]
        query = qkv[base : base + DH, :]
        key = qkv[width + base : width + base + DH, :]
        value = qkv[2 * width + base : 2 * width + base + DH, :]
        above = grad_att[base : base + DH]
        centre = jnp.sum(
            above.astype(single) * att[base : base + DH, :].astype(single), axis=0, keepdims=True
        )
        keys, values, queries, aboves = key.T, value.T, query.T, above.T
        grad_query = []
        for begin, size in BLOCKS:
            end = begin + size
            logs = log_ref[head : head + 1, begin:end]
            for row in range(0, end, KEYS):
                span = slice(row, row + KEYS)
                tile = mul(keys[span], query[:, begin:end])
                if row >= begin:
                    tile = masked(tile, row - begin)
                tile = jnp.exp(tile - logs)
                grad = mul(values[span], above[:, begin:end]) - centre[:, begin:end]
                probs[span, begin:end] = tile.astype(bfloat)
                scores[span, begin:end] = (tile * grad).astype(bfloat)
            grad_query.append(mul(key[:, :end], scores[:end, begin:end]))
        grad_query = jnp.concatenate(grad_query, axis=1) * DH ** (-0.5)
        turned[base : base + DH, :] = turn(grad_query, cosine, -sine).astype(bfloat)
        grad_key, grad_value = [], []
        for begin, size in BLOCKS:
            span = slice(begin, begin + size)
            grad_key.append(mul(scores[span, begin:], queries[begin:]))
            grad_value.append(mul(probs[span, begin:], aboves[begin:]))
        grad_key = jnp.concatenate(grad_key, axis=0).T
        turned[width + base : width + base + DH, :] = turn(grad_key, cosine, -sine).astype(bfloat)
        grad_value = jnp.concatenate(grad_value, axis=0).T
        turned[2 * width + base : 2 * width + base + DH, :] = grad_value.astype(bfloat)
    stores = go((turned, turned_ref))
    wait(later)
    hold[...] = mul(turned[...], tokens[...])
    result[: 3 * width, :] = hold[...].astype(result.dtype)
    stores += go((result, out_ref))
    part = jnp.zeros((8, hold.shape[1]), single)
    for span in spans(hold.shape[0]):
        part = part + fold_rows(hold[span, :] * qkv_weight[span, :].astype(single))
    gain = jnp.sum(part, axis=0, keepdims=True) / gain_ref[...].reshape(1, -1)
    if before_refs:
        gain_part_ref, mlp_part_ref, dwa_part_ref = before_refs
        small_ref[:1, :] = gain + gain_part_ref[...]
        small_ref[1:2, :] = mlp_part_ref[...]
        small_ref[2:, :] = dwa_part_ref[...]
    else:
        small_ref[...] = gain
    wait(stores)


def first_grad_body(
    core_ref, turned_a_ref, turned_b_ref, weight_a_ref, weight_b_ref, send_ref, keep_ref,
    turned_a, turned_b, weight_a, weight_b, whole, marks,
):
    low = pl.multiple_of(core_ref[0] * HALF, HALF)
    high = pl.multiple_of((1 - core_ref[0]) * HALF, HALF)
    go = Mover(marks)
    wait(go((turned_a_ref, turned_a), (weight_a_ref, weight_a), (turned_b_ref, turned_b), (weight_b_ref, weight_b)))
    whole[...] = mul(turned_a[...], weight_a[...], 0, 0) + mul(turned_b[...], weight_b[...], 0, 0)
    stores = go((whole.at[pl.ds(low, HALF), :], keep_ref))
    send_ref[...] = whole[pl.ds(high, HALF), :].astype(bfloat)
    wait(stores)


CURVE = float(np.sqrt(2.0 / np.pi))
STEP = 256


def mlp_body(second, *refs):
    if second:
        owner_ref, refs = refs[0], refs[1:]
    x_refs, refs = refs[: 2 * PARTS], refs[2 * PARTS :]
    g_own_ref, g_peer_ref, refs = refs[0], refs[1], refs[2:]
    if second:
        up_ref, down_refs, refs = refs[0], refs[1 : 1 + SQUARE], refs[1 + SQUARE :]
        before_refs, up_mine_ref = refs[:4], refs[4]
        down_grad_ref, part_refs = refs[9], refs[10:14]
        refs = refs[5:9] + refs[14:]
    else:
        up_ref, down_ref = refs[:2]
        down_grad_ref, up_grad_ref = refs[6:8]
        refs = refs[2:6] + refs[8:]
    send_norm_ref, keep_norm_ref, send_out_ref, keep_out_ref = refs[:4]
    x_all, g_all, up, down, active, grad_hidden, x_turned = refs[4:11]
    send_norm, keep_norm, send_out, keep_out, down_grad, up_grad, marks = refs[11:18]
    rows, size = x_all.shape[0] // 2, x_all.shape[0] // (2 * PARTS)
    units = down.shape[0]
    go = Mover(marks)
    x_loads = go(*[(x_refs[index], x_all.at[pl.ds(index * size, size), :]) for index in range(2 * PARTS)])
    if second:
        loads = go((up_ref, up), *joined(owner_ref[0], down_refs, down))
    else:
        loads = go((up_ref, up), (down_ref, down))
    loads += go((g_own_ref, g_all.at[pl.ds(0, rows), :]), (g_peer_ref, g_all.at[pl.ds(rows, rows), :]))
    more, mine, stores = [], [], []
    if second:
        (up_mine,) = refs[18:]
        more = go(*zip(before_refs, (send_norm, keep_norm, send_out, keep_out)))
        mine = go((up_mine_ref, up_mine))
    wait(x_loads)
    x_turned[...] = x_all[...].T
    wait(loads)
    for begin in range(0, units, STEP):
        columns = slice(begin, begin + STEP)
        for top in range(0, 2 * rows, rows):
            span = slice(top, top + rows)
            v = mul(x_all[span, :], up[:, columns])
            grad = mul(g_all[span, :], down[columns, :], 1, 1)
            square = v * v
            half = 0.5 + 0.5 * jnp.tanh(v * (CURVE + (CURVE * 0.044715) * square))
            act = v * half
            slope = half + act * (1.0 - half) * (2.0 * CURVE + (6.0 * CURVE * 0.044715) * square)
            active[span, columns] = act.astype(bfloat)
            grad_hidden[span, columns] = (grad * slope).astype(bfloat)

    def put(target, value):
        target[...] = (value + target[...].astype(single) if second else value).astype(target.dtype)

    wait(more)
    put(keep_norm, mul(grad_hidden[:rows, :], up[...], 1, 1))
    put(send_norm, mul(grad_hidden[rows:, :], up[...], 1, 1))
    stores += go((keep_norm, keep_norm_ref), (send_norm, send_norm_ref))
    down_grad[...] = mul(active[...], g_all[...], 0, 0).astype(down_grad.dtype)
    stores += go((down_grad, down_grad_ref))
    up_grad[...] = mul(x_turned[...], grad_hidden[...]).astype(bfloat)
    if second:
        wait(mine)
        part = up_grad.shape[0] // SQUARE
        for mask, part_ref in enumerate(part_refs):
            rows_of = quarter(owner_ref[0], mask, part)
            stores += go(
                (up_mine.at[rows_of, :], part_ref.at[pl.ds(0, part), :]),
                (up_grad.at[rows_of, :], part_ref.at[pl.ds(part, part), :]),
            )
    else:
        stores += go((up_grad, up_grad_ref))
    put(keep_out, mul(active[:rows, :], down[...]))
    stores += go((keep_out, keep_out_ref))
    put(send_out, mul(active[rows:, :], down[...]))
    wait(stores + go((send_out, send_out_ref)))


def mlp(x_own, x_peer, g_own, g_peer, up, down, upper=(), before=(), flops=0):
    rows, width = g_own.shape
    units = sum(piece.shape[0] for piece in down)
    tall = (2 * rows, width)
    pair = [((rows, width), bfloat), ((rows, width), single)] * 2
    outs = pair + [((units, width), bfloat)]
    outs += [((2 * width // SQUARE, units), bfloat)] * SQUARE if before else [((width, units), bfloat)]
    scratch = [
        pltpu.VMEM(tall, bfloat),
        pltpu.VMEM(tall, bfloat),
        pltpu.VMEM((width, units), bfloat),
        pltpu.VMEM((units, width), bfloat),
        pltpu.VMEM((2 * rows, units), bfloat),
        pltpu.VMEM((2 * rows, units), bfloat),
        pltpu.VMEM((width, 2 * rows), bfloat),
    ]
    scratch += [pltpu.VMEM(shape, kind) for shape, kind in pair]
    scratch += [
        pltpu.VMEM((units, width), bfloat), pltpu.VMEM((width, units), bfloat), pltpu.SemaphoreType.DMA((32,)),
    ]
    if before:
        scratch.append(pltpu.VMEM((width, units), bfloat))
    operands = (*upper, *x_own, *x_peer, g_own, g_peer, *up, *down, *before)
    return call(
        functools.partial(mlp_body, bool(before)),
        outs,
        operands,
        scratch,
        len(upper),
        vmem=60,
        flops=flops,
        far=len(operands) - len(upper),
        far_outs=len(outs),
    )


def shards(
    inputs,
    history,
    cotangent,
    qkv_weight,
    out_weight,
    up_weight,
    down_weight,
    gain_attn,
    gain_mlp,
    dwa_weights,
):
    rows, width = inputs.shape
    members = lax.axis_size("mp")
    copies = lax.axis_size("dp")
    bits = copies.bit_length() - 1
    core = lax.rem(lax.axis_index("mp"), 2).astype(jnp.int32).reshape(1)
    copy_index = lax.axis_index("dp").astype(jnp.int32).reshape(1)
    core_pairs = [(i, i ^ 1) for i in range(members)]
    chip_pairs = [(i, i ^ 2) for i in range(members)]
    depth = history.shape[0]
    part = out_weight.shape[0]

    def other_core(value):
        return lax.ppermute(value, "mp", core_pairs)

    def other_chip(value):
        return lax.ppermute(value, "mp", chip_pairs)

    def other_copy(value, mask):
        return lax.ppermute(value, "dp", [(i, i ^ mask) for i in range(copies)])

    owner = copy_index & (SQUARE - 1)
    cosine, sine = (jnp.asarray(table) for table in tables())

    qkv_own = qkv_weight.transpose(1, 2, 0).reshape(3 * part, width)
    fourth = (width // SQUARE, width)
    square = (width, width)
    masks = range(1, SQUARE)
    marks = pltpu.SemaphoreType.DMA((16,))
    (down_quarter,) = call(
        split_body,
        [(fourth, bfloat)],
        (owner, down_weight),
        [pltpu.VMEM(fourth, bfloat), marks],
        1,
        vmem=60,
        far=1,
        far_outs=1,
    )
    qkv_peer, out_peer = other_chip(qkv_own), other_chip(out_weight)
    down_come, up_peer = other_chip(down_quarter), other_chip(up_weight)

    full = (rows, width)
    (x_own,) = call(norm_body, [(full, bfloat)], (inputs, gain_attn), after=(down_quarter,))
    x_peer = other_core(x_own)
    tall = (SEQ, width)
    tokens = pltpu.VMEM(tall, bfloat)
    first_outs = [
        ((3 * part, SEQ), bfloat), ((part, SEQ), bfloat), ((SEQ, part), bfloat), ((8, SEQ), single),
    ]
    tiles = [tokens, pltpu.VMEM((2, SEQ, 256), single), pltpu.VMEM((2, SEQ, 256), bfloat)]
    qkv_a, att_a, nat_a, log_a = call(
        attend_placed, first_outs, (core, x_own, x_peer, cosine, sine, qkv_own), tiles, 1, vmem=32
    )
    history_grad, mixed, g_own, history_parts = average_history(dwa_weights, history, cotangent, (log_a,))
    g_peer = other_core(g_own)
    qkv_b, att_b, nat_b, log_b = call(
        attend_placed,
        first_outs,
        (core, x_own, x_peer, cosine, sine, qkv_peer),
        tiles,
        1,
        (history_parts,),
        32,
        MUCH,
    )
    third = (rows // PARTS, width)
    keep, *send, down_copy = call(
        branch_body,
        [(full, single)] + [(third, bfloat)] * PARTS + [(fourth, bfloat)],
        (core, nat_a, nat_b, out_weight, out_peer, down_come),
        [pltpu.VMEM(fourth, bfloat), marks],
        1,
        (g_peer,),
        far=1,
        far_outs=1,
    )
    down_pieces = [down_come] + [other_copy(down_copy, mask) for mask in masks]
    recv = [other_core(value) for value in send]
    middle, *y_own = call(
        middle_body, [(full, single)] + [(third, bfloat)] * PARTS, (inputs, keep, gain_mlp, *recv)
    )
    y_peer = [other_core(value) for value in y_own]

    first = mlp(y_own, y_peer, g_own, g_peer, (up_weight,), (down_weight,))
    down_mine, up_mine = first[4:]
    second = mlp(
        y_own, y_peer, g_own, g_peer, (up_peer,), down_pieces, (owner,), (*first[:4], up_mine)
    )
    send_norm, keep_norm, send_out, keep_out, down_theirs = second[:5]
    token = [send_norm]

    def step(body, outs, operands, scratch=(), scalars=0, vmem=16, flops=MUCH, far=0, far_outs=0):
        results = call(body, outs, operands, scratch, scalars, tuple(token), vmem, flops, far, far_outs)
        token[0] = results[0]
        return results

    down_come = other_chip(down_theirs)
    up_parts = [second[5]] + [other_copy(value, mask) for mask, value in zip(masks, second[6:])]
    out_come = other_core(send_out)
    grad_middle, gb_own, gain_mlp_part = step(
        middle_back_body,
        [(full, single), (full, bfloat), ((1, width), single)],
        (dwa_weights, middle, keep_norm, other_core(send_norm), cotangent, gain_mlp),
        scalars=1,
        flops=0,
    )
    gb_peer = other_core(gb_own)
    combined, dwa_part = step(
        combine_body,
        [(full, bfloat), ((depth + 1, width), single)],
        (dwa_weights, mixed, middle, keep_out, out_come, cotangent, history_parts),
        scalars=1,
        flops=0,
    )

    def back(weight, qkv_weight, qkv, att, log, flops, before=()):
        return step(
            attend_back,
            [
                ((depth + 3 if before else 1, width), single),
                ((4 * part, width), bfloat),
                ((3 * part, SEQ), bfloat),
            ],
            (
                core, log, cosine, sine, gain_attn, *before, gb_own, gb_peer, x_own, x_peer, weight, qkv_weight, qkv,
                att,
            ),
            [
                pltpu.VMEM(tall, bfloat),
                pltpu.VMEM(tall, bfloat),
                pltpu.VMEM((part, width), bfloat),
                pltpu.VMEM((3 * part, width), bfloat),
                pltpu.VMEM((3 * part, SEQ), bfloat),
                pltpu.VMEM((part, SEQ), bfloat),
                pltpu.VMEM((3 * part, SEQ), bfloat),
                pltpu.VMEM((4 * part, width), bfloat),
                pltpu.VMEM((2, SEQ, SEQ), bfloat),
                pltpu.VMEM((2, SEQ, SEQ), bfloat),
                pltpu.VMEM((3 * part, width), single),
                marks,
            ],
            1,
            60,
            flops,
            8,
            2,
        )

    gain_part, att_theirs, turned_b = back(out_peer, qkv_peer, qkv_b, att_b, log_b, 0)
    att_come = other_chip(att_theirs)
    def spread(mine, come, flops=MUCH):
        own, *sent = step(part_body, [(fourth, bfloat)] * SQUARE, (owner, mine, come), scalars=1, flops=flops)
        return [own] + [other_copy(value, mask) for mask, value in zip(masks, sent)]

    down_parts = spread(down_mine, down_come, 0)
    up, sent = step(four_two_body, [(fourth, bfloat)] * 2, up_parts, flops=0)
    up_come = other_chip(sent)
    part_sums, att_mine, turned_a = back(
        out_weight, qkv_own, qkv_a, att_a, log_a, MUCH, (gain_part, gain_mlp_part, dwa_part)
    )

    def exchange(value):
        for bit in range(2, bits):
            come = other_copy(value, 1 << bit)
            if bit < bits - 1:
                (value,) = step(low_body, [(value.shape, bfloat)], (value, come))
        return value, come

    def finish(value, come):
        (value,) = step(low_body, [(value.shape, bfloat)], (value, come), flops=COST)
        return [value] + [other_copy(value, mask) for mask in masks]

    core_sums = other_core(part_sums)
    (down,) = step(four_body, [(fourth, bfloat)], down_parts, flops=COST)
    down = exchange(down)
    att_parts = spread(att_mine, att_come, COST)
    (part_sums,) = step(add_body, [(part_sums.shape, single)], (part_sums, core_sums), flops=COST)
    more_sums = other_chip(part_sums)
    token.append(down[1])
    (up,) = step(low_body, [(fourth, bfloat)], (up, up_come), flops=COST)
    token.pop()
    up = exchange(up)
    send_first, keep_first = step(
        first_grad_body,
        [(full, bfloat), (full, single)],
        (core, turned_a, turned_b, qkv_own, qkv_peer),
        [pltpu.VMEM((3 * part, SEQ), bfloat)] * 2
        + [pltpu.VMEM((3 * part, width), bfloat)] * 2
        + [pltpu.VMEM(tall, single), marks],
        1,
        60,
        COST,
        4,
        1,
    )
    first_come = other_core(send_first)
    block = (width // SQUARE + EXTRA, width)
    (att,) = step(four_more_body, [(block, bfloat)], (part_sums, more_sums, *att_parts), flops=COST)
    att = exchange(att)
    pair = (2 * width // SQUARE, width)
    (both,) = step(pair_body, [(pair, bfloat)], (*down, *up), flops=COST)
    both = [both] + [other_copy(both, mask) for mask in masks]
    (input_grad,) = step(
        first_back_body,
        [(full, bfloat)],
        (inputs, keep_first, first_come, grad_middle, gain_attn),
        vmem=60,
        flops=COST,
    )
    att = finish(*att)
    down_grad, up_grad = step(
        pair_whole_body,
        [(square, single)] * 2,
        (owner, *both),
        [pltpu.VMEM((SQUARE * pair[0], width), bfloat)],
        1,
        flops=COST,
    )
    qkv_grad, out_grad, gain_attn_grad, gain_mlp_grad, dwa_grad = step(
        more_body,
        [
            ((3 * part, width), single),
            ((part, width), single),
            ((width,), single),
            ((width,), single),
            ((depth + 1,), single, "scalars"),
        ],
        (owner, *att),
        [pltpu.VMEM((SQUARE * block[0], width), bfloat)],
        1,
        flops=COST,
    )

    return (
        combined,
        input_grad,
        history_grad,
        qkv_grad.reshape(3, part, width).transpose(2, 0, 1),
        out_grad,
        up_grad,
        down_grad,
        gain_attn_grad,
        gain_mlp_grad,
        dwa_grad,
    )


def solution(mesh):
    placed = (
        P(("dp", "mp"), None),
        P(None, ("dp", "mp"), None),
        P(("dp", "mp"), None),
        P(None, None, "mp"),
        P("mp", None),
        P(None, "mp"),
        P("mp", None),
        P(),
        P(),
        P(),
    )
    return jax.shard_map(
        shards,
        mesh=mesh,
        in_specs=placed,
        out_specs=(
            P(("dp", "mp"), None),
            P(("dp", "mp"), None),
            P(None, ("dp", "mp"), None),
            P(None, None, "mp"),
            P("mp", None),
            P(None, "mp"),
            P("mp", None),
            P(),
            P(),
            P(),
        ),
        check_vma=False,
    )
```

```python
import functools

import jax
import jax.numpy as jnp
import numpy as np
from jax import lax
from jax.experimental import pallas as pl
from jax.experimental.pallas import tpu as pltpu
from jax.sharding import PartitionSpec as P

DH = 64
SEQ = 1152
HALF = SEQ // 2
EPS = 1e-05
bfloat = jnp.bfloat16
single = jnp.float32
MIB = 1 << 20
MUCH = 10**11
COST = 10**10


def tables():
    half_width = DH // 2
    places = np.arange(SEQ, dtype=np.float32)
    frequency = np.float32(10000.0) ** (-np.arange(half_width, dtype=np.float32) * np.float32(2.0 / DH))
    angles = frequency[:, None] * places[None, :]
    return (np.cos(angles).astype(np.float32), np.sin(angles).astype(np.float32))


def mul(a, b, ca=1, cb=0):
    return lax.dot_general(a, b, (((ca,), (cb,)), ((), ())), preferred_element_type=single)


def call(kernel, outs, operands, scratch=(), scalars=0, after=(), vmem=16, flops=0, far=0, far_outs=0):
    count, waits = len(operands), len(after)

    def body(*refs):
        kernel(*refs[:count], *refs[count + waits :])

    small = pl.BlockSpec(memory_space=pltpu.SMEM)
    whole = pl.BlockSpec(memory_space=pltpu.VMEM)
    apart = pl.BlockSpec(memory_space=pltpu.HBM)
    loose = pl.BlockSpec(memory_space=pl.ANY)
    inner = len(outs) - far_outs
    return pl.pallas_call(
        body,
        out_shape=[jax.ShapeDtypeStruct(out[0], out[1]) for out in outs],
        in_specs=[small] * scalars + [whole] * (count - scalars - far) + [apart] * far + [loose] * waits,
        out_specs=[small if len(out) > 2 else whole for out in outs[:inner]] + [apart] * far_outs,
        scratch_shapes=list(scratch),
        compiler_params=pltpu.CompilerParams(vmem_limit_bytes=vmem * MIB),
        cost_estimate=pl.CostEstimate(flops=flops, bytes_accessed=0, transcendentals=0),
    )(*operands, *after)


class Mover:
    def __init__(self, marks):
        self.marks = marks
        self.used = 0

    def __call__(self, *pairs):
        copies = []
        for source, target in pairs:
            copies.append(pltpu.make_async_copy(source, target, self.marks.at[self.used]))
            self.used += 1
        for copy in copies:
            copy.start()
        return copies


def wait(copies):
    for copy in copies:
        copy.wait()


ROWS = 64
PARTS = 1


def spans(rows, step=ROWS):
    return [slice(begin, begin + step) for begin in range(0, rows, step)]


def normal_of(x):
    centre = x - jnp.mean(x, axis=-1, keepdims=True)
    spread = jnp.mean(centre * centre, axis=-1, keepdims=True)
    scale = lax.rsqrt(spread + EPS)
    return centre * scale, scale


def split_body(owner_ref, in_ref, out_ref, hold, marks):
    go = Mover(marks)
    wait(go((in_ref.at[quarter(owner_ref[0], 0, hold.shape[0]), :], hold)))
    wait(go((hold, out_ref)))


def joined(owner, refs, target):
    size = refs[0].shape[0]
    return [(ref, target.at[quarter(owner, mask, size), :]) for mask, ref in enumerate(refs)]


def norm_body(x_ref, gain_ref, out_ref):
    gain = gain_ref[...].reshape(1, -1)
    for span in spans(x_ref.shape[0]):
        normal, _ = normal_of(x_ref[span, :].astype(single))
        out_ref[span, :] = (normal * gain).astype(bfloat)


def scaled_body(mix_ref, cot_ref, out_ref):
    out_ref[...] = (mix_ref[mix_ref.shape[0] - 1] * cot_ref[...]).astype(bfloat)


def middle_body(x_ref, keep_ref, gain_ref, *rest):
    recv_refs, mid_ref, out_refs = rest[:PARTS], rest[PARTS], rest[PARTS + 1 :]
    gain = gain_ref[...].reshape(1, -1)
    rows = x_ref.shape[0] // PARTS
    for index in range(PARTS):
        for span in spans(rows):
            here = slice(index * rows + span.start, index * rows + span.stop)
            recv = recv_refs[index][span, :].astype(single)
            x = x_ref[here, :].astype(single) + (keep_ref[here, :] + recv)
            mid_ref[here, :] = x
            normal, _ = normal_of(x)
            out_refs[index][span, :] = (normal * gain).astype(bfloat)


def norm_back(x, grad, gain):
    normal, scale = normal_of(x)
    lifted = grad * gain
    back = scale * (
        lifted
        - jnp.mean(lifted, axis=-1, keepdims=True)
        - normal * jnp.mean(lifted * normal, axis=-1, keepdims=True)
    )
    return back, normal


def fold_rows(value):
    total = value[:8]
    for begin in range(8, value.shape[0], 8):
        total = total + value[begin : begin + 8]
    return total


def middle_back_body(mix_ref, x_ref, keep_ref, recv_ref, cot_ref, gain_ref, mid_ref, low_ref, part_ref):
    gain = gain_ref[...].reshape(1, -1)
    part = jnp.zeros((8, x_ref.shape[1]), single)
    for span in spans(x_ref.shape[0]):
        grad = keep_ref[span, :] + recv_ref[span, :].astype(single)
        back, normal = norm_back(x_ref[span, :], grad, gain)
        total = mix_ref[mix_ref.shape[0] - 1] * cot_ref[span, :] + back
        mid_ref[span, :] = total
        low_ref[span, :] = total.astype(bfloat)
        part = part + fold_rows(grad * normal)
    part_ref[...] = jnp.sum(part, axis=0, keepdims=True)


def first_back_body(x_ref, keep_ref, recv_ref, mid_ref, gain_ref, out_ref):
    gain = gain_ref[...].reshape(1, -1)
    for span in spans(x_ref.shape[0]):
        grad = keep_ref[span, :] + recv_ref[span, :].astype(single)
        back, _ = norm_back(x_ref[span, :].astype(single), grad, gain)
        out_ref[span, :] = (mid_ref[span, :] + back).astype(bfloat)


def history_body(mix_ref, history_ref, cot_ref, grad_ref, mixed_ref, part_ref):
    depth = history_ref.shape[0]

    @pl.when(pl.program_id(0) == 0)
    def _():
        part_ref[...] = jnp.zeros_like(part_ref)

    for span in spans(cot_ref.shape[0], 32):
        cot = cot_ref[span, :]
        mixed = None
        for j in range(depth):
            layer = history_ref[j, span, :].astype(single)
            mixed = mix_ref[j] * layer if mixed is None else mixed + mix_ref[j] * layer
            grad_ref[j, span, :] = (mix_ref[j] * cot).astype(bfloat)
            part_ref[8 * j : 8 * j + 8, :] += fold_rows(layer * cot)
        mixed_ref[span, :] = mixed


def average_history(mix, history, cot, after=()):
    depth, rows, width = history.shape
    step = 96
    waits = len(after)

    def body(*refs):
        history_body(*refs[:3], *refs[3 + waits :])

    row_block = pl.BlockSpec((step, width), lambda i: (i, 0))
    deep_block = pl.BlockSpec((depth, step, width), lambda i: (0, i, 0))
    return pl.pallas_call(
        body,
        grid=(rows // step,),
        out_shape=[
            jax.ShapeDtypeStruct(history.shape, bfloat),
            jax.ShapeDtypeStruct((rows, width), single),
            jax.ShapeDtypeStruct((8 * depth, width), single),
        ],
        in_specs=[pl.BlockSpec(memory_space=pltpu.SMEM), deep_block, row_block]
        + [pl.BlockSpec(memory_space=pl.ANY)] * waits,
        out_specs=[deep_block, row_block, pl.BlockSpec((8 * depth, width), lambda i: (0, 0))],
        compiler_params=pltpu.CompilerParams(vmem_limit_bytes=16 * MIB),
        cost_estimate=pl.CostEstimate(flops=0, bytes_accessed=0, transcendentals=0),
    )(mix, history, cot, *after)


def combine_body(mix_ref, mixed_ref, mid_ref, keep_ref, recv_ref, cot_ref, parts_ref, out_ref, part_ref):
    depth = mix_ref.shape[0] - 1
    last = jnp.zeros((8, mid_ref.shape[1]), single)
    for span in spans(mid_ref.shape[0]):
        outputs = mid_ref[span, :] + (keep_ref[span, :] + recv_ref[span, :].astype(single))
        out_ref[span, :] = (mixed_ref[span, :] + mix_ref[depth] * outputs).astype(bfloat)
        last = last + fold_rows(outputs * cot_ref[span, :])
    for j in range(depth):
        part_ref[j : j + 1, :] = jnp.sum(parts_ref[8 * j : 8 * j + 8, :], axis=0, keepdims=True)
    part_ref[depth : depth + 1, :] = jnp.sum(last, axis=0, keepdims=True)


SQUARE = 4


def quarter(owner, mask, size):
    other = owner + (mask & 1) * (1 - 2 * (owner % 2)) + (mask & 2) * (1 - 2 * (owner // 2))
    return pl.ds(pl.multiple_of(other * size, size), size)


def part_body(owner_ref, mine_ref, come_ref, *out_refs):
    for mask, out_ref in enumerate(out_refs):
        rows = quarter(owner_ref[0], mask, out_ref.shape[0])
        out_ref[...] = (mine_ref[rows, :].astype(single) + come_ref[rows, :].astype(single)).astype(bfloat)


def sum_of(refs, rows):
    total = refs[0][rows, :].astype(single)
    for ref in refs[1:]:
        total = total + ref[rows, :].astype(single)
    return total


def four_body(*refs):
    refs[-1][...] = sum_of(refs[:-1], slice(None)).astype(bfloat)


def four_two_body(*refs):
    size = refs[-1].shape[0]
    refs[-2][...] = sum_of(refs[:-2], slice(0, size)).astype(bfloat)
    refs[-1][...] = sum_of(refs[:-2], slice(size, 2 * size)).astype(bfloat)


EXTRA = 16


def copy_body(in_ref, out_ref):
    out_ref[...] = in_ref[...]


def add_body(mine_ref, come_ref, out_ref):
    out_ref[...] = mine_ref[...] + come_ref[...]


def four_pass_body(small_ref, *refs):
    refs[-1][...] = small_ref[...]
    four_body(*refs[:-1])


def four_more_body(small_ref, more_ref, *refs):
    out_ref = refs[-1]
    size = out_ref.shape[0] - EXTRA
    out_ref[:size, :] = sum_of(refs[:-1], slice(None)).astype(bfloat)
    small = small_ref[...] + more_ref[...]
    rest = jnp.zeros((EXTRA - small.shape[0], small.shape[1]), single)
    out_ref[size:, :] = jnp.concatenate([small, rest], axis=0).astype(bfloat)


def gather(owner_ref, pieces, hold):
    for mask, piece in enumerate(pieces):
        hold[quarter(owner_ref[0], mask, piece.shape[0]), :] = piece[...]


def pair_body(a_ref, a_come_ref, b_ref, b_come_ref, out_ref):
    size = a_ref.shape[0]
    out_ref[:size, :] = sum_of((a_ref, a_come_ref), slice(None)).astype(bfloat)
    out_ref[size:, :] = sum_of((b_ref, b_come_ref), slice(None)).astype(bfloat)


def pair_whole_body(owner_ref, a_ref, b_ref, c_ref, d_ref, down_ref, up_ref, hold):
    gather(owner_ref, (a_ref, b_ref, c_ref, d_ref), hold)
    block = hold.shape[0] // SQUARE
    size = block // 2
    for index in range(SQUARE):
        begin, rows = index * block, slice(index * size, (index + 1) * size)
        down_ref[rows, :] = hold[begin : begin + size, :].astype(single)
        up_ref[rows, :] = hold[begin + size : begin + block, :].astype(single)


def more_body(owner_ref, a_ref, b_ref, c_ref, d_ref, top_ref, end_ref, attn_ref, mlp_ref, dwa_ref, hold):
    gather(owner_ref, (a_ref, b_ref, c_ref, d_ref), hold)
    block = hold.shape[0] // SQUARE
    rows = block - EXTRA
    small = jnp.zeros((EXTRA, hold.shape[1]), single)
    for index in range(SQUARE):
        begin = index * block
        target, place = (top_ref, index * rows) if index < SQUARE - 1 else (end_ref, 0)
        target[place : place + rows, :] = hold[begin : begin + rows, :].astype(single)
        small = small + hold[begin + rows : begin + block, :].astype(single)
    attn_ref[...] = small[0]
    mlp_ref[...] = small[1]
    for index in range(dwa_ref.shape[0]):
        dwa_ref[index] = jnp.sum(small[2 + index : 3 + index])


def low_body(mine_ref, come_ref, out_ref):
    out_ref[...] = (mine_ref[...].astype(single) + come_ref[...].astype(single)).astype(bfloat)


def copy_body(in_ref, out_ref):
    out_ref[...] = in_ref[...]


def add_body(mine_ref, come_ref, out_ref):
    out_ref[...] = mine_ref[...] + come_ref[...]


BLOCKS = tuple((begin, min(256, SEQ - begin)) for begin in range(0, SEQ, 256))


def place(core_ref, own_ref, peer_ref, whole):
    low = pl.multiple_of(core_ref[0] * HALF, HALF)
    high = pl.multiple_of((1 - core_ref[0]) * HALF, HALF)
    whole[pl.ds(low, HALF), :] = own_ref[...]
    whole[pl.ds(high, HALF), :] = peer_ref[...]
    return low, high


def allowed(size):
    key_pos = lax.broadcasted_iota(jnp.int32, (size, size), 0)
    query_pos = lax.broadcasted_iota(jnp.int32, (size, size), 1)
    return query_pos >= key_pos


def turn(rows, cosine, sine):
    half = rows.shape[0] // 2
    a, b = rows[:half], rows[half:]
    return jnp.concatenate([a * cosine - b * sine, b * cosine + a * sine], axis=0)


KEYS = 128


def fold_top(value):
    top = value[:8]
    for begin in range(8, value.shape[0], 8):
        top = jnp.maximum(top, value[begin : begin + 8])
    return top


def masked(scores, offset):
    key_pos = lax.broadcasted_iota(jnp.int32, scores.shape, 0) + offset
    query_pos = lax.broadcasted_iota(jnp.int32, scores.shape, 1)
    return jnp.where(query_pos >= key_pos, scores, -jnp.inf)


def attend_placed(core_ref, own_ref, peer_ref, cos_ref, sin_ref, weight_ref, *rest):
    place(core_ref, own_ref, peer_ref, rest[4])
    attend(weight_ref, cos_ref, sin_ref, *rest)


def attend(weight_ref, cos_ref, sin_ref, qkv_ref, att_ref, nat_ref, log_ref, tokens, all_scores, all_weights):
    width = weight_ref.shape[0] // 3
    projected = mul(weight_ref[...], tokens[...], 1, 1)
    cosine, sine = cos_ref[...], sin_ref[...]
    for part in range(3):
        for head in range(width // DH):
            begin = part * width + head * DH
            rows = projected[begin : begin + DH]
            if part < 2:
                rows = turn(rows, cosine, sine)
            if part == 0:
                rows = rows * DH ** (-0.5)
            qkv_ref[begin : begin + DH, :] = rows.astype(bfloat)
    log_ref[...] = jnp.zeros_like(log_ref)
    heads = range(width // DH)
    keys = [qkv_ref[width + head * DH : width + head * DH + DH, :].T for head in heads]
    for begin, size in BLOCKS:
        end = begin + size
        tops = [None for _ in heads]
        for row in range(0, end, KEYS):
            for head in heads:
                tile = mul(keys[head][row : row + KEYS], qkv_ref[head * DH : head * DH + DH, begin:end])
                if row >= begin:
                    tile = masked(tile, row - begin)
                all_scores[head, row : row + KEYS, :size] = tile
                top = fold_top(tile)
                tops[head] = top if row == 0 else jnp.maximum(tops[head], top)
        tops = [jnp.max(top, axis=0, keepdims=True) for top in tops]
        totals = [jnp.zeros((8, size), single) for _ in heads]
        for row in range(0, end, KEYS):
            for head in heads:
                tile = jnp.exp(all_scores[head, row : row + KEYS, :size] - tops[head])
                totals[head] = totals[head] + fold_rows(tile)
                all_weights[head, row : row + KEYS, :size] = tile.astype(bfloat)
        for head in heads:
            base = head * DH
            total = jnp.sum(totals[head], axis=0, keepdims=True)
            value = qkv_ref[2 * width + base : 2 * width + base + DH, :end]
            mixed = mul(value, all_weights[head, :end, :size]) / total
            att_ref[base : base + DH, begin:end] = mixed.astype(bfloat)
            log_ref[head : head + 1, begin:end] = tops[head] + jnp.log(total)
    nat_ref[...] = att_ref[...].T


def branch_body(core_ref, att_a_ref, att_b_ref, out_a_ref, out_b_ref, pass_ref, keep_ref, *rest):
    send_refs, pass_out = rest[:PARTS], rest[PARTS]
    pass_out[...] = pass_ref[...]
    low = pl.multiple_of(core_ref[0] * HALF, HALF)
    rows = HALF // PARTS
    for index in range(PARTS):
        high = pl.multiple_of((1 - core_ref[0]) * HALF + index * rows, rows)
        send = mul(att_a_ref[pl.ds(high, rows), :], out_a_ref[...])
        send_refs[index][...] = (send + mul(att_b_ref[pl.ds(high, rows), :], out_b_ref[...])).astype(bfloat)
    keep = mul(att_a_ref[pl.ds(low, HALF), :], out_a_ref[...])
    keep_ref[...] = keep + mul(att_b_ref[pl.ds(low, HALF), :], out_b_ref[...])


def attend_back(
    core_ref, log_ref, cos_ref, sin_ref, gain_ref, *rest
):
    before_refs, rest = rest[:-23], rest[-23:]
    grad_own_ref, grad_peer_ref, own_ref, peer_ref, weight_ref, qkv_weight_ref, qkv_ref, att_ref = rest[:8]
    small_ref, out_ref, turned_ref = rest[8:11]
    grads, tokens, weight, qkv_weight, qkv, att, turned, result, all_probs, all_scores, hold, marks = rest[11:]
    low = pl.multiple_of(core_ref[0] * HALF, HALF)
    high = pl.multiple_of((1 - core_ref[0]) * HALF, HALF)
    go = Mover(marks)
    first = go(
        (weight_ref, weight),
        (grad_own_ref, grads.at[pl.ds(low, HALF), :]),
        (grad_peer_ref, grads.at[pl.ds(high, HALF), :]),
        (att_ref, att),
        (qkv_ref, qkv),
    )
    later = go(
        (own_ref, tokens.at[pl.ds(low, HALF), :]),
        (peer_ref, tokens.at[pl.ds(high, HALF), :]),
        (qkv_weight_ref, qkv_weight),
    )
    wait(first)
    width = att.shape[0]
    grad_att = mul(weight[...], grads[...], 1, 1).astype(bfloat)
    result[3 * width :, :] = mul(att[...], grads[...]).astype(result.dtype)
    cosine, sine = cos_ref[...], sin_ref[...]
    heads = range(width // DH)
    spans_of = [slice(head * DH, head * DH + DH) for head in heads]
    query = [qkv[span, :] for span in spans_of]
    key = [qkv[width + span.start : width + span.stop, :] for span in spans_of]
    above = [grad_att[span] for span in spans_of]
    centre = [
        jnp.sum(above[head].astype(single) * att[span, :].astype(single), axis=0, keepdims=True)
        for head, span in enumerate(spans_of)
    ]
    keys = [value.T for value in key]
    values = [qkv[2 * width + span.start : 2 * width + span.stop, :].T for span in spans_of]
    queries = [value.T for value in query]
    aboves = [value.T for value in above]
    grad_query = [[] for _ in heads]
    for begin, size in BLOCKS:
        end = begin + size
        for row in range(0, end, KEYS):
            span = slice(row, row + KEYS)
            for head in heads:
                tile = mul(keys[head][span], query[head][:, begin:end])
                if row >= begin:
                    tile = masked(tile, row - begin)
                tile = jnp.exp(tile - log_ref[head : head + 1, begin:end])
                grad = mul(values[head][span], above[head][:, begin:end]) - centre[head][:, begin:end]
                all_probs[head, span, begin:end] = tile.astype(bfloat)
                all_scores[head, span, begin:end] = (tile * grad).astype(bfloat)
        for head in heads:
            grad_query[head].append(mul(key[head][:, :end], all_scores[head, :end, begin:end]))
    grad_key = [[] for _ in heads]
    grad_value = [[] for _ in heads]
    for begin, size in BLOCKS:
        span = slice(begin, begin + size)
        for head in heads:
            grad_key[head].append(mul(all_scores[head, span, begin:], queries[head][begin:]))
            grad_value[head].append(mul(all_probs[head, span, begin:], aboves[head][begin:]))
    for head, span in enumerate(spans_of):
        grad = jnp.concatenate(grad_query[head], axis=1) * DH ** (-0.5)
        turned[span, :] = turn(grad, cosine, -sine).astype(bfloat)
        grad = jnp.concatenate(grad_key[head], axis=0).T
        turned[width + span.start : width + span.stop, :] = turn(grad, cosine, -sine).astype(bfloat)
        grad = jnp.concatenate(grad_value[head], axis=0).T
        turned[2 * width + span.start : 2 * width + span.stop, :] = grad.astype(bfloat)
    stores = go((turned, turned_ref))
    wait(later)
    hold[...] = mul(turned[...], tokens[...])
    result[: 3 * width, :] = hold[...].astype(result.dtype)
    stores += go((result, out_ref))
    part = jnp.zeros((8, hold.shape[1]), single)
    for span in spans(hold.shape[0]):
        part = part + fold_rows(hold[span, :] * qkv_weight[span, :].astype(single))
    gain = jnp.sum(part, axis=0, keepdims=True) / gain_ref[...].reshape(1, -1)
    if before_refs:
        gain_part_ref, mlp_part_ref, dwa_part_ref = before_refs
        small_ref[:1, :] = gain + gain_part_ref[...]
        small_ref[1:2, :] = mlp_part_ref[...]
        small_ref[2:, :] = dwa_part_ref[...]
    else:
        small_ref[...] = gain
    wait(stores)


def first_grad_body(
    core_ref, turned_a_ref, turned_b_ref, weight_a_ref, weight_b_ref, send_ref, keep_ref,
    turned_a, turned_b, weight_a, weight_b, whole, marks,
):
    low = pl.multiple_of(core_ref[0] * HALF, HALF)
    high = pl.multiple_of((1 - core_ref[0]) * HALF, HALF)
    go = Mover(marks)
    wait(go((turned_a_ref, turned_a), (weight_a_ref, weight_a), (turned_b_ref, turned_b), (weight_b_ref, weight_b)))
    whole[...] = mul(turned_a[...], weight_a[...], 0, 0) + mul(turned_b[...], weight_b[...], 0, 0)
    stores = go((whole.at[pl.ds(low, HALF), :], keep_ref))
    send_ref[...] = whole[pl.ds(high, HALF), :].astype(bfloat)
    wait(stores)


CURVE = float(np.sqrt(2.0 / np.pi))
STEP = 256


def mlp_body(second, *refs):
    if second:
        owner_ref, refs = refs[0], refs[1:]
    x_refs, refs = refs[: 2 * PARTS], refs[2 * PARTS :]
    g_own_ref, g_peer_ref, refs = refs[0], refs[1], refs[2:]
    if second:
        up_ref, down_refs, refs = refs[0], refs[1 : 1 + SQUARE], refs[1 + SQUARE :]
        before_refs, up_mine_ref = refs[:4], refs[4]
        down_grad_ref, part_refs = refs[9], refs[10:14]
        refs = refs[5:9] + refs[14:]
    else:
        up_ref, down_ref = refs[:2]
        down_grad_ref, up_grad_ref = refs[6:8]
        refs = refs[2:6] + refs[8:]
    send_norm_ref, keep_norm_ref, send_out_ref, keep_out_ref = refs[:4]
    x_all, g_all, up, down, active, grad_hidden, x_turned = refs[4:11]
    send_norm, keep_norm, send_out, keep_out, down_grad, up_grad, marks = refs[11:18]
    rows, size = x_all.shape[0] // 2, x_all.shape[0] // (2 * PARTS)
    units = down.shape[0]
    go = Mover(marks)
    x_loads = go(*[(x_refs[index], x_all.at[pl.ds(index * size, size), :]) for index in range(2 * PARTS)])
    if second:
        loads = go((up_ref, up), *joined(owner_ref[0], down_refs, down))
    else:
        loads = go((up_ref, up), (down_ref, down))
    loads += go((g_own_ref, g_all.at[pl.ds(0, rows), :]), (g_peer_ref, g_all.at[pl.ds(rows, rows), :]))
    more, mine, stores = [], [], []
    if second:
        (up_mine,) = refs[18:]
        more = go(*zip(before_refs, (send_norm, keep_norm, send_out, keep_out)))
        mine = go((up_mine_ref, up_mine))
    wait(x_loads)
    x_turned[...] = x_all[...].T
    wait(loads)
    for begin in range(0, units, STEP):
        columns = slice(begin, begin + STEP)
        for top in range(0, 2 * rows, rows):
            span = slice(top, top + rows)
            v = mul(x_all[span, :], up[:, columns])
            grad = mul(g_all[span, :], down[columns, :], 1, 1)
            square = v * v
            half = 0.5 + 0.5 * jnp.tanh(v * (CURVE + (CURVE * 0.044715) * square))
            act = v * half
            slope = half + act * (1.0 - half) * (2.0 * CURVE + (6.0 * CURVE * 0.044715) * square)
            active[span, columns] = act.astype(bfloat)
            grad_hidden[span, columns] = (grad * slope).astype(bfloat)

    def put(target, value):
        target[...] = (value + target[...].astype(single) if second else value).astype(target.dtype)

    wait(more)
    put(keep_norm, mul(grad_hidden[:rows, :], up[...], 1, 1))
    put(send_norm, mul(grad_hidden[rows:, :], up[...], 1, 1))
    stores += go((keep_norm, keep_norm_ref), (send_norm, send_norm_ref))
    down_grad[...] = mul(active[...], g_all[...], 0, 0).astype(down_grad.dtype)
    stores += go((down_grad, down_grad_ref))
    up_grad[...] = mul(x_turned[...], grad_hidden[...]).astype(bfloat)
    if second:
        wait(mine)
        part = up_grad.shape[0] // SQUARE
        for mask, part_ref in enumerate(part_refs):
            rows_of = quarter(owner_ref[0], mask, part)
            stores += go(
                (up_mine.at[rows_of, :], part_ref.at[pl.ds(0, part), :]),
                (up_grad.at[rows_of, :], part_ref.at[pl.ds(part, part), :]),
            )
    else:
        stores += go((up_grad, up_grad_ref))
    put(keep_out, mul(active[:rows, :], down[...]))
    stores += go((keep_out, keep_out_ref))
    put(send_out, mul(active[rows:, :], down[...]))
    wait(stores + go((send_out, send_out_ref)))


def mlp(x_own, x_peer, g_own, g_peer, up, down, upper=(), before=(), after=()):
    rows, width = g_own.shape
    units = sum(piece.shape[0] for piece in down)
    tall = (2 * rows, width)
    pair = [((rows, width), bfloat), ((rows, width), single)] * 2
    outs = pair + [((units, width), bfloat)]
    outs += [((2 * width // SQUARE, units), bfloat)] * SQUARE if before else [((width, units), bfloat)]
    scratch = [
        pltpu.VMEM(tall, bfloat),
        pltpu.VMEM(tall, bfloat),
        pltpu.VMEM((width, units), bfloat),
        pltpu.VMEM((units, width), bfloat),
        pltpu.VMEM((2 * rows, units), bfloat),
        pltpu.VMEM((2 * rows, units), bfloat),
        pltpu.VMEM((width, 2 * rows), bfloat),
    ]
    scratch += [pltpu.VMEM(shape, kind) for shape, kind in pair]
    scratch += [
        pltpu.VMEM((units, width), bfloat), pltpu.VMEM((width, units), bfloat), pltpu.SemaphoreType.DMA((32,)),
    ]
    if before:
        scratch.append(pltpu.VMEM((width, units), bfloat))
    operands = (*upper, *x_own, *x_peer, g_own, g_peer, *up, *down, *before)
    return call(
        functools.partial(mlp_body, bool(before)),
        outs,
        operands,
        scratch,
        len(upper),
        after,
        60,
        far=len(operands) - len(upper),
        far_outs=len(outs),
    )


def shards(
    inputs,
    history,
    cotangent,
    qkv_weight,
    out_weight,
    up_weight,
    down_weight,
    gain_attn,
    gain_mlp,
    dwa_weights,
):
    rows, width = inputs.shape
    members = lax.axis_size("mp")
    copies = lax.axis_size("dp")
    bits = copies.bit_length() - 1
    core = lax.rem(lax.axis_index("mp"), 2).astype(jnp.int32).reshape(1)
    copy_index = lax.axis_index("dp").astype(jnp.int32).reshape(1)
    core_pairs = [(i, i ^ 1) for i in range(members)]
    chip_pairs = [(i, i ^ 2) for i in range(members)]
    depth = history.shape[0]
    part = out_weight.shape[0]

    def other_core(value):
        return lax.ppermute(value, "mp", core_pairs)

    def other_chip(value):
        return lax.ppermute(value, "mp", chip_pairs)

    def other_copy(value, mask):
        return lax.ppermute(value, "dp", [(i, i ^ mask) for i in range(copies)])

    owner = copy_index & (SQUARE - 1)
    cosine, sine = (jnp.asarray(table) for table in tables())

    qkv_own = qkv_weight.transpose(1, 2, 0).reshape(3 * part, width)
    fourth = (width // SQUARE, width)
    square = (width, width)
    masks = range(1, SQUARE)
    marks = pltpu.SemaphoreType.DMA((16,))
    (down_quarter,) = call(
        split_body,
        [(fourth, bfloat)],
        (owner, down_weight),
        [pltpu.VMEM(fourth, bfloat), marks],
        1,
        vmem=60,
        far=1,
        far_outs=1,
    )
    qkv_peer, out_peer = other_chip(qkv_own), other_chip(out_weight)
    down_come, up_peer = other_chip(down_quarter), other_chip(up_weight)

    full = (rows, width)
    (x_own,) = call(norm_body, [(full, bfloat)], (inputs, gain_attn), after=(down_quarter,))
    x_peer = other_core(x_own)
    tall = (SEQ, width)
    tokens = pltpu.VMEM(tall, bfloat)
    first_outs = [
        ((3 * part, SEQ), bfloat), ((part, SEQ), bfloat), ((SEQ, part), bfloat), ((8, SEQ), single),
    ]
    heads = part // DH
    tiles = [tokens, pltpu.VMEM((heads, SEQ, 256), single), pltpu.VMEM((heads, SEQ, 256), bfloat)]
    qkv_a, att_a, nat_a, log_a = call(
        attend_placed, first_outs, (core, x_own, x_peer, cosine, sine, qkv_own), tiles, 1, vmem=32
    )
    (g_own,) = call(scaled_body, [(full, bfloat)], (dwa_weights, cotangent), scalars=1, after=(log_a,))
    g_peer = other_core(g_own)
    qkv_b, att_b, nat_b, log_b = call(
        attend_placed,
        first_outs,
        (core, x_own, x_peer, cosine, sine, qkv_peer),
        tiles,
        1,
        (g_own,),
        32,
        MUCH,
    )
    third = (rows // PARTS, width)
    keep, *send, down_copy = call(
        branch_body,
        [(full, single)] + [(third, bfloat)] * PARTS + [(fourth, bfloat)],
        (core, nat_a, nat_b, out_weight, out_peer, down_come),
        (),
        1,
        (g_peer,),
    )
    down_pieces = [down_come] + [other_copy(down_copy, mask) for mask in masks]
    recv = [other_core(value) for value in send]
    middle, *y_own = call(
        middle_body, [(full, single)] + [(third, bfloat)] * PARTS, (inputs, keep, gain_mlp, *recv)
    )
    y_peer = [other_core(value) for value in y_own]

    first = mlp(y_own, y_peer, g_own, g_peer, (up_weight,), (down_weight,))
    down_mine, up_mine = first[4:]
    history_grad, mixed, history_parts = average_history(dwa_weights, history, cotangent, (first[0],))
    second = mlp(
        y_own, y_peer, g_own, g_peer, (up_peer,), down_pieces, (owner,), (*first[:4], up_mine),
        after=(history_parts,),
    )
    send_norm, keep_norm, send_out, keep_out, down_theirs = second[:5]
    token = [send_norm]

    def step(body, outs, operands, scratch=(), scalars=0, vmem=16, flops=MUCH, far=0, far_outs=0):
        results = call(body, outs, operands, scratch, scalars, tuple(token), vmem, flops, far, far_outs)
        token[0] = results[0]
        return results

    down_come = other_chip(down_theirs)
    up_parts = [second[5]] + [other_copy(value, mask) for mask, value in zip(masks, second[6:])]
    out_come = other_core(send_out)
    grad_middle, gb_own, gain_mlp_part = step(
        middle_back_body,
        [(full, single), (full, bfloat), ((1, width), single)],
        (dwa_weights, middle, keep_norm, other_core(send_norm), cotangent, gain_mlp),
        scalars=1,
        flops=0,
    )
    gb_peer = other_core(gb_own)
    def back(weight, qkv_weight, qkv, att, log, flops, before=()):
        return step(
            attend_back,
            [
                ((depth + 3 if before else 1, width), single),
                ((4 * part, width), bfloat),
                ((3 * part, SEQ), bfloat),
            ],
            (
                core, log, cosine, sine, gain_attn, *before, gb_own, gb_peer, x_own, x_peer, weight, qkv_weight, qkv,
                att,
            ),
            [
                pltpu.VMEM(tall, bfloat),
                pltpu.VMEM(tall, bfloat),
                pltpu.VMEM((part, width), bfloat),
                pltpu.VMEM((3 * part, width), bfloat),
                pltpu.VMEM((3 * part, SEQ), bfloat),
                pltpu.VMEM((part, SEQ), bfloat),
                pltpu.VMEM((3 * part, SEQ), bfloat),
                pltpu.VMEM((4 * part, width), bfloat),
                pltpu.VMEM((heads, SEQ, SEQ), bfloat),
                pltpu.VMEM((heads, SEQ, SEQ), bfloat),
                pltpu.VMEM((3 * part, width), single),
                marks,
            ],
            1,
            60,
            flops,
            8,
            2,
        )

    token.append(out_come)
    gain_part, att_theirs, turned_b = back(out_peer, qkv_peer, qkv_b, att_b, log_b, 0)
    token.pop()
    att_come = other_chip(att_theirs)
    def spread(mine, come, flops=MUCH):
        own, *sent = step(part_body, [(fourth, bfloat)] * SQUARE, (owner, mine, come), scalars=1, flops=flops)
        return [own] + [other_copy(value, mask) for mask, value in zip(masks, sent)]

    down_parts = spread(down_mine, down_come, 0)
    up, sent = step(four_two_body, [(fourth, bfloat)] * 2, up_parts, flops=0)
    up_come = other_chip(sent)
    combined, dwa_part = step(
        combine_body,
        [(full, bfloat), ((depth + 1, width), single)],
        (dwa_weights, mixed, middle, keep_out, out_come, cotangent, history_parts),
        scalars=1,
        flops=0,
    )

    part_sums, att_mine, turned_a = back(
        out_weight, qkv_own, qkv_a, att_a, log_a, MUCH, (gain_part, gain_mlp_part, dwa_part)
    )

    def exchange(value):
        for bit in range(2, bits):
            come = other_copy(value, 1 << bit)
            if bit < bits - 1:
                (value,) = step(low_body, [(value.shape, bfloat)], (value, come))
        return value, come

    def finish(value, come):
        (value,) = step(low_body, [(value.shape, bfloat)], (value, come), flops=COST)
        return [value] + [other_copy(value, mask) for mask in masks]

    down, part_sums = step(
        four_pass_body, [(fourth, bfloat), (part_sums.shape, single)], (part_sums, *down_parts), flops=COST
    )
    core_sums = other_core(part_sums)
    down = exchange(down)
    att_parts = spread(att_mine, att_come, COST)
    (part_sums,) = step(add_body, [(part_sums.shape, single)], (part_sums, core_sums), flops=COST)
    more_sums = other_chip(part_sums)
    token.append(down[1])
    (up,) = step(low_body, [(fourth, bfloat)], (up, up_come), flops=COST)
    token.pop()
    up = exchange(up)
    send_first, keep_first = step(
        first_grad_body,
        [(full, bfloat), (full, single)],
        (core, turned_a, turned_b, qkv_own, qkv_peer),
        [pltpu.VMEM((3 * part, SEQ), bfloat)] * 2
        + [pltpu.VMEM((3 * part, width), bfloat)] * 2
        + [pltpu.VMEM(tall, single), marks],
        1,
        60,
        COST,
        4,
        1,
    )
    first_come = other_core(send_first)
    block = (width // SQUARE + EXTRA, width)
    (att,) = step(four_more_body, [(block, bfloat)], (part_sums, more_sums, *att_parts), flops=COST)
    att = exchange(att)
    pair = (2 * width // SQUARE, width)
    (both,) = step(pair_body, [(pair, bfloat)], (*down, *up), flops=COST)
    both = [both, other_copy(both, 1), other_copy(both, 2)]
    (input_grad,) = step(
        first_back_body,
        [(full, bfloat)],
        (inputs, keep_first, first_come, grad_middle, gain_attn),
        vmem=60,
        flops=COST,
    )
    (both_copy,) = step(copy_body, [(pair, bfloat)], (both[2],), flops=COST)
    both.append(other_copy(both_copy, 1))
    att = finish(*att)
    down_grad, up_grad = step(
        pair_whole_body,
        [(square, single)] * 2,
        (owner, *both),
        [pltpu.VMEM((SQUARE * pair[0], width), bfloat)],
        1,
        flops=COST,
    )
    qkv_grad, out_grad, gain_attn_grad, gain_mlp_grad, dwa_grad = step(
        more_body,
        [
            ((3 * part, width), single),
            ((part, width), single),
            ((width,), single),
            ((width,), single),
            ((depth + 1,), single, "scalars"),
        ],
        (owner, *att),
        [pltpu.VMEM((SQUARE * block[0], width), bfloat)],
        1,
        flops=COST,
    )

    return (
        combined,
        input_grad,
        history_grad,
        qkv_grad.reshape(3, part, width).transpose(2, 0, 1),
        out_grad,
        up_grad,
        down_grad,
        gain_attn_grad,
        gain_mlp_grad,
        dwa_grad,
    )


def solution(mesh):
    placed = (
        P(("dp", "mp"), None),
        P(None, ("dp", "mp"), None),
        P(("dp", "mp"), None),
        P(None, None, "mp"),
        P("mp", None),
        P(None, "mp"),
        P("mp", None),
        P(),
        P(),
        P(),
    )
    return jax.shard_map(
        shards,
        mesh=mesh,
        in_specs=placed,
        out_specs=(
            P(("dp", "mp"), None),
            P(("dp", "mp"), None),
            P(None, ("dp", "mp"), None),
            P(None, None, "mp"),
            P("mp", None),
            P(None, "mp"),
            P("mp", None),
            P(),
            P(),
            P(),
        ),
        check_vma=False,
    )
```

```python
import functools

import jax
import jax.numpy as jnp
import numpy as np
from jax import lax
from jax.experimental import pallas as pl
from jax.experimental.pallas import tpu as pltpu
from jax.sharding import PartitionSpec as P

DH = 64
SEQ = 1152
HALF = SEQ // 2
EPS = 1e-05
bfloat = jnp.bfloat16
single = jnp.float32
MIB = 1 << 20
MUCH = 10**11
COST = 10**10


def tables():
    half_width = DH // 2
    places = np.arange(SEQ, dtype=np.float32)
    frequency = np.float32(10000.0) ** (-np.arange(half_width, dtype=np.float32) * np.float32(2.0 / DH))
    angles = frequency[:, None] * places[None, :]
    return (np.cos(angles).astype(np.float32), np.sin(angles).astype(np.float32))


def mul(a, b, ca=1, cb=0):
    return lax.dot_general(a, b, (((ca,), (cb,)), ((), ())), preferred_element_type=single)


def call(kernel, outs, operands, scratch=(), scalars=0, after=(), vmem=16, flops=0, far=0, far_outs=0):
    count, waits = len(operands), len(after)

    def body(*refs):
        kernel(*refs[:count], *refs[count + waits :])

    small = pl.BlockSpec(memory_space=pltpu.SMEM)
    whole = pl.BlockSpec(memory_space=pltpu.VMEM)
    apart = pl.BlockSpec(memory_space=pltpu.HBM)
    loose = pl.BlockSpec(memory_space=pl.ANY)
    inner = len(outs) - far_outs
    return pl.pallas_call(
        body,
        out_shape=[jax.ShapeDtypeStruct(out[0], out[1]) for out in outs],
        in_specs=[small] * scalars + [whole] * (count - scalars - far) + [apart] * far + [loose] * waits,
        out_specs=[small if len(out) > 2 else whole for out in outs[:inner]] + [apart] * far_outs,
        scratch_shapes=list(scratch),
        compiler_params=pltpu.CompilerParams(vmem_limit_bytes=vmem * MIB),
        cost_estimate=pl.CostEstimate(flops=flops, bytes_accessed=0, transcendentals=0),
    )(*operands, *after)


class Mover:
    def __init__(self, marks):
        self.marks = marks
        self.used = 0

    def __call__(self, *pairs):
        copies = []
        for source, target in pairs:
            copies.append(pltpu.make_async_copy(source, target, self.marks.at[self.used]))
            self.used += 1
        for copy in copies:
            copy.start()
        return copies


def wait(copies):
    for copy in copies:
        copy.wait()


ROWS = 64
PARTS = 1


def spans(rows, step=ROWS):
    return [slice(begin, begin + step) for begin in range(0, rows, step)]


def normal_of(x):
    centre = x - jnp.mean(x, axis=-1, keepdims=True)
    spread = jnp.mean(centre * centre, axis=-1, keepdims=True)
    scale = lax.rsqrt(spread + EPS)
    return centre * scale, scale


def split_body(owner_ref, in_ref, out_ref, hold, marks):
    go = Mover(marks)
    wait(go((in_ref.at[quarter(owner_ref[0], 0, hold.shape[0]), :], hold)))
    wait(go((hold, out_ref)))


def joined(owner, refs, target):
    size = refs[0].shape[0]
    return [(ref, target.at[quarter(owner, mask, size), :]) for mask, ref in enumerate(refs)]


def norm_body(x_ref, gain_ref, *out_refs):
    gain = gain_ref[...].reshape(1, -1)
    for index, out_ref in enumerate(out_refs):
        rows = out_ref.shape[0]
        for span in spans(rows, rows // 6):
            here = slice(index * rows + span.start, index * rows + span.stop)
            normal, _ = normal_of(x_ref[here, :].astype(single))
            out_ref[span, :] = (normal * gain).astype(bfloat)


def middle_body(x_ref, keep_ref, gain_ref, *rest):
    recv_refs, mid_ref, out_refs = rest[:PARTS], rest[PARTS], rest[PARTS + 1 :]
    gain = gain_ref[...].reshape(1, -1)
    rows = x_ref.shape[0] // PARTS
    for index in range(PARTS):
        for span in spans(rows):
            here = slice(index * rows + span.start, index * rows + span.stop)
            recv = recv_refs[index][span, :].astype(single)
            x = x_ref[here, :].astype(single) + (keep_ref[here, :] + recv)
            mid_ref[here, :] = x
            normal, _ = normal_of(x)
            out_refs[index][span, :] = (normal * gain).astype(bfloat)


def norm_back(x, grad, gain):
    normal, scale = normal_of(x)
    lifted = grad * gain
    back = scale * (
        lifted
        - jnp.mean(lifted, axis=-1, keepdims=True)
        - normal * jnp.mean(lifted * normal, axis=-1, keepdims=True)
    )
    return back, normal


def fold_rows(value):
    total = value[:8]
    for begin in range(8, value.shape[0], 8):
        total = total + value[begin : begin + 8]
    return total


def middle_back_body(mix_ref, x_ref, keep_ref, recv_ref, cot_ref, gain_ref, mid_ref, low_ref, part_ref):
    gain = gain_ref[...].reshape(1, -1)
    part = jnp.zeros((8, x_ref.shape[1]), single)
    for span in spans(x_ref.shape[0]):
        grad = keep_ref[span, :] + recv_ref[span, :].astype(single)
        back, normal = norm_back(x_ref[span, :], grad, gain)
        total = mix_ref[mix_ref.shape[0] - 1] * cot_ref[span, :] + back
        mid_ref[span, :] = total
        low_ref[span, :] = total.astype(bfloat)
        part = part + fold_rows(grad * normal)
    part_ref[...] = jnp.sum(part, axis=0, keepdims=True)


def first_back_body(x_ref, keep_ref, recv_ref, mid_ref, gain_ref, out_ref):
    gain = gain_ref[...].reshape(1, -1)
    for span in spans(x_ref.shape[0]):
        grad = keep_ref[span, :] + recv_ref[span, :].astype(single)
        back, _ = norm_back(x_ref[span, :].astype(single), grad, gain)
        out_ref[span, :] = (mid_ref[span, :] + back).astype(bfloat)


def history_body(mix_ref, history_ref, cot_ref, grad_ref, mixed_ref, low_ref, part_ref):
    depth = history_ref.shape[0]

    @pl.when(pl.program_id(0) == 0)
    def _():
        part_ref[...] = jnp.zeros_like(part_ref)

    for span in spans(cot_ref.shape[0], 32):
        cot = cot_ref[span, :]
        low_ref[span, :] = (mix_ref[depth] * cot).astype(bfloat)
        mixed = None
        for j in range(depth):
            layer = history_ref[j, span, :].astype(single)
            mixed = mix_ref[j] * layer if mixed is None else mixed + mix_ref[j] * layer
            grad_ref[j, span, :] = (mix_ref[j] * cot).astype(bfloat)
            part_ref[8 * j : 8 * j + 8, :] += fold_rows(layer * cot)
        mixed_ref[span, :] = mixed


def average_history(mix, history, cot, after=()):
    depth, rows, width = history.shape
    step = 96
    waits = len(after)

    def body(*refs):
        history_body(*refs[:3], *refs[3 + waits :])

    row_block = pl.BlockSpec((step, width), lambda i: (i, 0))
    deep_block = pl.BlockSpec((depth, step, width), lambda i: (0, i, 0))
    return pl.pallas_call(
        body,
        grid=(rows // step,),
        out_shape=[
            jax.ShapeDtypeStruct(history.shape, bfloat),
            jax.ShapeDtypeStruct((rows, width), single),
            jax.ShapeDtypeStruct((rows, width), bfloat),
            jax.ShapeDtypeStruct((8 * depth, width), single),
        ],
        in_specs=[pl.BlockSpec(memory_space=pltpu.SMEM), deep_block, row_block]
        + [pl.BlockSpec(memory_space=pl.ANY)] * waits,
        out_specs=[deep_block, row_block, row_block, pl.BlockSpec((8 * depth, width), lambda i: (0, 0))],
        compiler_params=pltpu.CompilerParams(vmem_limit_bytes=16 * MIB),
        cost_estimate=pl.CostEstimate(flops=0, bytes_accessed=0, transcendentals=0),
    )(mix, history, cot, *after)


def combine_body(mix_ref, mixed_ref, mid_ref, keep_ref, recv_ref, cot_ref, parts_ref, out_ref, part_ref):
    depth = mix_ref.shape[0] - 1
    last = jnp.zeros((8, mid_ref.shape[1]), single)
    for span in spans(mid_ref.shape[0]):
        outputs = mid_ref[span, :] + (keep_ref[span, :] + recv_ref[span, :].astype(single))
        out_ref[span, :] = (mixed_ref[span, :] + mix_ref[depth] * outputs).astype(bfloat)
        last = last + fold_rows(outputs * cot_ref[span, :])
    for j in range(depth):
        part_ref[j : j + 1, :] = jnp.sum(parts_ref[8 * j : 8 * j + 8, :], axis=0, keepdims=True)
    part_ref[depth : depth + 1, :] = jnp.sum(last, axis=0, keepdims=True)


SQUARE = 4


def quarter(owner, mask, size):
    other = owner + (mask & 1) * (1 - 2 * (owner % 2)) + (mask & 2) * (1 - 2 * (owner // 2))
    return pl.ds(pl.multiple_of(other * size, size), size)


def part_body(owner_ref, mine_ref, come_ref, *out_refs):
    for mask, out_ref in enumerate(out_refs):
        rows = quarter(owner_ref[0], mask, out_ref.shape[0])
        out_ref[...] = (mine_ref[rows, :].astype(single) + come_ref[rows, :].astype(single)).astype(bfloat)


def sum_of(refs, rows):
    total = refs[0][rows, :].astype(single)
    for ref in refs[1:]:
        total = total + ref[rows, :].astype(single)
    return total


def four_body(*refs):
    refs[-1][...] = sum_of(refs[:-1], slice(None)).astype(bfloat)


def four_two_body(*refs):
    size = refs[-1].shape[0]
    refs[-2][...] = sum_of(refs[:-2], slice(0, size)).astype(bfloat)
    refs[-1][...] = sum_of(refs[:-2], slice(size, 2 * size)).astype(bfloat)


EXTRA = 16


def small_body(small_ref, first_ref, out_ref):
    half = small_ref.shape[0]
    rows = first_ref.shape[0] - 2 * half
    come = first_ref[rows:, :].astype(single)
    out_ref[...] = small_ref[...] + (come[:half] + come[half:])


def four_more_body(small_ref, more_ref, *refs):
    out_ref = refs[-1]
    size = out_ref.shape[0] - EXTRA
    out_ref[:size, :] = sum_of(refs[:-1], slice(None)).astype(bfloat)
    small = small_ref[...] + more_ref[...]
    rest = jnp.zeros((EXTRA - small.shape[0], small.shape[1]), single)
    out_ref[size:, :] = jnp.concatenate([small, rest], axis=0).astype(bfloat)


def gather(owner_ref, pieces, hold):
    for mask, piece in enumerate(pieces):
        hold[quarter(owner_ref[0], mask, piece.shape[0]), :] = piece[...]


def pair_body(a_ref, a_come_ref, b_ref, b_come_ref, out_ref):
    size = a_ref.shape[0]
    out_ref[:size, :] = sum_of((a_ref, a_come_ref), slice(None)).astype(bfloat)
    out_ref[size:, :] = sum_of((b_ref, b_come_ref), slice(None)).astype(bfloat)


def pair_whole_body(owner_ref, a_ref, b_ref, c_ref, d_ref, down_ref, up_ref, hold):
    gather(owner_ref, (a_ref, b_ref, c_ref, d_ref), hold)
    block = hold.shape[0] // SQUARE
    size = block // 2
    for index in range(SQUARE):
        begin, rows = index * block, slice(index * size, (index + 1) * size)
        down_ref[rows, :] = hold[begin : begin + size, :].astype(single)
        up_ref[rows, :] = hold[begin + size : begin + block, :].astype(single)


def more_body(owner_ref, a_ref, b_ref, c_ref, d_ref, top_ref, end_ref, attn_ref, mlp_ref, dwa_ref, hold):
    gather(owner_ref, (a_ref, b_ref, c_ref, d_ref), hold)
    block = hold.shape[0] // SQUARE
    rows = block - EXTRA
    small = jnp.zeros((EXTRA, hold.shape[1]), single)
    for index in range(SQUARE):
        begin = index * block
        target, place = (top_ref, index * rows) if index < SQUARE - 1 else (end_ref, 0)
        target[place : place + rows, :] = hold[begin : begin + rows, :].astype(single)
        small = small + hold[begin + rows : begin + block, :].astype(single)
    attn_ref[...] = small[0]
    mlp_ref[...] = small[1]
    for index in range(dwa_ref.shape[0]):
        dwa_ref[index] = jnp.sum(small[2 + index : 3 + index])


def low_body(mine_ref, come_ref, out_ref):
    out_ref[...] = (mine_ref[...].astype(single) + come_ref[...].astype(single)).astype(bfloat)


def small_body(small_ref, first_ref, out_ref):
    half = small_ref.shape[0]
    rows = first_ref.shape[0] - 2 * half
    come = first_ref[rows:, :].astype(single)
    out_ref[...] = small_ref[...] + (come[:half] + come[half:])


BLOCKS = tuple((begin, min(256, SEQ - begin)) for begin in range(0, SEQ, 256))


def places(core_ref, refs):
    count, size = len(refs) // 2, refs[0].shape[0]
    for index, ref in enumerate(refs):
        core = core_ref[0] if index < count else 1 - core_ref[0]
        yield ref, pl.ds(pl.multiple_of(core * HALF + index % count * size, size), size)


def allowed(size):
    key_pos = lax.broadcasted_iota(jnp.int32, (size, size), 0)
    query_pos = lax.broadcasted_iota(jnp.int32, (size, size), 1)
    return query_pos >= key_pos


def turn(rows, cosine, sine):
    half = rows.shape[0] // 2
    a, b = rows[:half], rows[half:]
    return jnp.concatenate([a * cosine - b * sine, b * cosine + a * sine], axis=0)


KEYS = 128


def fold_top(value):
    top = value[:8]
    for begin in range(8, value.shape[0], 8):
        top = jnp.maximum(top, value[begin : begin + 8])
    return top


def masked(scores, offset):
    key_pos = lax.broadcasted_iota(jnp.int32, scores.shape, 0) + offset
    query_pos = lax.broadcasted_iota(jnp.int32, scores.shape, 1)
    return jnp.where(query_pos >= key_pos, scores, -jnp.inf)


def attend_placed(core_ref, *rest):
    for ref, where in places(core_ref, rest[:4]):
        rest[11][where, :] = ref[...]
    cos_ref, sin_ref, weight_ref, rest = rest[4], rest[5], rest[6], rest[7:]
    attend(weight_ref, cos_ref, sin_ref, *rest)


def attend(weight_ref, cos_ref, sin_ref, qkv_ref, att_ref, nat_ref, log_ref, tokens, all_scores, all_weights):
    width = weight_ref.shape[0] // 3
    projected = mul(weight_ref[...], tokens[...], 1, 1)
    cosine, sine = cos_ref[...], sin_ref[...]
    for part in range(3):
        for head in range(width // DH):
            begin = part * width + head * DH
            rows = projected[begin : begin + DH]
            if part < 2:
                rows = turn(rows, cosine, sine)
            if part == 0:
                rows = rows * DH ** (-0.5)
            qkv_ref[begin : begin + DH, :] = rows.astype(bfloat)
    log_ref[...] = jnp.zeros_like(log_ref)
    heads = range(width // DH)
    keys = [qkv_ref[width + head * DH : width + head * DH + DH, :].T for head in heads]
    for begin, size in BLOCKS:
        end = begin + size
        tops = [None for _ in heads]
        for row in range(0, end, KEYS):
            for head in heads:
                tile = mul(keys[head][row : row + KEYS], qkv_ref[head * DH : head * DH + DH, begin:end])
                if row >= begin:
                    tile = masked(tile, row - begin)
                all_scores[head, row : row + KEYS, :size] = tile
                top = fold_top(tile)
                tops[head] = top if row == 0 else jnp.maximum(tops[head], top)
        tops = [jnp.max(top, axis=0, keepdims=True) for top in tops]
        totals = [jnp.zeros((8, size), single) for _ in heads]
        for row in range(0, end, KEYS):
            for head in heads:
                tile = jnp.exp(all_scores[head, row : row + KEYS, :size] - tops[head])
                totals[head] = totals[head] + fold_rows(tile)
                all_weights[head, row : row + KEYS, :size] = tile.astype(bfloat)
        for head in heads:
            base = head * DH
            total = jnp.sum(totals[head], axis=0, keepdims=True)
            value = qkv_ref[2 * width + base : 2 * width + base + DH, :end]
            mixed = mul(value, all_weights[head, :end, :size]) / total
            att_ref[base : base + DH, begin:end] = mixed.astype(bfloat)
            log_ref[head : head + 1, begin:end] = tops[head] + jnp.log(total)
    nat_ref[...] = att_ref[...].T


def branch_body(core_ref, att_a_ref, att_b_ref, out_a_ref, out_b_ref, pass_ref, keep_ref, *rest):
    send_refs, pass_out = rest[:PARTS], rest[PARTS]
    pass_out[...] = pass_ref[...]
    low = pl.multiple_of(core_ref[0] * HALF, HALF)
    rows = HALF // PARTS
    for index in range(PARTS):
        high = pl.multiple_of((1 - core_ref[0]) * HALF + index * rows, rows)
        send = mul(att_a_ref[pl.ds(high, rows), :], out_a_ref[...])
        send_refs[index][...] = (send + mul(att_b_ref[pl.ds(high, rows), :], out_b_ref[...])).astype(bfloat)
    keep = mul(att_a_ref[pl.ds(low, HALF), :], out_a_ref[...])
    keep_ref[...] = keep + mul(att_b_ref[pl.ds(low, HALF), :], out_b_ref[...])


def attend_back(
    core_ref, log_ref, cos_ref, sin_ref, gain_ref, *rest
):
    before_refs, rest = rest[:-25], rest[-25:]
    grad_refs, x_refs = rest[:2], rest[2:6]
    weight_ref, qkv_weight_ref, qkv_ref, att_ref, small_ref, out_ref, turned_ref = rest[6:13]
    grads, tokens, weight, qkv_weight, qkv, att, turned, result, all_probs, all_scores, hold, marks = rest[13:]
    go = Mover(marks)
    first = go(
        (weight_ref, weight),
        *[(ref, grads.at[where, :]) for ref, where in places(core_ref, grad_refs)],
        (att_ref, att),
        (qkv_ref, qkv),
    )
    later = go(
        *[(ref, tokens.at[where, :]) for ref, where in places(core_ref, x_refs)],
        (qkv_weight_ref, qkv_weight),
    )
    wait(first)
    width = att.shape[0]
    grad_att = mul(weight[...], grads[...], 1, 1).astype(bfloat)
    result[3 * width :, :] = mul(att[...], grads[...]).astype(result.dtype)
    cosine, sine = cos_ref[...], sin_ref[...]
    heads = range(width // DH)
    spans_of = [slice(head * DH, head * DH + DH) for head in heads]
    query = [qkv[span, :] for span in spans_of]
    key = [qkv[width + span.start : width + span.stop, :] for span in spans_of]
    above = [grad_att[span] for span in spans_of]
    centre = [
        jnp.sum(above[head].astype(single) * att[span, :].astype(single), axis=0, keepdims=True)
        for head, span in enumerate(spans_of)
    ]
    keys = [value.T for value in key]
    values = [qkv[2 * width + span.start : 2 * width + span.stop, :].T for span in spans_of]
    queries = [value.T for value in query]
    aboves = [value.T for value in above]
    grad_query = [[] for _ in heads]
    for begin, size in BLOCKS:
        end = begin + size
        for row in range(0, end, KEYS):
            span = slice(row, row + KEYS)
            for head in heads:
                tile = mul(keys[head][span], query[head][:, begin:end])
                if row >= begin:
                    tile = masked(tile, row - begin)
                tile = jnp.exp(tile - log_ref[head : head + 1, begin:end])
                grad = mul(values[head][span], above[head][:, begin:end]) - centre[head][:, begin:end]
                all_probs[head, span, begin:end] = tile.astype(bfloat)
                all_scores[head, span, begin:end] = (tile * grad).astype(bfloat)
        for head in heads:
            grad_query[head].append(mul(key[head][:, :end], all_scores[head, :end, begin:end]))
    grad_key = [[] for _ in heads]
    grad_value = [[] for _ in heads]
    for begin, size in BLOCKS:
        span = slice(begin, begin + size)
        for head in heads:
            grad_key[head].append(mul(all_scores[head, span, begin:], queries[head][begin:]))
            grad_value[head].append(mul(all_probs[head, span, begin:], aboves[head][begin:]))
    for head, span in enumerate(spans_of):
        grad = jnp.concatenate(grad_query[head], axis=1) * DH ** (-0.5)
        turned[span, :] = turn(grad, cosine, -sine).astype(bfloat)
        grad = jnp.concatenate(grad_key[head], axis=0).T
        turned[width + span.start : width + span.stop, :] = turn(grad, cosine, -sine).astype(bfloat)
        grad = jnp.concatenate(grad_value[head], axis=0).T
        turned[2 * width + span.start : 2 * width + span.stop, :] = grad.astype(bfloat)
    stores = go((turned, turned_ref))
    wait(later)
    hold[...] = mul(turned[...], tokens[...])
    result[: 3 * width, :] = hold[...].astype(result.dtype)
    stores += go((result, out_ref))
    part = jnp.zeros((8, hold.shape[1]), single)
    for span in spans(hold.shape[0]):
        part = part + fold_rows(hold[span, :] * qkv_weight[span, :].astype(single))
    gain = jnp.sum(part, axis=0, keepdims=True) / gain_ref[...].reshape(1, -1)
    if before_refs:
        gain_part_ref, mlp_part_ref, dwa_part_ref = before_refs
        small_ref[:1, :] = gain + gain_part_ref[...]
        small_ref[1:2, :] = mlp_part_ref[...]
        small_ref[2:, :] = dwa_part_ref[...]
    else:
        small_ref[...] = gain
    wait(stores)


def first_grad_body(
    core_ref, small_ref, turned_a_ref, turned_b_ref, weight_a_ref, weight_b_ref, send_ref, keep_ref,
    turned_a, turned_b, weight_a, weight_b, whole, marks,
):
    low = pl.multiple_of(core_ref[0] * HALF, HALF)
    high = pl.multiple_of((1 - core_ref[0]) * HALF, HALF)
    go = Mover(marks)
    wait(go((turned_a_ref, turned_a), (weight_a_ref, weight_a), (turned_b_ref, turned_b), (weight_b_ref, weight_b)))
    whole[...] = mul(turned_a[...], weight_a[...], 0, 0) + mul(turned_b[...], weight_b[...], 0, 0)
    stores = go((whole.at[pl.ds(low, HALF), :], keep_ref))
    send_ref[:HALF, :] = whole[pl.ds(high, HALF), :].astype(bfloat)
    small = small_ref[...]
    high_part = small.astype(bfloat)
    low_part = (small - high_part.astype(single)).astype(bfloat)
    send_ref[HALF:, :] = jnp.concatenate([high_part, low_part], axis=0)
    wait(stores)


CURVE = float(np.sqrt(2.0 / np.pi))
STEP = 256


def mlp_body(second, *refs):
    if second:
        owner_ref, refs = refs[0], refs[1:]
    x_refs, refs = refs[: 2 * PARTS], refs[2 * PARTS :]
    g_own_ref, g_peer_ref, refs = refs[0], refs[1], refs[2:]
    if second:
        up_ref, down_refs, refs = refs[0], refs[1 : 1 + SQUARE], refs[1 + SQUARE :]
        before_refs, up_mine_ref = refs[:4], refs[4]
        down_grad_ref, part_refs = refs[9], refs[10:14]
        refs = refs[5:9] + refs[14:]
    else:
        up_ref, down_ref = refs[:2]
        down_grad_ref, up_grad_ref = refs[6:8]
        refs = refs[2:6] + refs[8:]
    send_norm_ref, keep_norm_ref, send_out_ref, keep_out_ref = refs[:4]
    x_all, g_all, up, down, active, grad_hidden, x_turned = refs[4:11]
    send_norm, keep_norm, send_out, keep_out, down_grad, up_grad, marks = refs[11:18]
    rows, size = x_all.shape[0] // 2, x_all.shape[0] // (2 * PARTS)
    units = down.shape[0]
    go = Mover(marks)
    x_loads = go(*[(x_refs[index], x_all.at[pl.ds(index * size, size), :]) for index in range(2 * PARTS)])
    if second:
        loads = go((up_ref, up), *joined(owner_ref[0], down_refs, down))
    else:
        loads = go((up_ref, up), (down_ref, down))
    loads += go((g_own_ref, g_all.at[pl.ds(0, rows), :]), (g_peer_ref, g_all.at[pl.ds(rows, rows), :]))
    more, mine, stores = [], [], []
    if second:
        (up_mine,) = refs[18:]
        more = go(*zip(before_refs, (send_norm, keep_norm, send_out, keep_out)))
        mine = go((up_mine_ref, up_mine))
    wait(x_loads)
    x_turned[...] = x_all[...].T
    wait(loads)
    for begin in range(0, units, STEP):
        columns = slice(begin, begin + STEP)
        for top in range(0, 2 * rows, rows):
            span = slice(top, top + rows)
            v = mul(x_all[span, :], up[:, columns])
            grad = mul(g_all[span, :], down[columns, :], 1, 1)
            square = v * v
            half = 0.5 + 0.5 * jnp.tanh(v * (CURVE + (CURVE * 0.044715) * square))
            act = v * half
            slope = half + act * (1.0 - half) * (2.0 * CURVE + (6.0 * CURVE * 0.044715) * square)
            active[span, columns] = act.astype(bfloat)
            grad_hidden[span, columns] = (grad * slope).astype(bfloat)

    def put(target, value):
        target[...] = (value + target[...].astype(single) if second else value).astype(target.dtype)

    wait(more)
    put(keep_norm, mul(grad_hidden[:rows, :], up[...], 1, 1))
    put(send_norm, mul(grad_hidden[rows:, :], up[...], 1, 1))
    stores += go((keep_norm, keep_norm_ref), (send_norm, send_norm_ref))
    down_grad[...] = mul(active[...], g_all[...], 0, 0).astype(down_grad.dtype)
    stores += go((down_grad, down_grad_ref))
    up_grad[...] = mul(x_turned[...], grad_hidden[...]).astype(bfloat)
    if second:
        wait(mine)
        part = up_grad.shape[0] // SQUARE
        for mask, part_ref in enumerate(part_refs):
            rows_of = quarter(owner_ref[0], mask, part)
            stores += go(
                (up_mine.at[rows_of, :], part_ref.at[pl.ds(0, part), :]),
                (up_grad.at[rows_of, :], part_ref.at[pl.ds(part, part), :]),
            )
    else:
        stores += go((up_grad, up_grad_ref))
    put(keep_out, mul(active[:rows, :], down[...]))
    stores += go((keep_out, keep_out_ref))
    put(send_out, mul(active[rows:, :], down[...]))
    wait(stores + go((send_out, send_out_ref)))


def mlp(x_own, x_peer, g_own, g_peer, up, down, upper=(), before=(), flops=0):
    rows, width = g_own.shape
    units = sum(piece.shape[0] for piece in down)
    tall = (2 * rows, width)
    pair = [((rows, width), bfloat), ((rows, width), single)] * 2
    outs = pair + [((units, width), bfloat)]
    outs += [((2 * width // SQUARE, units), bfloat)] * SQUARE if before else [((width, units), bfloat)]
    scratch = [
        pltpu.VMEM(tall, bfloat),
        pltpu.VMEM(tall, bfloat),
        pltpu.VMEM((width, units), bfloat),
        pltpu.VMEM((units, width), bfloat),
        pltpu.VMEM((2 * rows, units), bfloat),
        pltpu.VMEM((2 * rows, units), bfloat),
        pltpu.VMEM((width, 2 * rows), bfloat),
    ]
    scratch += [pltpu.VMEM(shape, kind) for shape, kind in pair]
    scratch += [
        pltpu.VMEM((units, width), bfloat), pltpu.VMEM((width, units), bfloat), pltpu.SemaphoreType.DMA((32,)),
    ]
    if before:
        scratch.append(pltpu.VMEM((width, units), bfloat))
    operands = (*upper, *x_own, *x_peer, g_own, g_peer, *up, *down, *before)
    return call(
        functools.partial(mlp_body, bool(before)),
        outs,
        operands,
        scratch,
        len(upper),
        vmem=60,
        flops=flops,
        far=len(operands) - len(upper),
        far_outs=len(outs),
    )


def shards(
    inputs,
    history,
    cotangent,
    qkv_weight,
    out_weight,
    up_weight,
    down_weight,
    gain_attn,
    gain_mlp,
    dwa_weights,
):
    rows, width = inputs.shape
    members = lax.axis_size("mp")
    copies = lax.axis_size("dp")
    bits = copies.bit_length() - 1
    core = lax.rem(lax.axis_index("mp"), 2).astype(jnp.int32).reshape(1)
    copy_index = lax.axis_index("dp").astype(jnp.int32).reshape(1)
    core_pairs = [(i, i ^ 1) for i in range(members)]
    chip_pairs = [(i, i ^ 2) for i in range(members)]
    depth = history.shape[0]
    part = out_weight.shape[0]

    def other_core(value):
        return lax.ppermute(value, "mp", core_pairs)

    def other_chip(value):
        return lax.ppermute(value, "mp", chip_pairs)

    def other_copy(value, mask):
        return lax.ppermute(value, "dp", [(i, i ^ mask) for i in range(copies)])

    owner = copy_index & (SQUARE - 1)
    cosine, sine = (jnp.asarray(table) for table in tables())

    qkv_own = qkv_weight.transpose(1, 2, 0).reshape(3 * part, width)
    fourth = (width // SQUARE, width)
    square = (width, width)
    masks = range(1, SQUARE)
    marks = pltpu.SemaphoreType.DMA((16,))
    (down_quarter,) = call(
        split_body,
        [(fourth, bfloat)],
        (owner, down_weight),
        [pltpu.VMEM(fourth, bfloat), marks],
        1,
        vmem=60,
        far=1,
        far_outs=1,
    )
    qkv_peer, out_peer = other_chip(qkv_own), other_chip(out_weight)
    down_come, up_peer = other_chip(down_quarter), other_chip(up_weight)

    full = (rows, width)
    x_own = call(norm_body, [((rows // 2, width), bfloat)] * 2, (inputs, gain_attn), after=(down_quarter,))
    x_peer = [other_core(value) for value in x_own]
    tall = (SEQ, width)
    tokens = pltpu.VMEM(tall, bfloat)
    first_outs = [
        ((3 * part, SEQ), bfloat), ((part, SEQ), bfloat), ((SEQ, part), bfloat), ((8, SEQ), single),
    ]
    heads = part // DH
    tiles = [tokens, pltpu.VMEM((heads, SEQ, 256), single), pltpu.VMEM((heads, SEQ, 256), bfloat)]
    qkv_a, att_a, nat_a, log_a = call(
        attend_placed, first_outs, (core, *x_own, *x_peer, cosine, sine, qkv_own), tiles, 1, vmem=32
    )
    history_grad, mixed, g_own, history_parts = average_history(dwa_weights, history, cotangent, (log_a,))
    g_peer = other_core(g_own)
    qkv_b, att_b, nat_b, log_b = call(
        attend_placed,
        first_outs,
        (core, *x_own, *x_peer, cosine, sine, qkv_peer),
        tiles,
        1,
        (history_parts,),
        32,
        MUCH,
    )
    third = (rows // PARTS, width)
    keep, *send, down_copy = call(
        branch_body,
        [(full, single)] + [(third, bfloat)] * PARTS + [(fourth, bfloat)],
        (core, nat_a, nat_b, out_weight, out_peer, down_come),
        (),
        1,
        (g_peer,),
    )
    down_pieces = [down_come] + [other_copy(down_copy, mask) for mask in masks]
    recv = [other_core(value) for value in send]
    middle, *y_own = call(
        middle_body, [(full, single)] + [(third, bfloat)] * PARTS, (inputs, keep, gain_mlp, *recv)
    )
    y_peer = [other_core(value) for value in y_own]

    first = mlp(y_own, y_peer, g_own, g_peer, (up_weight,), (down_weight,))
    down_mine, up_mine = first[4:]
    second = mlp(
        y_own, y_peer, g_own, g_peer, (up_peer,), down_pieces, (owner,), (*first[:4], up_mine)
    )
    send_norm, keep_norm, send_out, keep_out, down_theirs = second[:5]
    token = [send_norm]

    def step(body, outs, operands, scratch=(), scalars=0, vmem=16, flops=MUCH, far=0, far_outs=0):
        results = call(body, outs, operands, scratch, scalars, tuple(token), vmem, flops, far, far_outs)
        token[0] = results[0]
        return results

    down_come = other_chip(down_theirs)
    up_parts = [second[5]] + [other_copy(value, mask) for mask, value in zip(masks, second[6:])]
    out_come = other_core(send_out)
    grad_middle, gb_own, gain_mlp_part = step(
        middle_back_body,
        [(full, single), (full, bfloat), ((1, width), single)],
        (dwa_weights, middle, keep_norm, other_core(send_norm), cotangent, gain_mlp),
        scalars=1,
        flops=0,
    )
    gb_peer = other_core(gb_own)
    combined, dwa_part = step(
        combine_body,
        [(full, bfloat), ((depth + 1, width), single)],
        (dwa_weights, mixed, middle, keep_out, out_come, cotangent, history_parts),
        scalars=1,
        flops=0,
    )

    def back(weight, qkv_weight, qkv, att, log, flops, before=()):
        return step(
            attend_back,
            [
                ((depth + 3 if before else 1, width), single),
                ((4 * part, width), bfloat),
                ((3 * part, SEQ), bfloat),
            ],
            (
                core, log, cosine, sine, gain_attn, *before, gb_own, gb_peer, *x_own, *x_peer, weight, qkv_weight, qkv,
                att,
            ),
            [
                pltpu.VMEM(tall, bfloat),
                pltpu.VMEM(tall, bfloat),
                pltpu.VMEM((part, width), bfloat),
                pltpu.VMEM((3 * part, width), bfloat),
                pltpu.VMEM((3 * part, SEQ), bfloat),
                pltpu.VMEM((part, SEQ), bfloat),
                pltpu.VMEM((3 * part, SEQ), bfloat),
                pltpu.VMEM((4 * part, width), bfloat),
                pltpu.VMEM((heads, SEQ, SEQ), bfloat),
                pltpu.VMEM((heads, SEQ, SEQ), bfloat),
                pltpu.VMEM((3 * part, width), single),
                marks,
            ],
            1,
            60,
            flops,
            10,
            2,
        )

    gain_part, att_theirs, turned_b = back(out_peer, qkv_peer, qkv_b, att_b, log_b, 0)
    att_come = other_chip(att_theirs)
    def spread(mine, come, flops=MUCH):
        own, *sent = step(part_body, [(fourth, bfloat)] * SQUARE, (owner, mine, come), scalars=1, flops=flops)
        return [own] + [other_copy(value, mask) for mask, value in zip(masks, sent)]

    down_parts = spread(down_mine, down_come, 0)
    up, sent = step(four_two_body, [(fourth, bfloat)] * 2, up_parts, flops=0)
    up_come = other_chip(sent)
    part_sums, att_mine, turned_a = back(
        out_weight, qkv_own, qkv_a, att_a, log_a, MUCH, (gain_part, gain_mlp_part, dwa_part)
    )

    def exchange(value):
        for bit in range(2, bits):
            come = other_copy(value, 1 << bit)
            if bit < bits - 1:
                (value,) = step(low_body, [(value.shape, bfloat)], (value, come))
        return value, come

    def finish(value, come):
        (value,) = step(low_body, [(value.shape, bfloat)], (value, come), flops=COST)
        return [value] + [other_copy(value, mask) for mask in masks]

    (down,) = step(four_body, [(fourth, bfloat)], down_parts, flops=COST)
    down = exchange(down)
    att_parts = spread(att_mine, att_come, COST)
    send_first, keep_first = step(
        first_grad_body,
        [((rows + EXTRA, width), bfloat), (full, single)],
        (core, part_sums, turned_a, turned_b, qkv_own, qkv_peer),
        [pltpu.VMEM((3 * part, SEQ), bfloat)] * 2
        + [pltpu.VMEM((3 * part, width), bfloat)] * 2
        + [pltpu.VMEM(tall, single), marks],
        1,
        60,
        COST,
        4,
        1,
    )
    first_come = other_core(send_first)
    token.append(down[1])
    (up,) = step(low_body, [(fourth, bfloat)], (up, up_come), flops=COST)
    token.pop()
    up = exchange(up)
    (part_sums,) = step(small_body, [(part_sums.shape, single)], (part_sums, first_come), flops=COST)
    more_sums = other_chip(part_sums)
    (input_grad,) = step(
        first_back_body,
        [(full, bfloat)],
        (inputs, keep_first, first_come, grad_middle, gain_attn),
        vmem=60,
        flops=COST,
    )
    block = (width // SQUARE + EXTRA, width)
    (att,) = step(four_more_body, [(block, bfloat)], (part_sums, more_sums, *att_parts), flops=COST)
    att = exchange(att)
    pair = (2 * width // SQUARE, width)
    (both,) = step(pair_body, [(pair, bfloat)], (*down, *up), flops=COST)
    both = [both] + [other_copy(both, mask) for mask in masks]
    att = finish(*att)
    down_grad, up_grad = step(
        pair_whole_body,
        [(square, single)] * 2,
        (owner, *both),
        [pltpu.VMEM((SQUARE * pair[0], width), bfloat)],
        1,
        flops=COST,
    )
    qkv_grad, out_grad, gain_attn_grad, gain_mlp_grad, dwa_grad = step(
        more_body,
        [
            ((3 * part, width), single),
            ((part, width), single),
            ((width,), single),
            ((width,), single),
            ((depth + 1,), single, "scalars"),
        ],
        (owner, *att),
        [pltpu.VMEM((SQUARE * block[0], width), bfloat)],
        1,
        flops=COST,
    )

    return (
        combined,
        input_grad,
        history_grad,
        qkv_grad.reshape(3, part, width).transpose(2, 0, 1),
        out_grad,
        up_grad,
        down_grad,
        gain_attn_grad,
        gain_mlp_grad,
        dwa_grad,
    )


def solution(mesh):
    placed = (
        P(("dp", "mp"), None),
        P(None, ("dp", "mp"), None),
        P(("dp", "mp"), None),
        P(None, None, "mp"),
        P("mp", None),
        P(None, "mp"),
        P("mp", None),
        P(),
        P(),
        P(),
    )
    return jax.shard_map(
        shards,
        mesh=mesh,
        in_specs=placed,
        out_specs=(
            P(("dp", "mp"), None),
            P(("dp", "mp"), None),
            P(None, ("dp", "mp"), None),
            P(None, None, "mp"),
            P("mp", None),
            P(None, "mp"),
            P("mp", None),
            P(),
            P(),
            P(),
        ),
        check_vma=False,
    )
```

```python
import functools

import jax
import jax.numpy as jnp
import numpy as np
from jax import lax
from jax.experimental import pallas as pl
from jax.experimental.pallas import tpu as pltpu
from jax.sharding import PartitionSpec as P

DH = 64
SEQ = 1152
HALF = SEQ // 2
EPS = 1e-05
bfloat = jnp.bfloat16
single = jnp.float32
MIB = 1 << 20
MUCH = 10**11
COST = 10**10


def tables():
    half_width = DH // 2
    places = np.arange(SEQ, dtype=np.float32)
    frequency = np.float32(10000.0) ** (-np.arange(half_width, dtype=np.float32) * np.float32(2.0 / DH))
    angles = frequency[:, None] * places[None, :]
    return (np.cos(angles).astype(np.float32), np.sin(angles).astype(np.float32))


def mul(a, b, ca=1, cb=0):
    return lax.dot_general(a, b, (((ca,), (cb,)), ((), ())), preferred_element_type=single)


def call(kernel, outs, operands, scratch=(), scalars=0, after=(), vmem=16, flops=0, far=0, far_outs=0):
    count, waits = len(operands), len(after)

    def body(*refs):
        kernel(*refs[:count], *refs[count + waits :])

    small = pl.BlockSpec(memory_space=pltpu.SMEM)
    whole = pl.BlockSpec(memory_space=pltpu.VMEM)
    apart = pl.BlockSpec(memory_space=pltpu.HBM)
    loose = pl.BlockSpec(memory_space=pl.ANY)
    inner = len(outs) - far_outs
    return pl.pallas_call(
        body,
        out_shape=[jax.ShapeDtypeStruct(out[0], out[1]) for out in outs],
        in_specs=[small] * scalars + [whole] * (count - scalars - far) + [apart] * far + [loose] * waits,
        out_specs=[small if len(out) > 2 else whole for out in outs[:inner]] + [apart] * far_outs,
        scratch_shapes=list(scratch),
        compiler_params=pltpu.CompilerParams(vmem_limit_bytes=vmem * MIB),
        cost_estimate=pl.CostEstimate(flops=flops, bytes_accessed=0, transcendentals=0),
    )(*operands, *after)


class Mover:
    def __init__(self, marks):
        self.marks = marks
        self.used = 0

    def __call__(self, *pairs):
        copies = []
        for source, target in pairs:
            copies.append(pltpu.make_async_copy(source, target, self.marks.at[self.used]))
            self.used += 1
        for copy in copies:
            copy.start()
        return copies


def wait(copies):
    for copy in copies:
        copy.wait()


ROWS = 64
PARTS = 1


def spans(rows, step=ROWS):
    return [slice(begin, begin + step) for begin in range(0, rows, step)]


def normal_of(x):
    centre = x - jnp.mean(x, axis=-1, keepdims=True)
    spread = jnp.mean(centre * centre, axis=-1, keepdims=True)
    scale = lax.rsqrt(spread + EPS)
    return centre * scale, scale


def split_body(owner_ref, in_ref, out_ref, hold, marks):
    go = Mover(marks)
    wait(go((in_ref.at[quarter(owner_ref[0], 0, hold.shape[0]), :], hold)))
    wait(go((hold, out_ref)))


def joined(owner, refs, target):
    size = refs[0].shape[0]
    return [(ref, target.at[quarter(owner, mask, size), :]) for mask, ref in enumerate(refs)]


def norm_body(x_ref, gain_ref, *out_refs):
    gain = gain_ref[...].reshape(1, -1)
    for index, out_ref in enumerate(out_refs):
        rows = out_ref.shape[0]
        for span in spans(rows, rows // 6):
            here = slice(index * rows + span.start, index * rows + span.stop)
            normal, _ = normal_of(x_ref[here, :].astype(single))
            out_ref[span, :] = (normal * gain).astype(bfloat)


def middle_body(x_ref, keep_ref, gain_ref, *rest):
    recv_refs, mid_ref, out_refs = rest[:PARTS], rest[PARTS], rest[PARTS + 1 :]
    gain = gain_ref[...].reshape(1, -1)
    rows = x_ref.shape[0] // PARTS
    for index in range(PARTS):
        for span in spans(rows):
            here = slice(index * rows + span.start, index * rows + span.stop)
            recv = recv_refs[index][span, :].astype(single)
            x = x_ref[here, :].astype(single) + (keep_ref[here, :] + recv)
            mid_ref[here, :] = x
            normal, _ = normal_of(x)
            out_refs[index][span, :] = (normal * gain).astype(bfloat)


def norm_back(x, grad, gain):
    normal, scale = normal_of(x)
    lifted = grad * gain
    back = scale * (
        lifted
        - jnp.mean(lifted, axis=-1, keepdims=True)
        - normal * jnp.mean(lifted * normal, axis=-1, keepdims=True)
    )
    return back, normal


def fold_rows(value):
    total = value[:8]
    for begin in range(8, value.shape[0], 8):
        total = total + value[begin : begin + 8]
    return total


def middle_back_body(mix_ref, x_ref, keep_ref, recv_ref, cot_ref, gain_ref, mid_ref, low_ref, part_ref):
    gain = gain_ref[...].reshape(1, -1)
    part = jnp.zeros((8, x_ref.shape[1]), single)
    for span in spans(x_ref.shape[0]):
        grad = keep_ref[span, :] + recv_ref[span, :].astype(single)
        back, normal = norm_back(x_ref[span, :], grad, gain)
        total = mix_ref[mix_ref.shape[0] - 1] * cot_ref[span, :] + back
        mid_ref[span, :] = total
        low_ref[span, :] = total.astype(bfloat)
        part = part + fold_rows(grad * normal)
    part_ref[...] = jnp.sum(part, axis=0, keepdims=True)


def first_back_body(x_ref, keep_ref, recv_ref, mid_ref, gain_ref, out_ref):
    gain = gain_ref[...].reshape(1, -1)
    for span in spans(x_ref.shape[0]):
        grad = keep_ref[span, :] + recv_ref[span, :].astype(single)
        back, _ = norm_back(x_ref[span, :].astype(single), grad, gain)
        out_ref[span, :] = (mid_ref[span, :] + back).astype(bfloat)


def history_body(mix_ref, history_ref, cot_ref, grad_ref, mixed_ref, low_ref, part_ref):
    depth = history_ref.shape[0]

    @pl.when(pl.program_id(0) == 0)
    def _():
        part_ref[...] = jnp.zeros_like(part_ref)

    for span in spans(cot_ref.shape[0], 32):
        cot = cot_ref[span, :]
        low_ref[span, :] = (mix_ref[depth] * cot).astype(bfloat)
        mixed = None
        for j in range(depth):
            layer = history_ref[j, span, :].astype(single)
            mixed = mix_ref[j] * layer if mixed is None else mixed + mix_ref[j] * layer
            grad_ref[j, span, :] = (mix_ref[j] * cot).astype(bfloat)
            part_ref[8 * j : 8 * j + 8, :] += fold_rows(layer * cot)
        mixed_ref[span, :] = mixed


def average_history(mix, history, cot, after=()):
    depth, rows, width = history.shape
    step = 96
    waits = len(after)

    def body(*refs):
        history_body(*refs[:3], *refs[3 + waits :])

    row_block = pl.BlockSpec((step, width), lambda i: (i, 0))
    deep_block = pl.BlockSpec((depth, step, width), lambda i: (0, i, 0))
    return pl.pallas_call(
        body,
        grid=(rows // step,),
        out_shape=[
            jax.ShapeDtypeStruct(history.shape, bfloat),
            jax.ShapeDtypeStruct((rows, width), single),
            jax.ShapeDtypeStruct((rows, width), bfloat),
            jax.ShapeDtypeStruct((8 * depth, width), single),
        ],
        in_specs=[pl.BlockSpec(memory_space=pltpu.SMEM), deep_block, row_block]
        + [pl.BlockSpec(memory_space=pl.ANY)] * waits,
        out_specs=[deep_block, row_block, row_block, pl.BlockSpec((8 * depth, width), lambda i: (0, 0))],
        compiler_params=pltpu.CompilerParams(vmem_limit_bytes=16 * MIB),
        cost_estimate=pl.CostEstimate(flops=0, bytes_accessed=0, transcendentals=0),
    )(mix, history, cot, *after)


def combine_body(mix_ref, mixed_ref, mid_ref, keep_ref, recv_ref, cot_ref, parts_ref, out_ref, part_ref):
    depth = mix_ref.shape[0] - 1
    last = jnp.zeros((8, mid_ref.shape[1]), single)
    for span in spans(mid_ref.shape[0]):
        outputs = mid_ref[span, :] + (keep_ref[span, :] + recv_ref[span, :].astype(single))
        out_ref[span, :] = (mixed_ref[span, :] + mix_ref[depth] * outputs).astype(bfloat)
        last = last + fold_rows(outputs * cot_ref[span, :])
    for j in range(depth):
        part_ref[j : j + 1, :] = jnp.sum(parts_ref[8 * j : 8 * j + 8, :], axis=0, keepdims=True)
    part_ref[depth : depth + 1, :] = jnp.sum(last, axis=0, keepdims=True)


SQUARE = 4


def quarter(owner, mask, size):
    other = owner + (mask & 1) * (1 - 2 * (owner % 2)) + (mask & 2) * (1 - 2 * (owner // 2))
    return pl.ds(pl.multiple_of(other * size, size), size)


def part_body(owner_ref, mine_ref, come_ref, *out_refs):
    for mask, out_ref in enumerate(out_refs):
        rows = quarter(owner_ref[0], mask, out_ref.shape[0])
        out_ref[...] = (mine_ref[rows, :].astype(single) + come_ref[rows, :].astype(single)).astype(bfloat)


def sum_of(refs, rows):
    total = refs[0][rows, :].astype(single)
    for ref in refs[1:]:
        total = total + ref[rows, :].astype(single)
    return total


def four_body(*refs):
    refs[-1][...] = sum_of(refs[:-1], slice(None)).astype(bfloat)


def four_two_body(*refs):
    size = refs[-1].shape[0]
    refs[-2][...] = sum_of(refs[:-2], slice(0, size)).astype(bfloat)
    refs[-1][...] = sum_of(refs[:-2], slice(size, 2 * size)).astype(bfloat)


EXTRA = 16


def mark_body(out_ref):
    out_ref[...] = jnp.zeros_like(out_ref)


def small_body(small_ref, first_ref, out_ref):
    half = small_ref.shape[0]
    rows = first_ref.shape[0] - 2 * half
    come = first_ref[rows:, :].astype(single)
    out_ref[...] = small_ref[...] + (come[:half] + come[half:])


def four_more_body(small_ref, more_ref, *refs):
    out_ref = refs[-1]
    size = out_ref.shape[0] - EXTRA
    out_ref[:size, :] = sum_of(refs[:-1], slice(None)).astype(bfloat)
    small = small_ref[...] + more_ref[...]
    rest = jnp.zeros((EXTRA - small.shape[0], small.shape[1]), single)
    out_ref[size:, :] = jnp.concatenate([small, rest], axis=0).astype(bfloat)


def gather(owner_ref, pieces, hold):
    for mask, piece in enumerate(pieces):
        hold[quarter(owner_ref[0], mask, piece.shape[0]), :] = piece[...]


def pair_body(a_ref, a_come_ref, b_ref, b_come_ref, out_ref):
    size = a_ref.shape[0]
    out_ref[:size, :] = sum_of((a_ref, a_come_ref), slice(None)).astype(bfloat)
    out_ref[size:, :] = sum_of((b_ref, b_come_ref), slice(None)).astype(bfloat)


def whole_body(owner_ref, a_ref, b_ref, c_ref, d_ref, out_ref, hold):
    gather(owner_ref, (a_ref, b_ref, c_ref, d_ref), hold)
    out_ref[...] = hold[...].astype(single)


def more_body(owner_ref, a_ref, b_ref, c_ref, d_ref, top_ref, end_ref, up_ref, attn_ref, mlp_ref, dwa_ref, hold):
    gather(owner_ref, (a_ref, b_ref, c_ref, d_ref), hold)
    block = hold.shape[0] // SQUARE
    rows = up_ref.shape[0] // SQUARE
    small = jnp.zeros((EXTRA, hold.shape[1]), single)
    for index in range(SQUARE):
        begin = index * block
        target, place = (top_ref, index * rows) if index < SQUARE - 1 else (end_ref, 0)
        target[place : place + rows, :] = hold[begin : begin + rows, :].astype(single)
        small = small + hold[begin + rows : begin + rows + EXTRA, :].astype(single)
        up_ref[index * rows : (index + 1) * rows, :] = hold[begin + rows + EXTRA : begin + block, :].astype(single)
    attn_ref[...] = small[0]
    mlp_ref[...] = small[1]
    for index in range(dwa_ref.shape[0]):
        dwa_ref[index] = jnp.sum(small[2 + index : 3 + index])


def low_body(mine_ref, come_ref, out_ref):
    out_ref[...] = (mine_ref[...].astype(single) + come_ref[...].astype(single)).astype(bfloat)


def mark_body(out_ref):
    out_ref[...] = jnp.zeros_like(out_ref)


def small_body(small_ref, first_ref, out_ref):
    half = small_ref.shape[0]
    rows = first_ref.shape[0] - 2 * half
    come = first_ref[rows:, :].astype(single)
    out_ref[...] = small_ref[...] + (come[:half] + come[half:])


BLOCKS = tuple((begin, min(256, SEQ - begin)) for begin in range(0, SEQ, 256))


def places(core_ref, refs):
    count, size = len(refs) // 2, refs[0].shape[0]
    for index, ref in enumerate(refs):
        core = core_ref[0] if index < count else 1 - core_ref[0]
        yield ref, pl.ds(pl.multiple_of(core * HALF + index % count * size, size), size)


def allowed(size):
    key_pos = lax.broadcasted_iota(jnp.int32, (size, size), 0)
    query_pos = lax.broadcasted_iota(jnp.int32, (size, size), 1)
    return query_pos >= key_pos


def turn(rows, cosine, sine):
    half = rows.shape[0] // 2
    a, b = rows[:half], rows[half:]
    return jnp.concatenate([a * cosine - b * sine, b * cosine + a * sine], axis=0)


KEYS = 128


def fold_top(value):
    top = value[:8]
    for begin in range(8, value.shape[0], 8):
        top = jnp.maximum(top, value[begin : begin + 8])
    return top


def masked(scores, offset):
    key_pos = lax.broadcasted_iota(jnp.int32, scores.shape, 0) + offset
    query_pos = lax.broadcasted_iota(jnp.int32, scores.shape, 1)
    return jnp.where(query_pos >= key_pos, scores, -jnp.inf)


def attend_placed(core_ref, *rest):
    for ref, where in places(core_ref, rest[:4]):
        rest[11][where, :] = ref[...]
    cos_ref, sin_ref, weight_ref, rest = rest[4], rest[5], rest[6], rest[7:]
    attend(weight_ref, cos_ref, sin_ref, *rest)


def attend(weight_ref, cos_ref, sin_ref, qkv_ref, att_ref, nat_ref, log_ref, tokens, all_scores, all_weights):
    width = weight_ref.shape[0] // 3
    projected = mul(weight_ref[...], tokens[...], 1, 1)
    cosine, sine = cos_ref[...], sin_ref[...]
    for part in range(3):
        for head in range(width // DH):
            begin = part * width + head * DH
            rows = projected[begin : begin + DH]
            if part < 2:
                rows = turn(rows, cosine, sine)
            if part == 0:
                rows = rows * DH ** (-0.5)
            qkv_ref[begin : begin + DH, :] = rows.astype(bfloat)
    log_ref[...] = jnp.zeros_like(log_ref)
    heads = range(width // DH)
    keys = [qkv_ref[width + head * DH : width + head * DH + DH, :].T for head in heads]
    for begin, size in BLOCKS:
        end = begin + size
        tops = [None for _ in heads]
        for row in range(0, end, KEYS):
            for head in heads:
                tile = mul(keys[head][row : row + KEYS], qkv_ref[head * DH : head * DH + DH, begin:end])
                if row >= begin:
                    tile = masked(tile, row - begin)
                all_scores[head, row : row + KEYS, :size] = tile
                top = fold_top(tile)
                tops[head] = top if row == 0 else jnp.maximum(tops[head], top)
        tops = [jnp.max(top, axis=0, keepdims=True) for top in tops]
        totals = [jnp.zeros((8, size), single) for _ in heads]
        for row in range(0, end, KEYS):
            for head in heads:
                tile = jnp.exp(all_scores[head, row : row + KEYS, :size] - tops[head])
                totals[head] = totals[head] + fold_rows(tile)
                all_weights[head, row : row + KEYS, :size] = tile.astype(bfloat)
        for head in heads:
            base = head * DH
            total = jnp.sum(totals[head], axis=0, keepdims=True)
            value = qkv_ref[2 * width + base : 2 * width + base + DH, :end]
            mixed = mul(value, all_weights[head, :end, :size]) / total
            att_ref[base : base + DH, begin:end] = mixed.astype(bfloat)
            log_ref[head : head + 1, begin:end] = tops[head] + jnp.log(total)
    nat_ref[...] = att_ref[...].T


def branch_body(core_ref, att_a_ref, att_b_ref, out_a_ref, out_b_ref, pass_ref, keep_ref, *rest):
    send_refs, pass_out = rest[:PARTS], rest[PARTS]
    pass_out[...] = pass_ref[...]
    low = pl.multiple_of(core_ref[0] * HALF, HALF)
    rows = HALF // PARTS
    for index in range(PARTS):
        high = pl.multiple_of((1 - core_ref[0]) * HALF + index * rows, rows)
        send = mul(att_a_ref[pl.ds(high, rows), :], out_a_ref[...])
        send_refs[index][...] = (send + mul(att_b_ref[pl.ds(high, rows), :], out_b_ref[...])).astype(bfloat)
    keep = mul(att_a_ref[pl.ds(low, HALF), :], out_a_ref[...])
    keep_ref[...] = keep + mul(att_b_ref[pl.ds(low, HALF), :], out_b_ref[...])


def attend_back(
    core_ref, log_ref, cos_ref, sin_ref, gain_ref, *rest
):
    before_refs, rest = rest[:-25], rest[-25:]
    grad_refs, x_refs = rest[:2], rest[2:6]
    weight_ref, qkv_weight_ref, qkv_ref, att_ref, small_ref, out_ref, turned_ref = rest[6:13]
    grads, tokens, weight, qkv_weight, qkv, att, turned, result, all_probs, all_scores, hold, marks = rest[13:]
    go = Mover(marks)
    first = go(
        (weight_ref, weight),
        *[(ref, grads.at[where, :]) for ref, where in places(core_ref, grad_refs)],
        (att_ref, att),
        (qkv_ref, qkv),
    )
    later = go(
        *[(ref, tokens.at[where, :]) for ref, where in places(core_ref, x_refs)],
        (qkv_weight_ref, qkv_weight),
    )
    wait(first)
    width = att.shape[0]
    grad_att = mul(weight[...], grads[...], 1, 1).astype(bfloat)
    result[3 * width :, :] = mul(att[...], grads[...]).astype(result.dtype)
    cosine, sine = cos_ref[...], sin_ref[...]
    heads = range(width // DH)
    spans_of = [slice(head * DH, head * DH + DH) for head in heads]
    query = [qkv[span, :] for span in spans_of]
    key = [qkv[width + span.start : width + span.stop, :] for span in spans_of]
    above = [grad_att[span] for span in spans_of]
    centre = [
        jnp.sum(above[head].astype(single) * att[span, :].astype(single), axis=0, keepdims=True)
        for head, span in enumerate(spans_of)
    ]
    keys = [value.T for value in key]
    values = [qkv[2 * width + span.start : 2 * width + span.stop, :].T for span in spans_of]
    queries = [value.T for value in query]
    aboves = [value.T for value in above]
    grad_query = [[] for _ in heads]
    for begin, size in BLOCKS:
        end = begin + size
        for row in range(0, end, KEYS):
            span = slice(row, row + KEYS)
            for head in heads:
                tile = mul(keys[head][span], query[head][:, begin:end])
                if row >= begin:
                    tile = masked(tile, row - begin)
                tile = jnp.exp(tile - log_ref[head : head + 1, begin:end])
                grad = mul(values[head][span], above[head][:, begin:end]) - centre[head][:, begin:end]
                all_probs[head, span, begin:end] = tile.astype(bfloat)
                all_scores[head, span, begin:end] = (tile * grad).astype(bfloat)
        for head in heads:
            grad_query[head].append(mul(key[head][:, :end], all_scores[head, :end, begin:end]))
    grad_key = [[] for _ in heads]
    grad_value = [[] for _ in heads]
    for begin, size in BLOCKS:
        span = slice(begin, begin + size)
        for head in heads:
            grad_key[head].append(mul(all_scores[head, span, begin:], queries[head][begin:]))
            grad_value[head].append(mul(all_probs[head, span, begin:], aboves[head][begin:]))
    for head, span in enumerate(spans_of):
        grad = jnp.concatenate(grad_query[head], axis=1) * DH ** (-0.5)
        turned[span, :] = turn(grad, cosine, -sine).astype(bfloat)
        grad = jnp.concatenate(grad_key[head], axis=0).T
        turned[width + span.start : width + span.stop, :] = turn(grad, cosine, -sine).astype(bfloat)
        grad = jnp.concatenate(grad_value[head], axis=0).T
        turned[2 * width + span.start : 2 * width + span.stop, :] = grad.astype(bfloat)
    stores = go((turned, turned_ref))
    wait(later)
    hold[...] = mul(turned[...], tokens[...])
    result[: 3 * width, :] = hold[...].astype(result.dtype)
    stores += go((result, out_ref))
    part = jnp.zeros((8, hold.shape[1]), single)
    for span in spans(hold.shape[0]):
        part = part + fold_rows(hold[span, :] * qkv_weight[span, :].astype(single))
    gain = jnp.sum(part, axis=0, keepdims=True) / gain_ref[...].reshape(1, -1)
    if before_refs:
        gain_part_ref, mlp_part_ref, dwa_part_ref = before_refs
        small_ref[:1, :] = gain + gain_part_ref[...]
        small_ref[1:2, :] = mlp_part_ref[...]
        small_ref[2:, :] = dwa_part_ref[...]
    else:
        small_ref[...] = gain
    wait(stores)


def first_grad_body(
    core_ref, small_ref, turned_a_ref, turned_b_ref, weight_a_ref, weight_b_ref, send_ref, keep_ref,
    turned_a, turned_b, weight_a, weight_b, whole, marks,
):
    low = pl.multiple_of(core_ref[0] * HALF, HALF)
    high = pl.multiple_of((1 - core_ref[0]) * HALF, HALF)
    go = Mover(marks)
    wait(go((turned_a_ref, turned_a), (weight_a_ref, weight_a), (turned_b_ref, turned_b), (weight_b_ref, weight_b)))
    whole[...] = mul(turned_a[...], weight_a[...], 0, 0) + mul(turned_b[...], weight_b[...], 0, 0)
    stores = go((whole.at[pl.ds(low, HALF), :], keep_ref))
    send_ref[:HALF, :] = whole[pl.ds(high, HALF), :].astype(bfloat)
    small = small_ref[...]
    high_part = small.astype(bfloat)
    low_part = (small - high_part.astype(single)).astype(bfloat)
    send_ref[HALF:, :] = jnp.concatenate([high_part, low_part], axis=0)
    wait(stores)


CURVE = float(np.sqrt(2.0 / np.pi))
STEP = 256


def mlp_body(second, *refs):
    if second:
        owner_ref, refs = refs[0], refs[1:]
    x_refs, refs = refs[: 2 * PARTS], refs[2 * PARTS :]
    g_own_ref, g_peer_ref, refs = refs[0], refs[1], refs[2:]
    if second:
        up_ref, down_refs, refs = refs[0], refs[1 : 1 + SQUARE], refs[1 + SQUARE :]
        before_refs, up_mine_ref = refs[:4], refs[4]
        down_grad_ref, part_refs = refs[9], refs[10:14]
        refs = refs[5:9] + refs[14:]
    else:
        up_ref, down_ref = refs[:2]
        down_grad_ref, up_grad_ref = refs[6:8]
        refs = refs[2:6] + refs[8:]
    send_norm_ref, keep_norm_ref, send_out_ref, keep_out_ref = refs[:4]
    x_all, g_all, up, down, active, grad_hidden, x_turned = refs[4:11]
    send_norm, keep_norm, send_out, keep_out, down_grad, up_grad, marks = refs[11:18]
    rows, size = x_all.shape[0] // 2, x_all.shape[0] // (2 * PARTS)
    units = down.shape[0]
    go = Mover(marks)
    x_loads = go(*[(x_refs[index], x_all.at[pl.ds(index * size, size), :]) for index in range(2 * PARTS)])
    if second:
        loads = go((up_ref, up), *joined(owner_ref[0], down_refs, down))
    else:
        loads = go((up_ref, up), (down_ref, down))
    loads += go((g_own_ref, g_all.at[pl.ds(0, rows), :]), (g_peer_ref, g_all.at[pl.ds(rows, rows), :]))
    more, mine, stores = [], [], []
    if second:
        (up_mine,) = refs[18:]
        more = go(*zip(before_refs, (send_norm, keep_norm, send_out, keep_out)))
        mine = go((up_mine_ref, up_mine))
    wait(x_loads)
    x_turned[...] = x_all[...].T
    wait(loads)
    for begin in range(0, units, STEP):
        columns = slice(begin, begin + STEP)
        for top in range(0, 2 * rows, rows):
            span = slice(top, top + rows)
            v = mul(x_all[span, :], up[:, columns])
            grad = mul(g_all[span, :], down[columns, :], 1, 1)
            square = v * v
            half = 0.5 + 0.5 * jnp.tanh(v * (CURVE + (CURVE * 0.044715) * square))
            act = v * half
            slope = half + act * (1.0 - half) * (2.0 * CURVE + (6.0 * CURVE * 0.044715) * square)
            active[span, columns] = act.astype(bfloat)
            grad_hidden[span, columns] = (grad * slope).astype(bfloat)

    def put(target, value):
        target[...] = (value + target[...].astype(single) if second else value).astype(target.dtype)

    wait(more)
    put(keep_norm, mul(grad_hidden[:rows, :], up[...], 1, 1))
    put(send_norm, mul(grad_hidden[rows:, :], up[...], 1, 1))
    stores += go((keep_norm, keep_norm_ref), (send_norm, send_norm_ref))
    down_grad[...] = mul(active[...], g_all[...], 0, 0).astype(down_grad.dtype)
    stores += go((down_grad, down_grad_ref))
    up_grad[...] = mul(x_turned[...], grad_hidden[...]).astype(bfloat)
    if second:
        wait(mine)
        part = up_grad.shape[0] // SQUARE
        for mask, part_ref in enumerate(part_refs):
            rows_of = quarter(owner_ref[0], mask, part)
            stores += go(
                (up_mine.at[rows_of, :], part_ref.at[pl.ds(0, part), :]),
                (up_grad.at[rows_of, :], part_ref.at[pl.ds(part, part), :]),
            )
    else:
        stores += go((up_grad, up_grad_ref))
    put(keep_out, mul(active[:rows, :], down[...]))
    stores += go((keep_out, keep_out_ref))
    put(send_out, mul(active[rows:, :], down[...]))
    wait(stores + go((send_out, send_out_ref)))


def mlp(x_own, x_peer, g_own, g_peer, up, down, upper=(), before=(), flops=0):
    rows, width = g_own.shape
    units = sum(piece.shape[0] for piece in down)
    tall = (2 * rows, width)
    pair = [((rows, width), bfloat), ((rows, width), single)] * 2
    outs = pair + [((units, width), bfloat)]
    outs += [((2 * width // SQUARE, units), bfloat)] * SQUARE if before else [((width, units), bfloat)]
    scratch = [
        pltpu.VMEM(tall, bfloat),
        pltpu.VMEM(tall, bfloat),
        pltpu.VMEM((width, units), bfloat),
        pltpu.VMEM((units, width), bfloat),
        pltpu.VMEM((2 * rows, units), bfloat),
        pltpu.VMEM((2 * rows, units), bfloat),
        pltpu.VMEM((width, 2 * rows), bfloat),
    ]
    scratch += [pltpu.VMEM(shape, kind) for shape, kind in pair]
    scratch += [
        pltpu.VMEM((units, width), bfloat), pltpu.VMEM((width, units), bfloat), pltpu.SemaphoreType.DMA((32,)),
    ]
    if before:
        scratch.append(pltpu.VMEM((width, units), bfloat))
    operands = (*upper, *x_own, *x_peer, g_own, g_peer, *up, *down, *before)
    return call(
        functools.partial(mlp_body, bool(before)),
        outs,
        operands,
        scratch,
        len(upper),
        vmem=60,
        flops=flops,
        far=len(operands) - len(upper),
        far_outs=len(outs),
    )


def shards(
    inputs,
    history,
    cotangent,
    qkv_weight,
    out_weight,
    up_weight,
    down_weight,
    gain_attn,
    gain_mlp,
    dwa_weights,
):
    rows, width = inputs.shape
    members = lax.axis_size("mp")
    copies = lax.axis_size("dp")
    bits = copies.bit_length() - 1
    core = lax.rem(lax.axis_index("mp"), 2).astype(jnp.int32).reshape(1)
    copy_index = lax.axis_index("dp").astype(jnp.int32).reshape(1)
    core_pairs = [(i, i ^ 1) for i in range(members)]
    chip_pairs = [(i, i ^ 2) for i in range(members)]
    depth = history.shape[0]
    part = out_weight.shape[0]

    def other_core(value):
        return lax.ppermute(value, "mp", core_pairs)

    def other_chip(value):
        return lax.ppermute(value, "mp", chip_pairs)

    def other_copy(value, mask):
        return lax.ppermute(value, "dp", [(i, i ^ mask) for i in range(copies)])

    owner = copy_index & (SQUARE - 1)
    cosine, sine = (jnp.asarray(table) for table in tables())

    qkv_own = qkv_weight.transpose(1, 2, 0).reshape(3 * part, width)
    fourth = (width // SQUARE, width)
    square = (width, width)
    masks = range(1, SQUARE)
    marks = pltpu.SemaphoreType.DMA((16,))
    (down_quarter,) = call(
        split_body,
        [(fourth, bfloat)],
        (owner, down_weight),
        [pltpu.VMEM(fourth, bfloat), marks],
        1,
        vmem=60,
        far=1,
        far_outs=1,
    )
    qkv_peer, out_peer = other_chip(qkv_own), other_chip(out_weight)
    down_come, up_peer = other_chip(down_quarter), other_chip(up_weight)

    full = (rows, width)
    x_own = call(norm_body, [((rows // 2, width), bfloat)] * 2, (inputs, gain_attn), after=(down_quarter,))
    x_peer = [other_core(value) for value in x_own]
    tall = (SEQ, width)
    tokens = pltpu.VMEM(tall, bfloat)
    first_outs = [
        ((3 * part, SEQ), bfloat), ((part, SEQ), bfloat), ((SEQ, part), bfloat), ((8, SEQ), single),
    ]
    heads = part // DH
    tiles = [tokens, pltpu.VMEM((heads, SEQ, 256), single), pltpu.VMEM((heads, SEQ, 256), bfloat)]
    qkv_a, att_a, nat_a, log_a = call(
        attend_placed, first_outs, (core, *x_own, *x_peer, cosine, sine, qkv_own), tiles, 1, vmem=32
    )
    history_grad, mixed, g_own, history_parts = average_history(dwa_weights, history, cotangent, (log_a,))
    g_peer = other_core(g_own)
    qkv_b, att_b, nat_b, log_b = call(
        attend_placed,
        first_outs,
        (core, *x_own, *x_peer, cosine, sine, qkv_peer),
        tiles,
        1,
        (history_parts,),
        32,
        MUCH,
    )
    third = (rows // PARTS, width)
    keep, *send, down_copy = call(
        branch_body,
        [(full, single)] + [(third, bfloat)] * PARTS + [(fourth, bfloat)],
        (core, nat_a, nat_b, out_weight, out_peer, down_come),
        (),
        1,
        (g_peer,),
    )
    down_pieces = [down_come] + [other_copy(down_copy, mask) for mask in masks]
    recv = [other_core(value) for value in send]
    middle, *y_own = call(
        middle_body, [(full, single)] + [(third, bfloat)] * PARTS, (inputs, keep, gain_mlp, *recv)
    )
    y_peer = [other_core(value) for value in y_own]

    first = mlp(y_own, y_peer, g_own, g_peer, (up_weight,), (down_weight,))
    down_mine, up_mine = first[4:]
    second = mlp(
        y_own, y_peer, g_own, g_peer, (up_peer,), down_pieces, (owner,), (*first[:4], up_mine)
    )
    send_norm, keep_norm, send_out, keep_out, down_theirs = second[:5]
    token = [send_norm]

    def step(body, outs, operands, scratch=(), scalars=0, vmem=16, flops=MUCH, far=0, far_outs=0):
        results = call(body, outs, operands, scratch, scalars, tuple(token), vmem, flops, far, far_outs)
        token[0] = results[0]
        return results

    down_come = other_chip(down_theirs)
    up_parts = [second[5]] + [other_copy(value, mask) for mask, value in zip(masks, second[6:])]
    out_come = other_core(send_out)
    grad_middle, gb_own, gain_mlp_part = step(
        middle_back_body,
        [(full, single), (full, bfloat), ((1, width), single)],
        (dwa_weights, middle, keep_norm, other_core(send_norm), cotangent, gain_mlp),
        scalars=1,
        flops=0,
    )
    gb_peer = other_core(gb_own)
    combined, dwa_part = step(
        combine_body,
        [(full, bfloat), ((depth + 1, width), single)],
        (dwa_weights, mixed, middle, keep_out, out_come, cotangent, history_parts),
        scalars=1,
        flops=0,
    )

    def back(weight, qkv_weight, qkv, att, log, flops, before=()):
        return step(
            attend_back,
            [
                ((depth + 3 if before else 1, width), single),
                ((4 * part, width), bfloat),
                ((3 * part, SEQ), bfloat),
            ],
            (
                core, log, cosine, sine, gain_attn, *before, gb_own, gb_peer, *x_own, *x_peer, weight, qkv_weight, qkv,
                att,
            ),
            [
                pltpu.VMEM(tall, bfloat),
                pltpu.VMEM(tall, bfloat),
                pltpu.VMEM((part, width), bfloat),
                pltpu.VMEM((3 * part, width), bfloat),
                pltpu.VMEM((3 * part, SEQ), bfloat),
                pltpu.VMEM((part, SEQ), bfloat),
                pltpu.VMEM((3 * part, SEQ), bfloat),
                pltpu.VMEM((4 * part, width), bfloat),
                pltpu.VMEM((heads, SEQ, SEQ), bfloat),
                pltpu.VMEM((heads, SEQ, SEQ), bfloat),
                pltpu.VMEM((3 * part, width), single),
                marks,
            ],
            1,
            60,
            flops,
            10,
            2,
        )

    gain_part, att_theirs, turned_b = back(out_peer, qkv_peer, qkv_b, att_b, log_b, 0)
    att_come = other_chip(att_theirs)
    def spread(mine, come, flops=MUCH):
        own, *sent = step(part_body, [(fourth, bfloat)] * SQUARE, (owner, mine, come), scalars=1, flops=flops)
        return [own] + [other_copy(value, mask) for mask, value in zip(masks, sent)]

    down_parts = spread(down_mine, down_come, 0)
    up, sent = step(four_two_body, [(fourth, bfloat)] * 2, up_parts, flops=0)
    up_come = other_chip(sent)
    part_sums, att_mine, turned_a = back(
        out_weight, qkv_own, qkv_a, att_a, log_a, MUCH, (gain_part, gain_mlp_part, dwa_part)
    )

    def exchange(value):
        for bit in range(2, bits):
            come = other_copy(value, 1 << bit)
            if bit < bits - 1:
                (value,) = step(low_body, [(value.shape, bfloat)], (value, come))
        return value, come

    def finish(value, come):
        (value,) = step(low_body, [(value.shape, bfloat)], (value, come), flops=COST)
        return [value] + [other_copy(value, mask) for mask in masks]

    (down,) = step(four_body, [(fourth, bfloat)], down_parts, flops=COST)
    down = exchange(down)
    att_parts = spread(att_mine, att_come, COST)
    (up,) = step(low_body, [(fourth, bfloat)], (up, up_come), flops=COST)
    up = exchange(up)
    send_first, keep_first = step(
        first_grad_body,
        [((rows + EXTRA, width), bfloat), (full, single)],
        (core, part_sums, turned_a, turned_b, qkv_own, qkv_peer),
        [pltpu.VMEM((3 * part, SEQ), bfloat)] * 2
        + [pltpu.VMEM((3 * part, width), bfloat)] * 2
        + [pltpu.VMEM(tall, single), marks],
        1,
        60,
        COST,
        4,
        1,
    )
    first_come = other_core(send_first)
    token.append(down[1])
    step(mark_body, [((8, 128), single)], (), flops=COST)
    del token[1:]
    (part_sums,) = step(small_body, [(part_sums.shape, single)], (part_sums, first_come), flops=COST)
    more_sums = other_chip(part_sums)
    (input_grad,) = step(
        first_back_body,
        [(full, bfloat)],
        (inputs, keep_first, first_come, grad_middle, gain_attn),
        vmem=60,
        flops=COST,
    )
    block = (width // SQUARE + EXTRA, width)
    (att,) = step(four_more_body, [(block, bfloat)], (part_sums, more_sums, *att_parts), flops=COST)
    att = exchange(att)
    down = finish(*down)
    token += down[1:]
    pair = (block[0] + fourth[0], width)
    (both,) = step(pair_body, [(pair, bfloat)], (*att, *up), flops=COST)
    del token[1:]
    both = [both] + [other_copy(both, mask) for mask in masks]
    (down_grad,) = step(
        whole_body, [(square, single)], (owner, *down), [pltpu.VMEM(square, bfloat)], 1, flops=COST
    )
    qkv_grad, out_grad, up_grad, gain_attn_grad, gain_mlp_grad, dwa_grad = step(
        more_body,
        [
            ((3 * part, width), single),
            ((part, width), single),
            (square, single),
            ((width,), single),
            ((width,), single),
            ((depth + 1,), single, "scalars"),
        ],
        (owner, *both),
        [pltpu.VMEM((SQUARE * pair[0], width), bfloat)],
        1,
        flops=COST,
    )

    return (
        combined,
        input_grad,
        history_grad,
        qkv_grad.reshape(3, part, width).transpose(2, 0, 1),
        out_grad,
        up_grad,
        down_grad,
        gain_attn_grad,
        gain_mlp_grad,
        dwa_grad,
    )


def solution(mesh):
    placed = (
        P(("dp", "mp"), None),
        P(None, ("dp", "mp"), None),
        P(("dp", "mp"), None),
        P(None, None, "mp"),
        P("mp", None),
        P(None, "mp"),
        P("mp", None),
        P(),
        P(),
        P(),
    )
    return jax.shard_map(
        shards,
        mesh=mesh,
        in_specs=placed,
        out_specs=(
            P(("dp", "mp"), None),
            P(("dp", "mp"), None),
            P(None, ("dp", "mp"), None),
            P(None, None, "mp"),
            P("mp", None),
            P(None, "mp"),
            P("mp", None),
            P(),
            P(),
            P(),
        ),
        check_vma=False,
    )
```

```python
import functools

import jax
import jax.numpy as jnp
import numpy as np
from jax import lax
from jax.experimental import pallas as pl
from jax.experimental.pallas import tpu as pltpu
from jax.sharding import PartitionSpec as P

DH = 64
SEQ = 1152
HALF = SEQ // 2
EPS = 1e-05
bfloat = jnp.bfloat16
single = jnp.float32
MIB = 1 << 20
MUCH = 10**11
COST = 10**10


def tables():
    half_width = DH // 2
    places = np.arange(SEQ, dtype=np.float32)
    frequency = np.float32(10000.0) ** (-np.arange(half_width, dtype=np.float32) * np.float32(2.0 / DH))
    angles = frequency[:, None] * places[None, :]
    return (np.cos(angles).astype(np.float32), np.sin(angles).astype(np.float32))


def mul(a, b, ca=1, cb=0):
    return lax.dot_general(a, b, (((ca,), (cb,)), ((), ())), preferred_element_type=single)


def call(kernel, outs, operands, scratch=(), scalars=0, after=(), vmem=16, flops=0, far=0, far_outs=0):
    count, waits = len(operands), len(after)

    def body(*refs):
        kernel(*refs[:count], *refs[count + waits :])

    small = pl.BlockSpec(memory_space=pltpu.SMEM)
    whole = pl.BlockSpec(memory_space=pltpu.VMEM)
    apart = pl.BlockSpec(memory_space=pltpu.HBM)
    loose = pl.BlockSpec(memory_space=pl.ANY)
    inner = len(outs) - far_outs
    return pl.pallas_call(
        body,
        out_shape=[jax.ShapeDtypeStruct(out[0], out[1]) for out in outs],
        in_specs=[small] * scalars + [whole] * (count - scalars - far) + [apart] * far + [loose] * waits,
        out_specs=[small if len(out) > 2 else whole for out in outs[:inner]] + [apart] * far_outs,
        scratch_shapes=list(scratch),
        compiler_params=pltpu.CompilerParams(vmem_limit_bytes=vmem * MIB),
        cost_estimate=pl.CostEstimate(flops=flops, bytes_accessed=0, transcendentals=0),
    )(*operands, *after)


class Mover:
    def __init__(self, marks):
        self.marks = marks
        self.used = 0

    def __call__(self, *pairs):
        copies = []
        for source, target in pairs:
            copies.append(pltpu.make_async_copy(source, target, self.marks.at[self.used]))
            self.used += 1
        for copy in copies:
            copy.start()
        return copies


def wait(copies):
    for copy in copies:
        copy.wait()


ROWS = 64
PARTS = 1


def spans(rows, step=ROWS):
    return [slice(begin, begin + step) for begin in range(0, rows, step)]


def normal_of(x):
    centre = x - jnp.mean(x, axis=-1, keepdims=True)
    spread = jnp.mean(centre * centre, axis=-1, keepdims=True)
    scale = lax.rsqrt(spread + EPS)
    return centre * scale, scale


def split_body(owner_ref, in_ref, out_ref, hold, marks):
    go = Mover(marks)
    wait(go((in_ref.at[quarter(owner_ref[0], 0, hold.shape[0]), :], hold)))
    wait(go((hold, out_ref)))


def joined(owner, refs, target):
    size = refs[0].shape[0]
    return [(ref, target.at[quarter(owner, mask, size), :]) for mask, ref in enumerate(refs)]


def norm_body(x_ref, gain_ref, *out_refs):
    gain = gain_ref[...].reshape(1, -1)
    for index, out_ref in enumerate(out_refs):
        rows = out_ref.shape[0]
        for span in spans(rows, rows // 6):
            here = slice(index * rows + span.start, index * rows + span.stop)
            normal, _ = normal_of(x_ref[here, :].astype(single))
            out_ref[span, :] = (normal * gain).astype(bfloat)


def middle_body(x_ref, keep_ref, gain_ref, *rest):
    recv_refs, mid_ref, out_refs = rest[:PARTS], rest[PARTS], rest[PARTS + 1 :]
    gain = gain_ref[...].reshape(1, -1)
    rows = x_ref.shape[0] // PARTS
    for index in range(PARTS):
        for span in spans(rows):
            here = slice(index * rows + span.start, index * rows + span.stop)
            recv = recv_refs[index][span, :].astype(single)
            x = x_ref[here, :].astype(single) + (keep_ref[here, :] + recv)
            mid_ref[here, :] = x
            normal, _ = normal_of(x)
            out_refs[index][span, :] = (normal * gain).astype(bfloat)


def norm_back(x, grad, gain):
    normal, scale = normal_of(x)
    lifted = grad * gain
    back = scale * (
        lifted
        - jnp.mean(lifted, axis=-1, keepdims=True)
        - normal * jnp.mean(lifted * normal, axis=-1, keepdims=True)
    )
    return back, normal


def fold_rows(value):
    total = value[:8]
    for begin in range(8, value.shape[0], 8):
        total = total + value[begin : begin + 8]
    return total


def middle_back_body(mix_ref, x_ref, keep_ref, recv_ref, cot_ref, gain_ref, mid_ref, low_ref, part_ref):
    gain = gain_ref[...].reshape(1, -1)
    part = jnp.zeros((8, x_ref.shape[1]), single)
    for span in spans(x_ref.shape[0]):
        grad = keep_ref[span, :] + recv_ref[span, :].astype(single)
        back, normal = norm_back(x_ref[span, :], grad, gain)
        total = mix_ref[mix_ref.shape[0] - 1] * cot_ref[span, :] + back
        mid_ref[span, :] = total
        low_ref[span, :] = total.astype(bfloat)
        part = part + fold_rows(grad * normal)
    part_ref[...] = jnp.sum(part, axis=0, keepdims=True)


def first_back_body(x_ref, keep_ref, recv_ref, mid_ref, gain_ref, out_ref):
    gain = gain_ref[...].reshape(1, -1)
    for span in spans(x_ref.shape[0]):
        grad = keep_ref[span, :] + recv_ref[span, :].astype(single)
        back, _ = norm_back(x_ref[span, :].astype(single), grad, gain)
        out_ref[span, :] = (mid_ref[span, :] + back).astype(bfloat)


def history_body(mix_ref, history_ref, cot_ref, grad_ref, mixed_ref, low_ref, part_ref):
    depth = history_ref.shape[0]

    @pl.when(pl.program_id(0) == 0)
    def _():
        part_ref[...] = jnp.zeros_like(part_ref)

    for span in spans(cot_ref.shape[0], 32):
        cot = cot_ref[span, :]
        low_ref[span, :] = (mix_ref[depth] * cot).astype(bfloat)
        mixed = None
        for j in range(depth):
            layer = history_ref[j, span, :].astype(single)
            mixed = mix_ref[j] * layer if mixed is None else mixed + mix_ref[j] * layer
            grad_ref[j, span, :] = (mix_ref[j] * cot).astype(bfloat)
            part_ref[8 * j : 8 * j + 8, :] += fold_rows(layer * cot)
        mixed_ref[span, :] = mixed


def average_history(mix, history, cot, after=()):
    depth, rows, width = history.shape
    step = 96
    waits = len(after)

    def body(*refs):
        history_body(*refs[:3], *refs[3 + waits :])

    row_block = pl.BlockSpec((step, width), lambda i: (i, 0))
    deep_block = pl.BlockSpec((depth, step, width), lambda i: (0, i, 0))
    return pl.pallas_call(
        body,
        grid=(rows // step,),
        out_shape=[
            jax.ShapeDtypeStruct(history.shape, bfloat),
            jax.ShapeDtypeStruct((rows, width), single),
            jax.ShapeDtypeStruct((rows, width), bfloat),
            jax.ShapeDtypeStruct((8 * depth, width), single),
        ],
        in_specs=[pl.BlockSpec(memory_space=pltpu.SMEM), deep_block, row_block]
        + [pl.BlockSpec(memory_space=pl.ANY)] * waits,
        out_specs=[deep_block, row_block, row_block, pl.BlockSpec((8 * depth, width), lambda i: (0, 0))],
        compiler_params=pltpu.CompilerParams(vmem_limit_bytes=16 * MIB),
        cost_estimate=pl.CostEstimate(flops=0, bytes_accessed=0, transcendentals=0),
    )(mix, history, cot, *after)


def combine_body(mix_ref, mixed_ref, mid_ref, keep_ref, recv_ref, cot_ref, parts_ref, out_ref, part_ref):
    depth = mix_ref.shape[0] - 1
    last = jnp.zeros((8, mid_ref.shape[1]), single)
    for span in spans(mid_ref.shape[0]):
        outputs = mid_ref[span, :] + (keep_ref[span, :] + recv_ref[span, :].astype(single))
        out_ref[span, :] = (mixed_ref[span, :] + mix_ref[depth] * outputs).astype(bfloat)
        last = last + fold_rows(outputs * cot_ref[span, :])
    for j in range(depth):
        part_ref[j : j + 1, :] = jnp.sum(parts_ref[8 * j : 8 * j + 8, :], axis=0, keepdims=True)
    part_ref[depth : depth + 1, :] = jnp.sum(last, axis=0, keepdims=True)


SQUARE = 4


def quarter(owner, mask, size):
    other = owner + (mask & 1) * (1 - 2 * (owner % 2)) + (mask & 2) * (1 - 2 * (owner // 2))
    return pl.ds(pl.multiple_of(other * size, size), size)


def part_body(owner_ref, mine_ref, come_ref, *out_refs):
    for mask, out_ref in enumerate(out_refs):
        rows = quarter(owner_ref[0], mask, out_ref.shape[0])
        out_ref[...] = (mine_ref[rows, :].astype(single) + come_ref[rows, :].astype(single)).astype(bfloat)


def sum_of(refs, rows):
    total = refs[0][rows, :].astype(single)
    for ref in refs[1:]:
        total = total + ref[rows, :].astype(single)
    return total


def four_body(*refs):
    refs[-1][...] = sum_of(refs[:-1], slice(None)).astype(bfloat)


def four_two_body(*refs):
    size = refs[-1].shape[0]
    refs[-2][...] = sum_of(refs[:-2], slice(0, size)).astype(bfloat)
    refs[-1][...] = sum_of(refs[:-2], slice(size, 2 * size)).astype(bfloat)


EXTRA = 16


def mark_body(out_ref):
    out_ref[...] = jnp.zeros_like(out_ref)


def small_body(small_ref, first_ref, out_ref):
    half = small_ref.shape[0]
    rows = first_ref.shape[0] - 2 * half
    come = first_ref[rows:, :].astype(single)
    out_ref[...] = small_ref[...] + (come[:half] + come[half:])


def four_more_body(small_ref, more_ref, *refs):
    out_ref = refs[-1]
    size = out_ref.shape[0] - EXTRA
    out_ref[:size, :] = sum_of(refs[:-1], slice(None)).astype(bfloat)
    small = small_ref[...] + more_ref[...]
    rest = jnp.zeros((EXTRA - small.shape[0], small.shape[1]), single)
    out_ref[size:, :] = jnp.concatenate([small, rest], axis=0).astype(bfloat)


def gather(owner_ref, pieces, hold):
    for mask, piece in enumerate(pieces):
        hold[quarter(owner_ref[0], mask, piece.shape[0]), :] = piece[...]


def pair_body(a_ref, a_come_ref, b_ref, b_come_ref, out_ref):
    size = a_ref.shape[0]
    out_ref[:size, :] = sum_of((a_ref, a_come_ref), slice(None)).astype(bfloat)
    out_ref[size:, :] = sum_of((b_ref, b_come_ref), slice(None)).astype(bfloat)


def whole_body(owner_ref, a_ref, b_ref, c_ref, d_ref, out_ref, hold):
    gather(owner_ref, (a_ref, b_ref, c_ref, d_ref), hold)
    out_ref[...] = hold[...].astype(single)


def more_body(owner_ref, a_ref, b_ref, c_ref, d_ref, top_ref, end_ref, up_ref, attn_ref, mlp_ref, dwa_ref, hold):
    gather(owner_ref, (a_ref, b_ref, c_ref, d_ref), hold)
    block = hold.shape[0] // SQUARE
    rows = up_ref.shape[0] // SQUARE
    small = jnp.zeros((EXTRA, hold.shape[1]), single)
    for index in range(SQUARE):
        begin = index * block
        target, place = (top_ref, index * rows) if index < SQUARE - 1 else (end_ref, 0)
        target[place : place + rows, :] = hold[begin : begin + rows, :].astype(single)
        small = small + hold[begin + rows : begin + rows + EXTRA, :].astype(single)
        up_ref[index * rows : (index + 1) * rows, :] = hold[begin + rows + EXTRA : begin + block, :].astype(single)
    attn_ref[...] = small[0]
    mlp_ref[...] = small[1]
    for index in range(dwa_ref.shape[0]):
        dwa_ref[index] = jnp.sum(small[2 + index : 3 + index])


def low_body(mine_ref, come_ref, out_ref):
    out_ref[...] = (mine_ref[...].astype(single) + come_ref[...].astype(single)).astype(bfloat)


def mark_body(out_ref):
    out_ref[...] = jnp.zeros_like(out_ref)


def small_body(small_ref, first_ref, out_ref):
    half = small_ref.shape[0]
    rows = first_ref.shape[0] - 2 * half
    come = first_ref[rows:, :].astype(single)
    out_ref[...] = small_ref[...] + (come[:half] + come[half:])


BLOCKS = tuple((begin, min(256, SEQ - begin)) for begin in range(0, SEQ, 256))


def places(core_ref, refs):
    count, size = len(refs) // 2, refs[0].shape[0]
    for index, ref in enumerate(refs):
        core = core_ref[0] if index < count else 1 - core_ref[0]
        yield ref, pl.ds(pl.multiple_of(core * HALF + index % count * size, size), size)


def allowed(size):
    key_pos = lax.broadcasted_iota(jnp.int32, (size, size), 0)
    query_pos = lax.broadcasted_iota(jnp.int32, (size, size), 1)
    return query_pos >= key_pos


def turn(rows, cosine, sine):
    half = rows.shape[0] // 2
    a, b = rows[:half], rows[half:]
    return jnp.concatenate([a * cosine - b * sine, b * cosine + a * sine], axis=0)


KEYS = 128


def fold_top(value):
    top = value[:8]
    for begin in range(8, value.shape[0], 8):
        top = jnp.maximum(top, value[begin : begin + 8])
    return top


def masked(scores, offset):
    key_pos = lax.broadcasted_iota(jnp.int32, scores.shape, 0) + offset
    query_pos = lax.broadcasted_iota(jnp.int32, scores.shape, 1)
    return jnp.where(query_pos >= key_pos, scores, -jnp.inf)


def attend_placed(core_ref, *rest):
    for ref, where in places(core_ref, rest[:4]):
        rest[12][where, :] = ref[...]
    cos_ref, sin_ref, weight_ref, rest = rest[4], rest[5], rest[6], rest[7:]
    attend(weight_ref, cos_ref, sin_ref, *rest)


def attend(
    weight_ref, cos_ref, sin_ref, qkv_ref, att_ref, nat_ref, inverse_ref, out_ref, tokens, all_scores, all_weights, marks
):
    go = Mover(marks)
    stores = []
    width = weight_ref.shape[0] // 3
    projected = mul(weight_ref[...], tokens[...], 1, 1)
    cosine, sine = cos_ref[...], sin_ref[...]
    for part in range(3):
        for head in range(width // DH):
            begin = part * width + head * DH
            rows = projected[begin : begin + DH]
            if part < 2:
                rows = turn(rows, cosine, sine)
            if part == 0:
                rows = rows * DH ** (-0.5)
            qkv_ref[begin : begin + DH, :] = rows.astype(bfloat)
    inverse_ref[...] = jnp.zeros_like(inverse_ref)
    heads = range(width // DH)
    keys = [qkv_ref[width + head * DH : width + head * DH + DH, :].T for head in heads]
    for begin, size in BLOCKS:
        end = begin + size
        tops = [None for _ in heads]
        for row in range(0, end, KEYS):
            for head in heads:
                tile = mul(keys[head][row : row + KEYS], qkv_ref[head * DH : head * DH + DH, begin:end])
                if row >= begin:
                    tile = masked(tile, row - begin)
                all_scores[head, row : row + KEYS, :size] = tile
                top = fold_top(tile)
                tops[head] = top if row == 0 else jnp.maximum(tops[head], top)
        tops = [jnp.max(top, axis=0, keepdims=True) for top in tops]
        totals = [jnp.zeros((8, size), single) for _ in heads]
        for row in range(0, end, KEYS):
            for head in heads:
                tile = jnp.exp(all_scores[head, row : row + KEYS, :size] - tops[head])
                totals[head] = totals[head] + fold_rows(tile)
                all_weights[head, row : row + KEYS, begin:end] = tile.astype(bfloat)
        region = (slice(None), pl.ds(0, end), pl.ds(begin, size))
        stores += go((all_weights.at[region], out_ref.at[region]))
        for head in heads:
            base = head * DH
            inverse = 1.0 / jnp.sum(totals[head], axis=0, keepdims=True)
            value = qkv_ref[2 * width + base : 2 * width + base + DH, :end]
            mixed = mul(value, all_weights[head, :end, begin:end]) * inverse
            att_ref[base : base + DH, begin:end] = mixed.astype(bfloat)
            inverse_ref[head : head + 1, begin:end] = inverse
    nat_ref[...] = att_ref[...].T
    wait(stores)


def branch_body(core_ref, att_a_ref, att_b_ref, out_a_ref, out_b_ref, pass_ref, keep_ref, *rest):
    send_refs, pass_out = rest[:PARTS], rest[PARTS]
    pass_out[...] = pass_ref[...]
    low = pl.multiple_of(core_ref[0] * HALF, HALF)
    rows = HALF // PARTS
    for index in range(PARTS):
        high = pl.multiple_of((1 - core_ref[0]) * HALF + index * rows, rows)
        send = mul(att_a_ref[pl.ds(high, rows), :], out_a_ref[...])
        send_refs[index][...] = (send + mul(att_b_ref[pl.ds(high, rows), :], out_b_ref[...])).astype(bfloat)
    keep = mul(att_a_ref[pl.ds(low, HALF), :], out_a_ref[...])
    keep_ref[...] = keep + mul(att_b_ref[pl.ds(low, HALF), :], out_b_ref[...])


def attend_back(
    core_ref, inverse_ref, cos_ref, sin_ref, gain_ref, *rest
):
    before_refs, rest = rest[:-26], rest[-26:]
    grad_refs, x_refs, exp_ref = rest[:2], rest[2:6], rest[6]
    weight_ref, qkv_weight_ref, qkv_ref, att_ref, small_ref, out_ref, turned_ref = rest[7:14]
    grads, tokens, weight, qkv_weight, qkv, att, turned, result, all_probs, all_scores, hold, marks = rest[14:]
    go = Mover(marks)
    first = go(
        (weight_ref, weight),
        *[(ref, grads.at[where, :]) for ref, where in places(core_ref, grad_refs)],
        (att_ref, att),
        (qkv_ref, qkv),
    )
    regions = [(slice(None), pl.ds(0, begin + size), pl.ds(begin, size)) for begin, size in BLOCKS]
    parts = go(*[(exp_ref.at[region], all_probs.at[region]) for region in regions])
    later = go(
        *[(ref, tokens.at[where, :]) for ref, where in places(core_ref, x_refs)],
        (qkv_weight_ref, qkv_weight),
    )
    wait(first)
    width = att.shape[0]
    grad_att = mul(weight[...], grads[...], 1, 1)
    result[3 * width :, :] = mul(att[...], grads[...]).astype(result.dtype)
    cosine, sine = cos_ref[...], sin_ref[...]
    heads = range(width // DH)
    spans_of = [slice(head * DH, head * DH + DH) for head in heads]
    query = [qkv[span, :] for span in spans_of]
    key = [qkv[width + span.start : width + span.stop, :] for span in spans_of]
    above = [
        (grad_att[span] * inverse_ref[head : head + 1, :]).astype(bfloat) for head, span in enumerate(spans_of)
    ]
    centre = [
        jnp.sum(above[head].astype(single) * att[span, :].astype(single), axis=0, keepdims=True)
        for head, span in enumerate(spans_of)
    ]
    values = [qkv[2 * width + span.start : 2 * width + span.stop, :].T for span in spans_of]
    queries = [value.T for value in query]
    aboves = [value.T for value in above]
    grad_query = [[] for _ in heads]
    for (begin, size), part in zip(BLOCKS, parts):
        end = begin + size
        wait([part])
        for row in range(0, end, KEYS):
            span = slice(row, row + KEYS)
            for head in heads:
                tile = all_probs[head, span, begin:end].astype(single)
                grad = mul(values[head][span], above[head][:, begin:end]) - centre[head][:, begin:end]
                all_scores[head, span, begin:end] = (tile * grad).astype(bfloat)
        for head in heads:
            grad_query[head].append(mul(key[head][:, :end], all_scores[head, :end, begin:end]))
    grad_key = [[] for _ in heads]
    grad_value = [[] for _ in heads]
    for begin, size in BLOCKS:
        span = slice(begin, begin + size)
        for head in heads:
            grad_key[head].append(mul(all_scores[head, span, begin:], queries[head][begin:]))
            grad_value[head].append(mul(all_probs[head, span, begin:], aboves[head][begin:]))
    for head, span in enumerate(spans_of):
        grad = jnp.concatenate(grad_query[head], axis=1) * DH ** (-0.5)
        turned[span, :] = turn(grad, cosine, -sine).astype(bfloat)
        grad = jnp.concatenate(grad_key[head], axis=0).T
        turned[width + span.start : width + span.stop, :] = turn(grad, cosine, -sine).astype(bfloat)
        grad = jnp.concatenate(grad_value[head], axis=0).T
        turned[2 * width + span.start : 2 * width + span.stop, :] = grad.astype(bfloat)
    stores = go((turned, turned_ref))
    wait(later)
    hold[...] = mul(turned[...], tokens[...])
    result[: 3 * width, :] = hold[...].astype(result.dtype)
    stores += go((result, out_ref))
    part = jnp.zeros((8, hold.shape[1]), single)
    for span in spans(hold.shape[0]):
        part = part + fold_rows(hold[span, :] * qkv_weight[span, :].astype(single))
    gain = jnp.sum(part, axis=0, keepdims=True) / gain_ref[...].reshape(1, -1)
    if before_refs:
        gain_part_ref, mlp_part_ref, dwa_part_ref = before_refs
        small_ref[:1, :] = gain + gain_part_ref[...]
        small_ref[1:2, :] = mlp_part_ref[...]
        small_ref[2:, :] = dwa_part_ref[...]
    else:
        small_ref[...] = gain
    wait(stores)


def first_grad_body(
    core_ref, small_ref, turned_a_ref, turned_b_ref, weight_a_ref, weight_b_ref, send_ref, keep_ref,
    turned_a, turned_b, weight_a, weight_b, whole, marks,
):
    low = pl.multiple_of(core_ref[0] * HALF, HALF)
    high = pl.multiple_of((1 - core_ref[0]) * HALF, HALF)
    go = Mover(marks)
    wait(go((turned_a_ref, turned_a), (weight_a_ref, weight_a), (turned_b_ref, turned_b), (weight_b_ref, weight_b)))
    whole[...] = mul(turned_a[...], weight_a[...], 0, 0) + mul(turned_b[...], weight_b[...], 0, 0)
    stores = go((whole.at[pl.ds(low, HALF), :], keep_ref))
    send_ref[:HALF, :] = whole[pl.ds(high, HALF), :].astype(bfloat)
    small = small_ref[...]
    high_part = small.astype(bfloat)
    low_part = (small - high_part.astype(single)).astype(bfloat)
    send_ref[HALF:, :] = jnp.concatenate([high_part, low_part], axis=0)
    wait(stores)


CURVE = float(np.sqrt(2.0 / np.pi))
STEP = 256


def mlp_body(second, *refs):
    if second:
        owner_ref, refs = refs[0], refs[1:]
    x_refs, refs = refs[: 2 * PARTS], refs[2 * PARTS :]
    g_own_ref, g_peer_ref, refs = refs[0], refs[1], refs[2:]
    if second:
        up_ref, down_refs, refs = refs[0], refs[1 : 1 + SQUARE], refs[1 + SQUARE :]
        before_refs, up_mine_ref = refs[:4], refs[4]
        down_grad_ref, part_refs = refs[9], refs[10:14]
        refs = refs[5:9] + refs[14:]
    else:
        up_ref, down_ref = refs[:2]
        down_grad_ref, up_grad_ref = refs[6:8]
        refs = refs[2:6] + refs[8:]
    send_norm_ref, keep_norm_ref, send_out_ref, keep_out_ref = refs[:4]
    x_all, g_all, up, down, active, grad_hidden, x_turned = refs[4:11]
    send_norm, keep_norm, send_out, keep_out, down_grad, up_grad, marks = refs[11:18]
    rows, size = x_all.shape[0] // 2, x_all.shape[0] // (2 * PARTS)
    units = down.shape[0]
    go = Mover(marks)
    x_loads = go(*[(x_refs[index], x_all.at[pl.ds(index * size, size), :]) for index in range(2 * PARTS)])
    if second:
        loads = go((up_ref, up), *joined(owner_ref[0], down_refs, down))
    else:
        loads = go((up_ref, up), (down_ref, down))
    loads += go((g_own_ref, g_all.at[pl.ds(0, rows), :]), (g_peer_ref, g_all.at[pl.ds(rows, rows), :]))
    more, mine, stores = [], [], []
    if second:
        (up_mine,) = refs[18:]
        more = go(*zip(before_refs, (send_norm, keep_norm, send_out, keep_out)))
        mine = go((up_mine_ref, up_mine))
    wait(x_loads)
    x_turned[...] = x_all[...].T
    wait(loads)
    for begin in range(0, units, STEP):
        columns = slice(begin, begin + STEP)
        for top in range(0, 2 * rows, rows):
            span = slice(top, top + rows)
            v = mul(x_all[span, :], up[:, columns])
            grad = mul(g_all[span, :], down[columns, :], 1, 1)
            square = v * v
            half = 0.5 + 0.5 * jnp.tanh(v * (CURVE + (CURVE * 0.044715) * square))
            act = v * half
            slope = half + act * (1.0 - half) * (2.0 * CURVE + (6.0 * CURVE * 0.044715) * square)
            active[span, columns] = act.astype(bfloat)
            grad_hidden[span, columns] = (grad * slope).astype(bfloat)

    def put(target, value):
        target[...] = (value + target[...].astype(single) if second else value).astype(target.dtype)

    wait(more)
    put(keep_norm, mul(grad_hidden[:rows, :], up[...], 1, 1))
    put(send_norm, mul(grad_hidden[rows:, :], up[...], 1, 1))
    stores += go((keep_norm, keep_norm_ref), (send_norm, send_norm_ref))
    down_grad[...] = mul(active[...], g_all[...], 0, 0).astype(down_grad.dtype)
    stores += go((down_grad, down_grad_ref))
    up_grad[...] = mul(x_turned[...], grad_hidden[...]).astype(bfloat)
    if second:
        wait(mine)
        part = up_grad.shape[0] // SQUARE
        for mask, part_ref in enumerate(part_refs):
            rows_of = quarter(owner_ref[0], mask, part)
            stores += go(
                (up_mine.at[rows_of, :], part_ref.at[pl.ds(0, part), :]),
                (up_grad.at[rows_of, :], part_ref.at[pl.ds(part, part), :]),
            )
    else:
        stores += go((up_grad, up_grad_ref))
    put(keep_out, mul(active[:rows, :], down[...]))
    stores += go((keep_out, keep_out_ref))
    put(send_out, mul(active[rows:, :], down[...]))
    wait(stores + go((send_out, send_out_ref)))


def mlp(x_own, x_peer, g_own, g_peer, up, down, upper=(), before=(), flops=0):
    rows, width = g_own.shape
    units = sum(piece.shape[0] for piece in down)
    tall = (2 * rows, width)
    pair = [((rows, width), bfloat), ((rows, width), single)] * 2
    outs = pair + [((units, width), bfloat)]
    outs += [((2 * width // SQUARE, units), bfloat)] * SQUARE if before else [((width, units), bfloat)]
    scratch = [
        pltpu.VMEM(tall, bfloat),
        pltpu.VMEM(tall, bfloat),
        pltpu.VMEM((width, units), bfloat),
        pltpu.VMEM((units, width), bfloat),
        pltpu.VMEM((2 * rows, units), bfloat),
        pltpu.VMEM((2 * rows, units), bfloat),
        pltpu.VMEM((width, 2 * rows), bfloat),
    ]
    scratch += [pltpu.VMEM(shape, kind) for shape, kind in pair]
    scratch += [
        pltpu.VMEM((units, width), bfloat), pltpu.VMEM((width, units), bfloat), pltpu.SemaphoreType.DMA((32,)),
    ]
    if before:
        scratch.append(pltpu.VMEM((width, units), bfloat))
    operands = (*upper, *x_own, *x_peer, g_own, g_peer, *up, *down, *before)
    return call(
        functools.partial(mlp_body, bool(before)),
        outs,
        operands,
        scratch,
        len(upper),
        vmem=60,
        flops=flops,
        far=len(operands) - len(upper),
        far_outs=len(outs),
    )


def shards(
    inputs,
    history,
    cotangent,
    qkv_weight,
    out_weight,
    up_weight,
    down_weight,
    gain_attn,
    gain_mlp,
    dwa_weights,
):
    rows, width = inputs.shape
    members = lax.axis_size("mp")
    copies = lax.axis_size("dp")
    bits = copies.bit_length() - 1
    core = lax.rem(lax.axis_index("mp"), 2).astype(jnp.int32).reshape(1)
    copy_index = lax.axis_index("dp").astype(jnp.int32).reshape(1)
    core_pairs = [(i, i ^ 1) for i in range(members)]
    chip_pairs = [(i, i ^ 2) for i in range(members)]
    depth = history.shape[0]
    part = out_weight.shape[0]

    def other_core(value):
        return lax.ppermute(value, "mp", core_pairs)

    def other_chip(value):
        return lax.ppermute(value, "mp", chip_pairs)

    def other_copy(value, mask):
        return lax.ppermute(value, "dp", [(i, i ^ mask) for i in range(copies)])

    owner = copy_index & (SQUARE - 1)
    cosine, sine = (jnp.asarray(table) for table in tables())

    qkv_own = qkv_weight.transpose(1, 2, 0).reshape(3 * part, width)
    fourth = (width // SQUARE, width)
    square = (width, width)
    masks = range(1, SQUARE)
    marks = pltpu.SemaphoreType.DMA((24,))
    (down_quarter,) = call(
        split_body,
        [(fourth, bfloat)],
        (owner, down_weight),
        [pltpu.VMEM(fourth, bfloat), marks],
        1,
        vmem=60,
        far=1,
        far_outs=1,
    )
    qkv_peer, out_peer = other_chip(qkv_own), other_chip(out_weight)
    down_come, up_peer = other_chip(down_quarter), other_chip(up_weight)

    full = (rows, width)
    x_own = call(norm_body, [((rows // 2, width), bfloat)] * 2, (inputs, gain_attn), after=(down_quarter,))
    x_peer = [other_core(value) for value in x_own]
    tall = (SEQ, width)
    tokens = pltpu.VMEM(tall, bfloat)
    first_outs = [
        ((3 * part, SEQ), bfloat), ((part, SEQ), bfloat), ((SEQ, part), bfloat), ((8, SEQ), single),
    ]
    heads = part // DH
    first_outs.append(((heads, SEQ, SEQ), bfloat))
    tiles = [tokens, pltpu.VMEM((heads, SEQ, 256), single), pltpu.VMEM((heads, SEQ, SEQ), bfloat), marks]
    qkv_a, att_a, nat_a, log_a, exp_a = call(
        attend_placed, first_outs, (core, *x_own, *x_peer, cosine, sine, qkv_own), tiles, 1, vmem=32, far_outs=1
    )
    history_grad, mixed, g_own, history_parts = average_history(dwa_weights, history, cotangent, (log_a,))
    g_peer = other_core(g_own)
    qkv_b, att_b, nat_b, log_b, exp_b = call(
        attend_placed,
        first_outs,
        (core, *x_own, *x_peer, cosine, sine, qkv_peer),
        tiles,
        1,
        (history_parts,),
        32,
        MUCH,
        far_outs=1,
    )
    third = (rows // PARTS, width)
    keep, *send, down_copy = call(
        branch_body,
        [(full, single)] + [(third, bfloat)] * PARTS + [(fourth, bfloat)],
        (core, nat_a, nat_b, out_weight, out_peer, down_come),
        (),
        1,
        (g_peer,),
    )
    down_pieces = [down_come] + [other_copy(down_copy, mask) for mask in masks]
    recv = [other_core(value) for value in send]
    middle, *y_own = call(
        middle_body, [(full, single)] + [(third, bfloat)] * PARTS, (inputs, keep, gain_mlp, *recv)
    )
    y_peer = [other_core(value) for value in y_own]

    first = mlp(y_own, y_peer, g_own, g_peer, (up_weight,), (down_weight,))
    down_mine, up_mine = first[4:]
    second = mlp(
        y_own, y_peer, g_own, g_peer, (up_peer,), down_pieces, (owner,), (*first[:4], up_mine)
    )
    send_norm, keep_norm, send_out, keep_out, down_theirs = second[:5]
    token = [send_norm]

    def step(body, outs, operands, scratch=(), scalars=0, vmem=16, flops=MUCH, far=0, far_outs=0):
        results = call(body, outs, operands, scratch, scalars, tuple(token), vmem, flops, far, far_outs)
        token[0] = results[0]
        return results

    down_come = other_chip(down_theirs)
    up_parts = [second[5]] + [other_copy(value, mask) for mask, value in zip(masks, second[6:])]
    out_come = other_core(send_out)
    grad_middle, gb_own, gain_mlp_part = step(
        middle_back_body,
        [(full, single), (full, bfloat), ((1, width), single)],
        (dwa_weights, middle, keep_norm, other_core(send_norm), cotangent, gain_mlp),
        scalars=1,
        flops=0,
    )
    gb_peer = other_core(gb_own)
    def back(weight, qkv_weight, qkv, att, log, weights, flops, before=()):
        return step(
            attend_back,
            [
                ((depth + 3 if before else 1, width), single),
                ((4 * part, width), bfloat),
                ((3 * part, SEQ), bfloat),
            ],
            (
                core, log, cosine, sine, gain_attn, *before, gb_own, gb_peer, *x_own, *x_peer, weights, weight, qkv_weight, qkv,
                att,
            ),
            [
                pltpu.VMEM(tall, bfloat),
                pltpu.VMEM(tall, bfloat),
                pltpu.VMEM((part, width), bfloat),
                pltpu.VMEM((3 * part, width), bfloat),
                pltpu.VMEM((3 * part, SEQ), bfloat),
                pltpu.VMEM((part, SEQ), bfloat),
                pltpu.VMEM((3 * part, SEQ), bfloat),
                pltpu.VMEM((4 * part, width), bfloat),
                pltpu.VMEM((heads, SEQ, SEQ), bfloat),
                pltpu.VMEM((heads, SEQ, SEQ), bfloat),
                pltpu.VMEM((3 * part, width), single),
                marks,
            ],
            1,
            60,
            flops,
            11,
            2,
        )

    token.append(out_come)
    gain_part, att_theirs, turned_b = back(out_peer, qkv_peer, qkv_b, att_b, log_b, exp_b, 0)
    token.pop()
    att_come = other_chip(att_theirs)
    def spread(mine, come, flops=MUCH):
        own, *sent = step(part_body, [(fourth, bfloat)] * SQUARE, (owner, mine, come), scalars=1, flops=flops)
        return [own] + [other_copy(value, mask) for mask, value in zip(masks, sent)]

    down_parts = spread(down_mine, down_come, 0)
    combined, dwa_part = step(
        combine_body,
        [(full, bfloat), ((depth + 1, width), single)],
        (dwa_weights, mixed, middle, keep_out, out_come, cotangent, history_parts),
        scalars=1,
        flops=0,
    )

    up, sent = step(four_two_body, [(fourth, bfloat)] * 2, up_parts, flops=0)
    up_come = other_chip(sent)
    part_sums, att_mine, turned_a = back(
        out_weight, qkv_own, qkv_a, att_a, log_a, exp_a, MUCH, (gain_part, gain_mlp_part, dwa_part)
    )

    def exchange(value):
        for bit in range(2, bits):
            come = other_copy(value, 1 << bit)
            if bit < bits - 1:
                (value,) = step(low_body, [(value.shape, bfloat)], (value, come))
        return value, come

    def finish(value, come):
        (value,) = step(low_body, [(value.shape, bfloat)], (value, come), flops=COST)
        return [value] + [other_copy(value, mask) for mask in masks]

    (down,) = step(four_body, [(fourth, bfloat)], down_parts, flops=COST)
    down = exchange(down)
    att_parts = spread(att_mine, att_come, COST)
    (up,) = step(low_body, [(fourth, bfloat)], (up, up_come), flops=COST)
    up = exchange(up)
    send_first, keep_first = step(
        first_grad_body,
        [((rows + EXTRA, width), bfloat), (full, single)],
        (core, part_sums, turned_a, turned_b, qkv_own, qkv_peer),
        [pltpu.VMEM((3 * part, SEQ), bfloat)] * 2
        + [pltpu.VMEM((3 * part, width), bfloat)] * 2
        + [pltpu.VMEM(tall, single), marks],
        1,
        60,
        COST,
        4,
        1,
    )
    first_come = other_core(send_first)
    token.append(down[1])
    step(mark_body, [((8, 128), single)], (), flops=COST)
    del token[1:]
    (part_sums,) = step(small_body, [(part_sums.shape, single)], (part_sums, first_come), flops=COST)
    more_sums = other_chip(part_sums)
    (input_grad,) = step(
        first_back_body,
        [(full, bfloat)],
        (inputs, keep_first, first_come, grad_middle, gain_attn),
        vmem=60,
        flops=COST,
    )
    block = (width // SQUARE + EXTRA, width)
    (att,) = step(four_more_body, [(block, bfloat)], (part_sums, more_sums, *att_parts), flops=COST)
    att = exchange(att)
    down = finish(*down)
    token += down[1:]
    pair = (block[0] + fourth[0], width)
    (both,) = step(pair_body, [(pair, bfloat)], (*att, *up), flops=COST)
    del token[1:]
    both = [both] + [other_copy(both, mask) for mask in masks]
    (down_grad,) = step(
        whole_body, [(square, single)], (owner, *down), [pltpu.VMEM(square, bfloat)], 1, flops=COST
    )
    qkv_grad, out_grad, up_grad, gain_attn_grad, gain_mlp_grad, dwa_grad = step(
        more_body,
        [
            ((3 * part, width), single),
            ((part, width), single),
            (square, single),
            ((width,), single),
            ((width,), single),
            ((depth + 1,), single, "scalars"),
        ],
        (owner, *both),
        [pltpu.VMEM((SQUARE * pair[0], width), bfloat)],
        1,
        flops=COST,
    )

    return (
        combined,
        input_grad,
        history_grad,
        qkv_grad.reshape(3, part, width).transpose(2, 0, 1),
        out_grad,
        up_grad,
        down_grad,
        gain_attn_grad,
        gain_mlp_grad,
        dwa_grad,
    )


def solution(mesh):
    placed = (
        P(("dp", "mp"), None),
        P(None, ("dp", "mp"), None),
        P(("dp", "mp"), None),
        P(None, None, "mp"),
        P("mp", None),
        P(None, "mp"),
        P("mp", None),
        P(),
        P(),
        P(),
    )
    return jax.shard_map(
        shards,
        mesh=mesh,
        in_specs=placed,
        out_specs=(
            P(("dp", "mp"), None),
            P(("dp", "mp"), None),
            P(None, ("dp", "mp"), None),
            P(None, None, "mp"),
            P("mp", None),
            P(None, "mp"),
            P("mp", None),
            P(),
            P(),
            P(),
        ),
        check_vma=False,
    )
```

```python
import functools

import jax
import jax.numpy as jnp
import numpy as np
from jax import lax
from jax.experimental import pallas as pl
from jax.experimental.pallas import tpu as pltpu
from jax.sharding import PartitionSpec as P

DH = 64
SEQ = 1152
HALF = SEQ // 2
EPS = 1e-05
bfloat = jnp.bfloat16
single = jnp.float32
MIB = 1 << 20
MUCH = 10**11
COST = 10**10


def tables():
    half_width = DH // 2
    places = np.arange(SEQ, dtype=np.float32)
    frequency = np.float32(10000.0) ** (-np.arange(half_width, dtype=np.float32) * np.float32(2.0 / DH))
    angles = frequency[:, None] * places[None, :]
    return (np.cos(angles).astype(np.float32), np.sin(angles).astype(np.float32))


def mul(a, b, ca=1, cb=0):
    return lax.dot_general(a, b, (((ca,), (cb,)), ((), ())), preferred_element_type=single)


def call(kernel, outs, operands, scratch=(), scalars=0, after=(), vmem=16, flops=0, far=0, far_outs=0):
    count, waits = len(operands), len(after)

    def body(*refs):
        kernel(*refs[:count], *refs[count + waits :])

    small = pl.BlockSpec(memory_space=pltpu.SMEM)
    whole = pl.BlockSpec(memory_space=pltpu.VMEM)
    apart = pl.BlockSpec(memory_space=pltpu.HBM)
    loose = pl.BlockSpec(memory_space=pl.ANY)
    inner = len(outs) - far_outs
    return pl.pallas_call(
        body,
        out_shape=[jax.ShapeDtypeStruct(out[0], out[1]) for out in outs],
        in_specs=[small] * scalars + [whole] * (count - scalars - far) + [apart] * far + [loose] * waits,
        out_specs=[small if len(out) > 2 else whole for out in outs[:inner]] + [apart] * far_outs,
        scratch_shapes=list(scratch),
        compiler_params=pltpu.CompilerParams(vmem_limit_bytes=vmem * MIB),
        cost_estimate=pl.CostEstimate(flops=flops, bytes_accessed=0, transcendentals=0),
    )(*operands, *after)


class Mover:
    def __init__(self, marks):
        self.marks = marks
        self.used = 0

    def __call__(self, *pairs):
        copies = []
        for source, target in pairs:
            copies.append(pltpu.make_async_copy(source, target, self.marks.at[self.used]))
            self.used += 1
        for copy in copies:
            copy.start()
        return copies


def wait(copies):
    for copy in copies:
        copy.wait()


ROWS = 64
PARTS = 1


def spans(rows, step=ROWS):
    return [slice(begin, begin + step) for begin in range(0, rows, step)]


def normal_of(x):
    centre = x - jnp.mean(x, axis=-1, keepdims=True)
    spread = jnp.mean(centre * centre, axis=-1, keepdims=True)
    scale = lax.rsqrt(spread + EPS)
    return centre * scale, scale


def split_body(owner_ref, in_ref, out_ref, hold, marks):
    go = Mover(marks)
    wait(go((in_ref.at[quarter(owner_ref[0], 0, hold.shape[0]), :], hold)))
    wait(go((hold, out_ref)))


def joined(owner, refs, target):
    size = refs[0].shape[0]
    return [(ref, target.at[quarter(owner, mask, size), :]) for mask, ref in enumerate(refs)]


def norm_body(x_ref, gain_ref, *out_refs):
    gain = gain_ref[...].reshape(1, -1)
    for index, out_ref in enumerate(out_refs):
        rows = out_ref.shape[0]
        for span in spans(rows, rows // 6):
            here = slice(index * rows + span.start, index * rows + span.stop)
            normal, _ = normal_of(x_ref[here, :].astype(single))
            out_ref[span, :] = (normal * gain).astype(bfloat)


def middle_body(x_ref, keep_ref, gain_ref, *rest):
    recv_refs, mid_ref, out_refs = rest[:PARTS], rest[PARTS], rest[PARTS + 1 :]
    gain = gain_ref[...].reshape(1, -1)
    rows = x_ref.shape[0] // PARTS
    for index in range(PARTS):
        for span in spans(rows):
            here = slice(index * rows + span.start, index * rows + span.stop)
            recv = recv_refs[index][span, :].astype(single)
            x = x_ref[here, :].astype(single) + (keep_ref[here, :] + recv)
            mid_ref[here, :] = x
            normal, _ = normal_of(x)
            out_refs[index][span, :] = (normal * gain).astype(bfloat)


def norm_back(x, grad, gain):
    normal, scale = normal_of(x)
    lifted = grad * gain
    back = scale * (
        lifted
        - jnp.mean(lifted, axis=-1, keepdims=True)
        - normal * jnp.mean(lifted * normal, axis=-1, keepdims=True)
    )
    return back, normal


def fold_rows(value):
    total = value[:8]
    for begin in range(8, value.shape[0], 8):
        total = total + value[begin : begin + 8]
    return total


def middle_back_body(mix_ref, x_ref, keep_ref, recv_ref, cot_ref, gain_ref, mid_ref, low_ref, part_ref):
    gain = gain_ref[...].reshape(1, -1)
    part = jnp.zeros((8, x_ref.shape[1]), single)
    for span in spans(x_ref.shape[0]):
        grad = keep_ref[span, :] + recv_ref[span, :].astype(single)
        back, normal = norm_back(x_ref[span, :], grad, gain)
        total = mix_ref[mix_ref.shape[0] - 1] * cot_ref[span, :] + back
        mid_ref[span, :] = total
        low_ref[span, :] = total.astype(bfloat)
        part = part + fold_rows(grad * normal)
    part_ref[...] = jnp.sum(part, axis=0, keepdims=True)


def first_back_body(x_ref, keep_ref, recv_ref, mid_ref, gain_ref, out_ref):
    gain = gain_ref[...].reshape(1, -1)
    for span in spans(x_ref.shape[0]):
        grad = keep_ref[span, :] + recv_ref[span, :].astype(single)
        back, _ = norm_back(x_ref[span, :].astype(single), grad, gain)
        out_ref[span, :] = (mid_ref[span, :] + back).astype(bfloat)


def history_body(mix_ref, history_ref, cot_ref, grad_ref, mixed_ref, low_ref, part_ref):
    depth = history_ref.shape[0]

    @pl.when(pl.program_id(0) == 0)
    def _():
        part_ref[...] = jnp.zeros_like(part_ref)

    for span in spans(cot_ref.shape[0], 32):
        cot = cot_ref[span, :]
        low_ref[span, :] = (mix_ref[depth] * cot).astype(bfloat)
        mixed = None
        for j in range(depth):
            layer = history_ref[j, span, :].astype(single)
            mixed = mix_ref[j] * layer if mixed is None else mixed + mix_ref[j] * layer
            grad_ref[j, span, :] = (mix_ref[j] * cot).astype(bfloat)
            part_ref[8 * j : 8 * j + 8, :] += fold_rows(layer * cot)
        mixed_ref[span, :] = mixed


def average_history(mix, history, cot, after=()):
    depth, rows, width = history.shape
    step = 96
    waits = len(after)

    def body(*refs):
        history_body(*refs[:3], *refs[3 + waits :])

    row_block = pl.BlockSpec((step, width), lambda i: (i, 0))
    deep_block = pl.BlockSpec((depth, step, width), lambda i: (0, i, 0))
    return pl.pallas_call(
        body,
        grid=(rows // step,),
        out_shape=[
            jax.ShapeDtypeStruct(history.shape, bfloat),
            jax.ShapeDtypeStruct((rows, width), single),
            jax.ShapeDtypeStruct((rows, width), bfloat),
            jax.ShapeDtypeStruct((8 * depth, width), single),
        ],
        in_specs=[pl.BlockSpec(memory_space=pltpu.SMEM), deep_block, row_block]
        + [pl.BlockSpec(memory_space=pl.ANY)] * waits,
        out_specs=[deep_block, row_block, row_block, pl.BlockSpec((8 * depth, width), lambda i: (0, 0))],
        compiler_params=pltpu.CompilerParams(vmem_limit_bytes=16 * MIB),
        cost_estimate=pl.CostEstimate(flops=0, bytes_accessed=0, transcendentals=0),
    )(mix, history, cot, *after)


def combine_body(mix_ref, mixed_ref, mid_ref, keep_ref, recv_ref, cot_ref, parts_ref, out_ref, part_ref):
    depth = mix_ref.shape[0] - 1
    last = jnp.zeros((8, mid_ref.shape[1]), single)
    for span in spans(mid_ref.shape[0]):
        outputs = mid_ref[span, :] + (keep_ref[span, :] + recv_ref[span, :].astype(single))
        out_ref[span, :] = (mixed_ref[span, :] + mix_ref[depth] * outputs).astype(bfloat)
        last = last + fold_rows(outputs * cot_ref[span, :])
    for j in range(depth):
        part_ref[j : j + 1, :] = jnp.sum(parts_ref[8 * j : 8 * j + 8, :], axis=0, keepdims=True)
    part_ref[depth : depth + 1, :] = jnp.sum(last, axis=0, keepdims=True)


SQUARE = 4


def quarter(owner, mask, size):
    other = owner + (mask & 1) * (1 - 2 * (owner % 2)) + (mask & 2) * (1 - 2 * (owner // 2))
    return pl.ds(pl.multiple_of(other * size, size), size)


def part_body(owner_ref, mine_ref, come_ref, *out_refs):
    for mask, out_ref in enumerate(out_refs):
        rows = quarter(owner_ref[0], mask, out_ref.shape[0])
        out_ref[...] = (mine_ref[rows, :].astype(single) + come_ref[rows, :].astype(single)).astype(bfloat)


def sum_of(refs, rows):
    total = refs[0][rows, :].astype(single)
    for ref in refs[1:]:
        total = total + ref[rows, :].astype(single)
    return total


def four_body(*refs):
    refs[-1][...] = sum_of(refs[:-1], slice(None)).astype(bfloat)


def four_two_body(*refs):
    size = refs[-1].shape[0]
    refs[-2][...] = sum_of(refs[:-2], slice(0, size)).astype(bfloat)
    refs[-1][...] = sum_of(refs[:-2], slice(size, 2 * size)).astype(bfloat)


EXTRA = 16


def mark_body(out_ref):
    out_ref[...] = jnp.zeros_like(out_ref)


def small_body(small_ref, first_ref, out_ref):
    half = small_ref.shape[0]
    rows = first_ref.shape[0] - 2 * half
    come = first_ref[rows:, :].astype(single)
    out_ref[...] = small_ref[...] + (come[:half] + come[half:])


def four_more_body(small_ref, more_ref, *refs):
    out_ref = refs[-1]
    size = out_ref.shape[0] - EXTRA
    out_ref[:size, :] = sum_of(refs[:-1], slice(None)).astype(bfloat)
    small = small_ref[...] + more_ref[...]
    rest = jnp.zeros((EXTRA - small.shape[0], small.shape[1]), single)
    out_ref[size:, :] = jnp.concatenate([small, rest], axis=0).astype(bfloat)


def gather(owner_ref, pieces, hold):
    for mask, piece in enumerate(pieces):
        hold[quarter(owner_ref[0], mask, piece.shape[0]), :] = piece[...]


def pair_body(a_ref, a_come_ref, b_ref, b_come_ref, out_ref):
    size = a_ref.shape[0]
    out_ref[:size, :] = sum_of((a_ref, a_come_ref), slice(None)).astype(bfloat)
    out_ref[size:, :] = sum_of((b_ref, b_come_ref), slice(None)).astype(bfloat)


def whole_body(owner_ref, a_ref, b_ref, c_ref, d_ref, out_ref, hold):
    gather(owner_ref, (a_ref, b_ref, c_ref, d_ref), hold)
    out_ref[...] = hold[...].astype(single)


def more_body(owner_ref, a_ref, b_ref, c_ref, d_ref, top_ref, end_ref, up_ref, attn_ref, mlp_ref, dwa_ref, hold):
    gather(owner_ref, (a_ref, b_ref, c_ref, d_ref), hold)
    block = hold.shape[0] // SQUARE
    rows = up_ref.shape[0] // SQUARE
    small = jnp.zeros((EXTRA, hold.shape[1]), single)
    for index in range(SQUARE):
        begin = index * block
        target, place = (top_ref, index * rows) if index < SQUARE - 1 else (end_ref, 0)
        target[place : place + rows, :] = hold[begin : begin + rows, :].astype(single)
        small = small + hold[begin + rows : begin + rows + EXTRA, :].astype(single)
        up_ref[index * rows : (index + 1) * rows, :] = hold[begin + rows + EXTRA : begin + block, :].astype(single)
    attn_ref[...] = small[0]
    mlp_ref[...] = small[1]
    for index in range(dwa_ref.shape[0]):
        dwa_ref[index] = jnp.sum(small[2 + index : 3 + index])


def low_body(mine_ref, come_ref, out_ref):
    out_ref[...] = (mine_ref[...].astype(single) + come_ref[...].astype(single)).astype(bfloat)


def mark_body(out_ref):
    out_ref[...] = jnp.zeros_like(out_ref)


def small_body(small_ref, first_ref, out_ref):
    half = small_ref.shape[0]
    rows = first_ref.shape[0] - 2 * half
    come = first_ref[rows:, :].astype(single)
    out_ref[...] = small_ref[...] + (come[:half] + come[half:])


BLOCKS = tuple((begin, min(256, SEQ - begin)) for begin in range(0, SEQ, 256))


def places(core_ref, refs):
    count, size = len(refs) // 2, refs[0].shape[0]
    for index, ref in enumerate(refs):
        core = core_ref[0] if index < count else 1 - core_ref[0]
        yield ref, pl.ds(pl.multiple_of(core * HALF + index % count * size, size), size)


def allowed(size):
    key_pos = lax.broadcasted_iota(jnp.int32, (size, size), 0)
    query_pos = lax.broadcasted_iota(jnp.int32, (size, size), 1)
    return query_pos >= key_pos


def turn(rows, cosine, sine):
    half = rows.shape[0] // 2
    a, b = rows[:half], rows[half:]
    return jnp.concatenate([a * cosine - b * sine, b * cosine + a * sine], axis=0)


KEYS = 128


def fold_top(value):
    top = value[:8]
    for begin in range(8, value.shape[0], 8):
        top = jnp.maximum(top, value[begin : begin + 8])
    return top


def masked(scores, offset):
    key_pos = lax.broadcasted_iota(jnp.int32, scores.shape, 0) + offset
    query_pos = lax.broadcasted_iota(jnp.int32, scores.shape, 1)
    return jnp.where(query_pos >= key_pos, scores, -jnp.inf)


def attend_placed(core_ref, *rest):
    for ref, where in places(core_ref, rest[:4]):
        rest[11][where, :] = ref[...]
    cos_ref, sin_ref, weight_ref, rest = rest[4], rest[5], rest[6], rest[7:]
    attend(weight_ref, cos_ref, sin_ref, *rest)


def by_head(value, heads):
    head_of = lax.broadcasted_iota(jnp.int32, (1, value.shape[1]), 1) >> (DH.bit_length() - 1)
    return [value * (head_of == head).astype(single).astype(bfloat) for head in heads]


def attend(weight_ref, cos_ref, sin_ref, qkv_ref, att_ref, nat_ref, log_ref, tokens, all_scores, all_weights):
    width = weight_ref.shape[0] // 3
    projected = mul(weight_ref[...], tokens[...], 1, 1)
    cosine, sine = cos_ref[...], sin_ref[...]
    for part in range(3):
        for head in range(width // DH):
            begin = part * width + head * DH
            rows = projected[begin : begin + DH]
            if part < 2:
                rows = turn(rows, cosine, sine)
            if part == 0:
                rows = rows * DH ** (-0.5)
            qkv_ref[begin : begin + DH, :] = rows.astype(bfloat)
    log_ref[...] = jnp.zeros_like(log_ref)
    heads = range(width // DH)
    keys = by_head(qkv_ref[width : 2 * width, :].T, heads)
    for begin, size in BLOCKS:
        end = begin + size
        tops = [None for _ in heads]
        for row in range(0, end, KEYS):
            for head in heads:
                tile = mul(keys[head][row : row + KEYS], qkv_ref[:width, begin:end])
                if row >= begin:
                    tile = masked(tile, row - begin)
                all_scores[head, row : row + KEYS, :size] = tile
                top = fold_top(tile)
                tops[head] = top if row == 0 else jnp.maximum(tops[head], top)
        tops = [jnp.max(top, axis=0, keepdims=True) for top in tops]
        totals = [jnp.zeros((8, size), single) for _ in heads]
        for row in range(0, end, KEYS):
            for head in heads:
                tile = jnp.exp(all_scores[head, row : row + KEYS, :size] - tops[head])
                totals[head] = totals[head] + fold_rows(tile)
                all_weights[head, row : row + KEYS, :size] = tile.astype(bfloat)
        for head in heads:
            base = head * DH
            total = jnp.sum(totals[head], axis=0, keepdims=True)
            value = qkv_ref[2 * width + base : 2 * width + base + DH, :end]
            mixed = mul(value, all_weights[head, :end, :size]) / total
            att_ref[base : base + DH, begin:end] = mixed.astype(bfloat)
            log_ref[head : head + 1, begin:end] = tops[head] + jnp.log(total)
    nat_ref[...] = att_ref[...].T


def branch_body(core_ref, att_a_ref, att_b_ref, out_a_ref, out_b_ref, pass_ref, keep_ref, *rest):
    send_refs, pass_out = rest[:PARTS], rest[PARTS]
    pass_out[...] = pass_ref[...]
    low = pl.multiple_of(core_ref[0] * HALF, HALF)
    rows = HALF // PARTS
    for index in range(PARTS):
        high = pl.multiple_of((1 - core_ref[0]) * HALF + index * rows, rows)
        send = mul(att_a_ref[pl.ds(high, rows), :], out_a_ref[...])
        send_refs[index][...] = (send + mul(att_b_ref[pl.ds(high, rows), :], out_b_ref[...])).astype(bfloat)
    keep = mul(att_a_ref[pl.ds(low, HALF), :], out_a_ref[...])
    keep_ref[...] = keep + mul(att_b_ref[pl.ds(low, HALF), :], out_b_ref[...])


def attend_back(
    core_ref, log_ref, cos_ref, sin_ref, gain_ref, *rest
):
    before_refs, rest = rest[:-25], rest[-25:]
    grad_refs, x_refs = rest[:2], rest[2:6]
    weight_ref, qkv_weight_ref, qkv_ref, att_ref, small_ref, out_ref, turned_ref = rest[6:13]
    grads, tokens, weight, qkv_weight, qkv, att, turned, result, all_probs, all_scores, hold, marks = rest[13:]
    go = Mover(marks)
    first = go(
        (weight_ref, weight),
        *[(ref, grads.at[where, :]) for ref, where in places(core_ref, grad_refs)],
        (att_ref, att),
        (qkv_ref, qkv),
    )
    later = go(
        *[(ref, tokens.at[where, :]) for ref, where in places(core_ref, x_refs)],
        (qkv_weight_ref, qkv_weight),
    )
    wait(first)
    width = att.shape[0]
    grad_att = mul(weight[...], grads[...], 1, 1).astype(bfloat)
    result[3 * width :, :] = mul(att[...], grads[...]).astype(result.dtype)
    cosine, sine = cos_ref[...], sin_ref[...]
    heads = range(width // DH)
    spans_of = [slice(head * DH, head * DH + DH) for head in heads]
    key = [qkv[width + span.start : width + span.stop, :] for span in spans_of]
    above = [grad_att[span] for span in spans_of]
    centre = [
        jnp.sum(above[head].astype(single) * att[span, :].astype(single), axis=0, keepdims=True)
        for head, span in enumerate(spans_of)
    ]
    keys = by_head(qkv[width : 2 * width, :].T, heads)
    values = by_head(qkv[2 * width : 3 * width, :].T, heads)
    queries = by_head(qkv[:width, :].T, heads)
    aboves = by_head(grad_att.T, heads)
    grad_query = [[] for _ in heads]
    for begin, size in BLOCKS:
        end = begin + size
        for row in range(0, end, KEYS):
            span = slice(row, row + KEYS)
            for head in heads:
                tile = mul(keys[head][span], qkv[:width, begin:end])
                if row >= begin:
                    tile = masked(tile, row - begin)
                tile = jnp.exp(tile - log_ref[head : head + 1, begin:end])
                grad = mul(values[head][span], grad_att[:, begin:end]) - centre[head][:, begin:end]
                all_probs[head, span, begin:end] = tile.astype(bfloat)
                all_scores[head, span, begin:end] = (tile * grad).astype(bfloat)
        for head in heads:
            grad_query[head].append(mul(key[head][:, :end], all_scores[head, :end, begin:end]))
    grad_key, grad_value = [], []
    for begin, size in BLOCKS:
        span = slice(begin, begin + size)
        grad_key.append(sum(mul(all_scores[head, span, begin:], queries[head][begin:]) for head in heads))
        grad_value.append(sum(mul(all_probs[head, span, begin:], aboves[head][begin:]) for head in heads))
    grad_key = jnp.concatenate(grad_key, axis=0).T
    turned[2 * width :, :] = jnp.concatenate(grad_value, axis=0).T.astype(bfloat)
    for head, span in enumerate(spans_of):
        grad = jnp.concatenate(grad_query[head], axis=1) * DH ** (-0.5)
        turned[span, :] = turn(grad, cosine, -sine).astype(bfloat)
        turned[width + span.start : width + span.stop, :] = turn(grad_key[span], cosine, -sine).astype(bfloat)
    stores = go((turned, turned_ref))
    wait(later)
    hold[...] = mul(turned[...], tokens[...])
    result[: 3 * width, :] = hold[...].astype(result.dtype)
    stores += go((result, out_ref))
    part = jnp.zeros((8, hold.shape[1]), single)
    for span in spans(hold.shape[0]):
        part = part + fold_rows(hold[span, :] * qkv_weight[span, :].astype(single))
    gain = jnp.sum(part, axis=0, keepdims=True) / gain_ref[...].reshape(1, -1)
    if before_refs:
        gain_part_ref, mlp_part_ref, dwa_part_ref = before_refs
        small_ref[:1, :] = gain + gain_part_ref[...]
        small_ref[1:2, :] = mlp_part_ref[...]
        small_ref[2:, :] = dwa_part_ref[...]
    else:
        small_ref[...] = gain
    wait(stores)


def first_grad_body(
    core_ref, small_ref, turned_a_ref, turned_b_ref, weight_a_ref, weight_b_ref, send_ref, keep_ref,
    turned_a, turned_b, weight_a, weight_b, whole, marks,
):
    low = pl.multiple_of(core_ref[0] * HALF, HALF)
    high = pl.multiple_of((1 - core_ref[0]) * HALF, HALF)
    go = Mover(marks)
    wait(go((turned_a_ref, turned_a), (weight_a_ref, weight_a), (turned_b_ref, turned_b), (weight_b_ref, weight_b)))
    whole[...] = mul(turned_a[...], weight_a[...], 0, 0) + mul(turned_b[...], weight_b[...], 0, 0)
    stores = go((whole.at[pl.ds(low, HALF), :], keep_ref))
    send_ref[:HALF, :] = whole[pl.ds(high, HALF), :].astype(bfloat)
    small = small_ref[...]
    high_part = small.astype(bfloat)
    low_part = (small - high_part.astype(single)).astype(bfloat)
    send_ref[HALF:, :] = jnp.concatenate([high_part, low_part], axis=0)
    wait(stores)


CURVE = float(np.sqrt(2.0 / np.pi))
STEP = 256


def mlp_body(second, *refs):
    if second:
        owner_ref, refs = refs[0], refs[1:]
    x_refs, refs = refs[: 2 * PARTS], refs[2 * PARTS :]
    g_own_ref, g_peer_ref, refs = refs[0], refs[1], refs[2:]
    if second:
        up_ref, down_refs, refs = refs[0], refs[1 : 1 + SQUARE], refs[1 + SQUARE :]
        before_refs, up_mine_ref = refs[:4], refs[4]
        down_grad_ref, part_refs = refs[9], refs[10:14]
        refs = refs[5:9] + refs[14:]
    else:
        up_ref, down_ref = refs[:2]
        down_grad_ref, up_grad_ref = refs[6:8]
        refs = refs[2:6] + refs[8:]
    send_norm_ref, keep_norm_ref, send_out_ref, keep_out_ref = refs[:4]
    x_all, g_all, up, down, active, grad_hidden, x_turned = refs[4:11]
    send_norm, keep_norm, send_out, keep_out, down_grad, up_grad, marks = refs[11:18]
    rows, size = x_all.shape[0] // 2, x_all.shape[0] // (2 * PARTS)
    units = down.shape[0]
    go = Mover(marks)
    x_loads = go(*[(x_refs[index], x_all.at[pl.ds(index * size, size), :]) for index in range(2 * PARTS)])
    if second:
        loads = go((up_ref, up), *joined(owner_ref[0], down_refs, down))
    else:
        loads = go((up_ref, up), (down_ref, down))
    loads += go((g_own_ref, g_all.at[pl.ds(0, rows), :]), (g_peer_ref, g_all.at[pl.ds(rows, rows), :]))
    more, mine, stores = [], [], []
    if second:
        (up_mine,) = refs[18:]
        more = go(*zip(before_refs, (send_norm, keep_norm, send_out, keep_out)))
        mine = go((up_mine_ref, up_mine))
    wait(x_loads)
    x_turned[...] = x_all[...].T
    wait(loads)
    for begin in range(0, units, STEP):
        columns = slice(begin, begin + STEP)
        for top in range(0, 2 * rows, rows):
            span = slice(top, top + rows)
            v = mul(x_all[span, :], up[:, columns])
            grad = mul(g_all[span, :], down[columns, :], 1, 1)
            square = v * v
            half = 0.5 + 0.5 * jnp.tanh(v * (CURVE + (CURVE * 0.044715) * square))
            act = v * half
            slope = half + act * (1.0 - half) * (2.0 * CURVE + (6.0 * CURVE * 0.044715) * square)
            active[span, columns] = act.astype(bfloat)
            grad_hidden[span, columns] = (grad * slope).astype(bfloat)

    def put(target, value):
        target[...] = (value + target[...].astype(single) if second else value).astype(target.dtype)

    wait(more)
    put(keep_norm, mul(grad_hidden[:rows, :], up[...], 1, 1))
    put(send_norm, mul(grad_hidden[rows:, :], up[...], 1, 1))
    stores += go((keep_norm, keep_norm_ref), (send_norm, send_norm_ref))
    down_grad[...] = mul(active[...], g_all[...], 0, 0).astype(down_grad.dtype)
    stores += go((down_grad, down_grad_ref))
    up_grad[...] = mul(x_turned[...], grad_hidden[...]).astype(bfloat)
    if second:
        wait(mine)
        part = up_grad.shape[0] // SQUARE
        for mask, part_ref in enumerate(part_refs):
            rows_of = quarter(owner_ref[0], mask, part)
            stores += go(
                (up_mine.at[rows_of, :], part_ref.at[pl.ds(0, part), :]),
                (up_grad.at[rows_of, :], part_ref.at[pl.ds(part, part), :]),
            )
    else:
        stores += go((up_grad, up_grad_ref))
    put(keep_out, mul(active[:rows, :], down[...]))
    stores += go((keep_out, keep_out_ref))
    put(send_out, mul(active[rows:, :], down[...]))
    wait(stores + go((send_out, send_out_ref)))


def mlp(x_own, x_peer, g_own, g_peer, up, down, upper=(), before=(), flops=0):
    rows, width = g_own.shape
    units = sum(piece.shape[0] for piece in down)
    tall = (2 * rows, width)
    pair = [((rows, width), bfloat), ((rows, width), single)] * 2
    outs = pair + [((units, width), bfloat)]
    outs += [((2 * width // SQUARE, units), bfloat)] * SQUARE if before else [((width, units), bfloat)]
    scratch = [
        pltpu.VMEM(tall, bfloat),
        pltpu.VMEM(tall, bfloat),
        pltpu.VMEM((width, units), bfloat),
        pltpu.VMEM((units, width), bfloat),
        pltpu.VMEM((2 * rows, units), bfloat),
        pltpu.VMEM((2 * rows, units), bfloat),
        pltpu.VMEM((width, 2 * rows), bfloat),
    ]
    scratch += [pltpu.VMEM(shape, kind) for shape, kind in pair]
    scratch += [
        pltpu.VMEM((units, width), bfloat), pltpu.VMEM((width, units), bfloat), pltpu.SemaphoreType.DMA((32,)),
    ]
    if before:
        scratch.append(pltpu.VMEM((width, units), bfloat))
    operands = (*upper, *x_own, *x_peer, g_own, g_peer, *up, *down, *before)
    return call(
        functools.partial(mlp_body, bool(before)),
        outs,
        operands,
        scratch,
        len(upper),
        vmem=60,
        flops=flops,
        far=len(operands) - len(upper),
        far_outs=len(outs),
    )


def shards(
    inputs,
    history,
    cotangent,
    qkv_weight,
    out_weight,
    up_weight,
    down_weight,
    gain_attn,
    gain_mlp,
    dwa_weights,
):
    rows, width = inputs.shape
    members = lax.axis_size("mp")
    copies = lax.axis_size("dp")
    bits = copies.bit_length() - 1
    core = lax.rem(lax.axis_index("mp"), 2).astype(jnp.int32).reshape(1)
    copy_index = lax.axis_index("dp").astype(jnp.int32).reshape(1)
    core_pairs = [(i, i ^ 1) for i in range(members)]
    chip_pairs = [(i, i ^ 2) for i in range(members)]
    depth = history.shape[0]
    part = out_weight.shape[0]

    def other_core(value):
        return lax.ppermute(value, "mp", core_pairs)

    def other_chip(value):
        return lax.ppermute(value, "mp", chip_pairs)

    def other_copy(value, mask):
        return lax.ppermute(value, "dp", [(i, i ^ mask) for i in range(copies)])

    owner = copy_index & (SQUARE - 1)
    cosine, sine = (jnp.asarray(table) for table in tables())

    qkv_own = qkv_weight.transpose(1, 2, 0).reshape(3 * part, width)
    fourth = (width // SQUARE, width)
    square = (width, width)
    masks = range(1, SQUARE)
    marks = pltpu.SemaphoreType.DMA((16,))
    (down_quarter,) = call(
        split_body,
        [(fourth, bfloat)],
        (owner, down_weight),
        [pltpu.VMEM(fourth, bfloat), marks],
        1,
        vmem=60,
        far=1,
        far_outs=1,
    )
    qkv_peer, out_peer = other_chip(qkv_own), other_chip(out_weight)
    down_come, up_peer = other_chip(down_quarter), other_chip(up_weight)

    full = (rows, width)
    x_own = call(norm_body, [((rows // 2, width), bfloat)] * 2, (inputs, gain_attn), after=(down_quarter,))
    x_peer = [other_core(value) for value in x_own]
    tall = (SEQ, width)
    tokens = pltpu.VMEM(tall, bfloat)
    first_outs = [
        ((3 * part, SEQ), bfloat), ((part, SEQ), bfloat), ((SEQ, part), bfloat), ((8, SEQ), single),
    ]
    heads = part // DH
    tiles = [tokens, pltpu.VMEM((heads, SEQ, 256), single), pltpu.VMEM((heads, SEQ, 256), bfloat)]
    qkv_a, att_a, nat_a, log_a = call(
        attend_placed, first_outs, (core, *x_own, *x_peer, cosine, sine, qkv_own), tiles, 1, vmem=32
    )
    history_grad, mixed, g_own, history_parts = average_history(dwa_weights, history, cotangent, (log_a,))
    g_peer = other_core(g_own)
    qkv_b, att_b, nat_b, log_b = call(
        attend_placed,
        first_outs,
        (core, *x_own, *x_peer, cosine, sine, qkv_peer),
        tiles,
        1,
        (history_parts,),
        32,
        MUCH,
    )
    third = (rows // PARTS, width)
    keep, *send, down_copy = call(
        branch_body,
        [(full, single)] + [(third, bfloat)] * PARTS + [(fourth, bfloat)],
        (core, nat_a, nat_b, out_weight, out_peer, down_come),
        (),
        1,
        (g_peer,),
    )
    down_pieces = [down_come] + [other_copy(down_copy, mask) for mask in masks]
    recv = [other_core(value) for value in send]
    middle, *y_own = call(
        middle_body, [(full, single)] + [(third, bfloat)] * PARTS, (inputs, keep, gain_mlp, *recv)
    )
    y_peer = [other_core(value) for value in y_own]

    first = mlp(y_own, y_peer, g_own, g_peer, (up_weight,), (down_weight,))
    down_mine, up_mine = first[4:]
    second = mlp(
        y_own, y_peer, g_own, g_peer, (up_peer,), down_pieces, (owner,), (*first[:4], up_mine)
    )
    send_norm, keep_norm, send_out, keep_out, down_theirs = second[:5]
    token = [send_norm]

    def step(body, outs, operands, scratch=(), scalars=0, vmem=16, flops=MUCH, far=0, far_outs=0):
        results = call(body, outs, operands, scratch, scalars, tuple(token), vmem, flops, far, far_outs)
        token[0] = results[0]
        return results

    down_come = other_chip(down_theirs)
    up_parts = [second[5]] + [other_copy(value, mask) for mask, value in zip(masks, second[6:])]
    out_come = other_core(send_out)
    grad_middle, gb_own, gain_mlp_part = step(
        middle_back_body,
        [(full, single), (full, bfloat), ((1, width), single)],
        (dwa_weights, middle, keep_norm, other_core(send_norm), cotangent, gain_mlp),
        scalars=1,
        flops=0,
    )
    gb_peer = other_core(gb_own)
    combined, dwa_part = step(
        combine_body,
        [(full, bfloat), ((depth + 1, width), single)],
        (dwa_weights, mixed, middle, keep_out, out_come, cotangent, history_parts),
        scalars=1,
        flops=0,
    )

    def back(weight, qkv_weight, qkv, att, log, flops, before=()):
        return step(
            attend_back,
            [
                ((depth + 3 if before else 1, width), single),
                ((4 * part, width), bfloat),
                ((3 * part, SEQ), bfloat),
            ],
            (
                core, log, cosine, sine, gain_attn, *before, gb_own, gb_peer, *x_own, *x_peer, weight, qkv_weight, qkv,
                att,
            ),
            [
                pltpu.VMEM(tall, bfloat),
                pltpu.VMEM(tall, bfloat),
                pltpu.VMEM((part, width), bfloat),
                pltpu.VMEM((3 * part, width), bfloat),
                pltpu.VMEM((3 * part, SEQ), bfloat),
                pltpu.VMEM((part, SEQ), bfloat),
                pltpu.VMEM((3 * part, SEQ), bfloat),
                pltpu.VMEM((4 * part, width), bfloat),
                pltpu.VMEM((heads, SEQ, SEQ), bfloat),
                pltpu.VMEM((heads, SEQ, SEQ), bfloat),
                pltpu.VMEM((3 * part, width), single),
                marks,
            ],
            1,
            60,
            flops,
            10,
            2,
        )

    gain_part, att_theirs, turned_b = back(out_peer, qkv_peer, qkv_b, att_b, log_b, 0)
    att_come = other_chip(att_theirs)
    def spread(mine, come, flops=MUCH):
        own, *sent = step(part_body, [(fourth, bfloat)] * SQUARE, (owner, mine, come), scalars=1, flops=flops)
        return [own] + [other_copy(value, mask) for mask, value in zip(masks, sent)]

    down_parts = spread(down_mine, down_come, 0)
    up, sent = step(four_two_body, [(fourth, bfloat)] * 2, up_parts, flops=0)
    up_come = other_chip(sent)
    part_sums, att_mine, turned_a = back(
        out_weight, qkv_own, qkv_a, att_a, log_a, MUCH, (gain_part, gain_mlp_part, dwa_part)
    )

    def exchange(value):
        for bit in range(2, bits):
            come = other_copy(value, 1 << bit)
            if bit < bits - 1:
                (value,) = step(low_body, [(value.shape, bfloat)], (value, come))
        return value, come

    def finish(value, come):
        (value,) = step(low_body, [(value.shape, bfloat)], (value, come), flops=COST)
        return [value] + [other_copy(value, mask) for mask in masks]

    (down,) = step(four_body, [(fourth, bfloat)], down_parts, flops=COST)
    down = exchange(down)
    att_parts = spread(att_mine, att_come, COST)
    (up,) = step(low_body, [(fourth, bfloat)], (up, up_come), flops=COST)
    up = exchange(up)
    send_first, keep_first = step(
        first_grad_body,
        [((rows + EXTRA, width), bfloat), (full, single)],
        (core, part_sums, turned_a, turned_b, qkv_own, qkv_peer),
        [pltpu.VMEM((3 * part, SEQ), bfloat)] * 2
        + [pltpu.VMEM((3 * part, width), bfloat)] * 2
        + [pltpu.VMEM(tall, single), marks],
        1,
        60,
        COST,
        4,
        1,
    )
    first_come = other_core(send_first)
    token.append(down[1])
    step(mark_body, [((8, 128), single)], (), flops=COST)
    del token[1:]
    (part_sums,) = step(small_body, [(part_sums.shape, single)], (part_sums, first_come), flops=COST)
    more_sums = other_chip(part_sums)
    (input_grad,) = step(
        first_back_body,
        [(full, bfloat)],
        (inputs, keep_first, first_come, grad_middle, gain_attn),
        vmem=60,
        flops=COST,
    )
    block = (width // SQUARE + EXTRA, width)
    (att,) = step(four_more_body, [(block, bfloat)], (part_sums, more_sums, *att_parts), flops=COST)
    att = exchange(att)
    down = finish(*down)
    token += down[1:]
    pair = (block[0] + fourth[0], width)
    (both,) = step(pair_body, [(pair, bfloat)], (*att, *up), flops=COST)
    del token[1:]
    both = [both] + [other_copy(both, mask) for mask in masks]
    (down_grad,) = step(
        whole_body, [(square, single)], (owner, *down), [pltpu.VMEM(square, bfloat)], 1, flops=COST
    )
    qkv_grad, out_grad, up_grad, gain_attn_grad, gain_mlp_grad, dwa_grad = step(
        more_body,
        [
            ((3 * part, width), single),
            ((part, width), single),
            (square, single),
            ((width,), single),
            ((width,), single),
            ((depth + 1,), single, "scalars"),
        ],
        (owner, *both),
        [pltpu.VMEM((SQUARE * pair[0], width), bfloat)],
        1,
        flops=COST,
    )

    return (
        combined,
        input_grad,
        history_grad,
        qkv_grad.reshape(3, part, width).transpose(2, 0, 1),
        out_grad,
        up_grad,
        down_grad,
        gain_attn_grad,
        gain_mlp_grad,
        dwa_grad,
    )


def solution(mesh):
    placed = (
        P(("dp", "mp"), None),
        P(None, ("dp", "mp"), None),
        P(("dp", "mp"), None),
        P(None, None, "mp"),
        P("mp", None),
        P(None, "mp"),
        P("mp", None),
        P(),
        P(),
        P(),
    )
    return jax.shard_map(
        shards,
        mesh=mesh,
        in_specs=placed,
        out_specs=(
            P(("dp", "mp"), None),
            P(("dp", "mp"), None),
            P(None, ("dp", "mp"), None),
            P(None, None, "mp"),
            P("mp", None),
            P(None, "mp"),
            P("mp", None),
            P(),
            P(),
            P(),
        ),
        check_vma=False,
    )
```

```python
import functools

import jax
import jax.numpy as jnp
import numpy as np
from jax import lax
from jax.experimental import pallas as pl
from jax.experimental.pallas import tpu as pltpu
from jax.sharding import PartitionSpec as P

DH = 64
SEQ = 1152
HALF = SEQ // 2
EPS = 1e-05
bfloat = jnp.bfloat16
single = jnp.float32
MIB = 1 << 20
MUCH = 10**11
COST = 10**10


def tables():
    half_width = DH // 2
    places = np.arange(SEQ, dtype=np.float32)
    frequency = np.float32(10000.0) ** (-np.arange(half_width, dtype=np.float32) * np.float32(2.0 / DH))
    angles = frequency[:, None] * places[None, :]
    return (np.cos(angles).astype(np.float32), np.sin(angles).astype(np.float32))


def mul(a, b, ca=1, cb=0):
    return lax.dot_general(a, b, (((ca,), (cb,)), ((), ())), preferred_element_type=single)


def call(kernel, outs, operands, scratch=(), scalars=0, after=(), vmem=16, flops=0, far=0, far_outs=0):
    count, waits = len(operands), len(after)

    def body(*refs):
        kernel(*refs[:count], *refs[count + waits :])

    small = pl.BlockSpec(memory_space=pltpu.SMEM)
    whole = pl.BlockSpec(memory_space=pltpu.VMEM)
    apart = pl.BlockSpec(memory_space=pltpu.HBM)
    loose = pl.BlockSpec(memory_space=pl.ANY)
    inner = len(outs) - far_outs
    return pl.pallas_call(
        body,
        out_shape=[jax.ShapeDtypeStruct(out[0], out[1]) for out in outs],
        in_specs=[small] * scalars + [whole] * (count - scalars - far) + [apart] * far + [loose] * waits,
        out_specs=[small if len(out) > 2 else whole for out in outs[:inner]] + [apart] * far_outs,
        scratch_shapes=list(scratch),
        compiler_params=pltpu.CompilerParams(vmem_limit_bytes=vmem * MIB),
        cost_estimate=pl.CostEstimate(flops=flops, bytes_accessed=0, transcendentals=0),
    )(*operands, *after)


class Mover:
    def __init__(self, marks):
        self.marks = marks
        self.used = 0

    def __call__(self, *pairs):
        copies = []
        for source, target in pairs:
            copies.append(pltpu.make_async_copy(source, target, self.marks.at[self.used]))
            self.used += 1
        for copy in copies:
            copy.start()
        return copies


def wait(copies):
    for copy in copies:
        copy.wait()


ROWS = 64
PARTS = 1


def spans(rows, step=ROWS):
    return [slice(begin, begin + step) for begin in range(0, rows, step)]


def normal_of(x):
    centre = x - jnp.mean(x, axis=-1, keepdims=True)
    spread = jnp.mean(centre * centre, axis=-1, keepdims=True)
    scale = lax.rsqrt(spread + EPS)
    return centre * scale, scale


def split_body(owner_ref, in_ref, out_ref, hold, marks):
    go = Mover(marks)
    wait(go((in_ref.at[quarter(owner_ref[0], 0, hold.shape[0]), :], hold)))
    wait(go((hold, out_ref)))


def joined(owner, refs, target):
    size = refs[0].shape[0]
    return [(ref, target.at[quarter(owner, mask, size), :]) for mask, ref in enumerate(refs)]


def norm_body(x_ref, gain_ref, *out_refs):
    gain = gain_ref[...].reshape(1, -1)
    for index, out_ref in enumerate(out_refs):
        rows = out_ref.shape[0]
        for span in spans(rows, rows // 6):
            here = slice(index * rows + span.start, index * rows + span.stop)
            normal, _ = normal_of(x_ref[here, :].astype(single))
            out_ref[span, :] = (normal * gain).astype(bfloat)


def scaled_body(mix_ref, cot_ref, out_ref):
    out_ref[...] = (mix_ref[mix_ref.shape[0] - 1] * cot_ref[...]).astype(bfloat)


def middle_body(x_ref, keep_ref, gain_ref, pass_ref, *rest):
    recv_refs, pass_out, mid_ref, out_refs = rest[:PARTS], rest[PARTS], rest[PARTS + 1], rest[PARTS + 2 :]
    pass_out[...] = pass_ref[...]
    gain = gain_ref[...].reshape(1, -1)
    rows = x_ref.shape[0] // PARTS
    for index in range(PARTS):
        for span in spans(rows):
            here = slice(index * rows + span.start, index * rows + span.stop)
            recv = recv_refs[index][span, :].astype(single)
            x = x_ref[here, :].astype(single) + (keep_ref[here, :] + recv)
            mid_ref[here, :] = x
            normal, _ = normal_of(x)
            out_refs[index][span, :] = (normal * gain).astype(bfloat)


def norm_back(x, grad, gain):
    normal, scale = normal_of(x)
    lifted = grad * gain
    back = scale * (
        lifted
        - jnp.mean(lifted, axis=-1, keepdims=True)
        - normal * jnp.mean(lifted * normal, axis=-1, keepdims=True)
    )
    return back, normal


def fold_rows(value):
    total = value[:8]
    for begin in range(8, value.shape[0], 8):
        total = total + value[begin : begin + 8]
    return total


def middle_back_body(mix_ref, x_ref, keep_ref, recv_ref, cot_ref, gain_ref, mid_ref, low_ref, part_ref):
    gain = gain_ref[...].reshape(1, -1)
    part = jnp.zeros((8, x_ref.shape[1]), single)
    for span in spans(x_ref.shape[0]):
        grad = keep_ref[span, :] + recv_ref[span, :].astype(single)
        back, normal = norm_back(x_ref[span, :], grad, gain)
        total = mix_ref[mix_ref.shape[0] - 1] * cot_ref[span, :] + back
        mid_ref[span, :] = total
        low_ref[span, :] = total.astype(bfloat)
        part = part + fold_rows(grad * normal)
    part_ref[...] = jnp.sum(part, axis=0, keepdims=True)


def first_back_body(x_ref, keep_ref, recv_ref, mid_ref, gain_ref, out_ref):
    gain = gain_ref[...].reshape(1, -1)
    for span in spans(x_ref.shape[0]):
        grad = keep_ref[span, :] + recv_ref[span, :].astype(single)
        back, _ = norm_back(x_ref[span, :].astype(single), grad, gain)
        out_ref[span, :] = (mid_ref[span, :] + back).astype(bfloat)


def history_body(mix_ref, history_ref, cot_ref, grad_ref, mixed_ref, part_ref):
    depth = history_ref.shape[0]

    @pl.when(pl.program_id(0) == 0)
    def _():
        part_ref[...] = jnp.zeros_like(part_ref)

    for span in spans(cot_ref.shape[0], 32):
        cot = cot_ref[span, :]
        mixed = None
        for j in range(depth):
            layer = history_ref[j, span, :].astype(single)
            mixed = mix_ref[j] * layer if mixed is None else mixed + mix_ref[j] * layer
            grad_ref[j, span, :] = (mix_ref[j] * cot).astype(bfloat)
            part_ref[8 * j : 8 * j + 8, :] += fold_rows(layer * cot)
        mixed_ref[span, :] = mixed


def average_history(mix, history, cot, after=()):
    depth, rows, width = history.shape
    step = 96
    waits = len(after)

    def body(*refs):
        history_body(*refs[:3], *refs[3 + waits :])

    row_block = pl.BlockSpec((step, width), lambda i: (i, 0))
    deep_block = pl.BlockSpec((depth, step, width), lambda i: (0, i, 0))
    return pl.pallas_call(
        body,
        grid=(rows // step,),
        out_shape=[
            jax.ShapeDtypeStruct(history.shape, bfloat),
            jax.ShapeDtypeStruct((rows, width), single),
            jax.ShapeDtypeStruct((8 * depth, width), single),
        ],
        in_specs=[pl.BlockSpec(memory_space=pltpu.SMEM), deep_block, row_block]
        + [pl.BlockSpec(memory_space=pl.ANY)] * waits,
        out_specs=[deep_block, row_block, pl.BlockSpec((8 * depth, width), lambda i: (0, 0))],
        compiler_params=pltpu.CompilerParams(vmem_limit_bytes=60 * MIB),
        cost_estimate=pl.CostEstimate(flops=0, bytes_accessed=0, transcendentals=0),
    )(mix, history, cot, *after)


def combine_body(mix_ref, mixed_ref, mid_ref, keep_ref, recv_ref, cot_ref, parts_ref, out_ref, part_ref):
    depth = mix_ref.shape[0] - 1
    last = jnp.zeros((8, mid_ref.shape[1]), single)
    for span in spans(mid_ref.shape[0]):
        outputs = mid_ref[span, :] + (keep_ref[span, :] + recv_ref[span, :].astype(single))
        out_ref[span, :] = (mixed_ref[span, :] + mix_ref[depth] * outputs).astype(bfloat)
        last = last + fold_rows(outputs * cot_ref[span, :])
    for j in range(depth):
        part_ref[j : j + 1, :] = jnp.sum(parts_ref[8 * j : 8 * j + 8, :], axis=0, keepdims=True)
    part_ref[depth : depth + 1, :] = jnp.sum(last, axis=0, keepdims=True)


SQUARE = 4


def quarter(owner, mask, size):
    other = owner + (mask & 1) * (1 - 2 * (owner % 2)) + (mask & 2) * (1 - 2 * (owner // 2))
    return pl.ds(pl.multiple_of(other * size, size), size)


def part_body(owner_ref, mine_ref, come_ref, *out_refs):
    for mask, out_ref in enumerate(out_refs):
        rows = quarter(owner_ref[0], mask, out_ref.shape[0])
        out_ref[...] = (mine_ref[rows, :].astype(single) + come_ref[rows, :].astype(single)).astype(bfloat)


def sum_of(refs, rows):
    total = refs[0][rows, :].astype(single)
    for ref in refs[1:]:
        total = total + ref[rows, :].astype(single)
    return total


def four_body(*refs):
    refs[-1][...] = sum_of(refs[:-1], slice(None)).astype(bfloat)


def four_two_body(*refs):
    size = refs[-1].shape[0]
    refs[-2][...] = sum_of(refs[:-2], slice(0, size)).astype(bfloat)
    refs[-1][...] = sum_of(refs[:-2], slice(size, 2 * size)).astype(bfloat)


EXTRA = 16


def mark_body(out_ref):
    out_ref[...] = jnp.zeros_like(out_ref)


def small_body(small_ref, first_ref, out_ref):
    half = small_ref.shape[0]
    rows = first_ref.shape[0] - 2 * half
    come = first_ref[rows:, :].astype(single)
    out_ref[...] = small_ref[...] + (come[:half] + come[half:])


def four_more_body(small_ref, more_ref, *refs):
    out_ref = refs[-1]
    size = out_ref.shape[0] - EXTRA
    out_ref[:size, :] = sum_of(refs[:-1], slice(None)).astype(bfloat)
    small = small_ref[...] + more_ref[...]
    rest = jnp.zeros((EXTRA - small.shape[0], small.shape[1]), single)
    out_ref[size:, :] = jnp.concatenate([small, rest], axis=0).astype(bfloat)


def gather(owner_ref, pieces, hold):
    for mask, piece in enumerate(pieces):
        hold[quarter(owner_ref[0], mask, piece.shape[0]), :] = piece[...]


def pair_body(a_ref, a_come_ref, b_ref, b_come_ref, out_ref):
    size = a_ref.shape[0]
    out_ref[:size, :] = sum_of((a_ref, a_come_ref), slice(None)).astype(bfloat)
    out_ref[size:, :] = sum_of((b_ref, b_come_ref), slice(None)).astype(bfloat)


def whole_body(owner_ref, a_ref, b_ref, c_ref, d_ref, out_ref, hold):
    gather(owner_ref, (a_ref, b_ref, c_ref, d_ref), hold)
    out_ref[...] = hold[...].astype(single)


def more_body(owner_ref, a_ref, b_ref, c_ref, d_ref, top_ref, end_ref, up_ref, attn_ref, mlp_ref, dwa_ref, hold):
    gather(owner_ref, (a_ref, b_ref, c_ref, d_ref), hold)
    block = hold.shape[0] // SQUARE
    rows = up_ref.shape[0] // SQUARE
    small = jnp.zeros((EXTRA, hold.shape[1]), single)
    for index in range(SQUARE):
        begin = index * block
        target, place = (top_ref, index * rows) if index < SQUARE - 1 else (end_ref, 0)
        target[place : place + rows, :] = hold[begin : begin + rows, :].astype(single)
        small = small + hold[begin + rows : begin + rows + EXTRA, :].astype(single)
        up_ref[index * rows : (index + 1) * rows, :] = hold[begin + rows + EXTRA : begin + block, :].astype(single)
    attn_ref[...] = small[0]
    mlp_ref[...] = small[1]
    for index in range(dwa_ref.shape[0]):
        dwa_ref[index] = jnp.sum(small[2 + index : 3 + index])


def low_body(mine_ref, come_ref, out_ref):
    out_ref[...] = (mine_ref[...].astype(single) + come_ref[...].astype(single)).astype(bfloat)


def mark_body(out_ref):
    out_ref[...] = jnp.zeros_like(out_ref)


def small_body(small_ref, first_ref, out_ref):
    half = small_ref.shape[0]
    rows = first_ref.shape[0] - 2 * half
    come = first_ref[rows:, :].astype(single)
    out_ref[...] = small_ref[...] + (come[:half] + come[half:])


BLOCKS = tuple((begin, min(256, SEQ - begin)) for begin in range(0, SEQ, 256))


def places(core_ref, refs):
    count, size = len(refs) // 2, refs[0].shape[0]
    for index, ref in enumerate(refs):
        core = core_ref[0] if index < count else 1 - core_ref[0]
        yield ref, pl.ds(pl.multiple_of(core * HALF + index % count * size, size), size)


def allowed(size):
    key_pos = lax.broadcasted_iota(jnp.int32, (size, size), 0)
    query_pos = lax.broadcasted_iota(jnp.int32, (size, size), 1)
    return query_pos >= key_pos


def turn(rows, cosine, sine):
    half = rows.shape[0] // 2
    a, b = rows[:half], rows[half:]
    return jnp.concatenate([a * cosine - b * sine, b * cosine + a * sine], axis=0)


KEYS = 128


def fold_top(value):
    top = value[:8]
    for begin in range(8, value.shape[0], 8):
        top = jnp.maximum(top, value[begin : begin + 8])
    return top


def masked(scores, offset):
    key_pos = lax.broadcasted_iota(jnp.int32, scores.shape, 0) + offset
    query_pos = lax.broadcasted_iota(jnp.int32, scores.shape, 1)
    return jnp.where(query_pos >= key_pos, scores, -jnp.inf)


def attend_placed(core_ref, *rest):
    for ref, where in places(core_ref, rest[:4]):
        rest[11][where, :] = ref[...]
    cos_ref, sin_ref, weight_ref, rest = rest[4], rest[5], rest[6], rest[7:]
    attend(weight_ref, cos_ref, sin_ref, *rest)


def attend(weight_ref, cos_ref, sin_ref, qkv_ref, att_ref, nat_ref, log_ref, tokens, all_scores, all_weights):
    width = weight_ref.shape[0] // 3
    projected = mul(weight_ref[...], tokens[...], 1, 1)
    cosine, sine = cos_ref[...], sin_ref[...]
    for part in range(3):
        for head in range(width // DH):
            begin = part * width + head * DH
            rows = projected[begin : begin + DH]
            if part < 2:
                rows = turn(rows, cosine, sine)
            if part == 0:
                rows = rows * DH ** (-0.5)
            qkv_ref[begin : begin + DH, :] = rows.astype(bfloat)
    log_ref[...] = jnp.zeros_like(log_ref)
    heads = range(width // DH)
    keys = [qkv_ref[width + head * DH : width + head * DH + DH, :].T for head in heads]
    for begin, size in BLOCKS:
        end = begin + size
        tops = [None for _ in heads]
        for row in range(0, end, KEYS):
            for head in heads:
                tile = mul(keys[head][row : row + KEYS], qkv_ref[head * DH : head * DH + DH, begin:end])
                if row >= begin:
                    tile = masked(tile, row - begin)
                all_scores[head, row : row + KEYS, :size] = tile
                top = fold_top(tile)
                tops[head] = top if row == 0 else jnp.maximum(tops[head], top)
        tops = [jnp.max(top, axis=0, keepdims=True) for top in tops]
        totals = [jnp.zeros((8, size), single) for _ in heads]
        for row in range(0, end, KEYS):
            for head in heads:
                tile = jnp.exp(all_scores[head, row : row + KEYS, :size] - tops[head])
                totals[head] = totals[head] + fold_rows(tile)
                all_weights[head, row : row + KEYS, :size] = tile.astype(bfloat)
        for head in heads:
            base = head * DH
            total = jnp.sum(totals[head], axis=0, keepdims=True)
            value = qkv_ref[2 * width + base : 2 * width + base + DH, :end]
            mixed = mul(value, all_weights[head, :end, :size]) / total
            att_ref[base : base + DH, begin:end] = mixed.astype(bfloat)
            log_ref[head : head + 1, begin:end] = tops[head] + jnp.log(total)
    nat_ref[...] = att_ref[...].T


def branch_body(core_ref, att_a_ref, att_b_ref, out_a_ref, out_b_ref, keep_ref, *send_refs):
    low = pl.multiple_of(core_ref[0] * HALF, HALF)
    rows = HALF // PARTS
    for index in range(PARTS):
        high = pl.multiple_of((1 - core_ref[0]) * HALF + index * rows, rows)
        send = mul(att_a_ref[pl.ds(high, rows), :], out_a_ref[...])
        send_refs[index][...] = (send + mul(att_b_ref[pl.ds(high, rows), :], out_b_ref[...])).astype(bfloat)
    keep = mul(att_a_ref[pl.ds(low, HALF), :], out_a_ref[...])
    keep_ref[...] = keep + mul(att_b_ref[pl.ds(low, HALF), :], out_b_ref[...])


def attend_back(
    core_ref, log_ref, cos_ref, sin_ref, gain_ref, *rest
):
    before_refs, rest = rest[:-25], rest[-25:]
    grad_refs, x_refs = rest[:2], rest[2:6]
    weight_ref, qkv_weight_ref, qkv_ref, att_ref, small_ref, out_ref, turned_ref = rest[6:13]
    grads, tokens, weight, qkv_weight, qkv, att, turned, result, all_probs, all_scores, hold, marks = rest[13:]
    go = Mover(marks)
    first = go(
        (weight_ref, weight),
        *[(ref, grads.at[where, :]) for ref, where in places(core_ref, grad_refs)],
        (att_ref, att),
        (qkv_ref, qkv),
    )
    later = go(
        *[(ref, tokens.at[where, :]) for ref, where in places(core_ref, x_refs)],
        (qkv_weight_ref, qkv_weight),
    )
    wait(first)
    width = att.shape[0]
    grad_att = mul(weight[...], grads[...], 1, 1).astype(bfloat)
    result[3 * width :, :] = mul(att[...], grads[...]).astype(result.dtype)
    cosine, sine = cos_ref[...], sin_ref[...]
    heads = range(width // DH)
    spans_of = [slice(head * DH, head * DH + DH) for head in heads]
    query = [qkv[span, :] for span in spans_of]
    key = [qkv[width + span.start : width + span.stop, :] for span in spans_of]
    above = [grad_att[span] for span in spans_of]
    centre = [
        jnp.sum(above[head].astype(single) * att[span, :].astype(single), axis=0, keepdims=True)
        for head, span in enumerate(spans_of)
    ]
    keys = [value.T for value in key]
    values = [qkv[2 * width + span.start : 2 * width + span.stop, :].T for span in spans_of]
    queries = [value.T for value in query]
    aboves = [value.T for value in above]
    grad_query = [[] for _ in heads]
    for begin, size in BLOCKS:
        end = begin + size
        for row in range(0, end, KEYS):
            span = slice(row, row + KEYS)
            for head in heads:
                tile = mul(keys[head][span], query[head][:, begin:end])
                if row >= begin:
                    tile = masked(tile, row - begin)
                tile = jnp.exp(tile - log_ref[head : head + 1, begin:end])
                grad = mul(values[head][span], above[head][:, begin:end]) - centre[head][:, begin:end]
                all_probs[head, span, begin:end] = tile.astype(bfloat)
                all_scores[head, span, begin:end] = (tile * grad).astype(bfloat)
        for head in heads:
            grad_query[head].append(mul(key[head][:, :end], all_scores[head, :end, begin:end]))
    grad_key = [[] for _ in heads]
    grad_value = [[] for _ in heads]
    for begin, size in BLOCKS:
        span = slice(begin, begin + size)
        for head in heads:
            grad_key[head].append(mul(all_scores[head, span, begin:], queries[head][begin:]))
            grad_value[head].append(mul(all_probs[head, span, begin:], aboves[head][begin:]))
    for head, span in enumerate(spans_of):
        grad = jnp.concatenate(grad_query[head], axis=1) * DH ** (-0.5)
        turned[span, :] = turn(grad, cosine, -sine).astype(bfloat)
        grad = jnp.concatenate(grad_key[head], axis=0).T
        turned[width + span.start : width + span.stop, :] = turn(grad, cosine, -sine).astype(bfloat)
        grad = jnp.concatenate(grad_value[head], axis=0).T
        turned[2 * width + span.start : 2 * width + span.stop, :] = grad.astype(bfloat)
    stores = go((turned, turned_ref))
    wait(later)
    hold[...] = mul(turned[...], tokens[...])
    result[: 3 * width, :] = hold[...].astype(result.dtype)
    stores += go((result, out_ref))
    part = jnp.zeros((8, hold.shape[1]), single)
    for span in spans(hold.shape[0]):
        part = part + fold_rows(hold[span, :] * qkv_weight[span, :].astype(single))
    gain = jnp.sum(part, axis=0, keepdims=True) / gain_ref[...].reshape(1, -1)
    if before_refs:
        gain_part_ref, mlp_part_ref, dwa_part_ref = before_refs
        small_ref[:1, :] = gain + gain_part_ref[...]
        small_ref[1:2, :] = mlp_part_ref[...]
        small_ref[2:, :] = dwa_part_ref[...]
    else:
        small_ref[...] = gain
    wait(stores)


def first_grad_body(
    core_ref, small_ref, turned_a_ref, turned_b_ref, weight_a_ref, weight_b_ref, send_ref, keep_ref,
    turned_a, turned_b, weight_a, weight_b, whole, marks,
):
    low = pl.multiple_of(core_ref[0] * HALF, HALF)
    high = pl.multiple_of((1 - core_ref[0]) * HALF, HALF)
    go = Mover(marks)
    wait(go((turned_a_ref, turned_a), (weight_a_ref, weight_a), (turned_b_ref, turned_b), (weight_b_ref, weight_b)))
    whole[...] = mul(turned_a[...], weight_a[...], 0, 0) + mul(turned_b[...], weight_b[...], 0, 0)
    stores = go((whole.at[pl.ds(low, HALF), :], keep_ref))
    send_ref[:HALF, :] = whole[pl.ds(high, HALF), :].astype(bfloat)
    small = small_ref[...]
    high_part = small.astype(bfloat)
    low_part = (small - high_part.astype(single)).astype(bfloat)
    send_ref[HALF:, :] = jnp.concatenate([high_part, low_part], axis=0)
    wait(stores)


CURVE = float(np.sqrt(2.0 / np.pi))
STEP = 256


def mlp_body(second, *refs):
    if second:
        owner_ref, refs = refs[0], refs[1:]
    x_refs, refs = refs[: 2 * PARTS], refs[2 * PARTS :]
    g_own_ref, g_peer_ref, refs = refs[0], refs[1], refs[2:]
    if second:
        up_ref, down_refs, refs = refs[0], refs[1 : 1 + SQUARE], refs[1 + SQUARE :]
        before_refs, up_mine_ref = refs[:4], refs[4]
        down_grad_ref, part_refs = refs[9], refs[10:14]
        refs = refs[5:9] + refs[14:]
    else:
        up_ref, down_ref = refs[:2]
        down_grad_ref, up_grad_ref = refs[6:8]
        refs = refs[2:6] + refs[8:]
    send_norm_ref, keep_norm_ref, send_out_ref, keep_out_ref = refs[:4]
    x_all, g_all, up, down, active, grad_hidden, x_turned = refs[4:11]
    send_norm, keep_norm, send_out, keep_out, down_grad, up_grad, marks = refs[11:18]
    rows, size = x_all.shape[0] // 2, x_all.shape[0] // (2 * PARTS)
    units = down.shape[0]
    go = Mover(marks)
    x_loads = go(*[(x_refs[index], x_all.at[pl.ds(index * size, size), :]) for index in range(2 * PARTS)])
    if second:
        loads = go((up_ref, up), *joined(owner_ref[0], down_refs, down))
    else:
        loads = go((up_ref, up), (down_ref, down))
    loads += go((g_own_ref, g_all.at[pl.ds(0, rows), :]), (g_peer_ref, g_all.at[pl.ds(rows, rows), :]))
    more, mine, stores = [], [], []
    if second:
        (up_mine,) = refs[18:]
        more = go(*zip(before_refs, (send_norm, keep_norm, send_out, keep_out)))
        mine = go((up_mine_ref, up_mine))
    wait(x_loads)
    x_turned[...] = x_all[...].T
    wait(loads)
    for begin in range(0, units, STEP):
        columns = slice(begin, begin + STEP)
        for top in range(0, 2 * rows, rows):
            span = slice(top, top + rows)
            v = mul(x_all[span, :], up[:, columns])
            grad = mul(g_all[span, :], down[columns, :], 1, 1)
            square = v * v
            half = 0.5 + 0.5 * jnp.tanh(v * (CURVE + (CURVE * 0.044715) * square))
            act = v * half
            slope = half + act * (1.0 - half) * (2.0 * CURVE + (6.0 * CURVE * 0.044715) * square)
            active[span, columns] = act.astype(bfloat)
            grad_hidden[span, columns] = (grad * slope).astype(bfloat)

    def put(target, value):
        target[...] = (value + target[...].astype(single) if second else value).astype(target.dtype)

    wait(more)
    put(keep_norm, mul(grad_hidden[:rows, :], up[...], 1, 1))
    put(send_norm, mul(grad_hidden[rows:, :], up[...], 1, 1))
    stores += go((keep_norm, keep_norm_ref), (send_norm, send_norm_ref))
    down_grad[...] = mul(active[...], g_all[...], 0, 0).astype(down_grad.dtype)
    stores += go((down_grad, down_grad_ref))
    up_grad[...] = mul(x_turned[...], grad_hidden[...]).astype(bfloat)
    if second:
        wait(mine)
        part = up_grad.shape[0] // SQUARE
        for mask, part_ref in enumerate(part_refs):
            rows_of = quarter(owner_ref[0], mask, part)
            stores += go(
                (up_mine.at[rows_of, :], part_ref.at[pl.ds(0, part), :]),
                (up_grad.at[rows_of, :], part_ref.at[pl.ds(part, part), :]),
            )
    else:
        stores += go((up_grad, up_grad_ref))
    put(keep_out, mul(active[:rows, :], down[...]))
    stores += go((keep_out, keep_out_ref))
    put(send_out, mul(active[rows:, :], down[...]))
    wait(stores + go((send_out, send_out_ref)))


def mlp(x_own, x_peer, g_own, g_peer, up, down, upper=(), before=(), after=()):
    rows, width = g_own.shape
    units = sum(piece.shape[0] for piece in down)
    tall = (2 * rows, width)
    pair = [((rows, width), bfloat), ((rows, width), single)] * 2
    outs = pair + [((units, width), bfloat)]
    outs += [((2 * width // SQUARE, units), bfloat)] * SQUARE if before else [((width, units), bfloat)]
    scratch = [
        pltpu.VMEM(tall, bfloat),
        pltpu.VMEM(tall, bfloat),
        pltpu.VMEM((width, units), bfloat),
        pltpu.VMEM((units, width), bfloat),
        pltpu.VMEM((2 * rows, units), bfloat),
        pltpu.VMEM((2 * rows, units), bfloat),
        pltpu.VMEM((width, 2 * rows), bfloat),
    ]
    scratch += [pltpu.VMEM(shape, kind) for shape, kind in pair]
    scratch += [
        pltpu.VMEM((units, width), bfloat), pltpu.VMEM((width, units), bfloat), pltpu.SemaphoreType.DMA((32,)),
    ]
    if before:
        scratch.append(pltpu.VMEM((width, units), bfloat))
    operands = (*upper, *x_own, *x_peer, g_own, g_peer, *up, *down, *before)
    return call(
        functools.partial(mlp_body, bool(before)),
        outs,
        operands,
        scratch,
        len(upper),
        after,
        60,
        far=len(operands) - len(upper),
        far_outs=len(outs),
    )


def shards(
    inputs,
    history,
    cotangent,
    qkv_weight,
    out_weight,
    up_weight,
    down_weight,
    gain_attn,
    gain_mlp,
    dwa_weights,
):
    rows, width = inputs.shape
    members = lax.axis_size("mp")
    copies = lax.axis_size("dp")
    bits = copies.bit_length() - 1
    core = lax.rem(lax.axis_index("mp"), 2).astype(jnp.int32).reshape(1)
    copy_index = lax.axis_index("dp").astype(jnp.int32).reshape(1)
    core_pairs = [(i, i ^ 1) for i in range(members)]
    chip_pairs = [(i, i ^ 2) for i in range(members)]
    depth = history.shape[0]
    part = out_weight.shape[0]

    def other_core(value):
        return lax.ppermute(value, "mp", core_pairs)

    def other_chip(value):
        return lax.ppermute(value, "mp", chip_pairs)

    def other_copy(value, mask):
        return lax.ppermute(value, "dp", [(i, i ^ mask) for i in range(copies)])

    owner = copy_index & (SQUARE - 1)
    cosine, sine = (jnp.asarray(table) for table in tables())

    qkv_own = qkv_weight.transpose(1, 2, 0).reshape(3 * part, width)
    fourth = (width // SQUARE, width)
    square = (width, width)
    masks = range(1, SQUARE)
    marks = pltpu.SemaphoreType.DMA((16,))
    (down_quarter,) = call(
        split_body,
        [(fourth, bfloat)],
        (owner, down_weight),
        [pltpu.VMEM(fourth, bfloat), marks],
        1,
        vmem=60,
        far=1,
        far_outs=1,
    )
    qkv_peer, out_peer = other_chip(qkv_own), other_chip(out_weight)
    down_come, up_peer = other_chip(down_quarter), other_chip(up_weight)

    full = (rows, width)
    x_own = call(norm_body, [((rows // 2, width), bfloat)] * 2, (inputs, gain_attn), after=(down_quarter,))
    x_peer = [other_core(value) for value in x_own]
    tall = (SEQ, width)
    tokens = pltpu.VMEM(tall, bfloat)
    first_outs = [
        ((3 * part, SEQ), bfloat), ((part, SEQ), bfloat), ((SEQ, part), bfloat), ((8, SEQ), single),
    ]
    heads = part // DH
    tiles = [tokens, pltpu.VMEM((heads, SEQ, 256), single), pltpu.VMEM((heads, SEQ, 256), bfloat)]
    qkv_a, att_a, nat_a, log_a = call(
        attend_placed, first_outs, (core, *x_own, *x_peer, cosine, sine, qkv_own), tiles, 1, vmem=32
    )
    (g_own,) = call(scaled_body, [(full, bfloat)], (dwa_weights, cotangent), scalars=1, after=(log_a,))
    g_peer = other_core(g_own)
    qkv_b, att_b, nat_b, log_b = call(
        attend_placed,
        first_outs,
        (core, *x_own, *x_peer, cosine, sine, qkv_peer),
        tiles,
        1,
        (g_own,),
        32,
        MUCH,
    )
    third = (rows // PARTS, width)
    keep, *send = call(
        branch_body,
        [(full, single)] + [(third, bfloat)] * PARTS,
        (core, nat_a, nat_b, out_weight, out_peer),
        (),
        1,
        (g_peer,),
    )
    recv = [other_core(value) for value in send]
    down_copy, middle, *y_own = call(
        middle_body,
        [(fourth, bfloat), (full, single)] + [(third, bfloat)] * PARTS,
        (inputs, keep, gain_mlp, down_come, *recv),
    )
    down_pieces = [down_come] + [other_copy(down_copy, mask) for mask in masks]
    y_peer = [other_core(value) for value in y_own]

    first = mlp(y_own, y_peer, g_own, g_peer, (up_weight,), (down_weight,))
    down_mine, up_mine = first[4:]
    history_grad, mixed, history_parts = average_history(dwa_weights, history, cotangent, (first[0],))
    second = mlp(
        y_own, y_peer, g_own, g_peer, (up_peer,), down_pieces, (owner,), (*first[:4], up_mine),
        after=(history_parts,),
    )
    send_norm, keep_norm, send_out, keep_out, down_theirs = second[:5]
    token = [send_norm]

    def step(body, outs, operands, scratch=(), scalars=0, vmem=16, flops=MUCH, far=0, far_outs=0):
        results = call(body, outs, operands, scratch, scalars, tuple(token), vmem, flops, far, far_outs)
        token[0] = results[0]
        return results

    down_come = other_chip(down_theirs)
    up_parts = [second[5]] + [other_copy(value, mask) for mask, value in zip(masks, second[6:])]
    out_come = other_core(send_out)
    grad_middle, gb_own, gain_mlp_part = step(
        middle_back_body,
        [(full, single), (full, bfloat), ((1, width), single)],
        (dwa_weights, middle, keep_norm, other_core(send_norm), cotangent, gain_mlp),
        scalars=1,
        flops=0,
    )
    gb_peer = other_core(gb_own)
    combined, dwa_part = step(
        combine_body,
        [(full, bfloat), ((depth + 1, width), single)],
        (dwa_weights, mixed, middle, keep_out, out_come, cotangent, history_parts),
        scalars=1,
        flops=0,
    )

    def back(weight, qkv_weight, qkv, att, log, flops, before=()):
        return step(
            attend_back,
            [
                ((depth + 3 if before else 1, width), single),
                ((4 * part, width), bfloat),
                ((3 * part, SEQ), bfloat),
            ],
            (
                core, log, cosine, sine, gain_attn, *before, gb_own, gb_peer, *x_own, *x_peer, weight, qkv_weight, qkv,
                att,
            ),
            [
                pltpu.VMEM(tall, bfloat),
                pltpu.VMEM(tall, bfloat),
                pltpu.VMEM((part, width), bfloat),
                pltpu.VMEM((3 * part, width), bfloat),
                pltpu.VMEM((3 * part, SEQ), bfloat),
                pltpu.VMEM((part, SEQ), bfloat),
                pltpu.VMEM((3 * part, SEQ), bfloat),
                pltpu.VMEM((4 * part, width), bfloat),
                pltpu.VMEM((heads, SEQ, SEQ), bfloat),
                pltpu.VMEM((heads, SEQ, SEQ), bfloat),
                pltpu.VMEM((3 * part, width), single),
                marks,
            ],
            1,
            60,
            flops,
            10,
            2,
        )

    gain_part, att_theirs, turned_b = back(out_peer, qkv_peer, qkv_b, att_b, log_b, 0)
    att_come = other_chip(att_theirs)
    def spread(mine, come, flops=MUCH):
        own, *sent = step(part_body, [(fourth, bfloat)] * SQUARE, (owner, mine, come), scalars=1, flops=flops)
        return [own] + [other_copy(value, mask) for mask, value in zip(masks, sent)]

    down_parts = spread(down_mine, down_come, 0)
    up, sent = step(four_two_body, [(fourth, bfloat)] * 2, up_parts, flops=0)
    up_come = other_chip(sent)
    part_sums, att_mine, turned_a = back(
        out_weight, qkv_own, qkv_a, att_a, log_a, MUCH, (gain_part, gain_mlp_part, dwa_part)
    )

    def exchange(value):
        for bit in range(2, bits):
            come = other_copy(value, 1 << bit)
            if bit < bits - 1:
                (value,) = step(low_body, [(value.shape, bfloat)], (value, come))
        return value, come

    def finish(value, come):
        (value,) = step(low_body, [(value.shape, bfloat)], (value, come), flops=COST)
        return [value] + [other_copy(value, mask) for mask in masks]

    (down,) = step(four_body, [(fourth, bfloat)], down_parts, flops=COST)
    down = exchange(down)
    att_parts = spread(att_mine, att_come, COST)
    (up,) = step(low_body, [(fourth, bfloat)], (up, up_come), flops=COST)
    up = exchange(up)
    send_first, keep_first = step(
        first_grad_body,
        [((rows + EXTRA, width), bfloat), (full, single)],
        (core, part_sums, turned_a, turned_b, qkv_own, qkv_peer),
        [pltpu.VMEM((3 * part, SEQ), bfloat)] * 2
        + [pltpu.VMEM((3 * part, width), bfloat)] * 2
        + [pltpu.VMEM(tall, single), marks],
        1,
        60,
        COST,
        4,
        1,
    )
    first_come = other_core(send_first)
    token.append(down[1])
    step(mark_body, [((8, 128), single)], (), flops=COST)
    del token[1:]
    (part_sums,) = step(small_body, [(part_sums.shape, single)], (part_sums, first_come), flops=COST)
    more_sums = other_chip(part_sums)
    (input_grad,) = step(
        first_back_body,
        [(full, bfloat)],
        (inputs, keep_first, first_come, grad_middle, gain_attn),
        vmem=60,
        flops=COST,
    )
    block = (width // SQUARE + EXTRA, width)
    (att,) = step(four_more_body, [(block, bfloat)], (part_sums, more_sums, *att_parts), flops=COST)
    att = exchange(att)
    down = finish(*down)
    token += down[1:]
    pair = (block[0] + fourth[0], width)
    (both,) = step(pair_body, [(pair, bfloat)], (*att, *up), flops=COST)
    del token[1:]
    both = [both] + [other_copy(both, mask) for mask in masks]
    (down_grad,) = step(
        whole_body, [(square, single)], (owner, *down), [pltpu.VMEM(square, bfloat)], 1, flops=COST
    )
    qkv_grad, out_grad, up_grad, gain_attn_grad, gain_mlp_grad, dwa_grad = step(
        more_body,
        [
            ((3 * part, width), single),
            ((part, width), single),
            (square, single),
            ((width,), single),
            ((width,), single),
            ((depth + 1,), single, "scalars"),
        ],
        (owner, *both),
        [pltpu.VMEM((SQUARE * pair[0], width), bfloat)],
        1,
        flops=COST,
    )

    return (
        combined,
        input_grad,
        history_grad,
        qkv_grad.reshape(3, part, width).transpose(2, 0, 1),
        out_grad,
        up_grad,
        down_grad,
        gain_attn_grad,
        gain_mlp_grad,
        dwa_grad,
    )


def solution(mesh):
    placed = (
        P(("dp", "mp"), None),
        P(None, ("dp", "mp"), None),
        P(("dp", "mp"), None),
        P(None, None, "mp"),
        P("mp", None),
        P(None, "mp"),
        P("mp", None),
        P(),
        P(),
        P(),
    )
    return jax.shard_map(
        shards,
        mesh=mesh,
        in_specs=placed,
        out_specs=(
            P(("dp", "mp"), None),
            P(("dp", "mp"), None),
            P(None, ("dp", "mp"), None),
            P(None, None, "mp"),
            P("mp", None),
            P(None, "mp"),
            P("mp", None),
            P(),
            P(),
            P(),
        ),
        check_vma=False,
    )
```

```python
import functools

import jax
import jax.numpy as jnp
import numpy as np
from jax import lax
from jax.experimental import pallas as pl
from jax.experimental.pallas import tpu as pltpu
from jax.sharding import PartitionSpec as P

DH = 64
SEQ = 1152
HALF = SEQ // 2
EPS = 1e-05
bfloat = jnp.bfloat16
single = jnp.float32
MIB = 1 << 20
MUCH = 10**11
COST = 10**10


def tables():
    half_width = DH // 2
    places = np.arange(SEQ, dtype=np.float32)
    frequency = np.float32(10000.0) ** (-np.arange(half_width, dtype=np.float32) * np.float32(2.0 / DH))
    angles = frequency[:, None] * places[None, :]
    return (np.cos(angles).astype(np.float32), np.sin(angles).astype(np.float32))


def mul(a, b, ca=1, cb=0):
    return lax.dot_general(a, b, (((ca,), (cb,)), ((), ())), preferred_element_type=single)


def call(kernel, outs, operands, scratch=(), scalars=0, after=(), vmem=16, flops=0, far=0, far_outs=0):
    count, waits = len(operands), len(after)

    def body(*refs):
        kernel(*refs[:count], *refs[count + waits :])

    small = pl.BlockSpec(memory_space=pltpu.SMEM)
    whole = pl.BlockSpec(memory_space=pltpu.VMEM)
    apart = pl.BlockSpec(memory_space=pltpu.HBM)
    loose = pl.BlockSpec(memory_space=pl.ANY)
    inner = len(outs) - far_outs
    return pl.pallas_call(
        body,
        out_shape=[jax.ShapeDtypeStruct(out[0], out[1]) for out in outs],
        in_specs=[small] * scalars + [whole] * (count - scalars - far) + [apart] * far + [loose] * waits,
        out_specs=[small if len(out) > 2 else whole for out in outs[:inner]] + [apart] * far_outs,
        scratch_shapes=list(scratch),
        compiler_params=pltpu.CompilerParams(vmem_limit_bytes=vmem * MIB),
        cost_estimate=pl.CostEstimate(flops=flops, bytes_accessed=0, transcendentals=0),
    )(*operands, *after)


class Mover:
    def __init__(self, marks):
        self.marks = marks
        self.used = 0

    def __call__(self, *pairs):
        copies = []
        for source, target in pairs:
            copies.append(pltpu.make_async_copy(source, target, self.marks.at[self.used]))
            self.used += 1
        for copy in copies:
            copy.start()
        return copies


def wait(copies):
    for copy in copies:
        copy.wait()


ROWS = 64
PARTS = 1


def spans(rows, step=ROWS):
    return [slice(begin, begin + step) for begin in range(0, rows, step)]


def normal_of(x):
    centre = x - jnp.mean(x, axis=-1, keepdims=True)
    spread = jnp.mean(centre * centre, axis=-1, keepdims=True)
    scale = lax.rsqrt(spread + EPS)
    return centre * scale, scale


def split_body(owner_ref, in_ref, out_ref, hold, marks):
    go = Mover(marks)
    wait(go((in_ref.at[quarter(owner_ref[0], 0, hold.shape[0]), :], hold)))
    wait(go((hold, out_ref)))


def joined(owner, refs, target):
    size = refs[0].shape[0]
    return [(ref, target.at[quarter(owner, mask, size), :]) for mask, ref in enumerate(refs)]


def norm_body(x_ref, gain_ref, *out_refs):
    gain = gain_ref[...].reshape(1, -1)
    for index, out_ref in enumerate(out_refs):
        rows = out_ref.shape[0]
        for span in spans(rows, rows // 6):
            here = slice(index * rows + span.start, index * rows + span.stop)
            normal, _ = normal_of(x_ref[here, :].astype(single))
            out_ref[span, :] = (normal * gain).astype(bfloat)


def middle_body(x_ref, keep_ref, gain_ref, *rest):
    recv_refs, mid_ref, out_refs = rest[:PARTS], rest[PARTS], rest[PARTS + 1 :]
    gain = gain_ref[...].reshape(1, -1)
    rows = x_ref.shape[0] // PARTS
    for index in range(PARTS):
        for span in spans(rows):
            here = slice(index * rows + span.start, index * rows + span.stop)
            recv = recv_refs[index][span, :].astype(single)
            x = x_ref[here, :].astype(single) + (keep_ref[here, :] + recv)
            mid_ref[here, :] = x
            normal, _ = normal_of(x)
            out_refs[index][span, :] = (normal * gain).astype(bfloat)


def norm_back(x, grad, gain):
    normal, scale = normal_of(x)
    lifted = grad * gain
    back = scale * (
        lifted
        - jnp.mean(lifted, axis=-1, keepdims=True)
        - normal * jnp.mean(lifted * normal, axis=-1, keepdims=True)
    )
    return back, normal


def fold_rows(value):
    total = value[:8]
    for begin in range(8, value.shape[0], 8):
        total = total + value[begin : begin + 8]
    return total


def middle_back_body(mix_ref, x_ref, keep_ref, recv_ref, cot_ref, gain_ref, mid_ref, low_ref, part_ref):
    gain = gain_ref[...].reshape(1, -1)
    part = jnp.zeros((8, x_ref.shape[1]), single)
    for span in spans(x_ref.shape[0]):
        grad = keep_ref[span, :] + recv_ref[span, :].astype(single)
        back, normal = norm_back(x_ref[span, :], grad, gain)
        total = mix_ref[mix_ref.shape[0] - 1] * cot_ref[span, :] + back
        mid_ref[span, :] = total
        low_ref[span, :] = total.astype(bfloat)
        part = part + fold_rows(grad * normal)
    part_ref[...] = jnp.sum(part, axis=0, keepdims=True)


def first_back_body(x_ref, keep_ref, recv_ref, mid_ref, gain_ref, out_ref):
    gain = gain_ref[...].reshape(1, -1)
    for span in spans(x_ref.shape[0]):
        grad = keep_ref[span, :] + recv_ref[span, :].astype(single)
        back, _ = norm_back(x_ref[span, :].astype(single), grad, gain)
        out_ref[span, :] = (mid_ref[span, :] + back).astype(bfloat)


def history_body(mix_ref, history_ref, cot_ref, grad_ref, mixed_ref, low_ref, part_ref):
    depth = history_ref.shape[0]

    @pl.when(pl.program_id(0) == 0)
    def _():
        part_ref[...] = jnp.zeros_like(part_ref)

    for span in spans(cot_ref.shape[0], 32):
        cot = cot_ref[span, :]
        low_ref[span, :] = (mix_ref[depth] * cot).astype(bfloat)
        mixed = None
        for j in range(depth):
            layer = history_ref[j, span, :].astype(single)
            mixed = mix_ref[j] * layer if mixed is None else mixed + mix_ref[j] * layer
            grad_ref[j, span, :] = (mix_ref[j] * cot).astype(bfloat)
            part_ref[8 * j : 8 * j + 8, :] += fold_rows(layer * cot)
        mixed_ref[span, :] = mixed


def average_history(mix, history, cot, after=()):
    depth, rows, width = history.shape
    step = 96
    waits = len(after)

    def body(*refs):
        history_body(*refs[:3], *refs[3 + waits :])

    row_block = pl.BlockSpec((step, width), lambda i: (i, 0))
    deep_block = pl.BlockSpec((depth, step, width), lambda i: (0, i, 0))
    return pl.pallas_call(
        body,
        grid=(rows // step,),
        out_shape=[
            jax.ShapeDtypeStruct(history.shape, bfloat),
            jax.ShapeDtypeStruct((rows, width), single),
            jax.ShapeDtypeStruct((rows, width), bfloat),
            jax.ShapeDtypeStruct((8 * depth, width), single),
        ],
        in_specs=[pl.BlockSpec(memory_space=pltpu.SMEM), deep_block, row_block]
        + [pl.BlockSpec(memory_space=pl.ANY)] * waits,
        out_specs=[deep_block, row_block, row_block, pl.BlockSpec((8 * depth, width), lambda i: (0, 0))],
        compiler_params=pltpu.CompilerParams(vmem_limit_bytes=16 * MIB),
        cost_estimate=pl.CostEstimate(flops=0, bytes_accessed=0, transcendentals=0),
    )(mix, history, cot, *after)


def combine_body(mix_ref, mixed_ref, mid_ref, keep_ref, recv_ref, cot_ref, parts_ref, out_ref, part_ref):
    depth = mix_ref.shape[0] - 1
    last = jnp.zeros((8, mid_ref.shape[1]), single)
    for span in spans(mid_ref.shape[0]):
        outputs = mid_ref[span, :] + (keep_ref[span, :] + recv_ref[span, :].astype(single))
        out_ref[span, :] = (mixed_ref[span, :] + mix_ref[depth] * outputs).astype(bfloat)
        last = last + fold_rows(outputs * cot_ref[span, :])
    for j in range(depth):
        part_ref[j : j + 1, :] = jnp.sum(parts_ref[8 * j : 8 * j + 8, :], axis=0, keepdims=True)
    part_ref[depth : depth + 1, :] = jnp.sum(last, axis=0, keepdims=True)


SQUARE = 4


def quarter(owner, mask, size):
    other = owner + (mask & 1) * (1 - 2 * (owner % 2)) + (mask & 2) * (1 - 2 * (owner // 2))
    return pl.ds(pl.multiple_of(other * size, size), size)


def part_body(owner_ref, mine_ref, come_ref, *out_refs):
    for mask, out_ref in enumerate(out_refs):
        rows = quarter(owner_ref[0], mask, out_ref.shape[0])
        out_ref[...] = (mine_ref[rows, :].astype(single) + come_ref[rows, :].astype(single)).astype(bfloat)


def sum_of(refs, rows):
    total = refs[0][rows, :].astype(single)
    for ref in refs[1:]:
        total = total + ref[rows, :].astype(single)
    return total


def four_body(*refs):
    refs[-1][...] = sum_of(refs[:-1], slice(None)).astype(bfloat)


def four_two_body(*refs):
    size = refs[-1].shape[0]
    refs[-2][...] = sum_of(refs[:-2], slice(0, size)).astype(bfloat)
    refs[-1][...] = sum_of(refs[:-2], slice(size, 2 * size)).astype(bfloat)


EXTRA = 16


def mark_body(out_ref):
    out_ref[...] = jnp.zeros_like(out_ref)


def small_body(small_ref, first_ref, out_ref):
    half = small_ref.shape[0]
    rows = first_ref.shape[0] - 2 * half
    come = first_ref[rows:, :].astype(single)
    out_ref[...] = small_ref[...] + (come[:half] + come[half:])


def four_more_body(small_ref, more_ref, *refs):
    out_ref = refs[-1]
    size = out_ref.shape[0] - EXTRA
    out_ref[:size, :] = sum_of(refs[:-1], slice(None)).astype(bfloat)
    small = small_ref[...] + more_ref[...]
    rest = jnp.zeros((EXTRA - small.shape[0], small.shape[1]), single)
    out_ref[size:, :] = jnp.concatenate([small, rest], axis=0).astype(bfloat)


def gather(owner_ref, pieces, hold):
    for mask, piece in enumerate(pieces):
        hold[quarter(owner_ref[0], mask, piece.shape[0]), :] = piece[...]


def pair_body(a_ref, a_come_ref, b_ref, b_come_ref, out_ref):
    size = a_ref.shape[0]
    out_ref[:size, :] = sum_of((a_ref, a_come_ref), slice(None)).astype(bfloat)
    out_ref[size:, :] = sum_of((b_ref, b_come_ref), slice(None)).astype(bfloat)


def whole_body(owner_ref, a_ref, b_ref, c_ref, d_ref, out_ref, hold):
    gather(owner_ref, (a_ref, b_ref, c_ref, d_ref), hold)
    out_ref[...] = hold[...].astype(single)


def more_body(owner_ref, a_ref, b_ref, c_ref, d_ref, top_ref, end_ref, up_ref, attn_ref, mlp_ref, dwa_ref, hold):
    gather(owner_ref, (a_ref, b_ref, c_ref, d_ref), hold)
    block = hold.shape[0] // SQUARE
    rows = up_ref.shape[0] // SQUARE
    small = jnp.zeros((EXTRA, hold.shape[1]), single)
    for index in range(SQUARE):
        begin = index * block
        target, place = (top_ref, index * rows) if index < SQUARE - 1 else (end_ref, 0)
        target[place : place + rows, :] = hold[begin : begin + rows, :].astype(single)
        small = small + hold[begin + rows : begin + rows + EXTRA, :].astype(single)
        up_ref[index * rows : (index + 1) * rows, :] = hold[begin + rows + EXTRA : begin + block, :].astype(single)
    attn_ref[...] = small[0]
    mlp_ref[...] = small[1]
    for index in range(dwa_ref.shape[0]):
        dwa_ref[index] = jnp.sum(small[2 + index : 3 + index])


def low_body(mine_ref, come_ref, out_ref):
    out_ref[...] = (mine_ref[...].astype(single) + come_ref[...].astype(single)).astype(bfloat)


def mark_body(out_ref):
    out_ref[...] = jnp.zeros_like(out_ref)


def small_body(small_ref, first_ref, out_ref):
    half = small_ref.shape[0]
    rows = first_ref.shape[0] - 2 * half
    come = first_ref[rows:, :].astype(single)
    out_ref[...] = small_ref[...] + (come[:half] + come[half:])


BLOCKS = tuple((begin, min(256, SEQ - begin)) for begin in range(0, SEQ, 256))


def places(core_ref, refs):
    count, size = len(refs) // 2, refs[0].shape[0]
    for index, ref in enumerate(refs):
        core = core_ref[0] if index < count else 1 - core_ref[0]
        yield ref, pl.ds(pl.multiple_of(core * HALF + index % count * size, size), size)


def allowed(size):
    key_pos = lax.broadcasted_iota(jnp.int32, (size, size), 0)
    query_pos = lax.broadcasted_iota(jnp.int32, (size, size), 1)
    return query_pos >= key_pos


def turn(rows, cosine, sine):
    half = rows.shape[0] // 2
    a, b = rows[:half], rows[half:]
    return jnp.concatenate([a * cosine - b * sine, b * cosine + a * sine], axis=0)


KEYS = 128


def fold_top(value):
    top = value[:8]
    for begin in range(8, value.shape[0], 8):
        top = jnp.maximum(top, value[begin : begin + 8])
    return top


def masked(scores, offset):
    key_pos = lax.broadcasted_iota(jnp.int32, scores.shape, 0) + offset
    query_pos = lax.broadcasted_iota(jnp.int32, scores.shape, 1)
    return jnp.where(query_pos >= key_pos, scores, -jnp.inf)


def attend_placed(core_ref, *rest):
    for ref, where in places(core_ref, rest[:4]):
        rest[11][where, :] = ref[...]
    cos_ref, sin_ref, weight_ref, rest = rest[4], rest[5], rest[6], rest[7:]
    attend(weight_ref, cos_ref, sin_ref, *rest)


def attend(weight_ref, cos_ref, sin_ref, qkv_ref, att_ref, nat_ref, log_ref, tokens, all_scores, all_weights):
    width = weight_ref.shape[0] // 3
    projected = mul(weight_ref[...], tokens[...], 1, 1)
    cosine, sine = cos_ref[...], sin_ref[...]
    for part in range(3):
        for head in range(width // DH):
            begin = part * width + head * DH
            rows = projected[begin : begin + DH]
            if part < 2:
                rows = turn(rows, cosine, sine)
            if part == 0:
                rows = rows * DH ** (-0.5)
            qkv_ref[begin : begin + DH, :] = rows.astype(bfloat)
    log_ref[...] = jnp.zeros_like(log_ref)
    heads = range(width // DH)
    keys = [qkv_ref[width + head * DH : width + head * DH + DH, :].T for head in heads]
    for begin, size in BLOCKS:
        end = begin + size
        tops = [None for _ in heads]
        for row in range(0, end, KEYS):
            for head in heads:
                tile = mul(keys[head][row : row + KEYS], qkv_ref[head * DH : head * DH + DH, begin:end])
                if row >= begin:
                    tile = masked(tile, row - begin)
                all_scores[head, row : row + KEYS, :size] = tile
                top = fold_top(tile)
                tops[head] = top if row == 0 else jnp.maximum(tops[head], top)
        tops = [jnp.max(top, axis=0, keepdims=True) for top in tops]
        totals = [jnp.zeros((8, size), single) for _ in heads]
        for row in range(0, end, KEYS):
            for head in heads:
                tile = jnp.exp(all_scores[head, row : row + KEYS, :size] - tops[head])
                totals[head] = totals[head] + fold_rows(tile)
                all_weights[head, row : row + KEYS, :size] = tile.astype(bfloat)
        for head in heads:
            base = head * DH
            total = jnp.sum(totals[head], axis=0, keepdims=True)
            value = qkv_ref[2 * width + base : 2 * width + base + DH, :end]
            mixed = mul(value, all_weights[head, :end, :size]) / total
            att_ref[base : base + DH, begin:end] = mixed.astype(bfloat)
            log_ref[head : head + 1, begin:end] = tops[head] + jnp.log(total)
    nat_ref[...] = att_ref[...].T


def branch_body(core_ref, att_a_ref, att_b_ref, out_a_ref, out_b_ref, pass_ref, keep_ref, *rest):
    send_refs, pass_out = rest[:PARTS], rest[PARTS]
    pass_out[...] = pass_ref[...]
    low = pl.multiple_of(core_ref[0] * HALF, HALF)
    rows = HALF // PARTS
    for index in range(PARTS):
        high = pl.multiple_of((1 - core_ref[0]) * HALF + index * rows, rows)
        send = mul(att_a_ref[pl.ds(high, rows), :], out_a_ref[...])
        send_refs[index][...] = (send + mul(att_b_ref[pl.ds(high, rows), :], out_b_ref[...])).astype(bfloat)
    keep = mul(att_a_ref[pl.ds(low, HALF), :], out_a_ref[...])
    keep_ref[...] = keep + mul(att_b_ref[pl.ds(low, HALF), :], out_b_ref[...])


def attend_back(
    core_ref, log_ref, cos_ref, sin_ref, gain_ref, *rest
):
    before_refs, rest = rest[:-25], rest[-25:]
    grad_refs, x_refs = rest[:2], rest[2:6]
    weight_ref, qkv_weight_ref, qkv_ref, att_ref, small_ref, out_ref, turned_ref = rest[6:13]
    grads, tokens, weight, qkv_weight, qkv, att, turned, result, all_probs, all_scores, hold, marks = rest[13:]
    go = Mover(marks)
    first = go(
        (weight_ref, weight),
        *[(ref, grads.at[where, :]) for ref, where in places(core_ref, grad_refs)],
        (att_ref, att),
        (qkv_ref, qkv),
    )
    later = go(
        *[(ref, tokens.at[where, :]) for ref, where in places(core_ref, x_refs)],
        (qkv_weight_ref, qkv_weight),
    )
    wait(first)
    width = att.shape[0]
    grad_att = mul(weight[...], grads[...], 1, 1).astype(bfloat)
    result[3 * width :, :] = mul(att[...], grads[...]).astype(result.dtype)
    cosine, sine = cos_ref[...], sin_ref[...]
    heads = range(width // DH)
    spans_of = [slice(head * DH, head * DH + DH) for head in heads]
    query = [qkv[span, :] for span in spans_of]
    key = [qkv[width + span.start : width + span.stop, :] for span in spans_of]
    above = [grad_att[span] for span in spans_of]
    centre = [
        jnp.sum(above[head].astype(single) * att[span, :].astype(single), axis=0, keepdims=True)
        for head, span in enumerate(spans_of)
    ]
    keys = [value.T for value in key]
    values = [qkv[2 * width + span.start : 2 * width + span.stop, :].T for span in spans_of]
    queries = [value.T for value in query]
    aboves = [value.T for value in above]
    grad_query = [[] for _ in heads]
    for begin, size in BLOCKS:
        end = begin + size
        for row in range(0, end, KEYS):
            span = slice(row, row + KEYS)
            for head in heads:
                tile = mul(keys[head][span], query[head][:, begin:end])
                if row >= begin:
                    tile = masked(tile, row - begin)
                tile = jnp.exp(tile - log_ref[head : head + 1, begin:end])
                grad = mul(values[head][span], above[head][:, begin:end]) - centre[head][:, begin:end]
                all_probs[head, span, begin:end] = tile.astype(bfloat)
                all_scores[head, span, begin:end] = (tile * grad).astype(bfloat)
        for head in heads:
            grad_query[head].append(mul(key[head][:, :end], all_scores[head, :end, begin:end]))
    grad_key = [[] for _ in heads]
    grad_value = [[] for _ in heads]
    for begin, size in BLOCKS:
        span = slice(begin, begin + size)
        for head in heads:
            grad_key[head].append(mul(all_scores[head, span, begin:], queries[head][begin:]))
            grad_value[head].append(mul(all_probs[head, span, begin:], aboves[head][begin:]))
    for head, span in enumerate(spans_of):
        grad = jnp.concatenate(grad_query[head], axis=1) * DH ** (-0.5)
        turned[span, :] = turn(grad, cosine, -sine).astype(bfloat)
        grad = jnp.concatenate(grad_key[head], axis=0).T
        turned[width + span.start : width + span.stop, :] = turn(grad, cosine, -sine).astype(bfloat)
        grad = jnp.concatenate(grad_value[head], axis=0).T
        turned[2 * width + span.start : 2 * width + span.stop, :] = grad.astype(bfloat)
    stores = go((turned, turned_ref))
    wait(later)
    hold[...] = mul(turned[...], tokens[...])
    result[: 3 * width, :] = hold[...].astype(result.dtype)
    stores += go((result, out_ref))
    part = jnp.zeros((8, hold.shape[1]), single)
    for span in spans(hold.shape[0]):
        part = part + fold_rows(hold[span, :] * qkv_weight[span, :].astype(single))
    gain = jnp.sum(part, axis=0, keepdims=True) / gain_ref[...].reshape(1, -1)
    if before_refs:
        gain_part_ref, mlp_part_ref, dwa_part_ref = before_refs
        small_ref[:1, :] = gain + gain_part_ref[...]
        small_ref[1:2, :] = mlp_part_ref[...]
        small_ref[2:, :] = dwa_part_ref[...]
    else:
        small_ref[...] = gain
    wait(stores)


def first_grad_body(
    core_ref, small_ref, turned_a_ref, turned_b_ref, weight_a_ref, weight_b_ref, send_ref, keep_ref,
    turned_a, turned_b, weight_a, weight_b, whole, marks,
):
    low = pl.multiple_of(core_ref[0] * HALF, HALF)
    high = pl.multiple_of((1 - core_ref[0]) * HALF, HALF)
    go = Mover(marks)
    wait(go((turned_a_ref, turned_a), (weight_a_ref, weight_a), (turned_b_ref, turned_b), (weight_b_ref, weight_b)))
    whole[...] = mul(turned_a[...], weight_a[...], 0, 0) + mul(turned_b[...], weight_b[...], 0, 0)
    stores = go((whole.at[pl.ds(low, HALF), :], keep_ref))
    send_ref[:HALF, :] = whole[pl.ds(high, HALF), :].astype(bfloat)
    small = small_ref[...]
    high_part = small.astype(bfloat)
    low_part = (small - high_part.astype(single)).astype(bfloat)
    send_ref[HALF:, :] = jnp.concatenate([high_part, low_part], axis=0)
    wait(stores)


CURVE = float(np.sqrt(2.0 / np.pi))
STEP = 256


def mlp_body(second, *refs):
    if second:
        owner_ref, refs = refs[0], refs[1:]
    x_refs, refs = refs[: 2 * PARTS], refs[2 * PARTS :]
    g_own_ref, g_peer_ref, refs = refs[0], refs[1], refs[2:]
    if second:
        up_ref, down_refs, refs = refs[0], refs[1 : 1 + SQUARE], refs[1 + SQUARE :]
        before_refs, up_mine_ref = refs[:4], refs[4]
        down_grad_ref, part_refs = refs[9], refs[10:14]
        refs = refs[5:9] + refs[14:]
    else:
        up_ref, down_ref = refs[:2]
        down_grad_ref, up_grad_ref = refs[6:8]
        refs = refs[2:6] + refs[8:]
    send_norm_ref, keep_norm_ref, send_out_ref, keep_out_ref = refs[:4]
    x_all, g_all, up, down, active, grad_hidden, x_turned = refs[4:11]
    send_norm, keep_norm, send_out, keep_out, down_grad, up_grad, marks = refs[11:18]
    rows, size = x_all.shape[0] // 2, x_all.shape[0] // (2 * PARTS)
    units = down.shape[0]
    go = Mover(marks)
    x_loads = go(*[(x_refs[index], x_all.at[pl.ds(index * size, size), :]) for index in range(2 * PARTS)])
    if second:
        loads = go((up_ref, up), *joined(owner_ref[0], down_refs, down))
    else:
        loads = go((up_ref, up), (down_ref, down))
    loads += go((g_own_ref, g_all.at[pl.ds(0, rows), :]), (g_peer_ref, g_all.at[pl.ds(rows, rows), :]))
    more, mine, stores = [], [], []
    if second:
        (up_mine,) = refs[18:]
        more = go(*zip(before_refs, (send_norm, keep_norm, send_out, keep_out)))
        mine = go((up_mine_ref, up_mine))
    wait(x_loads)
    x_turned[...] = x_all[...].T
    wait(loads)
    for begin in range(0, units, STEP):
        columns = slice(begin, begin + STEP)
        for top in range(0, 2 * rows, rows):
            span = slice(top, top + rows)
            v = mul(x_all[span, :], up[:, columns])
            grad = mul(g_all[span, :], down[columns, :], 1, 1)
            square = v * v
            half = 0.5 + 0.5 * jnp.tanh(v * (CURVE + (CURVE * 0.044715) * square))
            act = v * half
            slope = half + act * (1.0 - half) * (2.0 * CURVE + (6.0 * CURVE * 0.044715) * square)
            active[span, columns] = act.astype(bfloat)
            grad_hidden[span, columns] = (grad * slope).astype(bfloat)

    def put(target, value):
        target[...] = (value + target[...].astype(single) if second else value).astype(target.dtype)

    wait(more)
    put(keep_norm, mul(grad_hidden[:rows, :], up[...], 1, 1))
    put(send_norm, mul(grad_hidden[rows:, :], up[...], 1, 1))
    stores += go((keep_norm, keep_norm_ref), (send_norm, send_norm_ref))
    down_grad[...] = mul(active[...], g_all[...], 0, 0).astype(down_grad.dtype)
    stores += go((down_grad, down_grad_ref))
    up_grad[...] = mul(x_turned[...], grad_hidden[...]).astype(bfloat)
    if second:
        wait(mine)
        part = up_grad.shape[0] // SQUARE
        for mask, part_ref in enumerate(part_refs):
            rows_of = quarter(owner_ref[0], mask, part)
            stores += go(
                (up_mine.at[rows_of, :], part_ref.at[pl.ds(0, part), :]),
                (up_grad.at[rows_of, :], part_ref.at[pl.ds(part, part), :]),
            )
    else:
        stores += go((up_grad, up_grad_ref))
    put(keep_out, mul(active[:rows, :], down[...]))
    stores += go((keep_out, keep_out_ref))
    put(send_out, mul(active[rows:, :], down[...]))
    wait(stores + go((send_out, send_out_ref)))


def mlp(x_own, x_peer, g_own, g_peer, up, down, upper=(), before=(), flops=0):
    rows, width = g_own.shape
    units = sum(piece.shape[0] for piece in down)
    tall = (2 * rows, width)
    pair = [((rows, width), bfloat), ((rows, width), single)] * 2
    outs = pair + [((units, width), bfloat)]
    outs += [((2 * width // SQUARE, units), bfloat)] * SQUARE if before else [((width, units), bfloat)]
    scratch = [
        pltpu.VMEM(tall, bfloat),
        pltpu.VMEM(tall, bfloat),
        pltpu.VMEM((width, units), bfloat),
        pltpu.VMEM((units, width), bfloat),
        pltpu.VMEM((2 * rows, units), bfloat),
        pltpu.VMEM((2 * rows, units), bfloat),
        pltpu.VMEM((width, 2 * rows), bfloat),
    ]
    scratch += [pltpu.VMEM(shape, kind) for shape, kind in pair]
    scratch += [
        pltpu.VMEM((units, width), bfloat), pltpu.VMEM((width, units), bfloat), pltpu.SemaphoreType.DMA((32,)),
    ]
    if before:
        scratch.append(pltpu.VMEM((width, units), bfloat))
    operands = (*upper, *x_own, *x_peer, g_own, g_peer, *up, *down, *before)
    return call(
        functools.partial(mlp_body, bool(before)),
        outs,
        operands,
        scratch,
        len(upper),
        vmem=32,
        flops=flops,
        far=len(operands) - len(upper),
        far_outs=len(outs),
    )


def shards(
    inputs,
    history,
    cotangent,
    qkv_weight,
    out_weight,
    up_weight,
    down_weight,
    gain_attn,
    gain_mlp,
    dwa_weights,
):
    rows, width = inputs.shape
    members = lax.axis_size("mp")
    copies = lax.axis_size("dp")
    bits = copies.bit_length() - 1
    core = lax.rem(lax.axis_index("mp"), 2).astype(jnp.int32).reshape(1)
    copy_index = lax.axis_index("dp").astype(jnp.int32).reshape(1)
    core_pairs = [(i, i ^ 1) for i in range(members)]
    chip_pairs = [(i, i ^ 2) for i in range(members)]
    depth = history.shape[0]
    part = out_weight.shape[0]

    def other_core(value):
        return lax.ppermute(value, "mp", core_pairs)

    def other_chip(value):
        return lax.ppermute(value, "mp", chip_pairs)

    def other_copy(value, mask):
        return lax.ppermute(value, "dp", [(i, i ^ mask) for i in range(copies)])

    owner = copy_index & (SQUARE - 1)
    cosine, sine = (jnp.asarray(table) for table in tables())

    qkv_own = qkv_weight.transpose(1, 2, 0).reshape(3 * part, width)
    fourth = (width // SQUARE, width)
    square = (width, width)
    masks = range(1, SQUARE)
    marks = pltpu.SemaphoreType.DMA((16,))
    (down_quarter,) = call(
        split_body,
        [(fourth, bfloat)],
        (owner, down_weight),
        [pltpu.VMEM(fourth, bfloat), marks],
        1,
        vmem=60,
        far=1,
        far_outs=1,
    )
    qkv_peer, out_peer = other_chip(qkv_own), other_chip(out_weight)
    down_come, up_peer = other_chip(down_quarter), other_chip(up_weight)

    full = (rows, width)
    x_own = call(norm_body, [((rows // 2, width), bfloat)] * 2, (inputs, gain_attn), after=(down_quarter,))
    x_peer = [other_core(value) for value in x_own]
    tall = (SEQ, width)
    tokens = pltpu.VMEM(tall, bfloat)
    first_outs = [
        ((3 * part, SEQ), bfloat), ((part, SEQ), bfloat), ((SEQ, part), bfloat), ((8, SEQ), single),
    ]
    heads = part // DH
    tiles = [tokens, pltpu.VMEM((heads, SEQ, 256), single), pltpu.VMEM((heads, SEQ, 256), bfloat)]
    qkv_a, att_a, nat_a, log_a = call(
        attend_placed, first_outs, (core, *x_own, *x_peer, cosine, sine, qkv_own), tiles, 1, vmem=32
    )
    history_grad, mixed, g_own, history_parts = average_history(dwa_weights, history, cotangent, (log_a,))
    g_peer = other_core(g_own)
    qkv_b, att_b, nat_b, log_b = call(
        attend_placed,
        first_outs,
        (core, *x_own, *x_peer, cosine, sine, qkv_peer),
        tiles,
        1,
        (history_parts,),
        32,
        MUCH,
    )
    third = (rows // PARTS, width)
    keep, *send, down_copy = call(
        branch_body,
        [(full, single)] + [(third, bfloat)] * PARTS + [(fourth, bfloat)],
        (core, nat_a, nat_b, out_weight, out_peer, down_come),
        (),
        1,
        (g_peer,),
    )
    down_pieces = [down_come] + [other_copy(down_copy, mask) for mask in masks]
    recv = [other_core(value) for value in send]
    middle, *y_own = call(
        middle_body, [(full, single)] + [(third, bfloat)] * PARTS, (inputs, keep, gain_mlp, *recv)
    )
    y_peer = [other_core(value) for value in y_own]

    first = mlp(y_own, y_peer, g_own, g_peer, (up_weight,), (down_weight,))
    down_mine, up_mine = first[4:]
    second = mlp(
        y_own, y_peer, g_own, g_peer, (up_peer,), down_pieces, (owner,), (*first[:4], up_mine)
    )
    send_norm, keep_norm, send_out, keep_out, down_theirs = second[:5]
    token = [send_norm]

    def step(body, outs, operands, scratch=(), scalars=0, vmem=16, flops=MUCH, far=0, far_outs=0):
        results = call(body, outs, operands, scratch, scalars, tuple(token), vmem, flops, far, far_outs)
        token[0] = results[0]
        return results

    down_come = other_chip(down_theirs)
    up_parts = [second[5]] + [other_copy(value, mask) for mask, value in zip(masks, second[6:])]
    out_come = other_core(send_out)
    grad_middle, gb_own, gain_mlp_part = step(
        middle_back_body,
        [(full, single), (full, bfloat), ((1, width), single)],
        (dwa_weights, middle, keep_norm, other_core(send_norm), cotangent, gain_mlp),
        scalars=1,
        flops=0,
    )
    gb_peer = other_core(gb_own)
    combined, dwa_part = step(
        combine_body,
        [(full, bfloat), ((depth + 1, width), single)],
        (dwa_weights, mixed, middle, keep_out, out_come, cotangent, history_parts),
        scalars=1,
        flops=0,
    )

    def back(weight, qkv_weight, qkv, att, log, flops, before=()):
        return step(
            attend_back,
            [
                ((depth + 3 if before else 1, width), single),
                ((4 * part, width), bfloat),
                ((3 * part, SEQ), bfloat),
            ],
            (
                core, log, cosine, sine, gain_attn, *before, gb_own, gb_peer, *x_own, *x_peer, weight, qkv_weight, qkv,
                att,
            ),
            [
                pltpu.VMEM(tall, bfloat),
                pltpu.VMEM(tall, bfloat),
                pltpu.VMEM((part, width), bfloat),
                pltpu.VMEM((3 * part, width), bfloat),
                pltpu.VMEM((3 * part, SEQ), bfloat),
                pltpu.VMEM((part, SEQ), bfloat),
                pltpu.VMEM((3 * part, SEQ), bfloat),
                pltpu.VMEM((4 * part, width), bfloat),
                pltpu.VMEM((heads, SEQ, SEQ), bfloat),
                pltpu.VMEM((heads, SEQ, SEQ), bfloat),
                pltpu.VMEM((3 * part, width), single),
                marks,
            ],
            1,
            36,
            flops,
            10,
            2,
        )

    gain_part, att_theirs, turned_b = back(out_peer, qkv_peer, qkv_b, att_b, log_b, 0)
    att_come = other_chip(att_theirs)
    def spread(mine, come, flops=MUCH):
        own, *sent = step(part_body, [(fourth, bfloat)] * SQUARE, (owner, mine, come), scalars=1, flops=flops)
        return [own] + [other_copy(value, mask) for mask, value in zip(masks, sent)]

    down_parts = spread(down_mine, down_come, 0)
    up, sent = step(four_two_body, [(fourth, bfloat)] * 2, up_parts, flops=0)
    up_come = other_chip(sent)
    part_sums, att_mine, turned_a = back(
        out_weight, qkv_own, qkv_a, att_a, log_a, MUCH, (gain_part, gain_mlp_part, dwa_part)
    )

    def exchange(value):
        for bit in range(2, bits):
            come = other_copy(value, 1 << bit)
            if bit < bits - 1:
                (value,) = step(low_body, [(value.shape, bfloat)], (value, come))
        return value, come

    def finish(value, come):
        (value,) = step(low_body, [(value.shape, bfloat)], (value, come), flops=COST)
        return [value] + [other_copy(value, mask) for mask in masks]

    (down,) = step(four_body, [(fourth, bfloat)], down_parts, flops=COST)
    down = exchange(down)
    att_parts = spread(att_mine, att_come, COST)
    (up,) = step(low_body, [(fourth, bfloat)], (up, up_come), flops=COST)
    up = exchange(up)
    send_first, keep_first = step(
        first_grad_body,
        [((rows + EXTRA, width), bfloat), (full, single)],
        (core, part_sums, turned_a, turned_b, qkv_own, qkv_peer),
        [pltpu.VMEM((3 * part, SEQ), bfloat)] * 2
        + [pltpu.VMEM((3 * part, width), bfloat)] * 2
        + [pltpu.VMEM(tall, single), marks],
        1,
        60,
        COST,
        4,
        1,
    )
    first_come = other_core(send_first)
    token.append(down[1])
    step(mark_body, [((8, 128), single)], (), flops=COST)
    del token[1:]
    (part_sums,) = step(small_body, [(part_sums.shape, single)], (part_sums, first_come), flops=COST)
    more_sums = other_chip(part_sums)
    (input_grad,) = step(
        first_back_body,
        [(full, bfloat)],
        (inputs, keep_first, first_come, grad_middle, gain_attn),
        vmem=60,
        flops=COST,
    )
    block = (width // SQUARE + EXTRA, width)
    (att,) = step(four_more_body, [(block, bfloat)], (part_sums, more_sums, *att_parts), flops=COST)
    att = exchange(att)
    down = finish(*down)
    token += down[1:]
    pair = (block[0] + fourth[0], width)
    (both,) = step(pair_body, [(pair, bfloat)], (*att, *up), flops=COST)
    del token[1:]
    both = [both] + [other_copy(both, mask) for mask in masks]
    (down_grad,) = step(
        whole_body, [(square, single)], (owner, *down), [pltpu.VMEM(square, bfloat)], 1, flops=COST
    )
    qkv_grad, out_grad, up_grad, gain_attn_grad, gain_mlp_grad, dwa_grad = step(
        more_body,
        [
            ((3 * part, width), single),
            ((part, width), single),
            (square, single),
            ((width,), single),
            ((width,), single),
            ((depth + 1,), single, "scalars"),
        ],
        (owner, *both),
        [pltpu.VMEM((SQUARE * pair[0], width), bfloat)],
        1,
        flops=COST,
    )

    return (
        combined,
        input_grad,
        history_grad,
        qkv_grad.reshape(3, part, width).transpose(2, 0, 1),
        out_grad,
        up_grad,
        down_grad,
        gain_attn_grad,
        gain_mlp_grad,
        dwa_grad,
    )


def solution(mesh):
    placed = (
        P(("dp", "mp"), None),
        P(None, ("dp", "mp"), None),
        P(("dp", "mp"), None),
        P(None, None, "mp"),
        P("mp", None),
        P(None, "mp"),
        P("mp", None),
        P(),
        P(),
        P(),
    )
    return jax.shard_map(
        shards,
        mesh=mesh,
        in_specs=placed,
        out_specs=(
            P(("dp", "mp"), None),
            P(("dp", "mp"), None),
            P(None, ("dp", "mp"), None),
            P(None, None, "mp"),
            P("mp", None),
            P(None, "mp"),
            P("mp", None),
            P(),
            P(),
            P(),
        ),
        check_vma=False,
    )
```

```python
import functools

import jax
import jax.numpy as jnp
import numpy as np
from jax import lax
from jax.experimental import pallas as pl
from jax.experimental.pallas import tpu as pltpu
from jax.sharding import PartitionSpec as P

DH = 64
SEQ = 1152
HALF = SEQ // 2
EPS = 1e-05
bfloat = jnp.bfloat16
single = jnp.float32
MIB = 1 << 20
MUCH = 10**11
COST = 10**10


def tables():
    half_width = DH // 2
    places = np.arange(SEQ, dtype=np.float32)
    frequency = np.float32(10000.0) ** (-np.arange(half_width, dtype=np.float32) * np.float32(2.0 / DH))
    angles = frequency[:, None] * places[None, :]
    return (np.cos(angles).astype(np.float32), np.sin(angles).astype(np.float32))


def mul(a, b, ca=1, cb=0):
    return lax.dot_general(a, b, (((ca,), (cb,)), ((), ())), preferred_element_type=single)


def call(kernel, outs, operands, scratch=(), scalars=0, after=(), vmem=16, flops=0, far=0, far_outs=0):
    count, waits = len(operands), len(after)

    def body(*refs):
        kernel(*refs[:count], *refs[count + waits :])

    small = pl.BlockSpec(memory_space=pltpu.SMEM)
    whole = pl.BlockSpec(memory_space=pltpu.VMEM)
    apart = pl.BlockSpec(memory_space=pltpu.HBM)
    loose = pl.BlockSpec(memory_space=pl.ANY)
    inner = len(outs) - far_outs
    return pl.pallas_call(
        body,
        out_shape=[jax.ShapeDtypeStruct(out[0], out[1]) for out in outs],
        in_specs=[small] * scalars + [whole] * (count - scalars - far) + [apart] * far + [loose] * waits,
        out_specs=[small if len(out) > 2 else whole for out in outs[:inner]] + [apart] * far_outs,
        scratch_shapes=list(scratch),
        compiler_params=pltpu.CompilerParams(vmem_limit_bytes=vmem * MIB),
        cost_estimate=pl.CostEstimate(flops=flops, bytes_accessed=0, transcendentals=0),
    )(*operands, *after)


class Mover:
    def __init__(self, marks):
        self.marks = marks
        self.used = 0

    def __call__(self, *pairs):
        copies = []
        for source, target in pairs:
            copies.append(pltpu.make_async_copy(source, target, self.marks.at[self.used]))
            self.used += 1
        for copy in copies:
            copy.start()
        return copies


def wait(copies):
    for copy in copies:
        copy.wait()


ROWS = 64
PARTS = 1


def spans(rows, step=ROWS):
    return [slice(begin, begin + step) for begin in range(0, rows, step)]


def normal_of(x):
    centre = x - jnp.mean(x, axis=-1, keepdims=True)
    spread = jnp.mean(centre * centre, axis=-1, keepdims=True)
    scale = lax.rsqrt(spread + EPS)
    return centre * scale, scale


def split_body(owner_ref, in_ref, out_ref, hold, marks):
    go = Mover(marks)
    wait(go((in_ref.at[quarter(owner_ref[0], 0, hold.shape[0]), :], hold)))
    wait(go((hold, out_ref)))


def joined(owner, refs, target):
    size = refs[0].shape[0]
    return [(ref, target.at[quarter(owner, mask, size), :]) for mask, ref in enumerate(refs)]


def norm_body(x_ref, gain_ref, *out_refs):
    gain = gain_ref[...].reshape(1, -1)
    for index, out_ref in enumerate(out_refs):
        rows = out_ref.shape[0]
        for span in spans(rows, rows // 6):
            here = slice(index * rows + span.start, index * rows + span.stop)
            normal, _ = normal_of(x_ref[here, :].astype(single))
            out_ref[span, :] = (normal * gain).astype(bfloat)


def middle_body(x_ref, keep_ref, gain_ref, *rest):
    recv_refs, mid_ref, out_refs = rest[:PARTS], rest[PARTS], rest[PARTS + 1 :]
    gain = gain_ref[...].reshape(1, -1)
    rows = x_ref.shape[0] // PARTS
    for index in range(PARTS):
        for span in spans(rows):
            here = slice(index * rows + span.start, index * rows + span.stop)
            recv = recv_refs[index][span, :].astype(single)
            x = x_ref[here, :].astype(single) + (keep_ref[here, :] + recv)
            mid_ref[here, :] = x
            normal, _ = normal_of(x)
            out_refs[index][span, :] = (normal * gain).astype(bfloat)


def norm_back(x, grad, gain):
    normal, scale = normal_of(x)
    lifted = grad * gain
    back = scale * (
        lifted
        - jnp.mean(lifted, axis=-1, keepdims=True)
        - normal * jnp.mean(lifted * normal, axis=-1, keepdims=True)
    )
    return back, normal


def fold_rows(value):
    total = value[:8]
    for begin in range(8, value.shape[0], 8):
        total = total + value[begin : begin + 8]
    return total


def middle_back_body(mix_ref, x_ref, keep_ref, recv_ref, cot_ref, gain_ref, mid_ref, low_ref, part_ref):
    gain = gain_ref[...].reshape(1, -1)
    part = jnp.zeros((8, x_ref.shape[1]), single)
    for span in spans(x_ref.shape[0]):
        grad = keep_ref[span, :] + recv_ref[span, :].astype(single)
        back, normal = norm_back(x_ref[span, :], grad, gain)
        total = mix_ref[mix_ref.shape[0] - 1] * cot_ref[span, :] + back
        mid_ref[span, :] = total
        low_ref[span, :] = total.astype(bfloat)
        part = part + fold_rows(grad * normal)
    part_ref[...] = jnp.sum(part, axis=0, keepdims=True)


def first_back_body(x_ref, keep_ref, recv_ref, mid_ref, gain_ref, out_ref):
    gain = gain_ref[...].reshape(1, -1)
    for span in spans(x_ref.shape[0]):
        grad = keep_ref[span, :] + recv_ref[span, :].astype(single)
        back, _ = norm_back(x_ref[span, :].astype(single), grad, gain)
        out_ref[span, :] = (mid_ref[span, :] + back).astype(bfloat)


def history_body(mix_ref, history_ref, cot_ref, grad_ref, mixed_ref, low_ref, part_ref):
    depth = history_ref.shape[0]

    @pl.when(pl.program_id(0) == 0)
    def _():
        part_ref[...] = jnp.zeros_like(part_ref)

    for span in spans(cot_ref.shape[0], 32):
        cot = cot_ref[span, :]
        low_ref[span, :] = (mix_ref[depth] * cot).astype(bfloat)
        mixed = None
        for j in range(depth):
            layer = history_ref[j, span, :].astype(single)
            mixed = mix_ref[j] * layer if mixed is None else mixed + mix_ref[j] * layer
            grad_ref[j, span, :] = (mix_ref[j] * cot).astype(bfloat)
            part_ref[8 * j : 8 * j + 8, :] += fold_rows(layer * cot)
        mixed_ref[span, :] = mixed


def average_history(mix, history, cot, after=()):
    depth, rows, width = history.shape
    step = 96
    waits = len(after)

    def body(*refs):
        history_body(*refs[:3], *refs[3 + waits :])

    row_block = pl.BlockSpec((step, width), lambda i: (i, 0))
    deep_block = pl.BlockSpec((depth, step, width), lambda i: (0, i, 0))
    return pl.pallas_call(
        body,
        grid=(rows // step,),
        out_shape=[
            jax.ShapeDtypeStruct(history.shape, bfloat),
            jax.ShapeDtypeStruct((rows, width), single),
            jax.ShapeDtypeStruct((rows, width), bfloat),
            jax.ShapeDtypeStruct((8 * depth, width), single),
        ],
        in_specs=[pl.BlockSpec(memory_space=pltpu.SMEM), deep_block, row_block]
        + [pl.BlockSpec(memory_space=pl.ANY)] * waits,
        out_specs=[deep_block, row_block, row_block, pl.BlockSpec((8 * depth, width), lambda i: (0, 0))],
        compiler_params=pltpu.CompilerParams(vmem_limit_bytes=16 * MIB),
        cost_estimate=pl.CostEstimate(flops=0, bytes_accessed=0, transcendentals=0),
    )(mix, history, cot, *after)


def combine_body(mix_ref, mixed_ref, mid_ref, keep_ref, recv_ref, cot_ref, parts_ref, out_ref, part_ref):
    depth = mix_ref.shape[0] - 1
    last = jnp.zeros((8, mid_ref.shape[1]), single)
    for span in spans(mid_ref.shape[0]):
        outputs = mid_ref[span, :] + (keep_ref[span, :] + recv_ref[span, :].astype(single))
        out_ref[span, :] = (mixed_ref[span, :] + mix_ref[depth] * outputs).astype(bfloat)
        last = last + fold_rows(outputs * cot_ref[span, :])
    for j in range(depth):
        part_ref[j : j + 1, :] = jnp.sum(parts_ref[8 * j : 8 * j + 8, :], axis=0, keepdims=True)
    part_ref[depth : depth + 1, :] = jnp.sum(last, axis=0, keepdims=True)


SQUARE = 4


def quarter(owner, mask, size):
    other = owner + (mask & 1) * (1 - 2 * (owner % 2)) + (mask & 2) * (1 - 2 * (owner // 2))
    return pl.ds(pl.multiple_of(other * size, size), size)


def part_body(owner_ref, mine_ref, come_ref, *out_refs):
    for mask, out_ref in enumerate(out_refs):
        rows = quarter(owner_ref[0], mask, out_ref.shape[0])
        out_ref[...] = (mine_ref[rows, :].astype(single) + come_ref[rows, :].astype(single)).astype(bfloat)


def sum_of(refs, rows):
    total = refs[0][rows, :].astype(single)
    for ref in refs[1:]:
        total = total + ref[rows, :].astype(single)
    return total


def four_body(*refs):
    refs[-1][...] = sum_of(refs[:-1], slice(None)).astype(bfloat)


def four_two_body(*refs):
    size = refs[-1].shape[0]
    refs[-2][...] = sum_of(refs[:-2], slice(0, size)).astype(bfloat)
    refs[-1][...] = sum_of(refs[:-2], slice(size, 2 * size)).astype(bfloat)


EXTRA = 16


def mark_body(out_ref):
    out_ref[...] = jnp.zeros_like(out_ref)


def small_body(small_ref, first_ref, out_ref):
    half = small_ref.shape[0]
    rows = first_ref.shape[0] - 2 * half
    come = first_ref[rows:, :].astype(single)
    out_ref[...] = small_ref[...] + (come[:half] + come[half:])


def four_more_body(small_ref, more_ref, *refs):
    out_ref = refs[-1]
    size = out_ref.shape[0] - EXTRA
    out_ref[:size, :] = sum_of(refs[:-1], slice(None)).astype(bfloat)
    small = small_ref[...] + more_ref[...]
    rest = jnp.zeros((EXTRA - small.shape[0], small.shape[1]), single)
    out_ref[size:, :] = jnp.concatenate([small, rest], axis=0).astype(bfloat)


def gather(owner_ref, pieces, hold):
    for mask, piece in enumerate(pieces):
        hold[quarter(owner_ref[0], mask, piece.shape[0]), :] = piece[...]


def pair_body(a_ref, a_come_ref, b_ref, b_come_ref, out_ref):
    size = a_ref.shape[0]
    out_ref[:size, :] = sum_of((a_ref, a_come_ref), slice(None)).astype(bfloat)
    out_ref[size:, :] = sum_of((b_ref, b_come_ref), slice(None)).astype(bfloat)


def pair_whole_body(owner_ref, a_ref, b_ref, c_ref, d_ref, down_ref, up_ref, hold):
    gather(owner_ref, (a_ref, b_ref, c_ref, d_ref), hold)
    block = hold.shape[0] // SQUARE
    size = block // 2
    for index in range(SQUARE):
        begin, rows = index * block, slice(index * size, (index + 1) * size)
        down_ref[rows, :] = hold[begin : begin + size, :].astype(single)
        up_ref[rows, :] = hold[begin + size : begin + block, :].astype(single)


def more_body(owner_ref, a_ref, b_ref, c_ref, d_ref, top_ref, end_ref, attn_ref, mlp_ref, dwa_ref, hold):
    gather(owner_ref, (a_ref, b_ref, c_ref, d_ref), hold)
    block = hold.shape[0] // SQUARE
    rows = block - EXTRA
    small = jnp.zeros((EXTRA, hold.shape[1]), single)
    for index in range(SQUARE):
        begin = index * block
        target, place = (top_ref, index * rows) if index < SQUARE - 1 else (end_ref, 0)
        target[place : place + rows, :] = hold[begin : begin + rows, :].astype(single)
        small = small + hold[begin + rows : begin + block, :].astype(single)
    attn_ref[...] = small[0]
    mlp_ref[...] = small[1]
    for index in range(dwa_ref.shape[0]):
        dwa_ref[index] = jnp.sum(small[2 + index : 3 + index])


def low_body(mine_ref, come_ref, out_ref):
    out_ref[...] = (mine_ref[...].astype(single) + come_ref[...].astype(single)).astype(bfloat)


def mark_body(out_ref):
    out_ref[...] = jnp.zeros_like(out_ref)


def small_body(small_ref, first_ref, out_ref):
    half = small_ref.shape[0]
    rows = first_ref.shape[0] - 2 * half
    come = first_ref[rows:, :].astype(single)
    out_ref[...] = small_ref[...] + (come[:half] + come[half:])


BLOCKS = tuple((begin, min(256, SEQ - begin)) for begin in range(0, SEQ, 256))


def places(core_ref, refs):
    count, size = len(refs) // 2, refs[0].shape[0]
    for index, ref in enumerate(refs):
        core = core_ref[0] if index < count else 1 - core_ref[0]
        yield ref, pl.ds(pl.multiple_of(core * HALF + index % count * size, size), size)


def allowed(size):
    key_pos = lax.broadcasted_iota(jnp.int32, (size, size), 0)
    query_pos = lax.broadcasted_iota(jnp.int32, (size, size), 1)
    return query_pos >= key_pos


def turn(rows, cosine, sine):
    half = rows.shape[0] // 2
    a, b = rows[:half], rows[half:]
    return jnp.concatenate([a * cosine - b * sine, b * cosine + a * sine], axis=0)


KEYS = 128


def fold_top(value):
    top = value[:8]
    for begin in range(8, value.shape[0], 8):
        top = jnp.maximum(top, value[begin : begin + 8])
    return top


def masked(scores, offset):
    key_pos = lax.broadcasted_iota(jnp.int32, scores.shape, 0) + offset
    query_pos = lax.broadcasted_iota(jnp.int32, scores.shape, 1)
    return jnp.where(query_pos >= key_pos, scores, -jnp.inf)


def attend_placed(core_ref, *rest):
    for ref, where in places(core_ref, rest[:4]):
        rest[11][where, :] = ref[...]
    cos_ref, sin_ref, weight_ref, rest = rest[4], rest[5], rest[6], rest[7:]
    attend(weight_ref, cos_ref, sin_ref, *rest)


def attend(weight_ref, cos_ref, sin_ref, qkv_ref, att_ref, nat_ref, log_ref, tokens, all_scores, all_weights):
    width = weight_ref.shape[0] // 3
    projected = mul(weight_ref[...], tokens[...], 1, 1)
    cosine, sine = cos_ref[...], sin_ref[...]
    for part in range(3):
        for head in range(width // DH):
            begin = part * width + head * DH
            rows = projected[begin : begin + DH]
            if part < 2:
                rows = turn(rows, cosine, sine)
            if part == 0:
                rows = rows * DH ** (-0.5)
            qkv_ref[begin : begin + DH, :] = rows.astype(bfloat)
    log_ref[...] = jnp.zeros_like(log_ref)
    heads = range(width // DH)
    keys = [qkv_ref[width + head * DH : width + head * DH + DH, :].T for head in heads]
    for begin, size in BLOCKS:
        end = begin + size
        tops = [None for _ in heads]
        for row in range(0, end, KEYS):
            for head in heads:
                tile = mul(keys[head][row : row + KEYS], qkv_ref[head * DH : head * DH + DH, begin:end])
                if row >= begin:
                    tile = masked(tile, row - begin)
                all_scores[head, row : row + KEYS, :size] = tile
                top = fold_top(tile)
                tops[head] = top if row == 0 else jnp.maximum(tops[head], top)
        tops = [jnp.max(top, axis=0, keepdims=True) for top in tops]
        totals = [jnp.zeros((8, size), single) for _ in heads]
        for row in range(0, end, KEYS):
            for head in heads:
                tile = jnp.exp(all_scores[head, row : row + KEYS, :size] - tops[head])
                totals[head] = totals[head] + fold_rows(tile)
                all_weights[head, row : row + KEYS, :size] = tile.astype(bfloat)
        for head in heads:
            base = head * DH
            total = jnp.sum(totals[head], axis=0, keepdims=True)
            value = qkv_ref[2 * width + base : 2 * width + base + DH, :end]
            mixed = mul(value, all_weights[head, :end, :size]) / total
            att_ref[base : base + DH, begin:end] = mixed.astype(bfloat)
            log_ref[head : head + 1, begin:end] = tops[head] + jnp.log(total)
    nat_ref[...] = att_ref[...].T


def branch_body(core_ref, att_a_ref, att_b_ref, out_a_ref, out_b_ref, pass_ref, keep_ref, *rest):
    send_refs, pass_out = rest[:PARTS], rest[PARTS]
    pass_out[...] = pass_ref[...]
    low = pl.multiple_of(core_ref[0] * HALF, HALF)
    rows = HALF // PARTS
    for index in range(PARTS):
        high = pl.multiple_of((1 - core_ref[0]) * HALF + index * rows, rows)
        send = mul(att_a_ref[pl.ds(high, rows), :], out_a_ref[...])
        send_refs[index][...] = (send + mul(att_b_ref[pl.ds(high, rows), :], out_b_ref[...])).astype(bfloat)
    keep = mul(att_a_ref[pl.ds(low, HALF), :], out_a_ref[...])
    keep_ref[...] = keep + mul(att_b_ref[pl.ds(low, HALF), :], out_b_ref[...])


def attend_back(
    core_ref, log_ref, cos_ref, sin_ref, gain_ref, *rest
):
    before_refs, rest = rest[:-25], rest[-25:]
    grad_refs, x_refs = rest[:2], rest[2:6]
    weight_ref, qkv_weight_ref, qkv_ref, att_ref, small_ref, out_ref, turned_ref = rest[6:13]
    grads, tokens, weight, qkv_weight, qkv, att, turned, result, all_probs, all_scores, hold, marks = rest[13:]
    go = Mover(marks)
    first = go(
        (weight_ref, weight),
        *[(ref, grads.at[where, :]) for ref, where in places(core_ref, grad_refs)],
        (att_ref, att),
        (qkv_ref, qkv),
    )
    later = go(
        *[(ref, tokens.at[where, :]) for ref, where in places(core_ref, x_refs)],
        (qkv_weight_ref, qkv_weight),
    )
    wait(first)
    width = att.shape[0]
    grad_att = mul(weight[...], grads[...], 1, 1).astype(bfloat)
    result[3 * width :, :] = mul(att[...], grads[...]).astype(result.dtype)
    cosine, sine = cos_ref[...], sin_ref[...]
    heads = range(width // DH)
    spans_of = [slice(head * DH, head * DH + DH) for head in heads]
    query = [qkv[span, :] for span in spans_of]
    key = [qkv[width + span.start : width + span.stop, :] for span in spans_of]
    above = [grad_att[span] for span in spans_of]
    centre = [
        jnp.sum(above[head].astype(single) * att[span, :].astype(single), axis=0, keepdims=True)
        for head, span in enumerate(spans_of)
    ]
    keys = [value.T for value in key]
    values = [qkv[2 * width + span.start : 2 * width + span.stop, :].T for span in spans_of]
    queries = [value.T for value in query]
    aboves = [value.T for value in above]
    grad_query = [[] for _ in heads]
    for begin, size in BLOCKS:
        end = begin + size
        for row in range(0, end, KEYS):
            span = slice(row, row + KEYS)
            for head in heads:
                tile = mul(keys[head][span], query[head][:, begin:end])
                if row >= begin:
                    tile = masked(tile, row - begin)
                tile = jnp.exp(tile - log_ref[head : head + 1, begin:end])
                grad = mul(values[head][span], above[head][:, begin:end]) - centre[head][:, begin:end]
                all_probs[head, span, begin:end] = tile.astype(bfloat)
                all_scores[head, span, begin:end] = (tile * grad).astype(bfloat)
        for head in heads:
            grad_query[head].append(mul(key[head][:, :end], all_scores[head, :end, begin:end]))
    grad_key = [[] for _ in heads]
    grad_value = [[] for _ in heads]
    for begin, size in BLOCKS:
        span = slice(begin, begin + size)
        for head in heads:
            grad_key[head].append(mul(all_scores[head, span, begin:], queries[head][begin:]))
            grad_value[head].append(mul(all_probs[head, span, begin:], aboves[head][begin:]))
    for head, span in enumerate(spans_of):
        grad = jnp.concatenate(grad_query[head], axis=1) * DH ** (-0.5)
        turned[span, :] = turn(grad, cosine, -sine).astype(bfloat)
        grad = jnp.concatenate(grad_key[head], axis=0).T
        turned[width + span.start : width + span.stop, :] = turn(grad, cosine, -sine).astype(bfloat)
        grad = jnp.concatenate(grad_value[head], axis=0).T
        turned[2 * width + span.start : 2 * width + span.stop, :] = grad.astype(bfloat)
    stores = go((turned, turned_ref))
    wait(later)
    hold[...] = mul(turned[...], tokens[...])
    result[: 3 * width, :] = hold[...].astype(result.dtype)
    stores += go((result, out_ref))
    part = jnp.zeros((8, hold.shape[1]), single)
    for span in spans(hold.shape[0]):
        part = part + fold_rows(hold[span, :] * qkv_weight[span, :].astype(single))
    gain = jnp.sum(part, axis=0, keepdims=True) / gain_ref[...].reshape(1, -1)
    if before_refs:
        gain_part_ref, mlp_part_ref, dwa_part_ref = before_refs
        small_ref[:1, :] = gain + gain_part_ref[...]
        small_ref[1:2, :] = mlp_part_ref[...]
        small_ref[2:, :] = dwa_part_ref[...]
    else:
        small_ref[...] = gain
    wait(stores)


def first_grad_body(
    core_ref, small_ref, turned_a_ref, turned_b_ref, weight_a_ref, weight_b_ref, send_ref, keep_ref,
    turned_a, turned_b, weight_a, weight_b, whole, marks,
):
    low = pl.multiple_of(core_ref[0] * HALF, HALF)
    high = pl.multiple_of((1 - core_ref[0]) * HALF, HALF)
    go = Mover(marks)
    wait(go((turned_a_ref, turned_a), (weight_a_ref, weight_a), (turned_b_ref, turned_b), (weight_b_ref, weight_b)))
    whole[...] = mul(turned_a[...], weight_a[...], 0, 0) + mul(turned_b[...], weight_b[...], 0, 0)
    stores = go((whole.at[pl.ds(low, HALF), :], keep_ref))
    send_ref[:HALF, :] = whole[pl.ds(high, HALF), :].astype(bfloat)
    small = small_ref[...]
    high_part = small.astype(bfloat)
    low_part = (small - high_part.astype(single)).astype(bfloat)
    send_ref[HALF:, :] = jnp.concatenate([high_part, low_part], axis=0)
    wait(stores)


CURVE = float(np.sqrt(2.0 / np.pi))
STEP = 256


def mlp_body(second, *refs):
    if second:
        owner_ref, refs = refs[0], refs[1:]
    x_refs, refs = refs[: 2 * PARTS], refs[2 * PARTS :]
    g_own_ref, g_peer_ref, refs = refs[0], refs[1], refs[2:]
    if second:
        up_ref, down_refs, refs = refs[0], refs[1 : 1 + SQUARE], refs[1 + SQUARE :]
        before_refs, up_mine_ref = refs[:4], refs[4]
        down_grad_ref, part_refs = refs[9], refs[10:14]
        refs = refs[5:9] + refs[14:]
    else:
        up_ref, down_ref = refs[:2]
        down_grad_ref, up_grad_ref = refs[6:8]
        refs = refs[2:6] + refs[8:]
    send_norm_ref, keep_norm_ref, send_out_ref, keep_out_ref = refs[:4]
    x_all, g_all, up, down, active, grad_hidden, x_turned = refs[4:11]
    send_norm, keep_norm, send_out, keep_out, down_grad, up_grad, marks = refs[11:18]
    rows, size = x_all.shape[0] // 2, x_all.shape[0] // (2 * PARTS)
    units = down.shape[0]
    go = Mover(marks)
    x_loads = go(*[(x_refs[index], x_all.at[pl.ds(index * size, size), :]) for index in range(2 * PARTS)])
    if second:
        loads = go((up_ref, up), *joined(owner_ref[0], down_refs, down))
    else:
        loads = go((up_ref, up), (down_ref, down))
    loads += go((g_own_ref, g_all.at[pl.ds(0, rows), :]), (g_peer_ref, g_all.at[pl.ds(rows, rows), :]))
    more, mine, stores = [], [], []
    if second:
        (up_mine,) = refs[18:]
        more = go(*zip(before_refs, (send_norm, keep_norm, send_out, keep_out)))
        mine = go((up_mine_ref, up_mine))
    wait(x_loads)
    x_turned[...] = x_all[...].T
    wait(loads)
    for begin in range(0, units, STEP):
        columns = slice(begin, begin + STEP)
        for top in range(0, 2 * rows, rows):
            span = slice(top, top + rows)
            v = mul(x_all[span, :], up[:, columns])
            grad = mul(g_all[span, :], down[columns, :], 1, 1)
            square = v * v
            half = 0.5 + 0.5 * jnp.tanh(v * (CURVE + (CURVE * 0.044715) * square))
            act = v * half
            slope = half + act * (1.0 - half) * (2.0 * CURVE + (6.0 * CURVE * 0.044715) * square)
            active[span, columns] = act.astype(bfloat)
            grad_hidden[span, columns] = (grad * slope).astype(bfloat)

    def put(target, value):
        target[...] = (value + target[...].astype(single) if second else value).astype(target.dtype)

    wait(more)
    put(keep_norm, mul(grad_hidden[:rows, :], up[...], 1, 1))
    put(send_norm, mul(grad_hidden[rows:, :], up[...], 1, 1))
    stores += go((keep_norm, keep_norm_ref), (send_norm, send_norm_ref))
    down_grad[...] = mul(active[...], g_all[...], 0, 0).astype(down_grad.dtype)
    stores += go((down_grad, down_grad_ref))
    up_grad[...] = mul(x_turned[...], grad_hidden[...]).astype(bfloat)
    if second:
        wait(mine)
        part = up_grad.shape[0] // SQUARE
        for mask, part_ref in enumerate(part_refs):
            rows_of = quarter(owner_ref[0], mask, part)
            stores += go(
                (up_mine.at[rows_of, :], part_ref.at[pl.ds(0, part), :]),
                (up_grad.at[rows_of, :], part_ref.at[pl.ds(part, part), :]),
            )
    else:
        stores += go((up_grad, up_grad_ref))
    put(keep_out, mul(active[:rows, :], down[...]))
    stores += go((keep_out, keep_out_ref))
    put(send_out, mul(active[rows:, :], down[...]))
    wait(stores + go((send_out, send_out_ref)))


def mlp(x_own, x_peer, g_own, g_peer, up, down, upper=(), before=(), flops=0):
    rows, width = g_own.shape
    units = sum(piece.shape[0] for piece in down)
    tall = (2 * rows, width)
    pair = [((rows, width), bfloat), ((rows, width), single)] * 2
    outs = pair + [((units, width), bfloat)]
    outs += [((2 * width // SQUARE, units), bfloat)] * SQUARE if before else [((width, units), bfloat)]
    scratch = [
        pltpu.VMEM(tall, bfloat),
        pltpu.VMEM(tall, bfloat),
        pltpu.VMEM((width, units), bfloat),
        pltpu.VMEM((units, width), bfloat),
        pltpu.VMEM((2 * rows, units), bfloat),
        pltpu.VMEM((2 * rows, units), bfloat),
        pltpu.VMEM((width, 2 * rows), bfloat),
    ]
    scratch += [pltpu.VMEM(shape, kind) for shape, kind in pair]
    scratch += [
        pltpu.VMEM((units, width), bfloat), pltpu.VMEM((width, units), bfloat), pltpu.SemaphoreType.DMA((32,)),
    ]
    if before:
        scratch.append(pltpu.VMEM((width, units), bfloat))
    operands = (*upper, *x_own, *x_peer, g_own, g_peer, *up, *down, *before)
    return call(
        functools.partial(mlp_body, bool(before)),
        outs,
        operands,
        scratch,
        len(upper),
        vmem=40,
        flops=flops,
        far=len(operands) - len(upper),
        far_outs=len(outs),
    )


def shards(
    inputs,
    history,
    cotangent,
    qkv_weight,
    out_weight,
    up_weight,
    down_weight,
    gain_attn,
    gain_mlp,
    dwa_weights,
):
    rows, width = inputs.shape
    members = lax.axis_size("mp")
    copies = lax.axis_size("dp")
    bits = copies.bit_length() - 1
    core = lax.rem(lax.axis_index("mp"), 2).astype(jnp.int32).reshape(1)
    copy_index = lax.axis_index("dp").astype(jnp.int32).reshape(1)
    core_pairs = [(i, i ^ 1) for i in range(members)]
    chip_pairs = [(i, i ^ 2) for i in range(members)]
    depth = history.shape[0]
    part = out_weight.shape[0]

    def other_core(value):
        return lax.ppermute(value, "mp", core_pairs)

    def other_chip(value):
        return lax.ppermute(value, "mp", chip_pairs)

    def other_copy(value, mask):
        return lax.ppermute(value, "dp", [(i, i ^ mask) for i in range(copies)])

    owner = copy_index & (SQUARE - 1)
    cosine, sine = (jnp.asarray(table) for table in tables())

    qkv_own = qkv_weight.transpose(1, 2, 0).reshape(3 * part, width)
    fourth = (width // SQUARE, width)
    square = (width, width)
    masks = range(1, SQUARE)
    marks = pltpu.SemaphoreType.DMA((16,))
    (down_quarter,) = call(
        split_body,
        [(fourth, bfloat)],
        (owner, down_weight),
        [pltpu.VMEM(fourth, bfloat), marks],
        1,
        vmem=60,
        far=1,
        far_outs=1,
    )
    qkv_peer, out_peer = other_chip(qkv_own), other_chip(out_weight)
    down_come, up_peer = other_chip(down_quarter), other_chip(up_weight)

    full = (rows, width)
    x_own = call(norm_body, [((rows // 2, width), bfloat)] * 2, (inputs, gain_attn), after=(down_quarter,))
    x_peer = [other_core(value) for value in x_own]
    tall = (SEQ, width)
    tokens = pltpu.VMEM(tall, bfloat)
    first_outs = [
        ((3 * part, SEQ), bfloat), ((part, SEQ), bfloat), ((SEQ, part), bfloat), ((8, SEQ), single),
    ]
    heads = part // DH
    tiles = [tokens, pltpu.VMEM((heads, SEQ, 256), single), pltpu.VMEM((heads, SEQ, 256), bfloat)]
    qkv_a, att_a, nat_a, log_a = call(
        attend_placed, first_outs, (core, *x_own, *x_peer, cosine, sine, qkv_own), tiles, 1, vmem=32
    )
    history_grad, mixed, g_own, history_parts = average_history(dwa_weights, history, cotangent, (log_a,))
    g_peer = other_core(g_own)
    qkv_b, att_b, nat_b, log_b = call(
        attend_placed,
        first_outs,
        (core, *x_own, *x_peer, cosine, sine, qkv_peer),
        tiles,
        1,
        (history_parts,),
        32,
        MUCH,
    )
    third = (rows // PARTS, width)
    keep, *send, down_copy = call(
        branch_body,
        [(full, single)] + [(third, bfloat)] * PARTS + [(fourth, bfloat)],
        (core, nat_a, nat_b, out_weight, out_peer, down_come),
        (),
        1,
        (g_peer,),
    )
    down_pieces = [down_come] + [other_copy(down_copy, mask) for mask in masks]
    recv = [other_core(value) for value in send]
    middle, *y_own = call(
        middle_body, [(full, single)] + [(third, bfloat)] * PARTS, (inputs, keep, gain_mlp, *recv)
    )
    y_peer = [other_core(value) for value in y_own]

    first = mlp(y_own, y_peer, g_own, g_peer, (up_weight,), (down_weight,))
    down_mine, up_mine = first[4:]
    second = mlp(
        y_own, y_peer, g_own, g_peer, (up_peer,), down_pieces, (owner,), (*first[:4], up_mine)
    )
    send_norm, keep_norm, send_out, keep_out, down_theirs = second[:5]
    token = [send_norm]

    def step(body, outs, operands, scratch=(), scalars=0, vmem=16, flops=MUCH, far=0, far_outs=0):
        results = call(body, outs, operands, scratch, scalars, tuple(token), vmem, flops, far, far_outs)
        token[0] = results[0]
        return results

    down_come = other_chip(down_theirs)
    up_parts = [second[5]] + [other_copy(value, mask) for mask, value in zip(masks, second[6:])]
    out_come = other_core(send_out)
    grad_middle, gb_own, gain_mlp_part = step(
        middle_back_body,
        [(full, single), (full, bfloat), ((1, width), single)],
        (dwa_weights, middle, keep_norm, other_core(send_norm), cotangent, gain_mlp),
        scalars=1,
        flops=0,
    )
    gb_peer = other_core(gb_own)
    combined, dwa_part = step(
        combine_body,
        [(full, bfloat), ((depth + 1, width), single)],
        (dwa_weights, mixed, middle, keep_out, out_come, cotangent, history_parts),
        scalars=1,
        flops=0,
    )

    def back(weight, qkv_weight, qkv, att, log, flops, before=()):
        return step(
            attend_back,
            [
                ((depth + 3 if before else 1, width), single),
                ((4 * part, width), bfloat),
                ((3 * part, SEQ), bfloat),
            ],
            (
                core, log, cosine, sine, gain_attn, *before, gb_own, gb_peer, *x_own, *x_peer, weight, qkv_weight, qkv,
                att,
            ),
            [
                pltpu.VMEM(tall, bfloat),
                pltpu.VMEM(tall, bfloat),
                pltpu.VMEM((part, width), bfloat),
                pltpu.VMEM((3 * part, width), bfloat),
                pltpu.VMEM((3 * part, SEQ), bfloat),
                pltpu.VMEM((part, SEQ), bfloat),
                pltpu.VMEM((3 * part, SEQ), bfloat),
                pltpu.VMEM((4 * part, width), bfloat),
                pltpu.VMEM((heads, SEQ, SEQ), bfloat),
                pltpu.VMEM((heads, SEQ, SEQ), bfloat),
                pltpu.VMEM((3 * part, width), single),
                marks,
            ],
            1,
            36,
            flops,
            10,
            2,
        )

    gain_part, att_theirs, turned_b = back(out_peer, qkv_peer, qkv_b, att_b, log_b, 0)
    att_come = other_chip(att_theirs)
    def spread(mine, come, flops=MUCH):
        own, *sent = step(part_body, [(fourth, bfloat)] * SQUARE, (owner, mine, come), scalars=1, flops=flops)
        return [own] + [other_copy(value, mask) for mask, value in zip(masks, sent)]

    down_parts = spread(down_mine, down_come, 0)
    up, sent = step(four_two_body, [(fourth, bfloat)] * 2, up_parts, flops=0)
    up_come = other_chip(sent)
    part_sums, att_mine, turned_a = back(
        out_weight, qkv_own, qkv_a, att_a, log_a, MUCH, (gain_part, gain_mlp_part, dwa_part)
    )

    def exchange(value):
        for bit in range(2, bits):
            come = other_copy(value, 1 << bit)
            if bit < bits - 1:
                (value,) = step(low_body, [(value.shape, bfloat)], (value, come))
        return value, come

    def finish(value, come):
        (value,) = step(low_body, [(value.shape, bfloat)], (value, come), flops=COST)
        return [value] + [other_copy(value, mask) for mask in masks]

    (down,) = step(four_body, [(fourth, bfloat)], down_parts, flops=COST)
    down = exchange(down)
    att_parts = spread(att_mine, att_come, COST)
    (up,) = step(low_body, [(fourth, bfloat)], (up, up_come), flops=COST)
    up = exchange(up)
    send_first, keep_first = step(
        first_grad_body,
        [((rows + EXTRA, width), bfloat), (full, single)],
        (core, part_sums, turned_a, turned_b, qkv_own, qkv_peer),
        [pltpu.VMEM((3 * part, SEQ), bfloat)] * 2
        + [pltpu.VMEM((3 * part, width), bfloat)] * 2
        + [pltpu.VMEM(tall, single), marks],
        1,
        60,
        COST,
        4,
        1,
    )
    first_come = other_core(send_first)
    token.append(down[1])
    step(mark_body, [((8, 128), single)], (), flops=COST)
    del token[1:]
    (part_sums,) = step(small_body, [(part_sums.shape, single)], (part_sums, first_come), flops=COST)
    more_sums = other_chip(part_sums)
    (input_grad,) = step(
        first_back_body,
        [(full, bfloat)],
        (inputs, keep_first, first_come, grad_middle, gain_attn),
        vmem=60,
        flops=COST,
    )
    block = (width // SQUARE + EXTRA, width)
    pair = (2 * fourth[0], width)
    token.append(more_sums)
    (both,) = step(pair_body, [(pair, bfloat)], (*down, *up), flops=COST)
    token.pop()
    both = [both] + [other_copy(both, mask) for mask in masks]
    (att,) = step(four_more_body, [(block, bfloat)], (part_sums, more_sums, *att_parts), flops=COST)
    att = exchange(att)
    (gate,) = step(mark_body, [((8, 128), single)], (), flops=COST)
    att = finish(*att)
    down_grad, up_grad = step(
        pair_whole_body,
        [(square, single)] * 2,
        (owner, *both),
        [pltpu.VMEM((SQUARE * pair[0], width), bfloat)],
        1,
        flops=COST,
    )
    qkv_grad, out_grad, gain_attn_grad, gain_mlp_grad, dwa_grad = step(
        more_body,
        [
            ((3 * part, width), single),
            ((part, width), single),
            ((width,), single),
            ((width,), single),
            ((depth + 1,), single, "scalars"),
        ],
        (owner, *att),
        [pltpu.VMEM((SQUARE * block[0], width), bfloat)],
        1,
        flops=COST,
    )

    return (
        combined,
        input_grad,
        history_grad,
        qkv_grad.reshape(3, part, width).transpose(2, 0, 1),
        out_grad,
        up_grad,
        down_grad,
        gain_attn_grad,
        gain_mlp_grad,
        dwa_grad,
    )


def solution(mesh):
    placed = (
        P(("dp", "mp"), None),
        P(None, ("dp", "mp"), None),
        P(("dp", "mp"), None),
        P(None, None, "mp"),
        P("mp", None),
        P(None, "mp"),
        P("mp", None),
        P(),
        P(),
        P(),
    )
    return jax.shard_map(
        shards,
        mesh=mesh,
        in_specs=placed,
        out_specs=(
            P(("dp", "mp"), None),
            P(("dp", "mp"), None),
            P(None, ("dp", "mp"), None),
            P(None, None, "mp"),
            P("mp", None),
            P(None, "mp"),
            P("mp", None),
            P(),
            P(),
            P(),
        ),
        check_vma=False,
    )
```

```python
import functools

import jax
import jax.numpy as jnp
import numpy as np
from jax import lax
from jax.experimental import pallas as pl
from jax.experimental.pallas import tpu as pltpu
from jax.sharding import PartitionSpec as P

DH = 64
SEQ = 1152
HALF = SEQ // 2
EPS = 1e-05
bfloat = jnp.bfloat16
single = jnp.float32
MIB = 1 << 20
MUCH = 10**11
COST = 10**10


def tables():
    half_width = DH // 2
    places = np.arange(SEQ, dtype=np.float32)
    frequency = np.float32(10000.0) ** (-np.arange(half_width, dtype=np.float32) * np.float32(2.0 / DH))
    angles = frequency[:, None] * places[None, :]
    return (np.cos(angles).astype(np.float32), np.sin(angles).astype(np.float32))


def mul(a, b, ca=1, cb=0):
    return lax.dot_general(a, b, (((ca,), (cb,)), ((), ())), preferred_element_type=single)


def call(kernel, outs, operands, scratch=(), scalars=0, after=(), vmem=16, flops=0, far=0, far_outs=0):
    count, waits = len(operands), len(after)

    def body(*refs):
        kernel(*refs[:count], *refs[count + waits :])

    small = pl.BlockSpec(memory_space=pltpu.SMEM)
    whole = pl.BlockSpec(memory_space=pltpu.VMEM)
    apart = pl.BlockSpec(memory_space=pltpu.HBM)
    loose = pl.BlockSpec(memory_space=pl.ANY)
    inner = len(outs) - far_outs
    return pl.pallas_call(
        body,
        out_shape=[jax.ShapeDtypeStruct(out[0], out[1]) for out in outs],
        in_specs=[small] * scalars + [whole] * (count - scalars - far) + [apart] * far + [loose] * waits,
        out_specs=[small if len(out) > 2 else whole for out in outs[:inner]] + [apart] * far_outs,
        scratch_shapes=list(scratch),
        compiler_params=pltpu.CompilerParams(vmem_limit_bytes=vmem * MIB),
        cost_estimate=pl.CostEstimate(flops=flops, bytes_accessed=0, transcendentals=0),
    )(*operands, *after)


class Mover:
    def __init__(self, marks):
        self.marks = marks
        self.used = 0

    def __call__(self, *pairs):
        copies = []
        for source, target in pairs:
            copies.append(pltpu.make_async_copy(source, target, self.marks.at[self.used]))
            self.used += 1
        for copy in copies:
            copy.start()
        return copies


def wait(copies):
    for copy in copies:
        copy.wait()


ROWS = 64
PARTS = 1


def spans(rows, step=ROWS):
    return [slice(begin, begin + step) for begin in range(0, rows, step)]


def normal_of(x):
    centre = x - jnp.mean(x, axis=-1, keepdims=True)
    spread = jnp.mean(centre * centre, axis=-1, keepdims=True)
    scale = lax.rsqrt(spread + EPS)
    return centre * scale, scale


def split_body(owner_ref, in_ref, out_ref, hold, marks):
    go = Mover(marks)
    wait(go((in_ref.at[quarter(owner_ref[0], 0, hold.shape[0]), :], hold)))
    wait(go((hold, out_ref)))


def joined(owner, refs, target):
    size = refs[0].shape[0]
    return [(ref, target.at[quarter(owner, mask, size), :]) for mask, ref in enumerate(refs)]


def norm_body(x_ref, gain_ref, *out_refs):
    gain = gain_ref[...].reshape(1, -1)
    for index, out_ref in enumerate(out_refs):
        rows = out_ref.shape[0]
        for span in spans(rows, rows // 6):
            here = slice(index * rows + span.start, index * rows + span.stop)
            normal, _ = normal_of(x_ref[here, :].astype(single))
            out_ref[span, :] = (normal * gain).astype(bfloat)


def middle_body(x_ref, keep_ref, gain_ref, *rest):
    recv_refs, mid_ref, out_refs = rest[:PARTS], rest[PARTS], rest[PARTS + 1 :]
    gain = gain_ref[...].reshape(1, -1)
    rows = x_ref.shape[0] // PARTS
    for index in range(PARTS):
        for span in spans(rows):
            here = slice(index * rows + span.start, index * rows + span.stop)
            recv = recv_refs[index][span, :].astype(single)
            x = x_ref[here, :].astype(single) + (keep_ref[here, :] + recv)
            mid_ref[here, :] = x
            normal, _ = normal_of(x)
            out_refs[index][span, :] = (normal * gain).astype(bfloat)


def norm_back(x, grad, gain):
    normal, scale = normal_of(x)
    lifted = grad * gain
    back = scale * (
        lifted
        - jnp.mean(lifted, axis=-1, keepdims=True)
        - normal * jnp.mean(lifted * normal, axis=-1, keepdims=True)
    )
    return back, normal


def fold_rows(value):
    total = value[:8]
    for begin in range(8, value.shape[0], 8):
        total = total + value[begin : begin + 8]
    return total


def middle_back_body(mix_ref, x_ref, keep_ref, recv_ref, cot_ref, gain_ref, mid_ref, low_ref, part_ref):
    gain = gain_ref[...].reshape(1, -1)
    part = jnp.zeros((8, x_ref.shape[1]), single)
    for span in spans(x_ref.shape[0]):
        grad = keep_ref[span, :] + recv_ref[span, :].astype(single)
        back, normal = norm_back(x_ref[span, :], grad, gain)
        total = mix_ref[mix_ref.shape[0] - 1] * cot_ref[span, :] + back
        mid_ref[span, :] = total
        low_ref[span, :] = total.astype(bfloat)
        part = part + fold_rows(grad * normal)
    part_ref[...] = jnp.sum(part, axis=0, keepdims=True)


def first_back_body(x_ref, keep_ref, recv_ref, mid_ref, gain_ref, out_ref):
    gain = gain_ref[...].reshape(1, -1)
    for span in spans(x_ref.shape[0]):
        grad = keep_ref[span, :] + recv_ref[span, :].astype(single)
        back, _ = norm_back(x_ref[span, :].astype(single), grad, gain)
        out_ref[span, :] = (mid_ref[span, :] + back).astype(bfloat)


def history_body(mix_ref, history_ref, cot_ref, grad_ref, mixed_ref, low_ref, part_ref):
    depth = history_ref.shape[0]

    @pl.when(pl.program_id(0) == 0)
    def _():
        part_ref[...] = jnp.zeros_like(part_ref)

    for span in spans(cot_ref.shape[0], 32):
        cot = cot_ref[span, :]
        low_ref[span, :] = (mix_ref[depth] * cot).astype(bfloat)
        mixed = None
        for j in range(depth):
            layer = history_ref[j, span, :].astype(single)
            mixed = mix_ref[j] * layer if mixed is None else mixed + mix_ref[j] * layer
            grad_ref[j, span, :] = (mix_ref[j] * cot).astype(bfloat)
            part_ref[8 * j : 8 * j + 8, :] += fold_rows(layer * cot)
        mixed_ref[span, :] = mixed


def average_history(mix, history, cot, after=()):
    depth, rows, width = history.shape
    step = 96
    waits = len(after)

    def body(*refs):
        history_body(*refs[:3], *refs[3 + waits :])

    row_block = pl.BlockSpec((step, width), lambda i: (i, 0))
    deep_block = pl.BlockSpec((depth, step, width), lambda i: (0, i, 0))
    return pl.pallas_call(
        body,
        grid=(rows // step,),
        out_shape=[
            jax.ShapeDtypeStruct(history.shape, bfloat),
            jax.ShapeDtypeStruct((rows, width), single),
            jax.ShapeDtypeStruct((rows, width), bfloat),
            jax.ShapeDtypeStruct((8 * depth, width), single),
        ],
        in_specs=[pl.BlockSpec(memory_space=pltpu.SMEM), deep_block, row_block]
        + [pl.BlockSpec(memory_space=pl.ANY)] * waits,
        out_specs=[deep_block, row_block, row_block, pl.BlockSpec((8 * depth, width), lambda i: (0, 0))],
        compiler_params=pltpu.CompilerParams(vmem_limit_bytes=16 * MIB),
        cost_estimate=pl.CostEstimate(flops=0, bytes_accessed=0, transcendentals=0),
    )(mix, history, cot, *after)


def combine_body(mix_ref, mixed_ref, mid_ref, keep_ref, recv_ref, cot_ref, parts_ref, out_ref, part_ref):
    depth = mix_ref.shape[0] - 1
    last = jnp.zeros((8, mid_ref.shape[1]), single)
    for span in spans(mid_ref.shape[0]):
        outputs = mid_ref[span, :] + (keep_ref[span, :] + recv_ref[span, :].astype(single))
        out_ref[span, :] = (mixed_ref[span, :] + mix_ref[depth] * outputs).astype(bfloat)
        last = last + fold_rows(outputs * cot_ref[span, :])
    for j in range(depth):
        part_ref[j : j + 1, :] = jnp.sum(parts_ref[8 * j : 8 * j + 8, :], axis=0, keepdims=True)
    part_ref[depth : depth + 1, :] = jnp.sum(last, axis=0, keepdims=True)


SQUARE = 4


def quarter(owner, mask, size):
    other = owner + (mask & 1) * (1 - 2 * (owner % 2)) + (mask & 2) * (1 - 2 * (owner // 2))
    return pl.ds(pl.multiple_of(other * size, size), size)


def part_body(owner_ref, mine_ref, come_ref, *out_refs):
    for mask, out_ref in enumerate(out_refs):
        rows = quarter(owner_ref[0], mask, out_ref.shape[0])
        out_ref[...] = (mine_ref[rows, :].astype(single) + come_ref[rows, :].astype(single)).astype(bfloat)


def sum_of(refs, rows):
    total = refs[0][rows, :].astype(single)
    for ref in refs[1:]:
        total = total + ref[rows, :].astype(single)
    return total


def four_body(*refs):
    refs[-1][...] = sum_of(refs[:-1], slice(None)).astype(bfloat)


def four_two_body(*refs):
    size = refs[-1].shape[0]
    refs[-2][...] = sum_of(refs[:-2], slice(0, size)).astype(bfloat)
    refs[-1][...] = sum_of(refs[:-2], slice(size, 2 * size)).astype(bfloat)


EXTRA = 16


def mark_body(out_ref):
    out_ref[...] = jnp.zeros_like(out_ref)


def copy_body(in_ref, out_ref):
    out_ref[...] = in_ref[...]


def small_body(small_ref, first_ref, out_ref):
    half = small_ref.shape[0]
    rows = first_ref.shape[0] - 2 * half
    come = first_ref[rows:, :].astype(single)
    out_ref[...] = small_ref[...] + (come[:half] + come[half:])


def four_more_body(small_ref, more_ref, *refs):
    out_ref = refs[-1]
    size = out_ref.shape[0] - EXTRA
    out_ref[:size, :] = sum_of(refs[:-1], slice(None)).astype(bfloat)
    small = small_ref[...] + more_ref[...]
    rest = jnp.zeros((EXTRA - small.shape[0], small.shape[1]), single)
    out_ref[size:, :] = jnp.concatenate([small, rest], axis=0).astype(bfloat)


def gather(owner_ref, pieces, hold):
    for mask, piece in enumerate(pieces):
        hold[quarter(owner_ref[0], mask, piece.shape[0]), :] = piece[...]


def pair_body(a_ref, a_come_ref, b_ref, b_come_ref, out_ref):
    size = a_ref.shape[0]
    out_ref[:size, :] = sum_of((a_ref, a_come_ref), slice(None)).astype(bfloat)
    out_ref[size:, :] = sum_of((b_ref, b_come_ref), slice(None)).astype(bfloat)


def pair_whole_body(owner_ref, a_ref, b_ref, c_ref, d_ref, down_ref, up_ref, hold):
    gather(owner_ref, (a_ref, b_ref, c_ref, d_ref), hold)
    block = hold.shape[0] // SQUARE
    size = block // 2
    for index in range(SQUARE):
        begin, rows = index * block, slice(index * size, (index + 1) * size)
        down_ref[rows, :] = hold[begin : begin + size, :].astype(single)
        up_ref[rows, :] = hold[begin + size : begin + block, :].astype(single)


def more_body(owner_ref, a_ref, b_ref, c_ref, d_ref, top_ref, end_ref, attn_ref, mlp_ref, dwa_ref, hold):
    gather(owner_ref, (a_ref, b_ref, c_ref, d_ref), hold)
    block = hold.shape[0] // SQUARE
    rows = block - EXTRA
    small = jnp.zeros((EXTRA, hold.shape[1]), single)
    for index in range(SQUARE):
        begin = index * block
        target, place = (top_ref, index * rows) if index < SQUARE - 1 else (end_ref, 0)
        target[place : place + rows, :] = hold[begin : begin + rows, :].astype(single)
        small = small + hold[begin + rows : begin + block, :].astype(single)
    attn_ref[...] = small[0]
    mlp_ref[...] = small[1]
    for index in range(dwa_ref.shape[0]):
        dwa_ref[index] = jnp.sum(small[2 + index : 3 + index])


def low_body(mine_ref, come_ref, out_ref):
    out_ref[...] = (mine_ref[...].astype(single) + come_ref[...].astype(single)).astype(bfloat)


def mark_body(out_ref):
    out_ref[...] = jnp.zeros_like(out_ref)


def copy_body(in_ref, out_ref):
    out_ref[...] = in_ref[...]


def small_body(small_ref, first_ref, out_ref):
    half = small_ref.shape[0]
    rows = first_ref.shape[0] - 2 * half
    come = first_ref[rows:, :].astype(single)
    out_ref[...] = small_ref[...] + (come[:half] + come[half:])


BLOCKS = tuple((begin, min(256, SEQ - begin)) for begin in range(0, SEQ, 256))


def places(core_ref, refs):
    count, size = len(refs) // 2, refs[0].shape[0]
    for index, ref in enumerate(refs):
        core = core_ref[0] if index < count else 1 - core_ref[0]
        yield ref, pl.ds(pl.multiple_of(core * HALF + index % count * size, size), size)


def allowed(size):
    key_pos = lax.broadcasted_iota(jnp.int32, (size, size), 0)
    query_pos = lax.broadcasted_iota(jnp.int32, (size, size), 1)
    return query_pos >= key_pos


def turn(rows, cosine, sine):
    half = rows.shape[0] // 2
    a, b = rows[:half], rows[half:]
    return jnp.concatenate([a * cosine - b * sine, b * cosine + a * sine], axis=0)


KEYS = 128


def fold_top(value):
    top = value[:8]
    for begin in range(8, value.shape[0], 8):
        top = jnp.maximum(top, value[begin : begin + 8])
    return top


def masked(scores, offset):
    key_pos = lax.broadcasted_iota(jnp.int32, scores.shape, 0) + offset
    query_pos = lax.broadcasted_iota(jnp.int32, scores.shape, 1)
    return jnp.where(query_pos >= key_pos, scores, -jnp.inf)


def attend_placed(core_ref, *rest):
    for ref, where in places(core_ref, rest[:4]):
        rest[11][where, :] = ref[...]
    cos_ref, sin_ref, weight_ref, rest = rest[4], rest[5], rest[6], rest[7:]
    attend(weight_ref, cos_ref, sin_ref, *rest)


def attend(weight_ref, cos_ref, sin_ref, qkv_ref, att_ref, nat_ref, log_ref, tokens, all_scores, all_weights):
    width = weight_ref.shape[0] // 3
    projected = mul(weight_ref[...], tokens[...], 1, 1)
    cosine, sine = cos_ref[...], sin_ref[...]
    for part in range(3):
        for head in range(width // DH):
            begin = part * width + head * DH
            rows = projected[begin : begin + DH]
            if part < 2:
                rows = turn(rows, cosine, sine)
            if part == 0:
                rows = rows * DH ** (-0.5)
            qkv_ref[begin : begin + DH, :] = rows.astype(bfloat)
    log_ref[...] = jnp.zeros_like(log_ref)
    heads = range(width // DH)
    keys = [qkv_ref[width + head * DH : width + head * DH + DH, :].T for head in heads]
    for begin, size in BLOCKS:
        end = begin + size
        tops = [None for _ in heads]
        for row in range(0, end, KEYS):
            for head in heads:
                tile = mul(keys[head][row : row + KEYS], qkv_ref[head * DH : head * DH + DH, begin:end])
                if row >= begin:
                    tile = masked(tile, row - begin)
                all_scores[head, row : row + KEYS, :size] = tile
                top = fold_top(tile)
                tops[head] = top if row == 0 else jnp.maximum(tops[head], top)
        tops = [jnp.max(top, axis=0, keepdims=True) for top in tops]
        totals = [jnp.zeros((8, size), single) for _ in heads]
        for row in range(0, end, KEYS):
            for head in heads:
                tile = jnp.exp(all_scores[head, row : row + KEYS, :size] - tops[head])
                totals[head] = totals[head] + fold_rows(tile)
                all_weights[head, row : row + KEYS, :size] = tile.astype(bfloat)
        for head in heads:
            base = head * DH
            total = jnp.sum(totals[head], axis=0, keepdims=True)
            value = qkv_ref[2 * width + base : 2 * width + base + DH, :end]
            mixed = mul(value, all_weights[head, :end, :size]) / total
            att_ref[base : base + DH, begin:end] = mixed.astype(bfloat)
            log_ref[head : head + 1, begin:end] = tops[head] + jnp.log(total)
    nat_ref[...] = att_ref[...].T


def branch_body(core_ref, att_a_ref, att_b_ref, out_a_ref, out_b_ref, pass_ref, keep_ref, *rest):
    send_refs, pass_out = rest[:PARTS], rest[PARTS]
    pass_out[...] = pass_ref[...]
    low = pl.multiple_of(core_ref[0] * HALF, HALF)
    rows = HALF // PARTS
    for index in range(PARTS):
        high = pl.multiple_of((1 - core_ref[0]) * HALF + index * rows, rows)
        send = mul(att_a_ref[pl.ds(high, rows), :], out_a_ref[...])
        send_refs[index][...] = (send + mul(att_b_ref[pl.ds(high, rows), :], out_b_ref[...])).astype(bfloat)
    keep = mul(att_a_ref[pl.ds(low, HALF), :], out_a_ref[...])
    keep_ref[...] = keep + mul(att_b_ref[pl.ds(low, HALF), :], out_b_ref[...])


def attend_back(
    core_ref, log_ref, cos_ref, sin_ref, gain_ref, *rest
):
    before_refs, rest = rest[:-25], rest[-25:]
    grad_refs, x_refs = rest[:2], rest[2:6]
    weight_ref, qkv_weight_ref, qkv_ref, att_ref, small_ref, out_ref, turned_ref = rest[6:13]
    grads, tokens, weight, qkv_weight, qkv, att, turned, result, all_probs, all_scores, hold, marks = rest[13:]
    go = Mover(marks)
    first = go(
        (weight_ref, weight),
        *[(ref, grads.at[where, :]) for ref, where in places(core_ref, grad_refs)],
        (att_ref, att),
        (qkv_ref, qkv),
    )
    later = go(
        *[(ref, tokens.at[where, :]) for ref, where in places(core_ref, x_refs)],
        (qkv_weight_ref, qkv_weight),
    )
    wait(first)
    width = att.shape[0]
    grad_att = mul(weight[...], grads[...], 1, 1).astype(bfloat)
    result[3 * width :, :] = mul(att[...], grads[...]).astype(result.dtype)
    cosine, sine = cos_ref[...], sin_ref[...]
    heads = range(width // DH)
    spans_of = [slice(head * DH, head * DH + DH) for head in heads]
    query = [qkv[span, :] for span in spans_of]
    key = [qkv[width + span.start : width + span.stop, :] for span in spans_of]
    above = [grad_att[span] for span in spans_of]
    centre = [
        jnp.sum(above[head].astype(single) * att[span, :].astype(single), axis=0, keepdims=True)
        for head, span in enumerate(spans_of)
    ]
    keys = [value.T for value in key]
    values = [qkv[2 * width + span.start : 2 * width + span.stop, :].T for span in spans_of]
    queries = [value.T for value in query]
    aboves = [value.T for value in above]
    grad_query = [[] for _ in heads]
    for begin, size in BLOCKS:
        end = begin + size
        for row in range(0, end, KEYS):
            span = slice(row, row + KEYS)
            for head in heads:
                tile = mul(keys[head][span], query[head][:, begin:end])
                if row >= begin:
                    tile = masked(tile, row - begin)
                tile = jnp.exp(tile - log_ref[head : head + 1, begin:end])
                grad = mul(values[head][span], above[head][:, begin:end]) - centre[head][:, begin:end]
                all_probs[head, span, begin:end] = tile.astype(bfloat)
                all_scores[head, span, begin:end] = (tile * grad).astype(bfloat)
        for head in heads:
            grad_query[head].append(mul(key[head][:, :end], all_scores[head, :end, begin:end]))
    grad_key = [[] for _ in heads]
    grad_value = [[] for _ in heads]
    for begin, size in BLOCKS:
        span = slice(begin, begin + size)
        for head in heads:
            grad_key[head].append(mul(all_scores[head, span, begin:], queries[head][begin:]))
            grad_value[head].append(mul(all_probs[head, span, begin:], aboves[head][begin:]))
    for head, span in enumerate(spans_of):
        grad = jnp.concatenate(grad_query[head], axis=1) * DH ** (-0.5)
        turned[span, :] = turn(grad, cosine, -sine).astype(bfloat)
        grad = jnp.concatenate(grad_key[head], axis=0).T
        turned[width + span.start : width + span.stop, :] = turn(grad, cosine, -sine).astype(bfloat)
        grad = jnp.concatenate(grad_value[head], axis=0).T
        turned[2 * width + span.start : 2 * width + span.stop, :] = grad.astype(bfloat)
    stores = go((turned, turned_ref))
    wait(later)
    hold[...] = mul(turned[...], tokens[...])
    result[: 3 * width, :] = hold[...].astype(result.dtype)
    stores += go((result, out_ref))
    part = jnp.zeros((8, hold.shape[1]), single)
    for span in spans(hold.shape[0]):
        part = part + fold_rows(hold[span, :] * qkv_weight[span, :].astype(single))
    gain = jnp.sum(part, axis=0, keepdims=True) / gain_ref[...].reshape(1, -1)
    if before_refs:
        gain_part_ref, mlp_part_ref, dwa_part_ref = before_refs
        small_ref[:1, :] = gain + gain_part_ref[...]
        small_ref[1:2, :] = mlp_part_ref[...]
        small_ref[2:, :] = dwa_part_ref[...]
    else:
        small_ref[...] = gain
    wait(stores)


def first_grad_body(
    core_ref, small_ref, turned_a_ref, turned_b_ref, weight_a_ref, weight_b_ref, send_ref, keep_ref,
    turned_a, turned_b, weight_a, weight_b, whole, marks,
):
    low = pl.multiple_of(core_ref[0] * HALF, HALF)
    high = pl.multiple_of((1 - core_ref[0]) * HALF, HALF)
    go = Mover(marks)
    wait(go((turned_a_ref, turned_a), (weight_a_ref, weight_a), (turned_b_ref, turned_b), (weight_b_ref, weight_b)))
    whole[...] = mul(turned_a[...], weight_a[...], 0, 0) + mul(turned_b[...], weight_b[...], 0, 0)
    stores = go((whole.at[pl.ds(low, HALF), :], keep_ref))
    send_ref[:HALF, :] = whole[pl.ds(high, HALF), :].astype(bfloat)
    small = small_ref[...]
    high_part = small.astype(bfloat)
    low_part = (small - high_part.astype(single)).astype(bfloat)
    send_ref[HALF:, :] = jnp.concatenate([high_part, low_part], axis=0)
    wait(stores)


CURVE = float(np.sqrt(2.0 / np.pi))
STEP = 256


def mlp_body(second, *refs):
    if second:
        owner_ref, refs = refs[0], refs[1:]
    x_refs, refs = refs[: 2 * PARTS], refs[2 * PARTS :]
    g_own_ref, g_peer_ref, refs = refs[0], refs[1], refs[2:]
    if second:
        up_ref, down_refs, refs = refs[0], refs[1 : 1 + SQUARE], refs[1 + SQUARE :]
        before_refs, up_mine_ref = refs[:4], refs[4]
        down_grad_ref, part_refs = refs[9], refs[10:14]
        refs = refs[5:9] + refs[14:]
    else:
        up_ref, down_ref = refs[:2]
        down_grad_ref, up_grad_ref = refs[6:8]
        refs = refs[2:6] + refs[8:]
    send_norm_ref, keep_norm_ref, send_out_ref, keep_out_ref = refs[:4]
    x_all, g_all, up, down, active, grad_hidden, x_turned = refs[4:11]
    send_norm, keep_norm, send_out, keep_out, down_grad, up_grad, marks = refs[11:18]
    rows, size = x_all.shape[0] // 2, x_all.shape[0] // (2 * PARTS)
    units = down.shape[0]
    go = Mover(marks)
    x_loads = go(*[(x_refs[index], x_all.at[pl.ds(index * size, size), :]) for index in range(2 * PARTS)])
    if second:
        loads = go((up_ref, up), *joined(owner_ref[0], down_refs, down))
    else:
        loads = go((up_ref, up), (down_ref, down))
    loads += go((g_own_ref, g_all.at[pl.ds(0, rows), :]), (g_peer_ref, g_all.at[pl.ds(rows, rows), :]))
    more, mine, stores = [], [], []
    if second:
        (up_mine,) = refs[18:]
        more = go(*zip(before_refs, (send_norm, keep_norm, send_out, keep_out)))
        mine = go((up_mine_ref, up_mine))
    wait(x_loads)
    x_turned[...] = x_all[...].T
    wait(loads)
    for begin in range(0, units, STEP):
        columns = slice(begin, begin + STEP)
        for top in range(0, 2 * rows, rows):
            span = slice(top, top + rows)
            v = mul(x_all[span, :], up[:, columns])
            grad = mul(g_all[span, :], down[columns, :], 1, 1)
            square = v * v
            half = 0.5 + 0.5 * jnp.tanh(v * (CURVE + (CURVE * 0.044715) * square))
            act = v * half
            slope = half + act * (1.0 - half) * (2.0 * CURVE + (6.0 * CURVE * 0.044715) * square)
            active[span, columns] = act.astype(bfloat)
            grad_hidden[span, columns] = (grad * slope).astype(bfloat)

    def put(target, value):
        target[...] = (value + target[...].astype(single) if second else value).astype(target.dtype)

    wait(more)
    put(keep_norm, mul(grad_hidden[:rows, :], up[...], 1, 1))
    put(send_norm, mul(grad_hidden[rows:, :], up[...], 1, 1))
    stores += go((keep_norm, keep_norm_ref), (send_norm, send_norm_ref))
    down_grad[...] = mul(active[...], g_all[...], 0, 0).astype(down_grad.dtype)
    stores += go((down_grad, down_grad_ref))
    up_grad[...] = mul(x_turned[...], grad_hidden[...]).astype(bfloat)
    if second:
        wait(mine)
        part = up_grad.shape[0] // SQUARE
        for mask, part_ref in enumerate(part_refs):
            rows_of = quarter(owner_ref[0], mask, part)
            stores += go(
                (up_mine.at[rows_of, :], part_ref.at[pl.ds(0, part), :]),
                (up_grad.at[rows_of, :], part_ref.at[pl.ds(part, part), :]),
            )
    else:
        stores += go((up_grad, up_grad_ref))
    put(keep_out, mul(active[:rows, :], down[...]))
    stores += go((keep_out, keep_out_ref))
    put(send_out, mul(active[rows:, :], down[...]))
    wait(stores + go((send_out, send_out_ref)))


def mlp(x_own, x_peer, g_own, g_peer, up, down, upper=(), before=(), flops=0):
    rows, width = g_own.shape
    units = sum(piece.shape[0] for piece in down)
    tall = (2 * rows, width)
    pair = [((rows, width), bfloat), ((rows, width), single)] * 2
    outs = pair + [((units, width), bfloat)]
    outs += [((2 * width // SQUARE, units), bfloat)] * SQUARE if before else [((width, units), bfloat)]
    scratch = [
        pltpu.VMEM(tall, bfloat),
        pltpu.VMEM(tall, bfloat),
        pltpu.VMEM((width, units), bfloat),
        pltpu.VMEM((units, width), bfloat),
        pltpu.VMEM((2 * rows, units), bfloat),
        pltpu.VMEM((2 * rows, units), bfloat),
        pltpu.VMEM((width, 2 * rows), bfloat),
    ]
    scratch += [pltpu.VMEM(shape, kind) for shape, kind in pair]
    scratch += [
        pltpu.VMEM((units, width), bfloat), pltpu.VMEM((width, units), bfloat), pltpu.SemaphoreType.DMA((32,)),
    ]
    if before:
        scratch.append(pltpu.VMEM((width, units), bfloat))
    operands = (*upper, *x_own, *x_peer, g_own, g_peer, *up, *down, *before)
    return call(
        functools.partial(mlp_body, bool(before)),
        outs,
        operands,
        scratch,
        len(upper),
        vmem=60,
        flops=flops,
        far=len(operands) - len(upper),
        far_outs=len(outs),
    )


def shards(
    inputs,
    history,
    cotangent,
    qkv_weight,
    out_weight,
    up_weight,
    down_weight,
    gain_attn,
    gain_mlp,
    dwa_weights,
):
    rows, width = inputs.shape
    members = lax.axis_size("mp")
    copies = lax.axis_size("dp")
    bits = copies.bit_length() - 1
    core = lax.rem(lax.axis_index("mp"), 2).astype(jnp.int32).reshape(1)
    copy_index = lax.axis_index("dp").astype(jnp.int32).reshape(1)
    core_pairs = [(i, i ^ 1) for i in range(members)]
    chip_pairs = [(i, i ^ 2) for i in range(members)]
    depth = history.shape[0]
    part = out_weight.shape[0]

    def other_core(value):
        return lax.ppermute(value, "mp", core_pairs)

    def other_chip(value):
        return lax.ppermute(value, "mp", chip_pairs)

    def other_copy(value, mask):
        return lax.ppermute(value, "dp", [(i, i ^ mask) for i in range(copies)])

    owner = copy_index & (SQUARE - 1)
    cosine, sine = (jnp.asarray(table) for table in tables())

    qkv_own = qkv_weight.transpose(1, 2, 0).reshape(3 * part, width)
    fourth = (width // SQUARE, width)
    square = (width, width)
    masks = range(1, SQUARE)
    marks = pltpu.SemaphoreType.DMA((16,))
    (down_quarter,) = call(
        split_body,
        [(fourth, bfloat)],
        (owner, down_weight),
        [pltpu.VMEM(fourth, bfloat), marks],
        1,
        vmem=60,
        far=1,
        far_outs=1,
    )
    qkv_peer, out_peer = other_chip(qkv_own), other_chip(out_weight)
    down_come, up_peer = other_chip(down_quarter), other_chip(up_weight)

    full = (rows, width)
    x_own = call(norm_body, [((rows // 2, width), bfloat)] * 2, (inputs, gain_attn), after=(down_quarter,))
    x_peer = [other_core(value) for value in x_own]
    tall = (SEQ, width)
    tokens = pltpu.VMEM(tall, bfloat)
    first_outs = [
        ((3 * part, SEQ), bfloat), ((part, SEQ), bfloat), ((SEQ, part), bfloat), ((8, SEQ), single),
    ]
    heads = part // DH
    tiles = [tokens, pltpu.VMEM((heads, SEQ, 256), single), pltpu.VMEM((heads, SEQ, 256), bfloat)]
    qkv_a, att_a, nat_a, log_a = call(
        attend_placed, first_outs, (core, *x_own, *x_peer, cosine, sine, qkv_own), tiles, 1, vmem=32
    )
    history_grad, mixed, g_own, history_parts = average_history(dwa_weights, history, cotangent, (log_a,))
    g_peer = other_core(g_own)
    qkv_b, att_b, nat_b, log_b = call(
        attend_placed,
        first_outs,
        (core, *x_own, *x_peer, cosine, sine, qkv_peer),
        tiles,
        1,
        (history_parts,),
        32,
        MUCH,
    )
    third = (rows // PARTS, width)
    keep, *send, down_copy = call(
        branch_body,
        [(full, single)] + [(third, bfloat)] * PARTS + [(fourth, bfloat)],
        (core, nat_a, nat_b, out_weight, out_peer, down_come),
        (),
        1,
        (g_peer,),
    )
    down_pieces = [down_come] + [other_copy(down_copy, mask) for mask in masks]
    recv = [other_core(value) for value in send]
    middle, *y_own = call(
        middle_body, [(full, single)] + [(third, bfloat)] * PARTS, (inputs, keep, gain_mlp, *recv)
    )
    y_peer = [other_core(value) for value in y_own]

    first = mlp(y_own, y_peer, g_own, g_peer, (up_weight,), (down_weight,))
    down_mine, up_mine = first[4:]
    second = mlp(
        y_own, y_peer, g_own, g_peer, (up_peer,), down_pieces, (owner,), (*first[:4], up_mine)
    )
    send_norm, keep_norm, send_out, keep_out, down_theirs = second[:5]
    token = [send_norm]

    def step(body, outs, operands, scratch=(), scalars=0, vmem=16, flops=MUCH, far=0, far_outs=0):
        results = call(body, outs, operands, scratch, scalars, tuple(token), vmem, flops, far, far_outs)
        token[0] = results[0]
        return results

    down_come = other_chip(down_theirs)
    up_parts = [second[5]] + [other_copy(value, mask) for mask, value in zip(masks, second[6:])]
    out_come = other_core(send_out)
    grad_middle, gb_own, gain_mlp_part = step(
        middle_back_body,
        [(full, single), (full, bfloat), ((1, width), single)],
        (dwa_weights, middle, keep_norm, other_core(send_norm), cotangent, gain_mlp),
        scalars=1,
        flops=0,
    )
    gb_peer = other_core(gb_own)
    combined, dwa_part = step(
        combine_body,
        [(full, bfloat), ((depth + 1, width), single)],
        (dwa_weights, mixed, middle, keep_out, out_come, cotangent, history_parts),
        scalars=1,
        flops=0,
    )

    def back(weight, qkv_weight, qkv, att, log, flops, before=()):
        return step(
            attend_back,
            [
                ((depth + 3 if before else 1, width), single),
                ((4 * part, width), bfloat),
                ((3 * part, SEQ), bfloat),
            ],
            (
                core, log, cosine, sine, gain_attn, *before, gb_own, gb_peer, *x_own, *x_peer, weight, qkv_weight, qkv,
                att,
            ),
            [
                pltpu.VMEM(tall, bfloat),
                pltpu.VMEM(tall, bfloat),
                pltpu.VMEM((part, width), bfloat),
                pltpu.VMEM((3 * part, width), bfloat),
                pltpu.VMEM((3 * part, SEQ), bfloat),
                pltpu.VMEM((part, SEQ), bfloat),
                pltpu.VMEM((3 * part, SEQ), bfloat),
                pltpu.VMEM((4 * part, width), bfloat),
                pltpu.VMEM((heads, SEQ, SEQ), bfloat),
                pltpu.VMEM((heads, SEQ, SEQ), bfloat),
                pltpu.VMEM((3 * part, width), single),
                marks,
            ],
            1,
            60,
            flops,
            10,
            2,
        )

    gain_part, att_theirs, turned_b = back(out_peer, qkv_peer, qkv_b, att_b, log_b, 0)
    att_come = other_chip(att_theirs)
    def spread(mine, come, flops=MUCH):
        own, *sent = step(part_body, [(fourth, bfloat)] * SQUARE, (owner, mine, come), scalars=1, flops=flops)
        return [own] + [other_copy(value, mask) for mask, value in zip(masks, sent)]

    down_parts = spread(down_mine, down_come, 0)
    up, sent = step(four_two_body, [(fourth, bfloat)] * 2, up_parts, flops=0)
    up_come = other_chip(sent)
    part_sums, att_mine, turned_a = back(
        out_weight, qkv_own, qkv_a, att_a, log_a, MUCH, (gain_part, gain_mlp_part, dwa_part)
    )

    def exchange(value):
        for bit in range(2, bits):
            come = other_copy(value, 1 << bit)
            if bit < bits - 1:
                (value,) = step(low_body, [(value.shape, bfloat)], (value, come))
        return value, come

    def finish(value, come):
        (value,) = step(low_body, [(value.shape, bfloat)], (value, come), flops=COST)
        return [value] + [other_copy(value, mask) for mask in masks]

    (down,) = step(four_body, [(fourth, bfloat)], down_parts, flops=COST)
    down = exchange(down)
    att_parts = spread(att_mine, att_come, COST)
    (up,) = step(low_body, [(fourth, bfloat)], (up, up_come), flops=COST)
    up = exchange(up)
    send_first, keep_first = step(
        first_grad_body,
        [((rows + EXTRA, width), bfloat), (full, single)],
        (core, part_sums, turned_a, turned_b, qkv_own, qkv_peer),
        [pltpu.VMEM((3 * part, SEQ), bfloat)] * 2
        + [pltpu.VMEM((3 * part, width), bfloat)] * 2
        + [pltpu.VMEM(tall, single), marks],
        1,
        60,
        COST,
        4,
        1,
    )
    first_come = other_core(send_first)
    token.append(down[1])
    step(mark_body, [((8, 128), single)], (), flops=COST)
    del token[1:]
    (part_sums,) = step(small_body, [(part_sums.shape, single)], (part_sums, first_come), flops=COST)
    more_sums = other_chip(part_sums)
    (input_grad,) = step(
        first_back_body,
        [(full, bfloat)],
        (inputs, keep_first, first_come, grad_middle, gain_attn),
        vmem=60,
        flops=COST,
    )
    block = (width // SQUARE + EXTRA, width)
    pair = (2 * fourth[0], width)
    token.append(more_sums)
    (both,) = step(pair_body, [(pair, bfloat)], (*down, *up), flops=COST)
    token.pop()
    both = [both, other_copy(both, 1), other_copy(both, 2)]
    (att,) = step(four_more_body, [(block, bfloat)], (part_sums, more_sums, *att_parts), flops=COST)
    att = exchange(att)
    (both_copy,) = step(copy_body, [(pair, bfloat)], (both[2],), flops=COST)
    both.append(other_copy(both_copy, 1))
    att = finish(*att)
    down_grad, up_grad = step(
        pair_whole_body,
        [(square, single)] * 2,
        (owner, *both),
        [pltpu.VMEM((SQUARE * pair[0], width), bfloat)],
        1,
        flops=COST,
    )
    qkv_grad, out_grad, gain_attn_grad, gain_mlp_grad, dwa_grad = step(
        more_body,
        [
            ((3 * part, width), single),
            ((part, width), single),
            ((width,), single),
            ((width,), single),
            ((depth + 1,), single, "scalars"),
        ],
        (owner, *att),
        [pltpu.VMEM((SQUARE * block[0], width), bfloat)],
        1,
        flops=COST,
    )

    return (
        combined,
        input_grad,
        history_grad,
        qkv_grad.reshape(3, part, width).transpose(2, 0, 1),
        out_grad,
        up_grad,
        down_grad,
        gain_attn_grad,
        gain_mlp_grad,
        dwa_grad,
    )


def solution(mesh):
    placed = (
        P(("dp", "mp"), None),
        P(None, ("dp", "mp"), None),
        P(("dp", "mp"), None),
        P(None, None, "mp"),
        P("mp", None),
        P(None, "mp"),
        P("mp", None),
        P(),
        P(),
        P(),
    )
    return jax.shard_map(
        shards,
        mesh=mesh,
        in_specs=placed,
        out_specs=(
            P(("dp", "mp"), None),
            P(("dp", "mp"), None),
            P(None, ("dp", "mp"), None),
            P(None, None, "mp"),
            P("mp", None),
            P(None, "mp"),
            P("mp", None),
            P(),
            P(),
            P(),
        ),
        check_vma=False,
    )
```

```python
import functools

import jax
import jax.numpy as jnp
import numpy as np
from jax import lax
from jax.experimental import pallas as pl
from jax.experimental.pallas import tpu as pltpu
from jax.sharding import PartitionSpec as P

DH = 64
SEQ = 1152
HALF = SEQ // 2
EPS = 1e-05
bfloat = jnp.bfloat16
single = jnp.float32
MIB = 1 << 20
MUCH = 10**11
COST = 10**10


def tables():
    half_width = DH // 2
    places = np.arange(SEQ, dtype=np.float32)
    frequency = np.float32(10000.0) ** (-np.arange(half_width, dtype=np.float32) * np.float32(2.0 / DH))
    angles = frequency[:, None] * places[None, :]
    return (np.cos(angles).astype(np.float32), np.sin(angles).astype(np.float32))


def mul(a, b, ca=1, cb=0):
    return lax.dot_general(a, b, (((ca,), (cb,)), ((), ())), preferred_element_type=single)


def call(kernel, outs, operands, scratch=(), scalars=0, after=(), vmem=16, flops=0, far=0, far_outs=0):
    count, waits = len(operands), len(after)

    def body(*refs):
        kernel(*refs[:count], *refs[count + waits :])

    small = pl.BlockSpec(memory_space=pltpu.SMEM)
    whole = pl.BlockSpec(memory_space=pltpu.VMEM)
    apart = pl.BlockSpec(memory_space=pltpu.HBM)
    loose = pl.BlockSpec(memory_space=pl.ANY)
    inner = len(outs) - far_outs
    return pl.pallas_call(
        body,
        out_shape=[jax.ShapeDtypeStruct(out[0], out[1]) for out in outs],
        in_specs=[small] * scalars + [whole] * (count - scalars - far) + [apart] * far + [loose] * waits,
        out_specs=[small if len(out) > 2 else whole for out in outs[:inner]] + [apart] * far_outs,
        scratch_shapes=list(scratch),
        compiler_params=pltpu.CompilerParams(vmem_limit_bytes=vmem * MIB),
        cost_estimate=pl.CostEstimate(flops=flops, bytes_accessed=0, transcendentals=0),
    )(*operands, *after)


class Mover:
    def __init__(self, marks):
        self.marks = marks
        self.used = 0

    def __call__(self, *pairs):
        copies = []
        for source, target in pairs:
            copies.append(pltpu.make_async_copy(source, target, self.marks.at[self.used]))
            self.used += 1
        for copy in copies:
            copy.start()
        return copies


def wait(copies):
    for copy in copies:
        copy.wait()


ROWS = 64
PARTS = 3


def spans(rows, step=ROWS):
    return [slice(begin, begin + step) for begin in range(0, rows, step)]


def normal_of(x):
    centre = x - jnp.mean(x, axis=-1, keepdims=True)
    spread = jnp.mean(centre * centre, axis=-1, keepdims=True)
    scale = lax.rsqrt(spread + EPS)
    return centre * scale, scale


def split_body(owner_ref, in_ref, out_ref, hold, marks):
    go = Mover(marks)
    wait(go((in_ref.at[quarter(owner_ref[0], 0, hold.shape[0]), :], hold)))
    wait(go((hold, out_ref)))


def joined(owner, refs, target):
    size = refs[0].shape[0]
    return [(ref, target.at[quarter(owner, mask, size), :]) for mask, ref in enumerate(refs)]


def norm_body(x_ref, gain_ref, *out_refs):
    gain = gain_ref[...].reshape(1, -1)
    for index, out_ref in enumerate(out_refs):
        rows = out_ref.shape[0]
        for span in spans(rows, rows // 6):
            here = slice(index * rows + span.start, index * rows + span.stop)
            normal, _ = normal_of(x_ref[here, :].astype(single))
            out_ref[span, :] = (normal * gain).astype(bfloat)


def middle_body(x_ref, keep_ref, gain_ref, *rest):
    recv_refs, mid_ref, out_refs = rest[:PARTS], rest[PARTS], rest[PARTS + 1 :]
    gain = gain_ref[...].reshape(1, -1)
    rows = x_ref.shape[0] // PARTS
    for index in range(PARTS):
        for span in spans(rows):
            here = slice(index * rows + span.start, index * rows + span.stop)
            recv = recv_refs[index][span, :].astype(single)
            x = x_ref[here, :].astype(single) + (keep_ref[here, :] + recv)
            mid_ref[here, :] = x
            normal, _ = normal_of(x)
            out_refs[index][span, :] = (normal * gain).astype(bfloat)


def norm_back(x, grad, gain):
    normal, scale = normal_of(x)
    lifted = grad * gain
    back = scale * (
        lifted
        - jnp.mean(lifted, axis=-1, keepdims=True)
        - normal * jnp.mean(lifted * normal, axis=-1, keepdims=True)
    )
    return back, normal


def fold_rows(value):
    total = value[:8]
    for begin in range(8, value.shape[0], 8):
        total = total + value[begin : begin + 8]
    return total


def middle_back_body(mix_ref, x_ref, keep_ref, recv_ref, cot_ref, gain_ref, mid_ref, low_ref, part_ref):
    gain = gain_ref[...].reshape(1, -1)
    part = jnp.zeros((8, x_ref.shape[1]), single)
    for span in spans(x_ref.shape[0]):
        grad = keep_ref[span, :] + recv_ref[span, :].astype(single)
        back, normal = norm_back(x_ref[span, :], grad, gain)
        total = mix_ref[mix_ref.shape[0] - 1] * cot_ref[span, :] + back
        mid_ref[span, :] = total
        low_ref[span, :] = total.astype(bfloat)
        part = part + fold_rows(grad * normal)
    part_ref[...] = jnp.sum(part, axis=0, keepdims=True)


def first_back_body(x_ref, keep_ref, recv_ref, mid_ref, gain_ref, out_ref):
    gain = gain_ref[...].reshape(1, -1)
    for span in spans(x_ref.shape[0]):
        grad = keep_ref[span, :] + recv_ref[span, :].astype(single)
        back, _ = norm_back(x_ref[span, :].astype(single), grad, gain)
        out_ref[span, :] = (mid_ref[span, :] + back).astype(bfloat)


def history_body(mix_ref, history_ref, cot_ref, grad_ref, mixed_ref, low_ref, part_ref):
    depth = history_ref.shape[0]

    @pl.when(pl.program_id(0) == 0)
    def _():
        part_ref[...] = jnp.zeros_like(part_ref)

    for span in spans(cot_ref.shape[0], 32):
        cot = cot_ref[span, :]
        low_ref[span, :] = (mix_ref[depth] * cot).astype(bfloat)
        mixed = None
        for j in range(depth):
            layer = history_ref[j, span, :].astype(single)
            mixed = mix_ref[j] * layer if mixed is None else mixed + mix_ref[j] * layer
            grad_ref[j, span, :] = (mix_ref[j] * cot).astype(bfloat)
            part_ref[8 * j : 8 * j + 8, :] += fold_rows(layer * cot)
        mixed_ref[span, :] = mixed


def average_history(mix, history, cot, after=()):
    depth, rows, width = history.shape
    step = 96
    waits = len(after)

    def body(*refs):
        history_body(*refs[:3], *refs[3 + waits :])

    row_block = pl.BlockSpec((step, width), lambda i: (i, 0))
    deep_block = pl.BlockSpec((depth, step, width), lambda i: (0, i, 0))
    return pl.pallas_call(
        body,
        grid=(rows // step,),
        out_shape=[
            jax.ShapeDtypeStruct(history.shape, bfloat),
            jax.ShapeDtypeStruct((rows, width), single),
            jax.ShapeDtypeStruct((rows, width), bfloat),
            jax.ShapeDtypeStruct((8 * depth, width), single),
        ],
        in_specs=[pl.BlockSpec(memory_space=pltpu.SMEM), deep_block, row_block]
        + [pl.BlockSpec(memory_space=pl.ANY)] * waits,
        out_specs=[deep_block, row_block, row_block, pl.BlockSpec((8 * depth, width), lambda i: (0, 0))],
        compiler_params=pltpu.CompilerParams(vmem_limit_bytes=16 * MIB),
        cost_estimate=pl.CostEstimate(flops=0, bytes_accessed=0, transcendentals=0),
    )(mix, history, cot, *after)


def combine_body(mix_ref, mixed_ref, mid_ref, keep_ref, recv_ref, cot_ref, parts_ref, out_ref, part_ref):
    depth = mix_ref.shape[0] - 1
    last = jnp.zeros((8, mid_ref.shape[1]), single)
    for span in spans(mid_ref.shape[0]):
        outputs = mid_ref[span, :] + (keep_ref[span, :] + recv_ref[span, :].astype(single))
        out_ref[span, :] = (mixed_ref[span, :] + mix_ref[depth] * outputs).astype(bfloat)
        last = last + fold_rows(outputs * cot_ref[span, :])
    for j in range(depth):
        part_ref[j : j + 1, :] = jnp.sum(parts_ref[8 * j : 8 * j + 8, :], axis=0, keepdims=True)
    part_ref[depth : depth + 1, :] = jnp.sum(last, axis=0, keepdims=True)


SQUARE = 4


def quarter(owner, mask, size):
    other = owner + (mask & 1) * (1 - 2 * (owner % 2)) + (mask & 2) * (1 - 2 * (owner // 2))
    return pl.ds(pl.multiple_of(other * size, size), size)


def part_body(owner_ref, mine_ref, come_ref, *out_refs):
    for mask, out_ref in enumerate(out_refs):
        rows = quarter(owner_ref[0], mask, out_ref.shape[0])
        out_ref[...] = (mine_ref[rows, :].astype(single) + come_ref[rows, :].astype(single)).astype(bfloat)


def sum_of(refs, rows):
    total = refs[0][rows, :].astype(single)
    for ref in refs[1:]:
        total = total + ref[rows, :].astype(single)
    return total


def four_body(*refs):
    refs[-1][...] = sum_of(refs[:-1], slice(None)).astype(bfloat)


def four_two_body(*refs):
    size = refs[-1].shape[0]
    refs[-2][...] = sum_of(refs[:-2], slice(0, size)).astype(bfloat)
    refs[-1][...] = sum_of(refs[:-2], slice(size, 2 * size)).astype(bfloat)


EXTRA = 16


def mark_body(out_ref):
    out_ref[...] = jnp.zeros_like(out_ref)


def small_body(small_ref, first_ref, out_ref):
    half = small_ref.shape[0]
    rows = first_ref.shape[0] - 2 * half
    come = first_ref[rows:, :].astype(single)
    out_ref[...] = small_ref[...] + (come[:half] + come[half:])


def four_more_body(small_ref, more_ref, *refs):
    out_ref = refs[-1]
    size = out_ref.shape[0] - EXTRA
    out_ref[:size, :] = sum_of(refs[:-1], slice(None)).astype(bfloat)
    small = small_ref[...] + more_ref[...]
    rest = jnp.zeros((EXTRA - small.shape[0], small.shape[1]), single)
    out_ref[size:, :] = jnp.concatenate([small, rest], axis=0).astype(bfloat)


def gather(owner_ref, pieces, hold):
    for mask, piece in enumerate(pieces):
        hold[quarter(owner_ref[0], mask, piece.shape[0]), :] = piece[...]


def pair_body(a_ref, a_come_ref, b_ref, b_come_ref, out_ref):
    size = a_ref.shape[0]
    out_ref[:size, :] = sum_of((a_ref, a_come_ref), slice(None)).astype(bfloat)
    out_ref[size:, :] = sum_of((b_ref, b_come_ref), slice(None)).astype(bfloat)


def whole_body(owner_ref, a_ref, b_ref, c_ref, d_ref, out_ref, hold):
    gather(owner_ref, (a_ref, b_ref, c_ref, d_ref), hold)
    out_ref[...] = hold[...].astype(single)


def more_body(owner_ref, a_ref, b_ref, c_ref, d_ref, top_ref, end_ref, up_ref, attn_ref, mlp_ref, dwa_ref, hold):
    gather(owner_ref, (a_ref, b_ref, c_ref, d_ref), hold)
    block = hold.shape[0] // SQUARE
    rows = up_ref.shape[0] // SQUARE
    small = jnp.zeros((EXTRA, hold.shape[1]), single)
    for index in range(SQUARE):
        begin = index * block
        target, place = (top_ref, index * rows) if index < SQUARE - 1 else (end_ref, 0)
        target[place : place + rows, :] = hold[begin : begin + rows, :].astype(single)
        small = small + hold[begin + rows : begin + rows + EXTRA, :].astype(single)
        up_ref[index * rows : (index + 1) * rows, :] = hold[begin + rows + EXTRA : begin + block, :].astype(single)
    attn_ref[...] = small[0]
    mlp_ref[...] = small[1]
    for index in range(dwa_ref.shape[0]):
        dwa_ref[index] = jnp.sum(small[2 + index : 3 + index])


def low_body(mine_ref, come_ref, out_ref):
    out_ref[...] = (mine_ref[...].astype(single) + come_ref[...].astype(single)).astype(bfloat)


def mark_body(out_ref):
    out_ref[...] = jnp.zeros_like(out_ref)


def small_body(small_ref, first_ref, out_ref):
    half = small_ref.shape[0]
    rows = first_ref.shape[0] - 2 * half
    come = first_ref[rows:, :].astype(single)
    out_ref[...] = small_ref[...] + (come[:half] + come[half:])


BLOCKS = tuple((begin, min(256, SEQ - begin)) for begin in range(0, SEQ, 256))


def places(core_ref, refs):
    count, size = len(refs) // 2, refs[0].shape[0]
    for index, ref in enumerate(refs):
        core = core_ref[0] if index < count else 1 - core_ref[0]
        yield ref, pl.ds(pl.multiple_of(core * HALF + index % count * size, size), size)


def allowed(size):
    key_pos = lax.broadcasted_iota(jnp.int32, (size, size), 0)
    query_pos = lax.broadcasted_iota(jnp.int32, (size, size), 1)
    return query_pos >= key_pos


def turn(rows, cosine, sine):
    half = rows.shape[0] // 2
    a, b = rows[:half], rows[half:]
    return jnp.concatenate([a * cosine - b * sine, b * cosine + a * sine], axis=0)


KEYS = 128


def fold_top(value):
    top = value[:8]
    for begin in range(8, value.shape[0], 8):
        top = jnp.maximum(top, value[begin : begin + 8])
    return top


def masked(scores, offset):
    key_pos = lax.broadcasted_iota(jnp.int32, scores.shape, 0) + offset
    query_pos = lax.broadcasted_iota(jnp.int32, scores.shape, 1)
    return jnp.where(query_pos >= key_pos, scores, -jnp.inf)


def attend_placed(core_ref, *rest):
    for ref, where in places(core_ref, rest[:4]):
        rest[11][where, :] = ref[...]
    cos_ref, sin_ref, weight_ref, rest = rest[4], rest[5], rest[6], rest[7:]
    attend(weight_ref, cos_ref, sin_ref, *rest)


def attend(weight_ref, cos_ref, sin_ref, qkv_ref, att_ref, nat_ref, log_ref, tokens, all_scores, all_weights):
    width = weight_ref.shape[0] // 3
    projected = mul(weight_ref[...], tokens[...], 1, 1)
    cosine, sine = cos_ref[...], sin_ref[...]
    for part in range(3):
        for head in range(width // DH):
            begin = part * width + head * DH
            rows = projected[begin : begin + DH]
            if part < 2:
                rows = turn(rows, cosine, sine)
            if part == 0:
                rows = rows * DH ** (-0.5)
            qkv_ref[begin : begin + DH, :] = rows.astype(bfloat)
    log_ref[...] = jnp.zeros_like(log_ref)
    heads = range(width // DH)
    keys = [qkv_ref[width + head * DH : width + head * DH + DH, :].T for head in heads]
    for begin, size in BLOCKS:
        end = begin + size
        tops = [None for _ in heads]
        for row in range(0, end, KEYS):
            for head in heads:
                tile = mul(keys[head][row : row + KEYS], qkv_ref[head * DH : head * DH + DH, begin:end])
                if row >= begin:
                    tile = masked(tile, row - begin)
                all_scores[head, row : row + KEYS, :size] = tile
                top = fold_top(tile)
                tops[head] = top if row == 0 else jnp.maximum(tops[head], top)
        tops = [jnp.max(top, axis=0, keepdims=True) for top in tops]
        totals = [jnp.zeros((8, size), single) for _ in heads]
        for row in range(0, end, KEYS):
            for head in heads:
                tile = jnp.exp(all_scores[head, row : row + KEYS, :size] - tops[head])
                totals[head] = totals[head] + fold_rows(tile)
                all_weights[head, row : row + KEYS, :size] = tile.astype(bfloat)
        for head in heads:
            base = head * DH
            total = jnp.sum(totals[head], axis=0, keepdims=True)
            value = qkv_ref[2 * width + base : 2 * width + base + DH, :end]
            mixed = mul(value, all_weights[head, :end, :size]) / total
            att_ref[base : base + DH, begin:end] = mixed.astype(bfloat)
            log_ref[head : head + 1, begin:end] = tops[head] + jnp.log(total)
    nat_ref[...] = att_ref[...].T


def branch_body(core_ref, att_a_ref, att_b_ref, out_a_ref, out_b_ref, pass_ref, keep_ref, *rest):
    send_refs, pass_out = rest[:PARTS], rest[PARTS]
    pass_out[...] = pass_ref[...]
    low = pl.multiple_of(core_ref[0] * HALF, HALF)
    rows = HALF // PARTS
    for index in range(PARTS):
        high = pl.multiple_of((1 - core_ref[0]) * HALF + index * rows, rows)
        send = mul(att_a_ref[pl.ds(high, rows), :], out_a_ref[...])
        send_refs[index][...] = (send + mul(att_b_ref[pl.ds(high, rows), :], out_b_ref[...])).astype(bfloat)
    keep = mul(att_a_ref[pl.ds(low, HALF), :], out_a_ref[...])
    keep_ref[...] = keep + mul(att_b_ref[pl.ds(low, HALF), :], out_b_ref[...])


def attend_back(
    core_ref, log_ref, cos_ref, sin_ref, gain_ref, *rest
):
    before_refs, rest = rest[:-25], rest[-25:]
    grad_refs, x_refs = rest[:2], rest[2:6]
    weight_ref, qkv_weight_ref, qkv_ref, att_ref, small_ref, out_ref, turned_ref = rest[6:13]
    grads, tokens, weight, qkv_weight, qkv, att, turned, result, all_probs, all_scores, hold, marks = rest[13:]
    go = Mover(marks)
    first = go(
        (weight_ref, weight),
        *[(ref, grads.at[where, :]) for ref, where in places(core_ref, grad_refs)],
        (att_ref, att),
        (qkv_ref, qkv),
    )
    later = go(
        *[(ref, tokens.at[where, :]) for ref, where in places(core_ref, x_refs)],
        (qkv_weight_ref, qkv_weight),
    )
    wait(first)
    width = att.shape[0]
    grad_att = mul(weight[...], grads[...], 1, 1).astype(bfloat)
    result[3 * width :, :] = mul(att[...], grads[...]).astype(result.dtype)
    cosine, sine = cos_ref[...], sin_ref[...]
    heads = range(width // DH)
    spans_of = [slice(head * DH, head * DH + DH) for head in heads]
    query = [qkv[span, :] for span in spans_of]
    key = [qkv[width + span.start : width + span.stop, :] for span in spans_of]
    above = [grad_att[span] for span in spans_of]
    centre = [
        jnp.sum(above[head].astype(single) * att[span, :].astype(single), axis=0, keepdims=True)
        for head, span in enumerate(spans_of)
    ]
    keys = [value.T for value in key]
    values = [qkv[2 * width + span.start : 2 * width + span.stop, :].T for span in spans_of]
    queries = [value.T for value in query]
    aboves = [value.T for value in above]
    grad_query = [[] for _ in heads]
    for begin, size in BLOCKS:
        end = begin + size
        for row in range(0, end, KEYS):
            span = slice(row, row + KEYS)
            for head in heads:
                tile = mul(keys[head][span], query[head][:, begin:end])
                if row >= begin:
                    tile = masked(tile, row - begin)
                tile = jnp.exp(tile - log_ref[head : head + 1, begin:end])
                grad = mul(values[head][span], above[head][:, begin:end]) - centre[head][:, begin:end]
                all_probs[head, span, begin:end] = tile.astype(bfloat)
                all_scores[head, span, begin:end] = (tile * grad).astype(bfloat)
        for head in heads:
            grad_query[head].append(mul(key[head][:, :end], all_scores[head, :end, begin:end]))
    grad_key = [[] for _ in heads]
    grad_value = [[] for _ in heads]
    for begin, size in BLOCKS:
        span = slice(begin, begin + size)
        for head in heads:
            grad_key[head].append(mul(all_scores[head, span, begin:], queries[head][begin:]))
            grad_value[head].append(mul(all_probs[head, span, begin:], aboves[head][begin:]))
    for head, span in enumerate(spans_of):
        grad = jnp.concatenate(grad_query[head], axis=1) * DH ** (-0.5)
        turned[span, :] = turn(grad, cosine, -sine).astype(bfloat)
        grad = jnp.concatenate(grad_key[head], axis=0).T
        turned[width + span.start : width + span.stop, :] = turn(grad, cosine, -sine).astype(bfloat)
        grad = jnp.concatenate(grad_value[head], axis=0).T
        turned[2 * width + span.start : 2 * width + span.stop, :] = grad.astype(bfloat)
    stores = go((turned, turned_ref))
    wait(later)
    hold[...] = mul(turned[...], tokens[...])
    result[: 3 * width, :] = hold[...].astype(result.dtype)
    stores += go((result, out_ref))
    part = jnp.zeros((8, hold.shape[1]), single)
    for span in spans(hold.shape[0]):
        part = part + fold_rows(hold[span, :] * qkv_weight[span, :].astype(single))
    gain = jnp.sum(part, axis=0, keepdims=True) / gain_ref[...].reshape(1, -1)
    if before_refs:
        gain_part_ref, mlp_part_ref, dwa_part_ref = before_refs
        small_ref[:1, :] = gain + gain_part_ref[...]
        small_ref[1:2, :] = mlp_part_ref[...]
        small_ref[2:, :] = dwa_part_ref[...]
    else:
        small_ref[...] = gain
    wait(stores)


def first_grad_body(
    core_ref, small_ref, turned_a_ref, turned_b_ref, weight_a_ref, weight_b_ref, send_ref, keep_ref,
    turned_a, turned_b, weight_a, weight_b, whole, marks,
):
    low = pl.multiple_of(core_ref[0] * HALF, HALF)
    high = pl.multiple_of((1 - core_ref[0]) * HALF, HALF)
    go = Mover(marks)
    wait(go((turned_a_ref, turned_a), (weight_a_ref, weight_a), (turned_b_ref, turned_b), (weight_b_ref, weight_b)))
    whole[...] = mul(turned_a[...], weight_a[...], 0, 0) + mul(turned_b[...], weight_b[...], 0, 0)
    stores = go((whole.at[pl.ds(low, HALF), :], keep_ref))
    send_ref[:HALF, :] = whole[pl.ds(high, HALF), :].astype(bfloat)
    small = small_ref[...]
    high_part = small.astype(bfloat)
    low_part = (small - high_part.astype(single)).astype(bfloat)
    send_ref[HALF:, :] = jnp.concatenate([high_part, low_part], axis=0)
    wait(stores)


CURVE = float(np.sqrt(2.0 / np.pi))
STEP = 256


def mlp_body(second, *refs):
    if second:
        owner_ref, refs = refs[0], refs[1:]
    x_refs, refs = refs[: 2 * PARTS], refs[2 * PARTS :]
    g_own_ref, g_peer_ref, refs = refs[0], refs[1], refs[2:]
    if second:
        up_ref, down_refs, refs = refs[0], refs[1 : 1 + SQUARE], refs[1 + SQUARE :]
        before_refs, up_mine_ref = refs[:4], refs[4]
        down_grad_ref, part_refs = refs[9], refs[10:14]
        refs = refs[5:9] + refs[14:]
    else:
        up_ref, down_ref = refs[:2]
        down_grad_ref, up_grad_ref = refs[6:8]
        refs = refs[2:6] + refs[8:]
    send_norm_ref, keep_norm_ref, send_out_ref, keep_out_ref = refs[:4]
    x_all, g_all, up, down, active, grad_hidden, x_turned = refs[4:11]
    send_norm, keep_norm, send_out, keep_out, down_grad, up_grad, marks = refs[11:18]
    rows, size = x_all.shape[0] // 2, x_all.shape[0] // (2 * PARTS)
    units = down.shape[0]
    go = Mover(marks)
    x_loads = go(*[(x_refs[index], x_all.at[pl.ds(index * size, size), :]) for index in range(2 * PARTS)])
    if second:
        loads = go((up_ref, up), *joined(owner_ref[0], down_refs, down))
    else:
        loads = go((up_ref, up), (down_ref, down))
    loads += go((g_own_ref, g_all.at[pl.ds(0, rows), :]), (g_peer_ref, g_all.at[pl.ds(rows, rows), :]))
    more, mine, stores = [], [], []
    if second:
        (up_mine,) = refs[18:]
        more = go(*zip(before_refs, (send_norm, keep_norm, send_out, keep_out)))
        mine = go((up_mine_ref, up_mine))
    wait(x_loads)
    x_turned[...] = x_all[...].T
    wait(loads)
    for begin in range(0, units, STEP):
        columns = slice(begin, begin + STEP)
        for top in range(0, 2 * rows, rows):
            span = slice(top, top + rows)
            v = mul(x_all[span, :], up[:, columns])
            grad = mul(g_all[span, :], down[columns, :], 1, 1)
            square = v * v
            half = 0.5 + 0.5 * jnp.tanh(v * (CURVE + (CURVE * 0.044715) * square))
            act = v * half
            slope = half + act * (1.0 - half) * (2.0 * CURVE + (6.0 * CURVE * 0.044715) * square)
            active[span, columns] = act.astype(bfloat)
            grad_hidden[span, columns] = (grad * slope).astype(bfloat)

    def put(target, value):
        target[...] = (value + target[...].astype(single) if second else value).astype(target.dtype)

    wait(more)
    put(keep_norm, mul(grad_hidden[:rows, :], up[...], 1, 1))
    put(send_norm, mul(grad_hidden[rows:, :], up[...], 1, 1))
    stores += go((keep_norm, keep_norm_ref), (send_norm, send_norm_ref))
    down_grad[...] = mul(active[...], g_all[...], 0, 0).astype(down_grad.dtype)
    stores += go((down_grad, down_grad_ref))
    up_grad[...] = mul(x_turned[...], grad_hidden[...]).astype(bfloat)
    if second:
        wait(mine)
        part = up_grad.shape[0] // SQUARE
        for mask, part_ref in enumerate(part_refs):
            rows_of = quarter(owner_ref[0], mask, part)
            stores += go(
                (up_mine.at[rows_of, :], part_ref.at[pl.ds(0, part), :]),
                (up_grad.at[rows_of, :], part_ref.at[pl.ds(part, part), :]),
            )
    else:
        stores += go((up_grad, up_grad_ref))
    put(keep_out, mul(active[:rows, :], down[...]))
    stores += go((keep_out, keep_out_ref))
    put(send_out, mul(active[rows:, :], down[...]))
    wait(stores + go((send_out, send_out_ref)))


def mlp(x_own, x_peer, g_own, g_peer, up, down, upper=(), before=(), flops=0):
    rows, width = g_own.shape
    units = sum(piece.shape[0] for piece in down)
    tall = (2 * rows, width)
    pair = [((rows, width), bfloat), ((rows, width), single)] * 2
    outs = pair + [((units, width), bfloat)]
    outs += [((2 * width // SQUARE, units), bfloat)] * SQUARE if before else [((width, units), bfloat)]
    scratch = [
        pltpu.VMEM(tall, bfloat),
        pltpu.VMEM(tall, bfloat),
        pltpu.VMEM((width, units), bfloat),
        pltpu.VMEM((units, width), bfloat),
        pltpu.VMEM((2 * rows, units), bfloat),
        pltpu.VMEM((2 * rows, units), bfloat),
        pltpu.VMEM((width, 2 * rows), bfloat),
    ]
    scratch += [pltpu.VMEM(shape, kind) for shape, kind in pair]
    scratch += [
        pltpu.VMEM((units, width), bfloat), pltpu.VMEM((width, units), bfloat), pltpu.SemaphoreType.DMA((32,)),
    ]
    if before:
        scratch.append(pltpu.VMEM((width, units), bfloat))
    operands = (*upper, *x_own, *x_peer, g_own, g_peer, *up, *down, *before)
    return call(
        functools.partial(mlp_body, bool(before)),
        outs,
        operands,
        scratch,
        len(upper),
        vmem=60,
        flops=flops,
        far=len(operands) - len(upper),
        far_outs=len(outs),
    )


def shards(
    inputs,
    history,
    cotangent,
    qkv_weight,
    out_weight,
    up_weight,
    down_weight,
    gain_attn,
    gain_mlp,
    dwa_weights,
):
    rows, width = inputs.shape
    members = lax.axis_size("mp")
    copies = lax.axis_size("dp")
    bits = copies.bit_length() - 1
    core = lax.rem(lax.axis_index("mp"), 2).astype(jnp.int32).reshape(1)
    copy_index = lax.axis_index("dp").astype(jnp.int32).reshape(1)
    core_pairs = [(i, i ^ 1) for i in range(members)]
    chip_pairs = [(i, i ^ 2) for i in range(members)]
    depth = history.shape[0]
    part = out_weight.shape[0]

    def other_core(value):
        return lax.ppermute(value, "mp", core_pairs)

    def other_chip(value):
        return lax.ppermute(value, "mp", chip_pairs)

    def other_copy(value, mask):
        return lax.ppermute(value, "dp", [(i, i ^ mask) for i in range(copies)])

    owner = copy_index & (SQUARE - 1)
    cosine, sine = (jnp.asarray(table) for table in tables())

    qkv_own = qkv_weight.transpose(1, 2, 0).reshape(3 * part, width)
    fourth = (width // SQUARE, width)
    square = (width, width)
    masks = range(1, SQUARE)
    marks = pltpu.SemaphoreType.DMA((16,))
    (down_quarter,) = call(
        split_body,
        [(fourth, bfloat)],
        (owner, down_weight),
        [pltpu.VMEM(fourth, bfloat), marks],
        1,
        vmem=60,
        far=1,
        far_outs=1,
    )
    qkv_peer, out_peer = other_chip(qkv_own), other_chip(out_weight)
    down_come, up_peer = other_chip(down_quarter), other_chip(up_weight)

    full = (rows, width)
    x_own = call(norm_body, [((rows // 2, width), bfloat)] * 2, (inputs, gain_attn), after=(down_quarter,))
    x_peer = [other_core(value) for value in x_own]
    tall = (SEQ, width)
    tokens = pltpu.VMEM(tall, bfloat)
    first_outs = [
        ((3 * part, SEQ), bfloat), ((part, SEQ), bfloat), ((SEQ, part), bfloat), ((8, SEQ), single),
    ]
    heads = part // DH
    tiles = [tokens, pltpu.VMEM((heads, SEQ, 256), single), pltpu.VMEM((heads, SEQ, 256), bfloat)]
    qkv_a, att_a, nat_a, log_a = call(
        attend_placed, first_outs, (core, *x_own, *x_peer, cosine, sine, qkv_own), tiles, 1, vmem=32
    )
    history_grad, mixed, g_own, history_parts = average_history(dwa_weights, history, cotangent, (log_a,))
    g_peer = other_core(g_own)
    qkv_b, att_b, nat_b, log_b = call(
        attend_placed,
        first_outs,
        (core, *x_own, *x_peer, cosine, sine, qkv_peer),
        tiles,
        1,
        (history_parts,),
        32,
        MUCH,
    )
    third = (rows // PARTS, width)
    keep, *send, down_copy = call(
        branch_body,
        [(full, single)] + [(third, bfloat)] * PARTS + [(fourth, bfloat)],
        (core, nat_a, nat_b, out_weight, out_peer, down_come),
        (),
        1,
        (g_peer,),
    )
    down_pieces = [down_come] + [other_copy(down_copy, mask) for mask in masks]
    recv = [other_core(value) for value in send]
    middle, *y_own = call(
        middle_body, [(full, single)] + [(third, bfloat)] * PARTS, (inputs, keep, gain_mlp, *recv)
    )
    y_peer = [other_core(value) for value in y_own]

    first = mlp(y_own, y_peer, g_own, g_peer, (up_weight,), (down_weight,))
    down_mine, up_mine = first[4:]
    second = mlp(
        y_own, y_peer, g_own, g_peer, (up_peer,), down_pieces, (owner,), (*first[:4], up_mine)
    )
    send_norm, keep_norm, send_out, keep_out, down_theirs = second[:5]
    token = [send_norm]

    def step(body, outs, operands, scratch=(), scalars=0, vmem=16, flops=MUCH, far=0, far_outs=0):
        results = call(body, outs, operands, scratch, scalars, tuple(token), vmem, flops, far, far_outs)
        token[0] = results[0]
        return results

    down_come = other_chip(down_theirs)
    up_parts = [second[5]] + [other_copy(value, mask) for mask, value in zip(masks, second[6:])]
    out_come = other_core(send_out)
    grad_middle, gb_own, gain_mlp_part = step(
        middle_back_body,
        [(full, single), (full, bfloat), ((1, width), single)],
        (dwa_weights, middle, keep_norm, other_core(send_norm), cotangent, gain_mlp),
        scalars=1,
        flops=0,
    )
    gb_peer = other_core(gb_own)
    combined, dwa_part = step(
        combine_body,
        [(full, bfloat), ((depth + 1, width), single)],
        (dwa_weights, mixed, middle, keep_out, out_come, cotangent, history_parts),
        scalars=1,
        flops=0,
    )

    def back(weight, qkv_weight, qkv, att, log, flops, before=()):
        return step(
            attend_back,
            [
                ((depth + 3 if before else 1, width), single),
                ((4 * part, width), bfloat),
                ((3 * part, SEQ), bfloat),
            ],
            (
                core, log, cosine, sine, gain_attn, *before, gb_own, gb_peer, *x_own, *x_peer, weight, qkv_weight, qkv,
                att,
            ),
            [
                pltpu.VMEM(tall, bfloat),
                pltpu.VMEM(tall, bfloat),
                pltpu.VMEM((part, width), bfloat),
                pltpu.VMEM((3 * part, width), bfloat),
                pltpu.VMEM((3 * part, SEQ), bfloat),
                pltpu.VMEM((part, SEQ), bfloat),
                pltpu.VMEM((3 * part, SEQ), bfloat),
                pltpu.VMEM((4 * part, width), bfloat),
                pltpu.VMEM((heads, SEQ, SEQ), bfloat),
                pltpu.VMEM((heads, SEQ, SEQ), bfloat),
                pltpu.VMEM((3 * part, width), single),
                marks,
            ],
            1,
            60,
            flops,
            10,
            2,
        )

    gain_part, att_theirs, turned_b = back(out_peer, qkv_peer, qkv_b, att_b, log_b, 0)
    att_come = other_chip(att_theirs)
    def spread(mine, come, flops=MUCH):
        own, *sent = step(part_body, [(fourth, bfloat)] * SQUARE, (owner, mine, come), scalars=1, flops=flops)
        return [own] + [other_copy(value, mask) for mask, value in zip(masks, sent)]

    down_parts = spread(down_mine, down_come, 0)
    up, sent = step(four_two_body, [(fourth, bfloat)] * 2, up_parts, flops=0)
    up_come = other_chip(sent)
    part_sums, att_mine, turned_a = back(
        out_weight, qkv_own, qkv_a, att_a, log_a, MUCH, (gain_part, gain_mlp_part, dwa_part)
    )

    def exchange(value):
        for bit in range(2, bits):
            come = other_copy(value, 1 << bit)
            if bit < bits - 1:
                (value,) = step(low_body, [(value.shape, bfloat)], (value, come))
        return value, come

    def finish(value, come):
        (value,) = step(low_body, [(value.shape, bfloat)], (value, come), flops=COST)
        return [value] + [other_copy(value, mask) for mask in masks]

    (down,) = step(four_body, [(fourth, bfloat)], down_parts, flops=COST)
    down = exchange(down)
    att_parts = spread(att_mine, att_come, COST)
    (up,) = step(low_body, [(fourth, bfloat)], (up, up_come), flops=COST)
    up = exchange(up)
    send_first, keep_first = step(
        first_grad_body,
        [((rows + EXTRA, width), bfloat), (full, single)],
        (core, part_sums, turned_a, turned_b, qkv_own, qkv_peer),
        [pltpu.VMEM((3 * part, SEQ), bfloat)] * 2
        + [pltpu.VMEM((3 * part, width), bfloat)] * 2
        + [pltpu.VMEM(tall, single), marks],
        1,
        60,
        COST,
        4,
        1,
    )
    first_come = other_core(send_first)
    token.append(down[1])
    step(mark_body, [((8, 128), single)], (), flops=COST)
    del token[1:]
    (part_sums,) = step(small_body, [(part_sums.shape, single)], (part_sums, first_come), flops=COST)
    more_sums = other_chip(part_sums)
    (input_grad,) = step(
        first_back_body,
        [(full, bfloat)],
        (inputs, keep_first, first_come, grad_middle, gain_attn),
        vmem=60,
        flops=COST,
    )
    block = (width // SQUARE + EXTRA, width)
    (att,) = step(four_more_body, [(block, bfloat)], (part_sums, more_sums, *att_parts), flops=COST)
    att = exchange(att)
    down = finish(*down)
    token += down[1:]
    pair = (block[0] + fourth[0], width)
    (both,) = step(pair_body, [(pair, bfloat)], (*att, *up), flops=COST)
    del token[1:]
    both = [both] + [other_copy(both, mask) for mask in masks]
    (down_grad,) = step(
        whole_body, [(square, single)], (owner, *down), [pltpu.VMEM(square, bfloat)], 1, flops=COST
    )
    qkv_grad, out_grad, up_grad, gain_attn_grad, gain_mlp_grad, dwa_grad = step(
        more_body,
        [
            ((3 * part, width), single),
            ((part, width), single),
            (square, single),
            ((width,), single),
            ((width,), single),
            ((depth + 1,), single, "scalars"),
        ],
        (owner, *both),
        [pltpu.VMEM((SQUARE * pair[0], width), bfloat)],
        1,
        flops=COST,
    )

    return (
        combined,
        input_grad,
        history_grad,
        qkv_grad.reshape(3, part, width).transpose(2, 0, 1),
        out_grad,
        up_grad,
        down_grad,
        gain_attn_grad,
        gain_mlp_grad,
        dwa_grad,
    )


def solution(mesh):
    placed = (
        P(("dp", "mp"), None),
        P(None, ("dp", "mp"), None),
        P(("dp", "mp"), None),
        P(None, None, "mp"),
        P("mp", None),
        P(None, "mp"),
        P("mp", None),
        P(),
        P(),
        P(),
    )
    return jax.shard_map(
        shards,
        mesh=mesh,
        in_specs=placed,
        out_specs=(
            P(("dp", "mp"), None),
            P(("dp", "mp"), None),
            P(None, ("dp", "mp"), None),
            P(None, None, "mp"),
            P("mp", None),
            P(None, "mp"),
            P("mp", None),
            P(),
            P(),
            P(),
        ),
        check_vma=False,
    )
```

```python
import functools

import jax
import jax.numpy as jnp
import numpy as np
from jax import lax
from jax.experimental import pallas as pl
from jax.experimental.pallas import tpu as pltpu
from jax.sharding import PartitionSpec as P

DH = 64
SEQ = 1152
HALF = SEQ // 2
EPS = 1e-05
bfloat = jnp.bfloat16
single = jnp.float32
MIB = 1 << 20
MUCH = 10**11
COST = 10**10


def tables():
    half_width = DH // 2
    places = np.arange(SEQ, dtype=np.float32)
    frequency = np.float32(10000.0) ** (-np.arange(half_width, dtype=np.float32) * np.float32(2.0 / DH))
    angles = frequency[:, None] * places[None, :]
    return (np.cos(angles).astype(np.float32), np.sin(angles).astype(np.float32))


def mul(a, b, ca=1, cb=0):
    return lax.dot_general(a, b, (((ca,), (cb,)), ((), ())), preferred_element_type=single)


def call(kernel, outs, operands, scratch=(), scalars=0, after=(), vmem=16, flops=0, far=0, far_outs=0):
    count, waits = len(operands), len(after)

    def body(*refs):
        kernel(*refs[:count], *refs[count + waits :])

    small = pl.BlockSpec(memory_space=pltpu.SMEM)
    whole = pl.BlockSpec(memory_space=pltpu.VMEM)
    apart = pl.BlockSpec(memory_space=pltpu.HBM)
    loose = pl.BlockSpec(memory_space=pl.ANY)
    inner = len(outs) - far_outs
    return pl.pallas_call(
        body,
        out_shape=[jax.ShapeDtypeStruct(out[0], out[1]) for out in outs],
        in_specs=[small] * scalars + [whole] * (count - scalars - far) + [apart] * far + [loose] * waits,
        out_specs=[small if len(out) > 2 else whole for out in outs[:inner]] + [apart] * far_outs,
        scratch_shapes=list(scratch),
        compiler_params=pltpu.CompilerParams(vmem_limit_bytes=vmem * MIB),
        cost_estimate=pl.CostEstimate(flops=flops, bytes_accessed=0, transcendentals=0),
    )(*operands, *after)


class Mover:
    def __init__(self, marks):
        self.marks = marks
        self.used = 0

    def __call__(self, *pairs):
        copies = []
        for source, target in pairs:
            copies.append(pltpu.make_async_copy(source, target, self.marks.at[self.used]))
            self.used += 1
        for copy in copies:
            copy.start()
        return copies


def wait(copies):
    for copy in copies:
        copy.wait()


ROWS = 64
PARTS = 3


def spans(rows, step=ROWS):
    return [slice(begin, begin + step) for begin in range(0, rows, step)]


def normal_of(x):
    centre = x - jnp.mean(x, axis=-1, keepdims=True)
    spread = jnp.mean(centre * centre, axis=-1, keepdims=True)
    scale = lax.rsqrt(spread + EPS)
    return centre * scale, scale


def split_body(owner_ref, in_ref, out_ref, hold, marks):
    go = Mover(marks)
    wait(go((in_ref.at[quarter(owner_ref[0], 0, hold.shape[0]), :], hold)))
    wait(go((hold, out_ref)))


def joined(owner, refs, target):
    size = refs[0].shape[0]
    return [(ref, target.at[quarter(owner, mask, size), :]) for mask, ref in enumerate(refs)]


def norm_body(x_ref, gain_ref, *out_refs):
    gain = gain_ref[...].reshape(1, -1)
    for index, out_ref in enumerate(out_refs):
        rows = out_ref.shape[0]
        for span in spans(rows, rows // 6):
            here = slice(index * rows + span.start, index * rows + span.stop)
            normal, _ = normal_of(x_ref[here, :].astype(single))
            out_ref[span, :] = (normal * gain).astype(bfloat)


def middle_body(x_ref, keep_ref, gain_ref, *rest):
    recv_refs, mid_ref, out_refs = rest[:PARTS], rest[PARTS], rest[PARTS + 1 :]
    gain = gain_ref[...].reshape(1, -1)
    rows = x_ref.shape[0] // PARTS
    for index in range(PARTS):
        for span in spans(rows):
            here = slice(index * rows + span.start, index * rows + span.stop)
            recv = recv_refs[index][span, :].astype(single)
            x = x_ref[here, :].astype(single) + (keep_ref[here, :] + recv)
            mid_ref[here, :] = x
            normal, _ = normal_of(x)
            out_refs[index][span, :] = (normal * gain).astype(bfloat)


def norm_back(x, grad, gain):
    normal, scale = normal_of(x)
    lifted = grad * gain
    back = scale * (
        lifted
        - jnp.mean(lifted, axis=-1, keepdims=True)
        - normal * jnp.mean(lifted * normal, axis=-1, keepdims=True)
    )
    return back, normal


def fold_rows(value):
    total = value[:8]
    for begin in range(8, value.shape[0], 8):
        total = total + value[begin : begin + 8]
    return total


def middle_back_body(mix_ref, x_ref, keep_ref, recv_ref, cot_ref, gain_ref, mid_ref, low_ref, part_ref):
    gain = gain_ref[...].reshape(1, -1)
    part = jnp.zeros((8, x_ref.shape[1]), single)
    for span in spans(x_ref.shape[0]):
        grad = keep_ref[span, :] + recv_ref[span, :].astype(single)
        back, normal = norm_back(x_ref[span, :], grad, gain)
        total = mix_ref[mix_ref.shape[0] - 1] * cot_ref[span, :] + back
        mid_ref[span, :] = total
        low_ref[span, :] = total.astype(bfloat)
        part = part + fold_rows(grad * normal)
    part_ref[...] = jnp.sum(part, axis=0, keepdims=True)


def first_back_body(x_ref, keep_ref, recv_ref, mid_ref, gain_ref, out_ref):
    gain = gain_ref[...].reshape(1, -1)
    for span in spans(x_ref.shape[0]):
        grad = keep_ref[span, :] + recv_ref[span, :].astype(single)
        back, _ = norm_back(x_ref[span, :].astype(single), grad, gain)
        out_ref[span, :] = (mid_ref[span, :] + back).astype(bfloat)


def history_body(mix_ref, history_ref, cot_ref, grad_ref, mixed_ref, low_ref, part_ref):
    depth = history_ref.shape[0]

    @pl.when(pl.program_id(0) == 0)
    def _():
        part_ref[...] = jnp.zeros_like(part_ref)

    for span in spans(cot_ref.shape[0], 32):
        cot = cot_ref[span, :]
        low_ref[span, :] = (mix_ref[depth] * cot).astype(bfloat)
        mixed = None
        for j in range(depth):
            layer = history_ref[j, span, :].astype(single)
            mixed = mix_ref[j] * layer if mixed is None else mixed + mix_ref[j] * layer
            grad_ref[j, span, :] = (mix_ref[j] * cot).astype(bfloat)
            part_ref[8 * j : 8 * j + 8, :] += fold_rows(layer * cot)
        mixed_ref[span, :] = mixed


def average_history(mix, history, cot, after=()):
    depth, rows, width = history.shape
    step = 96
    waits = len(after)

    def body(*refs):
        history_body(*refs[:3], *refs[3 + waits :])

    row_block = pl.BlockSpec((step, width), lambda i: (i, 0))
    deep_block = pl.BlockSpec((depth, step, width), lambda i: (0, i, 0))
    return pl.pallas_call(
        body,
        grid=(rows // step,),
        out_shape=[
            jax.ShapeDtypeStruct(history.shape, bfloat),
            jax.ShapeDtypeStruct((rows, width), single),
            jax.ShapeDtypeStruct((rows, width), bfloat),
            jax.ShapeDtypeStruct((8 * depth, width), single),
        ],
        in_specs=[pl.BlockSpec(memory_space=pltpu.SMEM), deep_block, row_block]
        + [pl.BlockSpec(memory_space=pl.ANY)] * waits,
        out_specs=[deep_block, row_block, row_block, pl.BlockSpec((8 * depth, width), lambda i: (0, 0))],
        compiler_params=pltpu.CompilerParams(vmem_limit_bytes=16 * MIB),
        cost_estimate=pl.CostEstimate(flops=0, bytes_accessed=0, transcendentals=0),
    )(mix, history, cot, *after)


def combine_body(
    mix_ref, mixed_ref, mid_ref, keep_ref, recv_ref, cot_ref, parts_ref, attn_ref, mlp_ref, out_ref, part_ref
):
    depth = mix_ref.shape[0] - 1
    last = jnp.zeros((8, mid_ref.shape[1]), single)
    for span in spans(mid_ref.shape[0]):
        outputs = mid_ref[span, :] + (keep_ref[span, :] + recv_ref[span, :].astype(single))
        out_ref[span, :] = (mixed_ref[span, :] + mix_ref[depth] * outputs).astype(bfloat)
        last = last + fold_rows(outputs * cot_ref[span, :])
    part_ref[:1, :] = attn_ref[...]
    part_ref[1:2, :] = mlp_ref[...]
    for j in range(depth):
        part_ref[2 + j : 3 + j, :] = jnp.sum(parts_ref[8 * j : 8 * j + 8, :], axis=0, keepdims=True)
    part_ref[2 + depth : 3 + depth, :] = jnp.sum(last, axis=0, keepdims=True)


SQUARE = 4


def quarter(owner, mask, size):
    other = owner + (mask & 1) * (1 - 2 * (owner % 2)) + (mask & 2) * (1 - 2 * (owner // 2))
    return pl.ds(pl.multiple_of(other * size, size), size)


def part_body(owner_ref, mine_ref, come_ref, *out_refs):
    for mask, out_ref in enumerate(out_refs):
        rows = quarter(owner_ref[0], mask, out_ref.shape[0])
        out_ref[...] = (mine_ref[rows, :].astype(single) + come_ref[rows, :].astype(single)).astype(bfloat)


def sum_of(refs, rows):
    total = refs[0][rows, :].astype(single)
    for ref in refs[1:]:
        total = total + ref[rows, :].astype(single)
    return total


def four_body(*refs):
    refs[-1][...] = sum_of(refs[:-1], slice(None)).astype(bfloat)


def four_two_body(*refs):
    size = refs[-1].shape[0]
    refs[-2][...] = sum_of(refs[:-2], slice(0, size)).astype(bfloat)
    refs[-1][...] = sum_of(refs[:-2], slice(size, 2 * size)).astype(bfloat)


EXTRA = 16


def mark_body(out_ref):
    out_ref[...] = jnp.zeros_like(out_ref)


def add_body(mine_ref, come_ref, out_ref):
    out_ref[...] = mine_ref[...] + come_ref[...]


def four_more_body(small_ref, more_ref, *refs):
    out_ref = refs[-1]
    size = out_ref.shape[0] - EXTRA
    out_ref[:size, :] = sum_of(refs[:-1], slice(None)).astype(bfloat)
    small = small_ref[...] + more_ref[...]
    rest = jnp.zeros((EXTRA - small.shape[0], small.shape[1]), single)
    out_ref[size:, :] = jnp.concatenate([small, rest], axis=0).astype(bfloat)


def gather(owner_ref, pieces, hold):
    for mask, piece in enumerate(pieces):
        hold[quarter(owner_ref[0], mask, piece.shape[0]), :] = piece[...]


def pair_body(a_ref, a_come_ref, b_ref, b_come_ref, out_ref):
    size = a_ref.shape[0]
    out_ref[:size, :] = sum_of((a_ref, a_come_ref), slice(None)).astype(bfloat)
    out_ref[size:, :] = sum_of((b_ref, b_come_ref), slice(None)).astype(bfloat)


def whole_body(owner_ref, a_ref, b_ref, c_ref, d_ref, out_ref, hold):
    gather(owner_ref, (a_ref, b_ref, c_ref, d_ref), hold)
    out_ref[...] = hold[...].astype(single)


def more_body(owner_ref, a_ref, b_ref, c_ref, d_ref, top_ref, end_ref, up_ref, attn_ref, mlp_ref, dwa_ref, hold):
    gather(owner_ref, (a_ref, b_ref, c_ref, d_ref), hold)
    block = hold.shape[0] // SQUARE
    rows = up_ref.shape[0] // SQUARE
    small = jnp.zeros((EXTRA, hold.shape[1]), single)
    for index in range(SQUARE):
        begin = index * block
        target, place = (top_ref, index * rows) if index < SQUARE - 1 else (end_ref, 0)
        target[place : place + rows, :] = hold[begin : begin + rows, :].astype(single)
        small = small + hold[begin + rows : begin + rows + EXTRA, :].astype(single)
        up_ref[index * rows : (index + 1) * rows, :] = hold[begin + rows + EXTRA : begin + block, :].astype(single)
    attn_ref[...] = small[0]
    mlp_ref[...] = small[1]
    for index in range(dwa_ref.shape[0]):
        dwa_ref[index] = jnp.sum(small[2 + index : 3 + index])


def low_body(mine_ref, come_ref, out_ref):
    out_ref[...] = (mine_ref[...].astype(single) + come_ref[...].astype(single)).astype(bfloat)


def mark_body(out_ref):
    out_ref[...] = jnp.zeros_like(out_ref)


def small_body(small_ref, first_ref, out_ref):
    half = small_ref.shape[0]
    rows = first_ref.shape[0] - 2 * half
    come = first_ref[rows:, :].astype(single)
    out_ref[...] = small_ref[...] + (come[:half] + come[half:])


BLOCKS = tuple((begin, min(256, SEQ - begin)) for begin in range(0, SEQ, 256))


def places(core_ref, refs):
    count, size = len(refs) // 2, refs[0].shape[0]
    for index, ref in enumerate(refs):
        core = core_ref[0] if index < count else 1 - core_ref[0]
        yield ref, pl.ds(pl.multiple_of(core * HALF + index % count * size, size), size)


def allowed(size):
    key_pos = lax.broadcasted_iota(jnp.int32, (size, size), 0)
    query_pos = lax.broadcasted_iota(jnp.int32, (size, size), 1)
    return query_pos >= key_pos


def turn(rows, cosine, sine):
    half = rows.shape[0] // 2
    a, b = rows[:half], rows[half:]
    return jnp.concatenate([a * cosine - b * sine, b * cosine + a * sine], axis=0)


KEYS = 128


def fold_top(value):
    top = value[:8]
    for begin in range(8, value.shape[0], 8):
        top = jnp.maximum(top, value[begin : begin + 8])
    return top


def masked(scores, offset):
    key_pos = lax.broadcasted_iota(jnp.int32, scores.shape, 0) + offset
    query_pos = lax.broadcasted_iota(jnp.int32, scores.shape, 1)
    return jnp.where(query_pos >= key_pos, scores, -jnp.inf)


def attend_placed(core_ref, *rest):
    for ref, where in places(core_ref, rest[:4]):
        rest[11][where, :] = ref[...]
    cos_ref, sin_ref, weight_ref, rest = rest[4], rest[5], rest[6], rest[7:]
    attend(weight_ref, cos_ref, sin_ref, *rest)


def attend(weight_ref, cos_ref, sin_ref, qkv_ref, att_ref, nat_ref, log_ref, tokens, all_scores, all_weights):
    width = weight_ref.shape[0] // 3
    projected = mul(weight_ref[...], tokens[...], 1, 1)
    cosine, sine = cos_ref[...], sin_ref[...]
    for part in range(3):
        for head in range(width // DH):
            begin = part * width + head * DH
            rows = projected[begin : begin + DH]
            if part < 2:
                rows = turn(rows, cosine, sine)
            if part == 0:
                rows = rows * DH ** (-0.5)
            qkv_ref[begin : begin + DH, :] = rows.astype(bfloat)
    log_ref[...] = jnp.zeros_like(log_ref)
    heads = range(width // DH)
    keys = [qkv_ref[width + head * DH : width + head * DH + DH, :].T for head in heads]
    for begin, size in BLOCKS:
        end = begin + size
        tops = [None for _ in heads]
        for row in range(0, end, KEYS):
            for head in heads:
                tile = mul(keys[head][row : row + KEYS], qkv_ref[head * DH : head * DH + DH, begin:end])
                if row >= begin:
                    tile = masked(tile, row - begin)
                all_scores[head, row : row + KEYS, :size] = tile
                top = fold_top(tile)
                tops[head] = top if row == 0 else jnp.maximum(tops[head], top)
        tops = [jnp.max(top, axis=0, keepdims=True) for top in tops]
        totals = [jnp.zeros((8, size), single) for _ in heads]
        for row in range(0, end, KEYS):
            for head in heads:
                tile = jnp.exp(all_scores[head, row : row + KEYS, :size] - tops[head])
                totals[head] = totals[head] + fold_rows(tile)
                all_weights[head, row : row + KEYS, :size] = tile.astype(bfloat)
        for head in heads:
            base = head * DH
            total = jnp.sum(totals[head], axis=0, keepdims=True)
            value = qkv_ref[2 * width + base : 2 * width + base + DH, :end]
            mixed = mul(value, all_weights[head, :end, :size]) / total
            att_ref[base : base + DH, begin:end] = mixed.astype(bfloat)
            log_ref[head : head + 1, begin:end] = tops[head] + jnp.log(total)
    nat_ref[...] = att_ref[...].T


def branch_body(core_ref, att_a_ref, att_b_ref, out_a_ref, out_b_ref, pass_ref, keep_ref, *rest):
    send_refs, pass_out = rest[:PARTS], rest[PARTS]
    pass_out[...] = pass_ref[...]
    low = pl.multiple_of(core_ref[0] * HALF, HALF)
    rows = HALF // PARTS
    for index in range(PARTS):
        high = pl.multiple_of((1 - core_ref[0]) * HALF + index * rows, rows)
        send = mul(att_a_ref[pl.ds(high, rows), :], out_a_ref[...])
        send_refs[index][...] = (send + mul(att_b_ref[pl.ds(high, rows), :], out_b_ref[...])).astype(bfloat)
    keep = mul(att_a_ref[pl.ds(low, HALF), :], out_a_ref[...])
    keep_ref[...] = keep + mul(att_b_ref[pl.ds(low, HALF), :], out_b_ref[...])


def attend_back(
    core_ref, log_ref, cos_ref, sin_ref, gain_ref, *rest
):
    before_refs, rest = rest[:-25], rest[-25:]
    grad_refs, x_refs = rest[:2], rest[2:6]
    weight_ref, qkv_weight_ref, qkv_ref, att_ref, small_ref, out_ref, turned_ref = rest[6:13]
    grads, tokens, weight, qkv_weight, qkv, att, turned, result, all_probs, all_scores, hold, marks = rest[13:]
    go = Mover(marks)
    first = go(
        (weight_ref, weight),
        *[(ref, grads.at[where, :]) for ref, where in places(core_ref, grad_refs)],
        (att_ref, att),
        (qkv_ref, qkv),
    )
    later = go(
        *[(ref, tokens.at[where, :]) for ref, where in places(core_ref, x_refs)],
        (qkv_weight_ref, qkv_weight),
    )
    wait(first)
    width = att.shape[0]
    grad_att = mul(weight[...], grads[...], 1, 1).astype(bfloat)
    result[3 * width :, :] = mul(att[...], grads[...]).astype(result.dtype)
    cosine, sine = cos_ref[...], sin_ref[...]
    heads = range(width // DH)
    spans_of = [slice(head * DH, head * DH + DH) for head in heads]
    query = [qkv[span, :] for span in spans_of]
    key = [qkv[width + span.start : width + span.stop, :] for span in spans_of]
    above = [grad_att[span] for span in spans_of]
    centre = [
        jnp.sum(above[head].astype(single) * att[span, :].astype(single), axis=0, keepdims=True)
        for head, span in enumerate(spans_of)
    ]
    keys = [value.T for value in key]
    values = [qkv[2 * width + span.start : 2 * width + span.stop, :].T for span in spans_of]
    queries = [value.T for value in query]
    aboves = [value.T for value in above]
    grad_query = [[] for _ in heads]
    for begin, size in BLOCKS:
        end = begin + size
        for row in range(0, end, KEYS):
            span = slice(row, row + KEYS)
            for head in heads:
                tile = mul(keys[head][span], query[head][:, begin:end])
                if row >= begin:
                    tile = masked(tile, row - begin)
                tile = jnp.exp(tile - log_ref[head : head + 1, begin:end])
                grad = mul(values[head][span], above[head][:, begin:end]) - centre[head][:, begin:end]
                all_probs[head, span, begin:end] = tile.astype(bfloat)
                all_scores[head, span, begin:end] = (tile * grad).astype(bfloat)
        for head in heads:
            grad_query[head].append(mul(key[head][:, :end], all_scores[head, :end, begin:end]))
    grad_key = [[] for _ in heads]
    grad_value = [[] for _ in heads]
    for begin, size in BLOCKS:
        span = slice(begin, begin + size)
        for head in heads:
            grad_key[head].append(mul(all_scores[head, span, begin:], queries[head][begin:]))
            grad_value[head].append(mul(all_probs[head, span, begin:], aboves[head][begin:]))
    for head, span in enumerate(spans_of):
        grad = jnp.concatenate(grad_query[head], axis=1) * DH ** (-0.5)
        turned[span, :] = turn(grad, cosine, -sine).astype(bfloat)
        grad = jnp.concatenate(grad_key[head], axis=0).T
        turned[width + span.start : width + span.stop, :] = turn(grad, cosine, -sine).astype(bfloat)
        grad = jnp.concatenate(grad_value[head], axis=0).T
        turned[2 * width + span.start : 2 * width + span.stop, :] = grad.astype(bfloat)
    stores = go((turned, turned_ref))
    wait(later)
    hold[...] = mul(turned[...], tokens[...])
    result[: 3 * width, :] = hold[...].astype(result.dtype)
    stores += go((result, out_ref))
    part = jnp.zeros((8, hold.shape[1]), single)
    for span in spans(hold.shape[0]):
        part = part + fold_rows(hold[span, :] * qkv_weight[span, :].astype(single))
    gain = jnp.sum(part, axis=0, keepdims=True) / gain_ref[...].reshape(1, -1)
    small_ref[...] = gain + before_refs[0][...] if before_refs else gain
    wait(stores)


def first_grad_body(
    core_ref, turned_a_ref, turned_b_ref, weight_a_ref, weight_b_ref, send_ref, keep_ref,
    turned_a, turned_b, weight_a, weight_b, whole, marks,
):
    low = pl.multiple_of(core_ref[0] * HALF, HALF)
    high = pl.multiple_of((1 - core_ref[0]) * HALF, HALF)
    go = Mover(marks)
    wait(go((turned_a_ref, turned_a), (weight_a_ref, weight_a), (turned_b_ref, turned_b), (weight_b_ref, weight_b)))
    whole[...] = mul(turned_a[...], weight_a[...], 0, 0) + mul(turned_b[...], weight_b[...], 0, 0)
    stores = go((whole.at[pl.ds(low, HALF), :], keep_ref))
    send_ref[...] = whole[pl.ds(high, HALF), :].astype(bfloat)
    wait(stores)


CURVE = float(np.sqrt(2.0 / np.pi))
STEP = 256


def mlp_body(second, *refs):
    if second:
        owner_ref, refs = refs[0], refs[1:]
    x_refs, refs = refs[: 2 * PARTS], refs[2 * PARTS :]
    g_own_ref, g_peer_ref, up_ref, refs = refs[0], refs[1], refs[2], refs[3:]
    if second:
        down_refs, before_refs, up_mine_ref = refs[:SQUARE], refs[SQUARE : SQUARE + 2], refs[SQUARE + 2]
        refs = refs[SQUARE + 3 :]
    else:
        down_ref, refs = refs[0], refs[1:]
    send_norm_ref, keep_norm_ref, active_ref, down_grad_ref = refs[:4]
    if second:
        part_refs, refs = refs[4 : 4 + SQUARE], refs[4 + SQUARE :]
    else:
        up_grad_ref, refs = refs[4], refs[5:]
    x_all, g_all, up, down, active, grad_hidden, x_turned = refs[:7]
    send_norm, keep_norm, down_grad, up_grad, marks = refs[7:12]
    rows, size = x_all.shape[0] // 2, x_all.shape[0] // (2 * PARTS)
    units = down.shape[0]
    go = Mover(marks)
    x_loads = go(*[(x_refs[index], x_all.at[pl.ds(index * size, size), :]) for index in range(2 * PARTS)])
    if second:
        loads = go((up_ref, up), *joined(owner_ref[0], down_refs, down))
    else:
        loads = go((up_ref, up), (down_ref, down))
    loads += go((g_own_ref, g_all.at[pl.ds(0, rows), :]), (g_peer_ref, g_all.at[pl.ds(rows, rows), :]))
    more, mine, stores = [], [], []
    if second:
        (up_mine,) = refs[12:]
        more = go(*zip(before_refs, (send_norm, keep_norm)))
        mine = go((up_mine_ref, up_mine))
    wait(x_loads)
    x_turned[...] = x_all[...].T
    wait(loads)
    for begin in range(0, units, STEP):
        columns = slice(begin, begin + STEP)
        for top in range(0, 2 * rows, rows):
            span = slice(top, top + rows)
            v = mul(x_all[span, :], up[:, columns])
            grad = mul(g_all[span, :], down[columns, :], 1, 1)
            square = v * v
            half = 0.5 + 0.5 * jnp.tanh(v * (CURVE + (CURVE * 0.044715) * square))
            act = v * half
            slope = half + act * (1.0 - half) * (2.0 * CURVE + (6.0 * CURVE * 0.044715) * square)
            active[span, columns] = act.astype(bfloat)
            grad_hidden[span, columns] = (grad * slope).astype(bfloat)

    stores += go((active, active_ref))

    def put(target, value):
        target[...] = (value + target[...].astype(single) if second else value).astype(target.dtype)

    wait(more)
    put(keep_norm, mul(grad_hidden[:rows, :], up[...], 1, 1))
    put(send_norm, mul(grad_hidden[rows:, :], up[...], 1, 1))
    stores += go((keep_norm, keep_norm_ref), (send_norm, send_norm_ref))
    down_grad[...] = mul(active[...], g_all[...], 0, 0).astype(down_grad.dtype)
    stores += go((down_grad, down_grad_ref))
    up_grad[...] = mul(x_turned[...], grad_hidden[...]).astype(bfloat)
    if second:
        wait(mine)
        part = up_grad.shape[0] // SQUARE
        for mask, part_ref in enumerate(part_refs):
            rows_of = quarter(owner_ref[0], mask, part)
            stores += go(
                (up_mine.at[rows_of, :], part_ref.at[pl.ds(0, part), :]),
                (up_grad.at[rows_of, :], part_ref.at[pl.ds(part, part), :]),
            )
    else:
        stores += go((up_grad, up_grad_ref))
    wait(stores)


def outputs_body(owner_ref, active_a_ref, down_a_ref, active_b_ref, *rest):
    down_b_refs, keep_ref, send_ref = rest[:SQUARE], rest[SQUARE], rest[SQUARE + 1]
    active_a, down_a, active_b, down_b, marks = rest[SQUARE + 2 :]
    go = Mover(marks)
    wait(
        go(
            (active_a_ref, active_a),
            (down_a_ref, down_a),
            (active_b_ref, active_b),
            *joined(owner_ref[0], down_b_refs, down_b),
        )
    )
    rows = keep_ref.shape[0]
    send = mul(active_a[rows:, :], down_a[...]) + mul(active_b[rows:, :], down_b[...])
    send_ref[...] = send.astype(bfloat)
    keep_ref[...] = mul(active_a[:rows, :], down_a[...]) + mul(active_b[:rows, :], down_b[...])


def mlp(x_own, x_peer, g_own, g_peer, up, down, upper=(), before=(), flops=0):
    rows, width = g_own.shape
    units = sum(piece.shape[0] for piece in down)
    tall = (2 * rows, width)
    pair = [((rows, width), bfloat), ((rows, width), single)]
    outs = pair + [((2 * rows, units), bfloat), ((units, width), bfloat)]
    outs += [((2 * width // SQUARE, units), bfloat)] * SQUARE if before else [((width, units), bfloat)]
    scratch = [
        pltpu.VMEM(tall, bfloat),
        pltpu.VMEM(tall, bfloat),
        pltpu.VMEM((width, units), bfloat),
        pltpu.VMEM((units, width), bfloat),
        pltpu.VMEM((2 * rows, units), bfloat),
        pltpu.VMEM((2 * rows, units), bfloat),
        pltpu.VMEM((width, 2 * rows), bfloat),
    ]
    scratch += [pltpu.VMEM(shape, kind) for shape, kind in pair]
    scratch += [
        pltpu.VMEM((units, width), bfloat), pltpu.VMEM((width, units), bfloat), pltpu.SemaphoreType.DMA((32,)),
    ]
    if before:
        scratch.append(pltpu.VMEM((width, units), bfloat))
    operands = (*upper, *x_own, *x_peer, g_own, g_peer, *up, *down, *before)
    return call(
        functools.partial(mlp_body, bool(before)),
        outs,
        operands,
        scratch,
        len(upper),
        vmem=60,
        flops=flops,
        far=len(operands) - len(upper),
        far_outs=len(outs),
    )


def shards(
    inputs,
    history,
    cotangent,
    qkv_weight,
    out_weight,
    up_weight,
    down_weight,
    gain_attn,
    gain_mlp,
    dwa_weights,
):
    rows, width = inputs.shape
    members = lax.axis_size("mp")
    copies = lax.axis_size("dp")
    bits = copies.bit_length() - 1
    core = lax.rem(lax.axis_index("mp"), 2).astype(jnp.int32).reshape(1)
    copy_index = lax.axis_index("dp").astype(jnp.int32).reshape(1)
    core_pairs = [(i, i ^ 1) for i in range(members)]
    chip_pairs = [(i, i ^ 2) for i in range(members)]
    depth = history.shape[0]
    part = out_weight.shape[0]

    def other_core(value):
        return lax.ppermute(value, "mp", core_pairs)

    def other_chip(value):
        return lax.ppermute(value, "mp", chip_pairs)

    def other_copy(value, mask):
        return lax.ppermute(value, "dp", [(i, i ^ mask) for i in range(copies)])

    owner = copy_index & (SQUARE - 1)
    cosine, sine = (jnp.asarray(table) for table in tables())

    qkv_own = qkv_weight.transpose(1, 2, 0).reshape(3 * part, width)
    fourth = (width // SQUARE, width)
    square = (width, width)
    masks = range(1, SQUARE)
    marks = pltpu.SemaphoreType.DMA((16,))
    (down_quarter,) = call(
        split_body,
        [(fourth, bfloat)],
        (owner, down_weight),
        [pltpu.VMEM(fourth, bfloat), marks],
        1,
        vmem=60,
        far=1,
        far_outs=1,
    )
    qkv_peer, out_peer = other_chip(qkv_own), other_chip(out_weight)
    down_come, up_peer = other_chip(down_quarter), other_chip(up_weight)

    full = (rows, width)
    x_own = call(norm_body, [((rows // 2, width), bfloat)] * 2, (inputs, gain_attn), after=(down_quarter,))
    x_peer = [other_core(value) for value in x_own]
    tall = (SEQ, width)
    tokens = pltpu.VMEM(tall, bfloat)
    first_outs = [
        ((3 * part, SEQ), bfloat), ((part, SEQ), bfloat), ((SEQ, part), bfloat), ((8, SEQ), single),
    ]
    heads = part // DH
    tiles = [tokens, pltpu.VMEM((heads, SEQ, 256), single), pltpu.VMEM((heads, SEQ, 256), bfloat)]
    qkv_a, att_a, nat_a, log_a = call(
        attend_placed, first_outs, (core, *x_own, *x_peer, cosine, sine, qkv_own), tiles, 1, vmem=32
    )
    history_grad, mixed, g_own, history_parts = average_history(dwa_weights, history, cotangent, (log_a,))
    g_peer = other_core(g_own)
    qkv_b, att_b, nat_b, log_b = call(
        attend_placed,
        first_outs,
        (core, *x_own, *x_peer, cosine, sine, qkv_peer),
        tiles,
        1,
        (history_parts,),
        32,
        MUCH,
    )
    third = (rows // PARTS, width)
    keep, *send, down_copy = call(
        branch_body,
        [(full, single)] + [(third, bfloat)] * PARTS + [(fourth, bfloat)],
        (core, nat_a, nat_b, out_weight, out_peer, down_come),
        (),
        1,
        (g_peer,),
    )
    down_pieces = [down_come] + [other_copy(down_copy, mask) for mask in masks]
    recv = [other_core(value) for value in send]
    middle, *y_own = call(
        middle_body, [(full, single)] + [(third, bfloat)] * PARTS, (inputs, keep, gain_mlp, *recv)
    )
    y_peer = [other_core(value) for value in y_own]

    first = mlp(y_own, y_peer, g_own, g_peer, (up_weight,), (down_weight,))
    active_a, down_mine, up_mine = first[2:]
    second = mlp(
        y_own, y_peer, g_own, g_peer, (up_peer,), down_pieces, (owner,), (*first[:2], up_mine)
    )
    send_norm, keep_norm, active_b, down_theirs = second[:4]
    token = [send_norm]

    def step(body, outs, operands, scratch=(), scalars=0, vmem=16, flops=MUCH, far=0, far_outs=0):
        results = call(body, outs, operands, scratch, scalars, tuple(token), vmem, flops, far, far_outs)
        token[0] = results[0]
        return results

    down_come = other_chip(down_theirs)
    up_parts = [second[4]] + [other_copy(value, mask) for mask, value in zip(masks, second[5:])]
    grad_middle, gb_own, gain_mlp_part = step(
        middle_back_body,
        [(full, single), (full, bfloat), ((1, width), single)],
        (dwa_weights, middle, keep_norm, other_core(send_norm), cotangent, gain_mlp),
        scalars=1,
        flops=0,
    )
    gb_peer = other_core(gb_own)
    def back(weight, qkv_weight, qkv, att, log, flops, before=()):
        return step(
            attend_back,
            [
                ((1, width), single),
                ((4 * part, width), bfloat),
                ((3 * part, SEQ), bfloat),
            ],
            (
                core, log, cosine, sine, gain_attn, *before, gb_own, gb_peer, *x_own, *x_peer, weight, qkv_weight, qkv,
                att,
            ),
            [
                pltpu.VMEM(tall, bfloat),
                pltpu.VMEM(tall, bfloat),
                pltpu.VMEM((part, width), bfloat),
                pltpu.VMEM((3 * part, width), bfloat),
                pltpu.VMEM((3 * part, SEQ), bfloat),
                pltpu.VMEM((part, SEQ), bfloat),
                pltpu.VMEM((3 * part, SEQ), bfloat),
                pltpu.VMEM((4 * part, width), bfloat),
                pltpu.VMEM((heads, SEQ, SEQ), bfloat),
                pltpu.VMEM((heads, SEQ, SEQ), bfloat),
                pltpu.VMEM((3 * part, width), single),
                marks,
            ],
            1,
            60,
            flops,
            10,
            2,
        )

    gain_part, att_theirs, turned_b = back(out_peer, qkv_peer, qkv_b, att_b, log_b, 0)
    att_come = other_chip(att_theirs)
    def spread(mine, come, flops=MUCH):
        own, *sent = step(part_body, [(fourth, bfloat)] * SQUARE, (owner, mine, come), scalars=1, flops=flops)
        return [own] + [other_copy(value, mask) for mask, value in zip(masks, sent)]

    down_parts = spread(down_mine, down_come, 0)
    up, sent = step(four_two_body, [(fourth, bfloat)] * 2, up_parts, flops=0)
    up_come = other_chip(sent)
    gain_part, att_mine, turned_a = back(
        out_weight, qkv_own, qkv_a, att_a, log_a, MUCH, (gain_part,)
    )

    def exchange(value):
        for bit in range(2, bits):
            come = other_copy(value, 1 << bit)
            if bit < bits - 1:
                (value,) = step(low_body, [(value.shape, bfloat)], (value, come))
        return value, come

    def finish(value, come):
        (value,) = step(low_body, [(value.shape, bfloat)], (value, come), flops=COST)
        return [value] + [other_copy(value, mask) for mask in masks]

    (down,) = step(four_body, [(fourth, bfloat)], down_parts, flops=COST)
    down = exchange(down)
    att_parts = spread(att_mine, att_come, COST)
    (up,) = step(low_body, [(fourth, bfloat)], (up, up_come), flops=COST)
    up = exchange(up)
    def gate():
        step(mark_body, [((8, 128), single)], (), flops=COST)

    keep_out, send_out = step(
        outputs_body,
        [(full, single), (full, bfloat)],
        (owner, active_a, down_weight, active_b, *down_pieces),
        [pltpu.VMEM(tall, bfloat), pltpu.VMEM(square, bfloat)] * 2 + [marks],
        1,
        60,
        COST,
        7,
    )
    out_come = other_core(send_out)
    token.append(down[1])
    gate()
    del token[1:]
    combined, part_sums = step(
        combine_body,
        [(full, bfloat), ((depth + 3, width), single)],
        (dwa_weights, mixed, middle, keep_out, out_come, cotangent, history_parts, gain_part, gain_mlp_part),
        scalars=1,
        flops=COST,
    )
    core_sums = other_core(part_sums)
    gate()
    (part_sums,) = step(add_body, [(part_sums.shape, single)], (part_sums, core_sums), flops=COST)
    more_sums = other_chip(part_sums)
    gate()
    block = (width // SQUARE + EXTRA, width)
    (att,) = step(four_more_body, [(block, bfloat)], (part_sums, more_sums, *att_parts), flops=COST)
    att = exchange(att)
    down = finish(*down)
    token += down[1:]
    pair = (block[0] + fourth[0], width)
    (both,) = step(pair_body, [(pair, bfloat)], (*att, *up), flops=COST)
    del token[1:]
    both = [both] + [other_copy(both, mask) for mask in masks]
    send_first, keep_first = step(
        first_grad_body,
        [(full, bfloat), (full, single)],
        (core, turned_a, turned_b, qkv_own, qkv_peer),
        [pltpu.VMEM((3 * part, SEQ), bfloat)] * 2
        + [pltpu.VMEM((3 * part, width), bfloat)] * 2
        + [pltpu.VMEM(tall, single), marks],
        1,
        60,
        COST,
        4,
        1,
    )
    first_come = other_core(send_first)
    (down_grad,) = step(
        whole_body, [(square, single)], (owner, *down), [pltpu.VMEM(square, bfloat)], 1, flops=COST
    )
    (input_grad,) = step(
        first_back_body,
        [(full, bfloat)],
        (inputs, keep_first, first_come, grad_middle, gain_attn),
        vmem=60,
        flops=COST,
    )
    qkv_grad, out_grad, up_grad, gain_attn_grad, gain_mlp_grad, dwa_grad = step(
        more_body,
        [
            ((3 * part, width), single),
            ((part, width), single),
            (square, single),
            ((width,), single),
            ((width,), single),
            ((depth + 1,), single, "scalars"),
        ],
        (owner, *both),
        [pltpu.VMEM((SQUARE * pair[0], width), bfloat)],
        1,
        flops=COST,
    )

    return (
        combined,
        input_grad,
        history_grad,
        qkv_grad.reshape(3, part, width).transpose(2, 0, 1),
        out_grad,
        up_grad,
        down_grad,
        gain_attn_grad,
        gain_mlp_grad,
        dwa_grad,
    )


def solution(mesh):
    placed = (
        P(("dp", "mp"), None),
        P(None, ("dp", "mp"), None),
        P(("dp", "mp"), None),
        P(None, None, "mp"),
        P("mp", None),
        P(None, "mp"),
        P("mp", None),
        P(),
        P(),
        P(),
    )
    return jax.shard_map(
        shards,
        mesh=mesh,
        in_specs=placed,
        out_specs=(
            P(("dp", "mp"), None),
            P(("dp", "mp"), None),
            P(None, ("dp", "mp"), None),
            P(None, None, "mp"),
            P("mp", None),
            P(None, "mp"),
            P("mp", None),
            P(),
            P(),
            P(),
        ),
        check_vma=False,
    )
```

```python
import functools

import jax
import jax.numpy as jnp
import numpy as np
from jax import lax
from jax.experimental import pallas as pl
from jax.experimental.pallas import tpu as pltpu
from jax.sharding import PartitionSpec as P

DH = 64
SEQ = 1152
HALF = SEQ // 2
EPS = 1e-05
bfloat = jnp.bfloat16
single = jnp.float32
MIB = 1 << 20
MUCH = 10**11
COST = 10**10


def tables():
    half_width = DH // 2
    places = np.arange(SEQ, dtype=np.float32)
    frequency = np.float32(10000.0) ** (-np.arange(half_width, dtype=np.float32) * np.float32(2.0 / DH))
    angles = frequency[:, None] * places[None, :]
    return (np.cos(angles).astype(np.float32), np.sin(angles).astype(np.float32))


def mul(a, b, ca=1, cb=0):
    return lax.dot_general(a, b, (((ca,), (cb,)), ((), ())), preferred_element_type=single)


def call(kernel, outs, operands, scratch=(), scalars=0, after=(), vmem=16, flops=0, far=0, far_outs=0):
    count, waits = len(operands), len(after)

    def body(*refs):
        kernel(*refs[:count], *refs[count + waits :])

    small = pl.BlockSpec(memory_space=pltpu.SMEM)
    whole = pl.BlockSpec(memory_space=pltpu.VMEM)
    apart = pl.BlockSpec(memory_space=pltpu.HBM)
    loose = pl.BlockSpec(memory_space=pl.ANY)
    inner = len(outs) - far_outs
    return pl.pallas_call(
        body,
        out_shape=[jax.ShapeDtypeStruct(out[0], out[1]) for out in outs],
        in_specs=[small] * scalars + [whole] * (count - scalars - far) + [apart] * far + [loose] * waits,
        out_specs=[small if len(out) > 2 else whole for out in outs[:inner]] + [apart] * far_outs,
        scratch_shapes=list(scratch),
        compiler_params=pltpu.CompilerParams(vmem_limit_bytes=vmem * MIB),
        cost_estimate=pl.CostEstimate(flops=flops, bytes_accessed=0, transcendentals=0),
    )(*operands, *after)


class Mover:
    def __init__(self, marks):
        self.marks = marks
        self.used = 0

    def __call__(self, *pairs):
        copies = []
        for source, target in pairs:
            copies.append(pltpu.make_async_copy(source, target, self.marks.at[self.used]))
            self.used += 1
        for copy in copies:
            copy.start()
        return copies


def wait(copies):
    for copy in copies:
        copy.wait()


ROWS = 64
PARTS = 3


def spans(rows, step=ROWS):
    return [slice(begin, begin + step) for begin in range(0, rows, step)]


def normal_of(x):
    centre = x - jnp.mean(x, axis=-1, keepdims=True)
    spread = jnp.mean(centre * centre, axis=-1, keepdims=True)
    scale = lax.rsqrt(spread + EPS)
    return centre * scale, scale


def split_body(owner_ref, in_ref, out_ref, hold, marks):
    go = Mover(marks)
    wait(go((in_ref.at[quarter(owner_ref[0], 0, hold.shape[0]), :], hold)))
    wait(go((hold, out_ref)))


def joined(owner, refs, target):
    size = refs[0].shape[0]
    return [(ref, target.at[quarter(owner, mask, size), :]) for mask, ref in enumerate(refs)]


def norm_body(x_ref, gain_ref, *out_refs):
    gain = gain_ref[...].reshape(1, -1)
    for index, out_ref in enumerate(out_refs):
        rows = out_ref.shape[0]
        for span in spans(rows, rows // 6):
            here = slice(index * rows + span.start, index * rows + span.stop)
            normal, _ = normal_of(x_ref[here, :].astype(single))
            out_ref[span, :] = (normal * gain).astype(bfloat)


def middle_body(x_ref, keep_ref, gain_ref, *rest):
    recv_refs, mid_ref, out_refs = rest[:PARTS], rest[PARTS], rest[PARTS + 1 :]
    gain = gain_ref[...].reshape(1, -1)
    rows = x_ref.shape[0] // PARTS
    for index in range(PARTS):
        for span in spans(rows):
            here = slice(index * rows + span.start, index * rows + span.stop)
            recv = recv_refs[index][span, :].astype(single)
            x = x_ref[here, :].astype(single) + (keep_ref[here, :] + recv)
            mid_ref[here, :] = x
            normal, _ = normal_of(x)
            out_refs[index][span, :] = (normal * gain).astype(bfloat)


def norm_back(x, grad, gain):
    normal, scale = normal_of(x)
    lifted = grad * gain
    back = scale * (
        lifted
        - jnp.mean(lifted, axis=-1, keepdims=True)
        - normal * jnp.mean(lifted * normal, axis=-1, keepdims=True)
    )
    return back, normal


def fold_rows(value):
    total = value[:8]
    for begin in range(8, value.shape[0], 8):
        total = total + value[begin : begin + 8]
    return total


def middle_back_body(mix_ref, x_ref, keep_ref, recv_ref, cot_ref, gain_ref, mid_ref, low_ref, part_ref):
    gain = gain_ref[...].reshape(1, -1)
    part = jnp.zeros((8, x_ref.shape[1]), single)
    for span in spans(x_ref.shape[0]):
        grad = keep_ref[span, :] + recv_ref[span, :].astype(single)
        back, normal = norm_back(x_ref[span, :], grad, gain)
        total = mix_ref[mix_ref.shape[0] - 1] * cot_ref[span, :] + back
        mid_ref[span, :] = total
        low_ref[span, :] = total.astype(bfloat)
        part = part + fold_rows(grad * normal)
    part_ref[...] = jnp.sum(part, axis=0, keepdims=True)


def first_back_body(x_ref, keep_ref, recv_ref, mid_ref, gain_ref, out_ref):
    gain = gain_ref[...].reshape(1, -1)
    for span in spans(x_ref.shape[0]):
        grad = keep_ref[span, :] + recv_ref[span, :].astype(single)
        back, _ = norm_back(x_ref[span, :].astype(single), grad, gain)
        out_ref[span, :] = (mid_ref[span, :] + back).astype(bfloat)


def history_body(mix_ref, history_ref, cot_ref, grad_ref, mixed_ref, low_ref, part_ref):
    depth = history_ref.shape[0]

    @pl.when(pl.program_id(0) == 0)
    def _():
        part_ref[...] = jnp.zeros_like(part_ref)

    for span in spans(cot_ref.shape[0], 32):
        cot = cot_ref[span, :]
        low_ref[span, :] = (mix_ref[depth] * cot).astype(bfloat)
        mixed = None
        for j in range(depth):
            layer = history_ref[j, span, :].astype(single)
            mixed = mix_ref[j] * layer if mixed is None else mixed + mix_ref[j] * layer
            grad_ref[j, span, :] = (mix_ref[j] * cot).astype(bfloat)
            part_ref[8 * j : 8 * j + 8, :] += fold_rows(layer * cot)
        mixed_ref[span, :] = mixed


def average_history(mix, history, cot, after=()):
    depth, rows, width = history.shape
    step = 96
    waits = len(after)

    def body(*refs):
        history_body(*refs[:3], *refs[3 + waits :])

    row_block = pl.BlockSpec((step, width), lambda i: (i, 0))
    deep_block = pl.BlockSpec((depth, step, width), lambda i: (0, i, 0))
    return pl.pallas_call(
        body,
        grid=(rows // step,),
        out_shape=[
            jax.ShapeDtypeStruct(history.shape, bfloat),
            jax.ShapeDtypeStruct((rows, width), single),
            jax.ShapeDtypeStruct((rows, width), bfloat),
            jax.ShapeDtypeStruct((8 * depth, width), single),
        ],
        in_specs=[pl.BlockSpec(memory_space=pltpu.SMEM), deep_block, row_block]
        + [pl.BlockSpec(memory_space=pl.ANY)] * waits,
        out_specs=[deep_block, row_block, row_block, pl.BlockSpec((8 * depth, width), lambda i: (0, 0))],
        compiler_params=pltpu.CompilerParams(vmem_limit_bytes=16 * MIB),
        cost_estimate=pl.CostEstimate(flops=0, bytes_accessed=0, transcendentals=0),
    )(mix, history, cot, *after)


def combine_body(
    mix_ref, mixed_ref, mid_ref, keep_ref, recv_ref, cot_ref, parts_ref, attn_ref, mlp_ref, out_ref, part_ref
):
    depth = mix_ref.shape[0] - 1
    last = jnp.zeros((8, mid_ref.shape[1]), single)
    for span in spans(mid_ref.shape[0]):
        outputs = mid_ref[span, :] + (keep_ref[span, :] + recv_ref[span, :].astype(single))
        out_ref[span, :] = (mixed_ref[span, :] + mix_ref[depth] * outputs).astype(bfloat)
        last = last + fold_rows(outputs * cot_ref[span, :])
    part_ref[:1, :] = attn_ref[...]
    part_ref[1:2, :] = mlp_ref[...]
    for j in range(depth):
        part_ref[2 + j : 3 + j, :] = jnp.sum(parts_ref[8 * j : 8 * j + 8, :], axis=0, keepdims=True)
    part_ref[2 + depth : 3 + depth, :] = jnp.sum(last, axis=0, keepdims=True)


SQUARE = 4


def quarter(owner, mask, size):
    other = owner + (mask & 1) * (1 - 2 * (owner % 2)) + (mask & 2) * (1 - 2 * (owner // 2))
    return pl.ds(pl.multiple_of(other * size, size), size)


def part_body(owner_ref, mine_ref, come_ref, *out_refs):
    for mask, out_ref in enumerate(out_refs):
        rows = quarter(owner_ref[0], mask, out_ref.shape[0])
        out_ref[...] = (mine_ref[rows, :].astype(single) + come_ref[rows, :].astype(single)).astype(bfloat)


def sum_of(refs, rows):
    total = refs[0][rows, :].astype(single)
    for ref in refs[1:]:
        total = total + ref[rows, :].astype(single)
    return total


def four_body(*refs):
    refs[-1][...] = sum_of(refs[:-1], slice(None)).astype(bfloat)


def four_two_body(*refs):
    size = refs[-1].shape[0]
    refs[-2][...] = sum_of(refs[:-2], slice(0, size)).astype(bfloat)
    refs[-1][...] = sum_of(refs[:-2], slice(size, 2 * size)).astype(bfloat)


EXTRA = 16


def mark_body(out_ref):
    out_ref[...] = jnp.zeros_like(out_ref)


def add_body(mine_ref, come_ref, out_ref):
    out_ref[...] = mine_ref[...] + come_ref[...]


def four_more_body(small_ref, more_ref, *refs):
    out_ref = refs[-1]
    size = out_ref.shape[0] - EXTRA
    out_ref[:size, :] = sum_of(refs[:-1], slice(None)).astype(bfloat)
    small = small_ref[...] + more_ref[...]
    rest = jnp.zeros((EXTRA - small.shape[0], small.shape[1]), single)
    out_ref[size:, :] = jnp.concatenate([small, rest], axis=0).astype(bfloat)


def gather(owner_ref, pieces, hold):
    for mask, piece in enumerate(pieces):
        hold[quarter(owner_ref[0], mask, piece.shape[0]), :] = piece[...]


def pair_body(a_ref, a_come_ref, b_ref, b_come_ref, out_ref):
    size = a_ref.shape[0]
    out_ref[:size, :] = sum_of((a_ref, a_come_ref), slice(None)).astype(bfloat)
    out_ref[size:, :] = sum_of((b_ref, b_come_ref), slice(None)).astype(bfloat)


def whole_body(owner_ref, a_ref, b_ref, c_ref, d_ref, out_ref, hold):
    gather(owner_ref, (a_ref, b_ref, c_ref, d_ref), hold)
    out_ref[...] = hold[...].astype(single)


def more_body(owner_ref, a_ref, b_ref, c_ref, d_ref, top_ref, end_ref, up_ref, attn_ref, mlp_ref, dwa_ref, hold):
    gather(owner_ref, (a_ref, b_ref, c_ref, d_ref), hold)
    block = hold.shape[0] // SQUARE
    rows = up_ref.shape[0] // SQUARE
    small = jnp.zeros((EXTRA, hold.shape[1]), single)
    for index in range(SQUARE):
        begin = index * block
        target, place = (top_ref, index * rows) if index < SQUARE - 1 else (end_ref, 0)
        target[place : place + rows, :] = hold[begin : begin + rows, :].astype(single)
        small = small + hold[begin + rows : begin + rows + EXTRA, :].astype(single)
        up_ref[index * rows : (index + 1) * rows, :] = hold[begin + rows + EXTRA : begin + block, :].astype(single)
    attn_ref[...] = small[0]
    mlp_ref[...] = small[1]
    for index in range(dwa_ref.shape[0]):
        dwa_ref[index] = jnp.sum(small[2 + index : 3 + index])


def low_body(mine_ref, come_ref, out_ref):
    out_ref[...] = (mine_ref[...].astype(single) + come_ref[...].astype(single)).astype(bfloat)


def mark_body(out_ref):
    out_ref[...] = jnp.zeros_like(out_ref)


def small_body(small_ref, first_ref, out_ref):
    half = small_ref.shape[0]
    rows = first_ref.shape[0] - 2 * half
    come = first_ref[rows:, :].astype(single)
    out_ref[...] = small_ref[...] + (come[:half] + come[half:])


BLOCKS = tuple((begin, min(256, SEQ - begin)) for begin in range(0, SEQ, 256))


def places(core_ref, refs):
    count, size = len(refs) // 2, refs[0].shape[0]
    for index, ref in enumerate(refs):
        core = core_ref[0] if index < count else 1 - core_ref[0]
        yield ref, pl.ds(pl.multiple_of(core * HALF + index % count * size, size), size)


def allowed(size):
    key_pos = lax.broadcasted_iota(jnp.int32, (size, size), 0)
    query_pos = lax.broadcasted_iota(jnp.int32, (size, size), 1)
    return query_pos >= key_pos


def turn(rows, cosine, sine):
    half = rows.shape[0] // 2
    a, b = rows[:half], rows[half:]
    return jnp.concatenate([a * cosine - b * sine, b * cosine + a * sine], axis=0)


KEYS = 128


def fold_top(value):
    top = value[:8]
    for begin in range(8, value.shape[0], 8):
        top = jnp.maximum(top, value[begin : begin + 8])
    return top


def masked(scores, offset):
    key_pos = lax.broadcasted_iota(jnp.int32, scores.shape, 0) + offset
    query_pos = lax.broadcasted_iota(jnp.int32, scores.shape, 1)
    return jnp.where(query_pos >= key_pos, scores, -jnp.inf)


def attend_placed(core_ref, *rest):
    for ref, where in places(core_ref, rest[:4]):
        rest[11][where, :] = ref[...]
    cos_ref, sin_ref, weight_ref, rest = rest[4], rest[5], rest[6], rest[7:]
    attend(weight_ref, cos_ref, sin_ref, *rest)


def attend(weight_ref, cos_ref, sin_ref, qkv_ref, att_ref, nat_ref, log_ref, tokens, all_scores, all_weights):
    width = weight_ref.shape[0] // 3
    projected = mul(weight_ref[...], tokens[...], 1, 1)
    cosine, sine = cos_ref[...], sin_ref[...]
    for part in range(3):
        for head in range(width // DH):
            begin = part * width + head * DH
            rows = projected[begin : begin + DH]
            if part < 2:
                rows = turn(rows, cosine, sine)
            if part == 0:
                rows = rows * DH ** (-0.5)
            qkv_ref[begin : begin + DH, :] = rows.astype(bfloat)
    log_ref[...] = jnp.zeros_like(log_ref)
    heads = range(width // DH)
    keys = [qkv_ref[width + head * DH : width + head * DH + DH, :].T for head in heads]
    for begin, size in BLOCKS:
        end = begin + size
        tops = [None for _ in heads]
        for row in range(0, end, KEYS):
            for head in heads:
                tile = mul(keys[head][row : row + KEYS], qkv_ref[head * DH : head * DH + DH, begin:end])
                if row >= begin:
                    tile = masked(tile, row - begin)
                all_scores[head, row : row + KEYS, :size] = tile
                top = fold_top(tile)
                tops[head] = top if row == 0 else jnp.maximum(tops[head], top)
        tops = [jnp.max(top, axis=0, keepdims=True) for top in tops]
        totals = [jnp.zeros((8, size), single) for _ in heads]
        for row in range(0, end, KEYS):
            for head in heads:
                tile = jnp.exp(all_scores[head, row : row + KEYS, :size] - tops[head])
                totals[head] = totals[head] + fold_rows(tile)
                all_weights[head, row : row + KEYS, :size] = tile.astype(bfloat)
        for head in heads:
            base = head * DH
            total = jnp.sum(totals[head], axis=0, keepdims=True)
            value = qkv_ref[2 * width + base : 2 * width + base + DH, :end]
            mixed = mul(value, all_weights[head, :end, :size]) / total
            att_ref[base : base + DH, begin:end] = mixed.astype(bfloat)
            log_ref[head : head + 1, begin:end] = tops[head] + jnp.log(total)
    nat_ref[...] = att_ref[...].T


def branch_body(core_ref, att_a_ref, att_b_ref, out_a_ref, out_b_ref, pass_ref, keep_ref, *rest):
    send_refs, pass_out = rest[:PARTS], rest[PARTS]
    pass_out[...] = pass_ref[...]
    low = pl.multiple_of(core_ref[0] * HALF, HALF)
    rows = HALF // PARTS
    for index in range(PARTS):
        high = pl.multiple_of((1 - core_ref[0]) * HALF + index * rows, rows)
        send = mul(att_a_ref[pl.ds(high, rows), :], out_a_ref[...])
        send_refs[index][...] = (send + mul(att_b_ref[pl.ds(high, rows), :], out_b_ref[...])).astype(bfloat)
    keep = mul(att_a_ref[pl.ds(low, HALF), :], out_a_ref[...])
    keep_ref[...] = keep + mul(att_b_ref[pl.ds(low, HALF), :], out_b_ref[...])


def attend_back(
    core_ref, log_ref, cos_ref, sin_ref, gain_ref, *rest
):
    before_refs, rest = rest[:-25], rest[-25:]
    grad_refs, x_refs = rest[:2], rest[2:6]
    weight_ref, qkv_weight_ref, qkv_ref, att_ref, small_ref, out_ref, turned_ref = rest[6:13]
    grads, tokens, weight, qkv_weight, qkv, att, turned, result, all_probs, all_scores, hold, marks = rest[13:]
    go = Mover(marks)
    first = go(
        (weight_ref, weight),
        *[(ref, grads.at[where, :]) for ref, where in places(core_ref, grad_refs)],
        (att_ref, att),
        (qkv_ref, qkv),
    )
    later = go(
        *[(ref, tokens.at[where, :]) for ref, where in places(core_ref, x_refs)],
        (qkv_weight_ref, qkv_weight),
    )
    wait(first)
    width = att.shape[0]
    grad_att = mul(weight[...], grads[...], 1, 1).astype(bfloat)
    result[3 * width :, :] = mul(att[...], grads[...]).astype(result.dtype)
    cosine, sine = cos_ref[...], sin_ref[...]
    heads = range(width // DH)
    spans_of = [slice(head * DH, head * DH + DH) for head in heads]
    query = [qkv[span, :] for span in spans_of]
    key = [qkv[width + span.start : width + span.stop, :] for span in spans_of]
    above = [grad_att[span] for span in spans_of]
    centre = [
        jnp.sum(above[head].astype(single) * att[span, :].astype(single), axis=0, keepdims=True)
        for head, span in enumerate(spans_of)
    ]
    keys = [value.T for value in key]
    values = [qkv[2 * width + span.start : 2 * width + span.stop, :].T for span in spans_of]
    queries = [value.T for value in query]
    aboves = [value.T for value in above]
    grad_query = [[] for _ in heads]
    for begin, size in BLOCKS:
        end = begin + size
        for row in range(0, end, KEYS):
            span = slice(row, row + KEYS)
            for head in heads:
                tile = mul(keys[head][span], query[head][:, begin:end])
                if row >= begin:
                    tile = masked(tile, row - begin)
                tile = jnp.exp(tile - log_ref[head : head + 1, begin:end])
                grad = mul(values[head][span], above[head][:, begin:end]) - centre[head][:, begin:end]
                all_probs[head, span, begin:end] = tile.astype(bfloat)
                all_scores[head, span, begin:end] = (tile * grad).astype(bfloat)
        for head in heads:
            grad_query[head].append(mul(key[head][:, :end], all_scores[head, :end, begin:end]))
    grad_key = [[] for _ in heads]
    grad_value = [[] for _ in heads]
    for begin, size in BLOCKS:
        span = slice(begin, begin + size)
        for head in heads:
            grad_key[head].append(mul(all_scores[head, span, begin:], queries[head][begin:]))
            grad_value[head].append(mul(all_probs[head, span, begin:], aboves[head][begin:]))
    for head, span in enumerate(spans_of):
        grad = jnp.concatenate(grad_query[head], axis=1) * DH ** (-0.5)
        turned[span, :] = turn(grad, cosine, -sine).astype(bfloat)
        grad = jnp.concatenate(grad_key[head], axis=0).T
        turned[width + span.start : width + span.stop, :] = turn(grad, cosine, -sine).astype(bfloat)
        grad = jnp.concatenate(grad_value[head], axis=0).T
        turned[2 * width + span.start : 2 * width + span.stop, :] = grad.astype(bfloat)
    stores = go((turned, turned_ref))
    wait(later)
    hold[...] = mul(turned[...], tokens[...])
    result[: 3 * width, :] = hold[...].astype(result.dtype)
    stores += go((result, out_ref))
    part = jnp.zeros((8, hold.shape[1]), single)
    for span in spans(hold.shape[0]):
        part = part + fold_rows(hold[span, :] * qkv_weight[span, :].astype(single))
    gain = jnp.sum(part, axis=0, keepdims=True) / gain_ref[...].reshape(1, -1)
    small_ref[...] = gain + before_refs[0][...] if before_refs else gain
    wait(stores)


def first_grad_body(
    core_ref, turned_a_ref, turned_b_ref, weight_a_ref, weight_b_ref, send_ref, keep_ref,
    turned_a, turned_b, weight_a, weight_b, whole, marks,
):
    low = pl.multiple_of(core_ref[0] * HALF, HALF)
    high = pl.multiple_of((1 - core_ref[0]) * HALF, HALF)
    go = Mover(marks)
    wait(go((turned_a_ref, turned_a), (weight_a_ref, weight_a), (turned_b_ref, turned_b), (weight_b_ref, weight_b)))
    whole[...] = mul(turned_a[...], weight_a[...], 0, 0) + mul(turned_b[...], weight_b[...], 0, 0)
    stores = go((whole.at[pl.ds(low, HALF), :], keep_ref))
    send_ref[...] = whole[pl.ds(high, HALF), :].astype(bfloat)
    wait(stores)


CURVE = float(np.sqrt(2.0 / np.pi))
STEP = 256


def mlp_body(second, *refs):
    if second:
        owner_ref, refs = refs[0], refs[1:]
    x_refs, refs = refs[: 2 * PARTS], refs[2 * PARTS :]
    g_own_ref, g_peer_ref, up_ref, refs = refs[0], refs[1], refs[2], refs[3:]
    if second:
        down_refs, before_refs, up_mine_ref = refs[:SQUARE], refs[SQUARE : SQUARE + 2], refs[SQUARE + 2]
        refs = refs[SQUARE + 3 :]
    else:
        down_ref, refs = refs[0], refs[1:]
    send_norm_ref, keep_norm_ref, active_ref, down_grad_ref = refs[:4]
    if second:
        part_refs, refs = refs[4 : 4 + SQUARE], refs[4 + SQUARE :]
    else:
        up_grad_ref, refs = refs[4], refs[5:]
    x_all, g_all, up, down, active, grad_hidden, x_turned = refs[:7]
    send_norm, keep_norm, down_grad, up_grad, marks = refs[7:12]
    rows, size = x_all.shape[0] // 2, x_all.shape[0] // (2 * PARTS)
    units = down.shape[0]
    go = Mover(marks)
    x_loads = go(*[(x_refs[index], x_all.at[pl.ds(index * size, size), :]) for index in range(2 * PARTS)])
    if second:
        loads = go((up_ref, up), *joined(owner_ref[0], down_refs, down))
    else:
        loads = go((up_ref, up), (down_ref, down))
    loads += go((g_own_ref, g_all.at[pl.ds(0, rows), :]), (g_peer_ref, g_all.at[pl.ds(rows, rows), :]))
    more, mine, stores = [], [], []
    if second:
        (up_mine,) = refs[12:]
        more = go(*zip(before_refs, (send_norm, keep_norm)))
        mine = go((up_mine_ref, up_mine))
    wait(x_loads)
    x_turned[...] = x_all[...].T
    wait(loads)
    for begin in range(0, units, STEP):
        columns = slice(begin, begin + STEP)
        for top in range(0, 2 * rows, rows):
            span = slice(top, top + rows)
            v = mul(x_all[span, :], up[:, columns])
            grad = mul(g_all[span, :], down[columns, :], 1, 1)
            square = v * v
            half = 0.5 + 0.5 * jnp.tanh(v * (CURVE + (CURVE * 0.044715) * square))
            act = v * half
            slope = half + act * (1.0 - half) * (2.0 * CURVE + (6.0 * CURVE * 0.044715) * square)
            active[span, columns] = act.astype(bfloat)
            grad_hidden[span, columns] = (grad * slope).astype(bfloat)

    stores += go((active, active_ref))

    def put(target, value):
        target[...] = (value + target[...].astype(single) if second else value).astype(target.dtype)

    wait(more)
    put(keep_norm, mul(grad_hidden[:rows, :], up[...], 1, 1))
    put(send_norm, mul(grad_hidden[rows:, :], up[...], 1, 1))
    stores += go((keep_norm, keep_norm_ref), (send_norm, send_norm_ref))
    down_grad[...] = mul(active[...], g_all[...], 0, 0).astype(down_grad.dtype)
    stores += go((down_grad, down_grad_ref))
    up_grad[...] = mul(x_turned[...], grad_hidden[...]).astype(bfloat)
    if second:
        wait(mine)
        part = up_grad.shape[0] // SQUARE
        for mask, part_ref in enumerate(part_refs):
            rows_of = quarter(owner_ref[0], mask, part)
            stores += go(
                (up_mine.at[rows_of, :], part_ref.at[pl.ds(0, part), :]),
                (up_grad.at[rows_of, :], part_ref.at[pl.ds(part, part), :]),
            )
    else:
        stores += go((up_grad, up_grad_ref))
    wait(stores)


def outputs_body(owner_ref, active_a_ref, down_a_ref, active_b_ref, *rest):
    down_b_refs, keep_ref, send_ref = rest[:SQUARE], rest[SQUARE], rest[SQUARE + 1]
    active_a, down_a, active_b, down_b, marks = rest[SQUARE + 2 :]
    go = Mover(marks)
    wait(
        go(
            (active_a_ref, active_a),
            (down_a_ref, down_a),
            (active_b_ref, active_b),
            *joined(owner_ref[0], down_b_refs, down_b),
        )
    )
    rows = keep_ref.shape[0]
    send = mul(active_a[rows:, :], down_a[...]) + mul(active_b[rows:, :], down_b[...])
    send_ref[...] = send.astype(bfloat)
    keep_ref[...] = mul(active_a[:rows, :], down_a[...]) + mul(active_b[:rows, :], down_b[...])


def mlp(x_own, x_peer, g_own, g_peer, up, down, upper=(), before=(), flops=0):
    rows, width = g_own.shape
    units = sum(piece.shape[0] for piece in down)
    tall = (2 * rows, width)
    pair = [((rows, width), bfloat), ((rows, width), single)]
    outs = pair + [((2 * rows, units), bfloat), ((units, width), bfloat)]
    outs += [((2 * width // SQUARE, units), bfloat)] * SQUARE if before else [((width, units), bfloat)]
    scratch = [
        pltpu.VMEM(tall, bfloat),
        pltpu.VMEM(tall, bfloat),
        pltpu.VMEM((width, units), bfloat),
        pltpu.VMEM((units, width), bfloat),
        pltpu.VMEM((2 * rows, units), bfloat),
        pltpu.VMEM((2 * rows, units), bfloat),
        pltpu.VMEM((width, 2 * rows), bfloat),
    ]
    scratch += [pltpu.VMEM(shape, kind) for shape, kind in pair]
    scratch += [
        pltpu.VMEM((units, width), bfloat), pltpu.VMEM((width, units), bfloat), pltpu.SemaphoreType.DMA((32,)),
    ]
    if before:
        scratch.append(pltpu.VMEM((width, units), bfloat))
    operands = (*upper, *x_own, *x_peer, g_own, g_peer, *up, *down, *before)
    return call(
        functools.partial(mlp_body, bool(before)),
        outs,
        operands,
        scratch,
        len(upper),
        vmem=60,
        flops=flops,
        far=len(operands) - len(upper),
        far_outs=len(outs),
    )


def shards(
    inputs,
    history,
    cotangent,
    qkv_weight,
    out_weight,
    up_weight,
    down_weight,
    gain_attn,
    gain_mlp,
    dwa_weights,
):
    rows, width = inputs.shape
    members = lax.axis_size("mp")
    copies = lax.axis_size("dp")
    bits = copies.bit_length() - 1
    core = lax.rem(lax.axis_index("mp"), 2).astype(jnp.int32).reshape(1)
    copy_index = lax.axis_index("dp").astype(jnp.int32).reshape(1)
    core_pairs = [(i, i ^ 1) for i in range(members)]
    chip_pairs = [(i, i ^ 2) for i in range(members)]
    depth = history.shape[0]
    part = out_weight.shape[0]

    def other_core(value):
        return lax.ppermute(value, "mp", core_pairs)

    def other_chip(value):
        return lax.ppermute(value, "mp", chip_pairs)

    def other_copy(value, mask):
        return lax.ppermute(value, "dp", [(i, i ^ mask) for i in range(copies)])

    owner = copy_index & (SQUARE - 1)
    cosine, sine = (jnp.asarray(table) for table in tables())

    qkv_own = qkv_weight.transpose(1, 2, 0).reshape(3 * part, width)
    fourth = (width // SQUARE, width)
    square = (width, width)
    masks = range(1, SQUARE)
    marks = pltpu.SemaphoreType.DMA((16,))
    (down_quarter,) = call(
        split_body,
        [(fourth, bfloat)],
        (owner, down_weight),
        [pltpu.VMEM(fourth, bfloat), marks],
        1,
        vmem=60,
        far=1,
        far_outs=1,
    )
    qkv_peer, out_peer = other_chip(qkv_own), other_chip(out_weight)
    down_come, up_peer = other_chip(down_quarter), other_chip(up_weight)

    full = (rows, width)
    x_own = call(norm_body, [((rows // 2, width), bfloat)] * 2, (inputs, gain_attn), after=(down_quarter,))
    x_peer = [other_core(value) for value in x_own]
    tall = (SEQ, width)
    tokens = pltpu.VMEM(tall, bfloat)
    first_outs = [
        ((3 * part, SEQ), bfloat), ((part, SEQ), bfloat), ((SEQ, part), bfloat), ((8, SEQ), single),
    ]
    heads = part // DH
    tiles = [tokens, pltpu.VMEM((heads, SEQ, 256), single), pltpu.VMEM((heads, SEQ, 256), bfloat)]
    qkv_a, att_a, nat_a, log_a = call(
        attend_placed, first_outs, (core, *x_own, *x_peer, cosine, sine, qkv_own), tiles, 1, vmem=32
    )
    history_grad, mixed, g_own, history_parts = average_history(dwa_weights, history, cotangent, (log_a,))
    g_peer = other_core(g_own)
    qkv_b, att_b, nat_b, log_b = call(
        attend_placed,
        first_outs,
        (core, *x_own, *x_peer, cosine, sine, qkv_peer),
        tiles,
        1,
        (history_parts,),
        32,
        MUCH,
    )
    third = (rows // PARTS, width)
    keep, *send, down_copy = call(
        branch_body,
        [(full, single)] + [(third, bfloat)] * PARTS + [(fourth, bfloat)],
        (core, nat_a, nat_b, out_weight, out_peer, down_come),
        (),
        1,
        (g_peer,),
    )
    down_pieces = [down_come] + [other_copy(down_copy, mask) for mask in masks]
    recv = [other_core(value) for value in send]
    middle, *y_own = call(
        middle_body, [(full, single)] + [(third, bfloat)] * PARTS, (inputs, keep, gain_mlp, *recv)
    )
    y_peer = [other_core(value) for value in y_own]

    first = mlp(y_own, y_peer, g_own, g_peer, (up_weight,), (down_weight,))
    active_a, down_mine, up_mine = first[2:]
    second = mlp(
        y_own, y_peer, g_own, g_peer, (up_peer,), down_pieces, (owner,), (*first[:2], up_mine)
    )
    send_norm, keep_norm, active_b, down_theirs = second[:4]
    token = [send_norm]

    def step(body, outs, operands, scratch=(), scalars=0, vmem=16, flops=MUCH, far=0, far_outs=0):
        results = call(body, outs, operands, scratch, scalars, tuple(token), vmem, flops, far, far_outs)
        token[0] = results[0]
        return results

    down_come = other_chip(down_theirs)
    up_parts = [second[4]] + [other_copy(value, mask) for mask, value in zip(masks, second[5:])]
    step(mark_body, [((8, 128), single)], ())
    grad_middle, gb_own, gain_mlp_part = step(
        middle_back_body,
        [(full, single), (full, bfloat), ((1, width), single)],
        (dwa_weights, middle, keep_norm, other_core(send_norm), cotangent, gain_mlp),
        scalars=1,
        flops=0,
    )
    gb_peer = other_core(gb_own)
    step(mark_body, [((8, 128), single)], ())
    def back(weight, qkv_weight, qkv, att, log, flops, before=()):
        return step(
            attend_back,
            [
                ((1, width), single),
                ((4 * part, width), bfloat),
                ((3 * part, SEQ), bfloat),
            ],
            (
                core, log, cosine, sine, gain_attn, *before, gb_own, gb_peer, *x_own, *x_peer, weight, qkv_weight, qkv,
                att,
            ),
            [
                pltpu.VMEM(tall, bfloat),
                pltpu.VMEM(tall, bfloat),
                pltpu.VMEM((part, width), bfloat),
                pltpu.VMEM((3 * part, width), bfloat),
                pltpu.VMEM((3 * part, SEQ), bfloat),
                pltpu.VMEM((part, SEQ), bfloat),
                pltpu.VMEM((3 * part, SEQ), bfloat),
                pltpu.VMEM((4 * part, width), bfloat),
                pltpu.VMEM((heads, SEQ, SEQ), bfloat),
                pltpu.VMEM((heads, SEQ, SEQ), bfloat),
                pltpu.VMEM((3 * part, width), single),
                marks,
            ],
            1,
            60,
            flops,
            10,
            2,
        )

    gain_part, att_theirs, turned_b = back(out_peer, qkv_peer, qkv_b, att_b, log_b, 0)
    att_come = other_chip(att_theirs)
    def spread(mine, come, flops=MUCH):
        own, *sent = step(part_body, [(fourth, bfloat)] * SQUARE, (owner, mine, come), scalars=1, flops=flops)
        return [own] + [other_copy(value, mask) for mask, value in zip(masks, sent)]

    down_parts = spread(down_mine, down_come, 0)
    up, sent = step(four_two_body, [(fourth, bfloat)] * 2, up_parts, flops=0)
    up_come = other_chip(sent)
    gain_part, att_mine, turned_a = back(
        out_weight, qkv_own, qkv_a, att_a, log_a, MUCH, (gain_part,)
    )

    def exchange(value):
        for bit in range(2, bits):
            come = other_copy(value, 1 << bit)
            if bit < bits - 1:
                (value,) = step(low_body, [(value.shape, bfloat)], (value, come))
        return value, come

    def finish(value, come):
        (value,) = step(low_body, [(value.shape, bfloat)], (value, come), flops=COST)
        return [value] + [other_copy(value, mask) for mask in masks]

    (down,) = step(four_body, [(fourth, bfloat)], down_parts, flops=COST)
    down = exchange(down)
    att_parts = spread(att_mine, att_come, COST)
    (up,) = step(low_body, [(fourth, bfloat)], (up, up_come), flops=COST)
    up = exchange(up)
    def gate():
        step(mark_body, [((8, 128), single)], (), flops=COST)

    keep_out, send_out = step(
        outputs_body,
        [(full, single), (full, bfloat)],
        (owner, active_a, down_weight, active_b, *down_pieces),
        [pltpu.VMEM(tall, bfloat), pltpu.VMEM(square, bfloat)] * 2 + [marks],
        1,
        60,
        COST,
        7,
    )
    out_come = other_core(send_out)
    token.append(down[1])
    gate()
    del token[1:]
    combined, part_sums = step(
        combine_body,
        [(full, bfloat), ((depth + 3, width), single)],
        (dwa_weights, mixed, middle, keep_out, out_come, cotangent, history_parts, gain_part, gain_mlp_part),
        scalars=1,
        flops=COST,
    )
    core_sums = other_core(part_sums)
    gate()
    (part_sums,) = step(add_body, [(part_sums.shape, single)], (part_sums, core_sums), flops=COST)
    more_sums = other_chip(part_sums)
    gate()
    block = (width // SQUARE + EXTRA, width)
    (att,) = step(four_more_body, [(block, bfloat)], (part_sums, more_sums, *att_parts), flops=COST)
    att = exchange(att)
    down = finish(*down)
    token += down[1:]
    pair = (block[0] + fourth[0], width)
    (both,) = step(pair_body, [(pair, bfloat)], (*att, *up), flops=COST)
    del token[1:]
    both = [both] + [other_copy(both, mask) for mask in masks]
    send_first, keep_first = step(
        first_grad_body,
        [(full, bfloat), (full, single)],
        (core, turned_a, turned_b, qkv_own, qkv_peer),
        [pltpu.VMEM((3 * part, SEQ), bfloat)] * 2
        + [pltpu.VMEM((3 * part, width), bfloat)] * 2
        + [pltpu.VMEM(tall, single), marks],
        1,
        30,
        COST,
        4,
        1,
    )
    first_come = other_core(send_first)
    (down_grad,) = step(
        whole_body, [(square, single)], (owner, *down), [pltpu.VMEM(square, bfloat)], 1, flops=COST
    )
    (input_grad,) = step(
        first_back_body,
        [(full, bfloat)],
        (inputs, keep_first, first_come, grad_middle, gain_attn),
        vmem=16,
        flops=COST,
    )
    qkv_grad, out_grad, up_grad, gain_attn_grad, gain_mlp_grad, dwa_grad = step(
        more_body,
        [
            ((3 * part, width), single),
            ((part, width), single),
            (square, single),
            ((width,), single),
            ((width,), single),
            ((depth + 1,), single, "scalars"),
        ],
        (owner, *both),
        [pltpu.VMEM((SQUARE * pair[0], width), bfloat)],
        1,
        flops=COST,
    )

    return (
        combined,
        input_grad,
        history_grad,
        qkv_grad.reshape(3, part, width).transpose(2, 0, 1),
        out_grad,
        up_grad,
        down_grad,
        gain_attn_grad,
        gain_mlp_grad,
        dwa_grad,
    )


def solution(mesh):
    placed = (
        P(("dp", "mp"), None),
        P(None, ("dp", "mp"), None),
        P(("dp", "mp"), None),
        P(None, None, "mp"),
        P("mp", None),
        P(None, "mp"),
        P("mp", None),
        P(),
        P(),
        P(),
    )
    return jax.shard_map(
        shards,
        mesh=mesh,
        in_specs=placed,
        out_specs=(
            P(("dp", "mp"), None),
            P(("dp", "mp"), None),
            P(None, ("dp", "mp"), None),
            P(None, None, "mp"),
            P("mp", None),
            P(None, "mp"),
            P("mp", None),
            P(),
            P(),
            P(),
        ),
        check_vma=False,
    )
```

```python
import functools

import jax
import jax.numpy as jnp
import numpy as np
from jax import lax
from jax.experimental import pallas as pl
from jax.experimental.pallas import tpu as pltpu
from jax.sharding import PartitionSpec as P

DH = 64
SEQ = 1152
HALF = SEQ // 2
EPS = 1e-05
bfloat = jnp.bfloat16
single = jnp.float32
MIB = 1 << 20
MUCH = 10**11
COST = 10**10


def tables():
    half_width = DH // 2
    places = np.arange(SEQ, dtype=np.float32)
    frequency = np.float32(10000.0) ** (-np.arange(half_width, dtype=np.float32) * np.float32(2.0 / DH))
    angles = frequency[:, None] * places[None, :]
    return (np.cos(angles).astype(np.float32), np.sin(angles).astype(np.float32))


def mul(a, b, ca=1, cb=0):
    return lax.dot_general(a, b, (((ca,), (cb,)), ((), ())), preferred_element_type=single)


def call(kernel, outs, operands, scratch=(), scalars=0, after=(), vmem=16, flops=0, far=0, far_outs=0):
    count, waits = len(operands), len(after)

    def body(*refs):
        kernel(*refs[:count], *refs[count + waits :])

    small = pl.BlockSpec(memory_space=pltpu.SMEM)
    whole = pl.BlockSpec(memory_space=pltpu.VMEM)
    apart = pl.BlockSpec(memory_space=pltpu.HBM)
    loose = pl.BlockSpec(memory_space=pl.ANY)
    inner = len(outs) - far_outs
    return pl.pallas_call(
        body,
        out_shape=[jax.ShapeDtypeStruct(out[0], out[1]) for out in outs],
        in_specs=[small] * scalars + [whole] * (count - scalars - far) + [apart] * far + [loose] * waits,
        out_specs=[small if len(out) > 2 else whole for out in outs[:inner]] + [apart] * far_outs,
        scratch_shapes=list(scratch),
        compiler_params=pltpu.CompilerParams(vmem_limit_bytes=vmem * MIB),
        cost_estimate=pl.CostEstimate(flops=flops, bytes_accessed=0, transcendentals=0),
    )(*operands, *after)


class Mover:
    def __init__(self, marks):
        self.marks = marks
        self.used = 0

    def __call__(self, *pairs):
        copies = []
        for source, target in pairs:
            copies.append(pltpu.make_async_copy(source, target, self.marks.at[self.used]))
            self.used += 1
        for copy in copies:
            copy.start()
        return copies


def wait(copies):
    for copy in copies:
        copy.wait()


ROWS = 64
PARTS = 3


def spans(rows, step=ROWS):
    return [slice(begin, begin + step) for begin in range(0, rows, step)]


def normal_of(x):
    centre = x - jnp.mean(x, axis=-1, keepdims=True)
    spread = jnp.mean(centre * centre, axis=-1, keepdims=True)
    scale = lax.rsqrt(spread + EPS)
    return centre * scale, scale


def split_body(owner_ref, in_ref, out_ref, hold, marks):
    go = Mover(marks)
    wait(go((in_ref.at[quarter(owner_ref[0], 0, hold.shape[0]), :], hold)))
    wait(go((hold, out_ref)))


def joined(owner, refs, target):
    size = refs[0].shape[0]
    return [(ref, target.at[quarter(owner, mask, size), :]) for mask, ref in enumerate(refs)]


def norm_body(x_ref, gain_ref, *out_refs):
    gain = gain_ref[...].reshape(1, -1)
    for index, out_ref in enumerate(out_refs):
        rows = out_ref.shape[0]
        for span in spans(rows, rows // 6):
            here = slice(index * rows + span.start, index * rows + span.stop)
            normal, _ = normal_of(x_ref[here, :].astype(single))
            out_ref[span, :] = (normal * gain).astype(bfloat)


def middle_body(x_ref, keep_ref, gain_ref, *rest):
    recv_refs, mid_ref, out_refs = rest[:PARTS], rest[PARTS], rest[PARTS + 1 :]
    gain = gain_ref[...].reshape(1, -1)
    rows = x_ref.shape[0] // PARTS
    for index in range(PARTS):
        for span in spans(rows):
            here = slice(index * rows + span.start, index * rows + span.stop)
            recv = recv_refs[index][span, :].astype(single)
            x = x_ref[here, :].astype(single) + (keep_ref[here, :] + recv)
            mid_ref[here, :] = x
            normal, _ = normal_of(x)
            out_refs[index][span, :] = (normal * gain).astype(bfloat)


def norm_back(x, grad, gain):
    normal, scale = normal_of(x)
    lifted = grad * gain
    back = scale * (
        lifted
        - jnp.mean(lifted, axis=-1, keepdims=True)
        - normal * jnp.mean(lifted * normal, axis=-1, keepdims=True)
    )
    return back, normal


def fold_rows(value):
    total = value[:8]
    for begin in range(8, value.shape[0], 8):
        total = total + value[begin : begin + 8]
    return total


def middle_back_body(mix_ref, x_ref, keep_ref, recv_ref, cot_ref, gain_ref, mid_ref, low_ref, part_ref):
    gain = gain_ref[...].reshape(1, -1)
    part = jnp.zeros((8, x_ref.shape[1]), single)
    for span in spans(x_ref.shape[0]):
        grad = keep_ref[span, :] + recv_ref[span, :].astype(single)
        back, normal = norm_back(x_ref[span, :], grad, gain)
        total = mix_ref[mix_ref.shape[0] - 1] * cot_ref[span, :] + back
        mid_ref[span, :] = total
        low_ref[span, :] = total.astype(bfloat)
        part = part + fold_rows(grad * normal)
    part_ref[...] = jnp.sum(part, axis=0, keepdims=True)


def first_back_body(x_ref, keep_ref, recv_ref, mid_ref, gain_ref, out_ref):
    gain = gain_ref[...].reshape(1, -1)
    for span in spans(x_ref.shape[0]):
        grad = keep_ref[span, :] + recv_ref[span, :].astype(single)
        back, _ = norm_back(x_ref[span, :].astype(single), grad, gain)
        out_ref[span, :] = (mid_ref[span, :] + back).astype(bfloat)


def history_body(mix_ref, history_ref, cot_ref, grad_ref, mixed_ref, low_ref, part_ref):
    depth = history_ref.shape[0]

    @pl.when(pl.program_id(0) == 0)
    def _():
        part_ref[...] = jnp.zeros_like(part_ref)

    for span in spans(cot_ref.shape[0], 32):
        cot = cot_ref[span, :]
        low_ref[span, :] = (mix_ref[depth] * cot).astype(bfloat)
        mixed = None
        for j in range(depth):
            layer = history_ref[j, span, :].astype(single)
            mixed = mix_ref[j] * layer if mixed is None else mixed + mix_ref[j] * layer
            grad_ref[j, span, :] = (mix_ref[j] * cot).astype(bfloat)
            part_ref[8 * j : 8 * j + 8, :] += fold_rows(layer * cot)
        mixed_ref[span, :] = mixed


def average_history(mix, history, cot, after=()):
    depth, rows, width = history.shape
    step = 96
    waits = len(after)

    def body(*refs):
        history_body(*refs[:3], *refs[3 + waits :])

    row_block = pl.BlockSpec((step, width), lambda i: (i, 0))
    deep_block = pl.BlockSpec((depth, step, width), lambda i: (0, i, 0))
    return pl.pallas_call(
        body,
        grid=(rows // step,),
        out_shape=[
            jax.ShapeDtypeStruct(history.shape, bfloat),
            jax.ShapeDtypeStruct((rows, width), single),
            jax.ShapeDtypeStruct((rows, width), bfloat),
            jax.ShapeDtypeStruct((8 * depth, width), single),
        ],
        in_specs=[pl.BlockSpec(memory_space=pltpu.SMEM), deep_block, row_block]
        + [pl.BlockSpec(memory_space=pl.ANY)] * waits,
        out_specs=[deep_block, row_block, row_block, pl.BlockSpec((8 * depth, width), lambda i: (0, 0))],
        compiler_params=pltpu.CompilerParams(vmem_limit_bytes=16 * MIB),
        cost_estimate=pl.CostEstimate(flops=0, bytes_accessed=0, transcendentals=0),
    )(mix, history, cot, *after)


def combine_body(mix_ref, mixed_ref, mid_ref, keep_ref, recv_ref, cot_ref, parts_ref, out_ref, part_ref):
    depth = mix_ref.shape[0] - 1
    last = jnp.zeros((8, mid_ref.shape[1]), single)
    for span in spans(mid_ref.shape[0]):
        outputs = mid_ref[span, :] + (keep_ref[span, :] + recv_ref[span, :].astype(single))
        out_ref[span, :] = (mixed_ref[span, :] + mix_ref[depth] * outputs).astype(bfloat)
        last = last + fold_rows(outputs * cot_ref[span, :])
    for j in range(depth):
        part_ref[j : j + 1, :] = jnp.sum(parts_ref[8 * j : 8 * j + 8, :], axis=0, keepdims=True)
    part_ref[depth : depth + 1, :] = jnp.sum(last, axis=0, keepdims=True)


SQUARE = 4


def quarter(owner, mask, size):
    other = owner + (mask & 1) * (1 - 2 * (owner % 2)) + (mask & 2) * (1 - 2 * (owner // 2))
    return pl.ds(pl.multiple_of(other * size, size), size)


def part_body(owner_ref, mine_ref, come_ref, *out_refs):
    for mask, out_ref in enumerate(out_refs):
        rows = quarter(owner_ref[0], mask, out_ref.shape[0])
        out_ref[...] = (mine_ref[rows, :].astype(single) + come_ref[rows, :].astype(single)).astype(bfloat)


def sum_of(refs, rows):
    total = refs[0][rows, :].astype(single)
    for ref in refs[1:]:
        total = total + ref[rows, :].astype(single)
    return total


def four_body(*refs):
    refs[-1][...] = sum_of(refs[:-1], slice(None)).astype(bfloat)


def four_two_body(*refs):
    size = refs[-1].shape[0]
    refs[-2][...] = sum_of(refs[:-2], slice(0, size)).astype(bfloat)
    refs[-1][...] = sum_of(refs[:-2], slice(size, 2 * size)).astype(bfloat)


EXTRA = 16


def mark_body(out_ref):
    out_ref[...] = jnp.zeros_like(out_ref)


def small_body(small_ref, first_ref, out_ref):
    half = small_ref.shape[0]
    rows = first_ref.shape[0] - 2 * half
    come = first_ref[rows:, :].astype(single)
    out_ref[...] = small_ref[...] + (come[:half] + come[half:])


def four_more_body(small_ref, more_ref, *refs):
    out_ref = refs[-1]
    size = out_ref.shape[0] - EXTRA
    out_ref[:size, :] = sum_of(refs[:-1], slice(None)).astype(bfloat)
    small = small_ref[...] + more_ref[...]
    rest = jnp.zeros((EXTRA - small.shape[0], small.shape[1]), single)
    out_ref[size:, :] = jnp.concatenate([small, rest], axis=0).astype(bfloat)


def gather(owner_ref, pieces, hold):
    for mask, piece in enumerate(pieces):
        hold[quarter(owner_ref[0], mask, piece.shape[0]), :] = piece[...]


def pair_body(a_ref, a_come_ref, b_ref, b_come_ref, out_ref):
    size = a_ref.shape[0]
    out_ref[:size, :] = sum_of((a_ref, a_come_ref), slice(None)).astype(bfloat)
    out_ref[size:, :] = sum_of((b_ref, b_come_ref), slice(None)).astype(bfloat)


def whole_body(owner_ref, a_ref, b_ref, c_ref, d_ref, out_ref, hold, full, marks):
    gather(owner_ref, (a_ref, b_ref, c_ref, d_ref), hold)
    go, stores = Mover(marks), []
    size = hold.shape[0] // SQUARE
    for index in range(SQUARE):
        rows = pl.ds(index * size, size)
        full[rows, :] = hold[rows, :].astype(single)
        stores += go((full.at[rows, :], out_ref.at[rows, :]))
    wait(stores)


def more_body(
    owner_ref, a_ref, b_ref, c_ref, d_ref, attn_ref, mlp_ref, dwa_ref, top_ref, end_ref, up_ref, hold, att, up, marks
):
    gather(owner_ref, (a_ref, b_ref, c_ref, d_ref), hold)
    go, stores = Mover(marks), []
    block = hold.shape[0] // SQUARE
    size = up.shape[0] // SQUARE
    small = jnp.zeros((EXTRA, hold.shape[1]), single)
    for index in range(SQUARE):
        begin = index * block
        rows = pl.ds(index * size, size)
        att[rows, :] = hold[begin : begin + size, :].astype(single)
        stores += go((att.at[rows, :], top_ref.at[rows, :] if index < SQUARE - 1 else end_ref))
        small = small + hold[begin + size : begin + size + EXTRA, :].astype(single)
        up[rows, :] = hold[begin + size + EXTRA : begin + block, :].astype(single)
        stores += go((up.at[rows, :], up_ref.at[rows, :]))
    attn_ref[...] = small[0]
    mlp_ref[...] = small[1]
    for index in range(dwa_ref.shape[0]):
        dwa_ref[index] = jnp.sum(small[2 + index : 3 + index])
    wait(stores)


def low_body(mine_ref, come_ref, out_ref):
    out_ref[...] = (mine_ref[...].astype(single) + come_ref[...].astype(single)).astype(bfloat)


def mark_body(out_ref):
    out_ref[...] = jnp.zeros_like(out_ref)


def small_body(small_ref, first_ref, out_ref):
    half = small_ref.shape[0]
    rows = first_ref.shape[0] - 2 * half
    come = first_ref[rows:, :].astype(single)
    out_ref[...] = small_ref[...] + (come[:half] + come[half:])


BLOCKS = tuple((begin, min(256, SEQ - begin)) for begin in range(0, SEQ, 256))


def places(core_ref, refs):
    count, size = len(refs) // 2, refs[0].shape[0]
    for index, ref in enumerate(refs):
        core = core_ref[0] if index < count else 1 - core_ref[0]
        yield ref, pl.ds(pl.multiple_of(core * HALF + index % count * size, size), size)


def allowed(size):
    key_pos = lax.broadcasted_iota(jnp.int32, (size, size), 0)
    query_pos = lax.broadcasted_iota(jnp.int32, (size, size), 1)
    return query_pos >= key_pos


def turn(rows, cosine, sine):
    half = rows.shape[0] // 2
    a, b = rows[:half], rows[half:]
    return jnp.concatenate([a * cosine - b * sine, b * cosine + a * sine], axis=0)


KEYS = 128


def fold_top(value):
    top = value[:8]
    for begin in range(8, value.shape[0], 8):
        top = jnp.maximum(top, value[begin : begin + 8])
    return top


def masked(scores, offset):
    key_pos = lax.broadcasted_iota(jnp.int32, scores.shape, 0) + offset
    query_pos = lax.broadcasted_iota(jnp.int32, scores.shape, 1)
    return jnp.where(query_pos >= key_pos, scores, -jnp.inf)


def attend_placed(core_ref, *rest):
    for ref, where in places(core_ref, rest[:4]):
        rest[11][where, :] = ref[...]
    cos_ref, sin_ref, weight_ref, rest = rest[4], rest[5], rest[6], rest[7:]
    attend(weight_ref, cos_ref, sin_ref, *rest)


def attend(weight_ref, cos_ref, sin_ref, qkv_ref, att_ref, nat_ref, log_ref, tokens, all_scores, all_weights):
    width = weight_ref.shape[0] // 3
    projected = mul(weight_ref[...], tokens[...], 1, 1)
    cosine, sine = cos_ref[...], sin_ref[...]
    for part in range(3):
        for head in range(width // DH):
            begin = part * width + head * DH
            rows = projected[begin : begin + DH]
            if part < 2:
                rows = turn(rows, cosine, sine)
            if part == 0:
                rows = rows * DH ** (-0.5)
            qkv_ref[begin : begin + DH, :] = rows.astype(bfloat)
    log_ref[...] = jnp.zeros_like(log_ref)
    heads = range(width // DH)
    keys = [qkv_ref[width + head * DH : width + head * DH + DH, :].T for head in heads]
    for begin, size in BLOCKS:
        end = begin + size
        tops = [None for _ in heads]
        for row in range(0, end, KEYS):
            for head in heads:
                tile = mul(keys[head][row : row + KEYS], qkv_ref[head * DH : head * DH + DH, begin:end])
                if row >= begin:
                    tile = masked(tile, row - begin)
                all_scores[head, row : row + KEYS, :size] = tile
                top = fold_top(tile)
                tops[head] = top if row == 0 else jnp.maximum(tops[head], top)
        tops = [jnp.max(top, axis=0, keepdims=True) for top in tops]
        totals = [jnp.zeros((8, size), single) for _ in heads]
        for row in range(0, end, KEYS):
            for head in heads:
                tile = jnp.exp(all_scores[head, row : row + KEYS, :size] - tops[head])
                totals[head] = totals[head] + fold_rows(tile)
                all_weights[head, row : row + KEYS, :size] = tile.astype(bfloat)
        for head in heads:
            base = head * DH
            total = jnp.sum(totals[head], axis=0, keepdims=True)
            value = qkv_ref[2 * width + base : 2 * width + base + DH, :end]
            mixed = mul(value, all_weights[head, :end, :size]) / total
            att_ref[base : base + DH, begin:end] = mixed.astype(bfloat)
            log_ref[head : head + 1, begin:end] = tops[head] + jnp.log(total)
    nat_ref[...] = att_ref[...].T


def branch_body(core_ref, att_a_ref, att_b_ref, out_a_ref, out_b_ref, pass_ref, keep_ref, *rest):
    send_refs, pass_out = rest[:PARTS], rest[PARTS]
    pass_out[...] = pass_ref[...]
    low = pl.multiple_of(core_ref[0] * HALF, HALF)
    rows = HALF // PARTS
    for index in range(PARTS):
        high = pl.multiple_of((1 - core_ref[0]) * HALF + index * rows, rows)
        send = mul(att_a_ref[pl.ds(high, rows), :], out_a_ref[...])
        send_refs[index][...] = (send + mul(att_b_ref[pl.ds(high, rows), :], out_b_ref[...])).astype(bfloat)
    keep = mul(att_a_ref[pl.ds(low, HALF), :], out_a_ref[...])
    keep_ref[...] = keep + mul(att_b_ref[pl.ds(low, HALF), :], out_b_ref[...])


def attend_back(
    core_ref, log_ref, cos_ref, sin_ref, gain_ref, *rest
):
    before_refs, rest = rest[:-25], rest[-25:]
    grad_refs, x_refs = rest[:2], rest[2:6]
    weight_ref, qkv_weight_ref, qkv_ref, att_ref, small_ref, out_ref, turned_ref = rest[6:13]
    grads, tokens, weight, qkv_weight, qkv, att, turned, result, all_probs, all_scores, hold, marks = rest[13:]
    go = Mover(marks)
    first = go(
        (weight_ref, weight),
        *[(ref, grads.at[where, :]) for ref, where in places(core_ref, grad_refs)],
        (att_ref, att),
        (qkv_ref, qkv),
    )
    later = go(
        *[(ref, tokens.at[where, :]) for ref, where in places(core_ref, x_refs)],
        (qkv_weight_ref, qkv_weight),
    )
    wait(first)
    width = att.shape[0]
    grad_att = mul(weight[...], grads[...], 1, 1).astype(bfloat)
    result[3 * width :, :] = mul(att[...], grads[...]).astype(result.dtype)
    cosine, sine = cos_ref[...], sin_ref[...]
    heads = range(width // DH)
    spans_of = [slice(head * DH, head * DH + DH) for head in heads]
    query = [qkv[span, :] for span in spans_of]
    key = [qkv[width + span.start : width + span.stop, :] for span in spans_of]
    above = [grad_att[span] for span in spans_of]
    centre = [
        jnp.sum(above[head].astype(single) * att[span, :].astype(single), axis=0, keepdims=True)
        for head, span in enumerate(spans_of)
    ]
    keys = [value.T for value in key]
    values = [qkv[2 * width + span.start : 2 * width + span.stop, :].T for span in spans_of]
    queries = [value.T for value in query]
    aboves = [value.T for value in above]
    grad_query = [[] for _ in heads]
    for begin, size in BLOCKS:
        end = begin + size
        for row in range(0, end, KEYS):
            span = slice(row, row + KEYS)
            for head in heads:
                tile = mul(keys[head][span], query[head][:, begin:end])
                if row >= begin:
                    tile = masked(tile, row - begin)
                tile = jnp.exp(tile - log_ref[head : head + 1, begin:end])
                grad = mul(values[head][span], above[head][:, begin:end]) - centre[head][:, begin:end]
                all_probs[head, span, begin:end] = tile.astype(bfloat)
                all_scores[head, span, begin:end] = (tile * grad).astype(bfloat)
        for head in heads:
            grad_query[head].append(mul(key[head][:, :end], all_scores[head, :end, begin:end]))
    grad_key = [[] for _ in heads]
    grad_value = [[] for _ in heads]
    for begin, size in BLOCKS:
        span = slice(begin, begin + size)
        for head in heads:
            grad_key[head].append(mul(all_scores[head, span, begin:], queries[head][begin:]))
            grad_value[head].append(mul(all_probs[head, span, begin:], aboves[head][begin:]))
    for head, span in enumerate(spans_of):
        grad = jnp.concatenate(grad_query[head], axis=1) * DH ** (-0.5)
        turned[span, :] = turn(grad, cosine, -sine).astype(bfloat)
        grad = jnp.concatenate(grad_key[head], axis=0).T
        turned[width + span.start : width + span.stop, :] = turn(grad, cosine, -sine).astype(bfloat)
        grad = jnp.concatenate(grad_value[head], axis=0).T
        turned[2 * width + span.start : 2 * width + span.stop, :] = grad.astype(bfloat)
    stores = go((turned, turned_ref))
    wait(later)
    hold[...] = mul(turned[...], tokens[...])
    result[: 3 * width, :] = hold[...].astype(result.dtype)
    stores += go((result, out_ref))
    part = jnp.zeros((8, hold.shape[1]), single)
    for span in spans(hold.shape[0]):
        part = part + fold_rows(hold[span, :] * qkv_weight[span, :].astype(single))
    gain = jnp.sum(part, axis=0, keepdims=True) / gain_ref[...].reshape(1, -1)
    if before_refs:
        gain_part_ref, mlp_part_ref, dwa_part_ref = before_refs
        small_ref[:1, :] = gain + gain_part_ref[...]
        small_ref[1:2, :] = mlp_part_ref[...]
        small_ref[2:, :] = dwa_part_ref[...]
    else:
        small_ref[...] = gain
    wait(stores)


def first_grad_body(
    core_ref, small_ref, turned_a_ref, turned_b_ref, weight_a_ref, weight_b_ref, send_ref, keep_ref,
    turned_a, turned_b, weight_a, weight_b, whole, marks,
):
    low = pl.multiple_of(core_ref[0] * HALF, HALF)
    high = pl.multiple_of((1 - core_ref[0]) * HALF, HALF)
    go = Mover(marks)
    wait(go((turned_a_ref, turned_a), (weight_a_ref, weight_a), (turned_b_ref, turned_b), (weight_b_ref, weight_b)))
    whole[...] = mul(turned_a[...], weight_a[...], 0, 0) + mul(turned_b[...], weight_b[...], 0, 0)
    stores = go((whole.at[pl.ds(low, HALF), :], keep_ref))
    send_ref[:HALF, :] = whole[pl.ds(high, HALF), :].astype(bfloat)
    small = small_ref[...]
    high_part = small.astype(bfloat)
    low_part = (small - high_part.astype(single)).astype(bfloat)
    send_ref[HALF:, :] = jnp.concatenate([high_part, low_part], axis=0)
    wait(stores)


CURVE = float(np.sqrt(2.0 / np.pi))
STEP = 256


def mlp_body(second, *refs):
    if second:
        owner_ref, refs = refs[0], refs[1:]
    x_refs, refs = refs[: 2 * PARTS], refs[2 * PARTS :]
    g_own_ref, g_peer_ref, refs = refs[0], refs[1], refs[2:]
    if second:
        up_ref, down_refs, refs = refs[0], refs[1 : 1 + SQUARE], refs[1 + SQUARE :]
        before_refs, up_mine_ref = refs[:4], refs[4]
        down_grad_ref, part_refs = refs[9], refs[10:14]
        refs = refs[5:9] + refs[14:]
    else:
        up_ref, down_ref = refs[:2]
        down_grad_ref, up_grad_ref = refs[6:8]
        refs = refs[2:6] + refs[8:]
    send_norm_ref, keep_norm_ref, send_out_ref, keep_out_ref = refs[:4]
    x_all, g_all, up, down, active, grad_hidden, x_turned = refs[4:11]
    send_norm, keep_norm, send_out, keep_out, down_grad, up_grad, marks = refs[11:18]
    rows, size = x_all.shape[0] // 2, x_all.shape[0] // (2 * PARTS)
    units = down.shape[0]
    go = Mover(marks)
    x_loads = go(*[(x_refs[index], x_all.at[pl.ds(index * size, size), :]) for index in range(2 * PARTS)])
    if second:
        loads = go((up_ref, up), *joined(owner_ref[0], down_refs, down))
    else:
        loads = go((up_ref, up), (down_ref, down))
    loads += go((g_own_ref, g_all.at[pl.ds(0, rows), :]), (g_peer_ref, g_all.at[pl.ds(rows, rows), :]))
    more, mine, stores = [], [], []
    if second:
        (up_mine,) = refs[18:]
        more = go(*zip(before_refs, (send_norm, keep_norm, send_out, keep_out)))
        mine = go((up_mine_ref, up_mine))
    wait(x_loads)
    x_turned[...] = x_all[...].T
    wait(loads)
    for begin in range(0, units, STEP):
        columns = slice(begin, begin + STEP)
        for top in range(0, 2 * rows, rows):
            span = slice(top, top + rows)
            v = mul(x_all[span, :], up[:, columns])
            grad = mul(g_all[span, :], down[columns, :], 1, 1)
            square = v * v
            half = 0.5 + 0.5 * jnp.tanh(v * (CURVE + (CURVE * 0.044715) * square))
            act = v * half
            slope = half + act * (1.0 - half) * (2.0 * CURVE + (6.0 * CURVE * 0.044715) * square)
            active[span, columns] = act.astype(bfloat)
            grad_hidden[span, columns] = (grad * slope).astype(bfloat)

    def put(target, value):
        target[...] = (value + target[...].astype(single) if second else value).astype(target.dtype)

    wait(more)
    put(keep_norm, mul(grad_hidden[:rows, :], up[...], 1, 1))
    put(send_norm, mul(grad_hidden[rows:, :], up[...], 1, 1))
    stores += go((keep_norm, keep_norm_ref), (send_norm, send_norm_ref))
    down_grad[...] = mul(active[...], g_all[...], 0, 0).astype(down_grad.dtype)
    stores += go((down_grad, down_grad_ref))
    up_grad[...] = mul(x_turned[...], grad_hidden[...]).astype(bfloat)
    if second:
        wait(mine)
        part = up_grad.shape[0] // SQUARE
        for mask, part_ref in enumerate(part_refs):
            rows_of = quarter(owner_ref[0], mask, part)
            stores += go(
                (up_mine.at[rows_of, :], part_ref.at[pl.ds(0, part), :]),
                (up_grad.at[rows_of, :], part_ref.at[pl.ds(part, part), :]),
            )
    else:
        stores += go((up_grad, up_grad_ref))
    put(keep_out, mul(active[:rows, :], down[...]))
    stores += go((keep_out, keep_out_ref))
    put(send_out, mul(active[rows:, :], down[...]))
    wait(stores + go((send_out, send_out_ref)))


def mlp(x_own, x_peer, g_own, g_peer, up, down, upper=(), before=(), flops=0):
    rows, width = g_own.shape
    units = sum(piece.shape[0] for piece in down)
    tall = (2 * rows, width)
    pair = [((rows, width), bfloat), ((rows, width), single)] * 2
    outs = pair + [((units, width), bfloat)]
    outs += [((2 * width // SQUARE, units), bfloat)] * SQUARE if before else [((width, units), bfloat)]
    scratch = [
        pltpu.VMEM(tall, bfloat),
        pltpu.VMEM(tall, bfloat),
        pltpu.VMEM((width, units), bfloat),
        pltpu.VMEM((units, width), bfloat),
        pltpu.VMEM((2 * rows, units), bfloat),
        pltpu.VMEM((2 * rows, units), bfloat),
        pltpu.VMEM((width, 2 * rows), bfloat),
    ]
    scratch += [pltpu.VMEM(shape, kind) for shape, kind in pair]
    scratch += [
        pltpu.VMEM((units, width), bfloat), pltpu.VMEM((width, units), bfloat), pltpu.SemaphoreType.DMA((32,)),
    ]
    if before:
        scratch.append(pltpu.VMEM((width, units), bfloat))
    operands = (*upper, *x_own, *x_peer, g_own, g_peer, *up, *down, *before)
    return call(
        functools.partial(mlp_body, bool(before)),
        outs,
        operands,
        scratch,
        len(upper),
        vmem=60,
        flops=flops,
        far=len(operands) - len(upper),
        far_outs=len(outs),
    )


def shards(
    inputs,
    history,
    cotangent,
    qkv_weight,
    out_weight,
    up_weight,
    down_weight,
    gain_attn,
    gain_mlp,
    dwa_weights,
):
    rows, width = inputs.shape
    members = lax.axis_size("mp")
    copies = lax.axis_size("dp")
    bits = copies.bit_length() - 1
    core = lax.rem(lax.axis_index("mp"), 2).astype(jnp.int32).reshape(1)
    copy_index = lax.axis_index("dp").astype(jnp.int32).reshape(1)
    core_pairs = [(i, i ^ 1) for i in range(members)]
    chip_pairs = [(i, i ^ 2) for i in range(members)]
    depth = history.shape[0]
    part = out_weight.shape[0]

    def other_core(value):
        return lax.ppermute(value, "mp", core_pairs)

    def other_chip(value):
        return lax.ppermute(value, "mp", chip_pairs)

    def other_copy(value, mask):
        return lax.ppermute(value, "dp", [(i, i ^ mask) for i in range(copies)])

    owner = copy_index & (SQUARE - 1)
    cosine, sine = (jnp.asarray(table) for table in tables())

    qkv_own = qkv_weight.transpose(1, 2, 0).reshape(3 * part, width)
    fourth = (width // SQUARE, width)
    square = (width, width)
    masks = range(1, SQUARE)
    marks = pltpu.SemaphoreType.DMA((16,))
    (down_quarter,) = call(
        split_body,
        [(fourth, bfloat)],
        (owner, down_weight),
        [pltpu.VMEM(fourth, bfloat), marks],
        1,
        vmem=60,
        far=1,
        far_outs=1,
    )
    qkv_peer, out_peer = other_chip(qkv_own), other_chip(out_weight)
    down_come, up_peer = other_chip(down_quarter), other_chip(up_weight)

    full = (rows, width)
    x_own = call(norm_body, [((rows // 2, width), bfloat)] * 2, (inputs, gain_attn), after=(down_quarter,))
    x_peer = [other_core(value) for value in x_own]
    tall = (SEQ, width)
    tokens = pltpu.VMEM(tall, bfloat)
    first_outs = [
        ((3 * part, SEQ), bfloat), ((part, SEQ), bfloat), ((SEQ, part), bfloat), ((8, SEQ), single),
    ]
    heads = part // DH
    tiles = [tokens, pltpu.VMEM((heads, SEQ, 256), single), pltpu.VMEM((heads, SEQ, 256), bfloat)]
    qkv_a, att_a, nat_a, log_a = call(
        attend_placed, first_outs, (core, *x_own, *x_peer, cosine, sine, qkv_own), tiles, 1, vmem=32
    )
    history_grad, mixed, g_own, history_parts = average_history(dwa_weights, history, cotangent, (log_a,))
    g_peer = other_core(g_own)
    qkv_b, att_b, nat_b, log_b = call(
        attend_placed,
        first_outs,
        (core, *x_own, *x_peer, cosine, sine, qkv_peer),
        tiles,
        1,
        (history_parts,),
        32,
        MUCH,
    )
    third = (rows // PARTS, width)
    keep, *send, down_copy = call(
        branch_body,
        [(full, single)] + [(third, bfloat)] * PARTS + [(fourth, bfloat)],
        (core, nat_a, nat_b, out_weight, out_peer, down_come),
        (),
        1,
        (g_peer,),
    )
    down_pieces = [down_come] + [other_copy(down_copy, mask) for mask in masks]
    recv = [other_core(value) for value in send]
    middle, *y_own = call(
        middle_body, [(full, single)] + [(third, bfloat)] * PARTS, (inputs, keep, gain_mlp, *recv)
    )
    y_peer = [other_core(value) for value in y_own]

    first = mlp(y_own, y_peer, g_own, g_peer, (up_weight,), (down_weight,))
    down_mine, up_mine = first[4:]
    second = mlp(
        y_own, y_peer, g_own, g_peer, (up_peer,), down_pieces, (owner,), (*first[:4], up_mine)
    )
    send_norm, keep_norm, send_out, keep_out, down_theirs = second[:5]
    token = [keep_norm]

    def step(body, outs, operands, scratch=(), scalars=0, vmem=16, flops=MUCH, far=0, far_outs=0, marked=False):
        count = len(operands)

        def marking(*refs):
            mark_body(refs[count])
            body(*refs[:count], *refs[count + 1 :])

        if marked:
            mark = [((8, 128), single)]
            results = call(marking, mark + outs, operands, scratch, scalars, tuple(token), vmem, flops, far, far_outs)
            token[0] = results[0]
            return results[1:]
        results = call(body, outs, operands, scratch, scalars, tuple(token), vmem, flops, far, far_outs)
        token[0] = min(results, key=lambda value: value.size * value.dtype.itemsize)
        return results

    down_come = other_chip(down_theirs)
    up_parts = [second[5]] + [other_copy(value, mask) for mask, value in zip(masks, second[6:])]
    out_come = other_core(send_out)
    grad_middle, gb_own, gain_mlp_part = step(
        middle_back_body,
        [(full, single), (full, bfloat), ((1, width), single)],
        (dwa_weights, middle, keep_norm, other_core(send_norm), cotangent, gain_mlp),
        scalars=1,
        flops=0,
    )
    gb_peer = other_core(gb_own)
    combined, dwa_part = step(
        combine_body,
        [(full, bfloat), ((depth + 1, width), single)],
        (dwa_weights, mixed, middle, keep_out, out_come, cotangent, history_parts),
        scalars=1,
        flops=0,
    )

    def back(weight, qkv_weight, qkv, att, log, flops, before=()):
        return step(
            attend_back,
            [
                ((depth + 3 if before else 1, width), single),
                ((4 * part, width), bfloat),
                ((3 * part, SEQ), bfloat),
            ],
            (
                core, log, cosine, sine, gain_attn, *before, gb_own, gb_peer, *x_own, *x_peer, weight, qkv_weight, qkv,
                att,
            ),
            [
                pltpu.VMEM(tall, bfloat),
                pltpu.VMEM(tall, bfloat),
                pltpu.VMEM((part, width), bfloat),
                pltpu.VMEM((3 * part, width), bfloat),
                pltpu.VMEM((3 * part, SEQ), bfloat),
                pltpu.VMEM((part, SEQ), bfloat),
                pltpu.VMEM((3 * part, SEQ), bfloat),
                pltpu.VMEM((4 * part, width), bfloat),
                pltpu.VMEM((heads, SEQ, SEQ), bfloat),
                pltpu.VMEM((heads, SEQ, SEQ), bfloat),
                pltpu.VMEM((3 * part, width), single),
                marks,
            ],
            1,
            60,
            flops,
            10,
            2,
        )

    gain_part, att_theirs, turned_b = back(out_peer, qkv_peer, qkv_b, att_b, log_b, 0)
    att_come = other_chip(att_theirs)
    def spread(mine, come, flops=MUCH):
        own, *sent = step(part_body, [(fourth, bfloat)] * SQUARE, (owner, mine, come), scalars=1, flops=flops)
        return [own] + [other_copy(value, mask) for mask, value in zip(masks, sent)]

    down_parts = spread(down_mine, down_come, 0)
    up, sent = step(four_two_body, [(fourth, bfloat)] * 2, up_parts, flops=0)
    up_come = other_chip(sent)
    part_sums, att_mine, turned_a = back(
        out_weight, qkv_own, qkv_a, att_a, log_a, MUCH, (gain_part, gain_mlp_part, dwa_part)
    )

    def exchange(value):
        for bit in range(2, bits):
            come = other_copy(value, 1 << bit)
            if bit < bits - 1:
                (value,) = step(low_body, [(value.shape, bfloat)], (value, come))
        return value, come

    def finish(value, come):
        (value,) = step(low_body, [(value.shape, bfloat)], (value, come), flops=COST)
        return [value] + [other_copy(value, mask) for mask in masks]

    (down,) = step(four_body, [(fourth, bfloat)], down_parts, flops=COST)
    down = exchange(down)
    att_parts = spread(att_mine, att_come, COST)
    (up,) = step(low_body, [(fourth, bfloat)], (up, up_come), flops=COST)
    up = exchange(up)
    send_first, keep_first = step(
        first_grad_body,
        [((rows + EXTRA, width), bfloat), (full, single)],
        (core, part_sums, turned_a, turned_b, qkv_own, qkv_peer),
        [pltpu.VMEM((3 * part, SEQ), bfloat)] * 2
        + [pltpu.VMEM((3 * part, width), bfloat)] * 2
        + [pltpu.VMEM(tall, single), marks],
        1,
        60,
        COST,
        4,
        1,
        True,
    )
    first_come = other_core(send_first)
    token.append(down[1])
    step(mark_body, [((8, 128), single)], (), flops=COST)
    del token[1:]
    (part_sums,) = step(small_body, [(part_sums.shape, single)], (part_sums, first_come), flops=COST)
    more_sums = other_chip(part_sums)
    (input_grad,) = step(
        first_back_body,
        [(full, bfloat)],
        (inputs, keep_first, first_come, grad_middle, gain_attn),
        vmem=60,
        flops=COST,
        marked=True,
    )
    block = (width // SQUARE + EXTRA, width)
    (att,) = step(four_more_body, [(block, bfloat)], (part_sums, more_sums, *att_parts), flops=COST)
    att = exchange(att)
    down = finish(*down)
    token += down[1:]
    pair = (block[0] + fourth[0], width)
    (both,) = step(pair_body, [(pair, bfloat)], (*att, *up), flops=COST)
    del token[1:]
    both = [both] + [other_copy(both, mask) for mask in masks]
    (down_grad,) = step(
        whole_body,
        [(square, single)],
        (owner, *down),
        [pltpu.VMEM(square, bfloat), pltpu.VMEM(square, single), marks],
        1,
        flops=COST,
        far_outs=1,
        marked=True,
    )
    gain_attn_grad, gain_mlp_grad, dwa_grad, qkv_grad, out_grad, up_grad = step(
        more_body,
        [
            ((width,), single),
            ((width,), single),
            ((depth + 1,), single, "scalars"),
            ((3 * part, width), single),
            ((part, width), single),
            (square, single),
        ],
        (owner, *both),
        [pltpu.VMEM((SQUARE * pair[0], width), bfloat), pltpu.VMEM(square, single), pltpu.VMEM(square, single), marks],
        1,
        flops=COST,
        far_outs=3,
    )

    return (
        combined,
        input_grad,
        history_grad,
        qkv_grad.reshape(3, part, width).transpose(2, 0, 1),
        out_grad,
        up_grad,
        down_grad,
        gain_attn_grad,
        gain_mlp_grad,
        dwa_grad,
    )


def solution(mesh):
    placed = (
        P(("dp", "mp"), None),
        P(None, ("dp", "mp"), None),
        P(("dp", "mp"), None),
        P(None, None, "mp"),
        P("mp", None),
        P(None, "mp"),
        P("mp", None),
        P(),
        P(),
        P(),
    )
    return jax.shard_map(
        shards,
        mesh=mesh,
        in_specs=placed,
        out_specs=(
            P(("dp", "mp"), None),
            P(("dp", "mp"), None),
            P(None, ("dp", "mp"), None),
            P(None, None, "mp"),
            P("mp", None),
            P(None, "mp"),
            P("mp", None),
            P(),
            P(),
            P(),
        ),
        check_vma=False,
    )
```

```python
import functools

import jax
import jax.numpy as jnp
import numpy as np
from jax import lax
from jax.experimental import pallas as pl
from jax.experimental.pallas import tpu as pltpu
from jax.sharding import PartitionSpec as P

DH = 64
SEQ = 1152
HALF = SEQ // 2
EPS = 1e-05
bfloat = jnp.bfloat16
single = jnp.float32
MIB = 1 << 20
MUCH = 10**11
COST = 10**10


def tables():
    half_width = DH // 2
    places = np.arange(SEQ, dtype=np.float32)
    frequency = np.float32(10000.0) ** (-np.arange(half_width, dtype=np.float32) * np.float32(2.0 / DH))
    angles = frequency[:, None] * places[None, :]
    return (np.cos(angles).astype(np.float32), np.sin(angles).astype(np.float32))


def mul(a, b, ca=1, cb=0):
    return lax.dot_general(a, b, (((ca,), (cb,)), ((), ())), preferred_element_type=single)


def call(kernel, outs, operands, scratch=(), scalars=0, after=(), vmem=16, flops=0, far=0, far_outs=0):
    count, waits = len(operands), len(after)

    def body(*refs):
        kernel(*refs[:count], *refs[count + waits :])

    small = pl.BlockSpec(memory_space=pltpu.SMEM)
    whole = pl.BlockSpec(memory_space=pltpu.VMEM)
    apart = pl.BlockSpec(memory_space=pltpu.HBM)
    loose = pl.BlockSpec(memory_space=pl.ANY)
    inner = len(outs) - far_outs
    return pl.pallas_call(
        body,
        out_shape=[jax.ShapeDtypeStruct(out[0], out[1]) for out in outs],
        in_specs=[small] * scalars + [whole] * (count - scalars - far) + [apart] * far + [loose] * waits,
        out_specs=[small if len(out) > 2 else whole for out in outs[:inner]] + [apart] * far_outs,
        scratch_shapes=list(scratch),
        compiler_params=pltpu.CompilerParams(vmem_limit_bytes=vmem * MIB),
        cost_estimate=pl.CostEstimate(flops=flops, bytes_accessed=0, transcendentals=0),
    )(*operands, *after)


class Mover:
    def __init__(self, marks):
        self.marks = marks
        self.used = 0

    def __call__(self, *pairs):
        copies = []
        for source, target in pairs:
            copies.append(pltpu.make_async_copy(source, target, self.marks.at[self.used]))
            self.used += 1
        for copy in copies:
            copy.start()
        return copies


def wait(copies):
    for copy in copies:
        copy.wait()


ROWS = 64
PARTS = 3


def spans(rows, step=ROWS):
    return [slice(begin, begin + step) for begin in range(0, rows, step)]


def normal_of(x):
    centre = x - jnp.mean(x, axis=-1, keepdims=True)
    spread = jnp.mean(centre * centre, axis=-1, keepdims=True)
    scale = lax.rsqrt(spread + EPS)
    return centre * scale, scale


def split_body(owner_ref, in_ref, out_ref, hold, marks):
    go = Mover(marks)
    wait(go((in_ref.at[quarter(owner_ref[0], 0, hold.shape[0]), :], hold)))
    wait(go((hold, out_ref)))


def joined(owner, refs, target):
    size = refs[0].shape[0]
    return [(ref, target.at[quarter(owner, mask, size), :]) for mask, ref in enumerate(refs)]


def norm_body(x_ref, gain_ref, *out_refs):
    gain = gain_ref[...].reshape(1, -1)
    for index, out_ref in enumerate(out_refs):
        rows = out_ref.shape[0]
        for span in spans(rows, rows // 6):
            here = slice(index * rows + span.start, index * rows + span.stop)
            normal, _ = normal_of(x_ref[here, :].astype(single))
            out_ref[span, :] = (normal * gain).astype(bfloat)


def middle_body(x_ref, keep_ref, gain_ref, *rest):
    recv_refs, mid_ref, out_refs = rest[:PARTS], rest[PARTS], rest[PARTS + 1 :]
    gain = gain_ref[...].reshape(1, -1)
    rows = x_ref.shape[0] // PARTS
    for index in range(PARTS):
        for span in spans(rows):
            here = slice(index * rows + span.start, index * rows + span.stop)
            recv = recv_refs[index][span, :].astype(single)
            x = x_ref[here, :].astype(single) + (keep_ref[here, :] + recv)
            mid_ref[here, :] = x
            normal, _ = normal_of(x)
            out_refs[index][span, :] = (normal * gain).astype(bfloat)


def norm_back(x, grad, gain):
    normal, scale = normal_of(x)
    lifted = grad * gain
    back = scale * (
        lifted
        - jnp.mean(lifted, axis=-1, keepdims=True)
        - normal * jnp.mean(lifted * normal, axis=-1, keepdims=True)
    )
    return back, normal


def fold_rows(value):
    total = value[:8]
    for begin in range(8, value.shape[0], 8):
        total = total + value[begin : begin + 8]
    return total


def middle_back_body(mix_ref, x_ref, keep_ref, recv_ref, cot_ref, gain_ref, mid_ref, low_ref, part_ref):
    gain = gain_ref[...].reshape(1, -1)
    part = jnp.zeros((8, x_ref.shape[1]), single)
    for span in spans(x_ref.shape[0]):
        grad = keep_ref[span, :] + recv_ref[span, :].astype(single)
        back, normal = norm_back(x_ref[span, :], grad, gain)
        total = mix_ref[mix_ref.shape[0] - 1] * cot_ref[span, :] + back
        mid_ref[span, :] = total
        low_ref[span, :] = total.astype(bfloat)
        part = part + fold_rows(grad * normal)
    part_ref[...] = jnp.sum(part, axis=0, keepdims=True)


def first_back_body(x_ref, keep_ref, recv_ref, mid_ref, gain_ref, out_ref):
    gain = gain_ref[...].reshape(1, -1)
    for span in spans(x_ref.shape[0]):
        grad = keep_ref[span, :] + recv_ref[span, :].astype(single)
        back, _ = norm_back(x_ref[span, :].astype(single), grad, gain)
        out_ref[span, :] = (mid_ref[span, :] + back).astype(bfloat)


def history_body(mix_ref, history_ref, cot_ref, grad_ref, mixed_ref, low_ref, part_ref):
    depth = history_ref.shape[0]

    @pl.when(pl.program_id(0) == 0)
    def _():
        part_ref[...] = jnp.zeros_like(part_ref)

    for span in spans(cot_ref.shape[0], 32):
        cot = cot_ref[span, :]
        low_ref[span, :] = (mix_ref[depth] * cot).astype(bfloat)
        mixed = None
        for j in range(depth):
            layer = history_ref[j, span, :].astype(single)
            mixed = mix_ref[j] * layer if mixed is None else mixed + mix_ref[j] * layer
            grad_ref[j, span, :] = (mix_ref[j] * cot).astype(bfloat)
            part_ref[8 * j : 8 * j + 8, :] += fold_rows(layer * cot)
        mixed_ref[span, :] = mixed


def average_history(mix, history, cot, after=()):
    depth, rows, width = history.shape
    step = 96
    waits = len(after)

    def body(*refs):
        history_body(*refs[:3], *refs[3 + waits :])

    row_block = pl.BlockSpec((step, width), lambda i: (i, 0))
    deep_block = pl.BlockSpec((depth, step, width), lambda i: (0, i, 0))
    return pl.pallas_call(
        body,
        grid=(rows // step,),
        out_shape=[
            jax.ShapeDtypeStruct(history.shape, bfloat),
            jax.ShapeDtypeStruct((rows, width), single),
            jax.ShapeDtypeStruct((rows, width), bfloat),
            jax.ShapeDtypeStruct((8 * depth, width), single),
        ],
        in_specs=[pl.BlockSpec(memory_space=pltpu.SMEM), deep_block, row_block]
        + [pl.BlockSpec(memory_space=pl.ANY)] * waits,
        out_specs=[deep_block, row_block, row_block, pl.BlockSpec((8 * depth, width), lambda i: (0, 0))],
        compiler_params=pltpu.CompilerParams(vmem_limit_bytes=16 * MIB),
        cost_estimate=pl.CostEstimate(flops=0, bytes_accessed=0, transcendentals=0),
    )(mix, history, cot, *after)


def combine_body(mix_ref, mixed_ref, mid_ref, keep_ref, recv_ref, cot_ref, parts_ref, out_ref, part_ref):
    depth = mix_ref.shape[0] - 1
    last = jnp.zeros((8, mid_ref.shape[1]), single)
    for span in spans(mid_ref.shape[0]):
        outputs = mid_ref[span, :] + (keep_ref[span, :] + recv_ref[span, :].astype(single))
        out_ref[span, :] = (mixed_ref[span, :] + mix_ref[depth] * outputs).astype(bfloat)
        last = last + fold_rows(outputs * cot_ref[span, :])
    for j in range(depth):
        part_ref[j : j + 1, :] = jnp.sum(parts_ref[8 * j : 8 * j + 8, :], axis=0, keepdims=True)
    part_ref[depth : depth + 1, :] = jnp.sum(last, axis=0, keepdims=True)


SQUARE = 4


def quarter(owner, mask, size):
    other = owner + (mask & 1) * (1 - 2 * (owner % 2)) + (mask & 2) * (1 - 2 * (owner // 2))
    return pl.ds(pl.multiple_of(other * size, size), size)


def part_body(owner_ref, mine_ref, come_ref, *out_refs):
    for mask, out_ref in enumerate(out_refs):
        rows = quarter(owner_ref[0], mask, out_ref.shape[0])
        out_ref[...] = (mine_ref[rows, :].astype(single) + come_ref[rows, :].astype(single)).astype(bfloat)


def sum_of(refs, rows):
    total = refs[0][rows, :].astype(single)
    for ref in refs[1:]:
        total = total + ref[rows, :].astype(single)
    return total


def four_body(*refs):
    refs[-1][...] = sum_of(refs[:-1], slice(None)).astype(bfloat)


def four_two_body(*refs):
    size = refs[-1].shape[0]
    refs[-2][...] = sum_of(refs[:-2], slice(0, size)).astype(bfloat)
    refs[-1][...] = sum_of(refs[:-2], slice(size, 2 * size)).astype(bfloat)


EXTRA = 16


def mark_body(out_ref):
    out_ref[...] = jnp.zeros_like(out_ref)


def small_body(small_ref, first_ref, out_ref):
    half = small_ref.shape[0]
    rows = first_ref.shape[0] - 2 * half
    come = first_ref[rows:, :].astype(single)
    out_ref[...] = small_ref[...] + (come[:half] + come[half:])


def four_more_body(small_ref, more_ref, *refs):
    out_ref = refs[-1]
    size = out_ref.shape[0] - EXTRA
    out_ref[:size, :] = sum_of(refs[:-1], slice(None)).astype(bfloat)
    small = small_ref[...] + more_ref[...]
    rest = jnp.zeros((EXTRA - small.shape[0], small.shape[1]), single)
    out_ref[size:, :] = jnp.concatenate([small, rest], axis=0).astype(bfloat)


def gather(owner_ref, pieces, hold):
    for mask, piece in enumerate(pieces):
        hold[quarter(owner_ref[0], mask, piece.shape[0]), :] = piece[...]


def pair_body(a_ref, a_come_ref, b_ref, b_come_ref, out_ref):
    size = a_ref.shape[0]
    out_ref[:size, :] = sum_of((a_ref, a_come_ref), slice(None)).astype(bfloat)
    out_ref[size:, :] = sum_of((b_ref, b_come_ref), slice(None)).astype(bfloat)


def whole_body(owner_ref, a_ref, b_ref, c_ref, d_ref, out_ref, hold, full, marks):
    gather(owner_ref, (a_ref, b_ref, c_ref, d_ref), hold)
    go, stores = Mover(marks), []
    size = hold.shape[0] // SQUARE
    for index in range(SQUARE):
        rows = pl.ds(index * size, size)
        full[rows, :] = hold[rows, :].astype(single)
        stores += go((full.at[rows, :], out_ref.at[rows, :]))
    wait(stores)


def more_body(
    owner_ref, a_ref, b_ref, c_ref, d_ref, attn_ref, mlp_ref, dwa_ref, top_ref, end_ref, up_ref, hold, att, up, marks
):
    gather(owner_ref, (a_ref, b_ref, c_ref, d_ref), hold)
    go, stores = Mover(marks), []
    block = hold.shape[0] // SQUARE
    size = up.shape[0] // SQUARE
    small = jnp.zeros((EXTRA, hold.shape[1]), single)
    for index in range(SQUARE):
        begin = index * block
        rows = pl.ds(index * size, size)
        att[rows, :] = hold[begin : begin + size, :].astype(single)
        stores += go((att.at[rows, :], top_ref.at[rows, :] if index < SQUARE - 1 else end_ref))
        small = small + hold[begin + size : begin + size + EXTRA, :].astype(single)
        up[rows, :] = hold[begin + size + EXTRA : begin + block, :].astype(single)
        stores += go((up.at[rows, :], up_ref.at[rows, :]))
    attn_ref[...] = small[0]
    mlp_ref[...] = small[1]
    for index in range(dwa_ref.shape[0]):
        dwa_ref[index] = jnp.sum(small[2 + index : 3 + index])
    wait(stores)


def low_body(mine_ref, come_ref, out_ref):
    out_ref[...] = (mine_ref[...].astype(single) + come_ref[...].astype(single)).astype(bfloat)


def mark_body(out_ref):
    out_ref[...] = jnp.zeros_like(out_ref)


def small_body(small_ref, first_ref, out_ref):
    half = small_ref.shape[0]
    rows = first_ref.shape[0] - 2 * half
    come = first_ref[rows:, :].astype(single)
    out_ref[...] = small_ref[...] + (come[:half] + come[half:])


BLOCKS = tuple((begin, min(256, SEQ - begin)) for begin in range(0, SEQ, 256))


def places(core_ref, refs):
    count, size = len(refs) // 2, refs[0].shape[0]
    for index, ref in enumerate(refs):
        core = core_ref[0] if index < count else 1 - core_ref[0]
        yield ref, pl.ds(pl.multiple_of(core * HALF + index % count * size, size), size)


def allowed(size):
    key_pos = lax.broadcasted_iota(jnp.int32, (size, size), 0)
    query_pos = lax.broadcasted_iota(jnp.int32, (size, size), 1)
    return query_pos >= key_pos


def turn(rows, cosine, sine):
    half = rows.shape[0] // 2
    a, b = rows[:half], rows[half:]
    return jnp.concatenate([a * cosine - b * sine, b * cosine + a * sine], axis=0)


KEYS = 128


def fold_top(value):
    top = value[:8]
    for begin in range(8, value.shape[0], 8):
        top = jnp.maximum(top, value[begin : begin + 8])
    return top


def masked(scores, offset):
    key_pos = lax.broadcasted_iota(jnp.int32, scores.shape, 0) + offset
    query_pos = lax.broadcasted_iota(jnp.int32, scores.shape, 1)
    return jnp.where(query_pos >= key_pos, scores, -jnp.inf)


def attend_placed(core_ref, *rest):
    for ref, where in places(core_ref, rest[:4]):
        rest[11][where, :] = ref[...]
    cos_ref, sin_ref, weight_ref, rest = rest[4], rest[5], rest[6], rest[7:]
    attend(weight_ref, cos_ref, sin_ref, *rest)


def attend(weight_ref, cos_ref, sin_ref, qkv_ref, att_ref, nat_ref, log_ref, tokens, all_scores, all_weights):
    width = weight_ref.shape[0] // 3
    projected = mul(weight_ref[...], tokens[...], 1, 1)
    cosine, sine = cos_ref[...], sin_ref[...]
    for part in range(3):
        for head in range(width // DH):
            begin = part * width + head * DH
            rows = projected[begin : begin + DH]
            if part < 2:
                rows = turn(rows, cosine, sine)
            if part == 0:
                rows = rows * DH ** (-0.5)
            qkv_ref[begin : begin + DH, :] = rows.astype(bfloat)
    log_ref[...] = jnp.zeros_like(log_ref)
    heads = range(width // DH)
    keys = [qkv_ref[width + head * DH : width + head * DH + DH, :].T for head in heads]
    for begin, size in BLOCKS:
        end = begin + size
        tops = [None for _ in heads]
        for row in range(0, end, KEYS):
            for head in heads:
                tile = mul(keys[head][row : row + KEYS], qkv_ref[head * DH : head * DH + DH, begin:end])
                if row >= begin:
                    tile = masked(tile, row - begin)
                all_scores[head, row : row + KEYS, :size] = tile
                top = fold_top(tile)
                tops[head] = top if row == 0 else jnp.maximum(tops[head], top)
        tops = [jnp.max(top, axis=0, keepdims=True) for top in tops]
        totals = [jnp.zeros((8, size), single) for _ in heads]
        for row in range(0, end, KEYS):
            for head in heads:
                tile = jnp.exp(all_scores[head, row : row + KEYS, :size] - tops[head])
                totals[head] = totals[head] + fold_rows(tile)
                all_weights[head, row : row + KEYS, :size] = tile.astype(bfloat)
        for head in heads:
            base = head * DH
            total = jnp.sum(totals[head], axis=0, keepdims=True)
            value = qkv_ref[2 * width + base : 2 * width + base + DH, :end]
            mixed = mul(value, all_weights[head, :end, :size]) / total
            att_ref[base : base + DH, begin:end] = mixed.astype(bfloat)
            log_ref[head : head + 1, begin:end] = tops[head] + jnp.log(total)
    nat_ref[...] = att_ref[...].T


def branch_body(core_ref, att_a_ref, att_b_ref, out_a_ref, out_b_ref, pass_ref, keep_ref, *rest):
    send_refs, pass_out = rest[:PARTS], rest[PARTS]
    pass_out[...] = pass_ref[...]
    low = pl.multiple_of(core_ref[0] * HALF, HALF)
    rows = HALF // PARTS
    for index in range(PARTS):
        high = pl.multiple_of((1 - core_ref[0]) * HALF + index * rows, rows)
        send = mul(att_a_ref[pl.ds(high, rows), :], out_a_ref[...])
        send_refs[index][...] = (send + mul(att_b_ref[pl.ds(high, rows), :], out_b_ref[...])).astype(bfloat)
    keep = mul(att_a_ref[pl.ds(low, HALF), :], out_a_ref[...])
    keep_ref[...] = keep + mul(att_b_ref[pl.ds(low, HALF), :], out_b_ref[...])


def attend_back(
    core_ref, log_ref, cos_ref, sin_ref, gain_ref, *rest
):
    before_refs, rest = rest[:-25], rest[-25:]
    grad_refs, x_refs = rest[:2], rest[2:6]
    weight_ref, qkv_weight_ref, qkv_ref, att_ref, small_ref, out_ref, turned_ref = rest[6:13]
    grads, tokens, weight, qkv_weight, qkv, att, turned, result, all_probs, all_scores, hold, marks = rest[13:]
    go = Mover(marks)
    first = go(
        (weight_ref, weight),
        *[(ref, grads.at[where, :]) for ref, where in places(core_ref, grad_refs)],
        (att_ref, att),
        (qkv_ref, qkv),
    )
    later = go(
        *[(ref, tokens.at[where, :]) for ref, where in places(core_ref, x_refs)],
        (qkv_weight_ref, qkv_weight),
    )
    wait(first)
    width = att.shape[0]
    grad_att = mul(weight[...], grads[...], 1, 1).astype(bfloat)
    result[3 * width :, :] = mul(att[...], grads[...]).astype(result.dtype)
    cosine, sine = cos_ref[...], sin_ref[...]
    heads = range(width // DH)
    spans_of = [slice(head * DH, head * DH + DH) for head in heads]
    query = [qkv[span, :] for span in spans_of]
    key = [qkv[width + span.start : width + span.stop, :] for span in spans_of]
    above = [grad_att[span] for span in spans_of]
    centre = [
        jnp.sum(above[head].astype(single) * att[span, :].astype(single), axis=0, keepdims=True)
        for head, span in enumerate(spans_of)
    ]
    keys = [value.T for value in key]
    values = [qkv[2 * width + span.start : 2 * width + span.stop, :].T for span in spans_of]
    queries = [value.T for value in query]
    aboves = [value.T for value in above]
    grad_query = [[] for _ in heads]
    for begin, size in BLOCKS:
        end = begin + size
        for row in range(0, end, KEYS):
            span = slice(row, row + KEYS)
            for head in heads:
                tile = mul(keys[head][span], query[head][:, begin:end])
                if row >= begin:
                    tile = masked(tile, row - begin)
                tile = jnp.exp(tile - log_ref[head : head + 1, begin:end])
                grad = mul(values[head][span], above[head][:, begin:end]) - centre[head][:, begin:end]
                all_probs[head, span, begin:end] = tile.astype(bfloat)
                all_scores[head, span, begin:end] = (tile * grad).astype(bfloat)
        for head in heads:
            grad_query[head].append(mul(key[head][:, :end], all_scores[head, :end, begin:end]))
    grad_key = [[] for _ in heads]
    grad_value = [[] for _ in heads]
    for begin, size in BLOCKS:
        span = slice(begin, begin + size)
        for head in heads:
            grad_key[head].append(mul(all_scores[head, span, begin:], queries[head][begin:]))
            grad_value[head].append(mul(all_probs[head, span, begin:], aboves[head][begin:]))
    for head, span in enumerate(spans_of):
        grad = jnp.concatenate(grad_query[head], axis=1) * DH ** (-0.5)
        turned[span, :] = turn(grad, cosine, -sine).astype(bfloat)
        grad = jnp.concatenate(grad_key[head], axis=0).T
        turned[width + span.start : width + span.stop, :] = turn(grad, cosine, -sine).astype(bfloat)
        grad = jnp.concatenate(grad_value[head], axis=0).T
        turned[2 * width + span.start : 2 * width + span.stop, :] = grad.astype(bfloat)
    stores = go((turned, turned_ref))
    wait(later)
    hold[...] = mul(turned[...], tokens[...])
    result[: 3 * width, :] = hold[...].astype(result.dtype)
    stores += go((result, out_ref))
    part = jnp.zeros((8, hold.shape[1]), single)
    for span in spans(hold.shape[0]):
        part = part + fold_rows(hold[span, :] * qkv_weight[span, :].astype(single))
    gain = jnp.sum(part, axis=0, keepdims=True) / gain_ref[...].reshape(1, -1)
    if before_refs:
        gain_part_ref, mlp_part_ref, dwa_part_ref = before_refs
        small_ref[:1, :] = gain + gain_part_ref[...]
        small_ref[1:2, :] = mlp_part_ref[...]
        small_ref[2:, :] = dwa_part_ref[...]
    else:
        small_ref[...] = gain
    wait(stores)


def first_grad_body(
    core_ref, small_ref, turned_a_ref, turned_b_ref, weight_a_ref, weight_b_ref, send_ref, keep_ref,
    turned_a, turned_b, weight_a, weight_b, whole, marks,
):
    low = pl.multiple_of(core_ref[0] * HALF, HALF)
    high = pl.multiple_of((1 - core_ref[0]) * HALF, HALF)
    go = Mover(marks)
    wait(go((turned_a_ref, turned_a), (weight_a_ref, weight_a), (turned_b_ref, turned_b), (weight_b_ref, weight_b)))
    whole[...] = mul(turned_a[...], weight_a[...], 0, 0) + mul(turned_b[...], weight_b[...], 0, 0)
    stores = go((whole.at[pl.ds(low, HALF), :], keep_ref))
    send_ref[:HALF, :] = whole[pl.ds(high, HALF), :].astype(bfloat)
    small = small_ref[...]
    high_part = small.astype(bfloat)
    low_part = (small - high_part.astype(single)).astype(bfloat)
    send_ref[HALF:, :] = jnp.concatenate([high_part, low_part], axis=0)
    wait(stores)


CURVE = float(np.sqrt(2.0 / np.pi))
STEP = 256


def mlp_body(second, *refs):
    if second:
        owner_ref, refs = refs[0], refs[1:]
    x_refs, refs = refs[: 2 * PARTS], refs[2 * PARTS :]
    g_own_ref, g_peer_ref, refs = refs[0], refs[1], refs[2:]
    if second:
        up_ref, down_refs, refs = refs[0], refs[1 : 1 + SQUARE], refs[1 + SQUARE :]
        before_refs, up_mine_ref = refs[:4], refs[4]
        down_grad_ref, part_refs = refs[9], refs[10:14]
        refs = refs[5:9] + refs[14:]
    else:
        up_ref, down_ref = refs[:2]
        down_grad_ref, up_grad_ref = refs[6:8]
        refs = refs[2:6] + refs[8:]
    send_norm_ref, keep_norm_ref, send_out_ref, keep_out_ref = refs[:4]
    x_all, g_all, up, down, active, grad_hidden, x_turned = refs[4:11]
    send_norm, keep_norm, send_out, keep_out, down_grad, up_grad, marks = refs[11:18]
    rows, size = x_all.shape[0] // 2, x_all.shape[0] // (2 * PARTS)
    units = down.shape[0]
    go = Mover(marks)
    x_loads = go(*[(x_refs[index], x_all.at[pl.ds(index * size, size), :]) for index in range(2 * PARTS)])
    if second:
        loads = go((up_ref, up), *joined(owner_ref[0], down_refs, down))
    else:
        loads = go((up_ref, up), (down_ref, down))
    loads += go((g_own_ref, g_all.at[pl.ds(0, rows), :]), (g_peer_ref, g_all.at[pl.ds(rows, rows), :]))
    more, mine, stores = [], [], []
    if second:
        (up_mine,) = refs[18:]
        more = go(*zip(before_refs, (send_norm, keep_norm, send_out, keep_out)))
        mine = go((up_mine_ref, up_mine))
    wait(x_loads)
    x_turned[...] = x_all[...].T
    wait(loads)
    for begin in range(0, units, STEP):
        columns = slice(begin, begin + STEP)
        for top in range(0, 2 * rows, rows):
            span = slice(top, top + rows)
            v = mul(x_all[span, :], up[:, columns])
            grad = mul(g_all[span, :], down[columns, :], 1, 1)
            square = v * v
            half = 0.5 + 0.5 * jnp.tanh(v * (CURVE + (CURVE * 0.044715) * square))
            act = v * half
            slope = half + act * (1.0 - half) * (2.0 * CURVE + (6.0 * CURVE * 0.044715) * square)
            active[span, columns] = act.astype(bfloat)
            grad_hidden[span, columns] = (grad * slope).astype(bfloat)

    def put(target, value):
        target[...] = (value + target[...].astype(single) if second else value).astype(target.dtype)

    wait(more)
    put(keep_norm, mul(grad_hidden[:rows, :], up[...], 1, 1))
    put(send_norm, mul(grad_hidden[rows:, :], up[...], 1, 1))
    stores += go((keep_norm, keep_norm_ref), (send_norm, send_norm_ref))
    down_grad[...] = mul(active[...], g_all[...], 0, 0).astype(down_grad.dtype)
    stores += go((down_grad, down_grad_ref))
    up_grad[...] = mul(x_turned[...], grad_hidden[...]).astype(bfloat)
    if second:
        wait(mine)
        part = up_grad.shape[0] // SQUARE
        for mask, part_ref in enumerate(part_refs):
            rows_of = quarter(owner_ref[0], mask, part)
            stores += go(
                (up_mine.at[rows_of, :], part_ref.at[pl.ds(0, part), :]),
                (up_grad.at[rows_of, :], part_ref.at[pl.ds(part, part), :]),
            )
    else:
        stores += go((up_grad, up_grad_ref))
    put(keep_out, mul(active[:rows, :], down[...]))
    stores += go((keep_out, keep_out_ref))
    put(send_out, mul(active[rows:, :], down[...]))
    wait(stores + go((send_out, send_out_ref)))


def mlp(x_own, x_peer, g_own, g_peer, up, down, upper=(), before=(), flops=0):
    rows, width = g_own.shape
    units = sum(piece.shape[0] for piece in down)
    tall = (2 * rows, width)
    pair = [((rows, width), bfloat), ((rows, width), single)] * 2
    outs = pair + [((units, width), bfloat)]
    outs += [((2 * width // SQUARE, units), bfloat)] * SQUARE if before else [((width, units), bfloat)]
    scratch = [
        pltpu.VMEM(tall, bfloat),
        pltpu.VMEM(tall, bfloat),
        pltpu.VMEM((width, units), bfloat),
        pltpu.VMEM((units, width), bfloat),
        pltpu.VMEM((2 * rows, units), bfloat),
        pltpu.VMEM((2 * rows, units), bfloat),
        pltpu.VMEM((width, 2 * rows), bfloat),
    ]
    scratch += [pltpu.VMEM(shape, kind) for shape, kind in pair]
    scratch += [
        pltpu.VMEM((units, width), bfloat), pltpu.VMEM((width, units), bfloat), pltpu.SemaphoreType.DMA((32,)),
    ]
    if before:
        scratch.append(pltpu.VMEM((width, units), bfloat))
    operands = (*upper, *x_own, *x_peer, g_own, g_peer, *up, *down, *before)
    return call(
        functools.partial(mlp_body, bool(before)),
        outs,
        operands,
        scratch,
        len(upper),
        vmem=60,
        flops=flops,
        far=len(operands) - len(upper),
        far_outs=len(outs),
    )


def shards(
    inputs,
    history,
    cotangent,
    qkv_weight,
    out_weight,
    up_weight,
    down_weight,
    gain_attn,
    gain_mlp,
    dwa_weights,
):
    rows, width = inputs.shape
    members = lax.axis_size("mp")
    copies = lax.axis_size("dp")
    bits = copies.bit_length() - 1
    core = lax.rem(lax.axis_index("mp"), 2).astype(jnp.int32).reshape(1)
    copy_index = lax.axis_index("dp").astype(jnp.int32).reshape(1)
    core_pairs = [(i, i ^ 1) for i in range(members)]
    chip_pairs = [(i, i ^ 2) for i in range(members)]
    depth = history.shape[0]
    part = out_weight.shape[0]

    def other_core(value):
        return lax.ppermute(value, "mp", core_pairs)

    def other_chip(value):
        return lax.ppermute(value, "mp", chip_pairs)

    def other_copy(value, mask):
        return lax.ppermute(value, "dp", [(i, i ^ mask) for i in range(copies)])

    owner = copy_index & (SQUARE - 1)
    cosine, sine = (jnp.asarray(table) for table in tables())

    qkv_own = qkv_weight.transpose(1, 2, 0).reshape(3 * part, width)
    fourth = (width // SQUARE, width)
    square = (width, width)
    masks = range(1, SQUARE)
    marks = pltpu.SemaphoreType.DMA((16,))
    (down_quarter,) = call(
        split_body,
        [(fourth, bfloat)],
        (owner, down_weight),
        [pltpu.VMEM(fourth, bfloat), marks],
        1,
        vmem=60,
        far=1,
        far_outs=1,
    )
    qkv_peer, out_peer = other_chip(qkv_own), other_chip(out_weight)
    down_come, up_peer = other_chip(down_quarter), other_chip(up_weight)

    full = (rows, width)
    x_own = call(norm_body, [((rows // 2, width), bfloat)] * 2, (inputs, gain_attn), after=(down_quarter,))
    x_peer = [other_core(value) for value in x_own]
    tall = (SEQ, width)
    tokens = pltpu.VMEM(tall, bfloat)
    first_outs = [
        ((3 * part, SEQ), bfloat), ((part, SEQ), bfloat), ((SEQ, part), bfloat), ((8, SEQ), single),
    ]
    heads = part // DH
    tiles = [tokens, pltpu.VMEM((heads, SEQ, 256), single), pltpu.VMEM((heads, SEQ, 256), bfloat)]
    qkv_a, att_a, nat_a, log_a = call(
        attend_placed, first_outs, (core, *x_own, *x_peer, cosine, sine, qkv_own), tiles, 1, vmem=32
    )
    history_grad, mixed, g_own, history_parts = average_history(dwa_weights, history, cotangent, (log_a,))
    g_peer = other_core(g_own)
    qkv_b, att_b, nat_b, log_b = call(
        attend_placed,
        first_outs,
        (core, *x_own, *x_peer, cosine, sine, qkv_peer),
        tiles,
        1,
        (history_parts,),
        32,
        MUCH,
    )
    third = (rows // PARTS, width)
    keep, *send, down_copy = call(
        branch_body,
        [(full, single)] + [(third, bfloat)] * PARTS + [(fourth, bfloat)],
        (core, nat_a, nat_b, out_weight, out_peer, down_come),
        (),
        1,
        (g_peer,),
    )
    down_pieces = [down_come] + [other_copy(down_copy, mask) for mask in masks]
    recv = [other_core(value) for value in send]
    middle, *y_own = call(
        middle_body, [(full, single)] + [(third, bfloat)] * PARTS, (inputs, keep, gain_mlp, *recv)
    )
    y_peer = [other_core(value) for value in y_own]

    first = mlp(y_own, y_peer, g_own, g_peer, (up_weight,), (down_weight,))
    down_mine, up_mine = first[4:]
    second = mlp(
        y_own, y_peer, g_own, g_peer, (up_peer,), down_pieces, (owner,), (*first[:4], up_mine)
    )
    send_norm, keep_norm, send_out, keep_out, down_theirs = second[:5]
    token = [keep_norm]

    def step(body, outs, operands, scratch=(), scalars=0, vmem=16, flops=MUCH, far=0, far_outs=0, marked=False):
        count = len(operands)

        def marking(*refs):
            mark_body(refs[count])
            body(*refs[:count], *refs[count + 1 :])

        if marked:
            mark = [((8, 128), single)]
            results = call(marking, mark + outs, operands, scratch, scalars, tuple(token), vmem, flops, far, far_outs)
            token[0] = results[0]
            return results[1:]
        results = call(body, outs, operands, scratch, scalars, tuple(token), vmem, flops, far, far_outs)
        token[0] = min(results, key=lambda value: value.size * value.dtype.itemsize)
        return results

    down_come = other_chip(down_theirs)
    up_parts = [second[5]] + [other_copy(value, mask) for mask, value in zip(masks, second[6:])]
    out_come = other_core(send_out)
    grad_middle, gb_own, gain_mlp_part = step(
        middle_back_body,
        [(full, single), (full, bfloat), ((1, width), single)],
        (dwa_weights, middle, keep_norm, other_core(send_norm), cotangent, gain_mlp),
        scalars=1,
        flops=0,
    )
    gb_peer = other_core(gb_own)
    combined, dwa_part = step(
        combine_body,
        [(full, bfloat), ((depth + 1, width), single)],
        (dwa_weights, mixed, middle, keep_out, out_come, cotangent, history_parts),
        scalars=1,
        flops=0,
    )

    def back(weight, qkv_weight, qkv, att, log, flops, before=()):
        return step(
            attend_back,
            [
                ((depth + 3 if before else 1, width), single),
                ((4 * part, width), bfloat),
                ((3 * part, SEQ), bfloat),
            ],
            (
                core, log, cosine, sine, gain_attn, *before, gb_own, gb_peer, *x_own, *x_peer, weight, qkv_weight, qkv,
                att,
            ),
            [
                pltpu.VMEM(tall, bfloat),
                pltpu.VMEM(tall, bfloat),
                pltpu.VMEM((part, width), bfloat),
                pltpu.VMEM((3 * part, width), bfloat),
                pltpu.VMEM((3 * part, SEQ), bfloat),
                pltpu.VMEM((part, SEQ), bfloat),
                pltpu.VMEM((3 * part, SEQ), bfloat),
                pltpu.VMEM((4 * part, width), bfloat),
                pltpu.VMEM((heads, SEQ, SEQ), bfloat),
                pltpu.VMEM((heads, SEQ, SEQ), bfloat),
                pltpu.VMEM((3 * part, width), single),
                marks,
            ],
            1,
            60,
            flops,
            10,
            2,
        )

    gain_part, att_theirs, turned_b = back(out_peer, qkv_peer, qkv_b, att_b, log_b, 0)
    att_come = other_chip(att_theirs)
    def spread(mine, come, flops=MUCH):
        own, *sent = step(part_body, [(fourth, bfloat)] * SQUARE, (owner, mine, come), scalars=1, flops=flops)
        return [own] + [other_copy(value, mask) for mask, value in zip(masks, sent)]

    down_parts = spread(down_mine, down_come, 0)
    up, sent = step(four_two_body, [(fourth, bfloat)] * 2, up_parts, flops=0)
    up_come = other_chip(sent)
    part_sums, att_mine, turned_a = back(
        out_weight, qkv_own, qkv_a, att_a, log_a, MUCH, (gain_part, gain_mlp_part, dwa_part)
    )

    def exchange(value):
        for bit in range(2, bits):
            come = other_copy(value, 1 << bit)
            if bit < bits - 1:
                (value,) = step(low_body, [(value.shape, bfloat)], (value, come))
        return value, come

    def finish(value, come):
        (value,) = step(low_body, [(value.shape, bfloat)], (value, come), flops=COST)
        return [value] + [other_copy(value, mask) for mask in masks]

    token += down_parts[1:]
    att_parts = spread(att_mine, att_come, COST)
    del token[1:]
    (down,) = step(four_body, [(fourth, bfloat)], down_parts, flops=COST)
    down = exchange(down)
    (up,) = step(low_body, [(fourth, bfloat)], (up, up_come), flops=COST)
    up = exchange(up)
    send_first, keep_first = step(
        first_grad_body,
        [((rows + EXTRA, width), bfloat), (full, single)],
        (core, part_sums, turned_a, turned_b, qkv_own, qkv_peer),
        [pltpu.VMEM((3 * part, SEQ), bfloat)] * 2
        + [pltpu.VMEM((3 * part, width), bfloat)] * 2
        + [pltpu.VMEM(tall, single), marks],
        1,
        60,
        COST,
        4,
        1,
        True,
    )
    first_come = other_core(send_first)
    token.append(down[1])
    step(mark_body, [((8, 128), single)], (), flops=COST)
    del token[1:]
    (part_sums,) = step(small_body, [(part_sums.shape, single)], (part_sums, first_come), flops=COST)
    more_sums = other_chip(part_sums)
    step(mark_body, [((8, 128), single)], (), flops=COST)
    block = (width // SQUARE + EXTRA, width)
    (att,) = step(four_more_body, [(block, bfloat)], (part_sums, more_sums, *att_parts), flops=COST)
    att = exchange(att)
    down = finish(*down)
    token += down[1:]
    pair = (block[0] + fourth[0], width)
    (both,) = step(pair_body, [(pair, bfloat)], (*att, *up), flops=COST)
    del token[1:]
    both = [both] + [other_copy(both, mask) for mask in masks]
    (down_grad,) = step(
        whole_body,
        [(square, single)],
        (owner, *down),
        [pltpu.VMEM(square, bfloat), pltpu.VMEM(square, single), marks],
        1,
        flops=COST,
        far_outs=1,
        marked=True,
    )
    (input_grad,) = step(
        first_back_body,
        [(full, bfloat)],
        (inputs, keep_first, first_come, grad_middle, gain_attn),
        vmem=60,
        flops=COST,
        marked=True,
    )
    gain_attn_grad, gain_mlp_grad, dwa_grad, qkv_grad, out_grad, up_grad = step(
        more_body,
        [
            ((width,), single),
            ((width,), single),
            ((depth + 1,), single, "scalars"),
            ((3 * part, width), single),
            ((part, width), single),
            (square, single),
        ],
        (owner, *both),
        [pltpu.VMEM((SQUARE * pair[0], width), bfloat), pltpu.VMEM(square, single), pltpu.VMEM(square, single), marks],
        1,
        flops=COST,
        far_outs=3,
    )

    return (
        combined,
        input_grad,
        history_grad,
        qkv_grad.reshape(3, part, width).transpose(2, 0, 1),
        out_grad,
        up_grad,
        down_grad,
        gain_attn_grad,
        gain_mlp_grad,
        dwa_grad,
    )


def solution(mesh):
    placed = (
        P(("dp", "mp"), None),
        P(None, ("dp", "mp"), None),
        P(("dp", "mp"), None),
        P(None, None, "mp"),
        P("mp", None),
        P(None, "mp"),
        P("mp", None),
        P(),
        P(),
        P(),
    )
    return jax.shard_map(
        shards,
        mesh=mesh,
        in_specs=placed,
        out_specs=(
            P(("dp", "mp"), None),
            P(("dp", "mp"), None),
            P(None, ("dp", "mp"), None),
            P(None, None, "mp"),
            P("mp", None),
            P(None, "mp"),
            P("mp", None),
            P(),
            P(),
            P(),
        ),
        check_vma=False,
    )
```

```python
import functools

import jax
import jax.numpy as jnp
import numpy as np
from jax import lax
from jax.experimental import pallas as pl
from jax.experimental.pallas import tpu as pltpu
from jax.sharding import PartitionSpec as P

DH = 64
SEQ = 1152
HALF = SEQ // 2
EPS = 1e-05
bfloat = jnp.bfloat16
single = jnp.float32
MIB = 1 << 20
MUCH = 10**11
COST = 10**10


def tables():
    half_width = DH // 2
    places = np.arange(SEQ, dtype=np.float32)
    frequency = np.float32(10000.0) ** (-np.arange(half_width, dtype=np.float32) * np.float32(2.0 / DH))
    angles = frequency[:, None] * places[None, :]
    return (np.cos(angles).astype(np.float32), np.sin(angles).astype(np.float32))


def mul(a, b, ca=1, cb=0):
    return lax.dot_general(a, b, (((ca,), (cb,)), ((), ())), preferred_element_type=single)


def call(kernel, outs, operands, scratch=(), scalars=0, after=(), vmem=16, flops=0, far=0, far_outs=0):
    count, waits = len(operands), len(after)

    def body(*refs):
        kernel(*refs[:count], *refs[count + waits :])

    small = pl.BlockSpec(memory_space=pltpu.SMEM)
    whole = pl.BlockSpec(memory_space=pltpu.VMEM)
    apart = pl.BlockSpec(memory_space=pltpu.HBM)
    loose = pl.BlockSpec(memory_space=pl.ANY)
    inner = len(outs) - far_outs
    return pl.pallas_call(
        body,
        out_shape=[jax.ShapeDtypeStruct(out[0], out[1]) for out in outs],
        in_specs=[small] * scalars + [whole] * (count - scalars - far) + [apart] * far + [loose] * waits,
        out_specs=[small if len(out) > 2 else whole for out in outs[:inner]] + [apart] * far_outs,
        scratch_shapes=list(scratch),
        compiler_params=pltpu.CompilerParams(vmem_limit_bytes=vmem * MIB),
        cost_estimate=pl.CostEstimate(flops=flops, bytes_accessed=0, transcendentals=0),
    )(*operands, *after)


class Mover:
    def __init__(self, marks):
        self.marks = marks
        self.used = 0

    def __call__(self, *pairs):
        copies = []
        for source, target in pairs:
            copies.append(pltpu.make_async_copy(source, target, self.marks.at[self.used]))
            self.used += 1
        for copy in copies:
            copy.start()
        return copies


def wait(copies):
    for copy in copies:
        copy.wait()


ROWS = 64
PARTS = 3


def spans(rows, step=ROWS):
    return [slice(begin, begin + step) for begin in range(0, rows, step)]


def normal_of(x):
    centre = x - jnp.mean(x, axis=-1, keepdims=True)
    spread = jnp.mean(centre * centre, axis=-1, keepdims=True)
    scale = lax.rsqrt(spread + EPS)
    return centre * scale, scale


def split_body(owner_ref, in_ref, out_ref, hold, marks):
    go = Mover(marks)
    wait(go((in_ref.at[quarter(owner_ref[0], 0, hold.shape[0]), :], hold)))
    wait(go((hold, out_ref)))


def joined(owner, refs, target):
    size = refs[0].shape[0]
    return [(ref, target.at[quarter(owner, mask, size), :]) for mask, ref in enumerate(refs)]


def norm_body(x_ref, gain_ref, *out_refs):
    gain = gain_ref[...].reshape(1, -1)
    for index, out_ref in enumerate(out_refs):
        rows = out_ref.shape[0]
        for span in spans(rows, rows // 6):
            here = slice(index * rows + span.start, index * rows + span.stop)
            normal, _ = normal_of(x_ref[here, :].astype(single))
            out_ref[span, :] = (normal * gain).astype(bfloat)


def middle_body(x_ref, keep_ref, gain_ref, *rest):
    recv_refs, mid_ref, out_refs = rest[:PARTS], rest[PARTS], rest[PARTS + 1 :]
    gain = gain_ref[...].reshape(1, -1)
    rows = x_ref.shape[0] // PARTS
    for index in range(PARTS):
        for span in spans(rows):
            here = slice(index * rows + span.start, index * rows + span.stop)
            recv = recv_refs[index][span, :].astype(single)
            x = x_ref[here, :].astype(single) + (keep_ref[here, :] + recv)
            mid_ref[here, :] = x
            normal, _ = normal_of(x)
            out_refs[index][span, :] = (normal * gain).astype(bfloat)


def norm_back(x, grad, gain):
    normal, scale = normal_of(x)
    lifted = grad * gain
    back = scale * (
        lifted
        - jnp.mean(lifted, axis=-1, keepdims=True)
        - normal * jnp.mean(lifted * normal, axis=-1, keepdims=True)
    )
    return back, normal


def fold_rows(value):
    total = value[:8]
    for begin in range(8, value.shape[0], 8):
        total = total + value[begin : begin + 8]
    return total


def middle_back_body(mix_ref, x_ref, keep_ref, recv_ref, cot_ref, gain_ref, mid_ref, low_ref, part_ref):
    gain = gain_ref[...].reshape(1, -1)
    part = jnp.zeros((8, x_ref.shape[1]), single)
    for span in spans(x_ref.shape[0]):
        grad = keep_ref[span, :] + recv_ref[span, :].astype(single)
        back, normal = norm_back(x_ref[span, :], grad, gain)
        total = mix_ref[mix_ref.shape[0] - 1] * cot_ref[span, :] + back
        mid_ref[span, :] = total
        low_ref[span, :] = total.astype(bfloat)
        part = part + fold_rows(grad * normal)
    part_ref[...] = jnp.sum(part, axis=0, keepdims=True)


def first_back_body(x_ref, keep_ref, recv_ref, mid_ref, gain_ref, out_ref):
    gain = gain_ref[...].reshape(1, -1)
    for span in spans(x_ref.shape[0]):
        grad = keep_ref[span, :] + recv_ref[span, :].astype(single)
        back, _ = norm_back(x_ref[span, :].astype(single), grad, gain)
        out_ref[span, :] = (mid_ref[span, :] + back).astype(bfloat)


def history_body(mix_ref, history_ref, cot_ref, grad_ref, mixed_ref, low_ref, part_ref):
    depth = history_ref.shape[0]

    @pl.when(pl.program_id(0) == 0)
    def _():
        part_ref[...] = jnp.zeros_like(part_ref)

    for span in spans(cot_ref.shape[0], 32):
        cot = cot_ref[span, :]
        low_ref[span, :] = (mix_ref[depth] * cot).astype(bfloat)
        mixed = None
        for j in range(depth):
            layer = history_ref[j, span, :].astype(single)
            mixed = mix_ref[j] * layer if mixed is None else mixed + mix_ref[j] * layer
            grad_ref[j, span, :] = (mix_ref[j] * cot).astype(bfloat)
            part_ref[8 * j : 8 * j + 8, :] += fold_rows(layer * cot)
        mixed_ref[span, :] = mixed


def average_history(mix, history, cot, after=()):
    depth, rows, width = history.shape
    step = 96
    waits = len(after)

    def body(*refs):
        history_body(*refs[:3], *refs[3 + waits :])

    row_block = pl.BlockSpec((step, width), lambda i: (i, 0))
    deep_block = pl.BlockSpec((depth, step, width), lambda i: (0, i, 0))
    return pl.pallas_call(
        body,
        grid=(rows // step,),
        out_shape=[
            jax.ShapeDtypeStruct(history.shape, bfloat),
            jax.ShapeDtypeStruct((rows, width), single),
            jax.ShapeDtypeStruct((rows, width), bfloat),
            jax.ShapeDtypeStruct((8 * depth, width), single),
        ],
        in_specs=[pl.BlockSpec(memory_space=pltpu.SMEM), deep_block, row_block]
        + [pl.BlockSpec(memory_space=pl.ANY)] * waits,
        out_specs=[deep_block, row_block, row_block, pl.BlockSpec((8 * depth, width), lambda i: (0, 0))],
        compiler_params=pltpu.CompilerParams(vmem_limit_bytes=16 * MIB),
        cost_estimate=pl.CostEstimate(flops=0, bytes_accessed=0, transcendentals=0),
    )(mix, history, cot, *after)


def combine_body(mix_ref, mixed_ref, mid_ref, keep_ref, recv_ref, cot_ref, parts_ref, out_ref, part_ref):
    depth = mix_ref.shape[0] - 1
    last = jnp.zeros((8, mid_ref.shape[1]), single)
    for span in spans(mid_ref.shape[0]):
        outputs = mid_ref[span, :] + (keep_ref[span, :] + recv_ref[span, :].astype(single))
        out_ref[span, :] = (mixed_ref[span, :] + mix_ref[depth] * outputs).astype(bfloat)
        last = last + fold_rows(outputs * cot_ref[span, :])
    for j in range(depth):
        part_ref[j : j + 1, :] = jnp.sum(parts_ref[8 * j : 8 * j + 8, :], axis=0, keepdims=True)
    part_ref[depth : depth + 1, :] = jnp.sum(last, axis=0, keepdims=True)


SQUARE = 4


def quarter(owner, mask, size):
    other = owner + (mask & 1) * (1 - 2 * (owner % 2)) + (mask & 2) * (1 - 2 * (owner // 2))
    return pl.ds(pl.multiple_of(other * size, size), size)


def part_body(owner_ref, mine_ref, come_ref, *out_refs):
    for mask, out_ref in enumerate(out_refs):
        rows = quarter(owner_ref[0], mask, out_ref.shape[0])
        out_ref[...] = (mine_ref[rows, :].astype(single) + come_ref[rows, :].astype(single)).astype(bfloat)


def sum_of(refs, rows):
    total = refs[0][rows, :].astype(single)
    for ref in refs[1:]:
        total = total + ref[rows, :].astype(single)
    return total


def four_body(*refs):
    refs[-1][...] = sum_of(refs[:-1], slice(None)).astype(bfloat)


def four_two_body(*refs):
    size = refs[-1].shape[0]
    refs[-2][...] = sum_of(refs[:-2], slice(0, size)).astype(bfloat)
    refs[-1][...] = sum_of(refs[:-2], slice(size, 2 * size)).astype(bfloat)


EXTRA = 16


def mark_body(out_ref):
    out_ref[...] = jnp.zeros_like(out_ref)


def small_body(small_ref, first_ref, out_ref):
    half = small_ref.shape[0]
    rows = first_ref.shape[0] - 2 * half
    come = first_ref[rows:, :].astype(single)
    out_ref[...] = small_ref[...] + (come[:half] + come[half:])


def four_more_body(small_ref, more_ref, *refs):
    out_ref = refs[-1]
    size = out_ref.shape[0] - EXTRA
    out_ref[:size, :] = sum_of(refs[:-1], slice(None)).astype(bfloat)
    small = small_ref[...] + more_ref[...]
    rest = jnp.zeros((EXTRA - small.shape[0], small.shape[1]), single)
    out_ref[size:, :] = jnp.concatenate([small, rest], axis=0).astype(bfloat)


def gather(owner_ref, pieces, hold):
    for mask, piece in enumerate(pieces):
        hold[quarter(owner_ref[0], mask, piece.shape[0]), :] = piece[...]


def pair_body(a_ref, a_come_ref, b_ref, b_come_ref, out_ref):
    size = a_ref.shape[0]
    out_ref[:size, :] = sum_of((a_ref, a_come_ref), slice(None)).astype(bfloat)
    out_ref[size:, :] = sum_of((b_ref, b_come_ref), slice(None)).astype(bfloat)


def whole_body(owner_ref, a_ref, b_ref, c_ref, d_ref, out_ref, hold, full, marks):
    gather(owner_ref, (a_ref, b_ref, c_ref, d_ref), hold)
    go, stores = Mover(marks), []
    size = hold.shape[0] // SQUARE
    for index in range(SQUARE):
        rows = pl.ds(index * size, size)
        full[rows, :] = hold[rows, :].astype(single)
        stores += go((full.at[rows, :], out_ref.at[rows, :]))
    wait(stores)


def more_body(
    owner_ref, a_ref, b_ref, c_ref, d_ref, attn_ref, mlp_ref, dwa_ref, top_ref, end_ref, up_ref, hold, att, up, marks
):
    gather(owner_ref, (a_ref, b_ref, c_ref, d_ref), hold)
    go, stores = Mover(marks), []
    block = hold.shape[0] // SQUARE
    size = up.shape[0] // SQUARE
    small = jnp.zeros((EXTRA, hold.shape[1]), single)
    for index in range(SQUARE):
        begin = index * block
        rows = pl.ds(index * size, size)
        att[rows, :] = hold[begin : begin + size, :].astype(single)
        stores += go((att.at[rows, :], top_ref.at[rows, :] if index < SQUARE - 1 else end_ref))
        small = small + hold[begin + size : begin + size + EXTRA, :].astype(single)
        up[rows, :] = hold[begin + size + EXTRA : begin + block, :].astype(single)
        stores += go((up.at[rows, :], up_ref.at[rows, :]))
    attn_ref[...] = small[0]
    mlp_ref[...] = small[1]
    for index in range(dwa_ref.shape[0]):
        dwa_ref[index] = jnp.sum(small[2 + index : 3 + index])
    wait(stores)


def low_body(mine_ref, come_ref, out_ref):
    out_ref[...] = (mine_ref[...].astype(single) + come_ref[...].astype(single)).astype(bfloat)


def mark_body(out_ref):
    out_ref[...] = jnp.zeros_like(out_ref)


def small_body(small_ref, first_ref, out_ref):
    half = small_ref.shape[0]
    rows = first_ref.shape[0] - 2 * half
    come = first_ref[rows:, :].astype(single)
    out_ref[...] = small_ref[...] + (come[:half] + come[half:])


BLOCKS = tuple((begin, min(256, SEQ - begin)) for begin in range(0, SEQ, 256))


def places(core_ref, refs):
    count, size = len(refs) // 2, refs[0].shape[0]
    for index, ref in enumerate(refs):
        core = core_ref[0] if index < count else 1 - core_ref[0]
        yield ref, pl.ds(pl.multiple_of(core * HALF + index % count * size, size), size)


def allowed(size):
    key_pos = lax.broadcasted_iota(jnp.int32, (size, size), 0)
    query_pos = lax.broadcasted_iota(jnp.int32, (size, size), 1)
    return query_pos >= key_pos


def turn(rows, cosine, sine):
    half = rows.shape[0] // 2
    a, b = rows[:half], rows[half:]
    return jnp.concatenate([a * cosine - b * sine, b * cosine + a * sine], axis=0)


KEYS = 128


def fold_top(value):
    top = value[:8]
    for begin in range(8, value.shape[0], 8):
        top = jnp.maximum(top, value[begin : begin + 8])
    return top


def masked(scores, offset):
    key_pos = lax.broadcasted_iota(jnp.int32, scores.shape, 0) + offset
    query_pos = lax.broadcasted_iota(jnp.int32, scores.shape, 1)
    return jnp.where(query_pos >= key_pos, scores, -jnp.inf)


def attend_placed(core_ref, *rest):
    for ref, where in places(core_ref, rest[:4]):
        rest[11][where, :] = ref[...]
    cos_ref, sin_ref, weight_ref, rest = rest[4], rest[5], rest[6], rest[7:]
    attend(weight_ref, cos_ref, sin_ref, *rest)


def attend(weight_ref, cos_ref, sin_ref, qkv_ref, att_ref, nat_ref, log_ref, tokens, all_scores, all_weights):
    width = weight_ref.shape[0] // 3
    projected = mul(weight_ref[...], tokens[...], 1, 1)
    cosine, sine = cos_ref[...], sin_ref[...]
    for part in range(3):
        for head in range(width // DH):
            begin = part * width + head * DH
            rows = projected[begin : begin + DH]
            if part < 2:
                rows = turn(rows, cosine, sine)
            if part == 0:
                rows = rows * DH ** (-0.5)
            qkv_ref[begin : begin + DH, :] = rows.astype(bfloat)
    log_ref[...] = jnp.zeros_like(log_ref)
    heads = range(width // DH)
    keys = [qkv_ref[width + head * DH : width + head * DH + DH, :].T for head in heads]
    for begin, size in BLOCKS:
        end = begin + size
        tops = [None for _ in heads]
        for row in range(0, end, KEYS):
            for head in heads:
                tile = mul(keys[head][row : row + KEYS], qkv_ref[head * DH : head * DH + DH, begin:end])
                if row >= begin:
                    tile = masked(tile, row - begin)
                all_scores[head, row : row + KEYS, :size] = tile
                top = fold_top(tile)
                tops[head] = top if row == 0 else jnp.maximum(tops[head], top)
        tops = [jnp.max(top, axis=0, keepdims=True) for top in tops]
        totals = [jnp.zeros((8, size), single) for _ in heads]
        for row in range(0, end, KEYS):
            for head in heads:
                tile = jnp.exp(all_scores[head, row : row + KEYS, :size] - tops[head])
                totals[head] = totals[head] + fold_rows(tile)
                all_weights[head, row : row + KEYS, :size] = tile.astype(bfloat)
        for head in heads:
            base = head * DH
            total = jnp.sum(totals[head], axis=0, keepdims=True)
            value = qkv_ref[2 * width + base : 2 * width + base + DH, :end]
            mixed = mul(value, all_weights[head, :end, :size]) / total
            att_ref[base : base + DH, begin:end] = mixed.astype(bfloat)
            log_ref[head : head + 1, begin:end] = tops[head] + jnp.log(total)
    nat_ref[...] = att_ref[...].T


def branch_body(core_ref, att_a_ref, att_b_ref, out_a_ref, out_b_ref, pass_ref, keep_ref, *rest):
    send_refs, pass_out = rest[:PARTS], rest[PARTS]
    pass_out[...] = pass_ref[...]
    low = pl.multiple_of(core_ref[0] * HALF, HALF)
    rows = HALF // PARTS
    for index in range(PARTS):
        high = pl.multiple_of((1 - core_ref[0]) * HALF + index * rows, rows)
        send = mul(att_a_ref[pl.ds(high, rows), :], out_a_ref[...])
        send_refs[index][...] = (send + mul(att_b_ref[pl.ds(high, rows), :], out_b_ref[...])).astype(bfloat)
    keep = mul(att_a_ref[pl.ds(low, HALF), :], out_a_ref[...])
    keep_ref[...] = keep + mul(att_b_ref[pl.ds(low, HALF), :], out_b_ref[...])


def attend_back(
    core_ref, log_ref, cos_ref, sin_ref, gain_ref, *rest
):
    before_refs, rest = rest[:-25], rest[-25:]
    grad_refs, x_refs = rest[:2], rest[2:6]
    weight_ref, qkv_weight_ref, qkv_ref, att_ref, small_ref, out_ref, turned_ref = rest[6:13]
    grads, tokens, weight, qkv_weight, qkv, att, turned, result, all_probs, all_scores, hold, marks = rest[13:]
    go = Mover(marks)
    first = go(
        (weight_ref, weight),
        *[(ref, grads.at[where, :]) for ref, where in places(core_ref, grad_refs)],
        (att_ref, att),
        (qkv_ref, qkv),
    )
    later = go(
        *[(ref, tokens.at[where, :]) for ref, where in places(core_ref, x_refs)],
        (qkv_weight_ref, qkv_weight),
    )
    wait(first)
    width = att.shape[0]
    grad_att = mul(weight[...], grads[...], 1, 1).astype(bfloat)
    result[3 * width :, :] = mul(att[...], grads[...]).astype(result.dtype)
    cosine, sine = cos_ref[...], sin_ref[...]
    heads = range(width // DH)
    spans_of = [slice(head * DH, head * DH + DH) for head in heads]
    query = [qkv[span, :] for span in spans_of]
    key = [qkv[width + span.start : width + span.stop, :] for span in spans_of]
    above = [grad_att[span] for span in spans_of]
    centre = [
        jnp.sum(above[head].astype(single) * att[span, :].astype(single), axis=0, keepdims=True)
        for head, span in enumerate(spans_of)
    ]
    keys = [value.T for value in key]
    values = [qkv[2 * width + span.start : 2 * width + span.stop, :].T for span in spans_of]
    queries = [value.T for value in query]
    aboves = [value.T for value in above]
    grad_query = [[] for _ in heads]
    for begin, size in BLOCKS:
        end = begin + size
        for row in range(0, end, KEYS):
            span = slice(row, row + KEYS)
            for head in heads:
                tile = mul(keys[head][span], query[head][:, begin:end])
                if row >= begin:
                    tile = masked(tile, row - begin)
                tile = jnp.exp(tile - log_ref[head : head + 1, begin:end])
                grad = mul(values[head][span], above[head][:, begin:end]) - centre[head][:, begin:end]
                all_probs[head, span, begin:end] = tile.astype(bfloat)
                all_scores[head, span, begin:end] = (tile * grad).astype(bfloat)
        for head in heads:
            grad_query[head].append(mul(key[head][:, :end], all_scores[head, :end, begin:end]))
    grad_key = [[] for _ in heads]
    grad_value = [[] for _ in heads]
    for begin, size in BLOCKS:
        span = slice(begin, begin + size)
        for head in heads:
            grad_key[head].append(mul(all_scores[head, span, begin:], queries[head][begin:]))
            grad_value[head].append(mul(all_probs[head, span, begin:], aboves[head][begin:]))
    for head, span in enumerate(spans_of):
        grad = jnp.concatenate(grad_query[head], axis=1) * DH ** (-0.5)
        turned[span, :] = turn(grad, cosine, -sine).astype(bfloat)
        grad = jnp.concatenate(grad_key[head], axis=0).T
        turned[width + span.start : width + span.stop, :] = turn(grad, cosine, -sine).astype(bfloat)
        grad = jnp.concatenate(grad_value[head], axis=0).T
        turned[2 * width + span.start : 2 * width + span.stop, :] = grad.astype(bfloat)
    stores = go((turned, turned_ref))
    wait(later)
    hold[...] = mul(turned[...], tokens[...])
    result[: 3 * width, :] = hold[...].astype(result.dtype)
    stores += go((result, out_ref))
    part = jnp.zeros((8, hold.shape[1]), single)
    for span in spans(hold.shape[0]):
        part = part + fold_rows(hold[span, :] * qkv_weight[span, :].astype(single))
    gain = jnp.sum(part, axis=0, keepdims=True) / gain_ref[...].reshape(1, -1)
    if before_refs:
        gain_part_ref, mlp_part_ref, dwa_part_ref = before_refs
        small_ref[:1, :] = gain + gain_part_ref[...]
        small_ref[1:2, :] = mlp_part_ref[...]
        small_ref[2:, :] = dwa_part_ref[...]
    else:
        small_ref[...] = gain
    wait(stores)


def first_grad_body(
    core_ref, small_ref, turned_a_ref, turned_b_ref, weight_a_ref, weight_b_ref, send_ref, keep_ref,
    turned_a, turned_b, weight_a, weight_b, whole, marks,
):
    low = pl.multiple_of(core_ref[0] * HALF, HALF)
    high = pl.multiple_of((1 - core_ref[0]) * HALF, HALF)
    go = Mover(marks)
    wait(go((turned_a_ref, turned_a), (weight_a_ref, weight_a), (turned_b_ref, turned_b), (weight_b_ref, weight_b)))
    whole[...] = mul(turned_a[...], weight_a[...], 0, 0) + mul(turned_b[...], weight_b[...], 0, 0)
    stores = go((whole.at[pl.ds(low, HALF), :], keep_ref))
    send_ref[:HALF, :] = whole[pl.ds(high, HALF), :].astype(bfloat)
    small = small_ref[...]
    high_part = small.astype(bfloat)
    low_part = (small - high_part.astype(single)).astype(bfloat)
    send_ref[HALF:, :] = jnp.concatenate([high_part, low_part], axis=0)
    wait(stores)


CURVE = float(np.sqrt(2.0 / np.pi))
STEP = 256


def mlp_body(second, *refs):
    if second:
        owner_ref, refs = refs[0], refs[1:]
    x_refs, refs = refs[: 2 * PARTS], refs[2 * PARTS :]
    g_own_ref, g_peer_ref, refs = refs[0], refs[1], refs[2:]
    if second:
        up_ref, down_refs, refs = refs[0], refs[1 : 1 + SQUARE], refs[1 + SQUARE :]
        before_refs, up_mine_ref = refs[:4], refs[4]
        down_grad_ref, part_refs = refs[9], refs[10:14]
        refs = refs[5:9] + refs[14:]
    else:
        up_ref, down_ref = refs[:2]
        down_grad_ref, up_grad_ref = refs[6:8]
        refs = refs[2:6] + refs[8:]
    send_norm_ref, keep_norm_ref, send_out_ref, keep_out_ref = refs[:4]
    x_all, g_all, up, down, active, grad_hidden, x_turned = refs[4:11]
    send_norm, keep_norm, send_out, keep_out, down_grad, up_grad, marks = refs[11:18]
    rows, size = x_all.shape[0] // 2, x_all.shape[0] // (2 * PARTS)
    units = down.shape[0]
    go = Mover(marks)
    x_loads = go(*[(x_refs[index], x_all.at[pl.ds(index * size, size), :]) for index in range(2 * PARTS)])
    if second:
        loads = go((up_ref, up), *joined(owner_ref[0], down_refs, down))
    else:
        loads = go((up_ref, up), (down_ref, down))
    loads += go((g_own_ref, g_all.at[pl.ds(0, rows), :]), (g_peer_ref, g_all.at[pl.ds(rows, rows), :]))
    more, mine, stores = [], [], []
    if second:
        (up_mine,) = refs[18:]
        more = go(*zip(before_refs, (send_norm, keep_norm, send_out, keep_out)))
        mine = go((up_mine_ref, up_mine))
    wait(x_loads)
    x_turned[...] = x_all[...].T
    wait(loads)
    for begin in range(0, units, STEP):
        columns = slice(begin, begin + STEP)
        for top in range(0, 2 * rows, rows):
            span = slice(top, top + rows)
            v = mul(x_all[span, :], up[:, columns])
            grad = mul(g_all[span, :], down[columns, :], 1, 1)
            square = v * v
            half = 0.5 + 0.5 * jnp.tanh(v * (CURVE + (CURVE * 0.044715) * square))
            act = v * half
            slope = half + act * (1.0 - half) * (2.0 * CURVE + (6.0 * CURVE * 0.044715) * square)
            active[span, columns] = act.astype(bfloat)
            grad_hidden[span, columns] = (grad * slope).astype(bfloat)

    def put(target, value):
        target[...] = (value + target[...].astype(single) if second else value).astype(target.dtype)

    wait(more)
    put(keep_norm, mul(grad_hidden[:rows, :], up[...], 1, 1))
    put(send_norm, mul(grad_hidden[rows:, :], up[...], 1, 1))
    stores += go((keep_norm, keep_norm_ref), (send_norm, send_norm_ref))
    down_grad[...] = mul(active[...], g_all[...], 0, 0).astype(down_grad.dtype)
    stores += go((down_grad, down_grad_ref))
    up_grad[...] = mul(x_turned[...], grad_hidden[...]).astype(bfloat)
    if second:
        wait(mine)
        part = up_grad.shape[0] // SQUARE
        for mask, part_ref in enumerate(part_refs):
            rows_of = quarter(owner_ref[0], mask, part)
            stores += go(
                (up_mine.at[rows_of, :], part_ref.at[pl.ds(0, part), :]),
                (up_grad.at[rows_of, :], part_ref.at[pl.ds(part, part), :]),
            )
    else:
        stores += go((up_grad, up_grad_ref))
    put(keep_out, mul(active[:rows, :], down[...]))
    stores += go((keep_out, keep_out_ref))
    put(send_out, mul(active[rows:, :], down[...]))
    wait(stores + go((send_out, send_out_ref)))


def mlp(x_own, x_peer, g_own, g_peer, up, down, upper=(), before=(), flops=0):
    rows, width = g_own.shape
    units = sum(piece.shape[0] for piece in down)
    tall = (2 * rows, width)
    pair = [((rows, width), bfloat), ((rows, width), single)] * 2
    outs = pair + [((units, width), bfloat)]
    outs += [((2 * width // SQUARE, units), bfloat)] * SQUARE if before else [((width, units), bfloat)]
    scratch = [
        pltpu.VMEM(tall, bfloat),
        pltpu.VMEM(tall, bfloat),
        pltpu.VMEM((width, units), bfloat),
        pltpu.VMEM((units, width), bfloat),
        pltpu.VMEM((2 * rows, units), bfloat),
        pltpu.VMEM((2 * rows, units), bfloat),
        pltpu.VMEM((width, 2 * rows), bfloat),
    ]
    scratch += [pltpu.VMEM(shape, kind) for shape, kind in pair]
    scratch += [
        pltpu.VMEM((units, width), bfloat), pltpu.VMEM((width, units), bfloat), pltpu.SemaphoreType.DMA((32,)),
    ]
    if before:
        scratch.append(pltpu.VMEM((width, units), bfloat))
    operands = (*upper, *x_own, *x_peer, g_own, g_peer, *up, *down, *before)
    return call(
        functools.partial(mlp_body, bool(before)),
        outs,
        operands,
        scratch,
        len(upper),
        vmem=60,
        flops=flops,
        far=len(operands) - len(upper),
        far_outs=len(outs),
    )


def shards(
    inputs,
    history,
    cotangent,
    qkv_weight,
    out_weight,
    up_weight,
    down_weight,
    gain_attn,
    gain_mlp,
    dwa_weights,
):
    rows, width = inputs.shape
    members = lax.axis_size("mp")
    copies = lax.axis_size("dp")
    bits = copies.bit_length() - 1
    core = lax.rem(lax.axis_index("mp"), 2).astype(jnp.int32).reshape(1)
    copy_index = lax.axis_index("dp").astype(jnp.int32).reshape(1)
    core_pairs = [(i, i ^ 1) for i in range(members)]
    chip_pairs = [(i, i ^ 2) for i in range(members)]
    depth = history.shape[0]
    part = out_weight.shape[0]

    def other_core(value):
        return lax.ppermute(value, "mp", core_pairs)

    def other_chip(value):
        return lax.ppermute(value, "mp", chip_pairs)

    def other_copy(value, mask):
        return lax.ppermute(value, "dp", [(i, i ^ mask) for i in range(copies)])

    owner = copy_index & (SQUARE - 1)
    cosine, sine = (jnp.asarray(table) for table in tables())

    qkv_own = qkv_weight.transpose(1, 2, 0).reshape(3 * part, width)
    fourth = (width // SQUARE, width)
    square = (width, width)
    masks = range(1, SQUARE)
    marks = pltpu.SemaphoreType.DMA((16,))
    (down_quarter,) = call(
        split_body,
        [(fourth, bfloat)],
        (owner, down_weight),
        [pltpu.VMEM(fourth, bfloat), marks],
        1,
        vmem=60,
        far=1,
        far_outs=1,
    )
    qkv_peer, out_peer = other_chip(qkv_own), other_chip(out_weight)
    down_come, up_peer = other_chip(down_quarter), other_chip(up_weight)

    full = (rows, width)
    x_own = call(norm_body, [((rows // 2, width), bfloat)] * 2, (inputs, gain_attn), after=(down_quarter,))
    x_peer = [other_core(value) for value in x_own]
    tall = (SEQ, width)
    tokens = pltpu.VMEM(tall, bfloat)
    first_outs = [
        ((3 * part, SEQ), bfloat), ((part, SEQ), bfloat), ((SEQ, part), bfloat), ((8, SEQ), single),
    ]
    heads = part // DH
    tiles = [tokens, pltpu.VMEM((heads, SEQ, 256), single), pltpu.VMEM((heads, SEQ, 256), bfloat)]
    qkv_a, att_a, nat_a, log_a = call(
        attend_placed, first_outs, (core, *x_own, *x_peer, cosine, sine, qkv_own), tiles, 1, vmem=32
    )
    history_grad, mixed, g_own, history_parts = average_history(dwa_weights, history, cotangent, (log_a,))
    g_peer = other_core(g_own)
    qkv_b, att_b, nat_b, log_b = call(
        attend_placed,
        first_outs,
        (core, *x_own, *x_peer, cosine, sine, qkv_peer),
        tiles,
        1,
        (history_parts,),
        32,
        MUCH,
    )
    third = (rows // PARTS, width)
    keep, *send, down_copy = call(
        branch_body,
        [(full, single)] + [(third, bfloat)] * PARTS + [(fourth, bfloat)],
        (core, nat_a, nat_b, out_weight, out_peer, down_come),
        (),
        1,
        (g_peer,),
    )
    down_pieces = [down_come] + [other_copy(down_copy, mask) for mask in masks]
    recv = [other_core(value) for value in send]
    middle, *y_own = call(
        middle_body, [(full, single)] + [(third, bfloat)] * PARTS, (inputs, keep, gain_mlp, *recv)
    )
    y_peer = [other_core(value) for value in y_own]

    first = mlp(y_own, y_peer, g_own, g_peer, (up_weight,), (down_weight,))
    down_mine, up_mine = first[4:]
    second = mlp(
        y_own, y_peer, g_own, g_peer, (up_peer,), down_pieces, (owner,), (*first[:4], up_mine)
    )
    send_norm, keep_norm, send_out, keep_out, down_theirs = second[:5]
    token = [keep_norm]

    def step(body, outs, operands, scratch=(), scalars=0, vmem=16, flops=MUCH, far=0, far_outs=0, marked=False):
        count = len(operands)

        def marking(*refs):
            mark_body(refs[count])
            body(*refs[:count], *refs[count + 1 :])

        if marked:
            mark = [((8, 128), single)]
            results = call(marking, mark + outs, operands, scratch, scalars, tuple(token), vmem, flops, far, far_outs)
            token[0] = results[0]
            return results[1:]
        results = call(body, outs, operands, scratch, scalars, tuple(token), vmem, flops, far, far_outs)
        token[0] = min(results, key=lambda value: value.size * value.dtype.itemsize)
        return results

    down_come = other_chip(down_theirs)
    up_parts = [second[5]] + [other_copy(value, mask) for mask, value in zip(masks, second[6:])]
    out_come = other_core(send_out)
    grad_middle, gb_own, gain_mlp_part = step(
        middle_back_body,
        [(full, single), (full, bfloat), ((1, width), single)],
        (dwa_weights, middle, keep_norm, other_core(send_norm), cotangent, gain_mlp),
        scalars=1,
        flops=0,
    )
    gb_peer = other_core(gb_own)
    combined, dwa_part = step(
        combine_body,
        [(full, bfloat), ((depth + 1, width), single)],
        (dwa_weights, mixed, middle, keep_out, out_come, cotangent, history_parts),
        scalars=1,
        flops=0,
    )

    def back(weight, qkv_weight, qkv, att, log, flops, before=()):
        return step(
            attend_back,
            [
                ((depth + 3 if before else 1, width), single),
                ((4 * part, width), bfloat),
                ((3 * part, SEQ), bfloat),
            ],
            (
                core, log, cosine, sine, gain_attn, *before, gb_own, gb_peer, *x_own, *x_peer, weight, qkv_weight, qkv,
                att,
            ),
            [
                pltpu.VMEM(tall, bfloat),
                pltpu.VMEM(tall, bfloat),
                pltpu.VMEM((part, width), bfloat),
                pltpu.VMEM((3 * part, width), bfloat),
                pltpu.VMEM((3 * part, SEQ), bfloat),
                pltpu.VMEM((part, SEQ), bfloat),
                pltpu.VMEM((3 * part, SEQ), bfloat),
                pltpu.VMEM((4 * part, width), bfloat),
                pltpu.VMEM((heads, SEQ, SEQ), bfloat),
                pltpu.VMEM((heads, SEQ, SEQ), bfloat),
                pltpu.VMEM((3 * part, width), single),
                marks,
            ],
            1,
            36,
            flops,
            10,
            2,
        )

    gain_part, att_theirs, turned_b = back(out_peer, qkv_peer, qkv_b, att_b, log_b, 0)
    att_come = other_chip(att_theirs)
    def spread(mine, come, flops=MUCH):
        own, *sent = step(part_body, [(fourth, bfloat)] * SQUARE, (owner, mine, come), scalars=1, flops=flops)
        return [own] + [other_copy(value, mask) for mask, value in zip(masks, sent)]

    down_parts = spread(down_mine, down_come, 0)
    up, sent = step(four_two_body, [(fourth, bfloat)] * 2, up_parts, flops=0)
    up_come = other_chip(sent)
    part_sums, att_mine, turned_a = back(
        out_weight, qkv_own, qkv_a, att_a, log_a, MUCH, (gain_part, gain_mlp_part, dwa_part)
    )

    def exchange(value):
        for bit in range(2, bits):
            come = other_copy(value, 1 << bit)
            if bit < bits - 1:
                (value,) = step(low_body, [(value.shape, bfloat)], (value, come))
        return value, come

    def finish(value, come):
        (value,) = step(low_body, [(value.shape, bfloat)], (value, come), flops=COST)
        return [value] + [other_copy(value, mask) for mask in masks]

    (down,) = step(four_body, [(fourth, bfloat)], down_parts, flops=COST)
    down = exchange(down)
    att_parts = spread(att_mine, att_come, COST)
    (up,) = step(low_body, [(fourth, bfloat)], (up, up_come), flops=COST)
    up = exchange(up)
    send_first, keep_first = step(
        first_grad_body,
        [((rows + EXTRA, width), bfloat), (full, single)],
        (core, part_sums, turned_a, turned_b, qkv_own, qkv_peer),
        [pltpu.VMEM((3 * part, SEQ), bfloat)] * 2
        + [pltpu.VMEM((3 * part, width), bfloat)] * 2
        + [pltpu.VMEM(tall, single), marks],
        1,
        60,
        COST,
        4,
        1,
        True,
    )
    first_come = other_core(send_first)
    token.append(down[1])
    step(mark_body, [((8, 128), single)], (), flops=COST)
    del token[1:]
    (part_sums,) = step(small_body, [(part_sums.shape, single)], (part_sums, first_come), flops=COST)
    more_sums = other_chip(part_sums)
    (input_grad,) = step(
        first_back_body,
        [(full, bfloat)],
        (inputs, keep_first, first_come, grad_middle, gain_attn),
        vmem=60,
        flops=COST,
        marked=True,
    )
    block = (width // SQUARE + EXTRA, width)
    (att,) = step(four_more_body, [(block, bfloat)], (part_sums, more_sums, *att_parts), flops=COST)
    att = exchange(att)
    down = finish(*down)
    token += down[1:]
    pair = (block[0] + fourth[0], width)
    (both,) = step(pair_body, [(pair, bfloat)], (*att, *up), flops=COST)
    del token[1:]
    both = [both] + [other_copy(both, mask) for mask in masks]
    (down_grad,) = step(
        whole_body,
        [(square, single)],
        (owner, *down),
        [pltpu.VMEM(square, bfloat), pltpu.VMEM(square, single), marks],
        1,
        flops=COST,
        far_outs=1,
        marked=True,
    )
    gain_attn_grad, gain_mlp_grad, dwa_grad, qkv_grad, out_grad, up_grad = step(
        more_body,
        [
            ((width,), single),
            ((width,), single),
            ((depth + 1,), single, "scalars"),
            ((3 * part, width), single),
            ((part, width), single),
            (square, single),
        ],
        (owner, *both),
        [pltpu.VMEM((SQUARE * pair[0], width), bfloat), pltpu.VMEM(square, single), pltpu.VMEM(square, single), marks],
        1,
        flops=COST,
        far_outs=3,
    )

    return (
        combined,
        input_grad,
        history_grad,
        qkv_grad.reshape(3, part, width).transpose(2, 0, 1),
        out_grad,
        up_grad,
        down_grad,
        gain_attn_grad,
        gain_mlp_grad,
        dwa_grad,
    )


def solution(mesh):
    placed = (
        P(("dp", "mp"), None),
        P(None, ("dp", "mp"), None),
        P(("dp", "mp"), None),
        P(None, None, "mp"),
        P("mp", None),
        P(None, "mp"),
        P("mp", None),
        P(),
        P(),
        P(),
    )
    return jax.shard_map(
        shards,
        mesh=mesh,
        in_specs=placed,
        out_specs=(
            P(("dp", "mp"), None),
            P(("dp", "mp"), None),
            P(None, ("dp", "mp"), None),
            P(None, None, "mp"),
            P("mp", None),
            P(None, "mp"),
            P("mp", None),
            P(),
            P(),
            P(),
        ),
        check_vma=False,
    )
```
